32 devices in a mesh: seq: 8 (over z, core), head: 4 (over y, x).
Axes of the slice: x: 2, y: 2, z: 4, core: 2. Of those that a mesh axis runs over, the one named last changes fastest.
Arguments:
- query_in: bfloat16 [4096, 2048], P(('seq', 'head')), may hold values from -4.6 to 4.6
- key_in: bfloat16 [4096, 2048], P(('seq', 'head')), may hold values from -4.6 to 4.6
- value_in: bfloat16 [4096, 2048], P(('seq', 'head')), may hold values from -6 to 6
- grad_out: bfloat16 [4096, 2048], P(('seq', 'head')), may hold values from -6 to 6
- module_lengths: int32 [128], replicated, may hold values from 1 to 64, 4096 in all
Outputs:
- attn_out: bfloat16 [4096, 2048], P(('seq', 'head'))
- grad_query: bfloat16 [4096, 2048], P(('seq', 'head'))
- grad_key: bfloat16 [4096, 2048], P(('seq', 'head'))
- grad_value: bfloat16 [4096, 2048], P(('seq', 'head'))
The draws below stay inside these ranges and needn't reach their ends.
Inputs may be any that keep to these rules, and one draw needn't show every extreme that they name: `module_lengths`: the lengths sum to 4096; the longest is exactly 64.
All inputs are finite; a program needn't handle non-finite values.
Results may differ from the reference program's by a relative error of at most 0.03.
Values may be sent and summed in bfloat16 or wider, within the bound.
No kernel may reach another device: no remote copies, remote signals or barrier semaphores. Data moves between devices by JAX's collectives and lax.ppermute only.
A program may use at most 64 MiB of HBM per device.

```python
import math
import jax
import jax.numpy as jnp
import numpy as np
from jax import lax

HEADS = 16
HEAD_DIM = 128
D = 2048
TOK_DEV = 128
PRIOR = 64
TOKENS = 4096
MODULES = 128
N_SEQ = 8
N_HEAD = 4


def drawn_rows(key, role_code):
    result = jnp.clip(jax.random.normal(jax.random.fold_in(key, role_code), (TOKENS, D), jnp.float32), -4.6, 4.6)
    return result.astype(jnp.bfloat16)


def draw_query_in(key, part):
    return drawn_rows(key, 1)


def draw_key_in(key, part):
    return drawn_rows(key, 2)


def shard_levels(stream_key, extent, shards, least, largest):
    loudness, own = 1.0, jax.random.fold_in(stream_key, 6)
    for axis_at, blocks in shards:
        steps = jnp.exp(jax.random.uniform(jax.random.fold_in(own, axis_at), (blocks,), jnp.float32, least / len(shards), largest / len(shards)))
        loudness = loudness * jnp.repeat(steps, extent[axis_at] // blocks).reshape([-1 if axis == axis_at else 1 for axis in range(len(extent))])
    return loudness


def length_profile(number_of, total, bound, lean):
    portions = [(1 << 20) // math.isqrt(standing ** lean) + 1 for standing in range(2, number_of + 1)]
    rest, given = total - bound - (number_of - 1), [1] * (number_of - 1)
    while rest > 0:
        movable = [i for i in range(number_of - 1) if given[i] < bound]
        whole, remaining = sum([portions[i] for i in movable]), rest
        for i in movable:
            more = min(bound - given[i], max(1, remaining * portions[i] // whole), rest)
            given[i] = given[i] + more
            rest = rest - more
    return np.array([bound] + given)


def uneven_parts(own_key, count, total, reach, slope):
    if count == 2:
        one = jax.random.randint(own_key, (), max(1, total - reach), min(reach, total - 1) + 1)
        return jnp.stack([one, total - one])
    sizes = jnp.asarray(length_profile(count, total, reach, slope), jnp.int32)
    pairs = (count - 1) // 2
    source_of, receiver = sizes[1:1 + 2 * pairs:2], sizes[2:2 + 2 * pairs:2]
    room = jnp.minimum(source_of - 1, reach - receiver)
    moved = jax.random.randint(jax.random.fold_in(own_key, 1), (pairs,), 0, 1 << 20) % (room + 1)
    sizes = sizes.at[1:1 + 2 * pairs:2].set(source_of - moved).at[2:2 + 2 * pairs:2].set(receiver + moved)
    return sizes[jax.random.permutation(jax.random.fold_in(own_key, 2), count)]


def noise(key, extent, spread, most, pieces=(), kind=jnp.bfloat16):
    factor_of = shard_levels(key, extent, pieces, -0.22, 0.18) if pieces else 1.0
    values = jax.random.normal(key, extent, jnp.float32) * spread * factor_of
    return jnp.minimum(jnp.maximum(values, -most), most).astype(kind)


def setup_inputs(seed: int = 0) -> dict:
    splits = jax.random.split(jax.random.key(seed), 6)
    query_in = draw_query_in(jax.random.fold_in(splits[5], 71), 0)
    key_in = draw_key_in(jax.random.fold_in(splits[5], 71), 0)
    value_in = noise(splits[2], (TOKENS, D), 1.0, 6.0, ((0, 32),))
    grad_out = noise(splits[3], (TOKENS, D), 1.0, 6.0, ((0, 32),))
    module_lengths = uneven_parts(splits[4], MODULES, TOKENS, PRIOR, 2).astype(jnp.int32)
    return dict(query_in=query_in, key_in=key_in, value_in=value_in, grad_out=grad_out, module_lengths=module_lengths)


def module_ids(module_lengths, positions):
    module_ends = jnp.cumsum(module_lengths)
    counted = jnp.sum((positions[:, None] >= module_ends[None, :]).astype(jnp.int32), axis=1).astype(jnp.int32)
    return jnp.where(positions >= 0, counted, -1)


def allowed_pairs(module_lengths, query_pos, key_pos):
    same = module_ids(module_lengths, query_pos)[:, None] == module_ids(module_lengths, key_pos)[None, :]
    return same & (key_pos[None, :] <= query_pos[:, None])


def attend_block(query_rows, key_block, value_block, grad_rows, allowed, score_scale):
    high = lax.Precision.HIGHEST
    query_f = query_rows.astype(jnp.float32)
    key_f = key_block.astype(jnp.float32)
    value_f = value_block.astype(jnp.float32)
    grad_f = grad_rows.astype(jnp.float32)
    scores = jnp.einsum('qhd,khd->hqk', query_f, key_f, precision=high) * score_scale
    allowed_mask = allowed[None]
    row_top = jnp.max(jnp.where(allowed_mask, scores, -jnp.inf), axis=2, keepdims=True)
    row_total = jnp.sum(jnp.where(allowed_mask, jnp.exp(scores - row_top), 0.0), axis=2, keepdims=True)
    log_total = row_top + jnp.log(row_total)
    weights = jnp.where(allowed_mask, jnp.exp(scores - log_total), 0.0)
    weight_bf = weights.astype(jnp.bfloat16)
    attn_rows = jnp.einsum('hqk,khd->qhd', weight_bf.astype(jnp.float32), value_f, precision=high).astype(jnp.bfloat16)
    row_delta = jnp.transpose(jnp.sum(grad_f * attn_rows.astype(jnp.float32), axis=2))
    dprobs = jnp.einsum('qhd,khd->hqk', grad_f, value_f, precision=high)
    dscores = (weights * (dprobs - row_delta[:, :, None]) * score_scale).astype(jnp.bfloat16)
    dscores_f = dscores.astype(jnp.float32)
    grad_q = jnp.einsum('hqk,khd->qhd', dscores_f, key_f, precision=high).astype(jnp.bfloat16)
    key_grad = jnp.einsum('hqk,qhd->khd', dscores_f, query_f, precision=high)
    value_grad = jnp.einsum('hqk,qhd->khd', weight_bf.astype(jnp.float32), grad_f, precision=high)
    return attn_rows, grad_q, key_grad, value_grad


def reference(query_in, key_in, value_in, grad_out, module_lengths):
    row_count = TOK_DEV * N_HEAD
    prior_rows = row_count // 8
    score_scale = HEAD_DIM ** -0.5

    def to_blocks(whole):
        return whole.reshape(N_SEQ, row_count, HEADS, HEAD_DIM)

    query_b = to_blocks(query_in)
    key_b = to_blocks(key_in)
    value_b = to_blocks(value_in)
    grad_b = to_blocks(grad_out)
    zero_block = jnp.zeros((1, prior_rows, HEADS, HEAD_DIM), key_b.dtype)
    prior_k = jnp.concatenate([zero_block, key_b[:-1, row_count - prior_rows:]], axis=0)
    prior_v = jnp.concatenate([zero_block, value_b[:-1, row_count - prior_rows:]], axis=0)

    def per_block(packed):
        block_idx, query_rows, own_k, own_v, before_k, before_v, grad_rows = packed
        block_start = block_idx * row_count
        query_pos = block_start + jnp.arange(row_count, dtype=jnp.int32)
        before_pos = block_start - prior_rows + jnp.arange(prior_rows, dtype=jnp.int32)
        key_pos = jnp.concatenate([before_pos, query_pos])
        allowed = allowed_pairs(module_lengths, query_pos, key_pos)
        key_block = jnp.concatenate([before_k, own_k], axis=0)
        value_block = jnp.concatenate([before_v, own_v], axis=0)
        return attend_block(query_rows, key_block, value_block, grad_rows, allowed, score_scale)

    block_ids = jnp.arange(N_SEQ, dtype=jnp.int32)
    attn_rows, grad_q, key_grad, value_grad = lax.map(per_block, (block_ids, query_b, key_b, value_b, prior_k, prior_v, grad_b))
    zero_f = jnp.zeros((1, prior_rows, HEADS, HEAD_DIM), jnp.float32)
    later_k = jnp.concatenate([key_grad[1:, :prior_rows], zero_f], axis=0)
    later_v = jnp.concatenate([value_grad[1:, :prior_rows], zero_f], axis=0)
    key_total = key_grad[:, prior_rows:].at[:, row_count - prior_rows:].add(later_k)
    value_total = value_grad[:, prior_rows:].at[:, row_count - prior_rows:].add(later_v)
    return (attn_rows.reshape(TOKENS, D), grad_q.reshape(TOKENS, D),
            key_total.astype(jnp.bfloat16).reshape(TOKENS, D), value_total.astype(jnp.bfloat16).reshape(TOKENS, D))
```

```python
import functools
import math

import jax
import jax.numpy as jnp
from jax import lax
from jax.experimental import pallas as pl
from jax.experimental.pallas import tpu as pltpu
from jax.sharding import PartitionSpec as P

HEAD_DIM = 128
SCALE = HEAD_DIM ** (-0.5)
LOG2E = math.log2(math.e)
MASKED = -1e30


def shifted(value, axis, by):
    peers = lax.axis_size(axis)
    pairs = [(i, i + by) for i in range(peers) if 0 <= i + by < peers]
    return lax.ppermute(value, axis, pairs)


def module_ids(module_lengths, positions):
    module_ends = jnp.cumsum(module_lengths)
    counted = jnp.sum((positions[:, None] >= module_ends[None, :]).astype(jnp.int32), axis=1)
    return jnp.where(positions >= 0, counted, -1)


def allowed_pairs(module_lengths, query_pos, key_pos):
    same = (
        module_ids(module_lengths, query_pos)[:, None]
        == module_ids(module_lengths, key_pos)[None, :]
    )
    return same & (key_pos[None, :] <= query_pos[:, None])


def score_grads(grad_rows, value_block, weights, row_delta, score_scale):
    dprobs = jnp.einsum("qd,kd->qk", grad_rows, value_block, preferred_element_type=jnp.float32)
    return (weights * (dprobs - row_delta[:, None]) * score_scale).astype(jnp.bfloat16)


def key_terms(dscores, weight_bf, query_rows, grad_rows):
    key_grad = jnp.einsum("qk,qd->kd", dscores, query_rows, preferred_element_type=jnp.float32)
    value_grad = jnp.einsum("qk,qd->kd", weight_bf, grad_rows, preferred_element_type=jnp.float32)
    return (key_grad, value_grad)


def one_block(query_rows, key_block, value_block, grad_rows, allowed, score_scale):
    scores = (
        jnp.einsum("qd,kd->qk", query_rows, key_block, preferred_element_type=jnp.float32)
        * score_scale
    )
    row_top = jnp.max(jnp.where(allowed, scores, -jnp.inf), axis=1, keepdims=True)
    row_total = jnp.sum(jnp.where(allowed, jnp.exp(scores - row_top), 0.0), axis=1, keepdims=True)
    log_total = row_top + jnp.log(row_total)
    weights = jnp.where(allowed, jnp.exp(scores - log_total), 0.0)
    weight_bf = weights.astype(jnp.bfloat16)
    attn_rows = jnp.einsum(
        "qk,kd->qd", weight_bf, value_block, preferred_element_type=jnp.float32
    ).astype(jnp.bfloat16)
    row_delta = jnp.sum(grad_rows.astype(jnp.float32) * attn_rows.astype(jnp.float32), axis=1)
    dscores = score_grads(grad_rows, value_block, weights, row_delta, score_scale)
    grad_q = jnp.einsum("qk,kd->qd", dscores, key_block, preferred_element_type=jnp.float32).astype(
        jnp.bfloat16
    )
    key_grad, value_grad = key_terms(dscores, weight_bf, query_rows, grad_rows)
    return (attn_rows, grad_q, key_grad, value_grad, log_total[:, 0], row_delta)


def gathered_shards(query_in, key_in, value_in, grad_out, module_lengths):
    head_q, head_k, head_v, head_do = (
        lax.all_to_all(query_in, "head", split_axis=1, concat_axis=0, tiled=True),
        lax.all_to_all(key_in, "head", split_axis=1, concat_axis=0, tiled=True),
        lax.all_to_all(value_in, "head", split_axis=1, concat_axis=0, tiled=True),
        lax.all_to_all(grad_out, "head", split_axis=1, concat_axis=0, tiled=True),
    )
    row_count = head_q.shape[0]
    width = head_q.shape[1]
    local_heads = width // HEAD_DIM
    prior_rows = row_count // 8
    score_scale = HEAD_DIM ** (-0.5)
    tail_start = row_count - prior_rows
    prior_k, prior_v = shifted((head_k[tail_start:], head_v[tail_start:]), "seq", 1)
    row_start = lax.axis_index("seq") * row_count
    query_pos = row_start + jnp.arange(row_count, dtype=jnp.int32)
    before_pos = row_start - prior_rows + jnp.arange(prior_rows, dtype=jnp.int32)
    key_pos = jnp.concatenate([before_pos, query_pos])
    block_rows = math.gcd(row_count, 512)
    block_count = row_count // block_rows
    pos_blocks = query_pos.reshape(block_count, block_rows)

    def by_head(flat, rows):
        return jnp.moveaxis(flat.reshape(rows, local_heads, HEAD_DIM), 1, 0)

    def to_flat(stacked):
        return jnp.moveaxis(stacked, 0, 1).reshape(stacked.shape[1], width)

    query_h = by_head(head_q, row_count)
    grad_h = by_head(head_do, row_count)
    key_h = by_head(jnp.concatenate([prior_k, head_k], axis=0), row_count + prior_rows)
    value_h = by_head(jnp.concatenate([prior_v, head_v], axis=0), row_count + prior_rows)

    def run_head(packed):
        query_rows, key_block, value_block, grad_rows = packed
        query_blocks = query_rows.reshape(block_count, block_rows, HEAD_DIM)
        grad_blocks = grad_rows.reshape(block_count, block_rows, HEAD_DIM)

        def run_block(inner):
            query_part, grad_part, pos_part = inner
            allowed = allowed_pairs(module_lengths, pos_part, key_pos)
            return one_block(query_part, key_block, value_block, grad_part, allowed, score_scale)

        attn_b, grad_qb, key_b, value_b, lse_b, delta_b = lax.map(
            run_block, (query_blocks, grad_blocks, pos_blocks)
        )
        return (
            attn_b.reshape(row_count, HEAD_DIM),
            grad_qb.reshape(row_count, HEAD_DIM),
            jnp.sum(key_b, axis=0),
            jnp.sum(value_b, axis=0),
            lse_b.reshape(row_count),
            delta_b.reshape(row_count),
        )

    attn_h, grad_qh, key_grad, value_grad, log_total, row_delta = lax.map(
        run_head, (query_h, key_h, value_h, grad_h)
    )
    attn_flat = to_flat(attn_h)
    attn_back = lax.all_to_all(attn_flat, "head", split_axis=0, concat_axis=1, tiled=True)
    grad_q = to_flat(grad_qh)
    later_k, later_v = shifted((key_grad[:, :prior_rows], value_grad[:, :prior_rows]), "seq", -1)
    key_total = key_grad[:, prior_rows:].at[:, tail_start:].add(later_k)
    value_total = value_grad[:, prior_rows:].at[:, tail_start:].add(later_v)
    grad_k = to_flat(key_total.astype(jnp.bfloat16))
    grad_v = to_flat(value_total.astype(jnp.bfloat16))
    back_q, back_k, back_v = (
        lax.all_to_all(grad_q, "head", split_axis=0, concat_axis=1, tiled=True),
        lax.all_to_all(grad_k, "head", split_axis=0, concat_axis=1, tiled=True),
        lax.all_to_all(grad_v, "head", split_axis=0, concat_axis=1, tiled=True),
    )
    return (attn_back, back_q, back_k, back_v)


def dot(left, right, left_dim, right_dim):
    return lax.dot_general(
        left, right, (((left_dim,), (right_dim,)), ((), ())), preferred_element_type=jnp.float32
    )


def module_ends_row(lengths_row):
    count = lengths_row.shape[1]
    row = lax.broadcasted_iota(jnp.int32, (count, count), 0)
    col = lax.broadcasted_iota(jnp.int32, (count, count), 1)
    lengths_col = jnp.sum(jnp.where(row == col, lengths_row, 0.0), axis=1, keepdims=True)
    return jnp.sum(jnp.where(row <= col, lengths_col, 0.0), axis=0, keepdims=True)


def module_ends_col(lengths_row):
    count = lengths_row.shape[1]
    row = lax.broadcasted_iota(jnp.int32, (count, count), 0)
    col = lax.broadcasted_iota(jnp.int32, (count, count), 1)
    return jnp.sum(jnp.where(col <= row, lengths_row, 0.0), axis=1, keepdims=True)


def bias_by_query(lengths_row, first_query, queries, first_key, keys):
    ends = module_ends_row(lengths_row)
    query = (first_query + lax.broadcasted_iota(jnp.int32, (queries, 1), 0)).astype(jnp.float32)
    start = jnp.max(jnp.where(ends <= query, ends, 0.0), axis=1, keepdims=True)
    key = (first_key + lax.broadcasted_iota(jnp.int32, (queries, keys), 1)).astype(jnp.float32)
    return jnp.where((key >= start) & (key <= query), 0.0, MASKED)


def bias_by_key(lengths_row, first_query, queries, first_key, keys):
    ends = module_ends_col(lengths_row)
    query = (first_query + lax.broadcasted_iota(jnp.int32, (1, queries), 1)).astype(jnp.float32)
    start = jnp.max(jnp.where(ends <= query, ends, 0.0), axis=0, keepdims=True)
    key = (first_key + lax.broadcasted_iota(jnp.int32, (keys, queries), 0)).astype(jnp.float32)
    return jnp.where((key >= start) & (key <= query), 0.0, MASKED)


def attend(q, do, k, v, bias):
    scores = dot(q, k, 1, 1) * (SCALE * LOG2E) + bias
    dprobs = dot(do, v, 1, 1)
    top = jnp.max(scores, axis=1, keepdims=True)
    raw = jnp.exp2(scores - top)
    weights = raw * (1.0 / jnp.sum(raw, axis=1, keepdims=True))
    delta = jnp.sum(weights * dprobs, axis=1, keepdims=True)
    dscores = weights * (dprobs - delta) * SCALE
    return weights.astype(jnp.bfloat16), dscores.astype(jnp.bfloat16)


def device_first(tok):
    place = lax.axis_index("seq") * lax.axis_size("head") + lax.axis_index("head")
    return place * tok


def own_kernel(
    prior, len_ref, q_ref, k_ref, v_ref, do_ref,
    attn_ref, gq_ref, gk_ref, gv_ref, stat_ref, bias_ref, lead_ref,
):
    tok, width = q_ref.shape
    rest = tok - prior
    heads = width // HEAD_DIM

    @pl.when(pl.program_id(0) == 0)
    def _():
        first = device_first(tok)
        lengths = len_ref[...].astype(jnp.float32)
        bias_ref[...] = bias_by_query(lengths, first + prior, rest, first, tok)
        lead_ref[...] = bias_by_key(lengths, first, prior, first, prior)

    bias, lead = bias_ref[...], lead_ref[...]
    for h in range(heads):
        cols = slice(h * HEAD_DIM, (h + 1) * HEAD_DIM)
        q, k, v, do = q_ref[:, cols], k_ref[:, cols], v_ref[:, cols], do_ref[:, cols]
        q_late, do_late = q[prior:], do[prior:]
        weights, dscores = attend(q_late, do_late, k, v, bias)
        attn_ref[:, cols] = dot(weights, v, 1, 0).astype(jnp.bfloat16)
        gq_ref[:, cols] = dot(dscores, k, 1, 0).astype(jnp.bfloat16)
        gk_ref[:, cols] = dot(dscores, q_late, 0, 0)
        gv_ref[:, cols] = dot(weights, do_late, 0, 0)
        scores = dot(k[:prior], q[:prior], 1, 1) * (SCALE * LOG2E) + lead
        dprobs = dot(v[:prior], do[:prior], 1, 1)
        top = jnp.max(scores, axis=0, keepdims=True)
        raw = jnp.exp2(scores - top)
        total = jnp.sum(raw, axis=0, keepdims=True)
        stat_ref[0, h : h + 1, :] = top + jnp.log2(total)
        stat_ref[0, heads + h : heads + h + 1, :] = (
            jnp.sum(raw * dprobs, axis=0, keepdims=True) / total
        )


def lead_kernel(
    prior, len_ref, q_ref, k_ref, v_ref, do_ref, before_ref, gk_part_ref, gv_part_ref,
    attn_in, gq_in, attn_ref, gq_ref, gk_ref, gv_ref, bias_ref,
):
    width = q_ref.shape[1]

    @pl.when(pl.program_id(0) == 0)
    def _():
        first = device_first(attn_in.shape[0])
        lengths = len_ref[...].astype(jnp.float32)
        bias_ref[...] = bias_by_query(lengths, first, prior, first - prior, 2 * prior)

    bias = bias_ref[...]
    for h in range(width // HEAD_DIM):
        cols = slice(h * HEAD_DIM, (h + 1) * HEAD_DIM)
        q, do = q_ref[:, cols], do_ref[:, cols]
        k = jnp.concatenate([before_ref[:prior, cols], k_ref[:, cols]], axis=0)
        v = jnp.concatenate([before_ref[prior:, cols], v_ref[:, cols]], axis=0)
        weights, dscores = attend(q, do, k, v, bias)
        attn_ref[:, cols] = dot(weights, v, 1, 0).astype(jnp.bfloat16)
        gq_ref[:, cols] = dot(dscores, k, 1, 0).astype(jnp.bfloat16)
        gk = gk_part_ref[:, cols] + dot(dscores[:, prior:], q, 0, 0)
        gv = gv_part_ref[:, cols] + dot(weights[:, prior:], do, 0, 0)
        gk_ref[:, cols] = gk.astype(jnp.bfloat16)
        gv_ref[:, cols] = gv.astype(jnp.bfloat16)


def tail_kernel(
    prior, len_ref, k_ref, v_ref, after_ref, stat_ref, gk_part_ref, gv_part_ref,
    gk_in, gv_in, gk_ref, gv_ref, bias_ref,
):
    width = k_ref.shape[1]
    heads = width // HEAD_DIM

    @pl.when(pl.program_id(0) == 0)
    def _():
        tok = gk_in.shape[0]
        first = device_first(tok)
        lengths = len_ref[...].astype(jnp.float32)
        bias_ref[...] = bias_by_key(lengths, first + tok, prior, first + tok - prior, prior)

    bias = bias_ref[...]
    for h in range(heads):
        cols = slice(h * HEAD_DIM, (h + 1) * HEAD_DIM)
        q, do = after_ref[:prior, cols], after_ref[prior:, cols]
        own_log = stat_ref[0, h : h + 1, :]
        own_delta = stat_ref[0, heads + h : heads + h + 1, :]
        scores = dot(k_ref[:, cols], q, 1, 1) * (SCALE * LOG2E) + bias
        dprobs = dot(v_ref[:, cols], do, 1, 1)
        top = jnp.maximum(jnp.max(scores, axis=0, keepdims=True), own_log)
        raw = jnp.exp2(scores - top)
        own_raw = jnp.exp2(own_log - top)
        part = 1.0 / (jnp.sum(raw, axis=0, keepdims=True) + own_raw)
        weights = raw * part
        delta = jnp.sum(weights * dprobs, axis=0, keepdims=True) + own_raw * part * own_delta
        dscores = weights * (dprobs - delta) * SCALE
        gk = gk_part_ref[:, cols] + dot(dscores.astype(jnp.bfloat16), q, 1, 0)
        gv = gv_part_ref[:, cols] + dot(weights.astype(jnp.bfloat16), do, 1, 0)
        gk_ref[:, cols] = gk.astype(jnp.bfloat16)
        gv_ref[:, cols] = gv.astype(jnp.bfloat16)


def neighbour(value, by):
    peers = lax.axis_size("seq") * lax.axis_size("head")
    pairs = [(i, i + by) for i in range(peers) if 0 <= i + by < peers]
    return lax.ppermute(value, ("seq", "head"), pairs)


def cost(heads, queries, keys, products, moved):
    return pl.CostEstimate(
        flops=2 * heads * queries * keys * HEAD_DIM * products,
        bytes_accessed=moved,
        transcendentals=heads * queries * keys,
    )


def halo_shards(query_in, key_in, value_in, grad_out, module_lengths):
    tok, width = query_in.shape
    prior = tok * lax.axis_size("head") // 8
    heads = width // HEAD_DIM
    step = 512
    groups = width // step
    per = step // HEAD_DIM
    lengths = module_lengths.reshape(1, -1)
    len_spec = pl.BlockSpec(lengths.shape, lambda g: (0, 0))
    whole = pl.BlockSpec((tok, step), lambda g: (0, g))
    early = pl.BlockSpec((prior, step), lambda g: (0, g))
    late = pl.BlockSpec((prior, step), lambda g: (tok // prior - 1, g))
    pair = pl.BlockSpec((2 * prior, step), lambda g: (0, g))
    stat_spec = pl.BlockSpec((1, 2 * per, prior), lambda g: (g, 0, 0))
    keep = pl.BlockSpec(memory_space=pl.ANY)
    full16 = jax.ShapeDtypeStruct((tok, width), jnp.bfloat16)
    full32 = jax.ShapeDtypeStruct((tok, width), jnp.float32)

    before = neighbour(jnp.concatenate([key_in[tok - prior :], value_in[tok - prior :]]), 1)
    after = neighbour(jnp.concatenate([query_in[:prior], grad_out[:prior]]), -1)

    attn, gq, gk_part, gv_part, stat = pl.pallas_call(
        functools.partial(own_kernel, prior),
        grid=(groups,),
        in_specs=[len_spec, whole, whole, whole, whole],
        out_specs=[late, late, whole, whole, stat_spec],
        out_shape=[
            full16, full16, full32, full32,
            jax.ShapeDtypeStruct((groups, 2 * per, prior), jnp.float32),
        ],
        scratch_shapes=[
            pltpu.VMEM((tok - prior, tok), jnp.float32),
            pltpu.VMEM((prior, prior), jnp.float32),
        ],
        cost_estimate=cost(heads, tok, tok, 4, 24 * tok * width),
        name="own_block",
    )(lengths, query_in, key_in, value_in, grad_out)
    stat_after = neighbour(stat, -1)

    attn, gq, gk, gv = pl.pallas_call(
        functools.partial(lead_kernel, prior),
        grid=(groups,),
        in_specs=[len_spec, early, early, early, early, pair, early, early, keep, keep],
        out_specs=[early, early, early, early],
        out_shape=[full16, full16, full16, full16],
        scratch_shapes=[pltpu.VMEM((prior, 2 * prior), jnp.float32)],
        input_output_aliases={8: 0, 9: 1},
        cost_estimate=cost(heads, prior, 2 * prior, 5, 14 * tok * width),
        name="lead_rows",
    )(lengths, query_in, key_in, value_in, grad_out, before, gk_part, gv_part, attn, gq)

    gk, gv = pl.pallas_call(
        functools.partial(tail_kernel, prior),
        grid=(groups,),
        in_specs=[len_spec, late, late, pair, stat_spec, late, late, keep, keep],
        out_specs=[late, late],
        out_shape=[full16, full16],
        scratch_shapes=[pltpu.VMEM((prior, prior), jnp.float32)],
        input_output_aliases={7: 0, 8: 1},
        cost_estimate=cost(heads, prior, prior, 4, 10 * tok * width),
        name="tail_keys",
    )(lengths, key_in, value_in, after, stat_after, gk_part, gv_part, gk, gv)
    return (attn, gq, gk, gv)


def shards(query_in, key_in, value_in, grad_out, module_lengths):
    tok = query_in.shape[0]
    prior = tok * lax.axis_size("head") // 8
    plan = halo_shards if 2 * prior <= tok else gathered_shards
    return plan(query_in, key_in, value_in, grad_out, module_lengths)


def solution(mesh):
    placed = (
        P(("seq", "head"), None),
        P(("seq", "head"), None),
        P(("seq", "head"), None),
        P(("seq", "head"), None),
        P(),
    )
    return jax.shard_map(
        shards,
        mesh=mesh,
        in_specs=placed,
        out_specs=(
            P(("seq", "head"), None),
            P(("seq", "head"), None),
            P(("seq", "head"), None),
            P(("seq", "head"), None),
        ),
        check_vma=False,
    )
```

```python
import functools
import math

import jax
import jax.numpy as jnp
from jax import lax
from jax.experimental import pallas as pl
from jax.experimental.pallas import tpu as pltpu
from jax.sharding import PartitionSpec as P

HEAD_DIM = 128
SCALE = HEAD_DIM ** (-0.5)
LOG2E = math.log2(math.e)
MASKED = -1e30


def shifted(value, axis, by):
    peers = lax.axis_size(axis)
    pairs = [(i, i + by) for i in range(peers) if 0 <= i + by < peers]
    return lax.ppermute(value, axis, pairs)


def module_ids(module_lengths, positions):
    module_ends = jnp.cumsum(module_lengths)
    counted = jnp.sum((positions[:, None] >= module_ends[None, :]).astype(jnp.int32), axis=1)
    return jnp.where(positions >= 0, counted, -1)


def allowed_pairs(module_lengths, query_pos, key_pos):
    same = (
        module_ids(module_lengths, query_pos)[:, None]
        == module_ids(module_lengths, key_pos)[None, :]
    )
    return same & (key_pos[None, :] <= query_pos[:, None])


def score_grads(grad_rows, value_block, weights, row_delta, score_scale):
    dprobs = jnp.einsum("qd,kd->qk", grad_rows, value_block, preferred_element_type=jnp.float32)
    return (weights * (dprobs - row_delta[:, None]) * score_scale).astype(jnp.bfloat16)


def key_terms(dscores, weight_bf, query_rows, grad_rows):
    key_grad = jnp.einsum("qk,qd->kd", dscores, query_rows, preferred_element_type=jnp.float32)
    value_grad = jnp.einsum("qk,qd->kd", weight_bf, grad_rows, preferred_element_type=jnp.float32)
    return (key_grad, value_grad)


def one_block(query_rows, key_block, value_block, grad_rows, allowed, score_scale):
    scores = (
        jnp.einsum("qd,kd->qk", query_rows, key_block, preferred_element_type=jnp.float32)
        * score_scale
    )
    row_top = jnp.max(jnp.where(allowed, scores, -jnp.inf), axis=1, keepdims=True)
    row_total = jnp.sum(jnp.where(allowed, jnp.exp(scores - row_top), 0.0), axis=1, keepdims=True)
    log_total = row_top + jnp.log(row_total)
    weights = jnp.where(allowed, jnp.exp(scores - log_total), 0.0)
    weight_bf = weights.astype(jnp.bfloat16)
    attn_rows = jnp.einsum(
        "qk,kd->qd", weight_bf, value_block, preferred_element_type=jnp.float32
    ).astype(jnp.bfloat16)
    row_delta = jnp.sum(grad_rows.astype(jnp.float32) * attn_rows.astype(jnp.float32), axis=1)
    dscores = score_grads(grad_rows, value_block, weights, row_delta, score_scale)
    grad_q = jnp.einsum("qk,kd->qd", dscores, key_block, preferred_element_type=jnp.float32).astype(
        jnp.bfloat16
    )
    key_grad, value_grad = key_terms(dscores, weight_bf, query_rows, grad_rows)
    return (attn_rows, grad_q, key_grad, value_grad, log_total[:, 0], row_delta)


def gathered_shards(query_in, key_in, value_in, grad_out, module_lengths):
    head_q, head_k, head_v, head_do = (
        lax.all_to_all(query_in, "head", split_axis=1, concat_axis=0, tiled=True),
        lax.all_to_all(key_in, "head", split_axis=1, concat_axis=0, tiled=True),
        lax.all_to_all(value_in, "head", split_axis=1, concat_axis=0, tiled=True),
        lax.all_to_all(grad_out, "head", split_axis=1, concat_axis=0, tiled=True),
    )
    row_count = head_q.shape[0]
    width = head_q.shape[1]
    local_heads = width // HEAD_DIM
    prior_rows = row_count // 8
    score_scale = HEAD_DIM ** (-0.5)
    tail_start = row_count - prior_rows
    prior_k, prior_v = shifted((head_k[tail_start:], head_v[tail_start:]), "seq", 1)
    row_start = lax.axis_index("seq") * row_count
    query_pos = row_start + jnp.arange(row_count, dtype=jnp.int32)
    before_pos = row_start - prior_rows + jnp.arange(prior_rows, dtype=jnp.int32)
    key_pos = jnp.concatenate([before_pos, query_pos])
    block_rows = math.gcd(row_count, 512)
    block_count = row_count // block_rows
    pos_blocks = query_pos.reshape(block_count, block_rows)

    def by_head(flat, rows):
        return jnp.moveaxis(flat.reshape(rows, local_heads, HEAD_DIM), 1, 0)

    def to_flat(stacked):
        return jnp.moveaxis(stacked, 0, 1).reshape(stacked.shape[1], width)

    query_h = by_head(head_q, row_count)
    grad_h = by_head(head_do, row_count)
    key_h = by_head(jnp.concatenate([prior_k, head_k], axis=0), row_count + prior_rows)
    value_h = by_head(jnp.concatenate([prior_v, head_v], axis=0), row_count + prior_rows)

    def run_head(packed):
        query_rows, key_block, value_block, grad_rows = packed
        query_blocks = query_rows.reshape(block_count, block_rows, HEAD_DIM)
        grad_blocks = grad_rows.reshape(block_count, block_rows, HEAD_DIM)

        def run_block(inner):
            query_part, grad_part, pos_part = inner
            allowed = allowed_pairs(module_lengths, pos_part, key_pos)
            return one_block(query_part, key_block, value_block, grad_part, allowed, score_scale)

        attn_b, grad_qb, key_b, value_b, lse_b, delta_b = lax.map(
            run_block, (query_blocks, grad_blocks, pos_blocks)
        )
        return (
            attn_b.reshape(row_count, HEAD_DIM),
            grad_qb.reshape(row_count, HEAD_DIM),
            jnp.sum(key_b, axis=0),
            jnp.sum(value_b, axis=0),
            lse_b.reshape(row_count),
            delta_b.reshape(row_count),
        )

    attn_h, grad_qh, key_grad, value_grad, log_total, row_delta = lax.map(
        run_head, (query_h, key_h, value_h, grad_h)
    )
    attn_flat = to_flat(attn_h)
    attn_back = lax.all_to_all(attn_flat, "head", split_axis=0, concat_axis=1, tiled=True)
    grad_q = to_flat(grad_qh)
    later_k, later_v = shifted((key_grad[:, :prior_rows], value_grad[:, :prior_rows]), "seq", -1)
    key_total = key_grad[:, prior_rows:].at[:, tail_start:].add(later_k)
    value_total = value_grad[:, prior_rows:].at[:, tail_start:].add(later_v)
    grad_k = to_flat(key_total.astype(jnp.bfloat16))
    grad_v = to_flat(value_total.astype(jnp.bfloat16))
    back_q, back_k, back_v = (
        lax.all_to_all(grad_q, "head", split_axis=0, concat_axis=1, tiled=True),
        lax.all_to_all(grad_k, "head", split_axis=0, concat_axis=1, tiled=True),
        lax.all_to_all(grad_v, "head", split_axis=0, concat_axis=1, tiled=True),
    )
    return (attn_back, back_q, back_k, back_v)


def dot(left, right, left_dim, right_dim):
    return lax.dot_general(
        left, right, (((left_dim,), (right_dim,)), ((), ())), preferred_element_type=jnp.float32
    )


def module_ends_row(lengths_row):
    count = lengths_row.shape[1]
    row = lax.broadcasted_iota(jnp.int32, (count, count), 0)
    col = lax.broadcasted_iota(jnp.int32, (count, count), 1)
    lengths_col = jnp.sum(jnp.where(row == col, lengths_row, 0.0), axis=1, keepdims=True)
    return jnp.sum(jnp.where(row <= col, lengths_col, 0.0), axis=0, keepdims=True)


def module_ends_col(lengths_row):
    count = lengths_row.shape[1]
    row = lax.broadcasted_iota(jnp.int32, (count, count), 0)
    col = lax.broadcasted_iota(jnp.int32, (count, count), 1)
    return jnp.sum(jnp.where(col <= row, lengths_row, 0.0), axis=1, keepdims=True)


def bias_by_query(lengths_row, first_query, queries, first_key, keys):
    ends = module_ends_row(lengths_row)
    query = (first_query + lax.broadcasted_iota(jnp.int32, (queries, 1), 0)).astype(jnp.float32)
    start = jnp.max(jnp.where(ends <= query, ends, 0.0), axis=1, keepdims=True)
    key = (first_key + lax.broadcasted_iota(jnp.int32, (queries, keys), 1)).astype(jnp.float32)
    return jnp.where((key >= start) & (key <= query), 0.0, MASKED)


def bias_by_key(lengths_row, first_query, queries, first_key, keys):
    ends = module_ends_col(lengths_row)
    query = (first_query + lax.broadcasted_iota(jnp.int32, (1, queries), 1)).astype(jnp.float32)
    start = jnp.max(jnp.where(ends <= query, ends, 0.0), axis=0, keepdims=True)
    key = (first_key + lax.broadcasted_iota(jnp.int32, (keys, queries), 0)).astype(jnp.float32)
    return jnp.where((key >= start) & (key <= query), 0.0, MASKED)


def by_query(q, k, do, v, bias):
    scores = dot(q, k, 1, 1) * (SCALE * LOG2E) + bias
    return scores, dot(do, v, 1, 1)


def full_rows(pairs):
    tops = [jnp.max(s, axis=1, keepdims=True) for s, _ in pairs]
    raws = [jnp.exp2(s - top) for (s, _), top in zip(pairs, tops)]
    parts = [1.0 / jnp.sum(raw, axis=1, keepdims=True) for raw in raws]
    weights = [raw * part for raw, part in zip(raws, parts)]
    deltas = [jnp.sum(w * dp, axis=1, keepdims=True) for w, (_, dp) in zip(weights, pairs)]
    grads = [w * (dp - delta) * SCALE for w, (_, dp), delta in zip(weights, pairs, deltas)]
    return [w.astype(jnp.bfloat16) for w in weights], [g.astype(jnp.bfloat16) for g in grads]


def merged_rows(pairs, own):
    tops = [
        jnp.maximum(jnp.max(s, axis=0, keepdims=True), log) for (s, _), (log, _) in zip(pairs, own)
    ]
    raws = [jnp.exp2(s - top) for (s, _), top in zip(pairs, tops)]
    own_raws = [jnp.exp2(log - top) for (log, _), top in zip(own, tops)]
    parts = [
        1.0 / (jnp.sum(raw, axis=0, keepdims=True) + own_raw)
        for raw, own_raw in zip(raws, own_raws)
    ]
    weights = [raw * part for raw, part in zip(raws, parts)]
    deltas = [
        jnp.sum(w * dp, axis=0, keepdims=True) + own_raw * part * own_delta
        for w, (_, dp), own_raw, part, (_, own_delta) in zip(weights, pairs, own_raws, parts, own)
    ]
    grads = [w * (dp - delta) * SCALE for w, (_, dp), delta in zip(weights, pairs, deltas)]
    return [w.astype(jnp.bfloat16) for w in weights], [g.astype(jnp.bfloat16) for g in grads]


def head_columns(width):
    return [slice(c, c + HEAD_DIM) for c in range(0, width, HEAD_DIM)]


def device_first(tok):
    place = lax.axis_index("seq") * lax.axis_size("head") + lax.axis_index("head")
    return place * tok


def own_kernel(
    prior, len_ref, q_ref, k_ref, v_ref, do_ref,
    attn_ref, gq_ref, gk_ref, gv_ref, stat_ref, bias_ref, lead_ref,
):
    tok, width = q_ref.shape
    rest = tok - prior
    columns = head_columns(width)
    heads = len(columns)

    @pl.when(pl.program_id(0) == 0)
    def _():
        first = device_first(tok)
        lengths = len_ref[...].astype(jnp.float32)
        bias_ref[...] = bias_by_query(lengths, first + prior, rest, first, tok)
        lead_ref[...] = bias_by_key(lengths, first, prior, first, prior)

    bias, lead = bias_ref[...], lead_ref[...]
    late = slice(prior, tok)
    early = slice(0, prior)
    pairs = [
        by_query(q_ref[late, c], k_ref[:, c], do_ref[late, c], v_ref[:, c], bias) for c in columns
    ]
    leads = [
        by_query(k_ref[early, c], q_ref[early, c], v_ref[early, c], do_ref[early, c], lead)
        for c in columns
    ]
    weights, grads = full_rows(pairs)
    for c, w, g in zip(columns, weights, grads):
        attn_ref[:, c] = dot(w, v_ref[:, c], 1, 0).astype(jnp.bfloat16)
        gq_ref[:, c] = dot(g, k_ref[:, c], 1, 0).astype(jnp.bfloat16)
        gk_ref[:, c] = dot(g, q_ref[late, c], 0, 0)
        gv_ref[:, c] = dot(w, do_ref[late, c], 0, 0)
    tops = [jnp.max(s, axis=0, keepdims=True) for s, _ in leads]
    raws = [jnp.exp2(s - top) for (s, _), top in zip(leads, tops)]
    totals = [jnp.sum(raw, axis=0, keepdims=True) for raw in raws]
    sums = [jnp.sum(raw * dp, axis=0, keepdims=True) for raw, (_, dp) in zip(raws, leads)]
    for h in range(heads):
        stat_ref[0, h : h + 1, :] = tops[h] + jnp.log2(totals[h])
        stat_ref[0, heads + h : heads + h + 1, :] = sums[h] / totals[h]


def edge_kernel(
    prior, len_ref, q_ref, k_ref, v_ref, do_ref, before_ref, after_ref, stat_ref,
    gk_part_ref, gv_part_ref, *refs,
):
    attn_ref, gq_ref, gk_ref, gv_ref, bias_ref, tail_ref = refs[-6:]
    tok, width = k_ref.shape
    columns = head_columns(width)
    heads = len(columns)

    @pl.when(pl.program_id(0) == 0)
    def _():
        first = device_first(tok)
        lengths = len_ref[...].astype(jnp.float32)
        bias_ref[...] = bias_by_query(lengths, first, prior, first - prior, 2 * prior)
        tail_ref[...] = bias_by_key(lengths, first + tok, prior, first + tok - prior, prior)

    bias, tail = bias_ref[...], tail_ref[...]
    early, late = slice(0, prior), slice(tok - prior, tok)
    second = slice(prior, 2 * prior)
    keys = [jnp.concatenate([before_ref[early, c], k_ref[early, c]], axis=0) for c in columns]
    values = [jnp.concatenate([before_ref[second, c], v_ref[early, c]], axis=0) for c in columns]
    leads = [
        by_query(q_ref[:, c], k, do_ref[:, c], v, bias) for c, k, v in zip(columns, keys, values)
    ]
    tails = [
        by_query(k_ref[late, c], after_ref[early, c], v_ref[late, c], after_ref[second, c], tail)
        for c in columns
    ]
    own = [
        (stat_ref[0, h : h + 1, :], stat_ref[0, heads + h : heads + h + 1, :])
        for h in range(heads)
    ]
    weights, grads = full_rows(leads)
    tail_weights, tail_grads = merged_rows(tails, own)
    for c, w, g, k, v in zip(columns, weights, grads, keys, values):
        attn_ref[:, c] = dot(w, v, 1, 0).astype(jnp.bfloat16)
        gq_ref[:, c] = dot(g, k, 1, 0).astype(jnp.bfloat16)
        gk = gk_part_ref[early, c] + dot(g[:, second], q_ref[:, c], 0, 0)
        gv = gv_part_ref[early, c] + dot(w[:, second], do_ref[:, c], 0, 0)
        gk_ref[early, c] = gk.astype(jnp.bfloat16)
        gv_ref[early, c] = gv.astype(jnp.bfloat16)
    for c, w, g in zip(columns, tail_weights, tail_grads):
        gk = gk_part_ref[late, c] + dot(g, after_ref[early, c], 1, 0)
        gv = gv_part_ref[late, c] + dot(w, after_ref[second, c], 1, 0)
        gk_ref[late, c] = gk.astype(jnp.bfloat16)
        gv_ref[late, c] = gv.astype(jnp.bfloat16)


def neighbour(value, by):
    peers = lax.axis_size("seq") * lax.axis_size("head")
    pairs = [(i, i + by) for i in range(peers) if 0 <= i + by < peers]
    return lax.ppermute(value, ("seq", "head"), pairs)


def cost(heads, queries, keys, products, moved):
    return pl.CostEstimate(
        flops=2 * heads * queries * keys * HEAD_DIM * products,
        bytes_accessed=moved,
        transcendentals=heads * queries * keys,
    )


def halo_shards(query_in, key_in, value_in, grad_out, module_lengths):
    tok, width = query_in.shape
    prior = tok * lax.axis_size("head") // 8
    heads = width // HEAD_DIM
    step = min(width, 4 * HEAD_DIM)
    groups = width // step
    per = step // HEAD_DIM
    lengths = module_lengths.reshape(1, -1)
    len_spec = pl.BlockSpec(lengths.shape, lambda g: (0, 0))
    keep = pl.BlockSpec(memory_space=pl.ANY)
    full16 = jax.ShapeDtypeStruct((tok, width), jnp.bfloat16)
    full32 = jax.ShapeDtypeStruct((tok, width), jnp.float32)

    def rows(count, at, base=0):
        return pl.BlockSpec((count, step), lambda g: (at, g + base))

    def stats(base=0):
        return pl.BlockSpec((1, 2 * per, prior), lambda g: (g + base, 0, 0))

    def halos(cols, after=None):
        k, v = key_in[tok - prior :, cols], value_in[tok - prior :, cols]
        q, do = query_in[:prior, cols], grad_out[:prior, cols]
        if after is not None:
            k, v, q, do, _ = lax.optimization_barrier((k, v, q, do, after))
        return neighbour(jnp.concatenate([k, v]), 1), neighbour(jnp.concatenate([q, do]), -1)

    cuts = [0, groups // 2, groups] if groups > 1 else [0, groups]
    spans = list(zip(cuts[:-1], cuts[1:]))
    moved = [halos(slice(spans[0][0] * step, spans[0][1] * step))]

    attn, gq, gk_part, gv_part, stat = pl.pallas_call(
        functools.partial(own_kernel, prior),
        grid=(groups,),
        in_specs=[len_spec, rows(tok, 0), rows(tok, 0), rows(tok, 0), rows(tok, 0)],
        out_specs=[
            rows(prior, tok // prior - 1), rows(prior, tok // prior - 1),
            rows(tok, 0), rows(tok, 0), stats(),
        ],
        out_shape=[
            full16, full16, full32, full32,
            jax.ShapeDtypeStruct((groups, 2 * per, prior), jnp.float32),
        ],
        scratch_shapes=[
            pltpu.VMEM((tok - prior, tok), jnp.float32),
            pltpu.VMEM((prior, prior), jnp.float32),
        ],
        cost_estimate=cost(heads, tok, tok, 4, 24 * tok * width),
        name="own_block",
    )(lengths, query_in, key_in, value_in, grad_out)
    stat_after = neighbour(stat, -1)
    for low, high in spans[1:]:
        moved.append(halos(slice(low * step, high * step), stat))

    outs = [attn, gq]
    for (low, high), (before, after) in zip(spans, moved):
        outs = pl.pallas_call(
            functools.partial(edge_kernel, prior),
            grid=(high - low,),
            in_specs=[
                len_spec, rows(prior, 0, low), rows(tok, 0, low), rows(tok, 0, low),
                rows(prior, 0, low), rows(2 * prior, 0), rows(2 * prior, 0), stats(low),
                rows(tok, 0, low), rows(tok, 0, low), *[keep] * len(outs),
            ],
            out_specs=[
                rows(prior, 0, low), rows(prior, 0, low), rows(tok, 0, low), rows(tok, 0, low),
            ],
            out_shape=[full16] * 4,
            scratch_shapes=[
                pltpu.VMEM((prior, 2 * prior), jnp.float32),
                pltpu.VMEM((prior, prior), jnp.float32),
            ],
            input_output_aliases={10 + i: i for i in range(len(outs))},
            cost_estimate=cost(
                (high - low) * per, prior, 2 * prior, 7, 20 * tok * step * (high - low)
            ),
            name="edges",
        )(
            lengths, query_in, key_in, value_in, grad_out, before, after, stat_after,
            gk_part, gv_part, *outs,
        )
    return tuple(outs)


def shards(query_in, key_in, value_in, grad_out, module_lengths):
    tok = query_in.shape[0]
    prior = tok * lax.axis_size("head") // 8
    plan = halo_shards if 2 * prior <= tok else gathered_shards
    return plan(query_in, key_in, value_in, grad_out, module_lengths)


def solution(mesh):
    placed = (
        P(("seq", "head"), None),
        P(("seq", "head"), None),
        P(("seq", "head"), None),
        P(("seq", "head"), None),
        P(),
    )
    return jax.shard_map(
        shards,
        mesh=mesh,
        in_specs=placed,
        out_specs=(
            P(("seq", "head"), None),
            P(("seq", "head"), None),
            P(("seq", "head"), None),
            P(("seq", "head"), None),
        ),
        check_vma=False,
    )
```

```python
import functools
import math

import jax
import jax.numpy as jnp
from jax import lax
from jax.experimental import pallas as pl
from jax.experimental.pallas import tpu as pltpu
from jax.sharding import PartitionSpec as P

HEAD_DIM = 128
SCALE = HEAD_DIM ** (-0.5)
LOG2E = math.log2(math.e)
MASKED = -1e30


def shifted(value, axis, by):
    peers = lax.axis_size(axis)
    pairs = [(i, i + by) for i in range(peers) if 0 <= i + by < peers]
    return lax.ppermute(value, axis, pairs)


def module_ids(module_lengths, positions):
    module_ends = jnp.cumsum(module_lengths)
    counted = jnp.sum((positions[:, None] >= module_ends[None, :]).astype(jnp.int32), axis=1)
    return jnp.where(positions >= 0, counted, -1)


def allowed_pairs(module_lengths, query_pos, key_pos):
    same = (
        module_ids(module_lengths, query_pos)[:, None]
        == module_ids(module_lengths, key_pos)[None, :]
    )
    return same & (key_pos[None, :] <= query_pos[:, None])


def score_grads(grad_rows, value_block, weights, row_delta, score_scale):
    dprobs = jnp.einsum("qd,kd->qk", grad_rows, value_block, preferred_element_type=jnp.float32)
    return (weights * (dprobs - row_delta[:, None]) * score_scale).astype(jnp.bfloat16)


def key_terms(dscores, weight_bf, query_rows, grad_rows):
    key_grad = jnp.einsum("qk,qd->kd", dscores, query_rows, preferred_element_type=jnp.float32)
    value_grad = jnp.einsum("qk,qd->kd", weight_bf, grad_rows, preferred_element_type=jnp.float32)
    return (key_grad, value_grad)


def one_block(query_rows, key_block, value_block, grad_rows, allowed, score_scale):
    scores = (
        jnp.einsum("qd,kd->qk", query_rows, key_block, preferred_element_type=jnp.float32)
        * score_scale
    )
    row_top = jnp.max(jnp.where(allowed, scores, -jnp.inf), axis=1, keepdims=True)
    row_total = jnp.sum(jnp.where(allowed, jnp.exp(scores - row_top), 0.0), axis=1, keepdims=True)
    log_total = row_top + jnp.log(row_total)
    weights = jnp.where(allowed, jnp.exp(scores - log_total), 0.0)
    weight_bf = weights.astype(jnp.bfloat16)
    attn_rows = jnp.einsum(
        "qk,kd->qd", weight_bf, value_block, preferred_element_type=jnp.float32
    ).astype(jnp.bfloat16)
    row_delta = jnp.sum(grad_rows.astype(jnp.float32) * attn_rows.astype(jnp.float32), axis=1)
    dscores = score_grads(grad_rows, value_block, weights, row_delta, score_scale)
    grad_q = jnp.einsum("qk,kd->qd", dscores, key_block, preferred_element_type=jnp.float32).astype(
        jnp.bfloat16
    )
    key_grad, value_grad = key_terms(dscores, weight_bf, query_rows, grad_rows)
    return (attn_rows, grad_q, key_grad, value_grad, log_total[:, 0], row_delta)


def gathered_shards(query_in, key_in, value_in, grad_out, module_lengths):
    head_q, head_k, head_v, head_do = (
        lax.all_to_all(query_in, "head", split_axis=1, concat_axis=0, tiled=True),
        lax.all_to_all(key_in, "head", split_axis=1, concat_axis=0, tiled=True),
        lax.all_to_all(value_in, "head", split_axis=1, concat_axis=0, tiled=True),
        lax.all_to_all(grad_out, "head", split_axis=1, concat_axis=0, tiled=True),
    )
    row_count = head_q.shape[0]
    width = head_q.shape[1]
    local_heads = width // HEAD_DIM
    prior_rows = row_count // 8
    score_scale = HEAD_DIM ** (-0.5)
    tail_start = row_count - prior_rows
    prior_k, prior_v = shifted((head_k[tail_start:], head_v[tail_start:]), "seq", 1)
    row_start = lax.axis_index("seq") * row_count
    query_pos = row_start + jnp.arange(row_count, dtype=jnp.int32)
    before_pos = row_start - prior_rows + jnp.arange(prior_rows, dtype=jnp.int32)
    key_pos = jnp.concatenate([before_pos, query_pos])
    block_rows = math.gcd(row_count, 512)
    block_count = row_count // block_rows
    pos_blocks = query_pos.reshape(block_count, block_rows)

    def by_head(flat, rows):
        return jnp.moveaxis(flat.reshape(rows, local_heads, HEAD_DIM), 1, 0)

    def to_flat(stacked):
        return jnp.moveaxis(stacked, 0, 1).reshape(stacked.shape[1], width)

    query_h = by_head(head_q, row_count)
    grad_h = by_head(head_do, row_count)
    key_h = by_head(jnp.concatenate([prior_k, head_k], axis=0), row_count + prior_rows)
    value_h = by_head(jnp.concatenate([prior_v, head_v], axis=0), row_count + prior_rows)

    def run_head(packed):
        query_rows, key_block, value_block, grad_rows = packed
        query_blocks = query_rows.reshape(block_count, block_rows, HEAD_DIM)
        grad_blocks = grad_rows.reshape(block_count, block_rows, HEAD_DIM)

        def run_block(inner):
            query_part, grad_part, pos_part = inner
            allowed = allowed_pairs(module_lengths, pos_part, key_pos)
            return one_block(query_part, key_block, value_block, grad_part, allowed, score_scale)

        attn_b, grad_qb, key_b, value_b, lse_b, delta_b = lax.map(
            run_block, (query_blocks, grad_blocks, pos_blocks)
        )
        return (
            attn_b.reshape(row_count, HEAD_DIM),
            grad_qb.reshape(row_count, HEAD_DIM),
            jnp.sum(key_b, axis=0),
            jnp.sum(value_b, axis=0),
            lse_b.reshape(row_count),
            delta_b.reshape(row_count),
        )

    attn_h, grad_qh, key_grad, value_grad, log_total, row_delta = lax.map(
        run_head, (query_h, key_h, value_h, grad_h)
    )
    attn_flat = to_flat(attn_h)
    attn_back = lax.all_to_all(attn_flat, "head", split_axis=0, concat_axis=1, tiled=True)
    grad_q = to_flat(grad_qh)
    later_k, later_v = shifted((key_grad[:, :prior_rows], value_grad[:, :prior_rows]), "seq", -1)
    key_total = key_grad[:, prior_rows:].at[:, tail_start:].add(later_k)
    value_total = value_grad[:, prior_rows:].at[:, tail_start:].add(later_v)
    grad_k = to_flat(key_total.astype(jnp.bfloat16))
    grad_v = to_flat(value_total.astype(jnp.bfloat16))
    back_q, back_k, back_v = (
        lax.all_to_all(grad_q, "head", split_axis=0, concat_axis=1, tiled=True),
        lax.all_to_all(grad_k, "head", split_axis=0, concat_axis=1, tiled=True),
        lax.all_to_all(grad_v, "head", split_axis=0, concat_axis=1, tiled=True),
    )
    return (attn_back, back_q, back_k, back_v)


def dot(left, right, left_dim, right_dim):
    return lax.dot_general(
        left, right, (((left_dim,), (right_dim,)), ((), ())), preferred_element_type=jnp.float32
    )


def module_ends_row(lengths_row):
    count = lengths_row.shape[1]
    row = lax.broadcasted_iota(jnp.int32, (count, count), 0)
    col = lax.broadcasted_iota(jnp.int32, (count, count), 1)
    lengths_col = jnp.sum(jnp.where(row == col, lengths_row, 0.0), axis=1, keepdims=True)
    return jnp.sum(jnp.where(row <= col, lengths_col, 0.0), axis=0, keepdims=True)


def module_ends_col(lengths_row):
    count = lengths_row.shape[1]
    row = lax.broadcasted_iota(jnp.int32, (count, count), 0)
    col = lax.broadcasted_iota(jnp.int32, (count, count), 1)
    return jnp.sum(jnp.where(col <= row, lengths_row, 0.0), axis=1, keepdims=True)


def bias_by_query(lengths_row, first_query, queries, first_key, keys):
    ends = module_ends_row(lengths_row)
    query = (first_query + lax.broadcasted_iota(jnp.int32, (queries, 1), 0)).astype(jnp.float32)
    start = jnp.max(jnp.where(ends <= query, ends, 0.0), axis=1, keepdims=True)
    key = (first_key + lax.broadcasted_iota(jnp.int32, (queries, keys), 1)).astype(jnp.float32)
    return jnp.where((key >= start) & (key <= query), 0.0, MASKED)


def bias_by_key(lengths_row, first_query, queries, first_key, keys):
    ends = module_ends_col(lengths_row)
    query = (first_query + lax.broadcasted_iota(jnp.int32, (1, queries), 1)).astype(jnp.float32)
    start = jnp.max(jnp.where(ends <= query, ends, 0.0), axis=0, keepdims=True)
    key = (first_key + lax.broadcasted_iota(jnp.int32, (keys, queries), 0)).astype(jnp.float32)
    return jnp.where((key >= start) & (key <= query), 0.0, MASKED)


def by_query(q, k, do, v, bias):
    scores = dot(q, k, 1, 1) * (SCALE * LOG2E) + bias
    return scores, dot(do, v, 1, 1)


def full_rows(pairs):
    tops = [jnp.max(s, axis=1, keepdims=True) for s, _ in pairs]
    raws = [jnp.exp2(s - top) for (s, _), top in zip(pairs, tops)]
    parts = [1.0 / jnp.sum(raw, axis=1, keepdims=True) for raw in raws]
    weights = [raw * part for raw, part in zip(raws, parts)]
    deltas = [jnp.sum(w * dp, axis=1, keepdims=True) for w, (_, dp) in zip(weights, pairs)]
    grads = [w * (dp - delta) * SCALE for w, (_, dp), delta in zip(weights, pairs, deltas)]
    return [w.astype(jnp.bfloat16) for w in weights], [g.astype(jnp.bfloat16) for g in grads]


def merged_rows(pairs, own):
    tops = [
        jnp.maximum(jnp.max(s, axis=0, keepdims=True), log) for (s, _), (log, _) in zip(pairs, own)
    ]
    raws = [jnp.exp2(s - top) for (s, _), top in zip(pairs, tops)]
    own_raws = [jnp.exp2(log - top) for (log, _), top in zip(own, tops)]
    parts = [
        1.0 / (jnp.sum(raw, axis=0, keepdims=True) + own_raw)
        for raw, own_raw in zip(raws, own_raws)
    ]
    weights = [raw * part for raw, part in zip(raws, parts)]
    deltas = [
        jnp.sum(w * dp, axis=0, keepdims=True) + own_raw * part * own_delta
        for w, (_, dp), own_raw, part, (_, own_delta) in zip(weights, pairs, own_raws, parts, own)
    ]
    grads = [w * (dp - delta) * SCALE for w, (_, dp), delta in zip(weights, pairs, deltas)]
    return [w.astype(jnp.bfloat16) for w in weights], [g.astype(jnp.bfloat16) for g in grads]


def head_columns(width):
    return [slice(c, c + HEAD_DIM) for c in range(0, width, HEAD_DIM)]


def device_first(tok):
    place = lax.axis_index("seq") * lax.axis_size("head") + lax.axis_index("head")
    return place * tok


def own_kernel(
    prior, len_ref, q_ref, k_ref, v_ref, do_ref,
    attn_ref, gq_ref, gk_ref, gv_ref, stat_ref, bias_ref, lead_ref,
):
    tok, width = q_ref.shape
    rest = tok - prior
    columns = head_columns(width)
    heads = len(columns)

    @pl.when(pl.program_id(0) == 0)
    def _():
        first = device_first(tok)
        lengths = len_ref[...].astype(jnp.float32)
        bias_ref[...] = bias_by_query(lengths, first + prior, rest, first, tok)
        lead_ref[...] = bias_by_key(lengths, first, prior, first, prior)

    bias, lead = bias_ref[...], lead_ref[...]
    late = slice(prior, tok)
    early = slice(0, prior)
    pairs = [
        by_query(q_ref[late, c], k_ref[:, c], do_ref[late, c], v_ref[:, c], bias) for c in columns
    ]
    leads = [
        by_query(k_ref[early, c], q_ref[early, c], v_ref[early, c], do_ref[early, c], lead)
        for c in columns
    ]
    weights, grads = full_rows(pairs)
    for c, w, g in zip(columns, weights, grads):
        attn_ref[:, c] = dot(w, v_ref[:, c], 1, 0).astype(jnp.bfloat16)
        gq_ref[:, c] = dot(g, k_ref[:, c], 1, 0).astype(jnp.bfloat16)
        gk_ref[:, c] = dot(g, q_ref[late, c], 0, 0)
        gv_ref[:, c] = dot(w, do_ref[late, c], 0, 0)
    tops = [jnp.max(s, axis=0, keepdims=True) for s, _ in leads]
    raws = [jnp.exp2(s - top) for (s, _), top in zip(leads, tops)]
    totals = [jnp.sum(raw, axis=0, keepdims=True) for raw in raws]
    sums = [jnp.sum(raw * dp, axis=0, keepdims=True) for raw, (_, dp) in zip(raws, leads)]
    for h in range(heads):
        stat_ref[0, h : h + 1, :] = tops[h] + jnp.log2(totals[h])
        stat_ref[0, heads + h : heads + h + 1, :] = sums[h] / totals[h]


def edge_kernel(
    prior, odd_ref, len_ref, q_ref, k_ref, v_ref, do_ref, even_pair_ref, odd_pair_ref, stat_ref,
    gk_part_ref, gv_part_ref, *refs,
):
    attn_ref, gq_ref, gk_ref, gv_ref, bias_ref, tail_ref, before_ref, after_ref = refs[-8:]
    tok, width = k_ref.shape
    columns = head_columns(width)
    heads = len(columns)

    @pl.when(pl.program_id(0) == 0)
    def _():
        first = device_first(tok)
        lengths = len_ref[...].astype(jnp.float32)
        bias_ref[...] = bias_by_query(lengths, first, prior, first - prior, 2 * prior)
        tail_ref[...] = bias_by_key(lengths, first + tok, prior, first + tok - prior, prior)

    odd = odd_ref[0] == 1
    before_ref[...] = jnp.where(odd, even_pair_ref[0], odd_pair_ref[0])
    after_ref[...] = jnp.where(odd, odd_pair_ref[0], even_pair_ref[0])
    bias, tail = bias_ref[...], tail_ref[...]
    early, late = slice(0, prior), slice(tok - prior, tok)
    second = slice(prior, 2 * prior)
    keys = [jnp.concatenate([before_ref[early, c], k_ref[early, c]], axis=0) for c in columns]
    values = [jnp.concatenate([before_ref[second, c], v_ref[early, c]], axis=0) for c in columns]
    leads = [
        by_query(q_ref[:, c], k, do_ref[:, c], v, bias) for c, k, v in zip(columns, keys, values)
    ]
    tails = [
        by_query(k_ref[late, c], after_ref[early, c], v_ref[late, c], after_ref[second, c], tail)
        for c in columns
    ]
    own = [
        (stat_ref[0, h : h + 1, :], stat_ref[0, heads + h : heads + h + 1, :])
        for h in range(heads)
    ]
    weights, grads = full_rows(leads)
    tail_weights, tail_grads = merged_rows(tails, own)
    for c, w, g, k, v in zip(columns, weights, grads, keys, values):
        attn_ref[:, c] = dot(w, v, 1, 0).astype(jnp.bfloat16)
        gq_ref[:, c] = dot(g, k, 1, 0).astype(jnp.bfloat16)
        gk = gk_part_ref[early, c] + dot(g[:, second], q_ref[:, c], 0, 0)
        gv = gv_part_ref[early, c] + dot(w[:, second], do_ref[:, c], 0, 0)
        gk_ref[early, c] = gk.astype(jnp.bfloat16)
        gv_ref[early, c] = gv.astype(jnp.bfloat16)
    for c, w, g in zip(columns, tail_weights, tail_grads):
        gk = gk_part_ref[late, c] + dot(g, after_ref[early, c], 1, 0)
        gv = gv_part_ref[late, c] + dot(w, after_ref[second, c], 1, 0)
        gk_ref[late, c] = gk.astype(jnp.bfloat16)
        gv_ref[late, c] = gv.astype(jnp.bfloat16)


def neighbour(value, by):
    peers = lax.axis_size("seq") * lax.axis_size("head")
    pairs = [(i, i + by) for i in range(peers) if 0 <= i + by < peers]
    return lax.ppermute(value, ("seq", "head"), pairs)


def cost(heads, queries, keys, products, moved):
    return pl.CostEstimate(
        flops=2 * heads * queries * keys * HEAD_DIM * products,
        bytes_accessed=moved,
        transcendentals=heads * queries * keys,
    )


def halo_shards(query_in, key_in, value_in, grad_out, module_lengths):
    tok, width = query_in.shape
    prior = tok * lax.axis_size("head") // 8
    heads = width // HEAD_DIM
    step = min(width, 4 * HEAD_DIM)
    groups = width // step
    per = step // HEAD_DIM
    lengths = module_lengths.reshape(1, -1)
    len_spec = pl.BlockSpec(lengths.shape, lambda g, *_: (0, 0))
    keep = pl.BlockSpec(memory_space=pl.ANY)
    full16 = jax.ShapeDtypeStruct((tok, width), jnp.bfloat16)
    full32 = jax.ShapeDtypeStruct((tok, width), jnp.float32)

    def rows(count, at):
        return pl.BlockSpec((count, step), lambda g, *_: (at, g))

    stats = pl.BlockSpec((1, 2 * per, prior), lambda g, *_: (g, 0, 0))

    peers = lax.axis_size("seq") * lax.axis_size("head")
    odd = lax.axis_index("head") % 2
    late_kv = jnp.concatenate([key_in[tok - prior :], value_in[tok - prior :]])
    early_qd = jnp.concatenate([query_in[:prior], grad_out[:prior]])
    even_pairs = [[i, i + 1] for i in range(0, peers, 2)]
    odd_pairs = [[i, (i + 1) % peers] for i in range(1, peers, 2)]
    even_gather = lax.all_gather(
        jnp.where(odd == 0, late_kv, early_qd), ("seq", "head"), axis_index_groups=even_pairs
    )
    odd_gather = lax.all_gather(
        jnp.where(odd == 0, early_qd, late_kv), ("seq", "head"), axis_index_groups=odd_pairs
    )

    attn, gq, gk_part, gv_part, stat = pl.pallas_call(
        functools.partial(own_kernel, prior),
        grid=(groups,),
        in_specs=[len_spec, rows(tok, 0), rows(tok, 0), rows(tok, 0), rows(tok, 0)],
        out_specs=[
            rows(prior, tok // prior - 1), rows(prior, tok // prior - 1),
            rows(tok, 0), rows(tok, 0), stats,
        ],
        out_shape=[
            full16, full16, full32, full32,
            jax.ShapeDtypeStruct((groups, 2 * per, prior), jnp.float32),
        ],
        scratch_shapes=[
            pltpu.VMEM((tok - prior, tok), jnp.float32),
            pltpu.VMEM((prior, prior), jnp.float32),
        ],
        cost_estimate=cost(heads, tok, tok, 4, 24 * tok * width),
        name="own_block",
    )(lengths, query_in, key_in, value_in, grad_out)
    stat_after = neighbour(stat, -1)

    return pl.pallas_call(
        functools.partial(edge_kernel, prior),
        grid_spec=pltpu.PrefetchScalarGridSpec(
            num_scalar_prefetch=1,
            grid=(groups,),
            in_specs=[
                len_spec, rows(prior, 0), rows(tok, 0), rows(tok, 0), rows(prior, 0),
                pl.BlockSpec((1, 2 * prior, step), lambda g, odd: (1 - odd[0], 0, g)),
                pl.BlockSpec((1, 2 * prior, step), lambda g, odd: (odd[0], 0, g)),
                stats, rows(tok, 0), rows(tok, 0), keep, keep,
            ],
            out_specs=[rows(prior, 0), rows(prior, 0), rows(tok, 0), rows(tok, 0)],
            scratch_shapes=[
                pltpu.VMEM((prior, 2 * prior), jnp.float32),
                pltpu.VMEM((prior, prior), jnp.float32),
                pltpu.VMEM((2 * prior, step), jnp.bfloat16),
                pltpu.VMEM((2 * prior, step), jnp.bfloat16),
            ],
        ),
        out_shape=[full16] * 4,
        input_output_aliases={11: 0, 12: 1},
        cost_estimate=cost(heads, prior, 2 * prior, 7, 20 * tok * width),
        name="edges",
    )(
        odd.astype(jnp.int32).reshape(1), lengths, query_in, key_in, value_in, grad_out,
        even_gather, odd_gather, stat_after, gk_part, gv_part, attn, gq,
    )


def shards(query_in, key_in, value_in, grad_out, module_lengths):
    tok = query_in.shape[0]
    prior = tok * lax.axis_size("head") // 8
    plan = halo_shards if 2 * prior <= tok else gathered_shards
    return plan(query_in, key_in, value_in, grad_out, module_lengths)


def solution(mesh):
    placed = (
        P(("seq", "head"), None),
        P(("seq", "head"), None),
        P(("seq", "head"), None),
        P(("seq", "head"), None),
        P(),
    )
    return jax.shard_map(
        shards,
        mesh=mesh,
        in_specs=placed,
        out_specs=(
            P(("seq", "head"), None),
            P(("seq", "head"), None),
            P(("seq", "head"), None),
            P(("seq", "head"), None),
        ),
        check_vma=False,
    )
```

```python
import functools
import math

import jax
import jax.numpy as jnp
from jax import lax
from jax.experimental import pallas as pl
from jax.experimental.pallas import tpu as pltpu
from jax.sharding import PartitionSpec as P

HEAD_DIM = 128
SCALE = HEAD_DIM ** (-0.5)
LOG2E = math.log2(math.e)
MASKED = -1e30
STAT_ROWS = 16


def shifted(value, axis, by):
    peers = lax.axis_size(axis)
    pairs = [(i, i + by) for i in range(peers) if 0 <= i + by < peers]
    return lax.ppermute(value, axis, pairs)


def module_ids(module_lengths, positions):
    module_ends = jnp.cumsum(module_lengths)
    counted = jnp.sum((positions[:, None] >= module_ends[None, :]).astype(jnp.int32), axis=1)
    return jnp.where(positions >= 0, counted, -1)


def allowed_pairs(module_lengths, query_pos, key_pos):
    same = (
        module_ids(module_lengths, query_pos)[:, None]
        == module_ids(module_lengths, key_pos)[None, :]
    )
    return same & (key_pos[None, :] <= query_pos[:, None])


def score_grads(grad_rows, value_block, weights, row_delta, score_scale):
    dprobs = jnp.einsum("qd,kd->qk", grad_rows, value_block, preferred_element_type=jnp.float32)
    return (weights * (dprobs - row_delta[:, None]) * score_scale).astype(jnp.bfloat16)


def key_terms(dscores, weight_bf, query_rows, grad_rows):
    key_grad = jnp.einsum("qk,qd->kd", dscores, query_rows, preferred_element_type=jnp.float32)
    value_grad = jnp.einsum("qk,qd->kd", weight_bf, grad_rows, preferred_element_type=jnp.float32)
    return (key_grad, value_grad)


def one_block(query_rows, key_block, value_block, grad_rows, allowed, score_scale):
    scores = (
        jnp.einsum("qd,kd->qk", query_rows, key_block, preferred_element_type=jnp.float32)
        * score_scale
    )
    row_top = jnp.max(jnp.where(allowed, scores, -jnp.inf), axis=1, keepdims=True)
    row_total = jnp.sum(jnp.where(allowed, jnp.exp(scores - row_top), 0.0), axis=1, keepdims=True)
    log_total = row_top + jnp.log(row_total)
    weights = jnp.where(allowed, jnp.exp(scores - log_total), 0.0)
    weight_bf = weights.astype(jnp.bfloat16)
    attn_rows = jnp.einsum(
        "qk,kd->qd", weight_bf, value_block, preferred_element_type=jnp.float32
    ).astype(jnp.bfloat16)
    row_delta = jnp.sum(grad_rows.astype(jnp.float32) * attn_rows.astype(jnp.float32), axis=1)
    dscores = score_grads(grad_rows, value_block, weights, row_delta, score_scale)
    grad_q = jnp.einsum("qk,kd->qd", dscores, key_block, preferred_element_type=jnp.float32).astype(
        jnp.bfloat16
    )
    key_grad, value_grad = key_terms(dscores, weight_bf, query_rows, grad_rows)
    return (attn_rows, grad_q, key_grad, value_grad, log_total[:, 0], row_delta)


def gathered_shards(query_in, key_in, value_in, grad_out, module_lengths):
    head_q, head_k, head_v, head_do = (
        lax.all_to_all(query_in, "head", split_axis=1, concat_axis=0, tiled=True),
        lax.all_to_all(key_in, "head", split_axis=1, concat_axis=0, tiled=True),
        lax.all_to_all(value_in, "head", split_axis=1, concat_axis=0, tiled=True),
        lax.all_to_all(grad_out, "head", split_axis=1, concat_axis=0, tiled=True),
    )
    row_count = head_q.shape[0]
    width = head_q.shape[1]
    local_heads = width // HEAD_DIM
    prior_rows = row_count // 8
    score_scale = HEAD_DIM ** (-0.5)
    tail_start = row_count - prior_rows
    prior_k, prior_v = shifted((head_k[tail_start:], head_v[tail_start:]), "seq", 1)
    row_start = lax.axis_index("seq") * row_count
    query_pos = row_start + jnp.arange(row_count, dtype=jnp.int32)
    before_pos = row_start - prior_rows + jnp.arange(prior_rows, dtype=jnp.int32)
    key_pos = jnp.concatenate([before_pos, query_pos])
    block_rows = math.gcd(row_count, 512)
    block_count = row_count // block_rows
    pos_blocks = query_pos.reshape(block_count, block_rows)

    def by_head(flat, rows):
        return jnp.moveaxis(flat.reshape(rows, local_heads, HEAD_DIM), 1, 0)

    def to_flat(stacked):
        return jnp.moveaxis(stacked, 0, 1).reshape(stacked.shape[1], width)

    query_h = by_head(head_q, row_count)
    grad_h = by_head(head_do, row_count)
    key_h = by_head(jnp.concatenate([prior_k, head_k], axis=0), row_count + prior_rows)
    value_h = by_head(jnp.concatenate([prior_v, head_v], axis=0), row_count + prior_rows)

    def run_head(packed):
        query_rows, key_block, value_block, grad_rows = packed
        query_blocks = query_rows.reshape(block_count, block_rows, HEAD_DIM)
        grad_blocks = grad_rows.reshape(block_count, block_rows, HEAD_DIM)

        def run_block(inner):
            query_part, grad_part, pos_part = inner
            allowed = allowed_pairs(module_lengths, pos_part, key_pos)
            return one_block(query_part, key_block, value_block, grad_part, allowed, score_scale)

        attn_b, grad_qb, key_b, value_b, lse_b, delta_b = lax.map(
            run_block, (query_blocks, grad_blocks, pos_blocks)
        )
        return (
            attn_b.reshape(row_count, HEAD_DIM),
            grad_qb.reshape(row_count, HEAD_DIM),
            jnp.sum(key_b, axis=0),
            jnp.sum(value_b, axis=0),
            lse_b.reshape(row_count),
            delta_b.reshape(row_count),
        )

    attn_h, grad_qh, key_grad, value_grad, log_total, row_delta = lax.map(
        run_head, (query_h, key_h, value_h, grad_h)
    )
    attn_flat = to_flat(attn_h)
    attn_back = lax.all_to_all(attn_flat, "head", split_axis=0, concat_axis=1, tiled=True)
    grad_q = to_flat(grad_qh)
    later_k, later_v = shifted((key_grad[:, :prior_rows], value_grad[:, :prior_rows]), "seq", -1)
    key_total = key_grad[:, prior_rows:].at[:, tail_start:].add(later_k)
    value_total = value_grad[:, prior_rows:].at[:, tail_start:].add(later_v)
    grad_k = to_flat(key_total.astype(jnp.bfloat16))
    grad_v = to_flat(value_total.astype(jnp.bfloat16))
    back_q, back_k, back_v = (
        lax.all_to_all(grad_q, "head", split_axis=0, concat_axis=1, tiled=True),
        lax.all_to_all(grad_k, "head", split_axis=0, concat_axis=1, tiled=True),
        lax.all_to_all(grad_v, "head", split_axis=0, concat_axis=1, tiled=True),
    )
    return (attn_back, back_q, back_k, back_v)


def dot(left, right, left_dim, right_dim):
    return lax.dot_general(
        left, right, (((left_dim,), (right_dim,)), ((), ())), preferred_element_type=jnp.float32
    )


def module_ends_row(lengths_row):
    count = lengths_row.shape[1]
    row = lax.broadcasted_iota(jnp.int32, (count, count), 0)
    col = lax.broadcasted_iota(jnp.int32, (count, count), 1)
    lengths_col = jnp.sum(jnp.where(row == col, lengths_row, 0.0), axis=1, keepdims=True)
    return jnp.sum(jnp.where(row <= col, lengths_col, 0.0), axis=0, keepdims=True)


def module_ends_col(lengths_row):
    count = lengths_row.shape[1]
    row = lax.broadcasted_iota(jnp.int32, (count, count), 0)
    col = lax.broadcasted_iota(jnp.int32, (count, count), 1)
    return jnp.sum(jnp.where(col <= row, lengths_row, 0.0), axis=1, keepdims=True)


def bias_by_query(lengths_row, first_query, queries, first_key, keys):
    ends = module_ends_row(lengths_row)
    query = (first_query + lax.broadcasted_iota(jnp.int32, (queries, 1), 0)).astype(jnp.float32)
    start = jnp.max(jnp.where(ends <= query, ends, 0.0), axis=1, keepdims=True)
    key = (first_key + lax.broadcasted_iota(jnp.int32, (queries, keys), 1)).astype(jnp.float32)
    return jnp.where((key >= start) & (key <= query), 0.0, MASKED)


def bias_by_key(lengths_row, first_query, queries, first_key, keys):
    ends = module_ends_col(lengths_row)
    query = (first_query + lax.broadcasted_iota(jnp.int32, (1, queries), 1)).astype(jnp.float32)
    start = jnp.max(jnp.where(ends <= query, ends, 0.0), axis=0, keepdims=True)
    key = (first_key + lax.broadcasted_iota(jnp.int32, (keys, queries), 0)).astype(jnp.float32)
    return jnp.where((key >= start) & (key <= query), 0.0, MASKED)


def by_query(q, k, do, v, bias):
    scores = dot(q, k, 1, 1) * (SCALE * LOG2E) + bias
    return scores, dot(do, v, 1, 1)


def full_rows(pairs):
    tops = [jnp.max(s, axis=1, keepdims=True) for s, _ in pairs]
    raws = [jnp.exp2(s - top) for (s, _), top in zip(pairs, tops)]
    parts = [1.0 / jnp.sum(raw, axis=1, keepdims=True) for raw in raws]
    weights = [raw * part for raw, part in zip(raws, parts)]
    deltas = [jnp.sum(w * dp, axis=1, keepdims=True) for w, (_, dp) in zip(weights, pairs)]
    grads = [w * (dp - delta) * SCALE for w, (_, dp), delta in zip(weights, pairs, deltas)]
    return [w.astype(jnp.bfloat16) for w in weights], [g.astype(jnp.bfloat16) for g in grads]


def merged_rows(pairs, own):
    tops = [
        jnp.maximum(jnp.max(s, axis=0, keepdims=True), log) for (s, _), (log, _) in zip(pairs, own)
    ]
    raws = [jnp.exp2(s - top) for (s, _), top in zip(pairs, tops)]
    own_raws = [jnp.exp2(log - top) for (log, _), top in zip(own, tops)]
    parts = [
        1.0 / (jnp.sum(raw, axis=0, keepdims=True) + own_raw)
        for raw, own_raw in zip(raws, own_raws)
    ]
    weights = [raw * part for raw, part in zip(raws, parts)]
    deltas = [
        jnp.sum(w * dp, axis=0, keepdims=True) + own_raw * part * own_delta
        for w, (_, dp), own_raw, part, (_, own_delta) in zip(weights, pairs, own_raws, parts, own)
    ]
    grads = [w * (dp - delta) * SCALE for w, (_, dp), delta in zip(weights, pairs, deltas)]
    return [w.astype(jnp.bfloat16) for w in weights], [g.astype(jnp.bfloat16) for g in grads]


def head_columns(width):
    return [slice(c, c + HEAD_DIM) for c in range(0, width, HEAD_DIM)]


def device_first(tok):
    place = lax.axis_index("seq") * lax.axis_size("head") + lax.axis_index("head")
    return place * tok


def split_bf16(value, terms):
    parts = []
    for _ in range(terms):
        part = value.astype(jnp.bfloat16)
        parts.append(part.astype(jnp.float32))
        value = value - parts[-1]
    return parts


def first_kernel(tok, prior, len_ref, q_ref, k_ref, v_ref, do_ref, out_ref, bias_ref):
    columns = head_columns(q_ref.shape[1])

    @pl.when(pl.program_id(0) == 0)
    def _():
        first = device_first(tok)
        lengths = len_ref[...].astype(jnp.float32)
        bias_ref[...] = bias_by_key(lengths, first, prior, first, prior)

    out_ref[:prior, :] = q_ref[...]
    out_ref[prior : 2 * prior, :] = do_ref[...]
    bias = bias_ref[...]
    pairs = [by_query(k_ref[:, c], q_ref[:, c], v_ref[:, c], do_ref[:, c], bias) for c in columns]
    tops = [jnp.max(s, axis=0, keepdims=True) for s, _ in pairs]
    raws = [jnp.exp2(s - top) for (s, _), top in zip(pairs, tops)]
    totals = [jnp.sum(raw, axis=0, keepdims=True) for raw in raws]
    sums = [jnp.sum(raw * dp, axis=0, keepdims=True) for raw, (_, dp) in zip(raws, pairs)]
    for c, top, total, summed in zip(columns, tops, totals, sums):
        rows = split_bf16(top + jnp.log2(total), 3) + split_bf16(summed / total, 2)
        rows.append(jnp.zeros((STAT_ROWS - len(rows), prior), jnp.float32))
        block = jnp.concatenate(rows, axis=0)
        block = jnp.concatenate([block, jnp.zeros_like(block)], axis=1)
        out_ref[2 * prior :, c] = block.astype(jnp.bfloat16)


def own_kernel(
    prior, len_ref, q_ref, k_ref, v_ref, do_ref, attn_ref, gq_ref, gk_ref, gv_ref, bias_ref
):
    tok, width = k_ref.shape
    rest = tok - prior
    columns = head_columns(width)

    @pl.when(pl.program_id(0) == 0)
    def _():
        first = device_first(tok)
        lengths = len_ref[...].astype(jnp.float32)
        bias_ref[...] = bias_by_query(lengths, first + prior, rest, first, tok)

    bias = bias_ref[...]
    pairs = [by_query(q_ref[:, c], k_ref[:, c], do_ref[:, c], v_ref[:, c], bias) for c in columns]
    weights, grads = full_rows(pairs)
    for c, w, g in zip(columns, weights, grads):
        attn_ref[:, c] = dot(w, v_ref[:, c], 1, 0).astype(jnp.bfloat16)
        gq_ref[:, c] = dot(g, k_ref[:, c], 1, 0).astype(jnp.bfloat16)
        gk_ref[:, c] = dot(g, q_ref[:, c], 0, 0)
        gv_ref[:, c] = dot(w, do_ref[:, c], 0, 0)


def lead_kernel(
    prior, len_ref, q_ref, k_ref, v_ref, do_ref, before_ref, gk_part_ref, gv_part_ref,
    attn_in, gq_in, attn_ref, gq_ref, gk_ref, gv_ref, bias_ref,
):
    columns = head_columns(q_ref.shape[1])

    @pl.when(pl.program_id(0) == 0)
    def _():
        first = device_first(attn_in.shape[0])
        lengths = len_ref[...].astype(jnp.float32)
        bias_ref[...] = bias_by_query(lengths, first, prior, first - prior, 2 * prior)

    bias = bias_ref[...]
    early, late = slice(0, prior), slice(prior, 2 * prior)
    keys = [jnp.concatenate([before_ref[early, c], k_ref[:, c]], axis=0) for c in columns]
    values = [jnp.concatenate([before_ref[late, c], v_ref[:, c]], axis=0) for c in columns]
    pairs = [
        by_query(q_ref[:, c], k, do_ref[:, c], v, bias) for c, k, v in zip(columns, keys, values)
    ]
    weights, grads = full_rows(pairs)
    for c, w, g, k, v in zip(columns, weights, grads, keys, values):
        attn_ref[:, c] = dot(w, v, 1, 0).astype(jnp.bfloat16)
        gq_ref[:, c] = dot(g, k, 1, 0).astype(jnp.bfloat16)
        gk = gk_part_ref[:, c] + dot(g[:, late], q_ref[:, c], 0, 0)
        gv = gv_part_ref[:, c] + dot(w[:, late], do_ref[:, c], 0, 0)
        gk_ref[:, c] = gk.astype(jnp.bfloat16)
        gv_ref[:, c] = gv.astype(jnp.bfloat16)


def tail_kernel(
    prior, len_ref, k_ref, v_ref, after_ref, gk_part_ref, gv_part_ref,
    gk_in, gv_in, gk_ref, gv_ref, bias_ref,
):
    columns = head_columns(k_ref.shape[1])

    @pl.when(pl.program_id(0) == 0)
    def _():
        tok = gk_in.shape[0]
        first = device_first(tok)
        lengths = len_ref[...].astype(jnp.float32)
        bias_ref[...] = bias_by_key(lengths, first + tok, prior, first + tok - prior, prior)

    bias = bias_ref[...]
    early, late = slice(0, prior), slice(prior, 2 * prior)
    pairs = [
        by_query(k_ref[:, c], after_ref[early, c], v_ref[:, c], after_ref[late, c], bias)
        for c in columns
    ]
    own = []
    for c in columns:
        stat = after_ref[2 * prior :, c].astype(jnp.float32)[:, :prior]
        own.append((stat[0:1] + stat[1:2] + stat[2:3], stat[3:4] + stat[4:5]))
    weights, grads = merged_rows(pairs, own)
    for c, w, g in zip(columns, weights, grads):
        gk = gk_part_ref[:, c] + dot(g, after_ref[early, c], 1, 0)
        gv = gv_part_ref[:, c] + dot(w, after_ref[late, c], 1, 0)
        gk_ref[:, c] = gk.astype(jnp.bfloat16)
        gv_ref[:, c] = gv.astype(jnp.bfloat16)


def neighbour(value, by):
    peers = lax.axis_size("seq") * lax.axis_size("head")
    pairs = [(i, i + by) for i in range(peers) if 0 <= i + by < peers]
    return lax.ppermute(value, ("seq", "head"), pairs)


def cost(heads, queries, keys, products, moved):
    return pl.CostEstimate(
        flops=2 * heads * queries * keys * HEAD_DIM * products,
        bytes_accessed=moved,
        transcendentals=heads * queries * keys,
    )


def halo_shards(query_in, key_in, value_in, grad_out, module_lengths):
    tok, width = query_in.shape
    prior = tok * lax.axis_size("head") // 8
    heads = width // HEAD_DIM
    step = min(width, 4 * HEAD_DIM)
    groups = width // step
    per = step // HEAD_DIM
    lengths = module_lengths.reshape(1, -1)
    len_spec = pl.BlockSpec(lengths.shape, lambda g: (0, 0))
    keep = pl.BlockSpec(memory_space=pl.ANY)
    full16 = jax.ShapeDtypeStruct((tok, width), jnp.bfloat16)
    full32 = jax.ShapeDtypeStruct((tok, width), jnp.float32)
    late_at = tok // prior - 1

    def rows(count, at=0, base=0):
        return pl.BlockSpec((count, step), lambda g: (at, g + base))

    def call(kernel, name, grid, ins, outs, shapes, bias, products, moved, aliases=None):
        return pl.pallas_call(
            functools.partial(kernel, prior),
            grid=(grid,),
            in_specs=[len_spec, *ins],
            out_specs=outs,
            out_shape=shapes,
            scratch_shapes=[pltpu.VMEM(bias, jnp.float32)],
            input_output_aliases=aliases or {},
            cost_estimate=cost(grid * per, *bias, products, moved * grid * step),
            name=name,
        )

    before = neighbour(jnp.concatenate([key_in[tok - prior :], value_in[tok - prior :]]), 1)

    cuts = [0, groups // 2, groups] if groups > 1 else [0, groups]
    spans = list(zip(cuts[:-1], cuts[1:]))
    sent = 2 * prior + STAT_ROWS
    afters = []
    for low, high in spans:
        packed = call(
            functools.partial(first_kernel, tok), "first_rows", high - low, [rows(prior, 0, low)] * 4, rows(sent),
            jax.ShapeDtypeStruct((sent, (high - low) * step), jnp.bfloat16), (prior, prior), 2,
            12 * prior,
        )(lengths, query_in, key_in, value_in, grad_out)
        afters.append(neighbour(packed, -1))

    attn, gq, gk_part, gv_part = call(
        own_kernel, "own_block", groups,
        [rows(prior, late_at), rows(tok), rows(tok), rows(prior, late_at)],
        [rows(prior, late_at), rows(prior, late_at), rows(tok), rows(tok)],
        [full16, full16, full32, full32], (tok - prior, tok), 6, 18 * tok,
    )(lengths, query_in, key_in, value_in, grad_out)

    attn, gq, gk, gv = call(
        lead_kernel, "lead_rows", groups,
        [rows(prior)] * 4 + [rows(2 * prior), rows(prior), rows(prior), keep, keep],
        [rows(prior)] * 4, [full16] * 4, (prior, 2 * prior), 5, 14 * tok, {8: 0, 9: 1},
    )(lengths, query_in, key_in, value_in, grad_out, before, gk_part, gv_part, attn, gq)

    for (low, high), after in zip(spans, afters):
        late = rows(prior, late_at, low)
        gk, gv = call(
            tail_kernel, "tail_keys", high - low,
            [late, late, rows(sent), late, late, keep, keep],
            [late, late], [full16] * 2, (prior, prior), 4, 10 * tok, {6: 0, 7: 1},
        )(lengths, key_in, value_in, after, gk_part, gv_part, gk, gv)
    return (attn, gq, gk, gv)


def shards(query_in, key_in, value_in, grad_out, module_lengths):
    tok = query_in.shape[0]
    prior = tok * lax.axis_size("head") // 8
    plan = halo_shards if 2 * prior <= tok else gathered_shards
    return plan(query_in, key_in, value_in, grad_out, module_lengths)


def solution(mesh):
    placed = (
        P(("seq", "head"), None),
        P(("seq", "head"), None),
        P(("seq", "head"), None),
        P(("seq", "head"), None),
        P(),
    )
    return jax.shard_map(
        shards,
        mesh=mesh,
        in_specs=placed,
        out_specs=(
            P(("seq", "head"), None),
            P(("seq", "head"), None),
            P(("seq", "head"), None),
            P(("seq", "head"), None),
        ),
        check_vma=False,
    )
```

```python
import functools
import math

import jax
import jax.numpy as jnp
from jax import lax
from jax.experimental import pallas as pl
from jax.experimental.pallas import tpu as pltpu
from jax.sharding import PartitionSpec as P

HEAD_DIM = 128
SCALE = HEAD_DIM ** (-0.5)
LOG2E = math.log2(math.e)
MASKED = -1e30
STAT_ROWS = 16


def shifted(value, axis, by):
    peers = lax.axis_size(axis)
    pairs = [(i, i + by) for i in range(peers) if 0 <= i + by < peers]
    return lax.ppermute(value, axis, pairs)


def module_ids(module_lengths, positions):
    module_ends = jnp.cumsum(module_lengths)
    counted = jnp.sum((positions[:, None] >= module_ends[None, :]).astype(jnp.int32), axis=1)
    return jnp.where(positions >= 0, counted, -1)


def allowed_pairs(module_lengths, query_pos, key_pos):
    same = (
        module_ids(module_lengths, query_pos)[:, None]
        == module_ids(module_lengths, key_pos)[None, :]
    )
    return same & (key_pos[None, :] <= query_pos[:, None])


def score_grads(grad_rows, value_block, weights, row_delta, score_scale):
    dprobs = jnp.einsum("qd,kd->qk", grad_rows, value_block, preferred_element_type=jnp.float32)
    return (weights * (dprobs - row_delta[:, None]) * score_scale).astype(jnp.bfloat16)


def key_terms(dscores, weight_bf, query_rows, grad_rows):
    key_grad = jnp.einsum("qk,qd->kd", dscores, query_rows, preferred_element_type=jnp.float32)
    value_grad = jnp.einsum("qk,qd->kd", weight_bf, grad_rows, preferred_element_type=jnp.float32)
    return (key_grad, value_grad)


def one_block(query_rows, key_block, value_block, grad_rows, allowed, score_scale):
    scores = (
        jnp.einsum("qd,kd->qk", query_rows, key_block, preferred_element_type=jnp.float32)
        * score_scale
    )
    row_top = jnp.max(jnp.where(allowed, scores, -jnp.inf), axis=1, keepdims=True)
    row_total = jnp.sum(jnp.where(allowed, jnp.exp(scores - row_top), 0.0), axis=1, keepdims=True)
    log_total = row_top + jnp.log(row_total)
    weights = jnp.where(allowed, jnp.exp(scores - log_total), 0.0)
    weight_bf = weights.astype(jnp.bfloat16)
    attn_rows = jnp.einsum(
        "qk,kd->qd", weight_bf, value_block, preferred_element_type=jnp.float32
    ).astype(jnp.bfloat16)
    row_delta = jnp.sum(grad_rows.astype(jnp.float32) * attn_rows.astype(jnp.float32), axis=1)
    dscores = score_grads(grad_rows, value_block, weights, row_delta, score_scale)
    grad_q = jnp.einsum("qk,kd->qd", dscores, key_block, preferred_element_type=jnp.float32).astype(
        jnp.bfloat16
    )
    key_grad, value_grad = key_terms(dscores, weight_bf, query_rows, grad_rows)
    return (attn_rows, grad_q, key_grad, value_grad, log_total[:, 0], row_delta)


def gathered_shards(query_in, key_in, value_in, grad_out, module_lengths):
    head_q, head_k, head_v, head_do = (
        lax.all_to_all(query_in, "head", split_axis=1, concat_axis=0, tiled=True),
        lax.all_to_all(key_in, "head", split_axis=1, concat_axis=0, tiled=True),
        lax.all_to_all(value_in, "head", split_axis=1, concat_axis=0, tiled=True),
        lax.all_to_all(grad_out, "head", split_axis=1, concat_axis=0, tiled=True),
    )
    row_count = head_q.shape[0]
    width = head_q.shape[1]
    local_heads = width // HEAD_DIM
    prior_rows = row_count // 8
    score_scale = HEAD_DIM ** (-0.5)
    tail_start = row_count - prior_rows
    prior_k, prior_v = shifted((head_k[tail_start:], head_v[tail_start:]), "seq", 1)
    row_start = lax.axis_index("seq") * row_count
    query_pos = row_start + jnp.arange(row_count, dtype=jnp.int32)
    before_pos = row_start - prior_rows + jnp.arange(prior_rows, dtype=jnp.int32)
    key_pos = jnp.concatenate([before_pos, query_pos])
    block_rows = math.gcd(row_count, 512)
    block_count = row_count // block_rows
    pos_blocks = query_pos.reshape(block_count, block_rows)

    def by_head(flat, rows):
        return jnp.moveaxis(flat.reshape(rows, local_heads, HEAD_DIM), 1, 0)

    def to_flat(stacked):
        return jnp.moveaxis(stacked, 0, 1).reshape(stacked.shape[1], width)

    query_h = by_head(head_q, row_count)
    grad_h = by_head(head_do, row_count)
    key_h = by_head(jnp.concatenate([prior_k, head_k], axis=0), row_count + prior_rows)
    value_h = by_head(jnp.concatenate([prior_v, head_v], axis=0), row_count + prior_rows)

    def run_head(packed):
        query_rows, key_block, value_block, grad_rows = packed
        query_blocks = query_rows.reshape(block_count, block_rows, HEAD_DIM)
        grad_blocks = grad_rows.reshape(block_count, block_rows, HEAD_DIM)

        def run_block(inner):
            query_part, grad_part, pos_part = inner
            allowed = allowed_pairs(module_lengths, pos_part, key_pos)
            return one_block(query_part, key_block, value_block, grad_part, allowed, score_scale)

        attn_b, grad_qb, key_b, value_b, lse_b, delta_b = lax.map(
            run_block, (query_blocks, grad_blocks, pos_blocks)
        )
        return (
            attn_b.reshape(row_count, HEAD_DIM),
            grad_qb.reshape(row_count, HEAD_DIM),
            jnp.sum(key_b, axis=0),
            jnp.sum(value_b, axis=0),
            lse_b.reshape(row_count),
            delta_b.reshape(row_count),
        )

    attn_h, grad_qh, key_grad, value_grad, log_total, row_delta = lax.map(
        run_head, (query_h, key_h, value_h, grad_h)
    )
    attn_flat = to_flat(attn_h)
    attn_back = lax.all_to_all(attn_flat, "head", split_axis=0, concat_axis=1, tiled=True)
    grad_q = to_flat(grad_qh)
    later_k, later_v = shifted((key_grad[:, :prior_rows], value_grad[:, :prior_rows]), "seq", -1)
    key_total = key_grad[:, prior_rows:].at[:, tail_start:].add(later_k)
    value_total = value_grad[:, prior_rows:].at[:, tail_start:].add(later_v)
    grad_k = to_flat(key_total.astype(jnp.bfloat16))
    grad_v = to_flat(value_total.astype(jnp.bfloat16))
    back_q, back_k, back_v = (
        lax.all_to_all(grad_q, "head", split_axis=0, concat_axis=1, tiled=True),
        lax.all_to_all(grad_k, "head", split_axis=0, concat_axis=1, tiled=True),
        lax.all_to_all(grad_v, "head", split_axis=0, concat_axis=1, tiled=True),
    )
    return (attn_back, back_q, back_k, back_v)


def dot(left, right, left_dim, right_dim):
    return lax.dot_general(
        left, right, (((left_dim,), (right_dim,)), ((), ())), preferred_element_type=jnp.float32
    )


def module_ends_row(lengths_row):
    count = lengths_row.shape[1]
    row = lax.broadcasted_iota(jnp.int32, (count, count), 0)
    col = lax.broadcasted_iota(jnp.int32, (count, count), 1)
    lengths_col = jnp.sum(jnp.where(row == col, lengths_row, 0.0), axis=1, keepdims=True)
    return jnp.sum(jnp.where(row <= col, lengths_col, 0.0), axis=0, keepdims=True)


def module_ends_col(lengths_row):
    count = lengths_row.shape[1]
    row = lax.broadcasted_iota(jnp.int32, (count, count), 0)
    col = lax.broadcasted_iota(jnp.int32, (count, count), 1)
    return jnp.sum(jnp.where(col <= row, lengths_row, 0.0), axis=1, keepdims=True)


def bias_by_query(lengths_row, first_query, queries, first_key, keys):
    ends = module_ends_row(lengths_row)
    query = (first_query + lax.broadcasted_iota(jnp.int32, (queries, 1), 0)).astype(jnp.float32)
    start = jnp.max(jnp.where(ends <= query, ends, 0.0), axis=1, keepdims=True)
    key = (first_key + lax.broadcasted_iota(jnp.int32, (queries, keys), 1)).astype(jnp.float32)
    return jnp.where((key >= start) & (key <= query), 0.0, MASKED)


def bias_by_key(lengths_row, first_query, queries, first_key, keys):
    ends = module_ends_col(lengths_row)
    query = (first_query + lax.broadcasted_iota(jnp.int32, (1, queries), 1)).astype(jnp.float32)
    start = jnp.max(jnp.where(ends <= query, ends, 0.0), axis=0, keepdims=True)
    key = (first_key + lax.broadcasted_iota(jnp.int32, (keys, queries), 0)).astype(jnp.float32)
    return jnp.where((key >= start) & (key <= query), 0.0, MASKED)


def by_query(q, k, do, v, bias):
    scores = dot(q, k, 1, 1) * (SCALE * LOG2E) + bias
    return scores, dot(do, v, 1, 1)


def full_rows(pairs):
    tops = [jnp.max(s, axis=1, keepdims=True) for s, _ in pairs]
    raws = [jnp.exp2(s - top) for (s, _), top in zip(pairs, tops)]
    parts = [1.0 / jnp.sum(raw, axis=1, keepdims=True) for raw in raws]
    weights = [raw * part for raw, part in zip(raws, parts)]
    deltas = [jnp.sum(w * dp, axis=1, keepdims=True) for w, (_, dp) in zip(weights, pairs)]
    grads = [w * (dp - delta) * SCALE for w, (_, dp), delta in zip(weights, pairs, deltas)]
    return [w.astype(jnp.bfloat16) for w in weights], [g.astype(jnp.bfloat16) for g in grads]


def merged_rows(pairs, own):
    tops = [
        jnp.maximum(jnp.max(s, axis=0, keepdims=True), log) for (s, _), (log, _) in zip(pairs, own)
    ]
    raws = [jnp.exp2(s - top) for (s, _), top in zip(pairs, tops)]
    own_raws = [jnp.exp2(log - top) for (log, _), top in zip(own, tops)]
    parts = [
        1.0 / (jnp.sum(raw, axis=0, keepdims=True) + own_raw)
        for raw, own_raw in zip(raws, own_raws)
    ]
    weights = [raw * part for raw, part in zip(raws, parts)]
    deltas = [
        jnp.sum(w * dp, axis=0, keepdims=True) + own_raw * part * own_delta
        for w, (_, dp), own_raw, part, (_, own_delta) in zip(weights, pairs, own_raws, parts, own)
    ]
    grads = [w * (dp - delta) * SCALE for w, (_, dp), delta in zip(weights, pairs, deltas)]
    return [w.astype(jnp.bfloat16) for w in weights], [g.astype(jnp.bfloat16) for g in grads]


def head_columns(width):
    return [slice(c, c + HEAD_DIM) for c in range(0, width, HEAD_DIM)]


def device_first(tok):
    place = lax.axis_index("seq") * lax.axis_size("head") + lax.axis_index("head")
    return place * tok


def split_bf16(value, terms):
    parts = []
    for _ in range(terms):
        part = value.astype(jnp.bfloat16)
        parts.append(part.astype(jnp.float32))
        value = value - parts[-1]
    return parts


def own_kernel(
    prior, len_ref, q_ref, k_ref, v_ref, do_ref, attn_ref, gq_ref, gk_ref, gv_ref,
    lead_bias_ref, tail_bias_ref, *refs,
):
    *packed_refs, bias_ref, first_bias_ref = refs
    tok, width = k_ref.shape
    columns = head_columns(width)
    early, late = slice(0, prior), slice(tok - prior, tok)

    @pl.when(pl.program_id(0) == 0)
    def _():
        first = device_first(tok)
        lengths = len_ref[...].astype(jnp.float32)
        bias_ref[...] = bias_by_query(lengths, first + prior, tok - prior, first, tok)
        first_bias_ref[...] = bias_by_key(lengths, first, prior, first, prior)
        lead_bias_ref[...] = bias_by_query(lengths, first, prior, first - prior, 2 * prior)
        tail_bias_ref[...] = bias_by_key(lengths, first + tok, prior, first + tok - prior, prior)

    bias, first_bias = bias_ref[...], first_bias_ref[...]
    pairs = [
        by_query(q_ref[late, c], k_ref[:, c], do_ref[late, c], v_ref[:, c], bias) for c in columns
    ]
    firsts = [
        by_query(k_ref[early, c], q_ref[early, c], v_ref[early, c], do_ref[early, c], first_bias)
        for c in columns
    ]
    weights, grads = full_rows(pairs)
    for c, w, g in zip(columns, weights, grads):
        attn_ref[:, c] = dot(w, v_ref[:, c], 1, 0).astype(jnp.bfloat16)
        gq_ref[:, c] = dot(g, k_ref[:, c], 1, 0).astype(jnp.bfloat16)
        gk_ref[:, c] = dot(g, q_ref[late, c], 0, 0)
        gv_ref[:, c] = dot(w, do_ref[late, c], 0, 0)
    tops = [jnp.max(s, axis=0, keepdims=True) for s, _ in firsts]
    raws = [jnp.exp2(s - top) for (s, _), top in zip(firsts, tops)]
    totals = [jnp.sum(raw, axis=0, keepdims=True) for raw in raws]
    sums = [jnp.sum(raw * dp, axis=0, keepdims=True) for raw, (_, dp) in zip(raws, firsts)]
    blocks = []
    for top, total, summed in zip(tops, totals, sums):
        rows = split_bf16(top + jnp.log2(total), 3) + split_bf16(summed / total, 2)
        rows.append(jnp.zeros((STAT_ROWS - len(rows), prior), jnp.float32))
        block = jnp.concatenate(rows, axis=0)
        blocks.append(jnp.concatenate([block, jnp.zeros_like(block)], axis=1).astype(jnp.bfloat16))
    for at, packed_ref in enumerate(packed_refs):

        @pl.when(pl.program_id(0) == at)
        def _(packed_ref=packed_ref):
            packed_ref[early, :] = q_ref[early, :]
            packed_ref[prior : 2 * prior, :] = do_ref[early, :]
            for c, block in zip(columns, blocks):
                packed_ref[2 * prior :, c] = block


def lead_kernel(
    prior, bias_ref, q_ref, k_ref, v_ref, do_ref, before_ref, gk_part_ref, gv_part_ref,
    attn_in, gq_in, attn_ref, gq_ref, gk_ref, gv_ref,
):
    columns = head_columns(q_ref.shape[1])
    bias = bias_ref[...]
    early, late = slice(0, prior), slice(prior, 2 * prior)
    keys = [jnp.concatenate([before_ref[early, c], k_ref[:, c]], axis=0) for c in columns]
    values = [jnp.concatenate([before_ref[late, c], v_ref[:, c]], axis=0) for c in columns]
    pairs = [
        by_query(q_ref[:, c], k, do_ref[:, c], v, bias) for c, k, v in zip(columns, keys, values)
    ]
    weights, grads = full_rows(pairs)
    for c, w, g, k, v in zip(columns, weights, grads, keys, values):
        attn_ref[:, c] = dot(w, v, 1, 0).astype(jnp.bfloat16)
        gq_ref[:, c] = dot(g, k, 1, 0).astype(jnp.bfloat16)
        gk = gk_part_ref[:, c] + dot(g[:, late], q_ref[:, c], 0, 0)
        gv = gv_part_ref[:, c] + dot(w[:, late], do_ref[:, c], 0, 0)
        gk_ref[:, c] = gk.astype(jnp.bfloat16)
        gv_ref[:, c] = gv.astype(jnp.bfloat16)


def tail_kernel(
    prior, bias_ref, k_ref, v_ref, after_ref, gk_part_ref, gv_part_ref,
    gk_in, gv_in, gk_ref, gv_ref,
):
    columns = head_columns(k_ref.shape[1])
    bias = bias_ref[...]
    early, late = slice(0, prior), slice(prior, 2 * prior)
    pairs = [
        by_query(k_ref[:, c], after_ref[early, c], v_ref[:, c], after_ref[late, c], bias)
        for c in columns
    ]
    own = []
    for c in columns:
        stat = after_ref[2 * prior :, c].astype(jnp.float32)[:, :prior]
        own.append((stat[0:1] + stat[1:2] + stat[2:3], stat[3:4] + stat[4:5]))
    weights, grads = merged_rows(pairs, own)
    for c, w, g in zip(columns, weights, grads):
        gk = gk_part_ref[:, c] + dot(g, after_ref[early, c], 1, 0)
        gv = gv_part_ref[:, c] + dot(w, after_ref[late, c], 1, 0)
        gk_ref[:, c] = gk.astype(jnp.bfloat16)
        gv_ref[:, c] = gv.astype(jnp.bfloat16)


def neighbour(value, by):
    peers = lax.axis_size("seq") * lax.axis_size("head")
    pairs = [(i, i + by) for i in range(peers) if 0 <= i + by < peers]
    return lax.ppermute(value, ("seq", "head"), pairs)


def cost(heads, queries, keys, products, moved):
    return pl.CostEstimate(
        flops=2 * heads * queries * keys * HEAD_DIM * products,
        bytes_accessed=moved,
        transcendentals=heads * queries * keys,
    )


def halo_shards(query_in, key_in, value_in, grad_out, module_lengths):
    tok, width = query_in.shape
    prior = tok * lax.axis_size("head") // 8
    step = math.gcd(width, 8 * HEAD_DIM)
    groups = width // step
    per = step // HEAD_DIM
    late_at = tok // prior - 1
    sent = 2 * prior + STAT_ROWS
    lengths = module_lengths.reshape(1, -1)
    keep = pl.BlockSpec(memory_space=pl.ANY)
    full16 = jax.ShapeDtypeStruct((tok, width), jnp.bfloat16)
    full32 = jax.ShapeDtypeStruct((tok, width), jnp.float32)
    packed = jax.ShapeDtypeStruct((sent, step), jnp.bfloat16)
    lead_shape, tail_shape = (prior, 2 * prior), (prior, prior)

    def rows(count, at=0, base=0):
        return pl.BlockSpec((count, step), lambda g: (at, g + base))

    def fixed(*shape):
        return pl.BlockSpec(shape, lambda g: (0, 0))

    def call(kernel, name, grid, ins, outs, shapes, work, moved, aliases=None, scratch=()):
        return pl.pallas_call(
            functools.partial(kernel, prior),
            grid=(grid,),
            in_specs=ins,
            out_specs=outs,
            out_shape=shapes,
            scratch_shapes=scratch,
            input_output_aliases=aliases or {},
            cost_estimate=cost(grid * per, *work, moved * grid * step),
            compiler_params=pltpu.CompilerParams(vmem_limit_bytes=16 * 2**20),
            name=name,
        )

    before = neighbour(jnp.concatenate([key_in[tok - prior :], value_in[tok - prior :]]), 1)

    attn, gq, gk_part, gv_part, lead_bias, tail_bias, *parts = call(
        own_kernel, "own_block", groups,
        [fixed(*lengths.shape), rows(tok), rows(tok), rows(tok), rows(tok)],
        [rows(prior, late_at), rows(prior, late_at), rows(tok), rows(tok)]
        + [fixed(*lead_shape), fixed(*tail_shape)] + [fixed(sent, step)] * groups,
        [full16, full16, full32, full32]
        + [jax.ShapeDtypeStruct(shape, jnp.float32) for shape in (lead_shape, tail_shape)]
        + [packed] * groups,
        (tok, tok, 4), 22 * tok,
        scratch=[
            pltpu.VMEM((tok - prior, tok), jnp.float32), pltpu.VMEM((prior, prior), jnp.float32)
        ],
    )(lengths, query_in, key_in, value_in, grad_out)
    afters = [neighbour(part, -1) for part in parts]

    attn, gq, gk, gv = call(
        lead_kernel, "lead_rows", groups,
        [fixed(*lead_shape)] + [rows(prior)] * 4 + [rows(2 * prior), rows(prior), rows(prior)]
        + [keep, keep],
        [rows(prior)] * 4, [full16] * 4, (prior, 2 * prior, 5), 14 * tok, {8: 0, 9: 1},
    )(lead_bias, query_in, key_in, value_in, grad_out, before, gk_part, gv_part, attn, gq)

    for at, after in enumerate(afters):
        late = rows(prior, late_at, at)
        gk, gv = call(
            tail_kernel, "tail_keys", 1,
            [fixed(*tail_shape), late, late, rows(sent), late, late, keep, keep],
            [late, late], [full16] * 2, (prior, prior, 4), 10 * tok, {6: 0, 7: 1},
        )(tail_bias, key_in, value_in, after, gk_part, gv_part, gk, gv)
    return (attn, gq, gk, gv)


def shards(query_in, key_in, value_in, grad_out, module_lengths):
    tok = query_in.shape[0]
    prior = tok * lax.axis_size("head") // 8
    plan = halo_shards if 2 * prior <= tok else gathered_shards
    return plan(query_in, key_in, value_in, grad_out, module_lengths)


def solution(mesh):
    placed = (
        P(("seq", "head"), None),
        P(("seq", "head"), None),
        P(("seq", "head"), None),
        P(("seq", "head"), None),
        P(),
    )
    return jax.shard_map(
        shards,
        mesh=mesh,
        in_specs=placed,
        out_specs=(
            P(("seq", "head"), None),
            P(("seq", "head"), None),
            P(("seq", "head"), None),
            P(("seq", "head"), None),
        ),
        check_vma=False,
    )
```

```python
import functools
import math

import jax
import jax.numpy as jnp
from jax import lax
from jax.experimental import pallas as pl
from jax.experimental.pallas import tpu as pltpu
from jax.sharding import PartitionSpec as P

HEAD_DIM = 128
SCALE = HEAD_DIM ** (-0.5)
LOG2E = math.log2(math.e)
MASKED = -1e30


def shifted(value, axis, by):
    peers = lax.axis_size(axis)
    pairs = [(i, i + by) for i in range(peers) if 0 <= i + by < peers]
    return lax.ppermute(value, axis, pairs)


def module_ids(module_lengths, positions):
    module_ends = jnp.cumsum(module_lengths)
    counted = jnp.sum((positions[:, None] >= module_ends[None, :]).astype(jnp.int32), axis=1)
    return jnp.where(positions >= 0, counted, -1)


def allowed_pairs(module_lengths, query_pos, key_pos):
    same = (
        module_ids(module_lengths, query_pos)[:, None]
        == module_ids(module_lengths, key_pos)[None, :]
    )
    return same & (key_pos[None, :] <= query_pos[:, None])


def score_grads(grad_rows, value_block, weights, row_delta, score_scale):
    dprobs = jnp.einsum("qd,kd->qk", grad_rows, value_block, preferred_element_type=jnp.float32)
    return (weights * (dprobs - row_delta[:, None]) * score_scale).astype(jnp.bfloat16)


def key_terms(dscores, weight_bf, query_rows, grad_rows):
    key_grad = jnp.einsum("qk,qd->kd", dscores, query_rows, preferred_element_type=jnp.float32)
    value_grad = jnp.einsum("qk,qd->kd", weight_bf, grad_rows, preferred_element_type=jnp.float32)
    return (key_grad, value_grad)


def one_block(query_rows, key_block, value_block, grad_rows, allowed, score_scale):
    scores = (
        jnp.einsum("qd,kd->qk", query_rows, key_block, preferred_element_type=jnp.float32)
        * score_scale
    )
    row_top = jnp.max(jnp.where(allowed, scores, -jnp.inf), axis=1, keepdims=True)
    row_total = jnp.sum(jnp.where(allowed, jnp.exp(scores - row_top), 0.0), axis=1, keepdims=True)
    log_total = row_top + jnp.log(row_total)
    weights = jnp.where(allowed, jnp.exp(scores - log_total), 0.0)
    weight_bf = weights.astype(jnp.bfloat16)
    attn_rows = jnp.einsum(
        "qk,kd->qd", weight_bf, value_block, preferred_element_type=jnp.float32
    ).astype(jnp.bfloat16)
    row_delta = jnp.sum(grad_rows.astype(jnp.float32) * attn_rows.astype(jnp.float32), axis=1)
    dscores = score_grads(grad_rows, value_block, weights, row_delta, score_scale)
    grad_q = jnp.einsum("qk,kd->qd", dscores, key_block, preferred_element_type=jnp.float32).astype(
        jnp.bfloat16
    )
    key_grad, value_grad = key_terms(dscores, weight_bf, query_rows, grad_rows)
    return (attn_rows, grad_q, key_grad, value_grad, log_total[:, 0], row_delta)


def gathered_shards(query_in, key_in, value_in, grad_out, module_lengths):
    head_q, head_k, head_v, head_do = (
        lax.all_to_all(query_in, "head", split_axis=1, concat_axis=0, tiled=True),
        lax.all_to_all(key_in, "head", split_axis=1, concat_axis=0, tiled=True),
        lax.all_to_all(value_in, "head", split_axis=1, concat_axis=0, tiled=True),
        lax.all_to_all(grad_out, "head", split_axis=1, concat_axis=0, tiled=True),
    )
    row_count = head_q.shape[0]
    width = head_q.shape[1]
    local_heads = width // HEAD_DIM
    prior_rows = row_count // 8
    score_scale = HEAD_DIM ** (-0.5)
    tail_start = row_count - prior_rows
    prior_k, prior_v = shifted((head_k[tail_start:], head_v[tail_start:]), "seq", 1)
    row_start = lax.axis_index("seq") * row_count
    query_pos = row_start + jnp.arange(row_count, dtype=jnp.int32)
    before_pos = row_start - prior_rows + jnp.arange(prior_rows, dtype=jnp.int32)
    key_pos = jnp.concatenate([before_pos, query_pos])
    block_rows = math.gcd(row_count, 512)
    block_count = row_count // block_rows
    pos_blocks = query_pos.reshape(block_count, block_rows)

    def by_head(flat, rows):
        return jnp.moveaxis(flat.reshape(rows, local_heads, HEAD_DIM), 1, 0)

    def to_flat(stacked):
        return jnp.moveaxis(stacked, 0, 1).reshape(stacked.shape[1], width)

    query_h = by_head(head_q, row_count)
    grad_h = by_head(head_do, row_count)
    key_h = by_head(jnp.concatenate([prior_k, head_k], axis=0), row_count + prior_rows)
    value_h = by_head(jnp.concatenate([prior_v, head_v], axis=0), row_count + prior_rows)

    def run_head(packed):
        query_rows, key_block, value_block, grad_rows = packed
        query_blocks = query_rows.reshape(block_count, block_rows, HEAD_DIM)
        grad_blocks = grad_rows.reshape(block_count, block_rows, HEAD_DIM)

        def run_block(inner):
            query_part, grad_part, pos_part = inner
            allowed = allowed_pairs(module_lengths, pos_part, key_pos)
            return one_block(query_part, key_block, value_block, grad_part, allowed, score_scale)

        attn_b, grad_qb, key_b, value_b, lse_b, delta_b = lax.map(
            run_block, (query_blocks, grad_blocks, pos_blocks)
        )
        return (
            attn_b.reshape(row_count, HEAD_DIM),
            grad_qb.reshape(row_count, HEAD_DIM),
            jnp.sum(key_b, axis=0),
            jnp.sum(value_b, axis=0),
            lse_b.reshape(row_count),
            delta_b.reshape(row_count),
        )

    attn_h, grad_qh, key_grad, value_grad, log_total, row_delta = lax.map(
        run_head, (query_h, key_h, value_h, grad_h)
    )
    attn_flat = to_flat(attn_h)
    attn_back = lax.all_to_all(attn_flat, "head", split_axis=0, concat_axis=1, tiled=True)
    grad_q = to_flat(grad_qh)
    later_k, later_v = shifted((key_grad[:, :prior_rows], value_grad[:, :prior_rows]), "seq", -1)
    key_total = key_grad[:, prior_rows:].at[:, tail_start:].add(later_k)
    value_total = value_grad[:, prior_rows:].at[:, tail_start:].add(later_v)
    grad_k = to_flat(key_total.astype(jnp.bfloat16))
    grad_v = to_flat(value_total.astype(jnp.bfloat16))
    back_q, back_k, back_v = (
        lax.all_to_all(grad_q, "head", split_axis=0, concat_axis=1, tiled=True),
        lax.all_to_all(grad_k, "head", split_axis=0, concat_axis=1, tiled=True),
        lax.all_to_all(grad_v, "head", split_axis=0, concat_axis=1, tiled=True),
    )
    return (attn_back, back_q, back_k, back_v)


def dot(left, right, left_dim, right_dim):
    return lax.dot_general(
        left, right, (((left_dim,), (right_dim,)), ((), ())), preferred_element_type=jnp.float32
    )


def module_ends_row(lengths_row):
    count = lengths_row.shape[1]
    row = lax.broadcasted_iota(jnp.int32, (count, count), 0)
    col = lax.broadcasted_iota(jnp.int32, (count, count), 1)
    lengths_col = jnp.sum(jnp.where(row == col, lengths_row, 0.0), axis=1, keepdims=True)
    return jnp.sum(jnp.where(row <= col, lengths_col, 0.0), axis=0, keepdims=True)


def module_ends_col(lengths_row):
    count = lengths_row.shape[1]
    row = lax.broadcasted_iota(jnp.int32, (count, count), 0)
    col = lax.broadcasted_iota(jnp.int32, (count, count), 1)
    return jnp.sum(jnp.where(col <= row, lengths_row, 0.0), axis=1, keepdims=True)


def bias_by_query(lengths_row, first_query, queries, first_key, keys):
    ends = module_ends_row(lengths_row)
    query = (first_query + lax.broadcasted_iota(jnp.int32, (queries, 1), 0)).astype(jnp.float32)
    start = jnp.max(jnp.where(ends <= query, ends, 0.0), axis=1, keepdims=True)
    key = (first_key + lax.broadcasted_iota(jnp.int32, (queries, keys), 1)).astype(jnp.float32)
    return jnp.where((key >= start) & (key <= query), 0.0, MASKED)


def bias_by_key(lengths_row, first_query, queries, first_key, keys):
    ends = module_ends_col(lengths_row)
    query = (first_query + lax.broadcasted_iota(jnp.int32, (1, queries), 1)).astype(jnp.float32)
    start = jnp.max(jnp.where(ends <= query, ends, 0.0), axis=0, keepdims=True)
    key = (first_key + lax.broadcasted_iota(jnp.int32, (keys, queries), 0)).astype(jnp.float32)
    return jnp.where((key >= start) & (key <= query), 0.0, MASKED)


def by_query(q, k, do, v, bias):
    scores = dot(q, k, 1, 1) * (SCALE * LOG2E) + bias
    return scores, dot(do, v, 1, 1)


def full_rows(pairs):
    tops = [jnp.max(s, axis=1, keepdims=True) for s, _ in pairs]
    raws = [jnp.exp2(s - top) for (s, _), top in zip(pairs, tops)]
    parts = [1.0 / jnp.sum(raw, axis=1, keepdims=True) for raw in raws]
    weights = [raw * part for raw, part in zip(raws, parts)]
    deltas = [jnp.sum(w * dp, axis=1, keepdims=True) for w, (_, dp) in zip(weights, pairs)]
    grads = [w * (dp - delta) * SCALE for w, (_, dp), delta in zip(weights, pairs, deltas)]
    return [w.astype(jnp.bfloat16) for w in weights], [g.astype(jnp.bfloat16) for g in grads]


def merged_rows(pairs, own):
    tops = [
        jnp.maximum(jnp.max(s, axis=0, keepdims=True), log) for (s, _), (log, _) in zip(pairs, own)
    ]
    raws = [jnp.exp2(s - top) for (s, _), top in zip(pairs, tops)]
    own_raws = [jnp.exp2(log - top) for (log, _), top in zip(own, tops)]
    parts = [
        1.0 / (jnp.sum(raw, axis=0, keepdims=True) + own_raw)
        for raw, own_raw in zip(raws, own_raws)
    ]
    weights = [raw * part for raw, part in zip(raws, parts)]
    deltas = [
        jnp.sum(w * dp, axis=0, keepdims=True) + own_raw * part * own_delta
        for w, (_, dp), own_raw, part, (_, own_delta) in zip(weights, pairs, own_raws, parts, own)
    ]
    grads = [w * (dp - delta) * SCALE for w, (_, dp), delta in zip(weights, pairs, deltas)]
    return [w.astype(jnp.bfloat16) for w in weights], [g.astype(jnp.bfloat16) for g in grads]


def head_columns(width):
    return [slice(c, c + HEAD_DIM) for c in range(0, width, HEAD_DIM)]


def device_first(tok):
    place = lax.axis_index("seq") * lax.axis_size("head") + lax.axis_index("head")
    return place * tok


def split_bf16(row):
    high = row.astype(jnp.bfloat16)
    low = (row - high.astype(jnp.float32)).astype(jnp.bfloat16)
    return jnp.concatenate([high, low], axis=1)


def joined(pair):
    pair = pair.astype(jnp.float32)
    half = pair.shape[1] // 2
    return pair[:, :half] + pair[:, half:]


def pack_kernel(prior, k_ref, v_ref, *refs):
    *packed_refs, sem = refs
    last = pl.ds(k_ref.shape[0] - prior, prior)
    copies = []
    for at, packed_ref in enumerate(packed_refs):
        width = packed_ref.shape[1]
        for half, ref in enumerate((k_ref, v_ref)):
            copies.append(
                pltpu.make_async_copy(
                    ref.at[last, pl.ds(at * width, width)],
                    packed_ref.at[pl.ds(half * prior, prior), :],
                    sem.at[2 * at + half],
                )
            )
    for copy in copies:
        copy.start()
    for copy in copies:
        copy.wait()


def own_kernel(
    prior, len_ref, q_ref, k_ref, v_ref, do_ref, attn_ref, gq_ref, gk_ref, gv_ref,
    lead_bias_ref, tail_bias_ref, *refs,
):
    *packed_refs, bias_ref, first_bias_ref = refs
    tok, width = k_ref.shape
    columns = head_columns(width)
    early, late = slice(0, prior), slice(tok - prior, tok)

    @pl.when(pl.program_id(0) == 0)
    def _():
        first = device_first(tok)
        lengths = len_ref[...].astype(jnp.float32)
        bias_ref[...] = bias_by_query(lengths, first + prior, tok - prior, first, tok)
        first_bias_ref[...] = bias_by_key(lengths, first, prior, first, prior)
        lead_bias_ref[...] = bias_by_query(lengths, first, prior, first - prior, 2 * prior)
        tail_bias_ref[...] = bias_by_key(lengths, first + tok, prior, first + tok - prior, prior)

    bias, first_bias = bias_ref[...], first_bias_ref[...]
    pairs = [
        by_query(q_ref[late, c], k_ref[:, c], do_ref[late, c], v_ref[:, c], bias) for c in columns
    ]
    firsts = [
        by_query(k_ref[early, c], q_ref[early, c], v_ref[early, c], do_ref[early, c], first_bias)
        for c in columns
    ]
    weights, grads = full_rows(pairs)
    for c, w, g in zip(columns, weights, grads):
        attn_ref[:, c] = dot(w, v_ref[:, c], 1, 0).astype(jnp.bfloat16)
        gq_ref[:, c] = dot(g, k_ref[:, c], 1, 0).astype(jnp.bfloat16)
        gk_ref[:, c] = dot(g, q_ref[late, c], 0, 0)
        gv_ref[:, c] = dot(w, do_ref[late, c], 0, 0)
    tops = [jnp.max(s, axis=0, keepdims=True) for s, _ in firsts]
    raws = [jnp.exp2(s - top) for (s, _), top in zip(firsts, tops)]
    totals = [jnp.sum(raw, axis=0, keepdims=True) for raw in raws]
    sums = [jnp.sum(raw * dp, axis=0, keepdims=True) for raw, (_, dp) in zip(raws, firsts)]
    logs = [split_bf16(top + jnp.log2(total)) for top, total in zip(tops, totals)]
    deltas = [split_bf16(summed / total) for summed, total in zip(sums, totals)]
    spare = lax.broadcasted_iota(jnp.int32, (prior, 1), 0) == prior - 1
    for at, packed_ref in enumerate(packed_refs):

        @pl.when(pl.program_id(0) == at)
        def _(packed_ref=packed_ref):
            for c, log, delta in zip(columns, logs, deltas):
                packed_ref[early, c] = jnp.where(spare, log, q_ref[early, c])
                packed_ref[prior : 2 * prior, c] = jnp.where(spare, delta, do_ref[early, c])


def lead_kernel(
    prior, bias_ref, q_ref, k_ref, v_ref, do_ref, before_ref, gk_part_ref, gv_part_ref, *refs
):
    attn_ref, gq_ref, gk_ref, gv_ref = refs[-4:]
    columns = head_columns(q_ref.shape[1])
    bias = bias_ref[...]
    early, late = slice(0, prior), slice(prior, 2 * prior)
    keys = [jnp.concatenate([before_ref[early, c], k_ref[:, c]], axis=0) for c in columns]
    values = [jnp.concatenate([before_ref[late, c], v_ref[:, c]], axis=0) for c in columns]
    pairs = [
        by_query(q_ref[:, c], k, do_ref[:, c], v, bias) for c, k, v in zip(columns, keys, values)
    ]
    weights, grads = full_rows(pairs)
    for c, w, g, k, v in zip(columns, weights, grads, keys, values):
        attn_ref[:, c] = dot(w, v, 1, 0).astype(jnp.bfloat16)
        gq_ref[:, c] = dot(g, k, 1, 0).astype(jnp.bfloat16)
        gk = gk_part_ref[:, c] + dot(g[:, late], q_ref[:, c], 0, 0)
        gv = gv_part_ref[:, c] + dot(w[:, late], do_ref[:, c], 0, 0)
        gk_ref[:, c] = gk.astype(jnp.bfloat16)
        gv_ref[:, c] = gv.astype(jnp.bfloat16)


def tail_kernel(
    prior, bias_ref, k_ref, v_ref, after_ref, gk_part_ref, gv_part_ref,
    gk_in, gv_in, gk_ref, gv_ref,
):
    columns = head_columns(k_ref.shape[1])
    bias = bias_ref[...]
    early, late = slice(0, prior), slice(prior, 2 * prior)
    pairs = [
        by_query(k_ref[:, c], after_ref[early, c], v_ref[:, c], after_ref[late, c], bias)
        for c in columns
    ]
    own = [
        (
            joined(after_ref[prior - 1 : prior, c]),
            joined(after_ref[2 * prior - 1 : 2 * prior, c]),
        )
        for c in columns
    ]
    weights, grads = merged_rows(pairs, own)
    for c, w, g in zip(columns, weights, grads):
        gk = gk_part_ref[:, c] + dot(g, after_ref[early, c], 1, 0)
        gv = gv_part_ref[:, c] + dot(w, after_ref[late, c], 1, 0)
        gk_ref[:, c] = gk.astype(jnp.bfloat16)
        gv_ref[:, c] = gv.astype(jnp.bfloat16)


def neighbour(value, by):
    peers = lax.axis_size("seq") * lax.axis_size("head")
    pairs = [(i, i + by) for i in range(peers) if 0 <= i + by < peers]
    return lax.ppermute(value, ("seq", "head"), pairs)


def cost(heads, queries, keys, products, moved):
    return pl.CostEstimate(
        flops=2 * heads * queries * keys * HEAD_DIM * products,
        bytes_accessed=moved,
        transcendentals=heads * queries * keys,
    )


def halo_shards(query_in, key_in, value_in, grad_out, module_lengths):
    tok, width = query_in.shape
    prior = tok * lax.axis_size("head") // 8
    step = math.gcd(width, 8 * HEAD_DIM)
    groups = width // step
    per = step // HEAD_DIM
    late_at = tok // prior - 1
    sent = 2 * prior
    lengths = module_lengths.reshape(1, -1)
    keep = pl.BlockSpec(memory_space=pl.ANY)
    full16 = jax.ShapeDtypeStruct((tok, width), jnp.bfloat16)
    full32 = jax.ShapeDtypeStruct((tok, width), jnp.float32)
    packed = jax.ShapeDtypeStruct((sent, step), jnp.bfloat16)
    lead_shape, tail_shape = (prior, 2 * prior), (prior, prior)

    def rows(count, at=0, base=0):
        return pl.BlockSpec((count, step), lambda g: (at, g + base))

    def fixed(*shape):
        return pl.BlockSpec(shape, lambda g: (0, 0))

    def call(kernel, name, grid, ins, outs, shapes, work, moved, aliases=None, scratch=()):
        return pl.pallas_call(
            functools.partial(kernel, prior),
            grid=(grid,),
            in_specs=ins,
            out_specs=outs,
            out_shape=shapes,
            scratch_shapes=scratch,
            input_output_aliases=aliases or {},
            cost_estimate=cost(grid * per, *work, moved * grid * step),
            compiler_params=pltpu.CompilerParams(vmem_limit_bytes=16 * 2**20),
            name=name,
        )

    befores = pl.pallas_call(
        functools.partial(pack_kernel, prior),
        in_specs=[pl.BlockSpec(memory_space=pltpu.HBM)] * 2,
        out_specs=[keep] * groups,
        out_shape=[packed] * groups,
        scratch_shapes=[pltpu.SemaphoreType.DMA((2 * groups,))],
        name="pack_late",
    )(key_in, value_in)
    befores = [neighbour(part, 1) for part in befores]

    attn, gq, gk_part, gv_part, lead_bias, tail_bias, *parts = call(
        own_kernel, "own_block", groups,
        [fixed(*lengths.shape), rows(tok), rows(tok), rows(tok), rows(tok)],
        [rows(prior, late_at), rows(prior, late_at), rows(tok), rows(tok)]
        + [fixed(*lead_shape), fixed(*tail_shape)] + [fixed(sent, step)] * groups,
        [full16, full16, full32, full32]
        + [jax.ShapeDtypeStruct(shape, jnp.float32) for shape in (lead_shape, tail_shape)]
        + [packed] * groups,
        (tok, tok, 4), 22 * tok,
        scratch=[
            pltpu.VMEM((tok - prior, tok), jnp.float32), pltpu.VMEM((prior, prior), jnp.float32)
        ],
    )(lengths, query_in, key_in, value_in, grad_out)
    outs = [attn, gq]
    afters = []
    for at, (part, before) in enumerate(zip(parts, befores)):
        part, before = lax.optimization_barrier((part, before))
        afters.append(neighbour(part, -1))
        outs = call(
            lead_kernel, "lead_rows", 1,
            [fixed(*lead_shape)] + [rows(prior, 0, at)] * 4
            + [rows(sent), rows(prior, 0, at), rows(prior, 0, at)] + [keep] * len(outs),
            [rows(prior, 0, at)] * 4, [full16] * 4, (prior, 2 * prior, 5), 14 * tok,
            {8 + i: i for i in range(len(outs))},
        )(lead_bias, query_in, key_in, value_in, grad_out, before, gk_part, gv_part, *outs)
    attn, gq, gk, gv = outs

    for at, after in enumerate(afters):
        late = rows(prior, late_at, at)
        gk, gv = call(
            tail_kernel, "tail_keys", 1,
            [fixed(*tail_shape), late, late, rows(sent), late, late, keep, keep],
            [late, late], [full16] * 2, (prior, prior, 4), 10 * tok, {6: 0, 7: 1},
        )(tail_bias, key_in, value_in, after, gk_part, gv_part, gk, gv)
    return (attn, gq, gk, gv)


def shards(query_in, key_in, value_in, grad_out, module_lengths):
    tok = query_in.shape[0]
    prior = tok * lax.axis_size("head") // 8
    plan = halo_shards if 2 * prior <= tok else gathered_shards
    return plan(query_in, key_in, value_in, grad_out, module_lengths)


def solution(mesh):
    placed = (
        P(("seq", "head"), None),
        P(("seq", "head"), None),
        P(("seq", "head"), None),
        P(("seq", "head"), None),
        P(),
    )
    return jax.shard_map(
        shards,
        mesh=mesh,
        in_specs=placed,
        out_specs=(
            P(("seq", "head"), None),
            P(("seq", "head"), None),
            P(("seq", "head"), None),
            P(("seq", "head"), None),
        ),
        check_vma=False,
    )
```

```python
import functools
import math

import jax
import jax.numpy as jnp
from jax import lax
from jax.experimental import pallas as pl
from jax.experimental.pallas import tpu as pltpu
from jax.sharding import PartitionSpec as P

HEAD_DIM = 128
SCALE = HEAD_DIM ** (-0.5)
LOG2E = math.log2(math.e)
MASKED = -1e30


def shifted(value, axis, by):
    peers = lax.axis_size(axis)
    pairs = [(i, i + by) for i in range(peers) if 0 <= i + by < peers]
    return lax.ppermute(value, axis, pairs)


def module_ids(module_lengths, positions):
    module_ends = jnp.cumsum(module_lengths)
    counted = jnp.sum((positions[:, None] >= module_ends[None, :]).astype(jnp.int32), axis=1)
    return jnp.where(positions >= 0, counted, -1)


def allowed_pairs(module_lengths, query_pos, key_pos):
    same = (
        module_ids(module_lengths, query_pos)[:, None]
        == module_ids(module_lengths, key_pos)[None, :]
    )
    return same & (key_pos[None, :] <= query_pos[:, None])


def score_grads(grad_rows, value_block, weights, row_delta, score_scale):
    dprobs = jnp.einsum("qd,kd->qk", grad_rows, value_block, preferred_element_type=jnp.float32)
    return (weights * (dprobs - row_delta[:, None]) * score_scale).astype(jnp.bfloat16)


def key_terms(dscores, weight_bf, query_rows, grad_rows):
    key_grad = jnp.einsum("qk,qd->kd", dscores, query_rows, preferred_element_type=jnp.float32)
    value_grad = jnp.einsum("qk,qd->kd", weight_bf, grad_rows, preferred_element_type=jnp.float32)
    return (key_grad, value_grad)


def one_block(query_rows, key_block, value_block, grad_rows, allowed, score_scale):
    scores = (
        jnp.einsum("qd,kd->qk", query_rows, key_block, preferred_element_type=jnp.float32)
        * score_scale
    )
    row_top = jnp.max(jnp.where(allowed, scores, -jnp.inf), axis=1, keepdims=True)
    row_total = jnp.sum(jnp.where(allowed, jnp.exp(scores - row_top), 0.0), axis=1, keepdims=True)
    log_total = row_top + jnp.log(row_total)
    weights = jnp.where(allowed, jnp.exp(scores - log_total), 0.0)
    weight_bf = weights.astype(jnp.bfloat16)
    attn_rows = jnp.einsum(
        "qk,kd->qd", weight_bf, value_block, preferred_element_type=jnp.float32
    ).astype(jnp.bfloat16)
    row_delta = jnp.sum(grad_rows.astype(jnp.float32) * attn_rows.astype(jnp.float32), axis=1)
    dscores = score_grads(grad_rows, value_block, weights, row_delta, score_scale)
    grad_q = jnp.einsum("qk,kd->qd", dscores, key_block, preferred_element_type=jnp.float32).astype(
        jnp.bfloat16
    )
    key_grad, value_grad = key_terms(dscores, weight_bf, query_rows, grad_rows)
    return (attn_rows, grad_q, key_grad, value_grad, log_total[:, 0], row_delta)


def gathered_shards(query_in, key_in, value_in, grad_out, module_lengths):
    head_q, head_k, head_v, head_do = (
        lax.all_to_all(query_in, "head", split_axis=1, concat_axis=0, tiled=True),
        lax.all_to_all(key_in, "head", split_axis=1, concat_axis=0, tiled=True),
        lax.all_to_all(value_in, "head", split_axis=1, concat_axis=0, tiled=True),
        lax.all_to_all(grad_out, "head", split_axis=1, concat_axis=0, tiled=True),
    )
    row_count = head_q.shape[0]
    width = head_q.shape[1]
    local_heads = width // HEAD_DIM
    prior_rows = row_count // 8
    score_scale = HEAD_DIM ** (-0.5)
    tail_start = row_count - prior_rows
    prior_k, prior_v = shifted((head_k[tail_start:], head_v[tail_start:]), "seq", 1)
    row_start = lax.axis_index("seq") * row_count
    query_pos = row_start + jnp.arange(row_count, dtype=jnp.int32)
    before_pos = row_start - prior_rows + jnp.arange(prior_rows, dtype=jnp.int32)
    key_pos = jnp.concatenate([before_pos, query_pos])
    block_rows = math.gcd(row_count, 512)
    block_count = row_count // block_rows
    pos_blocks = query_pos.reshape(block_count, block_rows)

    def by_head(flat, rows):
        return jnp.moveaxis(flat.reshape(rows, local_heads, HEAD_DIM), 1, 0)

    def to_flat(stacked):
        return jnp.moveaxis(stacked, 0, 1).reshape(stacked.shape[1], width)

    query_h = by_head(head_q, row_count)
    grad_h = by_head(head_do, row_count)
    key_h = by_head(jnp.concatenate([prior_k, head_k], axis=0), row_count + prior_rows)
    value_h = by_head(jnp.concatenate([prior_v, head_v], axis=0), row_count + prior_rows)

    def run_head(packed):
        query_rows, key_block, value_block, grad_rows = packed
        query_blocks = query_rows.reshape(block_count, block_rows, HEAD_DIM)
        grad_blocks = grad_rows.reshape(block_count, block_rows, HEAD_DIM)

        def run_block(inner):
            query_part, grad_part, pos_part = inner
            allowed = allowed_pairs(module_lengths, pos_part, key_pos)
            return one_block(query_part, key_block, value_block, grad_part, allowed, score_scale)

        attn_b, grad_qb, key_b, value_b, lse_b, delta_b = lax.map(
            run_block, (query_blocks, grad_blocks, pos_blocks)
        )
        return (
            attn_b.reshape(row_count, HEAD_DIM),
            grad_qb.reshape(row_count, HEAD_DIM),
            jnp.sum(key_b, axis=0),
            jnp.sum(value_b, axis=0),
            lse_b.reshape(row_count),
            delta_b.reshape(row_count),
        )

    attn_h, grad_qh, key_grad, value_grad, log_total, row_delta = lax.map(
        run_head, (query_h, key_h, value_h, grad_h)
    )
    attn_flat = to_flat(attn_h)
    attn_back = lax.all_to_all(attn_flat, "head", split_axis=0, concat_axis=1, tiled=True)
    grad_q = to_flat(grad_qh)
    later_k, later_v = shifted((key_grad[:, :prior_rows], value_grad[:, :prior_rows]), "seq", -1)
    key_total = key_grad[:, prior_rows:].at[:, tail_start:].add(later_k)
    value_total = value_grad[:, prior_rows:].at[:, tail_start:].add(later_v)
    grad_k = to_flat(key_total.astype(jnp.bfloat16))
    grad_v = to_flat(value_total.astype(jnp.bfloat16))
    back_q, back_k, back_v = (
        lax.all_to_all(grad_q, "head", split_axis=0, concat_axis=1, tiled=True),
        lax.all_to_all(grad_k, "head", split_axis=0, concat_axis=1, tiled=True),
        lax.all_to_all(grad_v, "head", split_axis=0, concat_axis=1, tiled=True),
    )
    return (attn_back, back_q, back_k, back_v)


def dot(left, right, left_dim, right_dim):
    return lax.dot_general(
        left, right, (((left_dim,), (right_dim,)), ((), ())), preferred_element_type=jnp.float32
    )


def module_ends_row(lengths_row):
    count = lengths_row.shape[1]
    row = lax.broadcasted_iota(jnp.int32, (count, count), 0)
    col = lax.broadcasted_iota(jnp.int32, (count, count), 1)
    lengths_col = jnp.sum(jnp.where(row == col, lengths_row, 0.0), axis=1, keepdims=True)
    return jnp.sum(jnp.where(row <= col, lengths_col, 0.0), axis=0, keepdims=True)


def module_ends_col(lengths_row):
    count = lengths_row.shape[1]
    row = lax.broadcasted_iota(jnp.int32, (count, count), 0)
    col = lax.broadcasted_iota(jnp.int32, (count, count), 1)
    return jnp.sum(jnp.where(col <= row, lengths_row, 0.0), axis=1, keepdims=True)


def bias_by_query(lengths_row, first_query, queries, first_key, keys):
    ends = module_ends_row(lengths_row)
    query = (first_query + lax.broadcasted_iota(jnp.int32, (queries, 1), 0)).astype(jnp.float32)
    start = jnp.max(jnp.where(ends <= query, ends, 0.0), axis=1, keepdims=True)
    key = (first_key + lax.broadcasted_iota(jnp.int32, (queries, keys), 1)).astype(jnp.float32)
    return jnp.where((key >= start) & (key <= query), 0.0, MASKED)


def bias_by_key(lengths_row, first_query, queries, first_key, keys):
    ends = module_ends_col(lengths_row)
    query = (first_query + lax.broadcasted_iota(jnp.int32, (1, queries), 1)).astype(jnp.float32)
    start = jnp.max(jnp.where(ends <= query, ends, 0.0), axis=0, keepdims=True)
    key = (first_key + lax.broadcasted_iota(jnp.int32, (keys, queries), 0)).astype(jnp.float32)
    return jnp.where((key >= start) & (key <= query), 0.0, MASKED)


def by_query(q, k, do, v, bias):
    scores = dot(q, k, 1, 1) * (SCALE * LOG2E) + bias
    return scores, dot(do, v, 1, 1)


def full_rows(pairs):
    tops = [jnp.max(s, axis=1, keepdims=True) for s, _ in pairs]
    raws = [jnp.exp2(s - top) for (s, _), top in zip(pairs, tops)]
    parts = [1.0 / jnp.sum(raw, axis=1, keepdims=True) for raw in raws]
    weights = [raw * part for raw, part in zip(raws, parts)]
    deltas = [jnp.sum(w * dp, axis=1, keepdims=True) for w, (_, dp) in zip(weights, pairs)]
    grads = [w * (dp - delta) * SCALE for w, (_, dp), delta in zip(weights, pairs, deltas)]
    return [w.astype(jnp.bfloat16) for w in weights], [g.astype(jnp.bfloat16) for g in grads]


def merged_rows(pairs, own):
    tops = [
        jnp.maximum(jnp.max(s, axis=0, keepdims=True), log) for (s, _), (log, _) in zip(pairs, own)
    ]
    raws = [jnp.exp2(s - top) for (s, _), top in zip(pairs, tops)]
    own_raws = [jnp.exp2(log - top) for (log, _), top in zip(own, tops)]
    parts = [
        1.0 / (jnp.sum(raw, axis=0, keepdims=True) + own_raw)
        for raw, own_raw in zip(raws, own_raws)
    ]
    weights = [raw * part for raw, part in zip(raws, parts)]
    deltas = [
        jnp.sum(w * dp, axis=0, keepdims=True) + own_raw * part * own_delta
        for w, (_, dp), own_raw, part, (_, own_delta) in zip(weights, pairs, own_raws, parts, own)
    ]
    grads = [w * (dp - delta) * SCALE for w, (_, dp), delta in zip(weights, pairs, deltas)]
    return [w.astype(jnp.bfloat16) for w in weights], [g.astype(jnp.bfloat16) for g in grads]


def head_columns(width):
    return [slice(c, c + HEAD_DIM) for c in range(0, width, HEAD_DIM)]


def device_first(tok):
    place = lax.axis_index("seq") * lax.axis_size("head") + lax.axis_index("head")
    return place * tok


def split_bf16(row):
    high = row.astype(jnp.bfloat16)
    low = (row - high.astype(jnp.float32)).astype(jnp.bfloat16)
    return jnp.concatenate([high, low], axis=1)


def joined(pair):
    pair = pair.astype(jnp.float32)
    half = pair.shape[1] // 2
    return pair[:, :half] + pair[:, half:]


def own_kernel(
    prior, len_ref, q_ref, k_ref, v_ref, do_ref, attn_ref, gq_ref, gk_ref, gv_ref,
    lead_bias_ref, tail_bias_ref, *refs,
):
    *packed_refs, bias_ref, first_bias_ref = refs
    tok, width = k_ref.shape
    columns = head_columns(width)
    early, late = slice(0, prior), slice(tok - prior, tok)

    @pl.when(pl.program_id(0) == 0)
    def _():
        first = device_first(tok)
        lengths = len_ref[...].astype(jnp.float32)
        bias_ref[...] = bias_by_query(lengths, first + prior, tok - prior, first, tok)
        first_bias_ref[...] = bias_by_key(lengths, first, prior, first, prior)
        lead_bias_ref[...] = bias_by_query(lengths, first, prior, first - prior, 2 * prior)
        tail_bias_ref[...] = bias_by_key(lengths, first + tok, prior, first + tok - prior, prior)

    bias, first_bias = bias_ref[...], first_bias_ref[...]
    pairs = [
        by_query(q_ref[late, c], k_ref[:, c], do_ref[late, c], v_ref[:, c], bias) for c in columns
    ]
    firsts = [
        by_query(k_ref[early, c], q_ref[early, c], v_ref[early, c], do_ref[early, c], first_bias)
        for c in columns
    ]
    weights, grads = full_rows(pairs)
    for c, w, g in zip(columns, weights, grads):
        attn_ref[:, c] = dot(w, v_ref[:, c], 1, 0).astype(jnp.bfloat16)
        gq_ref[:, c] = dot(g, k_ref[:, c], 1, 0).astype(jnp.bfloat16)
        gk_ref[:, c] = dot(g, q_ref[late, c], 0, 0)
        gv_ref[:, c] = dot(w, do_ref[late, c], 0, 0)
    tops = [jnp.max(s, axis=0, keepdims=True) for s, _ in firsts]
    raws = [jnp.exp2(s - top) for (s, _), top in zip(firsts, tops)]
    totals = [jnp.sum(raw, axis=0, keepdims=True) for raw in raws]
    sums = [jnp.sum(raw * dp, axis=0, keepdims=True) for raw, (_, dp) in zip(raws, firsts)]
    logs = [split_bf16(top + jnp.log2(total)) for top, total in zip(tops, totals)]
    deltas = [split_bf16(summed / total) for summed, total in zip(sums, totals)]
    spare = lax.broadcasted_iota(jnp.int32, (prior, 1), 0) == prior - 1
    for at, packed_ref in enumerate(packed_refs):

        @pl.when(pl.program_id(0) == at)
        def _(packed_ref=packed_ref):
            for c, log, delta in zip(columns, logs, deltas):
                packed_ref[early, c] = jnp.where(spare, log, q_ref[early, c])
                packed_ref[prior : 2 * prior, c] = jnp.where(spare, delta, do_ref[early, c])


def lead_kernel(
    prior, bias_ref, q_ref, k_ref, v_ref, do_ref, before_ref, gk_part_ref, gv_part_ref, *refs
):
    attn_ref, gq_ref, gk_ref, gv_ref = refs[-4:]
    columns = head_columns(q_ref.shape[1])
    bias = bias_ref[...]
    early, late = slice(0, prior), slice(prior, 2 * prior)
    keys = [jnp.concatenate([before_ref[early, c], k_ref[:, c]], axis=0) for c in columns]
    values = [jnp.concatenate([before_ref[late, c], v_ref[:, c]], axis=0) for c in columns]
    pairs = [
        by_query(q_ref[:, c], k, do_ref[:, c], v, bias) for c, k, v in zip(columns, keys, values)
    ]
    weights, grads = full_rows(pairs)
    for c, w, g, k, v in zip(columns, weights, grads, keys, values):
        attn_ref[:, c] = dot(w, v, 1, 0).astype(jnp.bfloat16)
        gq_ref[:, c] = dot(g, k, 1, 0).astype(jnp.bfloat16)
        gk = gk_part_ref[:, c] + dot(g[:, late], q_ref[:, c], 0, 0)
        gv = gv_part_ref[:, c] + dot(w[:, late], do_ref[:, c], 0, 0)
        gk_ref[:, c] = gk.astype(jnp.bfloat16)
        gv_ref[:, c] = gv.astype(jnp.bfloat16)


def tail_kernel(
    prior, bias_ref, k_ref, v_ref, after_ref, gk_part_ref, gv_part_ref,
    gk_in, gv_in, gk_ref, gv_ref,
):
    columns = head_columns(k_ref.shape[1])
    bias = bias_ref[...]
    early, late = slice(0, prior), slice(prior, 2 * prior)
    pairs = [
        by_query(k_ref[:, c], after_ref[early, c], v_ref[:, c], after_ref[late, c], bias)
        for c in columns
    ]
    own = [
        (
            joined(after_ref[prior - 1 : prior, c]),
            joined(after_ref[2 * prior - 1 : 2 * prior, c]),
        )
        for c in columns
    ]
    weights, grads = merged_rows(pairs, own)
    for c, w, g in zip(columns, weights, grads):
        gk = gk_part_ref[:, c] + dot(g, after_ref[early, c], 1, 0)
        gv = gv_part_ref[:, c] + dot(w, after_ref[late, c], 1, 0)
        gk_ref[:, c] = gk.astype(jnp.bfloat16)
        gv_ref[:, c] = gv.astype(jnp.bfloat16)


def neighbour(value, by):
    peers = lax.axis_size("seq") * lax.axis_size("head")
    pairs = [(i, i + by) for i in range(peers) if 0 <= i + by < peers]
    return lax.ppermute(value, ("seq", "head"), pairs)


def cost(heads, queries, keys, products, moved):
    return pl.CostEstimate(
        flops=2 * heads * queries * keys * HEAD_DIM * products,
        bytes_accessed=moved,
        transcendentals=heads * queries * keys,
    )


def halo_shards(query_in, key_in, value_in, grad_out, module_lengths):
    tok, width = query_in.shape
    prior = tok * lax.axis_size("head") // 8
    step = math.gcd(width, 8 * HEAD_DIM)
    groups = width // step
    per = step // HEAD_DIM
    late_at = tok // prior - 1
    sent = 2 * prior
    lengths = module_lengths.reshape(1, -1)
    keep = pl.BlockSpec(memory_space=pl.ANY)
    full16 = jax.ShapeDtypeStruct((tok, width), jnp.bfloat16)
    full32 = jax.ShapeDtypeStruct((tok, width), jnp.float32)
    packed = jax.ShapeDtypeStruct((sent, step), jnp.bfloat16)
    lead_shape, tail_shape = (prior, 2 * prior), (prior, prior)

    def rows(count, at=0, base=0):
        return pl.BlockSpec((count, step), lambda g: (at, g + base))

    def fixed(*shape):
        return pl.BlockSpec(shape, lambda g: (0, 0))

    def call(kernel, name, grid, ins, outs, shapes, work, moved, aliases=None, scratch=(), room=16):
        return pl.pallas_call(
            functools.partial(kernel, prior),
            grid=(grid,),
            in_specs=ins,
            out_specs=outs,
            out_shape=shapes,
            scratch_shapes=scratch,
            input_output_aliases=aliases or {},
            cost_estimate=cost(grid * per, *work, moved * grid * step),
            compiler_params=pltpu.CompilerParams(vmem_limit_bytes=room * 2**20),
            name=name,
        )

    befores = []
    for at in range(groups):
        cols = slice(at * step, (at + 1) * step)
        late_kv = [key_in[tok - prior :, cols], value_in[tok - prior :, cols]]
        befores.append(neighbour(jnp.concatenate(late_kv), 1))

    attn, gq, gk_part, gv_part, lead_bias, tail_bias, *parts = call(
        own_kernel, "own_block", groups,
        [fixed(*lengths.shape), rows(tok), rows(tok), rows(tok), rows(tok)],
        [rows(prior, late_at), rows(prior, late_at), rows(tok), rows(tok)]
        + [fixed(*lead_shape), fixed(*tail_shape)] + [fixed(sent, step)] * groups,
        [full16, full16, full32, full32]
        + [jax.ShapeDtypeStruct(shape, jnp.float32) for shape in (lead_shape, tail_shape)]
        + [packed] * groups,
        (tok, tok, 4), 22 * tok,
        scratch=[
            pltpu.VMEM((tok - prior, tok), jnp.float32), pltpu.VMEM((prior, prior), jnp.float32)
        ],
        room=56,
    )(lengths, query_in, key_in, value_in, grad_out)
    outs = [attn, gq]
    afters = []
    for at, (part, before) in enumerate(zip(parts, befores)):
        part, before = lax.optimization_barrier((part, before))
        afters.append(neighbour(part, -1))
        outs = call(
            lead_kernel, "lead_rows", 1,
            [fixed(*lead_shape)] + [rows(prior, 0, at)] * 4
            + [rows(sent), rows(prior, 0, at), rows(prior, 0, at)] + [keep] * len(outs),
            [rows(prior, 0, at)] * 4, [full16] * 4, (prior, 2 * prior, 5), 14 * tok,
            {8 + i: i for i in range(len(outs))},
        )(lead_bias, query_in, key_in, value_in, grad_out, before, gk_part, gv_part, *outs)
    attn, gq, gk, gv = outs

    for at, after in enumerate(afters):
        late = rows(prior, late_at, at)
        gk, gv = call(
            tail_kernel, "tail_keys", 1,
            [fixed(*tail_shape), late, late, rows(sent), late, late, keep, keep],
            [late, late], [full16] * 2, (prior, prior, 4), 10 * tok, {6: 0, 7: 1},
        )(tail_bias, key_in, value_in, after, gk_part, gv_part, gk, gv)
    return (attn, gq, gk, gv)


def shards(query_in, key_in, value_in, grad_out, module_lengths):
    tok = query_in.shape[0]
    prior = tok * lax.axis_size("head") // 8
    plan = halo_shards if 2 * prior <= tok else gathered_shards
    return plan(query_in, key_in, value_in, grad_out, module_lengths)


def solution(mesh):
    placed = (
        P(("seq", "head"), None),
        P(("seq", "head"), None),
        P(("seq", "head"), None),
        P(("seq", "head"), None),
        P(),
    )
    return jax.shard_map(
        shards,
        mesh=mesh,
        in_specs=placed,
        out_specs=(
            P(("seq", "head"), None),
            P(("seq", "head"), None),
            P(("seq", "head"), None),
            P(("seq", "head"), None),
        ),
        check_vma=False,
    )
```

```python
import functools
import math

import jax
import jax.numpy as jnp
from jax import lax
from jax.experimental import pallas as pl
from jax.experimental.pallas import tpu as pltpu
from jax.sharding import PartitionSpec as P

HEAD_DIM = 128
SCALE = HEAD_DIM ** (-0.5)
LOG2E = math.log2(math.e)
MASKED = -1e30


def shifted(value, axis, by):
    peers = lax.axis_size(axis)
    pairs = [(i, i + by) for i in range(peers) if 0 <= i + by < peers]
    return lax.ppermute(value, axis, pairs)


def module_ids(module_lengths, positions):
    module_ends = jnp.cumsum(module_lengths)
    counted = jnp.sum((positions[:, None] >= module_ends[None, :]).astype(jnp.int32), axis=1)
    return jnp.where(positions >= 0, counted, -1)


def allowed_pairs(module_lengths, query_pos, key_pos):
    same = (
        module_ids(module_lengths, query_pos)[:, None]
        == module_ids(module_lengths, key_pos)[None, :]
    )
    return same & (key_pos[None, :] <= query_pos[:, None])


def score_grads(grad_rows, value_block, weights, row_delta, score_scale):
    dprobs = jnp.einsum("qd,kd->qk", grad_rows, value_block, preferred_element_type=jnp.float32)
    return (weights * (dprobs - row_delta[:, None]) * score_scale).astype(jnp.bfloat16)


def key_terms(dscores, weight_bf, query_rows, grad_rows):
    key_grad = jnp.einsum("qk,qd->kd", dscores, query_rows, preferred_element_type=jnp.float32)
    value_grad = jnp.einsum("qk,qd->kd", weight_bf, grad_rows, preferred_element_type=jnp.float32)
    return (key_grad, value_grad)


def one_block(query_rows, key_block, value_block, grad_rows, allowed, score_scale):
    scores = (
        jnp.einsum("qd,kd->qk", query_rows, key_block, preferred_element_type=jnp.float32)
        * score_scale
    )
    row_top = jnp.max(jnp.where(allowed, scores, -jnp.inf), axis=1, keepdims=True)
    row_total = jnp.sum(jnp.where(allowed, jnp.exp(scores - row_top), 0.0), axis=1, keepdims=True)
    log_total = row_top + jnp.log(row_total)
    weights = jnp.where(allowed, jnp.exp(scores - log_total), 0.0)
    weight_bf = weights.astype(jnp.bfloat16)
    attn_rows = jnp.einsum(
        "qk,kd->qd", weight_bf, value_block, preferred_element_type=jnp.float32
    ).astype(jnp.bfloat16)
    row_delta = jnp.sum(grad_rows.astype(jnp.float32) * attn_rows.astype(jnp.float32), axis=1)
    dscores = score_grads(grad_rows, value_block, weights, row_delta, score_scale)
    grad_q = jnp.einsum("qk,kd->qd", dscores, key_block, preferred_element_type=jnp.float32).astype(
        jnp.bfloat16
    )
    key_grad, value_grad = key_terms(dscores, weight_bf, query_rows, grad_rows)
    return (attn_rows, grad_q, key_grad, value_grad, log_total[:, 0], row_delta)


def gathered_shards(query_in, key_in, value_in, grad_out, module_lengths):
    head_q, head_k, head_v, head_do = (
        lax.all_to_all(query_in, "head", split_axis=1, concat_axis=0, tiled=True),
        lax.all_to_all(key_in, "head", split_axis=1, concat_axis=0, tiled=True),
        lax.all_to_all(value_in, "head", split_axis=1, concat_axis=0, tiled=True),
        lax.all_to_all(grad_out, "head", split_axis=1, concat_axis=0, tiled=True),
    )
    row_count = head_q.shape[0]
    width = head_q.shape[1]
    local_heads = width // HEAD_DIM
    prior_rows = row_count // 8
    score_scale = HEAD_DIM ** (-0.5)
    tail_start = row_count - prior_rows
    prior_k, prior_v = shifted((head_k[tail_start:], head_v[tail_start:]), "seq", 1)
    row_start = lax.axis_index("seq") * row_count
    query_pos = row_start + jnp.arange(row_count, dtype=jnp.int32)
    before_pos = row_start - prior_rows + jnp.arange(prior_rows, dtype=jnp.int32)
    key_pos = jnp.concatenate([before_pos, query_pos])
    block_rows = math.gcd(row_count, 512)
    block_count = row_count // block_rows
    pos_blocks = query_pos.reshape(block_count, block_rows)

    def by_head(flat, rows):
        return jnp.moveaxis(flat.reshape(rows, local_heads, HEAD_DIM), 1, 0)

    def to_flat(stacked):
        return jnp.moveaxis(stacked, 0, 1).reshape(stacked.shape[1], width)

    query_h = by_head(head_q, row_count)
    grad_h = by_head(head_do, row_count)
    key_h = by_head(jnp.concatenate([prior_k, head_k], axis=0), row_count + prior_rows)
    value_h = by_head(jnp.concatenate([prior_v, head_v], axis=0), row_count + prior_rows)

    def run_head(packed):
        query_rows, key_block, value_block, grad_rows = packed
        query_blocks = query_rows.reshape(block_count, block_rows, HEAD_DIM)
        grad_blocks = grad_rows.reshape(block_count, block_rows, HEAD_DIM)

        def run_block(inner):
            query_part, grad_part, pos_part = inner
            allowed = allowed_pairs(module_lengths, pos_part, key_pos)
            return one_block(query_part, key_block, value_block, grad_part, allowed, score_scale)

        attn_b, grad_qb, key_b, value_b, lse_b, delta_b = lax.map(
            run_block, (query_blocks, grad_blocks, pos_blocks)
        )
        return (
            attn_b.reshape(row_count, HEAD_DIM),
            grad_qb.reshape(row_count, HEAD_DIM),
            jnp.sum(key_b, axis=0),
            jnp.sum(value_b, axis=0),
            lse_b.reshape(row_count),
            delta_b.reshape(row_count),
        )

    attn_h, grad_qh, key_grad, value_grad, log_total, row_delta = lax.map(
        run_head, (query_h, key_h, value_h, grad_h)
    )
    attn_flat = to_flat(attn_h)
    attn_back = lax.all_to_all(attn_flat, "head", split_axis=0, concat_axis=1, tiled=True)
    grad_q = to_flat(grad_qh)
    later_k, later_v = shifted((key_grad[:, :prior_rows], value_grad[:, :prior_rows]), "seq", -1)
    key_total = key_grad[:, prior_rows:].at[:, tail_start:].add(later_k)
    value_total = value_grad[:, prior_rows:].at[:, tail_start:].add(later_v)
    grad_k = to_flat(key_total.astype(jnp.bfloat16))
    grad_v = to_flat(value_total.astype(jnp.bfloat16))
    back_q, back_k, back_v = (
        lax.all_to_all(grad_q, "head", split_axis=0, concat_axis=1, tiled=True),
        lax.all_to_all(grad_k, "head", split_axis=0, concat_axis=1, tiled=True),
        lax.all_to_all(grad_v, "head", split_axis=0, concat_axis=1, tiled=True),
    )
    return (attn_back, back_q, back_k, back_v)


def dot(left, right, left_dim, right_dim):
    return lax.dot_general(
        left, right, (((left_dim,), (right_dim,)), ((), ())), preferred_element_type=jnp.float32
    )


def module_ends_row(lengths_row):
    count = lengths_row.shape[1]
    row = lax.broadcasted_iota(jnp.int32, (count, count), 0)
    col = lax.broadcasted_iota(jnp.int32, (count, count), 1)
    lengths_col = jnp.sum(jnp.where(row == col, lengths_row, 0.0), axis=1, keepdims=True)
    return jnp.sum(jnp.where(row <= col, lengths_col, 0.0), axis=0, keepdims=True)


def module_ends_col(lengths_row):
    count = lengths_row.shape[1]
    row = lax.broadcasted_iota(jnp.int32, (count, count), 0)
    col = lax.broadcasted_iota(jnp.int32, (count, count), 1)
    return jnp.sum(jnp.where(col <= row, lengths_row, 0.0), axis=1, keepdims=True)


def bias_by_query(lengths_row, first_query, queries, first_key, keys):
    ends = module_ends_row(lengths_row)
    query = (first_query + lax.broadcasted_iota(jnp.int32, (queries, 1), 0)).astype(jnp.float32)
    start = jnp.max(jnp.where(ends <= query, ends, 0.0), axis=1, keepdims=True)
    key = (first_key + lax.broadcasted_iota(jnp.int32, (queries, keys), 1)).astype(jnp.float32)
    return jnp.where((key >= start) & (key <= query), 0.0, MASKED)


def bias_by_key(lengths_row, first_query, queries, first_key, keys):
    ends = module_ends_col(lengths_row)
    query = (first_query + lax.broadcasted_iota(jnp.int32, (1, queries), 1)).astype(jnp.float32)
    start = jnp.max(jnp.where(ends <= query, ends, 0.0), axis=0, keepdims=True)
    key = (first_key + lax.broadcasted_iota(jnp.int32, (keys, queries), 0)).astype(jnp.float32)
    return jnp.where((key >= start) & (key <= query), 0.0, MASKED)


def by_query(q, k, do, v, bias):
    scores = dot(q, k, 1, 1) * (SCALE * LOG2E) + bias
    return scores, dot(do, v, 1, 1)


def full_rows(pairs):
    tops = [jnp.max(s, axis=1, keepdims=True) for s, _ in pairs]
    raws = [jnp.exp2(s - top) for (s, _), top in zip(pairs, tops)]
    totals = [jnp.sum(raw, axis=1, keepdims=True) for raw in raws]
    weights = [raw * (1.0 / total) for raw, total in zip(raws, totals)]
    deltas = [jnp.sum(w * dp, axis=1, keepdims=True) for w, (_, dp) in zip(weights, pairs)]
    grads = [w * (dp - delta) * SCALE for w, (_, dp), delta in zip(weights, pairs, deltas)]
    logs = [top + jnp.log2(total) for top, total in zip(tops, totals)]
    return (
        [w.astype(jnp.bfloat16) for w in weights],
        [g.astype(jnp.bfloat16) for g in grads],
        logs,
        deltas,
    )


def head_columns(width):
    return [slice(c, c + HEAD_DIM) for c in range(0, width, HEAD_DIM)]


def device_first(tok):
    place = lax.axis_index("seq") * lax.axis_size("head") + lax.axis_index("head")
    return place * tok


def as_rows(columns):
    count = columns[0].shape[0]
    lane = lax.broadcasted_iota(jnp.int32, (count, HEAD_DIM), 1)
    table = jnp.zeros((count, HEAD_DIM), jnp.float32)
    for at, column in enumerate(columns):
        table = jnp.where(lane == at, column, table)
    fill = jnp.zeros((HEAD_DIM - count, HEAD_DIM), jnp.float32)
    table = jnp.transpose(jnp.concatenate([table, fill], axis=0))
    return [table[at : at + 1, :count] for at in range(len(columns))]


def split_bf16(row):
    parts = []
    for _ in range(3):
        part = row.astype(jnp.bfloat16)
        parts.append(part)
        row = row - part.astype(jnp.float32)
    return jnp.concatenate([*parts, jnp.zeros_like(parts[0])], axis=1)


def joined(parts):
    parts = parts.astype(jnp.float32)
    count = parts.shape[1] // 4
    return parts[:, :count] + parts[:, count : 2 * count] + parts[:, 2 * count : 3 * count]


def own_kernel(
    prior, len_ref, q_ref, k_ref, v_ref, do_ref, attn_ref, gq_ref, gk_ref, gv_ref,
    lead_bias_ref, tail_bias_ref, bias_ref,
):
    tok, width = k_ref.shape
    columns = head_columns(width)

    @pl.when(pl.program_id(0) == 0)
    def _():
        first = device_first(tok)
        lengths = len_ref[...].astype(jnp.float32)
        bias_ref[...] = bias_by_query(lengths, first + prior, tok - prior, first, tok)
        lead_bias_ref[...] = bias_by_query(lengths, first, prior, first - prior, 2 * prior)
        tail_bias_ref[...] = bias_by_key(
            lengths, first + tok, prior // 2, first + tok - prior, prior
        )

    bias = bias_ref[...]
    pairs = [by_query(q_ref[:, c], k_ref[:, c], do_ref[:, c], v_ref[:, c], bias) for c in columns]
    weights, grads, _, _ = full_rows(pairs)
    for c, w, g in zip(columns, weights, grads):
        attn_ref[:, c] = dot(w, v_ref[:, c], 1, 0).astype(jnp.bfloat16)
        gq_ref[:, c] = dot(g, k_ref[:, c], 1, 0).astype(jnp.bfloat16)
        gk_ref[:, c] = dot(g, q_ref[:, c], 0, 0)
        gv_ref[:, c] = dot(w, do_ref[:, c], 0, 0)


def lead_kernel(
    prior, bias_ref, q_ref, k_ref, v_ref, do_ref, before_ref, gk_part_ref, gv_part_ref, *refs
):
    attn_ref, gq_ref, gk_ref, gv_ref, back_ref = refs[-5:]
    columns = head_columns(q_ref.shape[1])
    half = prior // 2
    bias = bias_ref[...]
    many = bias_ref[half - 1 : half, prior - 1 : prior] == 0.0
    spare = lax.broadcasted_iota(jnp.int32, (half, 1), 0) == half - 1
    early, late = slice(0, prior), slice(prior, 2 * prior)
    keys = [jnp.concatenate([before_ref[early, c], k_ref[:, c]], axis=0) for c in columns]
    values = [jnp.concatenate([before_ref[late, c], v_ref[:, c]], axis=0) for c in columns]
    pairs = [
        by_query(q_ref[:, c], k, do_ref[:, c], v, bias) for c, k, v in zip(columns, keys, values)
    ]
    weights, grads, logs, deltas = full_rows(pairs)
    rows = as_rows([column[:half] for column in logs + deltas])
    logs, deltas = rows[: len(columns)], rows[len(columns) :]
    for c, w, g, k, v, log, delta in zip(columns, weights, grads, keys, values, logs, deltas):
        attn_ref[:, c] = dot(w, v, 1, 0).astype(jnp.bfloat16)
        gq_ref[:, c] = dot(g, k, 1, 0).astype(jnp.bfloat16)
        gk = dot(g, q_ref[:, c], 0, 0)
        gv = dot(w, do_ref[:, c], 0, 0)
        gk_ref[:, c] = (gk_part_ref[:, c] + gk[prior:]).astype(jnp.bfloat16)
        gv_ref[:, c] = (gv_part_ref[:, c] + gv[prior:]).astype(jnp.bfloat16)
        few_q = jnp.where(spare, split_bf16(log), q_ref[:half, c])
        few_do = jnp.where(spare, split_bf16(delta), do_ref[:half, c])
        back_ref[:half, c] = jnp.where(many, gk[half:prior].astype(jnp.bfloat16), few_q)
        back_ref[half:, c] = jnp.where(many, gv[half:prior].astype(jnp.bfloat16), few_do)


def tail_kernel(
    prior, bias_ref, k_ref, v_ref, after_ref, gk_part_ref, gv_part_ref,
    gk_in, gv_in, gk_ref, gv_ref,
):
    columns = head_columns(k_ref.shape[1])
    half = prior // 2
    many = bias_ref[prior - 1 : prior, half - 1 : half] == 0.0
    bias = jnp.where(many, MASKED, bias_ref[...])
    first, second = slice(0, half), slice(half, prior)
    pairs = [
        by_query(k_ref[:, c], after_ref[first, c], v_ref[:, c], after_ref[second, c], bias)
        for c in columns
    ]
    weights = [
        jnp.exp2(s - joined(after_ref[half - 1 : half, c])) for (s, _), c in zip(pairs, columns)
    ]
    grads = [
        w * (dp - joined(after_ref[prior - 1 : prior, c])) * SCALE
        for w, (_, dp), c in zip(weights, pairs, columns)
    ]
    for c, w, g in zip(columns, weights, grads):
        for out_ref, part_ref, left, rows in (
            (gk_ref, gk_part_ref, g, first), (gv_ref, gv_part_ref, w, second)
        ):
            came = after_ref[rows, c]
            total = part_ref[:, c] + dot(left.astype(jnp.bfloat16), came, 1, 0)
            terms = jnp.where(many, came.astype(jnp.float32), 0.0)
            out_ref[first, c] = total[first].astype(jnp.bfloat16)
            out_ref[second, c] = (total[second] + terms).astype(jnp.bfloat16)


def neighbour(value, by):
    peers = lax.axis_size("seq") * lax.axis_size("head")
    pairs = [(i, i + by) for i in range(peers) if 0 <= i + by < peers]
    return lax.ppermute(value, ("seq", "head"), pairs)


def cost(heads, queries, keys, products, moved):
    return pl.CostEstimate(
        flops=2 * heads * queries * keys * HEAD_DIM * products,
        bytes_accessed=moved,
        transcendentals=heads * queries * keys,
    )


def halo_shards(query_in, key_in, value_in, grad_out, module_lengths):
    tok, width = query_in.shape
    prior = tok * lax.axis_size("head") // 8
    step = math.gcd(width, 8 * HEAD_DIM)
    groups = width // step
    per = step // HEAD_DIM
    late_at = tok // prior - 1
    lengths = module_lengths.reshape(1, -1)
    keep = pl.BlockSpec(memory_space=pl.ANY)
    full16 = jax.ShapeDtypeStruct((tok, width), jnp.bfloat16)
    part32 = pltpu.VMEM((tok, width), jnp.float32)
    back16 = jax.ShapeDtypeStruct((prior, step), jnp.bfloat16)
    lead_shape, tail_shape = (prior, 2 * prior), (prior, prior // 2)

    def rows(count, at=0, base=0):
        return pl.BlockSpec((count, step), lambda g: (at, g + base))

    def fixed(*shape):
        return pl.BlockSpec(shape, lambda g: (0, 0))

    def call(kernel, name, grid, ins, outs, shapes, work, moved, aliases=None, scratch=()):
        return pl.pallas_call(
            functools.partial(kernel, prior),
            grid=(grid,),
            in_specs=ins,
            out_specs=outs,
            out_shape=shapes,
            scratch_shapes=scratch,
            input_output_aliases=aliases or {},
            cost_estimate=cost(grid * per, *work, moved * grid * step),
            compiler_params=pltpu.CompilerParams(vmem_limit_bytes=16 * 2**20),
            name=name,
        )

    befores = []
    for at in range(groups):
        cols = slice(at * step, (at + 1) * step)
        late_kv = [key_in[tok - prior :, cols], value_in[tok - prior :, cols]]
        befores.append(neighbour(jnp.concatenate(late_kv), 1))

    in_hbm = [
        pltpu.with_memory_space_constraint(value, pltpu.HBM)
        for value in (query_in, key_in, value_in, grad_out)
    ]
    attn, gq, gk_part, gv_part, lead_bias, tail_bias = call(
        own_kernel, "own_block", groups,
        [fixed(*lengths.shape), rows(prior, late_at), rows(tok), rows(tok), rows(prior, late_at)],
        [rows(prior, late_at), rows(prior, late_at), rows(tok), rows(tok)]
        + [fixed(*lead_shape), fixed(*tail_shape)],
        [full16, full16, part32, part32]
        + [pltpu.VMEM(shape, jnp.float32) for shape in (lead_shape, tail_shape)],
        (tok - prior, tok, 6), 18 * tok,
        scratch=[pltpu.VMEM((tok - prior, tok), jnp.float32)],
    )(lengths, *in_hbm)

    outs = [attn, gq]
    afters = []
    for at, before in enumerate(befores):
        *outs, back = call(
            lead_kernel, "lead_rows", 1,
            [fixed(*lead_shape)] + [rows(prior, 0, at)] * 4
            + [rows(2 * prior), rows(prior, 0, at), rows(prior, 0, at)] + [keep] * len(outs),
            [rows(prior, 0, at)] * 4 + [rows(prior)], [full16] * 4 + [back16],
            (prior, 2 * prior, 6), 16 * tok, {8 + i: i for i in range(len(outs))},
        )(lead_bias, query_in, key_in, value_in, grad_out, before, gk_part, gv_part, *outs)
        afters.append(neighbour(back, -1))
    attn, gq, gk, gv = outs

    for at, after in enumerate(afters):
        late = rows(prior, late_at, at)
        gk, gv = call(
            tail_kernel, "tail_keys", 1,
            [fixed(*tail_shape), late, late, rows(prior), late, late, keep, keep],
            [late, late], [full16] * 2, (prior, prior // 2, 4), 10 * tok, {6: 0, 7: 1},
        )(tail_bias, key_in, value_in, after, gk_part, gv_part, gk, gv)
    return (attn, gq, gk, gv)


def shards(query_in, key_in, value_in, grad_out, module_lengths):
    tok = query_in.shape[0]
    prior = tok * lax.axis_size("head") // 8
    plan = halo_shards if 2 * prior <= tok else gathered_shards
    return plan(query_in, key_in, value_in, grad_out, module_lengths)


def solution(mesh):
    placed = (
        P(("seq", "head"), None),
        P(("seq", "head"), None),
        P(("seq", "head"), None),
        P(("seq", "head"), None),
        P(),
    )
    return jax.shard_map(
        shards,
        mesh=mesh,
        in_specs=placed,
        out_specs=(
            P(("seq", "head"), None),
            P(("seq", "head"), None),
            P(("seq", "head"), None),
            P(("seq", "head"), None),
        ),
        check_vma=False,
    )
```

```python
import functools
import math

import jax
import jax.numpy as jnp
from jax import lax
from jax.experimental import pallas as pl
from jax.experimental.pallas import tpu as pltpu
from jax.sharding import PartitionSpec as P

HEAD_DIM = 128
SCALE = HEAD_DIM ** (-0.5)
LOG2E = math.log2(math.e)
MASKED = -1e30


def shifted(value, axis, by):
    peers = lax.axis_size(axis)
    pairs = [(i, i + by) for i in range(peers) if 0 <= i + by < peers]
    return lax.ppermute(value, axis, pairs)


def module_ids(module_lengths, positions):
    module_ends = jnp.cumsum(module_lengths)
    counted = jnp.sum((positions[:, None] >= module_ends[None, :]).astype(jnp.int32), axis=1)
    return jnp.where(positions >= 0, counted, -1)


def allowed_pairs(module_lengths, query_pos, key_pos):
    same = (
        module_ids(module_lengths, query_pos)[:, None]
        == module_ids(module_lengths, key_pos)[None, :]
    )
    return same & (key_pos[None, :] <= query_pos[:, None])


def score_grads(grad_rows, value_block, weights, row_delta, score_scale):
    dprobs = jnp.einsum("qd,kd->qk", grad_rows, value_block, preferred_element_type=jnp.float32)
    return (weights * (dprobs - row_delta[:, None]) * score_scale).astype(jnp.bfloat16)


def key_terms(dscores, weight_bf, query_rows, grad_rows):
    key_grad = jnp.einsum("qk,qd->kd", dscores, query_rows, preferred_element_type=jnp.float32)
    value_grad = jnp.einsum("qk,qd->kd", weight_bf, grad_rows, preferred_element_type=jnp.float32)
    return (key_grad, value_grad)


def one_block(query_rows, key_block, value_block, grad_rows, allowed, score_scale):
    scores = (
        jnp.einsum("qd,kd->qk", query_rows, key_block, preferred_element_type=jnp.float32)
        * score_scale
    )
    row_top = jnp.max(jnp.where(allowed, scores, -jnp.inf), axis=1, keepdims=True)
    row_total = jnp.sum(jnp.where(allowed, jnp.exp(scores - row_top), 0.0), axis=1, keepdims=True)
    log_total = row_top + jnp.log(row_total)
    weights = jnp.where(allowed, jnp.exp(scores - log_total), 0.0)
    weight_bf = weights.astype(jnp.bfloat16)
    attn_rows = jnp.einsum(
        "qk,kd->qd", weight_bf, value_block, preferred_element_type=jnp.float32
    ).astype(jnp.bfloat16)
    row_delta = jnp.sum(grad_rows.astype(jnp.float32) * attn_rows.astype(jnp.float32), axis=1)
    dscores = score_grads(grad_rows, value_block, weights, row_delta, score_scale)
    grad_q = jnp.einsum("qk,kd->qd", dscores, key_block, preferred_element_type=jnp.float32).astype(
        jnp.bfloat16
    )
    key_grad, value_grad = key_terms(dscores, weight_bf, query_rows, grad_rows)
    return (attn_rows, grad_q, key_grad, value_grad, log_total[:, 0], row_delta)


def gathered_shards(query_in, key_in, value_in, grad_out, module_lengths):
    head_q, head_k, head_v, head_do = (
        lax.all_to_all(query_in, "head", split_axis=1, concat_axis=0, tiled=True),
        lax.all_to_all(key_in, "head", split_axis=1, concat_axis=0, tiled=True),
        lax.all_to_all(value_in, "head", split_axis=1, concat_axis=0, tiled=True),
        lax.all_to_all(grad_out, "head", split_axis=1, concat_axis=0, tiled=True),
    )
    row_count = head_q.shape[0]
    width = head_q.shape[1]
    local_heads = width // HEAD_DIM
    prior_rows = row_count // 8
    score_scale = HEAD_DIM ** (-0.5)
    tail_start = row_count - prior_rows
    prior_k, prior_v = shifted((head_k[tail_start:], head_v[tail_start:]), "seq", 1)
    row_start = lax.axis_index("seq") * row_count
    query_pos = row_start + jnp.arange(row_count, dtype=jnp.int32)
    before_pos = row_start - prior_rows + jnp.arange(prior_rows, dtype=jnp.int32)
    key_pos = jnp.concatenate([before_pos, query_pos])
    block_rows = math.gcd(row_count, 512)
    block_count = row_count // block_rows
    pos_blocks = query_pos.reshape(block_count, block_rows)

    def by_head(flat, rows):
        return jnp.moveaxis(flat.reshape(rows, local_heads, HEAD_DIM), 1, 0)

    def to_flat(stacked):
        return jnp.moveaxis(stacked, 0, 1).reshape(stacked.shape[1], width)

    query_h = by_head(head_q, row_count)
    grad_h = by_head(head_do, row_count)
    key_h = by_head(jnp.concatenate([prior_k, head_k], axis=0), row_count + prior_rows)
    value_h = by_head(jnp.concatenate([prior_v, head_v], axis=0), row_count + prior_rows)

    def run_head(packed):
        query_rows, key_block, value_block, grad_rows = packed
        query_blocks = query_rows.reshape(block_count, block_rows, HEAD_DIM)
        grad_blocks = grad_rows.reshape(block_count, block_rows, HEAD_DIM)

        def run_block(inner):
            query_part, grad_part, pos_part = inner
            allowed = allowed_pairs(module_lengths, pos_part, key_pos)
            return one_block(query_part, key_block, value_block, grad_part, allowed, score_scale)

        attn_b, grad_qb, key_b, value_b, lse_b, delta_b = lax.map(
            run_block, (query_blocks, grad_blocks, pos_blocks)
        )
        return (
            attn_b.reshape(row_count, HEAD_DIM),
            grad_qb.reshape(row_count, HEAD_DIM),
            jnp.sum(key_b, axis=0),
            jnp.sum(value_b, axis=0),
            lse_b.reshape(row_count),
            delta_b.reshape(row_count),
        )

    attn_h, grad_qh, key_grad, value_grad, log_total, row_delta = lax.map(
        run_head, (query_h, key_h, value_h, grad_h)
    )
    attn_flat = to_flat(attn_h)
    attn_back = lax.all_to_all(attn_flat, "head", split_axis=0, concat_axis=1, tiled=True)
    grad_q = to_flat(grad_qh)
    later_k, later_v = shifted((key_grad[:, :prior_rows], value_grad[:, :prior_rows]), "seq", -1)
    key_total = key_grad[:, prior_rows:].at[:, tail_start:].add(later_k)
    value_total = value_grad[:, prior_rows:].at[:, tail_start:].add(later_v)
    grad_k = to_flat(key_total.astype(jnp.bfloat16))
    grad_v = to_flat(value_total.astype(jnp.bfloat16))
    back_q, back_k, back_v = (
        lax.all_to_all(grad_q, "head", split_axis=0, concat_axis=1, tiled=True),
        lax.all_to_all(grad_k, "head", split_axis=0, concat_axis=1, tiled=True),
        lax.all_to_all(grad_v, "head", split_axis=0, concat_axis=1, tiled=True),
    )
    return (attn_back, back_q, back_k, back_v)


def dot(left, right, left_dim, right_dim):
    return lax.dot_general(
        left, right, (((left_dim,), (right_dim,)), ((), ())), preferred_element_type=jnp.float32
    )


def module_ends_row(lengths_row):
    count = lengths_row.shape[1]
    row = lax.broadcasted_iota(jnp.int32, (count, count), 0)
    col = lax.broadcasted_iota(jnp.int32, (count, count), 1)
    lengths_col = jnp.sum(jnp.where(row == col, lengths_row, 0.0), axis=1, keepdims=True)
    return jnp.sum(jnp.where(row <= col, lengths_col, 0.0), axis=0, keepdims=True)


def module_ends_col(lengths_row):
    count = lengths_row.shape[1]
    row = lax.broadcasted_iota(jnp.int32, (count, count), 0)
    col = lax.broadcasted_iota(jnp.int32, (count, count), 1)
    return jnp.sum(jnp.where(col <= row, lengths_row, 0.0), axis=1, keepdims=True)


def bias_by_query(lengths_row, first_query, queries, first_key, keys):
    ends = module_ends_row(lengths_row)
    query = (first_query + lax.broadcasted_iota(jnp.int32, (queries, 1), 0)).astype(jnp.float32)
    start = jnp.max(jnp.where(ends <= query, ends, 0.0), axis=1, keepdims=True)
    key = (first_key + lax.broadcasted_iota(jnp.int32, (queries, keys), 1)).astype(jnp.float32)
    return jnp.where((key >= start) & (key <= query), 0.0, MASKED)


def bias_by_key(lengths_row, first_query, queries, first_key, keys):
    ends = module_ends_col(lengths_row)
    query = (first_query + lax.broadcasted_iota(jnp.int32, (1, queries), 1)).astype(jnp.float32)
    start = jnp.max(jnp.where(ends <= query, ends, 0.0), axis=0, keepdims=True)
    key = (first_key + lax.broadcasted_iota(jnp.int32, (keys, queries), 0)).astype(jnp.float32)
    return jnp.where((key >= start) & (key <= query), 0.0, MASKED)


def by_query(q, k, do, v, bias):
    scores = dot(q, k, 1, 1) * (SCALE * LOG2E) + bias
    return scores, dot(do, v, 1, 1)


def full_rows(pairs):
    tops = [jnp.max(s, axis=1, keepdims=True) for s, _ in pairs]
    raws = [jnp.exp2(s - top) for (s, _), top in zip(pairs, tops)]
    totals = [jnp.sum(raw, axis=1, keepdims=True) for raw in raws]
    weights = [raw * (1.0 / total) for raw, total in zip(raws, totals)]
    deltas = [jnp.sum(w * dp, axis=1, keepdims=True) for w, (_, dp) in zip(weights, pairs)]
    grads = [w * (dp - delta) * SCALE for w, (_, dp), delta in zip(weights, pairs, deltas)]
    logs = [top + jnp.log2(total) for top, total in zip(tops, totals)]
    return (
        [w.astype(jnp.bfloat16) for w in weights],
        [g.astype(jnp.bfloat16) for g in grads],
        logs,
        deltas,
    )


def head_columns(width):
    return [slice(c, c + HEAD_DIM) for c in range(0, width, HEAD_DIM)]


def device_first(tok):
    place = lax.axis_index("seq") * lax.axis_size("head") + lax.axis_index("head")
    return place * tok


def as_rows(columns):
    count = columns[0].shape[0]
    lane = lax.broadcasted_iota(jnp.int32, (count, HEAD_DIM), 1)
    table = jnp.zeros((count, HEAD_DIM), jnp.float32)
    for at, column in enumerate(columns):
        table = jnp.where(lane == at, column, table)
    fill = jnp.zeros((HEAD_DIM - count, HEAD_DIM), jnp.float32)
    table = jnp.transpose(jnp.concatenate([table, fill], axis=0))
    return [table[at : at + 1, :count] for at in range(len(columns))]


def split_bf16(row):
    parts = []
    for _ in range(3):
        part = row.astype(jnp.bfloat16)
        parts.append(part)
        row = row - part.astype(jnp.float32)
    return jnp.concatenate([*parts, jnp.zeros_like(parts[0])], axis=1)


def joined(parts):
    parts = parts.astype(jnp.float32)
    count = parts.shape[1] // 4
    return parts[:, :count] + parts[:, count : 2 * count] + parts[:, 2 * count : 3 * count]


def own_kernel(
    prior, len_ref, q_ref, k_ref, v_ref, do_ref, attn_ref, gq_ref, gk_ref, gv_ref,
    lead_bias_ref, tail_bias_ref, bias_ref,
):
    tok, width = k_ref.shape
    columns = head_columns(width)

    @pl.when(pl.program_id(0) == 0)
    def _():
        first = device_first(tok)
        lengths = len_ref[...].astype(jnp.float32)
        bias_ref[...] = bias_by_query(lengths, first + prior, tok - prior, first, tok)
        lead_bias_ref[...] = bias_by_query(lengths, first, prior, first - prior, 2 * prior)
        tail_bias_ref[...] = bias_by_key(
            lengths, first + tok, prior // 2, first + tok - prior, prior
        )

    bias = bias_ref[...]
    pairs = [by_query(q_ref[:, c], k_ref[:, c], do_ref[:, c], v_ref[:, c], bias) for c in columns]
    weights, grads, _, _ = full_rows(pairs)
    for c, w, g in zip(columns, weights, grads):
        attn_ref[:, c] = dot(w, v_ref[:, c], 1, 0).astype(jnp.bfloat16)
        gq_ref[:, c] = dot(g, k_ref[:, c], 1, 0).astype(jnp.bfloat16)
        gk_ref[:, c] = dot(g, q_ref[:, c], 0, 0)
        gv_ref[:, c] = dot(w, do_ref[:, c], 0, 0)


def lead_kernel(
    prior, bias_ref, q_ref, k_ref, v_ref, do_ref, before_ref, gk_part_ref, gv_part_ref, *refs
):
    attn_ref, gq_ref, gk_ref, gv_ref, back_ref = refs[-5:]
    columns = head_columns(q_ref.shape[1])
    half = prior // 2
    bias = bias_ref[...]
    many = bias_ref[half - 1 : half, prior - 1 : prior] == 0.0
    spare = lax.broadcasted_iota(jnp.int32, (half, 1), 0) == half - 1
    early, late = slice(0, prior), slice(prior, 2 * prior)
    keys = [jnp.concatenate([before_ref[early, c], k_ref[:, c]], axis=0) for c in columns]
    values = [jnp.concatenate([before_ref[late, c], v_ref[:, c]], axis=0) for c in columns]
    pairs = [
        by_query(q_ref[:, c], k, do_ref[:, c], v, bias) for c, k, v in zip(columns, keys, values)
    ]
    weights, grads, logs, deltas = full_rows(pairs)
    rows = as_rows([column[:half] for column in logs + deltas])
    logs, deltas = rows[: len(columns)], rows[len(columns) :]
    for c, w, g, k, v, log, delta in zip(columns, weights, grads, keys, values, logs, deltas):
        attn_ref[:, c] = dot(w, v, 1, 0).astype(jnp.bfloat16)
        gq_ref[:, c] = dot(g, k, 1, 0).astype(jnp.bfloat16)
        gk = dot(g, q_ref[:, c], 0, 0)
        gv = dot(w, do_ref[:, c], 0, 0)
        gk_ref[:, c] = (gk_part_ref[:, c] + gk[prior:]).astype(jnp.bfloat16)
        gv_ref[:, c] = (gv_part_ref[:, c] + gv[prior:]).astype(jnp.bfloat16)
        few_q = jnp.where(spare, split_bf16(log), q_ref[:half, c])
        few_do = jnp.where(spare, split_bf16(delta), do_ref[:half, c])
        back_ref[:half, c] = jnp.where(many, gk[half:prior].astype(jnp.bfloat16), few_q)
        back_ref[half:, c] = jnp.where(many, gv[half:prior].astype(jnp.bfloat16), few_do)


def tail_kernel(
    prior, bias_ref, k_ref, v_ref, after_ref, gk_part_ref, gv_part_ref,
    gk_in, gv_in, gk_ref, gv_ref,
):
    columns = head_columns(k_ref.shape[1])
    half = prior // 2
    many = bias_ref[prior - 1 : prior, half - 1 : half] == 0.0
    bias = jnp.where(many, MASKED, bias_ref[...])
    first, second = slice(0, half), slice(half, prior)
    pairs = [
        by_query(k_ref[:, c], after_ref[first, c], v_ref[:, c], after_ref[second, c], bias)
        for c in columns
    ]
    weights = [
        jnp.exp2(s - joined(after_ref[half - 1 : half, c])) for (s, _), c in zip(pairs, columns)
    ]
    grads = [
        w * (dp - joined(after_ref[prior - 1 : prior, c])) * SCALE
        for w, (_, dp), c in zip(weights, pairs, columns)
    ]
    for c, w, g in zip(columns, weights, grads):
        for out_ref, part_ref, left, rows in (
            (gk_ref, gk_part_ref, g, first), (gv_ref, gv_part_ref, w, second)
        ):
            came = after_ref[rows, c]
            total = part_ref[:, c] + dot(left.astype(jnp.bfloat16), came, 1, 0)
            terms = jnp.where(many, came.astype(jnp.float32), 0.0)
            out_ref[first, c] = total[first].astype(jnp.bfloat16)
            out_ref[second, c] = (total[second] + terms).astype(jnp.bfloat16)


def neighbour(value, by):
    peers = lax.axis_size("seq") * lax.axis_size("head")
    pairs = [(i, i + by) for i in range(peers) if 0 <= i + by < peers]
    return lax.ppermute(value, ("seq", "head"), pairs)


def cost(heads, queries, keys, products, moved):
    return pl.CostEstimate(
        flops=2 * heads * queries * keys * HEAD_DIM * products,
        bytes_accessed=moved,
        transcendentals=heads * queries * keys,
    )


def halo_shards(query_in, key_in, value_in, grad_out, module_lengths):
    tok, width = query_in.shape
    prior = tok * lax.axis_size("head") // 8
    step = math.gcd(width, 8 * HEAD_DIM)
    cut = width - max(width // 4, HEAD_DIM)
    spans = [slice(0, cut), slice(cut, width)] if cut else [slice(0, width)]
    late_at = tok // prior - 1
    lengths = module_lengths.reshape(1, -1)
    keep = pl.BlockSpec(memory_space=pl.ANY)
    full16 = jax.ShapeDtypeStruct((tok, width), jnp.bfloat16)
    part32 = pltpu.VMEM((tok, width), jnp.float32)
    lead_shape, tail_shape = (prior, 2 * prior), (prior, prior // 2)

    def rows(count, at=0):
        return pl.BlockSpec((count, step), lambda g: (at, g))

    def part(span, count, at=0):
        wide = span.stop - span.start
        return pl.BlockSpec((count, wide), lambda g: (at, span.start // wide))

    def fixed(*shape):
        return pl.BlockSpec(shape, lambda g: (0, 0))

    def call(kernel, name, grid, ins, outs, shapes, work, moved, aliases=None, scratch=()):
        return pl.pallas_call(
            functools.partial(kernel, prior),
            grid=(grid,),
            in_specs=ins,
            out_specs=outs,
            out_shape=shapes,
            scratch_shapes=scratch,
            input_output_aliases=aliases or {},
            cost_estimate=cost(*work, moved),
            compiler_params=pltpu.CompilerParams(vmem_limit_bytes=16 * 2**20),
            name=name,
        )

    def before(span, held=None):
        late_kv = [key_in[tok - prior :, span], value_in[tok - prior :, span]]
        if held is not None:
            *late_kv, _ = lax.optimization_barrier((*late_kv, held))
        return neighbour(jnp.concatenate(late_kv), 1)

    befores = [before(spans[0])]

    in_hbm = [
        pltpu.with_memory_space_constraint(value, pltpu.HBM)
        for value in (query_in, key_in, value_in, grad_out)
    ]
    attn, gq, gk_part, gv_part, lead_bias, tail_bias = call(
        own_kernel, "own_block", width // step,
        [fixed(*lengths.shape), rows(prior, late_at), rows(tok), rows(tok), rows(prior, late_at)],
        [rows(prior, late_at), rows(prior, late_at), rows(tok), rows(tok)]
        + [fixed(*lead_shape), fixed(*tail_shape)],
        [full16, full16, part32, part32]
        + [pltpu.VMEM(shape, jnp.float32) for shape in (lead_shape, tail_shape)],
        (width // HEAD_DIM, tok - prior, tok, 6), 18 * tok * width,
        scratch=[pltpu.VMEM((tok - prior, tok), jnp.float32)],
    )(lengths, *in_hbm)

    befores += [before(span, lead_bias) for span in spans[1:]]

    outs = [attn, gq]
    afters = []
    for span, came in zip(spans, befores):
        wide = span.stop - span.start
        early = part(span, prior)
        *outs, back = call(
            lead_kernel, "lead_rows", 1,
            [fixed(*lead_shape)] + [early] * 4
            + [pl.BlockSpec((2 * prior, wide), lambda g: (0, 0)), early, early]
            + [keep] * len(outs),
            [early] * 4 + [pl.BlockSpec((prior, wide), lambda g: (0, 0))],
            [full16] * 4 + [jax.ShapeDtypeStruct((prior, wide), jnp.bfloat16)],
            (wide // HEAD_DIM, prior, 2 * prior, 6), 16 * tok * wide,
            {8 + i: i for i in range(len(outs))},
        )(lead_bias, query_in, key_in, value_in, grad_out, came, gk_part, gv_part, *outs)
        afters.append(neighbour(back, -1))
    attn, gq, gk, gv = outs

    for span, came in zip(spans, afters):
        wide = span.stop - span.start
        late = part(span, prior, late_at)
        gk, gv = call(
            tail_kernel, "tail_keys", 1,
            [fixed(*tail_shape), late, late, pl.BlockSpec((prior, wide), lambda g: (0, 0))]
            + [late, late, keep, keep],
            [late, late], [full16] * 2,
            (wide // HEAD_DIM, prior, prior // 2, 4), 10 * tok * wide, {6: 0, 7: 1},
        )(tail_bias, key_in, value_in, came, gk_part, gv_part, gk, gv)
    return (attn, gq, gk, gv)


def shards(query_in, key_in, value_in, grad_out, module_lengths):
    tok = query_in.shape[0]
    prior = tok * lax.axis_size("head") // 8
    plan = halo_shards if 2 * prior <= tok else gathered_shards
    return plan(query_in, key_in, value_in, grad_out, module_lengths)


def solution(mesh):
    placed = (
        P(("seq", "head"), None),
        P(("seq", "head"), None),
        P(("seq", "head"), None),
        P(("seq", "head"), None),
        P(),
    )
    return jax.shard_map(
        shards,
        mesh=mesh,
        in_specs=placed,
        out_specs=(
            P(("seq", "head"), None),
            P(("seq", "head"), None),
            P(("seq", "head"), None),
            P(("seq", "head"), None),
        ),
        check_vma=False,
    )
```

```python
import functools
import math

import jax
import jax.numpy as jnp
from jax import lax
from jax.experimental import pallas as pl
from jax.experimental.pallas import tpu as pltpu
from jax.sharding import PartitionSpec as P

HEAD_DIM = 128
SCALE = HEAD_DIM ** (-0.5)
LOG2E = math.log2(math.e)
MASKED = -1e30


def shifted(value, axis, by):
    peers = lax.axis_size(axis)
    pairs = [(i, i + by) for i in range(peers) if 0 <= i + by < peers]
    return lax.ppermute(value, axis, pairs)


def module_ids(module_lengths, positions):
    module_ends = jnp.cumsum(module_lengths)
    counted = jnp.sum((positions[:, None] >= module_ends[None, :]).astype(jnp.int32), axis=1)
    return jnp.where(positions >= 0, counted, -1)


def allowed_pairs(module_lengths, query_pos, key_pos):
    same = (
        module_ids(module_lengths, query_pos)[:, None]
        == module_ids(module_lengths, key_pos)[None, :]
    )
    return same & (key_pos[None, :] <= query_pos[:, None])


def score_grads(grad_rows, value_block, weights, row_delta, score_scale):
    dprobs = jnp.einsum("qd,kd->qk", grad_rows, value_block, preferred_element_type=jnp.float32)
    return (weights * (dprobs - row_delta[:, None]) * score_scale).astype(jnp.bfloat16)


def key_terms(dscores, weight_bf, query_rows, grad_rows):
    key_grad = jnp.einsum("qk,qd->kd", dscores, query_rows, preferred_element_type=jnp.float32)
    value_grad = jnp.einsum("qk,qd->kd", weight_bf, grad_rows, preferred_element_type=jnp.float32)
    return (key_grad, value_grad)


def one_block(query_rows, key_block, value_block, grad_rows, allowed, score_scale):
    scores = (
        jnp.einsum("qd,kd->qk", query_rows, key_block, preferred_element_type=jnp.float32)
        * score_scale
    )
    row_top = jnp.max(jnp.where(allowed, scores, -jnp.inf), axis=1, keepdims=True)
    row_total = jnp.sum(jnp.where(allowed, jnp.exp(scores - row_top), 0.0), axis=1, keepdims=True)
    log_total = row_top + jnp.log(row_total)
    weights = jnp.where(allowed, jnp.exp(scores - log_total), 0.0)
    weight_bf = weights.astype(jnp.bfloat16)
    attn_rows = jnp.einsum(
        "qk,kd->qd", weight_bf, value_block, preferred_element_type=jnp.float32
    ).astype(jnp.bfloat16)
    row_delta = jnp.sum(grad_rows.astype(jnp.float32) * attn_rows.astype(jnp.float32), axis=1)
    dscores = score_grads(grad_rows, value_block, weights, row_delta, score_scale)
    grad_q = jnp.einsum("qk,kd->qd", dscores, key_block, preferred_element_type=jnp.float32).astype(
        jnp.bfloat16
    )
    key_grad, value_grad = key_terms(dscores, weight_bf, query_rows, grad_rows)
    return (attn_rows, grad_q, key_grad, value_grad, log_total[:, 0], row_delta)


def gathered_shards(query_in, key_in, value_in, grad_out, module_lengths):
    head_q, head_k, head_v, head_do = (
        lax.all_to_all(query_in, "head", split_axis=1, concat_axis=0, tiled=True),
        lax.all_to_all(key_in, "head", split_axis=1, concat_axis=0, tiled=True),
        lax.all_to_all(value_in, "head", split_axis=1, concat_axis=0, tiled=True),
        lax.all_to_all(grad_out, "head", split_axis=1, concat_axis=0, tiled=True),
    )
    row_count = head_q.shape[0]
    width = head_q.shape[1]
    local_heads = width // HEAD_DIM
    prior_rows = row_count // 8
    score_scale = HEAD_DIM ** (-0.5)
    tail_start = row_count - prior_rows
    prior_k, prior_v = shifted((head_k[tail_start:], head_v[tail_start:]), "seq", 1)
    row_start = lax.axis_index("seq") * row_count
    query_pos = row_start + jnp.arange(row_count, dtype=jnp.int32)
    before_pos = row_start - prior_rows + jnp.arange(prior_rows, dtype=jnp.int32)
    key_pos = jnp.concatenate([before_pos, query_pos])
    block_rows = math.gcd(row_count, 512)
    block_count = row_count // block_rows
    pos_blocks = query_pos.reshape(block_count, block_rows)

    def by_head(flat, rows):
        return jnp.moveaxis(flat.reshape(rows, local_heads, HEAD_DIM), 1, 0)

    def to_flat(stacked):
        return jnp.moveaxis(stacked, 0, 1).reshape(stacked.shape[1], width)

    query_h = by_head(head_q, row_count)
    grad_h = by_head(head_do, row_count)
    key_h = by_head(jnp.concatenate([prior_k, head_k], axis=0), row_count + prior_rows)
    value_h = by_head(jnp.concatenate([prior_v, head_v], axis=0), row_count + prior_rows)

    def run_head(packed):
        query_rows, key_block, value_block, grad_rows = packed
        query_blocks = query_rows.reshape(block_count, block_rows, HEAD_DIM)
        grad_blocks = grad_rows.reshape(block_count, block_rows, HEAD_DIM)

        def run_block(inner):
            query_part, grad_part, pos_part = inner
            allowed = allowed_pairs(module_lengths, pos_part, key_pos)
            return one_block(query_part, key_block, value_block, grad_part, allowed, score_scale)

        attn_b, grad_qb, key_b, value_b, lse_b, delta_b = lax.map(
            run_block, (query_blocks, grad_blocks, pos_blocks)
        )
        return (
            attn_b.reshape(row_count, HEAD_DIM),
            grad_qb.reshape(row_count, HEAD_DIM),
            jnp.sum(key_b, axis=0),
            jnp.sum(value_b, axis=0),
            lse_b.reshape(row_count),
            delta_b.reshape(row_count),
        )

    attn_h, grad_qh, key_grad, value_grad, log_total, row_delta = lax.map(
        run_head, (query_h, key_h, value_h, grad_h)
    )
    attn_flat = to_flat(attn_h)
    attn_back = lax.all_to_all(attn_flat, "head", split_axis=0, concat_axis=1, tiled=True)
    grad_q = to_flat(grad_qh)
    later_k, later_v = shifted((key_grad[:, :prior_rows], value_grad[:, :prior_rows]), "seq", -1)
    key_total = key_grad[:, prior_rows:].at[:, tail_start:].add(later_k)
    value_total = value_grad[:, prior_rows:].at[:, tail_start:].add(later_v)
    grad_k = to_flat(key_total.astype(jnp.bfloat16))
    grad_v = to_flat(value_total.astype(jnp.bfloat16))
    back_q, back_k, back_v = (
        lax.all_to_all(grad_q, "head", split_axis=0, concat_axis=1, tiled=True),
        lax.all_to_all(grad_k, "head", split_axis=0, concat_axis=1, tiled=True),
        lax.all_to_all(grad_v, "head", split_axis=0, concat_axis=1, tiled=True),
    )
    return (attn_back, back_q, back_k, back_v)


def dot(left, right, left_dim, right_dim):
    return lax.dot_general(
        left, right, (((left_dim,), (right_dim,)), ((), ())), preferred_element_type=jnp.float32
    )


def module_ends_row(lengths_row):
    count = lengths_row.shape[1]
    row = lax.broadcasted_iota(jnp.int32, (count, count), 0)
    col = lax.broadcasted_iota(jnp.int32, (count, count), 1)
    lengths_col = jnp.sum(jnp.where(row == col, lengths_row, 0.0), axis=1, keepdims=True)
    return jnp.sum(jnp.where(row <= col, lengths_col, 0.0), axis=0, keepdims=True)


def module_ends_col(lengths_row):
    count = lengths_row.shape[1]
    row = lax.broadcasted_iota(jnp.int32, (count, count), 0)
    col = lax.broadcasted_iota(jnp.int32, (count, count), 1)
    return jnp.sum(jnp.where(col <= row, lengths_row, 0.0), axis=1, keepdims=True)


def bias_by_query(lengths_row, first_query, queries, first_key, keys):
    ends = module_ends_row(lengths_row)
    query = (first_query + lax.broadcasted_iota(jnp.int32, (queries, 1), 0)).astype(jnp.float32)
    start = jnp.max(jnp.where(ends <= query, ends, 0.0), axis=1, keepdims=True)
    key = (first_key + lax.broadcasted_iota(jnp.int32, (queries, keys), 1)).astype(jnp.float32)
    return jnp.where((key >= start) & (key <= query), 0.0, MASKED)


def bias_by_key(lengths_row, first_query, queries, first_key, keys):
    ends = module_ends_col(lengths_row)
    query = (first_query + lax.broadcasted_iota(jnp.int32, (1, queries), 1)).astype(jnp.float32)
    start = jnp.max(jnp.where(ends <= query, ends, 0.0), axis=0, keepdims=True)
    key = (first_key + lax.broadcasted_iota(jnp.int32, (keys, queries), 0)).astype(jnp.float32)
    return jnp.where((key >= start) & (key <= query), 0.0, MASKED)


def by_query(q, k, do, v, bias):
    scores = dot(q, k, 1, 1) * (SCALE * LOG2E) + bias
    return scores, dot(do, v, 1, 1)


def full_rows(pairs):
    tops = [jnp.max(s, axis=1, keepdims=True) for s, _ in pairs]
    raws = [jnp.exp2(s - top) for (s, _), top in zip(pairs, tops)]
    totals = [jnp.sum(raw, axis=1, keepdims=True) for raw in raws]
    weights = [raw * (1.0 / total) for raw, total in zip(raws, totals)]
    deltas = [jnp.sum(w * dp, axis=1, keepdims=True) for w, (_, dp) in zip(weights, pairs)]
    grads = [w * (dp - delta) * SCALE for w, (_, dp), delta in zip(weights, pairs, deltas)]
    logs = [top + jnp.log2(total) for top, total in zip(tops, totals)]
    return (
        [w.astype(jnp.bfloat16) for w in weights],
        [g.astype(jnp.bfloat16) for g in grads],
        logs,
        deltas,
    )


def head_columns(width):
    return [slice(c, c + HEAD_DIM) for c in range(0, width, HEAD_DIM)]


def device_first(tok):
    place = lax.axis_index("seq") * lax.axis_size("head") + lax.axis_index("head")
    return place * tok


def as_rows(columns):
    count = columns[0].shape[0]
    lane = lax.broadcasted_iota(jnp.int32, (count, HEAD_DIM), 1)
    table = jnp.zeros((count, HEAD_DIM), jnp.float32)
    for at, column in enumerate(columns):
        table = jnp.where(lane == at, column, table)
    fill = jnp.zeros((HEAD_DIM - count, HEAD_DIM), jnp.float32)
    table = jnp.transpose(jnp.concatenate([table, fill], axis=0))
    return [table[at : at + 1, :count] for at in range(len(columns))]


def split_bf16(row):
    parts = []
    for _ in range(3):
        part = row.astype(jnp.bfloat16)
        parts.append(part)
        row = row - part.astype(jnp.float32)
    return jnp.concatenate([*parts, jnp.zeros_like(parts[0])], axis=1)


def joined(parts):
    parts = parts.astype(jnp.float32)
    count = parts.shape[1] // 4
    return parts[:, :count] + parts[:, count : 2 * count] + parts[:, 2 * count : 3 * count]


def pack_kernel(prior, spans, k_ref, v_ref, *refs):
    *packed_refs, sems = refs
    last = pl.ds(k_ref.shape[0] - prior, prior)
    copies = []
    for span, packed_ref in zip(spans, packed_refs):
        for half, ref in enumerate((k_ref, v_ref)):
            copies.append(
                pltpu.make_async_copy(
                    ref.at[last, span],
                    packed_ref.at[pl.ds(half * prior, prior), :],
                    sems.at[len(copies)],
                )
            )
    for copy in copies:
        copy.start()
    for copy in copies:
        copy.wait()


def own_kernel(
    prior, step, len_hbm, q_hbm, k_hbm, v_hbm, do_hbm,
    q_ref, k_ref, v_ref, do_ref, attn_ref, gq_ref, gk_ref, gv_ref, lead_bias_ref, tail_bias_ref,
    len_ref, bias_ref, sems, len_sem,
):
    tok, width = k_ref.shape
    pairs = ((k_hbm, k_ref), (v_hbm, v_ref), (q_hbm, q_ref), (do_hbm, do_ref))

    def copies(at):
        cols = pl.ds(pl.multiple_of(at * step, step), step)
        return [
            pltpu.make_async_copy(hbm.at[:, cols], ref.at[:, cols], sems.at[at, n])
            for n, (hbm, ref) in enumerate(pairs)
        ]

    len_copy = pltpu.make_async_copy(len_hbm, len_ref, len_sem)
    len_copy.start()
    for at in range(width // step):
        for copy in copies(at):
            copy.start()
    len_copy.wait()
    first = device_first(tok)
    lengths = len_ref[...].astype(jnp.float32)
    bias_ref[...] = bias_by_query(lengths, first + prior, tok - prior, first, tok)
    lead_bias_ref[...] = bias_by_query(lengths, first, prior, first - prior, 2 * prior)
    tail_bias_ref[...] = bias_by_key(lengths, first + tok, prior // 2, first + tok - prior, prior)

    @pl.loop(0, width // step)
    def _(at):
        for copy in copies(at):
            copy.wait()
        bias = bias_ref[...]
        columns = [
            pl.ds(pl.multiple_of(at * step + c, HEAD_DIM), HEAD_DIM)
            for c in range(0, step, HEAD_DIM)
        ]
        late = slice(prior, tok)
        pairs = [
            by_query(q_ref[late, c], k_ref[:, c], do_ref[late, c], v_ref[:, c], bias)
            for c in columns
        ]
        weights, grads, _, _ = full_rows(pairs)
        for c, w, g in zip(columns, weights, grads):
            attn_ref[:, c] = dot(w, v_ref[:, c], 1, 0).astype(jnp.bfloat16)
            gq_ref[:, c] = dot(g, k_ref[:, c], 1, 0).astype(jnp.bfloat16)
            gk_ref[:, c] = dot(g, q_ref[late, c], 0, 0)
            gv_ref[:, c] = dot(w, do_ref[late, c], 0, 0)


def lead_kernel(
    prior, span, bias_ref, q_ref, k_ref, v_ref, do_ref, before_ref, gk_part_ref, gv_part_ref,
    attn_ref, gq_ref, gk_ref, gv_ref, back_ref,
):
    places = head_columns(span.stop - span.start)
    columns = [slice(span.start + c.start, span.start + c.stop) for c in places]
    half = prior // 2
    bias = bias_ref[...]
    many = bias_ref[half - 1 : half, prior - 1 : prior] == 0.0
    spare = lax.broadcasted_iota(jnp.int32, (half, 1), 0) == half - 1
    early, late = slice(0, prior), slice(prior, 2 * prior)
    keys = [
        jnp.concatenate([before_ref[early, p], k_ref[early, c]], axis=0)
        for p, c in zip(places, columns)
    ]
    values = [
        jnp.concatenate([before_ref[late, p], v_ref[early, c]], axis=0)
        for p, c in zip(places, columns)
    ]
    pairs = [
        by_query(q_ref[early, c], k, do_ref[early, c], v, bias)
        for c, k, v in zip(columns, keys, values)
    ]
    weights, grads, logs, deltas = full_rows(pairs)
    rows = as_rows([column[:half] for column in logs + deltas])
    logs, deltas = rows[: len(columns)], rows[len(columns) :]
    for at, (p, c) in enumerate(zip(places, columns)):
        w, g = weights[at], grads[at]
        gk = dot(g, q_ref[early, c], 0, 0)
        gv = dot(w, do_ref[early, c], 0, 0)
        few_q = jnp.where(spare, split_bf16(logs[at]), q_ref[:half, c])
        few_do = jnp.where(spare, split_bf16(deltas[at]), do_ref[:half, c])
        back_ref[:half, p] = jnp.where(many, gk[half:prior].astype(jnp.bfloat16), few_q)
        back_ref[half:, p] = jnp.where(many, gv[half:prior].astype(jnp.bfloat16), few_do)
        attn_ref[:, p] = dot(w, values[at], 1, 0).astype(jnp.bfloat16)
        gq_ref[:, p] = dot(g, keys[at], 1, 0).astype(jnp.bfloat16)
        gk_ref[:, p] = (gk_part_ref[early, c] + gk[prior:]).astype(jnp.bfloat16)
        gv_ref[:, p] = (gv_part_ref[early, c] + gv[prior:]).astype(jnp.bfloat16)


def tail_kernel(
    prior, span, places, bias_ref, k_ref, v_ref, after_ref, gk_part_ref, gv_part_ref, *refs
):
    outs = 4 if places else 2
    pieces, refs = refs[: len(places)], refs[len(places) :]
    *refs, gk_ref, gv_ref, gk_late_ref, gv_late_ref, sems = refs
    targets = (*refs[-2:], gk_ref, gv_ref) if outs == 4 else ()
    copies = []
    for piece, (target, row, col) in zip(pieces, places):
        rows, cols = pl.ds(row, piece.shape[0]), pl.ds(col, piece.shape[1])
        copies.append(
            pltpu.make_async_copy(piece, targets[target].at[rows, cols], sems.at[len(copies)])
        )
        copies[-1].start()

    tok = k_ref.shape[0]
    here = head_columns(span.stop - span.start)
    columns = [slice(span.start + c.start, span.start + c.stop) for c in here]
    half = prior // 2
    many = bias_ref[prior - 1 : prior, half - 1 : half] == 0.0
    bias = jnp.where(many, MASKED, bias_ref[...])
    first, second, last = slice(0, half), slice(half, prior), slice(tok - prior, tok)
    pairs = [
        by_query(k_ref[last, c], after_ref[first, p], v_ref[last, c], after_ref[second, p], bias)
        for p, c in zip(here, columns)
    ]
    weights = [
        jnp.exp2(s - joined(after_ref[half - 1 : half, p])) for (s, _), p in zip(pairs, here)
    ]
    grads = [
        w * (dp - joined(after_ref[prior - 1 : prior, p])) * SCALE
        for w, (_, dp), p in zip(weights, pairs, here)
    ]
    for p, c, w, g in zip(here, columns, weights, grads):
        for out_ref, part_ref, left, rows in (
            (gk_late_ref, gk_part_ref, g, first), (gv_late_ref, gv_part_ref, w, second)
        ):
            came = after_ref[rows, p]
            total = part_ref[last, c] + dot(left.astype(jnp.bfloat16), came, 1, 0)
            terms = jnp.where(many, came.astype(jnp.float32), 0.0)
            out_ref[first, p] = total[first].astype(jnp.bfloat16)
            out_ref[second, p] = (total[second] + terms).astype(jnp.bfloat16)
    for late_ref, out_ref in ((gk_late_ref, gk_ref), (gv_late_ref, gv_ref)):
        copies.append(
            pltpu.make_async_copy(
                late_ref, out_ref.at[pl.ds(tok - prior, prior), span], sems.at[len(copies)]
            )
        )
        copies[-1].start()
    for copy in copies:
        copy.wait()


def neighbour(value, by):
    peers = lax.axis_size("seq") * lax.axis_size("head")
    pairs = [(i, i + by) for i in range(peers) if 0 <= i + by < peers]
    return lax.ppermute(value, ("seq", "head"), pairs)


def cost(heads, queries, keys, products, moved):
    return pl.CostEstimate(
        flops=2 * heads * queries * keys * HEAD_DIM * products,
        bytes_accessed=moved,
        transcendentals=heads * queries * keys,
    )


def halo_shards(query_in, key_in, value_in, grad_out, module_lengths):
    tok, width = query_in.shape
    prior = tok * lax.axis_size("head") // 8
    step = math.gcd(width, 8 * HEAD_DIM)
    cut = width - max(width // 4, HEAD_DIM)
    spans = [slice(0, cut), slice(cut, width)] if cut else [slice(0, width)]
    wides = [span.stop - span.start for span in spans]
    anywhere = pl.BlockSpec(memory_space=pl.ANY)
    near = pl.BlockSpec(memory_space=pltpu.VMEM)
    full16 = jax.ShapeDtypeStruct((tok, width), jnp.bfloat16)

    def near16(rows, columns):
        return pltpu.VMEM((rows, columns), jnp.bfloat16)

    def near32(rows, columns):
        return pltpu.VMEM((rows, columns), jnp.float32)

    def in_hbm(*values):
        return [pltpu.with_memory_space_constraint(value, pltpu.HBM) for value in values]

    def in_vmem(*values):
        return [pltpu.with_memory_space_constraint(value, pltpu.VMEM) for value in values]

    def call(kernel, name, ins, outs, shapes, scratch, work, moved, aliases=None):
        return pl.pallas_call(
            kernel,
            in_specs=ins,
            out_specs=outs,
            out_shape=shapes,
            scratch_shapes=scratch,
            input_output_aliases=aliases or {},
            cost_estimate=cost(*work, moved),
            compiler_params=pltpu.CompilerParams(vmem_limit_bytes=16 * 2**20),
            name=name,
        )

    to_next = call(
        functools.partial(pack_kernel, prior, spans), "pack_late",
        [anywhere] * 2, [near] * len(spans), [near16(2 * prior, wide) for wide in wides],
        [pltpu.SemaphoreType.DMA((2 * len(spans),))], (0, 0, 0, 0), 8 * prior * width,
    )(*in_hbm(key_in, value_in))
    befores = [neighbour(to_next[0], 1)]

    q, k, v, do, attn, gq, gk_part, gv_part, lead_bias, tail_bias = call(
        functools.partial(own_kernel, prior, step), "own_block",
        [anywhere] * 5, [near] * 10,
        [near16(tok, width)] * 4 + [near16(tok - prior, width)] * 2 + [near32(tok, width)] * 2
        + [near32(prior, 2 * prior), near32(prior, prior // 2)],
        [
            pltpu.VMEM((1, module_lengths.shape[0]), jnp.int32), near32(tok - prior, tok),
            pltpu.SemaphoreType.DMA((width // step, 4)), pltpu.SemaphoreType.DMA(()),
        ],
        (width // HEAD_DIM, tok - prior, tok, 6), 24 * tok * width,
    )(*in_hbm(module_lengths.reshape(1, -1), query_in, key_in, value_in, grad_out))
    for part in to_next[1:]:
        part, _ = lax.optimization_barrier((part, lead_bias))
        befores.append(neighbour(part, 1))

    pieces, places, afters = [attn, gq], [(0, prior, 0), (1, prior, 0)], []
    for span, wide, before in zip(spans, wides, befores):
        *done, back = call(
            functools.partial(lead_kernel, prior, span), "lead_rows",
            [near] * 8, [near] * 5, [near16(prior, wide)] * 5, (),
            (wide // HEAD_DIM, prior, 2 * prior, 6), 16 * tok * wide,
        )(*in_vmem(lead_bias, q, k, v, do, before, gk_part, gv_part))
        pieces += done
        places += [(target, 0, span.start) for target in range(4)]
        afters.append(neighbour(back, -1))

    outs = []
    for span, wide, after in zip(spans, wides, afters):
        keep = outs[2:]
        done = call(
            functools.partial(tail_kernel, prior, span, [] if outs else places), "tail_keys",
            [near] * 6 + ([anywhere] * 2 if outs else [near] * len(pieces)),
            [anywhere] * (2 if outs else 4), [full16] * (2 if outs else 4),
            [
                near16(prior, wide), near16(prior, wide),
                pltpu.SemaphoreType.DMA((2 if outs else len(places) + 2,)),
            ],
            (wide // HEAD_DIM, prior, prior // 2, 4), 10 * tok * wide,
            {6: 0, 7: 1} if outs else None,
        )(
            *in_vmem(tail_bias, k, v, after, gk_part, gv_part),
            *(keep if outs else in_vmem(*pieces)),
        )
        outs = [*outs[:2], *done]
    return tuple(outs)


def shards(query_in, key_in, value_in, grad_out, module_lengths):
    tok = query_in.shape[0]
    prior = tok * lax.axis_size("head") // 8
    plan = halo_shards if 2 * prior == tok else gathered_shards
    return plan(query_in, key_in, value_in, grad_out, module_lengths)


def solution(mesh):
    placed = (
        P(("seq", "head"), None),
        P(("seq", "head"), None),
        P(("seq", "head"), None),
        P(("seq", "head"), None),
        P(),
    )
    return jax.shard_map(
        shards,
        mesh=mesh,
        in_specs=placed,
        out_specs=(
            P(("seq", "head"), None),
            P(("seq", "head"), None),
            P(("seq", "head"), None),
            P(("seq", "head"), None),
        ),
        check_vma=False,
    )
```

```python
import functools
import math

import jax
import jax.numpy as jnp
from jax import lax
from jax.experimental import pallas as pl
from jax.experimental.pallas import tpu as pltpu
from jax.sharding import PartitionSpec as P

HEAD_DIM = 128
SCALE = HEAD_DIM ** (-0.5)
LOG2E = math.log2(math.e)
MASKED = -1e30


def shifted(value, axis, by):
    peers = lax.axis_size(axis)
    pairs = [(i, i + by) for i in range(peers) if 0 <= i + by < peers]
    return lax.ppermute(value, axis, pairs)


def module_ids(module_lengths, positions):
    module_ends = jnp.cumsum(module_lengths)
    counted = jnp.sum((positions[:, None] >= module_ends[None, :]).astype(jnp.int32), axis=1)
    return jnp.where(positions >= 0, counted, -1)


def allowed_pairs(module_lengths, query_pos, key_pos):
    same = (
        module_ids(module_lengths, query_pos)[:, None]
        == module_ids(module_lengths, key_pos)[None, :]
    )
    return same & (key_pos[None, :] <= query_pos[:, None])


def score_grads(grad_rows, value_block, weights, row_delta, score_scale):
    dprobs = jnp.einsum("qd,kd->qk", grad_rows, value_block, preferred_element_type=jnp.float32)
    return (weights * (dprobs - row_delta[:, None]) * score_scale).astype(jnp.bfloat16)


def key_terms(dscores, weight_bf, query_rows, grad_rows):
    key_grad = jnp.einsum("qk,qd->kd", dscores, query_rows, preferred_element_type=jnp.float32)
    value_grad = jnp.einsum("qk,qd->kd", weight_bf, grad_rows, preferred_element_type=jnp.float32)
    return (key_grad, value_grad)


def one_block(query_rows, key_block, value_block, grad_rows, allowed, score_scale):
    scores = (
        jnp.einsum("qd,kd->qk", query_rows, key_block, preferred_element_type=jnp.float32)
        * score_scale
    )
    row_top = jnp.max(jnp.where(allowed, scores, -jnp.inf), axis=1, keepdims=True)
    row_total = jnp.sum(jnp.where(allowed, jnp.exp(scores - row_top), 0.0), axis=1, keepdims=True)
    log_total = row_top + jnp.log(row_total)
    weights = jnp.where(allowed, jnp.exp(scores - log_total), 0.0)
    weight_bf = weights.astype(jnp.bfloat16)
    attn_rows = jnp.einsum(
        "qk,kd->qd", weight_bf, value_block, preferred_element_type=jnp.float32
    ).astype(jnp.bfloat16)
    row_delta = jnp.sum(grad_rows.astype(jnp.float32) * attn_rows.astype(jnp.float32), axis=1)
    dscores = score_grads(grad_rows, value_block, weights, row_delta, score_scale)
    grad_q = jnp.einsum("qk,kd->qd", dscores, key_block, preferred_element_type=jnp.float32).astype(
        jnp.bfloat16
    )
    key_grad, value_grad = key_terms(dscores, weight_bf, query_rows, grad_rows)
    return (attn_rows, grad_q, key_grad, value_grad, log_total[:, 0], row_delta)


def gathered_shards(query_in, key_in, value_in, grad_out, module_lengths):
    head_q, head_k, head_v, head_do = (
        lax.all_to_all(query_in, "head", split_axis=1, concat_axis=0, tiled=True),
        lax.all_to_all(key_in, "head", split_axis=1, concat_axis=0, tiled=True),
        lax.all_to_all(value_in, "head", split_axis=1, concat_axis=0, tiled=True),
        lax.all_to_all(grad_out, "head", split_axis=1, concat_axis=0, tiled=True),
    )
    row_count = head_q.shape[0]
    width = head_q.shape[1]
    local_heads = width // HEAD_DIM
    prior_rows = row_count // 8
    score_scale = HEAD_DIM ** (-0.5)
    tail_start = row_count - prior_rows
    prior_k, prior_v = shifted((head_k[tail_start:], head_v[tail_start:]), "seq", 1)
    row_start = lax.axis_index("seq") * row_count
    query_pos = row_start + jnp.arange(row_count, dtype=jnp.int32)
    before_pos = row_start - prior_rows + jnp.arange(prior_rows, dtype=jnp.int32)
    key_pos = jnp.concatenate([before_pos, query_pos])
    block_rows = math.gcd(row_count, 512)
    block_count = row_count // block_rows
    pos_blocks = query_pos.reshape(block_count, block_rows)

    def by_head(flat, rows):
        return jnp.moveaxis(flat.reshape(rows, local_heads, HEAD_DIM), 1, 0)

    def to_flat(stacked):
        return jnp.moveaxis(stacked, 0, 1).reshape(stacked.shape[1], width)

    query_h = by_head(head_q, row_count)
    grad_h = by_head(head_do, row_count)
    key_h = by_head(jnp.concatenate([prior_k, head_k], axis=0), row_count + prior_rows)
    value_h = by_head(jnp.concatenate([prior_v, head_v], axis=0), row_count + prior_rows)

    def run_head(packed):
        query_rows, key_block, value_block, grad_rows = packed
        query_blocks = query_rows.reshape(block_count, block_rows, HEAD_DIM)
        grad_blocks = grad_rows.reshape(block_count, block_rows, HEAD_DIM)

        def run_block(inner):
            query_part, grad_part, pos_part = inner
            allowed = allowed_pairs(module_lengths, pos_part, key_pos)
            return one_block(query_part, key_block, value_block, grad_part, allowed, score_scale)

        attn_b, grad_qb, key_b, value_b, lse_b, delta_b = lax.map(
            run_block, (query_blocks, grad_blocks, pos_blocks)
        )
        return (
            attn_b.reshape(row_count, HEAD_DIM),
            grad_qb.reshape(row_count, HEAD_DIM),
            jnp.sum(key_b, axis=0),
            jnp.sum(value_b, axis=0),
            lse_b.reshape(row_count),
            delta_b.reshape(row_count),
        )

    attn_h, grad_qh, key_grad, value_grad, log_total, row_delta = lax.map(
        run_head, (query_h, key_h, value_h, grad_h)
    )
    attn_flat = to_flat(attn_h)
    attn_back = lax.all_to_all(attn_flat, "head", split_axis=0, concat_axis=1, tiled=True)
    grad_q = to_flat(grad_qh)
    later_k, later_v = shifted((key_grad[:, :prior_rows], value_grad[:, :prior_rows]), "seq", -1)
    key_total = key_grad[:, prior_rows:].at[:, tail_start:].add(later_k)
    value_total = value_grad[:, prior_rows:].at[:, tail_start:].add(later_v)
    grad_k = to_flat(key_total.astype(jnp.bfloat16))
    grad_v = to_flat(value_total.astype(jnp.bfloat16))
    back_q, back_k, back_v = (
        lax.all_to_all(grad_q, "head", split_axis=0, concat_axis=1, tiled=True),
        lax.all_to_all(grad_k, "head", split_axis=0, concat_axis=1, tiled=True),
        lax.all_to_all(grad_v, "head", split_axis=0, concat_axis=1, tiled=True),
    )
    return (attn_back, back_q, back_k, back_v)


def dot(left, right, left_dim, right_dim):
    return lax.dot_general(
        left, right, (((left_dim,), (right_dim,)), ((), ())), preferred_element_type=jnp.float32
    )


def module_ends_row(lengths_row):
    count = lengths_row.shape[1]
    row = lax.broadcasted_iota(jnp.int32, (count, count), 0)
    col = lax.broadcasted_iota(jnp.int32, (count, count), 1)
    lengths_col = jnp.sum(jnp.where(row == col, lengths_row, 0.0), axis=1, keepdims=True)
    return jnp.sum(jnp.where(row <= col, lengths_col, 0.0), axis=0, keepdims=True)


def module_ends_col(lengths_row):
    count = lengths_row.shape[1]
    row = lax.broadcasted_iota(jnp.int32, (count, count), 0)
    col = lax.broadcasted_iota(jnp.int32, (count, count), 1)
    return jnp.sum(jnp.where(col <= row, lengths_row, 0.0), axis=1, keepdims=True)


def bias_by_query(lengths_row, first_query, queries, first_key, keys):
    ends = module_ends_row(lengths_row)
    query = (first_query + lax.broadcasted_iota(jnp.int32, (queries, 1), 0)).astype(jnp.float32)
    start = jnp.max(jnp.where(ends <= query, ends, 0.0), axis=1, keepdims=True)
    key = (first_key + lax.broadcasted_iota(jnp.int32, (queries, keys), 1)).astype(jnp.float32)
    return jnp.where((key >= start) & (key <= query), 0.0, MASKED)


def bias_by_key(lengths_row, first_query, queries, first_key, keys):
    ends = module_ends_col(lengths_row)
    query = (first_query + lax.broadcasted_iota(jnp.int32, (1, queries), 1)).astype(jnp.float32)
    start = jnp.max(jnp.where(ends <= query, ends, 0.0), axis=0, keepdims=True)
    key = (first_key + lax.broadcasted_iota(jnp.int32, (keys, queries), 0)).astype(jnp.float32)
    return jnp.where((key >= start) & (key <= query), 0.0, MASKED)


def by_query(q, k, do, v, bias):
    scores = dot(q, k, 1, 1) * (SCALE * LOG2E) + bias
    return scores, dot(do, v, 1, 1)


def full_rows(pairs):
    tops = [jnp.max(s, axis=1, keepdims=True) for s, _ in pairs]
    raws = [jnp.exp2(s - top) for (s, _), top in zip(pairs, tops)]
    totals = [jnp.sum(raw, axis=1, keepdims=True) for raw in raws]
    weights = [raw * (1.0 / total) for raw, total in zip(raws, totals)]
    deltas = [jnp.sum(w * dp, axis=1, keepdims=True) for w, (_, dp) in zip(weights, pairs)]
    grads = [w * (dp - delta) * SCALE for w, (_, dp), delta in zip(weights, pairs, deltas)]
    logs = [top + jnp.log2(total) for top, total in zip(tops, totals)]
    return (
        [w.astype(jnp.bfloat16) for w in weights],
        [g.astype(jnp.bfloat16) for g in grads],
        logs,
        deltas,
    )


def merged_rows(pairs, own):
    tops = [
        jnp.maximum(jnp.max(s, axis=0, keepdims=True), log) for (s, _), (log, _) in zip(pairs, own)
    ]
    raws = [jnp.exp2(s - top) for (s, _), top in zip(pairs, tops)]
    own_raws = [jnp.exp2(log - top) for (log, _), top in zip(own, tops)]
    parts = [
        1.0 / (jnp.sum(raw, axis=0, keepdims=True) + own_raw)
        for raw, own_raw in zip(raws, own_raws)
    ]
    weights = [raw * part for raw, part in zip(raws, parts)]
    deltas = [
        jnp.sum(w * dp, axis=0, keepdims=True) + own_raw * part * own_delta
        for w, (_, dp), own_raw, part, (_, own_delta) in zip(weights, pairs, own_raws, parts, own)
    ]
    grads = [w * (dp - delta) * SCALE for w, (_, dp), delta in zip(weights, pairs, deltas)]
    return [w.astype(jnp.bfloat16) for w in weights], [g.astype(jnp.bfloat16) for g in grads]


def head_columns(low, high):
    return [slice(c, c + HEAD_DIM) for c in range(low, high, HEAD_DIM)]


def device_first(tok):
    place = lax.axis_index("seq") * lax.axis_size("head") + lax.axis_index("head")
    return place * tok


def as_rows(columns):
    count = columns[0].shape[0]
    lane = lax.broadcasted_iota(jnp.int32, (count, HEAD_DIM), 1)
    table = jnp.zeros((count, HEAD_DIM), jnp.float32)
    for at, column in enumerate(columns):
        table = jnp.where(lane == at, column, table)
    fill = jnp.zeros((HEAD_DIM - count, HEAD_DIM), jnp.float32)
    table = jnp.transpose(jnp.concatenate([table, fill], axis=0))
    return [table[at : at + 1, :count] for at in range(len(columns))]


def split_bf16(row):
    parts = []
    for _ in range(3):
        part = row.astype(jnp.bfloat16)
        parts.append(part)
        row = row - part.astype(jnp.float32)
    return jnp.concatenate([*parts, jnp.zeros_like(parts[0])], axis=1)


def joined(parts):
    parts = parts.astype(jnp.float32)
    count = parts.shape[1] // 4
    return parts[:, :count] + parts[:, count : 2 * count] + parts[:, 2 * count : 3 * count]


def pack_kernel(prior, k_ref, v_ref, near_ref, far_ref, sems):
    half, tok = prior // 2, k_ref.shape[0]
    copies = []
    for at, packed_ref in enumerate((near_ref, far_ref)):
        rows = pl.ds(tok - (at + 1) * half, half)
        for place, ref in enumerate((k_ref, v_ref)):
            copies.append(
                pltpu.make_async_copy(
                    ref.at[rows, :], packed_ref.at[pl.ds(place * half, half), :],
                    sems.at[len(copies)],
                )
            )
    for copy in copies:
        copy.start()
    for copy in copies:
        copy.wait()


def own_kernel(
    prior, step, len_hbm, q_hbm, k_hbm, v_hbm, do_hbm,
    q_ref, k_ref, v_ref, do_ref, attn_ref, gq_ref, gk_ref, gv_ref,
    near_bias_ref, lead_bias_ref, tail_bias_ref, len_ref, bias_ref, sems, len_sem,
):
    tok, width = k_ref.shape
    pairs = ((k_hbm, k_ref), (v_hbm, v_ref), (q_hbm, q_ref), (do_hbm, do_ref))

    def copies(at):
        cols = pl.ds(pl.multiple_of(at * step, step), step)
        return [
            pltpu.make_async_copy(hbm.at[:, cols], ref.at[:, cols], sems.at[at, n])
            for n, (hbm, ref) in enumerate(pairs)
        ]

    len_copy = pltpu.make_async_copy(len_hbm, len_ref, len_sem)
    len_copy.start()
    for at in range(width // step):
        for copy in copies(at):
            copy.start()
    len_copy.wait()
    first = device_first(tok)
    lengths = len_ref[...].astype(jnp.float32)
    bias_ref[...] = bias_by_query(lengths, first + prior, tok - prior, first, tok)
    lead_bias_ref[...] = bias_by_query(lengths, first, prior, first - prior, 2 * prior)
    near_bias_ref[...] = bias_by_query(
        lengths, first, prior, first - prior // 2, prior + prior // 2
    )
    tail_bias_ref[...] = bias_by_key(lengths, first + tok, prior // 2, first + tok - prior, prior)

    @pl.loop(0, width // step)
    def _(at):
        for copy in copies(at):
            copy.wait()
        bias = bias_ref[...]
        columns = [
            pl.ds(pl.multiple_of(at * step + c, HEAD_DIM), HEAD_DIM)
            for c in range(0, step, HEAD_DIM)
        ]
        late = slice(prior, tok)
        pairs = [
            by_query(q_ref[late, c], k_ref[:, c], do_ref[late, c], v_ref[:, c], bias)
            for c in columns
        ]
        weights, grads, _, _ = full_rows(pairs)
        for c, w, g in zip(columns, weights, grads):
            attn_ref[:, c] = dot(w, v_ref[:, c], 1, 0).astype(jnp.bfloat16)
            gq_ref[:, c] = dot(g, k_ref[:, c], 1, 0).astype(jnp.bfloat16)
            gk_ref[:, c] = dot(g, q_ref[late, c], 0, 0)
            gv_ref[:, c] = dot(w, do_ref[late, c], 0, 0)


def near_kernel(
    prior, near_bias_ref, lead_bias_ref, q_ref, k_ref, v_ref, do_ref, near_ref, back_ref
):
    half = prior // 2
    far = lead_bias_ref[0:1, half - 1 : half] == 0.0
    lane = lax.broadcasted_iota(jnp.int32, (1, prior + half), 1)
    bias = jnp.where(far & (lane < half), MASKED, near_bias_ref[...])
    spare = lax.broadcasted_iota(jnp.int32, (half, 1), 0) == half - 1
    early, first, second = slice(0, prior), slice(0, half), slice(half, prior)
    columns = head_columns(0, q_ref.shape[1])
    pairs = []
    for c in columns:
        k = jnp.concatenate([near_ref[first, c], k_ref[early, c]], axis=0)
        v = jnp.concatenate([near_ref[second, c], v_ref[early, c]], axis=0)
        pairs.append(by_query(q_ref[early, c], k, do_ref[early, c], v, bias))
    weights, grads, logs, deltas = full_rows(pairs)
    rows = as_rows([column[:half] for column in logs + deltas])
    for at, c in enumerate(columns):
        for row, left, ref, place in (
            (rows[at], grads[at], q_ref, first),
            (rows[len(columns) + at], weights[at], do_ref, second),
        ):
            terms = dot(left[:, :half], ref[early, c], 0, 0).astype(jnp.bfloat16)
            here = jnp.where(spare, split_bf16(row), ref[first, c])
            back_ref[place, c] = jnp.where(far, here, terms)


def lead_kernel(
    prior, step, bias_ref, q_ref, k_ref, v_ref, do_ref, near_ref, far_ref, gk_part_ref, gv_part_ref,
    attn_late_ref, gq_late_ref, attn_hbm, gq_hbm, gk_hbm, gv_hbm,
    attn_ref, gq_ref, gk_ref, gv_ref, sems, late_sems,
):
    tok, width = q_ref.shape
    half = prior // 2
    early, first, second = slice(0, prior), slice(0, half), slice(half, prior)
    late = pl.ds(prior, tok - prior)
    late_copies = [
        pltpu.make_async_copy(attn_late_ref, attn_hbm.at[late, :], late_sems.at[0]),
        pltpu.make_async_copy(gq_late_ref, gq_hbm.at[late, :], late_sems.at[1]),
    ]
    for copy in late_copies:
        copy.start()

    def copies(at):
        cols = pl.ds(pl.multiple_of(at * step, step), step)
        pairs = ((attn_ref, attn_hbm), (gq_ref, gq_hbm), (gk_ref, gk_hbm), (gv_ref, gv_hbm))
        return [
            pltpu.make_async_copy(ref.at[:, cols], hbm.at[pl.ds(0, prior), cols], sems.at[at, n])
            for n, (ref, hbm) in enumerate(pairs)
        ]

    @pl.loop(0, width // step)
    def _(at):
        bias = bias_ref[...]
        columns = [
            pl.ds(pl.multiple_of(at * step + c, HEAD_DIM), HEAD_DIM)
            for c in range(0, step, HEAD_DIM)
        ]
        keys = [
            jnp.concatenate([far_ref[first, c], near_ref[first, c], k_ref[early, c]], axis=0)
            for c in columns
        ]
        values = [
            jnp.concatenate([far_ref[second, c], near_ref[second, c], v_ref[early, c]], axis=0)
            for c in columns
        ]
        pairs = [
            by_query(q_ref[early, c], k, do_ref[early, c], v, bias)
            for c, k, v in zip(columns, keys, values)
        ]
        weights, grads, _, _ = full_rows(pairs)
        for c, w, g, k, v in zip(columns, weights, grads, keys, values):
            attn_ref[:, c] = dot(w, v, 1, 0).astype(jnp.bfloat16)
            gq_ref[:, c] = dot(g, k, 1, 0).astype(jnp.bfloat16)
            gk = dot(g, q_ref[early, c], 0, 0)
            gv = dot(w, do_ref[early, c], 0, 0)
            gk_ref[:, c] = (gk_part_ref[early, c] + gk[prior:]).astype(jnp.bfloat16)
            gv_ref[:, c] = (gv_part_ref[early, c] + gv[prior:]).astype(jnp.bfloat16)
        for copy in copies(at):
            copy.start()

    for at in range(width // step):
        for copy in copies(at):
            copy.wait()
    for copy in late_copies:
        copy.wait()


def tail_kernel(
    prior, step, bias_ref, k_ref, v_ref, after_ref, gk_part_ref, gv_part_ref, gk_in, gv_in,
    gk_hbm, gv_hbm, gk_ref, gv_ref, sems,
):
    tok, width = k_ref.shape
    half = prior // 2
    far = bias_ref[half - 1 : half, 0:1] == 0.0
    bias = jnp.where(far, bias_ref[...], MASKED)
    first, second, last = slice(0, half), slice(half, prior), slice(tok - prior, tok)
    copies = []
    for low in range(0, width, step):
        columns = head_columns(low, low + step)
        pairs = [
            by_query(k_ref[last, c], after_ref[first, c], v_ref[last, c], after_ref[second, c], bias)
            for c in columns
        ]
        own = [
            (joined(after_ref[half - 1 : half, c]), joined(after_ref[prior - 1 : prior, c]))
            for c in columns
        ]
        weights, grads = merged_rows(pairs, own)
        for c, w, g in zip(columns, weights, grads):
            for out_ref, part_ref, left, rows in (
                (gk_ref, gk_part_ref, g, first), (gv_ref, gv_part_ref, w, second)
            ):
                came = after_ref[rows, c]
                total = part_ref[last, c] + dot(left, came, 1, 0)
                terms = jnp.where(far, 0.0, came.astype(jnp.float32))
                out_ref[first, c] = total[first].astype(jnp.bfloat16)
                out_ref[second, c] = (total[second] + terms).astype(jnp.bfloat16)
        cols = pl.ds(low, step)
        for ref, hbm in ((gk_ref, gk_hbm), (gv_ref, gv_hbm)):
            copies.append(
                pltpu.make_async_copy(
                    ref.at[:, cols], hbm.at[pl.ds(tok - prior, prior), cols], sems.at[len(copies)]
                )
            )
            copies[-1].start()
    for copy in copies:
        copy.wait()


def neighbour(value, by):
    peers = lax.axis_size("seq") * lax.axis_size("head")
    pairs = [(i, i + by) for i in range(peers) if 0 <= i + by < peers]
    return lax.ppermute(value, ("seq", "head"), pairs)


def cost(heads, queries, keys, products, moved):
    return pl.CostEstimate(
        flops=2 * heads * queries * keys * HEAD_DIM * products,
        bytes_accessed=moved,
        transcendentals=heads * queries * keys,
    )


def halo_shards(query_in, key_in, value_in, grad_out, module_lengths):
    tok, width = query_in.shape
    prior = tok * lax.axis_size("head") // 8
    step = math.gcd(width, 8 * HEAD_DIM)
    groups = width // step
    anywhere = pl.BlockSpec(memory_space=pl.ANY)
    inside = pl.BlockSpec(memory_space=pltpu.VMEM)
    full16 = jax.ShapeDtypeStruct((tok, width), jnp.bfloat16)

    def near16(rows, columns):
        return pltpu.VMEM((rows, columns), jnp.bfloat16)

    def near32(rows, columns):
        return pltpu.VMEM((rows, columns), jnp.float32)

    def in_hbm(*values):
        return [pltpu.with_memory_space_constraint(value, pltpu.HBM) for value in values]

    def in_vmem(*values):
        return [pltpu.with_memory_space_constraint(value, pltpu.VMEM) for value in values]

    def call(kernel, name, ins, outs, shapes, scratch, work, moved, aliases=None):
        return pl.pallas_call(
            kernel,
            in_specs=ins,
            out_specs=outs,
            out_shape=shapes,
            scratch_shapes=scratch,
            input_output_aliases=aliases or {},
            cost_estimate=cost(*work, moved),
            compiler_params=pltpu.CompilerParams(vmem_limit_bytes=16 * 2**20),
            name=name,
        )

    near, far = call(
        functools.partial(pack_kernel, prior), "pack_late",
        [anywhere] * 2, [inside] * 2, [near16(prior, width)] * 2,
        [pltpu.SemaphoreType.DMA((4,))], (0, 0, 0, 0), 8 * prior * width,
    )(*in_hbm(key_in, value_in))
    near = neighbour(near, 1)

    q, k, v, do, attn, gq, gk_part, gv_part, near_bias, lead_bias, tail_bias = call(
        functools.partial(own_kernel, prior, step), "own_block",
        [anywhere] * 5, [inside] * 11,
        [near16(tok, width)] * 4 + [near16(tok - prior, width)] * 2 + [near32(tok, width)] * 2
        + [near32(prior, prior + prior // 2), near32(prior, 2 * prior), near32(prior, prior // 2)],
        [
            pltpu.VMEM((1, module_lengths.shape[0]), jnp.int32), near32(tok - prior, tok),
            pltpu.SemaphoreType.DMA((groups, 4)), pltpu.SemaphoreType.DMA(()),
        ],
        (width // HEAD_DIM, tok - prior, tok, 6), 24 * tok * width,
    )(*in_hbm(module_lengths.reshape(1, -1), query_in, key_in, value_in, grad_out))
    far, _ = lax.optimization_barrier((far, lead_bias))
    far = neighbour(far, 1)

    back = call(
        functools.partial(near_kernel, prior), "near_terms",
        [inside] * 7, inside, near16(prior, width), (),
        (width // HEAD_DIM, prior, prior + prior // 2, 3), 8 * tok * width,
    )(*in_vmem(near_bias, lead_bias, q, k, v, do, near))
    back = neighbour(back, -1)

    attn, gq, gk, gv = call(
        functools.partial(lead_kernel, prior, step), "lead_rows",
        [inside] * 11, [anywhere] * 4, [full16] * 4,
        [near16(prior, width)] * 4
        + [pltpu.SemaphoreType.DMA((groups, 4)), pltpu.SemaphoreType.DMA((2,))],
        (width // HEAD_DIM, prior, 2 * prior, 6), 20 * tok * width,
    )(*in_vmem(lead_bias, q, k, v, do, near, far, gk_part, gv_part, attn, gq))

    gk, gv = call(
        functools.partial(tail_kernel, prior, step), "tail_keys",
        [inside] * 6 + [anywhere] * 2, [anywhere] * 2, [full16] * 2,
        [near16(prior, width)] * 2 + [pltpu.SemaphoreType.DMA((2 * groups,))],
        (width // HEAD_DIM, prior, prior // 2, 4), 10 * tok * width, {6: 0, 7: 1},
    )(*in_vmem(tail_bias, k, v, back, gk_part, gv_part), gk, gv)
    return (attn, gq, gk, gv)


def shards(query_in, key_in, value_in, grad_out, module_lengths):
    tok = query_in.shape[0]
    prior = tok * lax.axis_size("head") // 8
    plan = halo_shards if 2 * prior == tok else gathered_shards
    return plan(query_in, key_in, value_in, grad_out, module_lengths)


def solution(mesh):
    placed = (
        P(("seq", "head"), None),
        P(("seq", "head"), None),
        P(("seq", "head"), None),
        P(("seq", "head"), None),
        P(),
    )
    return jax.shard_map(
        shards,
        mesh=mesh,
        in_specs=placed,
        out_specs=(
            P(("seq", "head"), None),
            P(("seq", "head"), None),
            P(("seq", "head"), None),
            P(("seq", "head"), None),
        ),
        check_vma=False,
    )
```

```python
import functools
import math

import jax
import jax.numpy as jnp
from jax import lax
from jax.experimental import pallas as pl
from jax.experimental.pallas import tpu as pltpu
from jax.sharding import PartitionSpec as P

HEAD_DIM = 128
SCALE = HEAD_DIM ** (-0.5)
LOG2E = math.log2(math.e)
MASKED = -1e30


def shifted(value, axis, by):
    peers = lax.axis_size(axis)
    pairs = [(i, i + by) for i in range(peers) if 0 <= i + by < peers]
    return lax.ppermute(value, axis, pairs)


def module_ids(module_lengths, positions):
    module_ends = jnp.cumsum(module_lengths)
    counted = jnp.sum((positions[:, None] >= module_ends[None, :]).astype(jnp.int32), axis=1)
    return jnp.where(positions >= 0, counted, -1)


def allowed_pairs(module_lengths, query_pos, key_pos):
    same = (
        module_ids(module_lengths, query_pos)[:, None]
        == module_ids(module_lengths, key_pos)[None, :]
    )
    return same & (key_pos[None, :] <= query_pos[:, None])


def score_grads(grad_rows, value_block, weights, row_delta, score_scale):
    dprobs = jnp.einsum("qd,kd->qk", grad_rows, value_block, preferred_element_type=jnp.float32)
    return (weights * (dprobs - row_delta[:, None]) * score_scale).astype(jnp.bfloat16)


def key_terms(dscores, weight_bf, query_rows, grad_rows):
    key_grad = jnp.einsum("qk,qd->kd", dscores, query_rows, preferred_element_type=jnp.float32)
    value_grad = jnp.einsum("qk,qd->kd", weight_bf, grad_rows, preferred_element_type=jnp.float32)
    return (key_grad, value_grad)


def one_block(query_rows, key_block, value_block, grad_rows, allowed, score_scale):
    scores = (
        jnp.einsum("qd,kd->qk", query_rows, key_block, preferred_element_type=jnp.float32)
        * score_scale
    )
    row_top = jnp.max(jnp.where(allowed, scores, -jnp.inf), axis=1, keepdims=True)
    row_total = jnp.sum(jnp.where(allowed, jnp.exp(scores - row_top), 0.0), axis=1, keepdims=True)
    log_total = row_top + jnp.log(row_total)
    weights = jnp.where(allowed, jnp.exp(scores - log_total), 0.0)
    weight_bf = weights.astype(jnp.bfloat16)
    attn_rows = jnp.einsum(
        "qk,kd->qd", weight_bf, value_block, preferred_element_type=jnp.float32
    ).astype(jnp.bfloat16)
    row_delta = jnp.sum(grad_rows.astype(jnp.float32) * attn_rows.astype(jnp.float32), axis=1)
    dscores = score_grads(grad_rows, value_block, weights, row_delta, score_scale)
    grad_q = jnp.einsum("qk,kd->qd", dscores, key_block, preferred_element_type=jnp.float32).astype(
        jnp.bfloat16
    )
    key_grad, value_grad = key_terms(dscores, weight_bf, query_rows, grad_rows)
    return (attn_rows, grad_q, key_grad, value_grad, log_total[:, 0], row_delta)


def gathered_shards(query_in, key_in, value_in, grad_out, module_lengths):
    head_q, head_k, head_v, head_do = (
        lax.all_to_all(query_in, "head", split_axis=1, concat_axis=0, tiled=True),
        lax.all_to_all(key_in, "head", split_axis=1, concat_axis=0, tiled=True),
        lax.all_to_all(value_in, "head", split_axis=1, concat_axis=0, tiled=True),
        lax.all_to_all(grad_out, "head", split_axis=1, concat_axis=0, tiled=True),
    )
    row_count = head_q.shape[0]
    width = head_q.shape[1]
    local_heads = width // HEAD_DIM
    prior_rows = row_count // 8
    score_scale = HEAD_DIM ** (-0.5)
    tail_start = row_count - prior_rows
    prior_k, prior_v = shifted((head_k[tail_start:], head_v[tail_start:]), "seq", 1)
    row_start = lax.axis_index("seq") * row_count
    query_pos = row_start + jnp.arange(row_count, dtype=jnp.int32)
    before_pos = row_start - prior_rows + jnp.arange(prior_rows, dtype=jnp.int32)
    key_pos = jnp.concatenate([before_pos, query_pos])
    block_rows = math.gcd(row_count, 512)
    block_count = row_count // block_rows
    pos_blocks = query_pos.reshape(block_count, block_rows)

    def by_head(flat, rows):
        return jnp.moveaxis(flat.reshape(rows, local_heads, HEAD_DIM), 1, 0)

    def to_flat(stacked):
        return jnp.moveaxis(stacked, 0, 1).reshape(stacked.shape[1], width)

    query_h = by_head(head_q, row_count)
    grad_h = by_head(head_do, row_count)
    key_h = by_head(jnp.concatenate([prior_k, head_k], axis=0), row_count + prior_rows)
    value_h = by_head(jnp.concatenate([prior_v, head_v], axis=0), row_count + prior_rows)

    def run_head(packed):
        query_rows, key_block, value_block, grad_rows = packed
        query_blocks = query_rows.reshape(block_count, block_rows, HEAD_DIM)
        grad_blocks = grad_rows.reshape(block_count, block_rows, HEAD_DIM)

        def run_block(inner):
            query_part, grad_part, pos_part = inner
            allowed = allowed_pairs(module_lengths, pos_part, key_pos)
            return one_block(query_part, key_block, value_block, grad_part, allowed, score_scale)

        attn_b, grad_qb, key_b, value_b, lse_b, delta_b = lax.map(
            run_block, (query_blocks, grad_blocks, pos_blocks)
        )
        return (
            attn_b.reshape(row_count, HEAD_DIM),
            grad_qb.reshape(row_count, HEAD_DIM),
            jnp.sum(key_b, axis=0),
            jnp.sum(value_b, axis=0),
            lse_b.reshape(row_count),
            delta_b.reshape(row_count),
        )

    attn_h, grad_qh, key_grad, value_grad, log_total, row_delta = lax.map(
        run_head, (query_h, key_h, value_h, grad_h)
    )
    attn_flat = to_flat(attn_h)
    attn_back = lax.all_to_all(attn_flat, "head", split_axis=0, concat_axis=1, tiled=True)
    grad_q = to_flat(grad_qh)
    later_k, later_v = shifted((key_grad[:, :prior_rows], value_grad[:, :prior_rows]), "seq", -1)
    key_total = key_grad[:, prior_rows:].at[:, tail_start:].add(later_k)
    value_total = value_grad[:, prior_rows:].at[:, tail_start:].add(later_v)
    grad_k = to_flat(key_total.astype(jnp.bfloat16))
    grad_v = to_flat(value_total.astype(jnp.bfloat16))
    back_q, back_k, back_v = (
        lax.all_to_all(grad_q, "head", split_axis=0, concat_axis=1, tiled=True),
        lax.all_to_all(grad_k, "head", split_axis=0, concat_axis=1, tiled=True),
        lax.all_to_all(grad_v, "head", split_axis=0, concat_axis=1, tiled=True),
    )
    return (attn_back, back_q, back_k, back_v)


def dot(left, right, left_dim, right_dim):
    return lax.dot_general(
        left, right, (((left_dim,), (right_dim,)), ((), ())), preferred_element_type=jnp.float32
    )


def module_ends_row(lengths_row):
    count = lengths_row.shape[1]
    row = lax.broadcasted_iota(jnp.int32, (count, count), 0)
    col = lax.broadcasted_iota(jnp.int32, (count, count), 1)
    lengths_col = jnp.sum(jnp.where(row == col, lengths_row, 0.0), axis=1, keepdims=True)
    return jnp.sum(jnp.where(row <= col, lengths_col, 0.0), axis=0, keepdims=True)


def module_ends_col(lengths_row):
    count = lengths_row.shape[1]
    row = lax.broadcasted_iota(jnp.int32, (count, count), 0)
    col = lax.broadcasted_iota(jnp.int32, (count, count), 1)
    return jnp.sum(jnp.where(col <= row, lengths_row, 0.0), axis=1, keepdims=True)


def bias_by_query(lengths_row, first_query, queries, first_key, keys):
    ends = module_ends_row(lengths_row)
    query = (first_query + lax.broadcasted_iota(jnp.int32, (queries, 1), 0)).astype(jnp.float32)
    start = jnp.max(jnp.where(ends <= query, ends, 0.0), axis=1, keepdims=True)
    key = (first_key + lax.broadcasted_iota(jnp.int32, (queries, keys), 1)).astype(jnp.float32)
    return jnp.where((key >= start) & (key <= query), 0.0, MASKED)


def bias_by_key(lengths_row, first_query, queries, first_key, keys):
    ends = module_ends_col(lengths_row)
    query = (first_query + lax.broadcasted_iota(jnp.int32, (1, queries), 1)).astype(jnp.float32)
    start = jnp.max(jnp.where(ends <= query, ends, 0.0), axis=0, keepdims=True)
    key = (first_key + lax.broadcasted_iota(jnp.int32, (keys, queries), 0)).astype(jnp.float32)
    return jnp.where((key >= start) & (key <= query), 0.0, MASKED)


def by_query(q, k, do, v, bias):
    scores = dot(q, k, 1, 1) * (SCALE * LOG2E) + bias
    return scores, dot(do, v, 1, 1)


def full_rows(pairs):
    tops = [jnp.max(s, axis=1, keepdims=True) for s, _ in pairs]
    raws = [jnp.exp2(s - top) for (s, _), top in zip(pairs, tops)]
    totals = [jnp.sum(raw, axis=1, keepdims=True) for raw in raws]
    weights = [raw * (1.0 / total) for raw, total in zip(raws, totals)]
    deltas = [jnp.sum(w * dp, axis=1, keepdims=True) for w, (_, dp) in zip(weights, pairs)]
    grads = [w * (dp - delta) * SCALE for w, (_, dp), delta in zip(weights, pairs, deltas)]
    logs = [top + jnp.log2(total) for top, total in zip(tops, totals)]
    return (
        [w.astype(jnp.bfloat16) for w in weights],
        [g.astype(jnp.bfloat16) for g in grads],
        logs,
        deltas,
    )


def merged_rows(pairs, own):
    tops = [
        jnp.maximum(jnp.max(s, axis=0, keepdims=True), log) for (s, _), (log, _) in zip(pairs, own)
    ]
    raws = [jnp.exp2(s - top) for (s, _), top in zip(pairs, tops)]
    own_raws = [jnp.exp2(log - top) for (log, _), top in zip(own, tops)]
    parts = [
        1.0 / (jnp.sum(raw, axis=0, keepdims=True) + own_raw)
        for raw, own_raw in zip(raws, own_raws)
    ]
    weights = [raw * part for raw, part in zip(raws, parts)]
    deltas = [
        jnp.sum(w * dp, axis=0, keepdims=True) + own_raw * part * own_delta
        for w, (_, dp), own_raw, part, (_, own_delta) in zip(weights, pairs, own_raws, parts, own)
    ]
    grads = [w * (dp - delta) * SCALE for w, (_, dp), delta in zip(weights, pairs, deltas)]
    return [w.astype(jnp.bfloat16) for w in weights], [g.astype(jnp.bfloat16) for g in grads]


def head_columns(low, high):
    return [slice(c, c + HEAD_DIM) for c in range(low, high, HEAD_DIM)]


def device_first(tok):
    place = lax.axis_index("seq") * lax.axis_size("head") + lax.axis_index("head")
    return place * tok


def as_rows(columns):
    count = columns[0].shape[0]
    lane = lax.broadcasted_iota(jnp.int32, (count, HEAD_DIM), 1)
    table = jnp.zeros((count, HEAD_DIM), jnp.float32)
    for at, column in enumerate(columns):
        table = jnp.where(lane == at, column, table)
    fill = jnp.zeros((HEAD_DIM - count, HEAD_DIM), jnp.float32)
    table = jnp.transpose(jnp.concatenate([table, fill], axis=0))
    return [table[at : at + 1, :count] for at in range(len(columns))]


def split_bf16(row):
    parts = []
    for _ in range(3):
        part = row.astype(jnp.bfloat16)
        parts.append(part)
        row = row - part.astype(jnp.float32)
    return jnp.concatenate([*parts, jnp.zeros_like(parts[0])], axis=1)


def joined(parts):
    parts = parts.astype(jnp.float32)
    count = parts.shape[1] // 4
    return parts[:, :count] + parts[:, count : 2 * count] + parts[:, 2 * count : 3 * count]


def pack_copies(prior, at, k_ref, v_ref, packed_ref, sems):
    half, tok = prior // 2, k_ref.shape[0]
    rows = pl.ds(tok - (at + 1) * half, half)
    return [
        pltpu.make_async_copy(
            ref.at[rows, :], packed_ref.at[pl.ds(n * half, half), :], sems.at[n]
        )
        for n, ref in enumerate((k_ref, v_ref))
    ]


def pack_kernel(prior, k_ref, v_ref, near_ref, sems):
    copies = pack_copies(prior, 0, k_ref, v_ref, near_ref, sems)
    for copy in copies:
        copy.start()
    for copy in copies:
        copy.wait()


def ready_kernel(
    prior, len_hbm, q_hbm, k_hbm, v_hbm, do_hbm, far_ref, q_ref, k_ref, v_ref, do_ref,
    own_bias_ref, near_bias_ref, lead_bias_ref, tail_bias_ref, len_ref, sems, far_sems, len_sem,
):
    tok, half = k_ref.shape[0], prior // 2
    pairs = ((q_hbm, q_ref), (k_hbm, k_ref), (v_hbm, v_ref), (do_hbm, do_ref))
    copies = pack_copies(prior, 1, k_hbm, v_hbm, far_ref, far_sems)
    copies += [pltpu.make_async_copy(hbm, ref, sems.at[n]) for n, (hbm, ref) in enumerate(pairs)]
    len_copy = pltpu.make_async_copy(len_hbm, len_ref, len_sem)
    len_copy.start()
    for copy in copies:
        copy.start()
    len_copy.wait()
    first = device_first(tok)
    lengths = len_ref[...].astype(jnp.float32)
    own_bias_ref[...] = bias_by_query(lengths, first + prior, tok - prior, first, tok)
    near_bias_ref[...] = bias_by_query(lengths, first, prior, first - half, prior + half)
    lead_bias_ref[...] = bias_by_query(lengths, first, prior, first - prior, 2 * prior)
    tail_bias_ref[...] = bias_by_key(lengths, first + tok, half, first + tok - prior, prior)
    for copy in copies:
        copy.wait()


def own_kernel(
    prior, step, bias_ref, q_ref, k_ref, v_ref, do_ref, attn_ref, gq_ref, gk_ref, gv_ref
):
    tok, width = k_ref.shape
    late = slice(prior, tok)

    @pl.loop(0, width // step)
    def _(at):
        bias = bias_ref[...]
        columns = [
            pl.ds(pl.multiple_of(at * step + c, HEAD_DIM), HEAD_DIM)
            for c in range(0, step, HEAD_DIM)
        ]
        pairs = [
            by_query(q_ref[late, c], k_ref[:, c], do_ref[late, c], v_ref[:, c], bias)
            for c in columns
        ]
        weights, grads, _, _ = full_rows(pairs)
        for c, w, g in zip(columns, weights, grads):
            attn_ref[:, c] = dot(w, v_ref[:, c], 1, 0).astype(jnp.bfloat16)
            gq_ref[:, c] = dot(g, k_ref[:, c], 1, 0).astype(jnp.bfloat16)
            gk_ref[:, c] = dot(g, q_ref[late, c], 0, 0)
            gv_ref[:, c] = dot(w, do_ref[late, c], 0, 0)


def near_kernel(
    prior, near_bias_ref, lead_bias_ref, q_ref, k_ref, v_ref, do_ref, near_ref, back_ref
):
    half = prior // 2
    far = lead_bias_ref[0:1, half - 1 : half] == 0.0
    lane = lax.broadcasted_iota(jnp.int32, (1, prior + half), 1)
    bias = jnp.where(far & (lane < half), MASKED, near_bias_ref[...])
    spare = lax.broadcasted_iota(jnp.int32, (half, 1), 0) == half - 1
    early, first, second = slice(0, prior), slice(0, half), slice(half, prior)
    columns = head_columns(0, q_ref.shape[1])
    pairs = []
    for c in columns:
        k = jnp.concatenate([near_ref[first, c], k_ref[early, c]], axis=0)
        v = jnp.concatenate([near_ref[second, c], v_ref[early, c]], axis=0)
        pairs.append(by_query(q_ref[early, c], k, do_ref[early, c], v, bias))
    weights, grads, logs, deltas = full_rows(pairs)
    rows = as_rows([column[:half] for column in logs + deltas])
    for at, c in enumerate(columns):
        for row, left, ref, place in (
            (rows[at], grads[at], q_ref, first),
            (rows[len(columns) + at], weights[at], do_ref, second),
        ):
            terms = dot(left[:, :half], ref[early, c], 0, 0).astype(jnp.bfloat16)
            here = jnp.where(spare, split_bf16(row), ref[first, c])
            back_ref[place, c] = jnp.where(far, here, terms)


def lead_kernel(
    prior, step, bias_ref, q_ref, k_ref, v_ref, do_ref, near_ref, far_ref, gk_part_ref, gv_part_ref,
    attn_late_ref, gq_late_ref, attn_hbm, gq_hbm, gk_hbm, gv_hbm,
    attn_ref, gq_ref, gk_ref, gv_ref, sems, late_sems,
):
    tok, width = q_ref.shape
    half = prior // 2
    early, first, second = slice(0, prior), slice(0, half), slice(half, prior)
    late = pl.ds(prior, tok - prior)
    late_copies = [
        pltpu.make_async_copy(attn_late_ref, attn_hbm.at[late, :], late_sems.at[0]),
        pltpu.make_async_copy(gq_late_ref, gq_hbm.at[late, :], late_sems.at[1]),
    ]
    for copy in late_copies:
        copy.start()

    def copies(at):
        cols = pl.ds(pl.multiple_of(at * step, step), step)
        pairs = ((attn_ref, attn_hbm), (gq_ref, gq_hbm), (gk_ref, gk_hbm), (gv_ref, gv_hbm))
        return [
            pltpu.make_async_copy(ref.at[:, cols], hbm.at[pl.ds(0, prior), cols], sems.at[at, n])
            for n, (ref, hbm) in enumerate(pairs)
        ]

    @pl.loop(0, width // step)
    def _(at):
        bias = bias_ref[...]
        columns = [
            pl.ds(pl.multiple_of(at * step + c, HEAD_DIM), HEAD_DIM)
            for c in range(0, step, HEAD_DIM)
        ]
        keys = [
            jnp.concatenate([far_ref[first, c], near_ref[first, c], k_ref[early, c]], axis=0)
            for c in columns
        ]
        values = [
            jnp.concatenate([far_ref[second, c], near_ref[second, c], v_ref[early, c]], axis=0)
            for c in columns
        ]
        pairs = [
            by_query(q_ref[early, c], k, do_ref[early, c], v, bias)
            for c, k, v in zip(columns, keys, values)
        ]
        weights, grads, _, _ = full_rows(pairs)
        for c, w, g, k, v in zip(columns, weights, grads, keys, values):
            attn_ref[:, c] = dot(w, v, 1, 0).astype(jnp.bfloat16)
            gq_ref[:, c] = dot(g, k, 1, 0).astype(jnp.bfloat16)
            gk = dot(g, q_ref[early, c], 0, 0)
            gv = dot(w, do_ref[early, c], 0, 0)
            gk_ref[:, c] = (gk_part_ref[early, c] + gk[prior:]).astype(jnp.bfloat16)
            gv_ref[:, c] = (gv_part_ref[early, c] + gv[prior:]).astype(jnp.bfloat16)
        for copy in copies(at):
            copy.start()

    for at in range(width // step):
        for copy in copies(at):
            copy.wait()
    for copy in late_copies:
        copy.wait()


def tail_kernel(
    prior, step, bias_ref, k_ref, v_ref, after_ref, gk_part_ref, gv_part_ref, gk_in, gv_in,
    gk_hbm, gv_hbm, gk_ref, gv_ref, sems,
):
    tok, width = k_ref.shape
    half = prior // 2
    far = bias_ref[half - 1 : half, 0:1] == 0.0
    bias = jnp.where(far, bias_ref[...], MASKED)
    first, second, last = slice(0, half), slice(half, prior), slice(tok - prior, tok)
    copies = []
    for low in range(0, width, step):
        columns = head_columns(low, low + step)
        pairs = [
            by_query(k_ref[last, c], after_ref[first, c], v_ref[last, c], after_ref[second, c], bias)
            for c in columns
        ]
        own = [
            (joined(after_ref[half - 1 : half, c]), joined(after_ref[prior - 1 : prior, c]))
            for c in columns
        ]
        weights, grads = merged_rows(pairs, own)
        for c, w, g in zip(columns, weights, grads):
            for out_ref, part_ref, left, rows in (
                (gk_ref, gk_part_ref, g, first), (gv_ref, gv_part_ref, w, second)
            ):
                came = after_ref[rows, c]
                total = part_ref[last, c] + dot(left, came, 1, 0)
                terms = jnp.where(far, 0.0, came.astype(jnp.float32))
                out_ref[first, c] = total[first].astype(jnp.bfloat16)
                out_ref[second, c] = (total[second] + terms).astype(jnp.bfloat16)
        cols = pl.ds(low, step)
        for ref, hbm in ((gk_ref, gk_hbm), (gv_ref, gv_hbm)):
            copies.append(
                pltpu.make_async_copy(
                    ref.at[:, cols], hbm.at[pl.ds(tok - prior, prior), cols], sems.at[len(copies)]
                )
            )
            copies[-1].start()
    for copy in copies:
        copy.wait()


def neighbour(value, by):
    peers = lax.axis_size("seq") * lax.axis_size("head")
    pairs = [(i, i + by) for i in range(peers) if 0 <= i + by < peers]
    return lax.ppermute(value, ("seq", "head"), pairs)


def cost(heads, queries, keys, products, moved):
    return pl.CostEstimate(
        flops=2 * heads * queries * keys * HEAD_DIM * products,
        bytes_accessed=moved,
        transcendentals=heads * queries * keys,
    )


def halo_shards(query_in, key_in, value_in, grad_out, module_lengths):
    tok, width = query_in.shape
    prior = tok * lax.axis_size("head") // 8
    step = math.gcd(width, 8 * HEAD_DIM)
    groups = width // step
    anywhere = pl.BlockSpec(memory_space=pl.ANY)
    inside = pl.BlockSpec(memory_space=pltpu.VMEM)
    full16 = jax.ShapeDtypeStruct((tok, width), jnp.bfloat16)

    def near16(rows, columns):
        return pltpu.VMEM((rows, columns), jnp.bfloat16)

    def near32(rows, columns):
        return pltpu.VMEM((rows, columns), jnp.float32)

    def in_hbm(*values):
        return [pltpu.with_memory_space_constraint(value, pltpu.HBM) for value in values]

    def in_vmem(*values):
        return [pltpu.with_memory_space_constraint(value, pltpu.VMEM) for value in values]

    def call(kernel, name, ins, outs, shapes, scratch, work, moved, aliases=None):
        return pl.pallas_call(
            kernel,
            in_specs=ins,
            out_specs=outs,
            out_shape=shapes,
            scratch_shapes=scratch,
            input_output_aliases=aliases or {},
            cost_estimate=cost(*work, moved),
            compiler_params=pltpu.CompilerParams(vmem_limit_bytes=16 * 2**20),
            name=name,
        )

    near = call(
        functools.partial(pack_kernel, prior), "near_keys",
        [anywhere] * 2, inside, near16(prior, width),
        [pltpu.SemaphoreType.DMA((2,))], (0, 0, 0, 0), 4 * prior * width,
    )(*in_hbm(key_in, value_in))
    near = neighbour(near, 1)

    lengths = module_lengths.reshape(1, -1)
    far, q, k, v, do, own_bias, near_bias, lead_bias, tail_bias = call(
        functools.partial(ready_kernel, prior), "operands",
        [anywhere] * 5, [inside] * 9,
        [near16(prior, width)] + [near16(tok, width)] * 4
        + [near32(tok - prior, tok), near32(prior, prior + prior // 2)]
        + [near32(prior, 2 * prior), near32(prior, prior // 2)],
        [
            pltpu.VMEM(lengths.shape, jnp.int32), pltpu.SemaphoreType.DMA((4,)),
            pltpu.SemaphoreType.DMA((2,)), pltpu.SemaphoreType.DMA(()),
        ],
        (0, 0, 0, 0), 18 * tok * width,
    )(*in_hbm(lengths, query_in, key_in, value_in, grad_out))
    far = neighbour(far, 1)

    back = call(
        functools.partial(near_kernel, prior), "near_terms",
        [inside] * 7, inside, near16(prior, width), (),
        (width // HEAD_DIM, prior, prior + prior // 2, 3), 8 * tok * width,
    )(*in_vmem(near_bias, lead_bias, q, k, v, do, near))
    own_bias, back = lax.optimization_barrier((own_bias, back))
    back = neighbour(back, -1)

    attn, gq, gk_part, gv_part = call(
        functools.partial(own_kernel, prior, step), "own_block",
        [inside] * 5, [inside] * 4,
        [near16(tok - prior, width)] * 2 + [near32(tok, width)] * 2, (),
        (width // HEAD_DIM, tok - prior, tok, 6), 18 * tok * width,
    )(*in_vmem(own_bias, q, k, v, do))

    attn, gq, gk, gv = call(
        functools.partial(lead_kernel, prior, step), "lead_rows",
        [inside] * 11, [anywhere] * 4, [full16] * 4,
        [near16(prior, width)] * 4
        + [pltpu.SemaphoreType.DMA((groups, 4)), pltpu.SemaphoreType.DMA((2,))],
        (width // HEAD_DIM, prior, 2 * prior, 6), 20 * tok * width,
    )(*in_vmem(lead_bias, q, k, v, do, near, far, gk_part, gv_part, attn, gq))

    gk, gv = call(
        functools.partial(tail_kernel, prior, step), "tail_keys",
        [inside] * 6 + [anywhere] * 2, [anywhere] * 2, [full16] * 2,
        [near16(prior, width)] * 2 + [pltpu.SemaphoreType.DMA((2 * groups,))],
        (width // HEAD_DIM, prior, prior // 2, 4), 10 * tok * width, {6: 0, 7: 1},
    )(*in_vmem(tail_bias, k, v, back, gk_part, gv_part), gk, gv)
    return (attn, gq, gk, gv)


def shards(query_in, key_in, value_in, grad_out, module_lengths):
    tok = query_in.shape[0]
    prior = tok * lax.axis_size("head") // 8
    plan = halo_shards if 2 * prior == tok else gathered_shards
    return plan(query_in, key_in, value_in, grad_out, module_lengths)


def solution(mesh):
    placed = (
        P(("seq", "head"), None),
        P(("seq", "head"), None),
        P(("seq", "head"), None),
        P(("seq", "head"), None),
        P(),
    )
    return jax.shard_map(
        shards,
        mesh=mesh,
        in_specs=placed,
        out_specs=(
            P(("seq", "head"), None),
            P(("seq", "head"), None),
            P(("seq", "head"), None),
            P(("seq", "head"), None),
        ),
        check_vma=False,
    )
```

```python
import functools
import math

import jax
import jax.numpy as jnp
from jax import lax
from jax.experimental import pallas as pl
from jax.experimental.pallas import tpu as pltpu
from jax.sharding import PartitionSpec as P

HEAD_DIM = 128
SCALE = HEAD_DIM ** (-0.5)
LOG2E = math.log2(math.e)
MASKED = -1e30


def shifted(value, axis, by):
    peers = lax.axis_size(axis)
    pairs = [(i, i + by) for i in range(peers) if 0 <= i + by < peers]
    return lax.ppermute(value, axis, pairs)


def module_ids(module_lengths, positions):
    module_ends = jnp.cumsum(module_lengths)
    counted = jnp.sum((positions[:, None] >= module_ends[None, :]).astype(jnp.int32), axis=1)
    return jnp.where(positions >= 0, counted, -1)


def allowed_pairs(module_lengths, query_pos, key_pos):
    same = (
        module_ids(module_lengths, query_pos)[:, None]
        == module_ids(module_lengths, key_pos)[None, :]
    )
    return same & (key_pos[None, :] <= query_pos[:, None])


def score_grads(grad_rows, value_block, weights, row_delta, score_scale):
    dprobs = jnp.einsum("qd,kd->qk", grad_rows, value_block, preferred_element_type=jnp.float32)
    return (weights * (dprobs - row_delta[:, None]) * score_scale).astype(jnp.bfloat16)


def key_terms(dscores, weight_bf, query_rows, grad_rows):
    key_grad = jnp.einsum("qk,qd->kd", dscores, query_rows, preferred_element_type=jnp.float32)
    value_grad = jnp.einsum("qk,qd->kd", weight_bf, grad_rows, preferred_element_type=jnp.float32)
    return (key_grad, value_grad)


def one_block(query_rows, key_block, value_block, grad_rows, allowed, score_scale):
    scores = (
        jnp.einsum("qd,kd->qk", query_rows, key_block, preferred_element_type=jnp.float32)
        * score_scale
    )
    row_top = jnp.max(jnp.where(allowed, scores, -jnp.inf), axis=1, keepdims=True)
    row_total = jnp.sum(jnp.where(allowed, jnp.exp(scores - row_top), 0.0), axis=1, keepdims=True)
    log_total = row_top + jnp.log(row_total)
    weights = jnp.where(allowed, jnp.exp(scores - log_total), 0.0)
    weight_bf = weights.astype(jnp.bfloat16)
    attn_rows = jnp.einsum(
        "qk,kd->qd", weight_bf, value_block, preferred_element_type=jnp.float32
    ).astype(jnp.bfloat16)
    row_delta = jnp.sum(grad_rows.astype(jnp.float32) * attn_rows.astype(jnp.float32), axis=1)
    dscores = score_grads(grad_rows, value_block, weights, row_delta, score_scale)
    grad_q = jnp.einsum("qk,kd->qd", dscores, key_block, preferred_element_type=jnp.float32).astype(
        jnp.bfloat16
    )
    key_grad, value_grad = key_terms(dscores, weight_bf, query_rows, grad_rows)
    return (attn_rows, grad_q, key_grad, value_grad, log_total[:, 0], row_delta)


def gathered_shards(query_in, key_in, value_in, grad_out, module_lengths):
    head_q, head_k, head_v, head_do = (
        lax.all_to_all(query_in, "head", split_axis=1, concat_axis=0, tiled=True),
        lax.all_to_all(key_in, "head", split_axis=1, concat_axis=0, tiled=True),
        lax.all_to_all(value_in, "head", split_axis=1, concat_axis=0, tiled=True),
        lax.all_to_all(grad_out, "head", split_axis=1, concat_axis=0, tiled=True),
    )
    row_count = head_q.shape[0]
    width = head_q.shape[1]
    local_heads = width // HEAD_DIM
    prior_rows = row_count // 8
    score_scale = HEAD_DIM ** (-0.5)
    tail_start = row_count - prior_rows
    prior_k, prior_v = shifted((head_k[tail_start:], head_v[tail_start:]), "seq", 1)
    row_start = lax.axis_index("seq") * row_count
    query_pos = row_start + jnp.arange(row_count, dtype=jnp.int32)
    before_pos = row_start - prior_rows + jnp.arange(prior_rows, dtype=jnp.int32)
    key_pos = jnp.concatenate([before_pos, query_pos])
    block_rows = math.gcd(row_count, 512)
    block_count = row_count // block_rows
    pos_blocks = query_pos.reshape(block_count, block_rows)

    def by_head(flat, rows):
        return jnp.moveaxis(flat.reshape(rows, local_heads, HEAD_DIM), 1, 0)

    def to_flat(stacked):
        return jnp.moveaxis(stacked, 0, 1).reshape(stacked.shape[1], width)

    query_h = by_head(head_q, row_count)
    grad_h = by_head(head_do, row_count)
    key_h = by_head(jnp.concatenate([prior_k, head_k], axis=0), row_count + prior_rows)
    value_h = by_head(jnp.concatenate([prior_v, head_v], axis=0), row_count + prior_rows)

    def run_head(packed):
        query_rows, key_block, value_block, grad_rows = packed
        query_blocks = query_rows.reshape(block_count, block_rows, HEAD_DIM)
        grad_blocks = grad_rows.reshape(block_count, block_rows, HEAD_DIM)

        def run_block(inner):
            query_part, grad_part, pos_part = inner
            allowed = allowed_pairs(module_lengths, pos_part, key_pos)
            return one_block(query_part, key_block, value_block, grad_part, allowed, score_scale)

        attn_b, grad_qb, key_b, value_b, lse_b, delta_b = lax.map(
            run_block, (query_blocks, grad_blocks, pos_blocks)
        )
        return (
            attn_b.reshape(row_count, HEAD_DIM),
            grad_qb.reshape(row_count, HEAD_DIM),
            jnp.sum(key_b, axis=0),
            jnp.sum(value_b, axis=0),
            lse_b.reshape(row_count),
            delta_b.reshape(row_count),
        )

    attn_h, grad_qh, key_grad, value_grad, log_total, row_delta = lax.map(
        run_head, (query_h, key_h, value_h, grad_h)
    )
    attn_flat = to_flat(attn_h)
    attn_back = lax.all_to_all(attn_flat, "head", split_axis=0, concat_axis=1, tiled=True)
    grad_q = to_flat(grad_qh)
    later_k, later_v = shifted((key_grad[:, :prior_rows], value_grad[:, :prior_rows]), "seq", -1)
    key_total = key_grad[:, prior_rows:].at[:, tail_start:].add(later_k)
    value_total = value_grad[:, prior_rows:].at[:, tail_start:].add(later_v)
    grad_k = to_flat(key_total.astype(jnp.bfloat16))
    grad_v = to_flat(value_total.astype(jnp.bfloat16))
    back_q, back_k, back_v = (
        lax.all_to_all(grad_q, "head", split_axis=0, concat_axis=1, tiled=True),
        lax.all_to_all(grad_k, "head", split_axis=0, concat_axis=1, tiled=True),
        lax.all_to_all(grad_v, "head", split_axis=0, concat_axis=1, tiled=True),
    )
    return (attn_back, back_q, back_k, back_v)


def dot(left, right, left_dim, right_dim):
    return lax.dot_general(
        left, right, (((left_dim,), (right_dim,)), ((), ())), preferred_element_type=jnp.float32
    )


def module_ends_row(lengths_row):
    count = lengths_row.shape[1]
    row = lax.broadcasted_iota(jnp.int32, (count, count), 0)
    col = lax.broadcasted_iota(jnp.int32, (count, count), 1)
    lengths_col = jnp.sum(jnp.where(row == col, lengths_row, 0.0), axis=1, keepdims=True)
    return jnp.sum(jnp.where(row <= col, lengths_col, 0.0), axis=0, keepdims=True)


def module_ends_col(lengths_row):
    count = lengths_row.shape[1]
    row = lax.broadcasted_iota(jnp.int32, (count, count), 0)
    col = lax.broadcasted_iota(jnp.int32, (count, count), 1)
    return jnp.sum(jnp.where(col <= row, lengths_row, 0.0), axis=1, keepdims=True)


def bias_by_query(lengths_row, first_query, queries, first_key, keys):
    ends = module_ends_row(lengths_row)
    query = (first_query + lax.broadcasted_iota(jnp.int32, (queries, 1), 0)).astype(jnp.float32)
    start = jnp.max(jnp.where(ends <= query, ends, 0.0), axis=1, keepdims=True)
    key = (first_key + lax.broadcasted_iota(jnp.int32, (queries, keys), 1)).astype(jnp.float32)
    return jnp.where((key >= start) & (key <= query), 0.0, MASKED)


def bias_by_key(lengths_row, first_query, queries, first_key, keys, heads):
    ends = module_ends_col(lengths_row)
    lane = lax.broadcasted_iota(jnp.int32, (1, heads * queries), 1)
    query = (first_query + lane % queries).astype(jnp.float32)
    start = jnp.max(jnp.where(ends <= query, ends, 0.0), axis=0, keepdims=True)
    key = (first_key + lax.broadcasted_iota(jnp.int32, (keys, heads * queries), 0)).astype(
        jnp.float32
    )
    return jnp.where((key >= start) & (key <= query), 0.0, MASKED)


def by_query(q, k, do, v, bias):
    scores = dot(q, k, 1, 1) * (SCALE * LOG2E) + bias
    return scores, dot(do, v, 1, 1)


def full_rows(pairs):
    tops = [jnp.max(s, axis=1, keepdims=True) for s, _ in pairs]
    raws = [jnp.exp2(s - top) for (s, _), top in zip(pairs, tops)]
    weights = [raw * (1.0 / jnp.sum(raw, axis=1, keepdims=True)) for raw in raws]
    deltas = [jnp.sum(w * dp, axis=1, keepdims=True) for w, (_, dp) in zip(weights, pairs)]
    grads = [w * (dp - delta) * SCALE for w, (_, dp), delta in zip(weights, pairs, deltas)]
    return [w.astype(jnp.bfloat16) for w in weights], [g.astype(jnp.bfloat16) for g in grads]


def merged_columns(pairs, own):
    tops = [
        jnp.maximum(jnp.max(s, axis=0, keepdims=True), log) for (s, _), (log, _) in zip(pairs, own)
    ]
    raws = [jnp.exp2(s - top) for (s, _), top in zip(pairs, tops)]
    own_raws = [jnp.exp2(log - top) for (log, _), top in zip(own, tops)]
    parts = [
        1.0 / (jnp.sum(raw, axis=0, keepdims=True) + own_raw)
        for raw, own_raw in zip(raws, own_raws)
    ]
    weights = [raw * part for raw, part in zip(raws, parts)]
    deltas = [
        jnp.sum(w * dp, axis=0, keepdims=True) + own_raw * part * own_delta
        for w, (_, dp), own_raw, part, (_, own_delta) in zip(weights, pairs, own_raws, parts, own)
    ]
    grads = [w * (dp - delta) * SCALE for w, (_, dp), delta in zip(weights, pairs, deltas)]
    return [w.astype(jnp.bfloat16) for w in weights], [g.astype(jnp.bfloat16) for g in grads]


def side_by_side(rows):
    heads = rows.shape[1] // HEAD_DIM
    zero = jnp.zeros((rows.shape[0], HEAD_DIM), rows.dtype)
    blocks = [rows[:, c] for c in head_columns(0, rows.shape[1])]
    return jnp.concatenate(
        [
            jnp.concatenate([blocks[h] if g == h else zero for g in range(heads)], axis=1)
            for h in range(heads)
        ],
        axis=0,
    )


def head_columns(low, high, heads=1):
    wide = heads * HEAD_DIM
    return [slice(c, c + wide) for c in range(low, high, wide)]


def device_first(tok):
    place = lax.axis_index("seq") * lax.axis_size("head") + lax.axis_index("head")
    return place * tok


def fours(rows):
    table = jnp.concatenate(rows, axis=0)
    half = table.shape[1] // 4
    lane = lax.broadcasted_iota(jnp.int32, (1, table.shape[1]), 1)
    turned = [pltpu.roll(table, turn * half, 1) for turn in (3, 2, 1)]
    merged = []
    for at in range(0, len(rows), 2):
        now, after = slice(at, at + 1), slice(at + 1, at + 2)
        row = jnp.where(lane < 3 * half, turned[1][after], turned[2][after])
        row = jnp.where(lane < 2 * half, turned[0][now], row)
        merged.append(jnp.where(lane < half, table[now], row))
    return merged


def split_bf16(row):
    parts = []
    for _ in range(3):
        part = row.astype(jnp.bfloat16)
        parts.append(part)
        row = row - part.astype(jnp.float32)
    return jnp.concatenate([*parts, jnp.zeros_like(parts[0])], axis=1)


def joined(parts):
    parts = parts.astype(jnp.float32)
    count = parts.shape[1] // 4
    return parts[:, :count] + parts[:, count : 2 * count] + parts[:, 2 * count : 3 * count]


def pack_copies(prior, at, k_ref, v_ref, packed_ref, sems):
    half, tok = prior // 2, k_ref.shape[0]
    rows = pl.ds(tok - (at + 1) * half, half)
    return [
        pltpu.make_async_copy(
            ref.at[rows, :], packed_ref.at[pl.ds(n * half, half), :], sems.at[n]
        )
        for n, ref in enumerate((k_ref, v_ref))
    ]


def pack_kernel(prior, k_ref, v_ref, near_ref, sems):
    copies = pack_copies(prior, 0, k_ref, v_ref, near_ref, sems)
    for copy in copies:
        copy.start()
    for copy in copies:
        copy.wait()


def ready_kernel(
    prior, len_hbm, q_hbm, k_hbm, v_hbm, do_hbm, far_ref, q_ref, k_ref, v_ref, do_ref,
    own_bias_ref, near_bias_ref, lead_bias_ref, tail_bias_ref, len_ref, sems, far_sems, len_sem,
):
    tok, half = k_ref.shape[0], prior // 2
    pairs = ((q_hbm, q_ref), (k_hbm, k_ref), (v_hbm, v_ref), (do_hbm, do_ref))
    copies = pack_copies(prior, 1, k_hbm, v_hbm, far_ref, far_sems)
    copies += [pltpu.make_async_copy(hbm, ref, sems.at[n]) for n, (hbm, ref) in enumerate(pairs)]
    len_copy = pltpu.make_async_copy(len_hbm, len_ref, len_sem)
    len_copy.start()
    for copy in copies:
        copy.start()
    len_copy.wait()
    first = device_first(tok)
    lengths = len_ref[...].astype(jnp.float32)
    own_bias_ref[...] = bias_by_query(lengths, first + prior, tok - prior, first, tok)
    near_bias_ref[...] = bias_by_key(lengths, first, prior, first - half, prior + half, 2)
    lead_bias_ref[...] = bias_by_query(lengths, first, prior, first - prior, 2 * prior)
    tail_bias_ref[...] = bias_by_key(lengths, first + tok, half, first + tok - prior, prior, 4)
    for copy in copies:
        copy.wait()


def own_kernel(
    prior, step, bias_ref, q_ref, k_ref, v_ref, do_ref, attn_ref, gq_ref, gk_ref, gv_ref
):
    tok, width = k_ref.shape
    late = slice(prior, tok)

    @pl.loop(0, width // step)
    def _(at):
        bias = bias_ref[...]
        columns = [
            pl.ds(pl.multiple_of(at * step + c, HEAD_DIM), HEAD_DIM)
            for c in range(0, step, HEAD_DIM)
        ]
        pairs = [
            by_query(q_ref[late, c], k_ref[:, c], do_ref[late, c], v_ref[:, c], bias)
            for c in columns
        ]
        weights, grads = full_rows(pairs)
        for c, w, g in zip(columns, weights, grads):
            attn_ref[:, c] = dot(w, v_ref[:, c], 1, 0).astype(jnp.bfloat16)
            gq_ref[:, c] = dot(g, k_ref[:, c], 1, 0).astype(jnp.bfloat16)
            gk_ref[:, c] = dot(g, q_ref[late, c], 0, 0)
            gv_ref[:, c] = dot(w, do_ref[late, c], 0, 0)


def near_kernel(
    prior, near_bias_ref, lead_bias_ref, q_ref, k_ref, v_ref, do_ref, near_ref, back_ref
):
    half = prior // 2
    far = lead_bias_ref[0:1, half - 1 : half] == 0.0
    key = lax.broadcasted_iota(jnp.int32, (prior + half, 1), 0)
    bias = jnp.where(far & (key < half), MASKED, near_bias_ref[...])
    spare = lax.broadcasted_iota(jnp.int32, (half, 1), 0) == half - 1
    early, first, second = slice(0, prior), slice(0, half), slice(half, prior)
    columns = head_columns(0, q_ref.shape[1], 2)
    queries = [side_by_side(q_ref[early, c]) for c in columns]
    cotangents = [side_by_side(do_ref[early, c]) for c in columns]
    pairs = []
    for c, q, do in zip(columns, queries, cotangents):
        k = jnp.concatenate([near_ref[first, c], k_ref[early, c]], axis=0)
        v = jnp.concatenate([near_ref[second, c], v_ref[early, c]], axis=0)
        pairs.append(by_query(k, q, v, do, bias))
    tops = [jnp.max(s, axis=0, keepdims=True) for s, _ in pairs]
    raws = [jnp.exp2(s - top) for (s, _), top in zip(pairs, tops)]
    totals = [jnp.sum(raw, axis=0, keepdims=True) for raw in raws]
    weights = [raw * (1.0 / total) for raw, total in zip(raws, totals)]
    deltas = [jnp.sum(w * dp, axis=0, keepdims=True) for w, (_, dp) in zip(weights, pairs)]
    grads = [
        w[:half] * (dp[:half] - delta) * SCALE for w, (_, dp), delta in zip(weights, pairs, deltas)
    ]
    k_terms = [dot(g.astype(jnp.bfloat16), q, 1, 0) for g, q in zip(grads, queries)]
    v_terms = [dot(w[:half].astype(jnp.bfloat16), do, 1, 0) for w, do in zip(weights, cotangents)]
    logs = fours([top + jnp.log2(total) for top, total in zip(tops, totals)])
    deltas = fours(deltas)
    for at, c in enumerate(head_columns(0, q_ref.shape[1], 4)):
        for row, terms, ref, place in (
            (logs[at], k_terms, q_ref, first), (deltas[at], v_terms, do_ref, second)
        ):
            here = jnp.where(spare, split_bf16(row), ref[first, c])
            terms = jnp.concatenate(terms[2 * at : 2 * at + 2], axis=1).astype(jnp.bfloat16)
            back_ref[place, c] = jnp.where(far, here, terms)


def lead_kernel(
    prior, step, bias_ref, q_ref, k_ref, v_ref, do_ref, near_ref, far_ref, gk_part_ref, gv_part_ref,
    attn_late_ref, gq_late_ref, attn_hbm, gq_hbm, gk_hbm, gv_hbm,
    attn_ref, gq_ref, gk_ref, gv_ref, sems, late_sems,
):
    tok, width = q_ref.shape
    half = prior // 2
    early, first, second = slice(0, prior), slice(0, half), slice(half, prior)
    late = pl.ds(prior, tok - prior)
    late_copies = [
        pltpu.make_async_copy(attn_late_ref, attn_hbm.at[late, :], late_sems.at[0]),
        pltpu.make_async_copy(gq_late_ref, gq_hbm.at[late, :], late_sems.at[1]),
    ]
    for copy in late_copies:
        copy.start()

    def copies(at):
        cols = pl.ds(pl.multiple_of(at * step, step), step)
        pairs = ((attn_ref, attn_hbm), (gq_ref, gq_hbm), (gk_ref, gk_hbm), (gv_ref, gv_hbm))
        return [
            pltpu.make_async_copy(ref.at[:, cols], hbm.at[pl.ds(0, prior), cols], sems.at[at, n])
            for n, (ref, hbm) in enumerate(pairs)
        ]

    @pl.loop(0, width // step)
    def _(at):
        bias = bias_ref[...]
        columns = [
            pl.ds(pl.multiple_of(at * step + c, HEAD_DIM), HEAD_DIM)
            for c in range(0, step, HEAD_DIM)
        ]
        keys = [
            jnp.concatenate([far_ref[first, c], near_ref[first, c], k_ref[early, c]], axis=0)
            for c in columns
        ]
        values = [
            jnp.concatenate([far_ref[second, c], near_ref[second, c], v_ref[early, c]], axis=0)
            for c in columns
        ]
        pairs = [
            by_query(q_ref[early, c], k, do_ref[early, c], v, bias)
            for c, k, v in zip(columns, keys, values)
        ]
        weights, grads = full_rows(pairs)
        for c, w, g, k, v in zip(columns, weights, grads, keys, values):
            attn_ref[:, c] = dot(w, v, 1, 0).astype(jnp.bfloat16)
            gq_ref[:, c] = dot(g, k, 1, 0).astype(jnp.bfloat16)
            gk = dot(g, q_ref[early, c], 0, 0)
            gv = dot(w, do_ref[early, c], 0, 0)
            gk_ref[:, c] = (gk_part_ref[early, c] + gk[prior:]).astype(jnp.bfloat16)
            gv_ref[:, c] = (gv_part_ref[early, c] + gv[prior:]).astype(jnp.bfloat16)
        for copy in copies(at):
            copy.start()

    for at in range(width // step):
        for copy in copies(at):
            copy.wait()
    for copy in late_copies:
        copy.wait()


def tail_kernel(
    prior, step, bias_ref, k_ref, v_ref, after_ref, gk_part_ref, gv_part_ref, gk_in, gv_in,
    gk_hbm, gv_hbm, gk_ref, gv_ref, sems,
):
    tok, width = k_ref.shape
    half = prior // 2
    far = bias_ref[half - 1 : half, 0:1] == 0.0
    bias = jnp.where(far, bias_ref[...], MASKED)
    first, second, last = slice(0, half), slice(half, prior), slice(tok - prior, tok)
    copies = []
    for low in range(0, width, step):
        columns = head_columns(low, low + step, 4)
        queries = [side_by_side(after_ref[first, c]) for c in columns]
        cotangents = [side_by_side(after_ref[second, c]) for c in columns]
        pairs = [
            by_query(k_ref[last, c], q, v_ref[last, c], do, bias)
            for c, q, do in zip(columns, queries, cotangents)
        ]
        own = [
            (joined(after_ref[half - 1 : half, c]), joined(after_ref[prior - 1 : prior, c]))
            for c in columns
        ]
        weights, grads = merged_columns(pairs, own)
        for c, w, g, q, do in zip(columns, weights, grads, queries, cotangents):
            for out_ref, part_ref, left, right, rows in (
                (gk_ref, gk_part_ref, g, q, first), (gv_ref, gv_part_ref, w, do, second)
            ):
                total = part_ref[last, c] + dot(left, right, 1, 0)
                terms = jnp.where(far, 0.0, after_ref[rows, c].astype(jnp.float32))
                out_ref[first, c] = total[first].astype(jnp.bfloat16)
                out_ref[second, c] = (total[second] + terms).astype(jnp.bfloat16)
        cols = pl.ds(low, step)
        for ref, hbm in ((gk_ref, gk_hbm), (gv_ref, gv_hbm)):
            copies.append(
                pltpu.make_async_copy(
                    ref.at[:, cols], hbm.at[pl.ds(tok - prior, prior), cols], sems.at[len(copies)]
                )
            )
            copies[-1].start()
    for copy in copies:
        copy.wait()


def neighbour(value, by):
    peers = lax.axis_size("seq") * lax.axis_size("head")
    pairs = [(i, i + by) for i in range(peers) if 0 <= i + by < peers]
    return lax.ppermute(value, ("seq", "head"), pairs)


def cost(heads, queries, keys, products, moved):
    return pl.CostEstimate(
        flops=2 * heads * queries * keys * HEAD_DIM * products,
        bytes_accessed=moved,
        transcendentals=heads * queries * keys,
    )


def halo_shards(query_in, key_in, value_in, grad_out, module_lengths):
    tok, width = query_in.shape
    prior = tok * lax.axis_size("head") // 8
    step = math.gcd(width, 8 * HEAD_DIM)
    groups = width // step
    anywhere = pl.BlockSpec(memory_space=pl.ANY)
    inside = pl.BlockSpec(memory_space=pltpu.VMEM)
    full16 = jax.ShapeDtypeStruct((tok, width), jnp.bfloat16)

    def near16(rows, columns):
        return pltpu.VMEM((rows, columns), jnp.bfloat16)

    def near32(rows, columns):
        return pltpu.VMEM((rows, columns), jnp.float32)

    def in_hbm(*values):
        return [pltpu.with_memory_space_constraint(value, pltpu.HBM) for value in values]

    def in_vmem(*values):
        return [pltpu.with_memory_space_constraint(value, pltpu.VMEM) for value in values]

    def call(kernel, name, ins, outs, shapes, scratch, work, moved, aliases=None):
        return pl.pallas_call(
            kernel,
            in_specs=ins,
            out_specs=outs,
            out_shape=shapes,
            scratch_shapes=scratch,
            input_output_aliases=aliases or {},
            cost_estimate=cost(*work, moved),
            compiler_params=pltpu.CompilerParams(vmem_limit_bytes=16 * 2**20),
            name=name,
        )

    near = call(
        functools.partial(pack_kernel, prior), "near_keys",
        [anywhere] * 2, inside, near16(prior, width),
        [pltpu.SemaphoreType.DMA((2,))], (0, 0, 0, 0), 4 * prior * width,
    )(*in_hbm(key_in, value_in))
    near = neighbour(near, 1)

    lengths = module_lengths.reshape(1, -1)
    far, q, k, v, do, own_bias, near_bias, lead_bias, tail_bias = call(
        functools.partial(ready_kernel, prior), "operands",
        [anywhere] * 5, [inside] * 9,
        [near16(prior, width)] + [near16(tok, width)] * 4
        + [near32(tok - prior, tok), near32(prior + prior // 2, 2 * prior)]
        + [near32(prior, 2 * prior), near32(prior, 2 * prior)],
        [
            pltpu.VMEM(lengths.shape, jnp.int32), pltpu.SemaphoreType.DMA((4,)),
            pltpu.SemaphoreType.DMA((2,)), pltpu.SemaphoreType.DMA(()),
        ],
        (0, 0, 0, 0), 18 * tok * width,
    )(*in_hbm(lengths, query_in, key_in, value_in, grad_out))
    far = neighbour(far, 1)

    back = call(
        functools.partial(near_kernel, prior), "near_terms",
        [inside] * 7, inside, near16(prior, width), (),
        (width // HEAD_DIM, prior, prior + prior // 2, 3), 8 * tok * width,
    )(*in_vmem(near_bias, lead_bias, q, k, v, do, near))
    own_bias, back = lax.optimization_barrier((own_bias, back))
    back = neighbour(back, -1)

    attn, gq, gk_part, gv_part = call(
        functools.partial(own_kernel, prior, step), "own_block",
        [inside] * 5, [inside] * 4,
        [near16(tok - prior, width)] * 2 + [near32(tok, width)] * 2, (),
        (width // HEAD_DIM, tok - prior, tok, 6), 18 * tok * width,
    )(*in_vmem(own_bias, q, k, v, do))

    attn, gq, gk, gv = call(
        functools.partial(lead_kernel, prior, step), "lead_rows",
        [inside] * 11, [anywhere] * 4, [full16] * 4,
        [near16(prior, width)] * 4
        + [pltpu.SemaphoreType.DMA((groups, 4)), pltpu.SemaphoreType.DMA((2,))],
        (width // HEAD_DIM, prior, 2 * prior, 6), 20 * tok * width,
    )(*in_vmem(lead_bias, q, k, v, do, near, far, gk_part, gv_part, attn, gq))

    gk, gv = call(
        functools.partial(tail_kernel, prior, step), "tail_keys",
        [inside] * 6 + [anywhere] * 2, [anywhere] * 2, [full16] * 2,
        [near16(prior, width)] * 2 + [pltpu.SemaphoreType.DMA((2 * groups,))],
        (width // HEAD_DIM, prior, prior // 2, 4), 10 * tok * width, {6: 0, 7: 1},
    )(*in_vmem(tail_bias, k, v, back, gk_part, gv_part), gk, gv)
    return (attn, gq, gk, gv)


def shards(query_in, key_in, value_in, grad_out, module_lengths):
    tok = query_in.shape[0]
    prior = tok * lax.axis_size("head") // 8
    plan = halo_shards if 2 * prior == tok else gathered_shards
    return plan(query_in, key_in, value_in, grad_out, module_lengths)


def solution(mesh):
    placed = (
        P(("seq", "head"), None),
        P(("seq", "head"), None),
        P(("seq", "head"), None),
        P(("seq", "head"), None),
        P(),
    )
    return jax.shard_map(
        shards,
        mesh=mesh,
        in_specs=placed,
        out_specs=(
            P(("seq", "head"), None),
            P(("seq", "head"), None),
            P(("seq", "head"), None),
            P(("seq", "head"), None),
        ),
        check_vma=False,
    )
```

```python
import functools
import math

import jax
import jax.numpy as jnp
from jax import lax
from jax.experimental import pallas as pl
from jax.experimental.pallas import tpu as pltpu
from jax.sharding import PartitionSpec as P

HEAD_DIM = 128
SCALE = HEAD_DIM ** (-0.5)
LOG2E = math.log2(math.e)
MASKED = -1e30


def shifted(value, axis, by):
    peers = lax.axis_size(axis)
    pairs = [(i, i + by) for i in range(peers) if 0 <= i + by < peers]
    return lax.ppermute(value, axis, pairs)


def module_ids(module_lengths, positions):
    module_ends = jnp.cumsum(module_lengths)
    counted = jnp.sum((positions[:, None] >= module_ends[None, :]).astype(jnp.int32), axis=1)
    return jnp.where(positions >= 0, counted, -1)


def allowed_pairs(module_lengths, query_pos, key_pos):
    same = (
        module_ids(module_lengths, query_pos)[:, None]
        == module_ids(module_lengths, key_pos)[None, :]
    )
    return same & (key_pos[None, :] <= query_pos[:, None])


def score_grads(grad_rows, value_block, weights, row_delta, score_scale):
    dprobs = jnp.einsum("qd,kd->qk", grad_rows, value_block, preferred_element_type=jnp.float32)
    return (weights * (dprobs - row_delta[:, None]) * score_scale).astype(jnp.bfloat16)


def key_terms(dscores, weight_bf, query_rows, grad_rows):
    key_grad = jnp.einsum("qk,qd->kd", dscores, query_rows, preferred_element_type=jnp.float32)
    value_grad = jnp.einsum("qk,qd->kd", weight_bf, grad_rows, preferred_element_type=jnp.float32)
    return (key_grad, value_grad)


def one_block(query_rows, key_block, value_block, grad_rows, allowed, score_scale):
    scores = (
        jnp.einsum("qd,kd->qk", query_rows, key_block, preferred_element_type=jnp.float32)
        * score_scale
    )
    row_top = jnp.max(jnp.where(allowed, scores, -jnp.inf), axis=1, keepdims=True)
    row_total = jnp.sum(jnp.where(allowed, jnp.exp(scores - row_top), 0.0), axis=1, keepdims=True)
    log_total = row_top + jnp.log(row_total)
    weights = jnp.where(allowed, jnp.exp(scores - log_total), 0.0)
    weight_bf = weights.astype(jnp.bfloat16)
    attn_rows = jnp.einsum(
        "qk,kd->qd", weight_bf, value_block, preferred_element_type=jnp.float32
    ).astype(jnp.bfloat16)
    row_delta = jnp.sum(grad_rows.astype(jnp.float32) * attn_rows.astype(jnp.float32), axis=1)
    dscores = score_grads(grad_rows, value_block, weights, row_delta, score_scale)
    grad_q = jnp.einsum("qk,kd->qd", dscores, key_block, preferred_element_type=jnp.float32).astype(
        jnp.bfloat16
    )
    key_grad, value_grad = key_terms(dscores, weight_bf, query_rows, grad_rows)
    return (attn_rows, grad_q, key_grad, value_grad, log_total[:, 0], row_delta)


def gathered_shards(query_in, key_in, value_in, grad_out, module_lengths):
    head_q, head_k, head_v, head_do = (
        lax.all_to_all(query_in, "head", split_axis=1, concat_axis=0, tiled=True),
        lax.all_to_all(key_in, "head", split_axis=1, concat_axis=0, tiled=True),
        lax.all_to_all(value_in, "head", split_axis=1, concat_axis=0, tiled=True),
        lax.all_to_all(grad_out, "head", split_axis=1, concat_axis=0, tiled=True),
    )
    row_count = head_q.shape[0]
    width = head_q.shape[1]
    local_heads = width // HEAD_DIM
    prior_rows = row_count // 8
    score_scale = HEAD_DIM ** (-0.5)
    tail_start = row_count - prior_rows
    prior_k, prior_v = shifted((head_k[tail_start:], head_v[tail_start:]), "seq", 1)
    row_start = lax.axis_index("seq") * row_count
    query_pos = row_start + jnp.arange(row_count, dtype=jnp.int32)
    before_pos = row_start - prior_rows + jnp.arange(prior_rows, dtype=jnp.int32)
    key_pos = jnp.concatenate([before_pos, query_pos])
    block_rows = math.gcd(row_count, 512)
    block_count = row_count // block_rows
    pos_blocks = query_pos.reshape(block_count, block_rows)

    def by_head(flat, rows):
        return jnp.moveaxis(flat.reshape(rows, local_heads, HEAD_DIM), 1, 0)

    def to_flat(stacked):
        return jnp.moveaxis(stacked, 0, 1).reshape(stacked.shape[1], width)

    query_h = by_head(head_q, row_count)
    grad_h = by_head(head_do, row_count)
    key_h = by_head(jnp.concatenate([prior_k, head_k], axis=0), row_count + prior_rows)
    value_h = by_head(jnp.concatenate([prior_v, head_v], axis=0), row_count + prior_rows)

    def run_head(packed):
        query_rows, key_block, value_block, grad_rows = packed
        query_blocks = query_rows.reshape(block_count, block_rows, HEAD_DIM)
        grad_blocks = grad_rows.reshape(block_count, block_rows, HEAD_DIM)

        def run_block(inner):
            query_part, grad_part, pos_part = inner
            allowed = allowed_pairs(module_lengths, pos_part, key_pos)
            return one_block(query_part, key_block, value_block, grad_part, allowed, score_scale)

        attn_b, grad_qb, key_b, value_b, lse_b, delta_b = lax.map(
            run_block, (query_blocks, grad_blocks, pos_blocks)
        )
        return (
            attn_b.reshape(row_count, HEAD_DIM),
            grad_qb.reshape(row_count, HEAD_DIM),
            jnp.sum(key_b, axis=0),
            jnp.sum(value_b, axis=0),
            lse_b.reshape(row_count),
            delta_b.reshape(row_count),
        )

    attn_h, grad_qh, key_grad, value_grad, log_total, row_delta = lax.map(
        run_head, (query_h, key_h, value_h, grad_h)
    )
    attn_flat = to_flat(attn_h)
    attn_back = lax.all_to_all(attn_flat, "head", split_axis=0, concat_axis=1, tiled=True)
    grad_q = to_flat(grad_qh)
    later_k, later_v = shifted((key_grad[:, :prior_rows], value_grad[:, :prior_rows]), "seq", -1)
    key_total = key_grad[:, prior_rows:].at[:, tail_start:].add(later_k)
    value_total = value_grad[:, prior_rows:].at[:, tail_start:].add(later_v)
    grad_k = to_flat(key_total.astype(jnp.bfloat16))
    grad_v = to_flat(value_total.astype(jnp.bfloat16))
    back_q, back_k, back_v = (
        lax.all_to_all(grad_q, "head", split_axis=0, concat_axis=1, tiled=True),
        lax.all_to_all(grad_k, "head", split_axis=0, concat_axis=1, tiled=True),
        lax.all_to_all(grad_v, "head", split_axis=0, concat_axis=1, tiled=True),
    )
    return (attn_back, back_q, back_k, back_v)


def dot(left, right, left_dim, right_dim):
    return lax.dot_general(
        left, right, (((left_dim,), (right_dim,)), ((), ())), preferred_element_type=jnp.float32
    )


def module_ends_row(lengths_row):
    count = lengths_row.shape[1]
    row = lax.broadcasted_iota(jnp.int32, (count, count), 0)
    col = lax.broadcasted_iota(jnp.int32, (count, count), 1)
    lengths_col = jnp.sum(jnp.where(row == col, lengths_row, 0.0), axis=1, keepdims=True)
    return jnp.sum(jnp.where(row <= col, lengths_col, 0.0), axis=0, keepdims=True)


def module_ends_col(lengths_row):
    count = lengths_row.shape[1]
    row = lax.broadcasted_iota(jnp.int32, (count, count), 0)
    col = lax.broadcasted_iota(jnp.int32, (count, count), 1)
    return jnp.sum(jnp.where(col <= row, lengths_row, 0.0), axis=1, keepdims=True)


def bias_by_query(lengths_row, first_query, queries, first_key, keys):
    ends = module_ends_row(lengths_row)
    query = (first_query + lax.broadcasted_iota(jnp.int32, (queries, 1), 0)).astype(jnp.float32)
    start = jnp.max(jnp.where(ends <= query, ends, 0.0), axis=1, keepdims=True)
    key = (first_key + lax.broadcasted_iota(jnp.int32, (queries, keys), 1)).astype(jnp.float32)
    return jnp.where((key >= start) & (key <= query), 0.0, MASKED)


def bias_by_key(lengths_row, first_query, queries, first_key, keys, heads):
    ends = module_ends_col(lengths_row)
    lane = lax.broadcasted_iota(jnp.int32, (1, heads * queries), 1)
    query = (first_query + lane % queries).astype(jnp.float32)
    start = jnp.max(jnp.where(ends <= query, ends, 0.0), axis=0, keepdims=True)
    key = (first_key + lax.broadcasted_iota(jnp.int32, (keys, heads * queries), 0)).astype(
        jnp.float32
    )
    return jnp.where((key >= start) & (key <= query), 0.0, MASKED)


def by_query(q, k, do, v, bias):
    scores = dot(q, k, 1, 1) * (SCALE * LOG2E) + bias
    return scores, dot(do, v, 1, 1)


def full_rows(pairs):
    tops = [jnp.max(s, axis=1, keepdims=True) for s, _ in pairs]
    raws = [jnp.exp2(s - top) for (s, _), top in zip(pairs, tops)]
    weights = [raw * (1.0 / jnp.sum(raw, axis=1, keepdims=True)) for raw in raws]
    deltas = [jnp.sum(w * dp, axis=1, keepdims=True) for w, (_, dp) in zip(weights, pairs)]
    grads = [w * (dp - delta) * SCALE for w, (_, dp), delta in zip(weights, pairs, deltas)]
    return [w.astype(jnp.bfloat16) for w in weights], [g.astype(jnp.bfloat16) for g in grads]


def merged_columns(pairs, own):
    tops = [
        jnp.maximum(jnp.max(s, axis=0, keepdims=True), log) for (s, _), (log, _) in zip(pairs, own)
    ]
    raws = [jnp.exp2(s - top) for (s, _), top in zip(pairs, tops)]
    own_raws = [jnp.exp2(log - top) for (log, _), top in zip(own, tops)]
    parts = [
        1.0 / (jnp.sum(raw, axis=0, keepdims=True) + own_raw)
        for raw, own_raw in zip(raws, own_raws)
    ]
    weights = [raw * part for raw, part in zip(raws, parts)]
    deltas = [
        jnp.sum(w * dp, axis=0, keepdims=True) + own_raw * part * own_delta
        for w, (_, dp), own_raw, part, (_, own_delta) in zip(weights, pairs, own_raws, parts, own)
    ]
    grads = [w * (dp - delta) * SCALE for w, (_, dp), delta in zip(weights, pairs, deltas)]
    return [w.astype(jnp.bfloat16) for w in weights], [g.astype(jnp.bfloat16) for g in grads]


def side_by_side(rows):
    heads = rows.shape[1] // HEAD_DIM
    zero = jnp.zeros((rows.shape[0], HEAD_DIM), rows.dtype)
    blocks = [rows[:, c] for c in head_columns(0, rows.shape[1])]
    return jnp.concatenate(
        [
            jnp.concatenate([blocks[h] if g == h else zero for g in range(heads)], axis=1)
            for h in range(heads)
        ],
        axis=0,
    )


def head_columns(low, high, heads=1):
    wide = heads * HEAD_DIM
    return [slice(c, c + wide) for c in range(low, high, wide)]


def device_first(tok):
    place = lax.axis_index("seq") * lax.axis_size("head") + lax.axis_index("head")
    return place * tok


def fours(rows):
    table = jnp.concatenate(rows, axis=0)
    half = table.shape[1] // 4
    lane = lax.broadcasted_iota(jnp.int32, (1, table.shape[1]), 1)
    turned = [pltpu.roll(table, turn * half, 1) for turn in (3, 2, 1)]
    merged = []
    for at in range(0, len(rows), 2):
        now, after = slice(at, at + 1), slice(at + 1, at + 2)
        row = jnp.where(lane < 3 * half, turned[1][after], turned[2][after])
        row = jnp.where(lane < 2 * half, turned[0][now], row)
        merged.append(jnp.where(lane < half, table[now], row))
    return merged


def split_bf16(row):
    parts = []
    for _ in range(3):
        part = row.astype(jnp.bfloat16)
        parts.append(part)
        row = row - part.astype(jnp.float32)
    return jnp.concatenate([*parts, jnp.zeros_like(parts[0])], axis=1)


def joined(parts):
    parts = parts.astype(jnp.float32)
    count = parts.shape[1] // 4
    return parts[:, :count] + parts[:, count : 2 * count] + parts[:, 2 * count : 3 * count]


def pack_copies(prior, at, k_ref, v_ref, packed_ref, sems):
    half, tok = prior // 2, k_ref.shape[0]
    rows = pl.ds(tok - (at + 1) * half, half)
    return [
        pltpu.make_async_copy(
            ref.at[rows, :], packed_ref.at[pl.ds(n * half, half), :], sems.at[n]
        )
        for n, ref in enumerate((k_ref, v_ref))
    ]


def pack_kernel(prior, k_ref, v_ref, near_ref, far_ref, near_sems, far_sems):
    copies = pack_copies(prior, 0, k_ref, v_ref, near_ref, near_sems)
    copies += pack_copies(prior, 1, k_ref, v_ref, far_ref, far_sems)
    for copy in copies:
        copy.start()
    for copy in copies:
        copy.wait()


def ready_kernel(
    prior, len_hbm, q_hbm, k_hbm, v_hbm, do_hbm, q_ref, k_ref, v_ref, do_ref,
    own_bias_ref, near_bias_ref, lead_bias_ref, tail_bias_ref, len_ref, sems, len_sem,
):
    tok, half = k_ref.shape[0], prior // 2
    pairs = ((q_hbm, q_ref), (k_hbm, k_ref), (v_hbm, v_ref), (do_hbm, do_ref))
    copies = [pltpu.make_async_copy(hbm, ref, sems.at[n]) for n, (hbm, ref) in enumerate(pairs)]
    len_copy = pltpu.make_async_copy(len_hbm, len_ref, len_sem)
    len_copy.start()
    for copy in copies:
        copy.start()
    len_copy.wait()
    first = device_first(tok)
    lengths = len_ref[...].astype(jnp.float32)
    own_bias_ref[...] = bias_by_query(lengths, first + prior, tok - prior, first, tok)
    near_bias_ref[...] = bias_by_key(lengths, first, prior, first - half, prior + half, 2)
    lead_bias_ref[...] = bias_by_query(lengths, first, prior, first - prior, 2 * prior)
    tail_bias_ref[...] = bias_by_key(lengths, first + tok, half, first + tok - prior, prior, 4)
    for copy in copies:
        copy.wait()


def own_kernel(
    prior, step, bias_ref, q_ref, k_ref, v_ref, do_ref, attn_ref, gq_ref, gk_ref, gv_ref
):
    tok, width = k_ref.shape
    late = slice(prior, tok)

    @pl.loop(0, width // step)
    def _(at):
        bias = bias_ref[...]
        columns = [
            pl.ds(pl.multiple_of(at * step + c, HEAD_DIM), HEAD_DIM)
            for c in range(0, step, HEAD_DIM)
        ]
        pairs = [
            by_query(q_ref[late, c], k_ref[:, c], do_ref[late, c], v_ref[:, c], bias)
            for c in columns
        ]
        weights, grads = full_rows(pairs)
        for c, w, g in zip(columns, weights, grads):
            attn_ref[:, c] = dot(w, v_ref[:, c], 1, 0).astype(jnp.bfloat16)
            gq_ref[:, c] = dot(g, k_ref[:, c], 1, 0).astype(jnp.bfloat16)
            gk_ref[:, c] = dot(g, q_ref[late, c], 0, 0)
            gv_ref[:, c] = dot(w, do_ref[late, c], 0, 0)


def near_kernel(
    prior, near_bias_ref, lead_bias_ref, q_ref, k_ref, v_ref, do_ref, near_ref, back_ref
):
    half = prior // 2
    far = lead_bias_ref[0:1, half - 1 : half] == 0.0
    key = lax.broadcasted_iota(jnp.int32, (prior + half, 1), 0)
    bias = jnp.where(far & (key < half), MASKED, near_bias_ref[...])
    spare = lax.broadcasted_iota(jnp.int32, (half, 1), 0) == half - 1
    early, first, second = slice(0, prior), slice(0, half), slice(half, prior)
    columns = head_columns(0, q_ref.shape[1], 2)
    queries = [side_by_side(q_ref[early, c]) for c in columns]
    cotangents = [side_by_side(do_ref[early, c]) for c in columns]
    pairs = []
    for c, q, do in zip(columns, queries, cotangents):
        k = jnp.concatenate([near_ref[first, c], k_ref[early, c]], axis=0)
        v = jnp.concatenate([near_ref[second, c], v_ref[early, c]], axis=0)
        pairs.append(by_query(k, q, v, do, bias))
    tops = [jnp.max(s, axis=0, keepdims=True) for s, _ in pairs]
    raws = [jnp.exp2(s - top) for (s, _), top in zip(pairs, tops)]
    totals = [jnp.sum(raw, axis=0, keepdims=True) for raw in raws]
    weights = [raw * (1.0 / total) for raw, total in zip(raws, totals)]
    deltas = [jnp.sum(w * dp, axis=0, keepdims=True) for w, (_, dp) in zip(weights, pairs)]
    grads = [
        w[:half] * (dp[:half] - delta) * SCALE for w, (_, dp), delta in zip(weights, pairs, deltas)
    ]
    k_terms = [dot(g.astype(jnp.bfloat16), q, 1, 0) for g, q in zip(grads, queries)]
    v_terms = [dot(w[:half].astype(jnp.bfloat16), do, 1, 0) for w, do in zip(weights, cotangents)]
    logs = fours([top + jnp.log2(total) for top, total in zip(tops, totals)])
    deltas = fours(deltas)
    for at, c in enumerate(head_columns(0, q_ref.shape[1], 4)):
        for row, terms, ref, place in (
            (logs[at], k_terms, q_ref, first), (deltas[at], v_terms, do_ref, second)
        ):
            here = jnp.where(spare, split_bf16(row), ref[first, c])
            terms = jnp.concatenate(terms[2 * at : 2 * at + 2], axis=1).astype(jnp.bfloat16)
            back_ref[place, c] = jnp.where(far, here, terms)


def lead_kernel(
    prior, step, bias_ref, q_ref, k_ref, v_ref, do_ref, near_ref, far_ref, gk_part_ref, gv_part_ref,
    attn_late_ref, gq_late_ref, attn_hbm, gq_hbm, gk_hbm, gv_hbm,
    attn_ref, gq_ref, gk_ref, gv_ref, sems, late_sems,
):
    tok, width = q_ref.shape
    half = prior // 2
    early, first, second = slice(0, prior), slice(0, half), slice(half, prior)
    late = pl.ds(prior, tok - prior)
    late_copies = [
        pltpu.make_async_copy(attn_late_ref, attn_hbm.at[late, :], late_sems.at[0]),
        pltpu.make_async_copy(gq_late_ref, gq_hbm.at[late, :], late_sems.at[1]),
    ]
    for copy in late_copies:
        copy.start()

    def copies(at):
        cols = pl.ds(pl.multiple_of(at * step, step), step)
        pairs = ((attn_ref, attn_hbm), (gq_ref, gq_hbm), (gk_ref, gk_hbm), (gv_ref, gv_hbm))
        return [
            pltpu.make_async_copy(ref.at[:, cols], hbm.at[pl.ds(0, prior), cols], sems.at[at, n])
            for n, (ref, hbm) in enumerate(pairs)
        ]

    @pl.loop(0, width // step)
    def _(at):
        bias = bias_ref[...]
        columns = [
            pl.ds(pl.multiple_of(at * step + c, HEAD_DIM), HEAD_DIM)
            for c in range(0, step, HEAD_DIM)
        ]
        keys = [
            jnp.concatenate([far_ref[first, c], near_ref[first, c], k_ref[early, c]], axis=0)
            for c in columns
        ]
        values = [
            jnp.concatenate([far_ref[second, c], near_ref[second, c], v_ref[early, c]], axis=0)
            for c in columns
        ]
        pairs = [
            by_query(q_ref[early, c], k, do_ref[early, c], v, bias)
            for c, k, v in zip(columns, keys, values)
        ]
        weights, grads = full_rows(pairs)
        for c, w, g, k, v in zip(columns, weights, grads, keys, values):
            attn_ref[:, c] = dot(w, v, 1, 0).astype(jnp.bfloat16)
            gq_ref[:, c] = dot(g, k, 1, 0).astype(jnp.bfloat16)
            gk = dot(g, q_ref[early, c], 0, 0)
            gv = dot(w, do_ref[early, c], 0, 0)
            gk_ref[:, c] = (gk_part_ref[early, c] + gk[prior:]).astype(jnp.bfloat16)
            gv_ref[:, c] = (gv_part_ref[early, c] + gv[prior:]).astype(jnp.bfloat16)
        for copy in copies(at):
            copy.start()

    for at in range(width // step):
        for copy in copies(at):
            copy.wait()
    for copy in late_copies:
        copy.wait()


def tail_kernel(
    prior, step, bias_ref, k_ref, v_ref, after_ref, gk_part_ref, gv_part_ref, gk_in, gv_in,
    gk_hbm, gv_hbm, gk_ref, gv_ref, sems,
):
    tok, width = k_ref.shape
    half = prior // 2
    far = bias_ref[half - 1 : half, 0:1] == 0.0
    bias = jnp.where(far, bias_ref[...], MASKED)
    first, second, last = slice(0, half), slice(half, prior), slice(tok - prior, tok)
    copies = []
    for low in range(0, width, step):
        columns = head_columns(low, low + step, 4)
        queries = [side_by_side(after_ref[first, c]) for c in columns]
        cotangents = [side_by_side(after_ref[second, c]) for c in columns]
        pairs = [
            by_query(k_ref[last, c], q, v_ref[last, c], do, bias)
            for c, q, do in zip(columns, queries, cotangents)
        ]
        own = [
            (joined(after_ref[half - 1 : half, c]), joined(after_ref[prior - 1 : prior, c]))
            for c in columns
        ]
        weights, grads = merged_columns(pairs, own)
        for c, w, g, q, do in zip(columns, weights, grads, queries, cotangents):
            for out_ref, part_ref, left, right, rows in (
                (gk_ref, gk_part_ref, g, q, first), (gv_ref, gv_part_ref, w, do, second)
            ):
                total = part_ref[last, c] + dot(left, right, 1, 0)
                terms = jnp.where(far, 0.0, after_ref[rows, c].astype(jnp.float32))
                out_ref[first, c] = total[first].astype(jnp.bfloat16)
                out_ref[second, c] = (total[second] + terms).astype(jnp.bfloat16)
        cols = pl.ds(low, step)
        for ref, hbm in ((gk_ref, gk_hbm), (gv_ref, gv_hbm)):
            copies.append(
                pltpu.make_async_copy(
                    ref.at[:, cols], hbm.at[pl.ds(tok - prior, prior), cols], sems.at[len(copies)]
                )
            )
            copies[-1].start()
    for copy in copies:
        copy.wait()


def neighbour(value, by):
    peers = lax.axis_size("seq") * lax.axis_size("head")
    pairs = [(i, i + by) for i in range(peers) if 0 <= i + by < peers]
    return lax.ppermute(value, ("seq", "head"), pairs)


def cost(heads, queries, keys, products, moved):
    return pl.CostEstimate(
        flops=2 * heads * queries * keys * HEAD_DIM * products,
        bytes_accessed=moved,
        transcendentals=heads * queries * keys,
    )


def halo_shards(query_in, key_in, value_in, grad_out, module_lengths):
    tok, width = query_in.shape
    prior = tok * lax.axis_size("head") // 8
    step = math.gcd(width, 8 * HEAD_DIM)
    groups = width // step
    anywhere = pl.BlockSpec(memory_space=pl.ANY)
    inside = pl.BlockSpec(memory_space=pltpu.VMEM)
    full16 = jax.ShapeDtypeStruct((tok, width), jnp.bfloat16)

    def near16(rows, columns):
        return pltpu.VMEM((rows, columns), jnp.bfloat16)

    def near32(rows, columns):
        return pltpu.VMEM((rows, columns), jnp.float32)

    def in_hbm(*values):
        return [pltpu.with_memory_space_constraint(value, pltpu.HBM) for value in values]

    def in_vmem(*values):
        return [pltpu.with_memory_space_constraint(value, pltpu.VMEM) for value in values]

    def call(kernel, name, ins, outs, shapes, scratch, work, moved, aliases=None):
        return pl.pallas_call(
            kernel,
            in_specs=ins,
            out_specs=outs,
            out_shape=shapes,
            scratch_shapes=scratch,
            input_output_aliases=aliases or {},
            cost_estimate=cost(*work, moved),
            compiler_params=pltpu.CompilerParams(vmem_limit_bytes=16 * 2**20),
            name=name,
        )

    near, far = call(
        functools.partial(pack_kernel, prior), "late_keys",
        [anywhere] * 2, [inside] * 2, [near16(prior, width)] * 2,
        [pltpu.SemaphoreType.DMA((2,))] * 2, (0, 0, 0, 0), 8 * prior * width,
    )(*in_hbm(key_in, value_in))
    near, far = neighbour(near, 1), neighbour(far, 1)

    lengths = module_lengths.reshape(1, -1)
    q, k, v, do, own_bias, near_bias, lead_bias, tail_bias = call(
        functools.partial(ready_kernel, prior), "operands",
        [anywhere] * 5, [inside] * 8,
        [near16(tok, width)] * 4
        + [near32(tok - prior, tok), near32(prior + prior // 2, 2 * prior)]
        + [near32(prior, 2 * prior), near32(prior, 2 * prior)],
        [
            pltpu.VMEM(lengths.shape, jnp.int32), pltpu.SemaphoreType.DMA((4,)),
            pltpu.SemaphoreType.DMA(()),
        ],
        (0, 0, 0, 0), 16 * tok * width,
    )(*in_hbm(lengths, query_in, key_in, value_in, grad_out))

    attn, gq, gk_part, gv_part = call(
        functools.partial(own_kernel, prior, step), "own_block",
        [inside] * 5, [inside] * 4,
        [near16(tok - prior, width)] * 2 + [near32(tok, width)] * 2, (),
        (width // HEAD_DIM, tok - prior, tok, 6), 18 * tok * width,
    )(*in_vmem(own_bias, q, k, v, do))
    near_bias, attn = lax.optimization_barrier((near_bias, attn))

    back = call(
        functools.partial(near_kernel, prior), "near_terms",
        [inside] * 7, inside, near16(prior, width), (),
        (width // HEAD_DIM, prior, prior + prior // 2, 3), 8 * tok * width,
    )(*in_vmem(near_bias, lead_bias, q, k, v, do, near))
    back = neighbour(back, -1)

    attn, gq, gk, gv = call(
        functools.partial(lead_kernel, prior, step), "lead_rows",
        [inside] * 11, [anywhere] * 4, [full16] * 4,
        [near16(prior, width)] * 4
        + [pltpu.SemaphoreType.DMA((groups, 4)), pltpu.SemaphoreType.DMA((2,))],
        (width // HEAD_DIM, prior, 2 * prior, 6), 20 * tok * width,
    )(*in_vmem(lead_bias, q, k, v, do, near, far, gk_part, gv_part, attn, gq))

    gk, gv = call(
        functools.partial(tail_kernel, prior, step), "tail_keys",
        [inside] * 6 + [anywhere] * 2, [anywhere] * 2, [full16] * 2,
        [near16(prior, width)] * 2 + [pltpu.SemaphoreType.DMA((2 * groups,))],
        (width // HEAD_DIM, prior, prior // 2, 4), 10 * tok * width, {6: 0, 7: 1},
    )(*in_vmem(tail_bias, k, v, back, gk_part, gv_part), gk, gv)
    return (attn, gq, gk, gv)


def shards(query_in, key_in, value_in, grad_out, module_lengths):
    tok = query_in.shape[0]
    prior = tok * lax.axis_size("head") // 8
    plan = halo_shards if 2 * prior == tok else gathered_shards
    return plan(query_in, key_in, value_in, grad_out, module_lengths)


def solution(mesh):
    placed = (
        P(("seq", "head"), None),
        P(("seq", "head"), None),
        P(("seq", "head"), None),
        P(("seq", "head"), None),
        P(),
    )
    return jax.shard_map(
        shards,
        mesh=mesh,
        in_specs=placed,
        out_specs=(
            P(("seq", "head"), None),
            P(("seq", "head"), None),
            P(("seq", "head"), None),
            P(("seq", "head"), None),
        ),
        check_vma=False,
    )
```

```python
import functools
import math

import jax
import jax.numpy as jnp
from jax import lax
from jax.experimental import pallas as pl
from jax.experimental.pallas import tpu as pltpu
from jax.sharding import PartitionSpec as P

HEAD_DIM = 128
SCALE = HEAD_DIM ** (-0.5)
LOG2E = math.log2(math.e)
MASKED = -1e30


def shifted(value, axis, by):
    peers = lax.axis_size(axis)
    pairs = [(i, i + by) for i in range(peers) if 0 <= i + by < peers]
    return lax.ppermute(value, axis, pairs)


def module_ids(module_lengths, positions):
    module_ends = jnp.cumsum(module_lengths)
    counted = jnp.sum((positions[:, None] >= module_ends[None, :]).astype(jnp.int32), axis=1)
    return jnp.where(positions >= 0, counted, -1)


def allowed_pairs(module_lengths, query_pos, key_pos):
    same = (
        module_ids(module_lengths, query_pos)[:, None]
        == module_ids(module_lengths, key_pos)[None, :]
    )
    return same & (key_pos[None, :] <= query_pos[:, None])


def score_grads(grad_rows, value_block, weights, row_delta, score_scale):
    dprobs = jnp.einsum("qd,kd->qk", grad_rows, value_block, preferred_element_type=jnp.float32)
    return (weights * (dprobs - row_delta[:, None]) * score_scale).astype(jnp.bfloat16)


def key_terms(dscores, weight_bf, query_rows, grad_rows):
    key_grad = jnp.einsum("qk,qd->kd", dscores, query_rows, preferred_element_type=jnp.float32)
    value_grad = jnp.einsum("qk,qd->kd", weight_bf, grad_rows, preferred_element_type=jnp.float32)
    return (key_grad, value_grad)


def one_block(query_rows, key_block, value_block, grad_rows, allowed, score_scale):
    scores = (
        jnp.einsum("qd,kd->qk", query_rows, key_block, preferred_element_type=jnp.float32)
        * score_scale
    )
    row_top = jnp.max(jnp.where(allowed, scores, -jnp.inf), axis=1, keepdims=True)
    row_total = jnp.sum(jnp.where(allowed, jnp.exp(scores - row_top), 0.0), axis=1, keepdims=True)
    log_total = row_top + jnp.log(row_total)
    weights = jnp.where(allowed, jnp.exp(scores - log_total), 0.0)
    weight_bf = weights.astype(jnp.bfloat16)
    attn_rows = jnp.einsum(
        "qk,kd->qd", weight_bf, value_block, preferred_element_type=jnp.float32
    ).astype(jnp.bfloat16)
    row_delta = jnp.sum(grad_rows.astype(jnp.float32) * attn_rows.astype(jnp.float32), axis=1)
    dscores = score_grads(grad_rows, value_block, weights, row_delta, score_scale)
    grad_q = jnp.einsum("qk,kd->qd", dscores, key_block, preferred_element_type=jnp.float32).astype(
        jnp.bfloat16
    )
    key_grad, value_grad = key_terms(dscores, weight_bf, query_rows, grad_rows)
    return (attn_rows, grad_q, key_grad, value_grad, log_total[:, 0], row_delta)


def gathered_shards(query_in, key_in, value_in, grad_out, module_lengths):
    head_q, head_k, head_v, head_do = (
        lax.all_to_all(query_in, "head", split_axis=1, concat_axis=0, tiled=True),
        lax.all_to_all(key_in, "head", split_axis=1, concat_axis=0, tiled=True),
        lax.all_to_all(value_in, "head", split_axis=1, concat_axis=0, tiled=True),
        lax.all_to_all(grad_out, "head", split_axis=1, concat_axis=0, tiled=True),
    )
    row_count = head_q.shape[0]
    width = head_q.shape[1]
    local_heads = width // HEAD_DIM
    prior_rows = row_count // 8
    score_scale = HEAD_DIM ** (-0.5)
    tail_start = row_count - prior_rows
    prior_k, prior_v = shifted((head_k[tail_start:], head_v[tail_start:]), "seq", 1)
    row_start = lax.axis_index("seq") * row_count
    query_pos = row_start + jnp.arange(row_count, dtype=jnp.int32)
    before_pos = row_start - prior_rows + jnp.arange(prior_rows, dtype=jnp.int32)
    key_pos = jnp.concatenate([before_pos, query_pos])
    block_rows = math.gcd(row_count, 512)
    block_count = row_count // block_rows
    pos_blocks = query_pos.reshape(block_count, block_rows)

    def by_head(flat, rows):
        return jnp.moveaxis(flat.reshape(rows, local_heads, HEAD_DIM), 1, 0)

    def to_flat(stacked):
        return jnp.moveaxis(stacked, 0, 1).reshape(stacked.shape[1], width)

    query_h = by_head(head_q, row_count)
    grad_h = by_head(head_do, row_count)
    key_h = by_head(jnp.concatenate([prior_k, head_k], axis=0), row_count + prior_rows)
    value_h = by_head(jnp.concatenate([prior_v, head_v], axis=0), row_count + prior_rows)

    def run_head(packed):
        query_rows, key_block, value_block, grad_rows = packed
        query_blocks = query_rows.reshape(block_count, block_rows, HEAD_DIM)
        grad_blocks = grad_rows.reshape(block_count, block_rows, HEAD_DIM)

        def run_block(inner):
            query_part, grad_part, pos_part = inner
            allowed = allowed_pairs(module_lengths, pos_part, key_pos)
            return one_block(query_part, key_block, value_block, grad_part, allowed, score_scale)

        attn_b, grad_qb, key_b, value_b, lse_b, delta_b = lax.map(
            run_block, (query_blocks, grad_blocks, pos_blocks)
        )
        return (
            attn_b.reshape(row_count, HEAD_DIM),
            grad_qb.reshape(row_count, HEAD_DIM),
            jnp.sum(key_b, axis=0),
            jnp.sum(value_b, axis=0),
            lse_b.reshape(row_count),
            delta_b.reshape(row_count),
        )

    attn_h, grad_qh, key_grad, value_grad, log_total, row_delta = lax.map(
        run_head, (query_h, key_h, value_h, grad_h)
    )
    attn_flat = to_flat(attn_h)
    attn_back = lax.all_to_all(attn_flat, "head", split_axis=0, concat_axis=1, tiled=True)
    grad_q = to_flat(grad_qh)
    later_k, later_v = shifted((key_grad[:, :prior_rows], value_grad[:, :prior_rows]), "seq", -1)
    key_total = key_grad[:, prior_rows:].at[:, tail_start:].add(later_k)
    value_total = value_grad[:, prior_rows:].at[:, tail_start:].add(later_v)
    grad_k = to_flat(key_total.astype(jnp.bfloat16))
    grad_v = to_flat(value_total.astype(jnp.bfloat16))
    back_q, back_k, back_v = (
        lax.all_to_all(grad_q, "head", split_axis=0, concat_axis=1, tiled=True),
        lax.all_to_all(grad_k, "head", split_axis=0, concat_axis=1, tiled=True),
        lax.all_to_all(grad_v, "head", split_axis=0, concat_axis=1, tiled=True),
    )
    return (attn_back, back_q, back_k, back_v)


def dot(left, right, left_dim, right_dim):
    return lax.dot_general(
        left, right, (((left_dim,), (right_dim,)), ((), ())), preferred_element_type=jnp.float32
    )


def module_ends_row(lengths_row):
    count = lengths_row.shape[1]
    row = lax.broadcasted_iota(jnp.int32, (count, count), 0)
    col = lax.broadcasted_iota(jnp.int32, (count, count), 1)
    lengths_col = jnp.sum(jnp.where(row == col, lengths_row, 0.0), axis=1, keepdims=True)
    return jnp.sum(jnp.where(row <= col, lengths_col, 0.0), axis=0, keepdims=True)


def module_ends_col(lengths_row):
    count = lengths_row.shape[1]
    row = lax.broadcasted_iota(jnp.int32, (count, count), 0)
    col = lax.broadcasted_iota(jnp.int32, (count, count), 1)
    return jnp.sum(jnp.where(col <= row, lengths_row, 0.0), axis=1, keepdims=True)


def bias_by_query(lengths_row, first_query, queries, first_key, keys):
    ends = module_ends_row(lengths_row)
    query = (first_query + lax.broadcasted_iota(jnp.int32, (queries, 1), 0)).astype(jnp.float32)
    start = jnp.max(jnp.where(ends <= query, ends, 0.0), axis=1, keepdims=True)
    key = (first_key + lax.broadcasted_iota(jnp.int32, (queries, keys), 1)).astype(jnp.float32)
    return jnp.where((key >= start) & (key <= query), 0.0, MASKED)


def bias_by_key(lengths_row, first_query, queries, first_key, keys, heads):
    ends = module_ends_col(lengths_row)
    lane = lax.broadcasted_iota(jnp.int32, (1, heads * queries), 1)
    query = (first_query + lane % queries).astype(jnp.float32)
    start = jnp.max(jnp.where(ends <= query, ends, 0.0), axis=0, keepdims=True)
    key = (first_key + lax.broadcasted_iota(jnp.int32, (keys, heads * queries), 0)).astype(
        jnp.float32
    )
    return jnp.where((key >= start) & (key <= query), 0.0, MASKED)


def by_query(q, k, do, v, bias):
    scores = dot(q, k, 1, 1) * (SCALE * LOG2E) + bias
    return scores, dot(do, v, 1, 1)


def full_rows(pairs):
    tops = [jnp.max(s, axis=1, keepdims=True) for s, _ in pairs]
    raws = [jnp.exp2(s - top) for (s, _), top in zip(pairs, tops)]
    weights = [raw * (1.0 / jnp.sum(raw, axis=1, keepdims=True)) for raw in raws]
    deltas = [jnp.sum(w * dp, axis=1, keepdims=True) for w, (_, dp) in zip(weights, pairs)]
    grads = [w * (dp - delta) * SCALE for w, (_, dp), delta in zip(weights, pairs, deltas)]
    return [w.astype(jnp.bfloat16) for w in weights], [g.astype(jnp.bfloat16) for g in grads]


def merged_columns(pairs, own):
    tops = [
        jnp.maximum(jnp.max(s, axis=0, keepdims=True), log) for (s, _), (log, _) in zip(pairs, own)
    ]
    raws = [jnp.exp2(s - top) for (s, _), top in zip(pairs, tops)]
    own_raws = [jnp.exp2(log - top) for (log, _), top in zip(own, tops)]
    parts = [
        1.0 / (jnp.sum(raw, axis=0, keepdims=True) + own_raw)
        for raw, own_raw in zip(raws, own_raws)
    ]
    weights = [raw * part for raw, part in zip(raws, parts)]
    deltas = [
        jnp.sum(w * dp, axis=0, keepdims=True) + own_raw * part * own_delta
        for w, (_, dp), own_raw, part, (_, own_delta) in zip(weights, pairs, own_raws, parts, own)
    ]
    grads = [w * (dp - delta) * SCALE for w, (_, dp), delta in zip(weights, pairs, deltas)]
    return [w.astype(jnp.bfloat16) for w in weights], [g.astype(jnp.bfloat16) for g in grads]


def side_by_side(rows):
    heads = rows.shape[1] // HEAD_DIM
    zero = jnp.zeros((rows.shape[0], HEAD_DIM), rows.dtype)
    blocks = [rows[:, c] for c in head_columns(0, rows.shape[1])]
    return jnp.concatenate(
        [
            jnp.concatenate([blocks[h] if g == h else zero for g in range(heads)], axis=1)
            for h in range(heads)
        ],
        axis=0,
    )


def head_columns(low, high, heads=1):
    wide = heads * HEAD_DIM
    return [slice(c, c + wide) for c in range(low, high, wide)]


def device_first(tok):
    place = lax.axis_index("seq") * lax.axis_size("head") + lax.axis_index("head")
    return place * tok


def fours(rows):
    table = jnp.concatenate(rows, axis=0)
    half = table.shape[1] // 4
    lane = lax.broadcasted_iota(jnp.int32, (1, table.shape[1]), 1)
    turned = [pltpu.roll(table, turn * half, 1) for turn in (3, 2, 1)]
    merged = []
    for at in range(0, len(rows), 2):
        now, after = slice(at, at + 1), slice(at + 1, at + 2)
        row = jnp.where(lane < 3 * half, turned[1][after], turned[2][after])
        row = jnp.where(lane < 2 * half, turned[0][now], row)
        merged.append(jnp.where(lane < half, table[now], row))
    return merged


def split_bf16(row):
    parts = []
    for _ in range(3):
        part = row.astype(jnp.bfloat16)
        parts.append(part)
        row = row - part.astype(jnp.float32)
    return jnp.concatenate([*parts, jnp.zeros_like(parts[0])], axis=1)


def joined(parts):
    parts = parts.astype(jnp.float32)
    count = parts.shape[1] // 4
    return parts[:, :count] + parts[:, count : 2 * count] + parts[:, 2 * count : 3 * count]


def pack_copies(prior, at, k_ref, v_ref, packed_ref, sems):
    half, tok = prior // 2, k_ref.shape[0]
    rows = pl.ds(tok - (at + 1) * half, half)
    return [
        pltpu.make_async_copy(
            ref.at[rows, :], packed_ref.at[pl.ds(n * half, half), :], sems.at[n]
        )
        for n, ref in enumerate((k_ref, v_ref))
    ]


def pack_kernel(prior, k_ref, v_ref, near_ref, sems):
    copies = pack_copies(prior, 0, k_ref, v_ref, near_ref, sems)
    for copy in copies:
        copy.start()
    for copy in copies:
        copy.wait()


def ready_kernel(
    prior, len_hbm, q_hbm, k_hbm, v_hbm, do_hbm, far_ref, q_ref, k_ref, v_ref, do_ref,
    own_bias_ref, near_bias_ref, lead_bias_ref, tail_bias_ref, len_ref, sems, far_sems, len_sem,
):
    tok, half = k_ref.shape[0], prior // 2
    pairs = ((q_hbm, q_ref), (k_hbm, k_ref), (v_hbm, v_ref), (do_hbm, do_ref))
    copies = pack_copies(prior, 1, k_hbm, v_hbm, far_ref, far_sems)
    copies += [pltpu.make_async_copy(hbm, ref, sems.at[n]) for n, (hbm, ref) in enumerate(pairs)]
    len_copy = pltpu.make_async_copy(len_hbm, len_ref, len_sem)
    len_copy.start()
    for copy in copies:
        copy.start()
    len_copy.wait()
    first = device_first(tok)
    lengths = len_ref[...].astype(jnp.float32)
    own_bias_ref[...] = bias_by_query(lengths, first + prior, tok - prior, first, tok)
    near_bias_ref[...] = bias_by_key(lengths, first, prior, first - half, prior + half, 2)
    lead_bias_ref[...] = bias_by_query(lengths, first, prior, first - prior, 2 * prior)
    tail_bias_ref[...] = bias_by_key(lengths, first + tok, half, first + tok - prior, prior, 4)
    for copy in copies:
        copy.wait()


def own_kernel(
    prior, step, bias_ref, q_ref, k_ref, v_ref, do_ref, attn_ref, gq_ref, gk_ref, gv_ref
):
    tok, width = k_ref.shape
    late = slice(prior, tok)

    @pl.loop(0, width // step)
    def _(at):
        bias = bias_ref[...]
        columns = [
            pl.ds(pl.multiple_of(at * step + c, HEAD_DIM), HEAD_DIM)
            for c in range(0, step, HEAD_DIM)
        ]
        pairs = [
            by_query(q_ref[late, c], k_ref[:, c], do_ref[late, c], v_ref[:, c], bias)
            for c in columns
        ]
        weights, grads = full_rows(pairs)
        for c, w, g in zip(columns, weights, grads):
            attn_ref[:, c] = dot(w, v_ref[:, c], 1, 0).astype(jnp.bfloat16)
            gq_ref[:, c] = dot(g, k_ref[:, c], 1, 0).astype(jnp.bfloat16)
            gk_ref[:, c] = dot(g, q_ref[late, c], 0, 0)
            gv_ref[:, c] = dot(w, do_ref[late, c], 0, 0)


def near_kernel(
    prior, near_bias_ref, lead_bias_ref, q_ref, k_ref, v_ref, do_ref, near_ref, back_ref
):
    half = prior // 2
    far = lead_bias_ref[0:1, half - 1 : half] == 0.0
    key = lax.broadcasted_iota(jnp.int32, (prior + half, 1), 0)
    bias = jnp.where(far & (key < half), MASKED, near_bias_ref[...])
    spare = lax.broadcasted_iota(jnp.int32, (half, 1), 0) == half - 1
    early, first, second = slice(0, prior), slice(0, half), slice(half, prior)
    columns = head_columns(0, q_ref.shape[1], 2)
    queries = [side_by_side(q_ref[early, c]) for c in columns]
    cotangents = [side_by_side(do_ref[early, c]) for c in columns]
    pairs = []
    for c, q, do in zip(columns, queries, cotangents):
        k = jnp.concatenate([near_ref[first, c], k_ref[early, c]], axis=0)
        v = jnp.concatenate([near_ref[second, c], v_ref[early, c]], axis=0)
        pairs.append(by_query(k, q, v, do, bias))
    tops = [jnp.max(s, axis=0, keepdims=True) for s, _ in pairs]
    raws = [jnp.exp2(s - top) for (s, _), top in zip(pairs, tops)]
    totals = [jnp.sum(raw, axis=0, keepdims=True) for raw in raws]
    weights = [raw * (1.0 / total) for raw, total in zip(raws, totals)]
    deltas = [jnp.sum(w * dp, axis=0, keepdims=True) for w, (_, dp) in zip(weights, pairs)]
    grads = [
        w[:half] * (dp[:half] - delta) * SCALE for w, (_, dp), delta in zip(weights, pairs, deltas)
    ]
    k_terms = [dot(g.astype(jnp.bfloat16), q, 1, 0) for g, q in zip(grads, queries)]
    v_terms = [dot(w[:half].astype(jnp.bfloat16), do, 1, 0) for w, do in zip(weights, cotangents)]
    logs = fours([top + jnp.log2(total) for top, total in zip(tops, totals)])
    deltas = fours(deltas)
    for at, c in enumerate(head_columns(0, q_ref.shape[1], 4)):
        for row, terms, ref, place in (
            (logs[at], k_terms, q_ref, first), (deltas[at], v_terms, do_ref, second)
        ):
            here = jnp.where(spare, split_bf16(row), ref[first, c])
            terms = jnp.concatenate(terms[2 * at : 2 * at + 2], axis=1).astype(jnp.bfloat16)
            back_ref[place, c] = jnp.where(far, here, terms)


def lead_kernel(
    prior, step, bias_ref, q_ref, k_ref, v_ref, do_ref, near_ref, far_ref, gk_part_ref, gv_part_ref,
    attn_late_ref, gq_late_ref, attn_hbm, gq_hbm, gk_hbm, gv_hbm,
    attn_ref, gq_ref, gk_ref, gv_ref, sems, late_sems,
):
    tok, width = q_ref.shape
    half = prior // 2
    early, first, second = slice(0, prior), slice(0, half), slice(half, prior)
    late = pl.ds(prior, tok - prior)
    late_copies = [
        pltpu.make_async_copy(attn_late_ref, attn_hbm.at[late, :], late_sems.at[0]),
        pltpu.make_async_copy(gq_late_ref, gq_hbm.at[late, :], late_sems.at[1]),
    ]
    for copy in late_copies:
        copy.start()

    def copies(at):
        cols = pl.ds(pl.multiple_of(at * step, step), step)
        pairs = ((attn_ref, attn_hbm), (gq_ref, gq_hbm), (gk_ref, gk_hbm), (gv_ref, gv_hbm))
        return [
            pltpu.make_async_copy(ref.at[:, cols], hbm.at[pl.ds(0, prior), cols], sems.at[at, n])
            for n, (ref, hbm) in enumerate(pairs)
        ]

    @pl.loop(0, width // step)
    def _(at):
        bias = bias_ref[...]
        columns = [
            pl.ds(pl.multiple_of(at * step + c, HEAD_DIM), HEAD_DIM)
            for c in range(0, step, HEAD_DIM)
        ]
        keys = [
            jnp.concatenate([far_ref[first, c], near_ref[first, c], k_ref[early, c]], axis=0)
            for c in columns
        ]
        values = [
            jnp.concatenate([far_ref[second, c], near_ref[second, c], v_ref[early, c]], axis=0)
            for c in columns
        ]
        pairs = [
            by_query(q_ref[early, c], k, do_ref[early, c], v, bias)
            for c, k, v in zip(columns, keys, values)
        ]
        weights, grads = full_rows(pairs)
        for c, w, g, k, v in zip(columns, weights, grads, keys, values):
            attn_ref[:, c] = dot(w, v, 1, 0).astype(jnp.bfloat16)
            gq_ref[:, c] = dot(g, k, 1, 0).astype(jnp.bfloat16)
            gk = dot(g, q_ref[early, c], 0, 0)
            gv = dot(w, do_ref[early, c], 0, 0)
            gk_ref[:, c] = (gk_part_ref[early, c] + gk[prior:]).astype(jnp.bfloat16)
            gv_ref[:, c] = (gv_part_ref[early, c] + gv[prior:]).astype(jnp.bfloat16)
        for copy in copies(at):
            copy.start()

    for at in range(width // step):
        for copy in copies(at):
            copy.wait()
    for copy in late_copies:
        copy.wait()


def tail_kernel(
    prior, bias_ref, k_ref, v_ref, after_ref, gk_part_ref, gv_part_ref, gk_in, gv_in,
    gk_hbm, gv_hbm, gk_ref, gv_ref, sems,
):
    tok, width = k_ref.shape
    half = prior // 2
    far = bias_ref[half - 1 : half, 0:1] == 0.0
    bias = jnp.where(far, bias_ref[...], MASKED)
    first, second, last = slice(0, half), slice(half, prior), slice(tok - prior, tok)
    columns = head_columns(0, width, 4)
    queries = [side_by_side(after_ref[first, c]) for c in columns]
    cotangents = [side_by_side(after_ref[second, c]) for c in columns]
    pairs = [
        by_query(k_ref[last, c], q, v_ref[last, c], do, bias)
        for c, q, do in zip(columns, queries, cotangents)
    ]
    own = [
        (joined(after_ref[half - 1 : half, c]), joined(after_ref[prior - 1 : prior, c]))
        for c in columns
    ]
    weights, grads = merged_columns(pairs, own)
    copies = []
    for at, (ref, hbm, part_ref, lefts, rights, rows) in enumerate(
        (
            (gv_ref, gv_hbm, gv_part_ref, weights, cotangents, second),
            (gk_ref, gk_hbm, gk_part_ref, grads, queries, first),
        )
    ):
        for c, left, right in zip(columns, lefts, rights):
            total = part_ref[last, c] + dot(left, right, 1, 0)
            terms = jnp.where(far, 0.0, after_ref[rows, c].astype(jnp.float32))
            ref[first, c] = total[first].astype(jnp.bfloat16)
            ref[second, c] = (total[second] + terms).astype(jnp.bfloat16)
        copies.append(
            pltpu.make_async_copy(ref, hbm.at[pl.ds(tok - prior, prior), :], sems.at[at])
        )
        copies[-1].start()
    for copy in copies:
        copy.wait()


def neighbour(value, by):
    peers = lax.axis_size("seq") * lax.axis_size("head")
    pairs = [(i, i + by) for i in range(peers) if 0 <= i + by < peers]
    return lax.ppermute(value, ("seq", "head"), pairs)


def cost(heads, queries, keys, products, moved):
    return pl.CostEstimate(
        flops=2 * heads * queries * keys * HEAD_DIM * products,
        bytes_accessed=moved,
        transcendentals=heads * queries * keys,
    )


def halo_shards(query_in, key_in, value_in, grad_out, module_lengths):
    tok, width = query_in.shape
    prior = tok * lax.axis_size("head") // 8
    step = math.gcd(width, 8 * HEAD_DIM)
    groups = width // step
    anywhere = pl.BlockSpec(memory_space=pl.ANY)
    inside = pl.BlockSpec(memory_space=pltpu.VMEM)
    full16 = jax.ShapeDtypeStruct((tok, width), jnp.bfloat16)

    def near16(rows, columns):
        return pltpu.VMEM((rows, columns), jnp.bfloat16)

    def near32(rows, columns):
        return pltpu.VMEM((rows, columns), jnp.float32)

    def in_hbm(*values):
        return [pltpu.with_memory_space_constraint(value, pltpu.HBM) for value in values]

    def in_vmem(*values):
        return [pltpu.with_memory_space_constraint(value, pltpu.VMEM) for value in values]

    def call(kernel, name, ins, outs, shapes, scratch, work, moved, aliases=None):
        return pl.pallas_call(
            kernel,
            in_specs=ins,
            out_specs=outs,
            out_shape=shapes,
            scratch_shapes=scratch,
            input_output_aliases=aliases or {},
            cost_estimate=cost(*work, moved),
            compiler_params=pltpu.CompilerParams(vmem_limit_bytes=16 * 2**20),
            name=name,
        )

    near = call(
        functools.partial(pack_kernel, prior), "near_keys",
        [anywhere] * 2, inside, near16(prior, width),
        [pltpu.SemaphoreType.DMA((2,))], (0, 0, 0, 0), 4 * prior * width,
    )(*in_hbm(key_in, value_in))
    near = neighbour(near, 1)

    lengths = module_lengths.reshape(1, -1)
    far, q, k, v, do, own_bias, near_bias, lead_bias, tail_bias = call(
        functools.partial(ready_kernel, prior), "operands",
        [anywhere] * 5, [inside] * 9,
        [near16(prior, width)] + [near16(tok, width)] * 4
        + [near32(tok - prior, tok), near32(prior + prior // 2, 2 * prior)]
        + [near32(prior, 2 * prior), near32(prior, 2 * prior)],
        [
            pltpu.VMEM(lengths.shape, jnp.int32), pltpu.SemaphoreType.DMA((4,)),
            pltpu.SemaphoreType.DMA((2,)), pltpu.SemaphoreType.DMA(()),
        ],
        (0, 0, 0, 0), 18 * tok * width,
    )(*in_hbm(lengths, query_in, key_in, value_in, grad_out))
    far = neighbour(far, 1)

    back = call(
        functools.partial(near_kernel, prior), "near_terms",
        [inside] * 7, inside, near16(prior, width), (),
        (width // HEAD_DIM, prior, prior + prior // 2, 3), 8 * tok * width,
    )(*in_vmem(near_bias, lead_bias, q, k, v, do, near))
    own_bias, back = lax.optimization_barrier((own_bias, back))
    back = neighbour(back, -1)

    attn, gq, gk_part, gv_part = call(
        functools.partial(own_kernel, prior, step), "own_block",
        [inside] * 5, [inside] * 4,
        [near16(tok - prior, width)] * 2 + [near32(tok, width)] * 2, (),
        (width // HEAD_DIM, tok - prior, tok, 6), 18 * tok * width,
    )(*in_vmem(own_bias, q, k, v, do))

    attn, gq, gk, gv = call(
        functools.partial(lead_kernel, prior, step), "lead_rows",
        [inside] * 11, [anywhere] * 4, [full16] * 4,
        [near16(prior, width)] * 4
        + [pltpu.SemaphoreType.DMA((groups, 4)), pltpu.SemaphoreType.DMA((2,))],
        (width // HEAD_DIM, prior, 2 * prior, 6), 20 * tok * width,
    )(*in_vmem(lead_bias, q, k, v, do, near, far, gk_part, gv_part, attn, gq))

    gk, gv = call(
        functools.partial(tail_kernel, prior), "tail_keys",
        [inside] * 6 + [anywhere] * 2, [anywhere] * 2, [full16] * 2,
        [near16(prior, width)] * 2 + [pltpu.SemaphoreType.DMA((2,))],
        (width // HEAD_DIM, prior, prior // 2, 4), 10 * tok * width, {6: 0, 7: 1},
    )(*in_vmem(tail_bias, k, v, back, gk_part, gv_part), gk, gv)
    return (attn, gq, gk, gv)


def shards(query_in, key_in, value_in, grad_out, module_lengths):
    tok = query_in.shape[0]
    prior = tok * lax.axis_size("head") // 8
    plan = halo_shards if 2 * prior == tok else gathered_shards
    return plan(query_in, key_in, value_in, grad_out, module_lengths)


def solution(mesh):
    placed = (
        P(("seq", "head"), None),
        P(("seq", "head"), None),
        P(("seq", "head"), None),
        P(("seq", "head"), None),
        P(),
    )
    return jax.shard_map(
        shards,
        mesh=mesh,
        in_specs=placed,
        out_specs=(
            P(("seq", "head"), None),
            P(("seq", "head"), None),
            P(("seq", "head"), None),
            P(("seq", "head"), None),
        ),
        check_vma=False,
    )
```

```python
import functools
import math

import jax
import jax.numpy as jnp
from jax import lax
from jax.experimental import pallas as pl
from jax.experimental.pallas import tpu as pltpu
from jax.sharding import PartitionSpec as P

HEAD_DIM = 128
SCALE = HEAD_DIM ** (-0.5)
LOG2E = math.log2(math.e)
MASKED = -1e30


def shifted(value, axis, by):
    peers = lax.axis_size(axis)
    pairs = [(i, i + by) for i in range(peers) if 0 <= i + by < peers]
    return lax.ppermute(value, axis, pairs)


def module_ids(module_lengths, positions):
    module_ends = jnp.cumsum(module_lengths)
    counted = jnp.sum((positions[:, None] >= module_ends[None, :]).astype(jnp.int32), axis=1)
    return jnp.where(positions >= 0, counted, -1)


def allowed_pairs(module_lengths, query_pos, key_pos):
    same = (
        module_ids(module_lengths, query_pos)[:, None]
        == module_ids(module_lengths, key_pos)[None, :]
    )
    return same & (key_pos[None, :] <= query_pos[:, None])


def score_grads(grad_rows, value_block, weights, row_delta, score_scale):
    dprobs = jnp.einsum("qd,kd->qk", grad_rows, value_block, preferred_element_type=jnp.float32)
    return (weights * (dprobs - row_delta[:, None]) * score_scale).astype(jnp.bfloat16)


def key_terms(dscores, weight_bf, query_rows, grad_rows):
    key_grad = jnp.einsum("qk,qd->kd", dscores, query_rows, preferred_element_type=jnp.float32)
    value_grad = jnp.einsum("qk,qd->kd", weight_bf, grad_rows, preferred_element_type=jnp.float32)
    return (key_grad, value_grad)


def one_block(query_rows, key_block, value_block, grad_rows, allowed, score_scale):
    scores = (
        jnp.einsum("qd,kd->qk", query_rows, key_block, preferred_element_type=jnp.float32)
        * score_scale
    )
    row_top = jnp.max(jnp.where(allowed, scores, -jnp.inf), axis=1, keepdims=True)
    row_total = jnp.sum(jnp.where(allowed, jnp.exp(scores - row_top), 0.0), axis=1, keepdims=True)
    log_total = row_top + jnp.log(row_total)
    weights = jnp.where(allowed, jnp.exp(scores - log_total), 0.0)
    weight_bf = weights.astype(jnp.bfloat16)
    attn_rows = jnp.einsum(
        "qk,kd->qd", weight_bf, value_block, preferred_element_type=jnp.float32
    ).astype(jnp.bfloat16)
    row_delta = jnp.sum(grad_rows.astype(jnp.float32) * attn_rows.astype(jnp.float32), axis=1)
    dscores = score_grads(grad_rows, value_block, weights, row_delta, score_scale)
    grad_q = jnp.einsum("qk,kd->qd", dscores, key_block, preferred_element_type=jnp.float32).astype(
        jnp.bfloat16
    )
    key_grad, value_grad = key_terms(dscores, weight_bf, query_rows, grad_rows)
    return (attn_rows, grad_q, key_grad, value_grad, log_total[:, 0], row_delta)


def gathered_shards(query_in, key_in, value_in, grad_out, module_lengths):
    head_q, head_k, head_v, head_do = (
        lax.all_to_all(query_in, "head", split_axis=1, concat_axis=0, tiled=True),
        lax.all_to_all(key_in, "head", split_axis=1, concat_axis=0, tiled=True),
        lax.all_to_all(value_in, "head", split_axis=1, concat_axis=0, tiled=True),
        lax.all_to_all(grad_out, "head", split_axis=1, concat_axis=0, tiled=True),
    )
    row_count = head_q.shape[0]
    width = head_q.shape[1]
    local_heads = width // HEAD_DIM
    prior_rows = row_count // 8
    score_scale = HEAD_DIM ** (-0.5)
    tail_start = row_count - prior_rows
    prior_k, prior_v = shifted((head_k[tail_start:], head_v[tail_start:]), "seq", 1)
    row_start = lax.axis_index("seq") * row_count
    query_pos = row_start + jnp.arange(row_count, dtype=jnp.int32)
    before_pos = row_start - prior_rows + jnp.arange(prior_rows, dtype=jnp.int32)
    key_pos = jnp.concatenate([before_pos, query_pos])
    block_rows = math.gcd(row_count, 512)
    block_count = row_count // block_rows
    pos_blocks = query_pos.reshape(block_count, block_rows)

    def by_head(flat, rows):
        return jnp.moveaxis(flat.reshape(rows, local_heads, HEAD_DIM), 1, 0)

    def to_flat(stacked):
        return jnp.moveaxis(stacked, 0, 1).reshape(stacked.shape[1], width)

    query_h = by_head(head_q, row_count)
    grad_h = by_head(head_do, row_count)
    key_h = by_head(jnp.concatenate([prior_k, head_k], axis=0), row_count + prior_rows)
    value_h = by_head(jnp.concatenate([prior_v, head_v], axis=0), row_count + prior_rows)

    def run_head(packed):
        query_rows, key_block, value_block, grad_rows = packed
        query_blocks = query_rows.reshape(block_count, block_rows, HEAD_DIM)
        grad_blocks = grad_rows.reshape(block_count, block_rows, HEAD_DIM)

        def run_block(inner):
            query_part, grad_part, pos_part = inner
            allowed = allowed_pairs(module_lengths, pos_part, key_pos)
            return one_block(query_part, key_block, value_block, grad_part, allowed, score_scale)

        attn_b, grad_qb, key_b, value_b, lse_b, delta_b = lax.map(
            run_block, (query_blocks, grad_blocks, pos_blocks)
        )
        return (
            attn_b.reshape(row_count, HEAD_DIM),
            grad_qb.reshape(row_count, HEAD_DIM),
            jnp.sum(key_b, axis=0),
            jnp.sum(value_b, axis=0),
            lse_b.reshape(row_count),
            delta_b.reshape(row_count),
        )

    attn_h, grad_qh, key_grad, value_grad, log_total, row_delta = lax.map(
        run_head, (query_h, key_h, value_h, grad_h)
    )
    attn_flat = to_flat(attn_h)
    attn_back = lax.all_to_all(attn_flat, "head", split_axis=0, concat_axis=1, tiled=True)
    grad_q = to_flat(grad_qh)
    later_k, later_v = shifted((key_grad[:, :prior_rows], value_grad[:, :prior_rows]), "seq", -1)
    key_total = key_grad[:, prior_rows:].at[:, tail_start:].add(later_k)
    value_total = value_grad[:, prior_rows:].at[:, tail_start:].add(later_v)
    grad_k = to_flat(key_total.astype(jnp.bfloat16))
    grad_v = to_flat(value_total.astype(jnp.bfloat16))
    back_q, back_k, back_v = (
        lax.all_to_all(grad_q, "head", split_axis=0, concat_axis=1, tiled=True),
        lax.all_to_all(grad_k, "head", split_axis=0, concat_axis=1, tiled=True),
        lax.all_to_all(grad_v, "head", split_axis=0, concat_axis=1, tiled=True),
    )
    return (attn_back, back_q, back_k, back_v)


def dot(left, right, left_dim, right_dim):
    return lax.dot_general(
        left, right, (((left_dim,), (right_dim,)), ((), ())), preferred_element_type=jnp.float32
    )


def module_ends_col(lengths_row):
    count = lengths_row.shape[1]
    row = lax.broadcasted_iota(jnp.int32, (count, count), 0)
    col = lax.broadcasted_iota(jnp.int32, (count, count), 1)
    return jnp.sum(jnp.where(col <= row, lengths_row, 0.0), axis=1, keepdims=True)


def bias_by_key(lengths_row, first_query, queries, first_key, keys, heads):
    ends = module_ends_col(lengths_row)
    lane = lax.broadcasted_iota(jnp.int32, (1, heads * queries), 1)
    query = (first_query + lane % queries).astype(jnp.float32)
    start = jnp.max(jnp.where(ends <= query, ends, 0.0), axis=0, keepdims=True)
    key = (first_key + lax.broadcasted_iota(jnp.int32, (keys, heads * queries), 0)).astype(
        jnp.float32
    )
    return jnp.where((key >= start) & (key <= query), 0.0, MASKED)


def score_pair(k, q, v, do, bias):
    return dot(k, q, 1, 1) * (SCALE * LOG2E) + bias, dot(v, do, 1, 1)


def softmax_columns(pairs):
    tops = [jnp.max(s, axis=0, keepdims=True) for s, _ in pairs]
    raws = [jnp.exp2(s - top) for (s, _), top in zip(pairs, tops)]
    totals = [jnp.sum(raw, axis=0, keepdims=True) for raw in raws]
    weights = [raw * (1.0 / total) for raw, total in zip(raws, totals)]
    deltas = [jnp.sum(w * dp, axis=0, keepdims=True) for w, (_, dp) in zip(weights, pairs)]
    logs = [top + jnp.log2(total) for top, total in zip(tops, totals)]
    return weights, logs, deltas


def score_grads_of(pairs, weights, deltas):
    return [
        (w * (dp - delta) * SCALE).astype(jnp.bfloat16)
        for w, (_, dp), delta in zip(weights, pairs, deltas)
    ]


def merged_columns(pairs, own):
    tops = [
        jnp.maximum(jnp.max(s, axis=0, keepdims=True), log) for (s, _), (log, _) in zip(pairs, own)
    ]
    raws = [jnp.exp2(s - top) for (s, _), top in zip(pairs, tops)]
    own_raws = [jnp.exp2(log - top) for (log, _), top in zip(own, tops)]
    parts = [
        1.0 / (jnp.sum(raw, axis=0, keepdims=True) + own_raw)
        for raw, own_raw in zip(raws, own_raws)
    ]
    weights = [raw * part for raw, part in zip(raws, parts)]
    deltas = [
        jnp.sum(w * dp, axis=0, keepdims=True) + own_raw * part * own_delta
        for w, (_, dp), own_raw, part, (_, own_delta) in zip(weights, pairs, own_raws, parts, own)
    ]
    grads = [w * (dp - delta) * SCALE for w, (_, dp), delta in zip(weights, pairs, deltas)]
    return [w.astype(jnp.bfloat16) for w in weights], [g.astype(jnp.bfloat16) for g in grads]


def side_by_side(rows):
    heads = rows.shape[1] // HEAD_DIM
    zero = jnp.zeros((rows.shape[0], HEAD_DIM), rows.dtype)
    blocks = [rows[:, c] for c in head_columns(0, rows.shape[1])]
    return jnp.concatenate(
        [
            jnp.concatenate([blocks[h] if g == h else zero for g in range(heads)], axis=1)
            for h in range(heads)
        ],
        axis=0,
    )


def head_columns(low, high, heads=1):
    wide = heads * HEAD_DIM
    return [slice(c, c + wide) for c in range(low, high, wide)]


def device_first(tok):
    place = lax.axis_index("seq") * lax.axis_size("head") + lax.axis_index("head")
    return place * tok


def fours(rows):
    table = jnp.concatenate(rows, axis=0)
    half = table.shape[1] // 4
    lane = lax.broadcasted_iota(jnp.int32, (1, table.shape[1]), 1)
    turned = [pltpu.roll(table, turn * half, 1) for turn in (3, 2, 1)]
    merged = []
    for at in range(0, len(rows), 2):
        now, after = slice(at, at + 1), slice(at + 1, at + 2)
        row = jnp.where(lane < 3 * half, turned[1][after], turned[2][after])
        row = jnp.where(lane < 2 * half, turned[0][now], row)
        merged.append(jnp.where(lane < half, table[now], row))
    return merged


def split_bf16(row):
    parts = []
    for _ in range(3):
        part = row.astype(jnp.bfloat16)
        parts.append(part)
        row = row - part.astype(jnp.float32)
    return jnp.concatenate([*parts, jnp.zeros_like(parts[0])], axis=1)


def joined(parts):
    parts = parts.astype(jnp.float32)
    count = parts.shape[1] // 4
    return parts[:, :count] + parts[:, count : 2 * count] + parts[:, 2 * count : 3 * count]


def pack_copies(prior, at, k_ref, v_ref, packed_ref, sems):
    half, tok = prior // 2, k_ref.shape[0]
    rows = pl.ds(tok - (at + 1) * half, half)
    return [
        pltpu.make_async_copy(
            ref.at[rows, :], packed_ref.at[pl.ds(n * half, half), :], sems.at[n]
        )
        for n, ref in enumerate((k_ref, v_ref))
    ]


def pack_kernel(prior, k_ref, v_ref, near_ref, sems):
    copies = pack_copies(prior, 0, k_ref, v_ref, near_ref, sems)
    for copy in copies:
        copy.start()
    for copy in copies:
        copy.wait()


def ready_kernel(
    prior, len_hbm, q_hbm, k_hbm, v_hbm, do_hbm, far_ref, q_ref, k_ref, v_ref, do_ref,
    own_bias_ref, near_bias_ref, lead_bias_ref, tail_bias_ref, len_ref, sems, far_sems, len_sem,
):
    tok, half = k_ref.shape[0], prior // 2
    pairs = ((q_hbm, q_ref), (k_hbm, k_ref), (v_hbm, v_ref), (do_hbm, do_ref))
    copies = pack_copies(prior, 1, k_hbm, v_hbm, far_ref, far_sems)
    copies += [pltpu.make_async_copy(hbm, ref, sems.at[n]) for n, (hbm, ref) in enumerate(pairs)]
    len_copy = pltpu.make_async_copy(len_hbm, len_ref, len_sem)
    len_copy.start()
    for copy in copies:
        copy.start()
    len_copy.wait()
    first = device_first(tok)
    lengths = len_ref[...].astype(jnp.float32)
    own_bias_ref[...] = bias_by_key(lengths, first + prior, tok - prior, first, tok, 2)
    near_bias_ref[...] = bias_by_key(lengths, first, prior, first - half, prior + half, 2)
    lead_bias_ref[...] = bias_by_key(lengths, first, prior, first - prior, 2 * prior, 2)
    tail_bias_ref[...] = bias_by_key(lengths, first + tok, half, first + tok - prior, prior, 4)
    for copy in copies:
        copy.wait()


def own_diagonal(both):
    rows = both.shape[0] // 2
    return jnp.concatenate([both[:rows, :HEAD_DIM], both[rows:, HEAD_DIM:]], axis=1)


def pair_columns(at, step):
    wide = 2 * HEAD_DIM
    return [pl.ds(pl.multiple_of(at * step + c, wide), wide) for c in range(0, step, wide)]


def own_kernel(
    prior, step, bias_ref, q_ref, k_ref, v_ref, do_ref, attn_ref, gq_ref, gk_ref, gv_ref
):
    tok, width = k_ref.shape
    late = slice(prior, tok)

    @pl.loop(0, width // step)
    def _(at):
        bias = bias_ref[...]
        columns = pair_columns(at, step)
        queries = [side_by_side(q_ref[late, c]) for c in columns]
        cotangents = [side_by_side(do_ref[late, c]) for c in columns]
        pairs = [
            score_pair(k_ref[:, c], q, v_ref[:, c], do, bias)
            for c, q, do in zip(columns, queries, cotangents)
        ]
        weights, _, deltas = softmax_columns(pairs)
        grads = score_grads_of(pairs, weights, deltas)
        for c, w, g, q, do in zip(columns, weights, grads, queries, cotangents):
            w = w.astype(jnp.bfloat16)
            attn_ref[:, c] = own_diagonal(dot(w, v_ref[:, c], 0, 0)).astype(jnp.bfloat16)
            gq_ref[:, c] = own_diagonal(dot(g, k_ref[:, c], 0, 0)).astype(jnp.bfloat16)
            gk_ref[:, c] = dot(g, q, 1, 0)
            gv_ref[:, c] = dot(w, do, 1, 0)


def near_kernel(
    prior, near_bias_ref, lead_bias_ref, q_ref, k_ref, v_ref, do_ref, near_ref, *back_refs
):
    width, half = q_ref.shape[1], prior // 2
    far = lead_bias_ref[half - 1 : half, 0:1] == 0.0
    key = lax.broadcasted_iota(jnp.int32, (prior + half, 1), 0)
    bias = jnp.where(far & (key < half), MASKED, near_bias_ref[...])
    spare = lax.broadcasted_iota(jnp.int32, (half, 1), 0) == half - 1
    early, first, second = slice(0, prior), slice(0, half), slice(half, prior)
    columns = head_columns(0, width, 2)
    queries = [side_by_side(q_ref[early, c]) for c in columns]
    cotangents = [side_by_side(do_ref[early, c]) for c in columns]
    pairs = []
    for c, q, do in zip(columns, queries, cotangents):
        k = jnp.concatenate([near_ref[first, c], k_ref[early, c]], axis=0)
        v = jnp.concatenate([near_ref[second, c], v_ref[early, c]], axis=0)
        pairs.append(score_pair(k, q, v, do, bias))
    weights, logs, deltas = softmax_columns(pairs)
    weights = [w[:half] for w in weights]
    grads = score_grads_of([(s[:half], dp[:half]) for s, dp in pairs], weights, deltas)
    k_terms = [dot(g, q, 1, 0) for g, q in zip(grads, queries)]
    v_terms = [dot(w.astype(jnp.bfloat16), do, 1, 0) for w, do in zip(weights, cotangents)]
    logs, deltas = fours(logs), fours(deltas)
    for at, c in enumerate(head_columns(0, width, 4)):
        back_ref = back_refs[c.start * len(back_refs) // width]
        low = c.start % back_ref.shape[1]
        here = slice(low, low + c.stop - c.start)
        for row, terms, ref, place in (
            (logs[at], k_terms, q_ref, first), (deltas[at], v_terms, do_ref, second)
        ):
            rows = jnp.where(spare, split_bf16(row), ref[first, c])
            terms = jnp.concatenate(terms[2 * at : 2 * at + 2], axis=1).astype(jnp.bfloat16)
            back_ref[place, here] = jnp.where(far, rows, terms)


def lead_kernel(
    prior, step, bias_ref, q_ref, k_ref, v_ref, do_ref, near_ref, far_ref, gk_part_ref, gv_part_ref,
    attn_late_ref, gq_late_ref, attn_hbm, gq_hbm, gk_hbm, gv_hbm,
    attn_ref, gq_ref, gk_ref, gv_ref, sems, late_sems,
):
    tok, width = q_ref.shape
    half = prior // 2
    early, first, second = slice(0, prior), slice(0, half), slice(half, prior)
    late = pl.ds(prior, tok - prior)
    late_copies = [
        pltpu.make_async_copy(attn_late_ref, attn_hbm.at[late, :], late_sems.at[0]),
        pltpu.make_async_copy(gq_late_ref, gq_hbm.at[late, :], late_sems.at[1]),
    ]
    for copy in late_copies:
        copy.start()

    def copies(at):
        cols = pl.ds(pl.multiple_of(at * step, step), step)
        pairs = ((attn_ref, attn_hbm), (gq_ref, gq_hbm), (gk_ref, gk_hbm), (gv_ref, gv_hbm))
        return [
            pltpu.make_async_copy(ref.at[:, cols], hbm.at[pl.ds(0, prior), cols], sems.at[at, n])
            for n, (ref, hbm) in enumerate(pairs)
        ]

    @pl.loop(0, width // step)
    def _(at):
        bias = bias_ref[...]
        columns = pair_columns(at, step)
        queries = [side_by_side(q_ref[early, c]) for c in columns]
        cotangents = [side_by_side(do_ref[early, c]) for c in columns]
        keys = [
            jnp.concatenate([far_ref[first, c], near_ref[first, c], k_ref[early, c]], axis=0)
            for c in columns
        ]
        values = [
            jnp.concatenate([far_ref[second, c], near_ref[second, c], v_ref[early, c]], axis=0)
            for c in columns
        ]
        pairs = [
            score_pair(k, q, v, do, bias)
            for k, q, v, do in zip(keys, queries, values, cotangents)
        ]
        weights, _, deltas = softmax_columns(pairs)
        grads = score_grads_of(pairs, weights, deltas)
        for n, c in enumerate(columns):
            w, g = weights[n].astype(jnp.bfloat16), grads[n]
            attn_ref[:, c] = own_diagonal(dot(w, values[n], 0, 0)).astype(jnp.bfloat16)
            gq_ref[:, c] = own_diagonal(dot(g, keys[n], 0, 0)).astype(jnp.bfloat16)
            gk = gk_part_ref[early, c] + dot(g[prior:], queries[n], 1, 0)
            gv = gv_part_ref[early, c] + dot(w[prior:], cotangents[n], 1, 0)
            gk_ref[:, c] = gk.astype(jnp.bfloat16)
            gv_ref[:, c] = gv.astype(jnp.bfloat16)
        for copy in copies(at):
            copy.start()

    for at in range(width // step):
        for copy in copies(at):
            copy.wait()
    for copy in late_copies:
        copy.wait()


def tail_kernel(
    prior, low, bias_ref, k_ref, v_ref, after_ref, gk_part_ref, gv_part_ref, gk_in, gv_in,
    gk_hbm, gv_hbm, gk_ref, gv_ref, sems,
):
    tok, width = k_ref.shape[0], after_ref.shape[1]
    half = prior // 2
    far = bias_ref[half - 1 : half, 0:1] == 0.0
    bias = jnp.where(far, bias_ref[...], MASKED)
    first, second, last = slice(0, half), slice(half, prior), slice(tok - prior, tok)
    places = head_columns(0, width, 4)
    columns = head_columns(low, low + width, 4)
    queries = [side_by_side(after_ref[first, p]) for p in places]
    cotangents = [side_by_side(after_ref[second, p]) for p in places]
    pairs = [
        score_pair(k_ref[last, c], q, v_ref[last, c], do, bias)
        for c, q, do in zip(columns, queries, cotangents)
    ]
    own = [
        (joined(after_ref[half - 1 : half, p]), joined(after_ref[prior - 1 : prior, p]))
        for p in places
    ]
    weights, grads = merged_columns(pairs, own)
    copies = []
    for at, (ref, hbm, part_ref, lefts, rights, rows) in enumerate(
        (
            (gv_ref, gv_hbm, gv_part_ref, weights, cotangents, second),
            (gk_ref, gk_hbm, gk_part_ref, grads, queries, first),
        )
    ):
        for p, c, left, right in zip(places, columns, lefts, rights):
            total = part_ref[last, c] + dot(left, right, 1, 0)
            terms = jnp.where(far, 0.0, after_ref[rows, p].astype(jnp.float32))
            ref[first, p] = total[first].astype(jnp.bfloat16)
            ref[second, p] = (total[second] + terms).astype(jnp.bfloat16)
        copies.append(
            pltpu.make_async_copy(
                ref, hbm.at[pl.ds(tok - prior, prior), pl.ds(low, width)], sems.at[at]
            )
        )
        copies[-1].start()
    for copy in copies:
        copy.wait()


def neighbour(value, by):
    peers = lax.axis_size("seq") * lax.axis_size("head")
    pairs = [(i, i + by) for i in range(peers) if 0 <= i + by < peers]
    return lax.ppermute(value, ("seq", "head"), pairs)


def cost(heads, queries, keys, products, moved):
    return pl.CostEstimate(
        flops=2 * heads * queries * keys * HEAD_DIM * products,
        bytes_accessed=moved,
        transcendentals=heads * queries * keys,
    )


def halo_shards(query_in, key_in, value_in, grad_out, module_lengths):
    tok, width = query_in.shape
    prior = tok * lax.axis_size("head") // 8
    step = math.gcd(width, 8 * HEAD_DIM)
    groups = width // step
    anywhere = pl.BlockSpec(memory_space=pl.ANY)
    inside = pl.BlockSpec(memory_space=pltpu.VMEM)
    full16 = jax.ShapeDtypeStruct((tok, width), jnp.bfloat16)

    def near16(rows, columns):
        return pltpu.VMEM((rows, columns), jnp.bfloat16)

    def near32(rows, columns):
        return pltpu.VMEM((rows, columns), jnp.float32)

    def in_hbm(*values):
        return [pltpu.with_memory_space_constraint(value, pltpu.HBM) for value in values]

    def in_vmem(*values):
        return [pltpu.with_memory_space_constraint(value, pltpu.VMEM) for value in values]

    def call(kernel, name, ins, outs, shapes, scratch, work, moved, aliases=None):
        return pl.pallas_call(
            kernel,
            in_specs=ins,
            out_specs=outs,
            out_shape=shapes,
            scratch_shapes=scratch,
            input_output_aliases=aliases or {},
            cost_estimate=cost(*work, moved),
            compiler_params=pltpu.CompilerParams(vmem_limit_bytes=16 * 2**20),
            name=name,
        )

    near = call(
        functools.partial(pack_kernel, prior), "near_keys",
        [anywhere] * 2, inside, near16(prior, width),
        [pltpu.SemaphoreType.DMA((2,))], (0, 0, 0, 0), 4 * prior * width,
    )(*in_hbm(key_in, value_in))
    near = neighbour(near, 1)

    lengths = module_lengths.reshape(1, -1)
    far, q, k, v, do, own_bias, near_bias, lead_bias, tail_bias = call(
        functools.partial(ready_kernel, prior), "operands",
        [anywhere] * 5, [inside] * 9,
        [near16(prior, width)] + [near16(tok, width)] * 4
        + [near32(tok, 2 * prior), near32(prior + prior // 2, 2 * prior)]
        + [near32(2 * prior, 2 * prior), near32(prior, 2 * prior)],
        [
            pltpu.VMEM(lengths.shape, jnp.int32), pltpu.SemaphoreType.DMA((4,)),
            pltpu.SemaphoreType.DMA((2,)), pltpu.SemaphoreType.DMA(()),
        ],
        (0, 0, 0, 0), 18 * tok * width,
    )(*in_hbm(lengths, query_in, key_in, value_in, grad_out))
    far = neighbour(far, 1)

    backs = call(
        functools.partial(near_kernel, prior), "near_terms",
        [inside] * 7, [inside] * groups, [near16(prior, step)] * groups, (),
        (width // HEAD_DIM, prior, prior + prior // 2, 3), 8 * tok * width,
    )(*in_vmem(near_bias, lead_bias, q, k, v, do, near))
    own_bias, *backs = lax.optimization_barrier((own_bias, *backs))
    backs = [neighbour(back, -1) for back in backs]

    attn, gq, gk_part, gv_part = call(
        functools.partial(own_kernel, prior, step), "own_block",
        [inside] * 5, [inside] * 4,
        [near16(tok - prior, width)] * 2 + [near32(tok, width)] * 2, (),
        (width // HEAD_DIM, tok - prior, tok, 6), 18 * tok * width,
    )(*in_vmem(own_bias, q, k, v, do))

    attn, gq, gk, gv = call(
        functools.partial(lead_kernel, prior, step), "lead_rows",
        [inside] * 11, [anywhere] * 4, [full16] * 4,
        [near16(prior, width)] * 4
        + [pltpu.SemaphoreType.DMA((groups, 4)), pltpu.SemaphoreType.DMA((2,))],
        (width // HEAD_DIM, prior, 2 * prior, 6), 20 * tok * width,
    )(*in_vmem(lead_bias, q, k, v, do, near, far, gk_part, gv_part, attn, gq))

    for at, back in enumerate(backs):
        gk, gv = call(
            functools.partial(tail_kernel, prior, at * step), "tail_keys",
            [inside] * 6 + [anywhere] * 2, [anywhere] * 2, [full16] * 2,
            [near16(prior, step)] * 2 + [pltpu.SemaphoreType.DMA((2,))],
            (step // HEAD_DIM, prior, prior // 2, 4), 10 * tok * step, {6: 0, 7: 1},
        )(*in_vmem(tail_bias, k, v, back, gk_part, gv_part), gk, gv)
    return (attn, gq, gk, gv)


def shards(query_in, key_in, value_in, grad_out, module_lengths):
    tok = query_in.shape[0]
    prior = tok * lax.axis_size("head") // 8
    plan = halo_shards if 2 * prior == tok else gathered_shards
    return plan(query_in, key_in, value_in, grad_out, module_lengths)


def solution(mesh):
    placed = (
        P(("seq", "head"), None),
        P(("seq", "head"), None),
        P(("seq", "head"), None),
        P(("seq", "head"), None),
        P(),
    )
    return jax.shard_map(
        shards,
        mesh=mesh,
        in_specs=placed,
        out_specs=(
            P(("seq", "head"), None),
            P(("seq", "head"), None),
            P(("seq", "head"), None),
            P(("seq", "head"), None),
        ),
        check_vma=False,
    )
```

```python
import functools
import math

import jax
import jax.numpy as jnp
from jax import lax
from jax.experimental import pallas as pl
from jax.experimental.pallas import tpu as pltpu
from jax.sharding import PartitionSpec as P

HEAD_DIM = 128
SCALE = HEAD_DIM ** (-0.5)
LOG2E = math.log2(math.e)
MASKED = -1e30


def shifted(value, axis, by):
    peers = lax.axis_size(axis)
    pairs = [(i, i + by) for i in range(peers) if 0 <= i + by < peers]
    return lax.ppermute(value, axis, pairs)


def module_ids(module_lengths, positions):
    module_ends = jnp.cumsum(module_lengths)
    counted = jnp.sum((positions[:, None] >= module_ends[None, :]).astype(jnp.int32), axis=1)
    return jnp.where(positions >= 0, counted, -1)


def allowed_pairs(module_lengths, query_pos, key_pos):
    same = (
        module_ids(module_lengths, query_pos)[:, None]
        == module_ids(module_lengths, key_pos)[None, :]
    )
    return same & (key_pos[None, :] <= query_pos[:, None])


def score_grads(grad_rows, value_block, weights, row_delta, score_scale):
    dprobs = jnp.einsum("qd,kd->qk", grad_rows, value_block, preferred_element_type=jnp.float32)
    return (weights * (dprobs - row_delta[:, None]) * score_scale).astype(jnp.bfloat16)


def key_terms(dscores, weight_bf, query_rows, grad_rows):
    key_grad = jnp.einsum("qk,qd->kd", dscores, query_rows, preferred_element_type=jnp.float32)
    value_grad = jnp.einsum("qk,qd->kd", weight_bf, grad_rows, preferred_element_type=jnp.float32)
    return (key_grad, value_grad)


def one_block(query_rows, key_block, value_block, grad_rows, allowed, score_scale):
    scores = (
        jnp.einsum("qd,kd->qk", query_rows, key_block, preferred_element_type=jnp.float32)
        * score_scale
    )
    row_top = jnp.max(jnp.where(allowed, scores, -jnp.inf), axis=1, keepdims=True)
    row_total = jnp.sum(jnp.where(allowed, jnp.exp(scores - row_top), 0.0), axis=1, keepdims=True)
    log_total = row_top + jnp.log(row_total)
    weights = jnp.where(allowed, jnp.exp(scores - log_total), 0.0)
    weight_bf = weights.astype(jnp.bfloat16)
    attn_rows = jnp.einsum(
        "qk,kd->qd", weight_bf, value_block, preferred_element_type=jnp.float32
    ).astype(jnp.bfloat16)
    row_delta = jnp.sum(grad_rows.astype(jnp.float32) * attn_rows.astype(jnp.float32), axis=1)
    dscores = score_grads(grad_rows, value_block, weights, row_delta, score_scale)
    grad_q = jnp.einsum("qk,kd->qd", dscores, key_block, preferred_element_type=jnp.float32).astype(
        jnp.bfloat16
    )
    key_grad, value_grad = key_terms(dscores, weight_bf, query_rows, grad_rows)
    return (attn_rows, grad_q, key_grad, value_grad, log_total[:, 0], row_delta)


def gathered_shards(query_in, key_in, value_in, grad_out, module_lengths):
    head_q, head_k, head_v, head_do = (
        lax.all_to_all(query_in, "head", split_axis=1, concat_axis=0, tiled=True),
        lax.all_to_all(key_in, "head", split_axis=1, concat_axis=0, tiled=True),
        lax.all_to_all(value_in, "head", split_axis=1, concat_axis=0, tiled=True),
        lax.all_to_all(grad_out, "head", split_axis=1, concat_axis=0, tiled=True),
    )
    row_count = head_q.shape[0]
    width = head_q.shape[1]
    local_heads = width // HEAD_DIM
    prior_rows = row_count // 8
    score_scale = HEAD_DIM ** (-0.5)
    tail_start = row_count - prior_rows
    prior_k, prior_v = shifted((head_k[tail_start:], head_v[tail_start:]), "seq", 1)
    row_start = lax.axis_index("seq") * row_count
    query_pos = row_start + jnp.arange(row_count, dtype=jnp.int32)
    before_pos = row_start - prior_rows + jnp.arange(prior_rows, dtype=jnp.int32)
    key_pos = jnp.concatenate([before_pos, query_pos])
    block_rows = math.gcd(row_count, 512)
    block_count = row_count // block_rows
    pos_blocks = query_pos.reshape(block_count, block_rows)

    def by_head(flat, rows):
        return jnp.moveaxis(flat.reshape(rows, local_heads, HEAD_DIM), 1, 0)

    def to_flat(stacked):
        return jnp.moveaxis(stacked, 0, 1).reshape(stacked.shape[1], width)

    query_h = by_head(head_q, row_count)
    grad_h = by_head(head_do, row_count)
    key_h = by_head(jnp.concatenate([prior_k, head_k], axis=0), row_count + prior_rows)
    value_h = by_head(jnp.concatenate([prior_v, head_v], axis=0), row_count + prior_rows)

    def run_head(packed):
        query_rows, key_block, value_block, grad_rows = packed
        query_blocks = query_rows.reshape(block_count, block_rows, HEAD_DIM)
        grad_blocks = grad_rows.reshape(block_count, block_rows, HEAD_DIM)

        def run_block(inner):
            query_part, grad_part, pos_part = inner
            allowed = allowed_pairs(module_lengths, pos_part, key_pos)
            return one_block(query_part, key_block, value_block, grad_part, allowed, score_scale)

        attn_b, grad_qb, key_b, value_b, lse_b, delta_b = lax.map(
            run_block, (query_blocks, grad_blocks, pos_blocks)
        )
        return (
            attn_b.reshape(row_count, HEAD_DIM),
            grad_qb.reshape(row_count, HEAD_DIM),
            jnp.sum(key_b, axis=0),
            jnp.sum(value_b, axis=0),
            lse_b.reshape(row_count),
            delta_b.reshape(row_count),
        )

    attn_h, grad_qh, key_grad, value_grad, log_total, row_delta = lax.map(
        run_head, (query_h, key_h, value_h, grad_h)
    )
    attn_flat = to_flat(attn_h)
    attn_back = lax.all_to_all(attn_flat, "head", split_axis=0, concat_axis=1, tiled=True)
    grad_q = to_flat(grad_qh)
    later_k, later_v = shifted((key_grad[:, :prior_rows], value_grad[:, :prior_rows]), "seq", -1)
    key_total = key_grad[:, prior_rows:].at[:, tail_start:].add(later_k)
    value_total = value_grad[:, prior_rows:].at[:, tail_start:].add(later_v)
    grad_k = to_flat(key_total.astype(jnp.bfloat16))
    grad_v = to_flat(value_total.astype(jnp.bfloat16))
    back_q, back_k, back_v = (
        lax.all_to_all(grad_q, "head", split_axis=0, concat_axis=1, tiled=True),
        lax.all_to_all(grad_k, "head", split_axis=0, concat_axis=1, tiled=True),
        lax.all_to_all(grad_v, "head", split_axis=0, concat_axis=1, tiled=True),
    )
    return (attn_back, back_q, back_k, back_v)


def dot(left, right, left_dim, right_dim):
    return lax.dot_general(
        left, right, (((left_dim,), (right_dim,)), ((), ())), preferred_element_type=jnp.float32
    )


def module_ends_col(lengths_row):
    count = lengths_row.shape[1]
    row = lax.broadcasted_iota(jnp.int32, (count, count), 0)
    col = lax.broadcasted_iota(jnp.int32, (count, count), 1)
    return jnp.sum(jnp.where(col <= row, lengths_row, 0.0), axis=1, keepdims=True)


def bias_by_key(lengths_row, first_query, queries, first_key, keys, heads):
    ends = module_ends_col(lengths_row)
    lane = lax.broadcasted_iota(jnp.int32, (1, heads * queries), 1)
    query = (first_query + lane % queries).astype(jnp.float32)
    start = jnp.max(jnp.where(ends <= query, ends, 0.0), axis=0, keepdims=True)
    key = (first_key + lax.broadcasted_iota(jnp.int32, (keys, heads * queries), 0)).astype(
        jnp.float32
    )
    return jnp.where((key >= start) & (key <= query), 0.0, MASKED)


def score_pair(k, q, v, do, bias):
    return dot(k, q, 1, 1) * (SCALE * LOG2E) + bias, dot(v, do, 1, 1)


def softmax_columns(pairs):
    tops = [jnp.max(s, axis=0, keepdims=True) for s, _ in pairs]
    raws = [jnp.exp2(s - top) for (s, _), top in zip(pairs, tops)]
    totals = [jnp.sum(raw, axis=0, keepdims=True) for raw in raws]
    weights = [raw * (1.0 / total) for raw, total in zip(raws, totals)]
    deltas = [jnp.sum(w * dp, axis=0, keepdims=True) for w, (_, dp) in zip(weights, pairs)]
    logs = [top + jnp.log2(total) for top, total in zip(tops, totals)]
    return weights, logs, deltas


def score_grads_of(pairs, weights, deltas):
    return [
        (w * (dp - delta) * SCALE).astype(jnp.bfloat16)
        for w, (_, dp), delta in zip(weights, pairs, deltas)
    ]


def merged_columns(pairs, own):
    tops = [
        jnp.maximum(jnp.max(s, axis=0, keepdims=True), log) for (s, _), (log, _) in zip(pairs, own)
    ]
    raws = [jnp.exp2(s - top) for (s, _), top in zip(pairs, tops)]
    own_raws = [jnp.exp2(log - top) for (log, _), top in zip(own, tops)]
    parts = [
        1.0 / (jnp.sum(raw, axis=0, keepdims=True) + own_raw)
        for raw, own_raw in zip(raws, own_raws)
    ]
    weights = [raw * part for raw, part in zip(raws, parts)]
    deltas = [
        jnp.sum(w * dp, axis=0, keepdims=True) + own_raw * part * own_delta
        for w, (_, dp), own_raw, part, (_, own_delta) in zip(weights, pairs, own_raws, parts, own)
    ]
    grads = [w * (dp - delta) * SCALE for w, (_, dp), delta in zip(weights, pairs, deltas)]
    return [w.astype(jnp.bfloat16) for w in weights], [g.astype(jnp.bfloat16) for g in grads]


def side_by_side(rows):
    heads = rows.shape[1] // HEAD_DIM
    zero = jnp.zeros((rows.shape[0], HEAD_DIM), rows.dtype)
    blocks = [rows[:, c] for c in head_columns(0, rows.shape[1])]
    return jnp.concatenate(
        [
            jnp.concatenate([blocks[h] if g == h else zero for g in range(heads)], axis=1)
            for h in range(heads)
        ],
        axis=0,
    )


def head_columns(low, high, heads=1):
    wide = heads * HEAD_DIM
    return [slice(c, c + wide) for c in range(low, high, wide)]


def device_first(tok):
    place = lax.axis_index("seq") * lax.axis_size("head") + lax.axis_index("head")
    return place * tok


def fours(rows):
    table = jnp.concatenate(rows, axis=0)
    half = table.shape[1] // 4
    lane = lax.broadcasted_iota(jnp.int32, (1, table.shape[1]), 1)
    turned = [pltpu.roll(table, turn * half, 1) for turn in (3, 2, 1)]
    merged = []
    for at in range(0, len(rows), 2):
        now, after = slice(at, at + 1), slice(at + 1, at + 2)
        row = jnp.where(lane < 3 * half, turned[1][after], turned[2][after])
        row = jnp.where(lane < 2 * half, turned[0][now], row)
        merged.append(jnp.where(lane < half, table[now], row))
    return merged


def split_bf16(row):
    parts = []
    for _ in range(3):
        part = row.astype(jnp.bfloat16)
        parts.append(part)
        row = row - part.astype(jnp.float32)
    return jnp.concatenate([*parts, jnp.zeros_like(parts[0])], axis=1)


def joined(parts):
    parts = parts.astype(jnp.float32)
    count = parts.shape[1] // 4
    return parts[:, :count] + parts[:, count : 2 * count] + parts[:, 2 * count : 3 * count]


def pack_copies(prior, at, k_ref, v_ref, packed_ref, sems):
    half, tok = prior // 2, k_ref.shape[0]
    rows = pl.ds(tok - (at + 1) * half, half)
    return [
        pltpu.make_async_copy(
            ref.at[rows, :], packed_ref.at[pl.ds(n * half, half), :], sems.at[n]
        )
        for n, ref in enumerate((k_ref, v_ref))
    ]


def pack_kernel(prior, k_ref, v_ref, near_ref, sems):
    copies = pack_copies(prior, 0, k_ref, v_ref, near_ref, sems)
    for copy in copies:
        copy.start()
    for copy in copies:
        copy.wait()


def ready_kernel(
    prior, len_hbm, q_hbm, k_hbm, v_hbm, do_hbm, far_ref, q_ref, k_ref, v_ref, do_ref,
    own_bias_ref, near_bias_ref, lead_bias_ref, tail_bias_ref, len_ref, sems, far_sems, len_sem,
):
    tok, half = k_ref.shape[0], prior // 2
    pairs = ((q_hbm, q_ref), (k_hbm, k_ref), (v_hbm, v_ref), (do_hbm, do_ref))
    copies = pack_copies(prior, 1, k_hbm, v_hbm, far_ref, far_sems)
    copies += [pltpu.make_async_copy(hbm, ref, sems.at[n]) for n, (hbm, ref) in enumerate(pairs)]
    len_copy = pltpu.make_async_copy(len_hbm, len_ref, len_sem)
    len_copy.start()
    for copy in copies:
        copy.start()
    len_copy.wait()
    first = device_first(tok)
    lengths = len_ref[...].astype(jnp.float32)
    own_bias_ref[...] = bias_by_key(lengths, first + prior, tok - prior, first, tok, 2)
    near_bias_ref[...] = bias_by_key(lengths, first, prior, first - half, prior + half, 2)
    lead_bias_ref[...] = bias_by_key(lengths, first, prior, first - prior, 2 * prior, 2)
    tail_bias_ref[...] = bias_by_key(lengths, first + tok, half, first + tok - prior, prior, 4)
    for copy in copies:
        copy.wait()


def own_diagonal(both):
    rows = both.shape[0] // 2
    return jnp.concatenate([both[:rows, :HEAD_DIM], both[rows:, HEAD_DIM:]], axis=1)


def pair_columns(at, step):
    wide = 2 * HEAD_DIM
    return [pl.ds(pl.multiple_of(at * step + c, wide), wide) for c in range(0, step, wide)]


def own_kernel(
    prior, step, bias_ref, q_ref, k_ref, v_ref, do_ref, attn_ref, gq_ref, gk_ref, gv_ref
):
    tok, width = k_ref.shape
    late = slice(prior, tok)

    @pl.loop(0, width // step)
    def _(at):
        bias = bias_ref[...]
        columns = pair_columns(at, step)
        queries = [side_by_side(q_ref[late, c]) for c in columns]
        cotangents = [side_by_side(do_ref[late, c]) for c in columns]
        pairs = [
            score_pair(k_ref[:, c], q, v_ref[:, c], do, bias)
            for c, q, do in zip(columns, queries, cotangents)
        ]
        weights, _, deltas = softmax_columns(pairs)
        grads = score_grads_of(pairs, weights, deltas)
        for c, w, g, q, do in zip(columns, weights, grads, queries, cotangents):
            w = w.astype(jnp.bfloat16)
            attn_ref[:, c] = own_diagonal(dot(w, v_ref[:, c], 0, 0)).astype(jnp.bfloat16)
            gq_ref[:, c] = own_diagonal(dot(g, k_ref[:, c], 0, 0)).astype(jnp.bfloat16)
            gk_ref[:, c] = dot(g, q, 1, 0)
            gv_ref[:, c] = dot(w, do, 1, 0)


def near_kernel(
    prior, near_bias_ref, lead_bias_ref, q_ref, k_ref, v_ref, do_ref, near_ref, *back_refs
):
    width, half = q_ref.shape[1], prior // 2
    far = lead_bias_ref[half - 1 : half, 0:1] == 0.0
    key = lax.broadcasted_iota(jnp.int32, (prior + half, 1), 0)
    bias = jnp.where(far & (key < half), MASKED, near_bias_ref[...])
    spare = lax.broadcasted_iota(jnp.int32, (half, 1), 0) == half - 1
    early, first, second = slice(0, prior), slice(0, half), slice(half, prior)
    columns = head_columns(0, width, 2)
    queries = [side_by_side(q_ref[early, c]) for c in columns]
    cotangents = [side_by_side(do_ref[early, c]) for c in columns]
    pairs = []
    for c, q, do in zip(columns, queries, cotangents):
        k = jnp.concatenate([near_ref[first, c], k_ref[early, c]], axis=0)
        v = jnp.concatenate([near_ref[second, c], v_ref[early, c]], axis=0)
        pairs.append(score_pair(k, q, v, do, bias))
    weights, logs, deltas = softmax_columns(pairs)
    weights = [w[:half] for w in weights]
    grads = score_grads_of([(s[:half], dp[:half]) for s, dp in pairs], weights, deltas)
    k_terms = [dot(g, q, 1, 0) for g, q in zip(grads, queries)]
    v_terms = [dot(w.astype(jnp.bfloat16), do, 1, 0) for w, do in zip(weights, cotangents)]
    logs, deltas = fours(logs), fours(deltas)
    for at, c in enumerate(head_columns(0, width, 4)):
        back_ref = back_refs[c.start * len(back_refs) // width]
        low = c.start % back_ref.shape[1]
        here = slice(low, low + c.stop - c.start)
        for row, terms, ref, place in (
            (logs[at], k_terms, q_ref, first), (deltas[at], v_terms, do_ref, second)
        ):
            rows = jnp.where(spare, split_bf16(row), ref[first, c])
            terms = jnp.concatenate(terms[2 * at : 2 * at + 2], axis=1).astype(jnp.bfloat16)
            back_ref[place, here] = jnp.where(far, rows, terms)


def lead_kernel(
    prior, step, bias_ref, q_ref, k_ref, v_ref, do_ref, near_ref, far_ref, gk_part_ref, gv_part_ref,
    attn_late_ref, gq_late_ref, attn_hbm, gq_hbm, gk_hbm, gv_hbm,
    attn_ref, gq_ref, gk_ref, gv_ref, sems, late_sems,
):
    tok, width = q_ref.shape
    half = prior // 2
    early, first, second = slice(0, prior), slice(0, half), slice(half, prior)
    late = pl.ds(prior, tok - prior)
    late_copies = [
        pltpu.make_async_copy(attn_late_ref, attn_hbm.at[late, :], late_sems.at[0]),
        pltpu.make_async_copy(gq_late_ref, gq_hbm.at[late, :], late_sems.at[1]),
    ]
    for copy in late_copies:
        copy.start()

    def copies(at):
        cols = pl.ds(pl.multiple_of(at * step, step), step)
        pairs = ((attn_ref, attn_hbm), (gq_ref, gq_hbm), (gk_ref, gk_hbm), (gv_ref, gv_hbm))
        return [
            pltpu.make_async_copy(ref.at[:, cols], hbm.at[pl.ds(0, prior), cols], sems.at[at, n])
            for n, (ref, hbm) in enumerate(pairs)
        ]

    @pl.loop(0, width // step)
    def _(at):
        bias = bias_ref[...]
        columns = pair_columns(at, step)
        queries = [side_by_side(q_ref[early, c]) for c in columns]
        cotangents = [side_by_side(do_ref[early, c]) for c in columns]
        keys = [
            jnp.concatenate([far_ref[first, c], near_ref[first, c], k_ref[early, c]], axis=0)
            for c in columns
        ]
        values = [
            jnp.concatenate([far_ref[second, c], near_ref[second, c], v_ref[early, c]], axis=0)
            for c in columns
        ]
        pairs = [
            score_pair(k, q, v, do, bias)
            for k, q, v, do in zip(keys, queries, values, cotangents)
        ]
        weights, _, deltas = softmax_columns(pairs)
        grads = score_grads_of(pairs, weights, deltas)
        for n, c in enumerate(columns):
            w, g = weights[n].astype(jnp.bfloat16), grads[n]
            attn_ref[:, c] = own_diagonal(dot(w, values[n], 0, 0)).astype(jnp.bfloat16)
            gq_ref[:, c] = own_diagonal(dot(g, keys[n], 0, 0)).astype(jnp.bfloat16)
            gk = gk_part_ref[early, c] + dot(g[prior:], queries[n], 1, 0)
            gv = gv_part_ref[early, c] + dot(w[prior:], cotangents[n], 1, 0)
            gk_ref[:, c] = gk.astype(jnp.bfloat16)
            gv_ref[:, c] = gv.astype(jnp.bfloat16)
        for copy in copies(at):
            copy.start()

    for at in range(width // step):
        for copy in copies(at):
            copy.wait()
    for copy in late_copies:
        copy.wait()


def tail_kernel(prior, bias_ref, k_ref, v_ref, gk_part_ref, gv_part_ref, *refs):
    *after_refs, _, _, gk_hbm, gv_hbm, gk_ref, gv_ref, sems = refs
    tok, width = k_ref.shape
    half = prior // 2
    far = bias_ref[half - 1 : half, 0:1] == 0.0
    bias = jnp.where(far, bias_ref[...], MASKED)
    first, second, last = slice(0, half), slice(half, prior), slice(tok - prior, tok)
    columns = head_columns(0, width, 4)
    afters = [
        (after_ref, p) for after_ref in after_refs for p in head_columns(0, after_ref.shape[1], 4)
    ]
    queries = [side_by_side(after_ref[first, p]) for after_ref, p in afters]
    cotangents = [side_by_side(after_ref[second, p]) for after_ref, p in afters]
    pairs = [
        score_pair(k_ref[last, c], q, v_ref[last, c], do, bias)
        for c, q, do in zip(columns, queries, cotangents)
    ]
    own = [
        (joined(after_ref[half - 1 : half, p]), joined(after_ref[prior - 1 : prior, p]))
        for after_ref, p in afters
    ]
    weights, grads = merged_columns(pairs, own)
    copies = []
    for at, (ref, hbm, part_ref, lefts, rights, rows) in enumerate(
        (
            (gv_ref, gv_hbm, gv_part_ref, weights, cotangents, second),
            (gk_ref, gk_hbm, gk_part_ref, grads, queries, first),
        )
    ):
        for (after_ref, p), c, left, right in zip(afters, columns, lefts, rights):
            total = part_ref[last, c] + dot(left, right, 1, 0)
            terms = jnp.where(far, 0.0, after_ref[rows, p].astype(jnp.float32))
            ref[first, c] = total[first].astype(jnp.bfloat16)
            ref[second, c] = (total[second] + terms).astype(jnp.bfloat16)
        copies.append(
            pltpu.make_async_copy(ref, hbm.at[pl.ds(tok - prior, prior), :], sems.at[at])
        )
        copies[-1].start()
    for copy in copies:
        copy.wait()


def neighbour(value, by):
    peers = lax.axis_size("seq") * lax.axis_size("head")
    pairs = [(i, i + by) for i in range(peers) if 0 <= i + by < peers]
    return lax.ppermute(value, ("seq", "head"), pairs)


def cost(heads, queries, keys, products, moved):
    return pl.CostEstimate(
        flops=2 * heads * queries * keys * HEAD_DIM * products,
        bytes_accessed=moved,
        transcendentals=heads * queries * keys,
    )


def halo_shards(query_in, key_in, value_in, grad_out, module_lengths):
    tok, width = query_in.shape
    prior = tok * lax.axis_size("head") // 8
    step = math.gcd(width, 8 * HEAD_DIM)
    groups = width // step
    anywhere = pl.BlockSpec(memory_space=pl.ANY)
    inside = pl.BlockSpec(memory_space=pltpu.VMEM)
    full16 = jax.ShapeDtypeStruct((tok, width), jnp.bfloat16)

    def near16(rows, columns):
        return pltpu.VMEM((rows, columns), jnp.bfloat16)

    def near32(rows, columns):
        return pltpu.VMEM((rows, columns), jnp.float32)

    def in_hbm(*values):
        return [pltpu.with_memory_space_constraint(value, pltpu.HBM) for value in values]

    def in_vmem(*values):
        return [pltpu.with_memory_space_constraint(value, pltpu.VMEM) for value in values]

    def call(kernel, name, ins, outs, shapes, scratch, work, moved, aliases=None):
        return pl.pallas_call(
            kernel,
            in_specs=ins,
            out_specs=outs,
            out_shape=shapes,
            scratch_shapes=scratch,
            input_output_aliases=aliases or {},
            cost_estimate=cost(*work, moved),
            compiler_params=pltpu.CompilerParams(vmem_limit_bytes=16 * 2**20),
            name=name,
        )

    near = call(
        functools.partial(pack_kernel, prior), "near_keys",
        [anywhere] * 2, inside, near16(prior, width),
        [pltpu.SemaphoreType.DMA((2,))], (0, 0, 0, 0), 4 * prior * width,
    )(*in_hbm(key_in, value_in))
    near = neighbour(near, 1)

    lengths = module_lengths.reshape(1, -1)
    far, q, k, v, do, own_bias, near_bias, lead_bias, tail_bias = call(
        functools.partial(ready_kernel, prior), "operands",
        [anywhere] * 5, [inside] * 9,
        [near16(prior, width)] + [near16(tok, width)] * 4
        + [near32(tok, 2 * prior), near32(prior + prior // 2, 2 * prior)]
        + [near32(2 * prior, 2 * prior), near32(prior, 2 * prior)],
        [
            pltpu.VMEM(lengths.shape, jnp.int32), pltpu.SemaphoreType.DMA((4,)),
            pltpu.SemaphoreType.DMA((2,)), pltpu.SemaphoreType.DMA(()),
        ],
        (0, 0, 0, 0), 18 * tok * width,
    )(*in_hbm(lengths, query_in, key_in, value_in, grad_out))
    far = neighbour(far, 1)

    attn, gq, gk_part, gv_part = call(
        functools.partial(own_kernel, prior, step), "own_block",
        [inside] * 5, [inside] * 4,
        [near16(tok - prior, width)] * 2 + [near32(tok, width)] * 2, (),
        (width // HEAD_DIM, tok - prior, tok, 6), 18 * tok * width,
    )(*in_vmem(own_bias, q, k, v, do))

    near_bias, attn = lax.optimization_barrier((near_bias, attn))
    backs = call(
        functools.partial(near_kernel, prior), "near_terms",
        [inside] * 7, [inside] * groups, [near16(prior, step)] * groups, (),
        (width // HEAD_DIM, prior, prior + prior // 2, 3), 8 * tok * width,
    )(*in_vmem(near_bias, lead_bias, q, k, v, do, near))
    backs = [neighbour(back, -1) for back in backs]

    attn, gq, gk, gv = call(
        functools.partial(lead_kernel, prior, step), "lead_rows",
        [inside] * 11, [anywhere] * 4, [full16] * 4,
        [near16(prior, width)] * 4
        + [pltpu.SemaphoreType.DMA((groups, 4)), pltpu.SemaphoreType.DMA((2,))],
        (width // HEAD_DIM, prior, 2 * prior, 6), 20 * tok * width,
    )(*in_vmem(lead_bias, q, k, v, do, near, far, gk_part, gv_part, attn, gq))

    gk, gv = call(
        functools.partial(tail_kernel, prior), "tail_keys",
        [inside] * (5 + groups) + [anywhere] * 2, [anywhere] * 2, [full16] * 2,
        [near16(prior, width)] * 2 + [pltpu.SemaphoreType.DMA((2,))],
        (width // HEAD_DIM, prior, prior // 2, 4), 10 * tok * width,
        {5 + groups: 0, 6 + groups: 1},
    )(*in_vmem(tail_bias, k, v, gk_part, gv_part, *backs), gk, gv)
    return (attn, gq, gk, gv)


def shards(query_in, key_in, value_in, grad_out, module_lengths):
    tok = query_in.shape[0]
    prior = tok * lax.axis_size("head") // 8
    plan = halo_shards if 2 * prior == tok else gathered_shards
    return plan(query_in, key_in, value_in, grad_out, module_lengths)


def solution(mesh):
    placed = (
        P(("seq", "head"), None),
        P(("seq", "head"), None),
        P(("seq", "head"), None),
        P(("seq", "head"), None),
        P(),
    )
    return jax.shard_map(
        shards,
        mesh=mesh,
        in_specs=placed,
        out_specs=(
            P(("seq", "head"), None),
            P(("seq", "head"), None),
            P(("seq", "head"), None),
            P(("seq", "head"), None),
        ),
        check_vma=False,
    )
```

```python
import functools
import math

import jax
import jax.numpy as jnp
from jax import lax
from jax.experimental import pallas as pl
from jax.experimental.pallas import tpu as pltpu
from jax.sharding import PartitionSpec as P

HEAD_DIM = 128
SCALE = HEAD_DIM ** (-0.5)
LOG2E = math.log2(math.e)
MASKED = -1e30


def shifted(value, axis, by):
    peers = lax.axis_size(axis)
    pairs = [(i, i + by) for i in range(peers) if 0 <= i + by < peers]
    return lax.ppermute(value, axis, pairs)


def module_ids(module_lengths, positions):
    module_ends = jnp.cumsum(module_lengths)
    counted = jnp.sum((positions[:, None] >= module_ends[None, :]).astype(jnp.int32), axis=1)
    return jnp.where(positions >= 0, counted, -1)


def allowed_pairs(module_lengths, query_pos, key_pos):
    same = (
        module_ids(module_lengths, query_pos)[:, None]
        == module_ids(module_lengths, key_pos)[None, :]
    )
    return same & (key_pos[None, :] <= query_pos[:, None])


def score_grads(grad_rows, value_block, weights, row_delta, score_scale):
    dprobs = jnp.einsum("qd,kd->qk", grad_rows, value_block, preferred_element_type=jnp.float32)
    return (weights * (dprobs - row_delta[:, None]) * score_scale).astype(jnp.bfloat16)


def key_terms(dscores, weight_bf, query_rows, grad_rows):
    key_grad = jnp.einsum("qk,qd->kd", dscores, query_rows, preferred_element_type=jnp.float32)
    value_grad = jnp.einsum("qk,qd->kd", weight_bf, grad_rows, preferred_element_type=jnp.float32)
    return (key_grad, value_grad)


def one_block(query_rows, key_block, value_block, grad_rows, allowed, score_scale):
    scores = (
        jnp.einsum("qd,kd->qk", query_rows, key_block, preferred_element_type=jnp.float32)
        * score_scale
    )
    row_top = jnp.max(jnp.where(allowed, scores, -jnp.inf), axis=1, keepdims=True)
    row_total = jnp.sum(jnp.where(allowed, jnp.exp(scores - row_top), 0.0), axis=1, keepdims=True)
    log_total = row_top + jnp.log(row_total)
    weights = jnp.where(allowed, jnp.exp(scores - log_total), 0.0)
    weight_bf = weights.astype(jnp.bfloat16)
    attn_rows = jnp.einsum(
        "qk,kd->qd", weight_bf, value_block, preferred_element_type=jnp.float32
    ).astype(jnp.bfloat16)
    row_delta = jnp.sum(grad_rows.astype(jnp.float32) * attn_rows.astype(jnp.float32), axis=1)
    dscores = score_grads(grad_rows, value_block, weights, row_delta, score_scale)
    grad_q = jnp.einsum("qk,kd->qd", dscores, key_block, preferred_element_type=jnp.float32).astype(
        jnp.bfloat16
    )
    key_grad, value_grad = key_terms(dscores, weight_bf, query_rows, grad_rows)
    return (attn_rows, grad_q, key_grad, value_grad, log_total[:, 0], row_delta)


def gathered_shards(query_in, key_in, value_in, grad_out, module_lengths):
    head_q, head_k, head_v, head_do = (
        lax.all_to_all(query_in, "head", split_axis=1, concat_axis=0, tiled=True),
        lax.all_to_all(key_in, "head", split_axis=1, concat_axis=0, tiled=True),
        lax.all_to_all(value_in, "head", split_axis=1, concat_axis=0, tiled=True),
        lax.all_to_all(grad_out, "head", split_axis=1, concat_axis=0, tiled=True),
    )
    row_count = head_q.shape[0]
    width = head_q.shape[1]
    local_heads = width // HEAD_DIM
    prior_rows = row_count // 8
    score_scale = HEAD_DIM ** (-0.5)
    tail_start = row_count - prior_rows
    prior_k, prior_v = shifted((head_k[tail_start:], head_v[tail_start:]), "seq", 1)
    row_start = lax.axis_index("seq") * row_count
    query_pos = row_start + jnp.arange(row_count, dtype=jnp.int32)
    before_pos = row_start - prior_rows + jnp.arange(prior_rows, dtype=jnp.int32)
    key_pos = jnp.concatenate([before_pos, query_pos])
    block_rows = math.gcd(row_count, 512)
    block_count = row_count // block_rows
    pos_blocks = query_pos.reshape(block_count, block_rows)

    def by_head(flat, rows):
        return jnp.moveaxis(flat.reshape(rows, local_heads, HEAD_DIM), 1, 0)

    def to_flat(stacked):
        return jnp.moveaxis(stacked, 0, 1).reshape(stacked.shape[1], width)

    query_h = by_head(head_q, row_count)
    grad_h = by_head(head_do, row_count)
    key_h = by_head(jnp.concatenate([prior_k, head_k], axis=0), row_count + prior_rows)
    value_h = by_head(jnp.concatenate([prior_v, head_v], axis=0), row_count + prior_rows)

    def run_head(packed):
        query_rows, key_block, value_block, grad_rows = packed
        query_blocks = query_rows.reshape(block_count, block_rows, HEAD_DIM)
        grad_blocks = grad_rows.reshape(block_count, block_rows, HEAD_DIM)

        def run_block(inner):
            query_part, grad_part, pos_part = inner
            allowed = allowed_pairs(module_lengths, pos_part, key_pos)
            return one_block(query_part, key_block, value_block, grad_part, allowed, score_scale)

        attn_b, grad_qb, key_b, value_b, lse_b, delta_b = lax.map(
            run_block, (query_blocks, grad_blocks, pos_blocks)
        )
        return (
            attn_b.reshape(row_count, HEAD_DIM),
            grad_qb.reshape(row_count, HEAD_DIM),
            jnp.sum(key_b, axis=0),
            jnp.sum(value_b, axis=0),
            lse_b.reshape(row_count),
            delta_b.reshape(row_count),
        )

    attn_h, grad_qh, key_grad, value_grad, log_total, row_delta = lax.map(
        run_head, (query_h, key_h, value_h, grad_h)
    )
    attn_flat = to_flat(attn_h)
    attn_back = lax.all_to_all(attn_flat, "head", split_axis=0, concat_axis=1, tiled=True)
    grad_q = to_flat(grad_qh)
    later_k, later_v = shifted((key_grad[:, :prior_rows], value_grad[:, :prior_rows]), "seq", -1)
    key_total = key_grad[:, prior_rows:].at[:, tail_start:].add(later_k)
    value_total = value_grad[:, prior_rows:].at[:, tail_start:].add(later_v)
    grad_k = to_flat(key_total.astype(jnp.bfloat16))
    grad_v = to_flat(value_total.astype(jnp.bfloat16))
    back_q, back_k, back_v = (
        lax.all_to_all(grad_q, "head", split_axis=0, concat_axis=1, tiled=True),
        lax.all_to_all(grad_k, "head", split_axis=0, concat_axis=1, tiled=True),
        lax.all_to_all(grad_v, "head", split_axis=0, concat_axis=1, tiled=True),
    )
    return (attn_back, back_q, back_k, back_v)


def dot(left, right, left_dim, right_dim):
    return lax.dot_general(
        left, right, (((left_dim,), (right_dim,)), ((), ())), preferred_element_type=jnp.float32
    )


def module_ends_col(lengths_row):
    count = lengths_row.shape[1]
    row = lax.broadcasted_iota(jnp.int32, (count, count), 0)
    col = lax.broadcasted_iota(jnp.int32, (count, count), 1)
    return jnp.sum(jnp.where(col <= row, lengths_row, 0.0), axis=1, keepdims=True)


def bias_by_key(lengths_row, first_query, queries, first_key, keys, heads):
    ends = module_ends_col(lengths_row)
    lane = lax.broadcasted_iota(jnp.int32, (1, heads * queries), 1)
    query = (first_query + lane % queries).astype(jnp.float32)
    start = jnp.max(jnp.where(ends <= query, ends, 0.0), axis=0, keepdims=True)
    key = (first_key + lax.broadcasted_iota(jnp.int32, (keys, heads * queries), 0)).astype(
        jnp.float32
    )
    return jnp.where((key >= start) & (key <= query), 0.0, MASKED)


def score_pair(k, q, v, do, bias):
    return dot(k, q, 1, 1) * (SCALE * LOG2E) + bias, dot(v, do, 1, 1)


def softmax_columns(pairs):
    tops = [jnp.max(s, axis=0, keepdims=True) for s, _ in pairs]
    raws = [jnp.exp2(s - top) for (s, _), top in zip(pairs, tops)]
    totals = [jnp.sum(raw, axis=0, keepdims=True) for raw in raws]
    weights = [raw * (1.0 / total) for raw, total in zip(raws, totals)]
    deltas = [jnp.sum(w * dp, axis=0, keepdims=True) for w, (_, dp) in zip(weights, pairs)]
    logs = [top + jnp.log2(total) for top, total in zip(tops, totals)]
    return weights, logs, deltas


def score_grads_of(pairs, weights, deltas):
    return [
        (w * (dp - delta) * SCALE).astype(jnp.bfloat16)
        for w, (_, dp), delta in zip(weights, pairs, deltas)
    ]


def merged_columns(pairs, own):
    tops = [
        jnp.maximum(jnp.max(s, axis=0, keepdims=True), log) for (s, _), (log, _) in zip(pairs, own)
    ]
    raws = [jnp.exp2(s - top) for (s, _), top in zip(pairs, tops)]
    own_raws = [jnp.exp2(log - top) for (log, _), top in zip(own, tops)]
    parts = [
        1.0 / (jnp.sum(raw, axis=0, keepdims=True) + own_raw)
        for raw, own_raw in zip(raws, own_raws)
    ]
    weights = [raw * part for raw, part in zip(raws, parts)]
    deltas = [
        jnp.sum(w * dp, axis=0, keepdims=True) + own_raw * part * own_delta
        for w, (_, dp), own_raw, part, (_, own_delta) in zip(weights, pairs, own_raws, parts, own)
    ]
    grads = [w * (dp - delta) * SCALE for w, (_, dp), delta in zip(weights, pairs, deltas)]
    return [w.astype(jnp.bfloat16) for w in weights], [g.astype(jnp.bfloat16) for g in grads]


def side_by_side(rows):
    heads = rows.shape[1] // HEAD_DIM
    zero = jnp.zeros((rows.shape[0], HEAD_DIM), rows.dtype)
    blocks = [rows[:, c] for c in head_columns(0, rows.shape[1])]
    return jnp.concatenate(
        [
            jnp.concatenate([blocks[h] if g == h else zero for g in range(heads)], axis=1)
            for h in range(heads)
        ],
        axis=0,
    )


def head_columns(low, high, heads=1):
    wide = heads * HEAD_DIM
    return [slice(c, c + wide) for c in range(low, high, wide)]


def device_first(tok):
    place = lax.axis_index("seq") * lax.axis_size("head") + lax.axis_index("head")
    return place * tok


def fours(rows):
    table = jnp.concatenate(rows, axis=0)
    half = table.shape[1] // 4
    lane = lax.broadcasted_iota(jnp.int32, (1, table.shape[1]), 1)
    turned = [pltpu.roll(table, turn * half, 1) for turn in (3, 2, 1)]
    merged = []
    for at in range(0, len(rows), 2):
        now, after = slice(at, at + 1), slice(at + 1, at + 2)
        row = jnp.where(lane < 3 * half, turned[1][after], turned[2][after])
        row = jnp.where(lane < 2 * half, turned[0][now], row)
        merged.append(jnp.where(lane < half, table[now], row))
    return merged


def split_bf16(row):
    parts = []
    for _ in range(3):
        part = row.astype(jnp.bfloat16)
        parts.append(part)
        row = row - part.astype(jnp.float32)
    return jnp.concatenate([*parts, jnp.zeros_like(parts[0])], axis=1)


def joined(parts):
    parts = parts.astype(jnp.float32)
    count = parts.shape[1] // 4
    return parts[:, :count] + parts[:, count : 2 * count] + parts[:, 2 * count : 3 * count]


def pack_copies(prior, at, k_ref, v_ref, packed_ref, sems):
    half, tok = prior // 2, k_ref.shape[0]
    rows = pl.ds(tok - (at + 1) * half, half)
    return [
        pltpu.make_async_copy(
            ref.at[rows, :], packed_ref.at[pl.ds(n * half, half), :], sems.at[n]
        )
        for n, ref in enumerate((k_ref, v_ref))
    ]


def pack_kernel(prior, k_ref, v_ref, near_ref, sems):
    copies = pack_copies(prior, 0, k_ref, v_ref, near_ref, sems)
    for copy in copies:
        copy.start()
    for copy in copies:
        copy.wait()


def ready_kernel(
    prior, len_hbm, q_hbm, k_hbm, v_hbm, do_hbm, far_ref, q_ref, k_ref, v_ref, do_ref,
    own_bias_ref, near_bias_ref, lead_bias_ref, tail_bias_ref, len_ref, sems, far_sems, len_sem,
):
    tok, half = k_ref.shape[0], prior // 2
    pairs = ((q_hbm, q_ref), (k_hbm, k_ref), (v_hbm, v_ref), (do_hbm, do_ref))
    copies = pack_copies(prior, 1, k_hbm, v_hbm, far_ref, far_sems)
    copies += [pltpu.make_async_copy(hbm, ref, sems.at[n]) for n, (hbm, ref) in enumerate(pairs)]
    len_copy = pltpu.make_async_copy(len_hbm, len_ref, len_sem)
    len_copy.start()
    for copy in copies:
        copy.start()
    len_copy.wait()
    first = device_first(tok)
    lengths = len_ref[...].astype(jnp.float32)
    own_bias_ref[...] = bias_by_key(lengths, first + prior, tok - prior, first, tok, 2)
    near_bias_ref[...] = bias_by_key(lengths, first, prior, first - half, prior + half, 2)
    lead_bias_ref[...] = bias_by_key(lengths, first, prior, first - prior, 2 * prior, 2)
    tail_bias_ref[...] = bias_by_key(lengths, first + tok, half, first + tok - prior, prior, 4)
    for copy in copies:
        copy.wait()


def own_diagonal(both):
    rows = both.shape[0] // 2
    return jnp.concatenate([both[:rows, :HEAD_DIM], both[rows:, HEAD_DIM:]], axis=1)


def pair_columns(at, step):
    wide = 2 * HEAD_DIM
    return [pl.ds(pl.multiple_of(at * step + c, wide), wide) for c in range(0, step, wide)]


def own_kernel(
    prior, step, bias_ref, q_ref, k_ref, v_ref, do_ref, attn_ref, gq_ref, gk_ref, gv_ref
):
    tok, width = k_ref.shape
    late = slice(prior, tok)

    @pl.loop(0, width // step)
    def _(at):
        bias = bias_ref[...]
        columns = pair_columns(at, step)
        queries = [side_by_side(q_ref[late, c]) for c in columns]
        cotangents = [side_by_side(do_ref[late, c]) for c in columns]
        pairs = [
            score_pair(k_ref[:, c], q, v_ref[:, c], do, bias)
            for c, q, do in zip(columns, queries, cotangents)
        ]
        weights, _, deltas = softmax_columns(pairs)
        grads = score_grads_of(pairs, weights, deltas)
        for c, w, g, q, do in zip(columns, weights, grads, queries, cotangents):
            w = w.astype(jnp.bfloat16)
            attn_ref[:, c] = own_diagonal(dot(w, v_ref[:, c], 0, 0)).astype(jnp.bfloat16)
            gq_ref[:, c] = own_diagonal(dot(g, k_ref[:, c], 0, 0)).astype(jnp.bfloat16)
            gk_ref[:, c] = dot(g, q, 1, 0)
            gv_ref[:, c] = dot(w, do, 1, 0)


def near_kernel(
    prior, near_bias_ref, lead_bias_ref, q_ref, k_ref, v_ref, do_ref, near_ref, *back_refs
):
    width, half = q_ref.shape[1], prior // 2
    far = lead_bias_ref[half - 1 : half, 0:1] == 0.0
    key = lax.broadcasted_iota(jnp.int32, (prior + half, 1), 0)
    bias = jnp.where(far & (key < half), MASKED, near_bias_ref[...])
    spare = lax.broadcasted_iota(jnp.int32, (half, 1), 0) == half - 1
    early, first, second = slice(0, prior), slice(0, half), slice(half, prior)
    columns = head_columns(0, width, 2)
    queries = [side_by_side(q_ref[early, c]) for c in columns]
    cotangents = [side_by_side(do_ref[early, c]) for c in columns]
    pairs = []
    for c, q, do in zip(columns, queries, cotangents):
        k = jnp.concatenate([near_ref[first, c], k_ref[early, c]], axis=0)
        v = jnp.concatenate([near_ref[second, c], v_ref[early, c]], axis=0)
        pairs.append(score_pair(k, q, v, do, bias))
    weights, logs, deltas = softmax_columns(pairs)
    weights = [w[:half] for w in weights]
    grads = score_grads_of([(s[:half], dp[:half]) for s, dp in pairs], weights, deltas)
    k_terms = [dot(g, q, 1, 0) for g, q in zip(grads, queries)]
    v_terms = [dot(w.astype(jnp.bfloat16), do, 1, 0) for w, do in zip(weights, cotangents)]
    logs, deltas = fours(logs), fours(deltas)
    places = [(ref, p) for ref in back_refs for p in head_columns(0, ref.shape[1], 4)]
    for at, (c, (back_ref, here)) in enumerate(zip(head_columns(0, width, 4), places)):
        for row, terms, ref, place in (
            (logs[at], k_terms, q_ref, first), (deltas[at], v_terms, do_ref, second)
        ):
            rows = jnp.where(spare, split_bf16(row), ref[first, c])
            terms = jnp.concatenate(terms[2 * at : 2 * at + 2], axis=1).astype(jnp.bfloat16)
            back_ref[place, here] = jnp.where(far, rows, terms)


def lead_kernel(
    prior, step, bias_ref, q_ref, k_ref, v_ref, do_ref, near_ref, far_ref, gk_part_ref, gv_part_ref,
    attn_late_ref, gq_late_ref, attn_hbm, gq_hbm, gk_hbm, gv_hbm,
    attn_ref, gq_ref, gk_ref, gv_ref, sems, late_sems,
):
    tok, width = q_ref.shape
    half = prior // 2
    early, first, second = slice(0, prior), slice(0, half), slice(half, prior)
    late = pl.ds(prior, tok - prior)
    late_copies = [
        pltpu.make_async_copy(attn_late_ref, attn_hbm.at[late, :], late_sems.at[0]),
        pltpu.make_async_copy(gq_late_ref, gq_hbm.at[late, :], late_sems.at[1]),
    ]
    for copy in late_copies:
        copy.start()

    def copies(at):
        cols = pl.ds(pl.multiple_of(at * step, step), step)
        pairs = ((attn_ref, attn_hbm), (gq_ref, gq_hbm), (gk_ref, gk_hbm), (gv_ref, gv_hbm))
        return [
            pltpu.make_async_copy(ref.at[:, cols], hbm.at[pl.ds(0, prior), cols], sems.at[at, n])
            for n, (ref, hbm) in enumerate(pairs)
        ]

    @pl.loop(0, width // step)
    def _(at):
        bias = bias_ref[...]
        columns = pair_columns(at, step)
        queries = [side_by_side(q_ref[early, c]) for c in columns]
        cotangents = [side_by_side(do_ref[early, c]) for c in columns]
        keys = [
            jnp.concatenate([far_ref[first, c], near_ref[first, c], k_ref[early, c]], axis=0)
            for c in columns
        ]
        values = [
            jnp.concatenate([far_ref[second, c], near_ref[second, c], v_ref[early, c]], axis=0)
            for c in columns
        ]
        pairs = [
            score_pair(k, q, v, do, bias)
            for k, q, v, do in zip(keys, queries, values, cotangents)
        ]
        weights, _, deltas = softmax_columns(pairs)
        grads = score_grads_of(pairs, weights, deltas)
        for n, c in enumerate(columns):
            w, g = weights[n].astype(jnp.bfloat16), grads[n]
            attn_ref[:, c] = own_diagonal(dot(w, values[n], 0, 0)).astype(jnp.bfloat16)
            gq_ref[:, c] = own_diagonal(dot(g, keys[n], 0, 0)).astype(jnp.bfloat16)
            gk = gk_part_ref[early, c] + dot(g[prior:], queries[n], 1, 0)
            gv = gv_part_ref[early, c] + dot(w[prior:], cotangents[n], 1, 0)
            gk_ref[:, c] = gk.astype(jnp.bfloat16)
            gv_ref[:, c] = gv.astype(jnp.bfloat16)
        for copy in copies(at):
            copy.start()

    for at in range(width // step):
        for copy in copies(at):
            copy.wait()
    for copy in late_copies:
        copy.wait()


def tail_kernel(prior, bias_ref, k_ref, v_ref, gk_part_ref, gv_part_ref, *refs):
    *after_refs, _, _, gk_hbm, gv_hbm, gk_ref, gv_ref, sems = refs
    tok, width = k_ref.shape
    half = prior // 2
    far = bias_ref[half - 1 : half, 0:1] == 0.0
    bias = jnp.where(far, bias_ref[...], MASKED)
    first, second, last = slice(0, half), slice(half, prior), slice(tok - prior, tok)
    columns = head_columns(0, width, 4)
    afters = [
        (after_ref, p) for after_ref in after_refs for p in head_columns(0, after_ref.shape[1], 4)
    ]
    queries = [side_by_side(after_ref[first, p]) for after_ref, p in afters]
    cotangents = [side_by_side(after_ref[second, p]) for after_ref, p in afters]
    pairs = [
        score_pair(k_ref[last, c], q, v_ref[last, c], do, bias)
        for c, q, do in zip(columns, queries, cotangents)
    ]
    own = [
        (joined(after_ref[half - 1 : half, p]), joined(after_ref[prior - 1 : prior, p]))
        for after_ref, p in afters
    ]
    weights, grads = merged_columns(pairs, own)
    copies = []
    for at, (ref, hbm, part_ref, lefts, rights, rows) in enumerate(
        (
            (gv_ref, gv_hbm, gv_part_ref, weights, cotangents, second),
            (gk_ref, gk_hbm, gk_part_ref, grads, queries, first),
        )
    ):
        for (after_ref, p), c, left, right in zip(afters, columns, lefts, rights):
            total = part_ref[last, c] + dot(left, right, 1, 0)
            terms = jnp.where(far, 0.0, after_ref[rows, p].astype(jnp.float32))
            ref[first, c] = total[first].astype(jnp.bfloat16)
            ref[second, c] = (total[second] + terms).astype(jnp.bfloat16)
        copies.append(
            pltpu.make_async_copy(ref, hbm.at[pl.ds(tok - prior, prior), :], sems.at[at])
        )
        copies[-1].start()
    for copy in copies:
        copy.wait()


def neighbour(value, by):
    peers = lax.axis_size("seq") * lax.axis_size("head")
    pairs = [(i, i + by) for i in range(peers) if 0 <= i + by < peers]
    return lax.ppermute(value, ("seq", "head"), pairs)


def cost(heads, queries, keys, products, moved):
    return pl.CostEstimate(
        flops=2 * heads * queries * keys * HEAD_DIM * products,
        bytes_accessed=moved,
        transcendentals=heads * queries * keys,
    )


def halo_shards(query_in, key_in, value_in, grad_out, module_lengths):
    tok, width = query_in.shape
    prior = tok * lax.axis_size("head") // 8
    step = math.gcd(width, 8 * HEAD_DIM)
    groups = width // step
    four = 4 * HEAD_DIM
    parts = [four, width - four]
    anywhere = pl.BlockSpec(memory_space=pl.ANY)
    inside = pl.BlockSpec(memory_space=pltpu.VMEM)
    full16 = jax.ShapeDtypeStruct((tok, width), jnp.bfloat16)

    def near16(rows, columns):
        return pltpu.VMEM((rows, columns), jnp.bfloat16)

    def near32(rows, columns):
        return pltpu.VMEM((rows, columns), jnp.float32)

    def in_hbm(*values):
        return [pltpu.with_memory_space_constraint(value, pltpu.HBM) for value in values]

    def in_vmem(*values):
        return [pltpu.with_memory_space_constraint(value, pltpu.VMEM) for value in values]

    def call(kernel, name, ins, outs, shapes, scratch, work, moved, aliases=None):
        return pl.pallas_call(
            kernel,
            in_specs=ins,
            out_specs=outs,
            out_shape=shapes,
            scratch_shapes=scratch,
            input_output_aliases=aliases or {},
            cost_estimate=cost(*work, moved),
            compiler_params=pltpu.CompilerParams(vmem_limit_bytes=16 * 2**20),
            name=name,
        )

    near = call(
        functools.partial(pack_kernel, prior), "near_keys",
        [anywhere] * 2, inside, near16(prior, width),
        [pltpu.SemaphoreType.DMA((2,))], (0, 0, 0, 0), 4 * prior * width,
    )(*in_hbm(key_in, value_in))
    near = neighbour(near, 1)

    lengths = module_lengths.reshape(1, -1)
    far, q, k, v, do, own_bias, near_bias, lead_bias, tail_bias = call(
        functools.partial(ready_kernel, prior), "operands",
        [anywhere] * 5, [inside] * 9,
        [near16(prior, width)] + [near16(tok, width)] * 4
        + [near32(tok, 2 * prior), near32(prior + prior // 2, 2 * prior)]
        + [near32(2 * prior, 2 * prior), near32(prior, 2 * prior)],
        [
            pltpu.VMEM(lengths.shape, jnp.int32), pltpu.SemaphoreType.DMA((4,)),
            pltpu.SemaphoreType.DMA((2,)), pltpu.SemaphoreType.DMA(()),
        ],
        (0, 0, 0, 0), 18 * tok * width,
    )(*in_hbm(lengths, query_in, key_in, value_in, grad_out))
    far = neighbour(far, 1)

    attn, gq, gk_part, gv_part = call(
        functools.partial(own_kernel, prior, step), "own_block",
        [inside] * 5, [inside] * 4,
        [near16(tok - prior, width)] * 2 + [near32(tok, width)] * 2, (),
        (width // HEAD_DIM, tok - prior, tok, 6), 18 * tok * width,
    )(*in_vmem(own_bias, q, k, v, do))

    near_bias, attn = lax.optimization_barrier((near_bias, attn))
    backs = call(
        functools.partial(near_kernel, prior), "near_terms",
        [inside] * 7, [inside] * len(parts), [near16(prior, wide) for wide in parts], (),
        (width // HEAD_DIM, prior, prior + prior // 2, 3), 8 * tok * width,
    )(*in_vmem(near_bias, lead_bias, q, k, v, do, near))
    backs = [neighbour(back, -1) for back in backs]

    attn, gq, gk, gv = call(
        functools.partial(lead_kernel, prior, step), "lead_rows",
        [inside] * 11, [anywhere] * 4, [full16] * 4,
        [near16(prior, width)] * 4
        + [pltpu.SemaphoreType.DMA((groups, 4)), pltpu.SemaphoreType.DMA((2,))],
        (width // HEAD_DIM, prior, 2 * prior, 6), 20 * tok * width,
    )(*in_vmem(lead_bias, q, k, v, do, near, far, gk_part, gv_part, attn, gq))

    gk, gv = call(
        functools.partial(tail_kernel, prior), "tail_keys",
        [inside] * (5 + len(parts)) + [anywhere] * 2, [anywhere] * 2, [full16] * 2,
        [near16(prior, width)] * 2 + [pltpu.SemaphoreType.DMA((2,))],
        (width // HEAD_DIM, prior, prior // 2, 4), 10 * tok * width,
        {5 + len(parts): 0, 6 + len(parts): 1},
    )(*in_vmem(tail_bias, k, v, gk_part, gv_part, *backs), gk, gv)
    return (attn, gq, gk, gv)


def shards(query_in, key_in, value_in, grad_out, module_lengths):
    tok = query_in.shape[0]
    prior = tok * lax.axis_size("head") // 8
    plan = halo_shards if 2 * prior == tok else gathered_shards
    return plan(query_in, key_in, value_in, grad_out, module_lengths)


def solution(mesh):
    placed = (
        P(("seq", "head"), None),
        P(("seq", "head"), None),
        P(("seq", "head"), None),
        P(("seq", "head"), None),
        P(),
    )
    return jax.shard_map(
        shards,
        mesh=mesh,
        in_specs=placed,
        out_specs=(
            P(("seq", "head"), None),
            P(("seq", "head"), None),
            P(("seq", "head"), None),
            P(("seq", "head"), None),
        ),
        check_vma=False,
    )
```

```python
import functools
import math

import jax
import jax.numpy as jnp
from jax import lax
from jax.experimental import pallas as pl
from jax.experimental.pallas import tpu as pltpu
from jax.sharding import PartitionSpec as P

HEAD_DIM = 128
SCALE = HEAD_DIM ** (-0.5)
LOG2E = math.log2(math.e)
MASKED = -1e30


def shifted(value, axis, by):
    peers = lax.axis_size(axis)
    pairs = [(i, i + by) for i in range(peers) if 0 <= i + by < peers]
    return lax.ppermute(value, axis, pairs)


def module_ids(module_lengths, positions):
    module_ends = jnp.cumsum(module_lengths)
    counted = jnp.sum((positions[:, None] >= module_ends[None, :]).astype(jnp.int32), axis=1)
    return jnp.where(positions >= 0, counted, -1)


def allowed_pairs(module_lengths, query_pos, key_pos):
    same = (
        module_ids(module_lengths, query_pos)[:, None]
        == module_ids(module_lengths, key_pos)[None, :]
    )
    return same & (key_pos[None, :] <= query_pos[:, None])


def score_grads(grad_rows, value_block, weights, row_delta, score_scale):
    dprobs = jnp.einsum("qd,kd->qk", grad_rows, value_block, preferred_element_type=jnp.float32)
    return (weights * (dprobs - row_delta[:, None]) * score_scale).astype(jnp.bfloat16)


def key_terms(dscores, weight_bf, query_rows, grad_rows):
    key_grad = jnp.einsum("qk,qd->kd", dscores, query_rows, preferred_element_type=jnp.float32)
    value_grad = jnp.einsum("qk,qd->kd", weight_bf, grad_rows, preferred_element_type=jnp.float32)
    return (key_grad, value_grad)


def one_block(query_rows, key_block, value_block, grad_rows, allowed, score_scale):
    scores = (
        jnp.einsum("qd,kd->qk", query_rows, key_block, preferred_element_type=jnp.float32)
        * score_scale
    )
    row_top = jnp.max(jnp.where(allowed, scores, -jnp.inf), axis=1, keepdims=True)
    row_total = jnp.sum(jnp.where(allowed, jnp.exp(scores - row_top), 0.0), axis=1, keepdims=True)
    log_total = row_top + jnp.log(row_total)
    weights = jnp.where(allowed, jnp.exp(scores - log_total), 0.0)
    weight_bf = weights.astype(jnp.bfloat16)
    attn_rows = jnp.einsum(
        "qk,kd->qd", weight_bf, value_block, preferred_element_type=jnp.float32
    ).astype(jnp.bfloat16)
    row_delta = jnp.sum(grad_rows.astype(jnp.float32) * attn_rows.astype(jnp.float32), axis=1)
    dscores = score_grads(grad_rows, value_block, weights, row_delta, score_scale)
    grad_q = jnp.einsum("qk,kd->qd", dscores, key_block, preferred_element_type=jnp.float32).astype(
        jnp.bfloat16
    )
    key_grad, value_grad = key_terms(dscores, weight_bf, query_rows, grad_rows)
    return (attn_rows, grad_q, key_grad, value_grad, log_total[:, 0], row_delta)


def gathered_shards(query_in, key_in, value_in, grad_out, module_lengths):
    head_q, head_k, head_v, head_do = (
        lax.all_to_all(query_in, "head", split_axis=1, concat_axis=0, tiled=True),
        lax.all_to_all(key_in, "head", split_axis=1, concat_axis=0, tiled=True),
        lax.all_to_all(value_in, "head", split_axis=1, concat_axis=0, tiled=True),
        lax.all_to_all(grad_out, "head", split_axis=1, concat_axis=0, tiled=True),
    )
    row_count = head_q.shape[0]
    width = head_q.shape[1]
    local_heads = width // HEAD_DIM
    prior_rows = row_count // 8
    score_scale = HEAD_DIM ** (-0.5)
    tail_start = row_count - prior_rows
    prior_k, prior_v = shifted((head_k[tail_start:], head_v[tail_start:]), "seq", 1)
    row_start = lax.axis_index("seq") * row_count
    query_pos = row_start + jnp.arange(row_count, dtype=jnp.int32)
    before_pos = row_start - prior_rows + jnp.arange(prior_rows, dtype=jnp.int32)
    key_pos = jnp.concatenate([before_pos, query_pos])
    block_rows = math.gcd(row_count, 512)
    block_count = row_count // block_rows
    pos_blocks = query_pos.reshape(block_count, block_rows)

    def by_head(flat, rows):
        return jnp.moveaxis(flat.reshape(rows, local_heads, HEAD_DIM), 1, 0)

    def to_flat(stacked):
        return jnp.moveaxis(stacked, 0, 1).reshape(stacked.shape[1], width)

    query_h = by_head(head_q, row_count)
    grad_h = by_head(head_do, row_count)
    key_h = by_head(jnp.concatenate([prior_k, head_k], axis=0), row_count + prior_rows)
    value_h = by_head(jnp.concatenate([prior_v, head_v], axis=0), row_count + prior_rows)

    def run_head(packed):
        query_rows, key_block, value_block, grad_rows = packed
        query_blocks = query_rows.reshape(block_count, block_rows, HEAD_DIM)
        grad_blocks = grad_rows.reshape(block_count, block_rows, HEAD_DIM)

        def run_block(inner):
            query_part, grad_part, pos_part = inner
            allowed = allowed_pairs(module_lengths, pos_part, key_pos)
            return one_block(query_part, key_block, value_block, grad_part, allowed, score_scale)

        attn_b, grad_qb, key_b, value_b, lse_b, delta_b = lax.map(
            run_block, (query_blocks, grad_blocks, pos_blocks)
        )
        return (
            attn_b.reshape(row_count, HEAD_DIM),
            grad_qb.reshape(row_count, HEAD_DIM),
            jnp.sum(key_b, axis=0),
            jnp.sum(value_b, axis=0),
            lse_b.reshape(row_count),
            delta_b.reshape(row_count),
        )

    attn_h, grad_qh, key_grad, value_grad, log_total, row_delta = lax.map(
        run_head, (query_h, key_h, value_h, grad_h)
    )
    attn_flat = to_flat(attn_h)
    attn_back = lax.all_to_all(attn_flat, "head", split_axis=0, concat_axis=1, tiled=True)
    grad_q = to_flat(grad_qh)
    later_k, later_v = shifted((key_grad[:, :prior_rows], value_grad[:, :prior_rows]), "seq", -1)
    key_total = key_grad[:, prior_rows:].at[:, tail_start:].add(later_k)
    value_total = value_grad[:, prior_rows:].at[:, tail_start:].add(later_v)
    grad_k = to_flat(key_total.astype(jnp.bfloat16))
    grad_v = to_flat(value_total.astype(jnp.bfloat16))
    back_q, back_k, back_v = (
        lax.all_to_all(grad_q, "head", split_axis=0, concat_axis=1, tiled=True),
        lax.all_to_all(grad_k, "head", split_axis=0, concat_axis=1, tiled=True),
        lax.all_to_all(grad_v, "head", split_axis=0, concat_axis=1, tiled=True),
    )
    return (attn_back, back_q, back_k, back_v)


def dot(left, right, left_dim, right_dim):
    return lax.dot_general(
        left, right, (((left_dim,), (right_dim,)), ((), ())), preferred_element_type=jnp.float32
    )


def module_ends_col(lengths_row):
    count = lengths_row.shape[1]
    row = lax.broadcasted_iota(jnp.int32, (count, count), 0)
    col = lax.broadcasted_iota(jnp.int32, (count, count), 1)
    return jnp.sum(jnp.where(col <= row, lengths_row, 0.0), axis=1, keepdims=True)


def bias_by_key(lengths_row, first_query, queries, first_key, keys, heads):
    ends = module_ends_col(lengths_row)
    lane = lax.broadcasted_iota(jnp.int32, (1, heads * queries), 1)
    query = (first_query + lane % queries).astype(jnp.float32)
    start = jnp.max(jnp.where(ends <= query, ends, 0.0), axis=0, keepdims=True)
    key = (first_key + lax.broadcasted_iota(jnp.int32, (keys, heads * queries), 0)).astype(
        jnp.float32
    )
    return jnp.where((key >= start) & (key <= query), 0.0, MASKED)


def score_pair(k, q, v, do, bias):
    return dot(k, q, 1, 1) * (SCALE * LOG2E) + bias, dot(v, do, 1, 1)


def softmax_columns(pairs):
    tops = [jnp.max(s, axis=0, keepdims=True) for s, _ in pairs]
    raws = [jnp.exp2(s - top) for (s, _), top in zip(pairs, tops)]
    totals = [jnp.sum(raw, axis=0, keepdims=True) for raw in raws]
    weights = [raw * (1.0 / total) for raw, total in zip(raws, totals)]
    deltas = [jnp.sum(w * dp, axis=0, keepdims=True) for w, (_, dp) in zip(weights, pairs)]
    logs = [top + jnp.log2(total) for top, total in zip(tops, totals)]
    return weights, logs, deltas


def score_grads_of(pairs, weights, deltas):
    return [
        (w * (dp - delta) * SCALE).astype(jnp.bfloat16)
        for w, (_, dp), delta in zip(weights, pairs, deltas)
    ]


def merged_columns(pairs, own):
    tops = [
        jnp.maximum(jnp.max(s, axis=0, keepdims=True), log) for (s, _), (log, _) in zip(pairs, own)
    ]
    raws = [jnp.exp2(s - top) for (s, _), top in zip(pairs, tops)]
    own_raws = [jnp.exp2(log - top) for (log, _), top in zip(own, tops)]
    parts = [
        1.0 / (jnp.sum(raw, axis=0, keepdims=True) + own_raw)
        for raw, own_raw in zip(raws, own_raws)
    ]
    weights = [raw * part for raw, part in zip(raws, parts)]
    deltas = [
        jnp.sum(w * dp, axis=0, keepdims=True) + own_raw * part * own_delta
        for w, (_, dp), own_raw, part, (_, own_delta) in zip(weights, pairs, own_raws, parts, own)
    ]
    grads = [w * (dp - delta) * SCALE for w, (_, dp), delta in zip(weights, pairs, deltas)]
    return [w.astype(jnp.bfloat16) for w in weights], [g.astype(jnp.bfloat16) for g in grads]


def side_by_side(rows):
    heads = rows.shape[1] // HEAD_DIM
    zero = jnp.zeros((rows.shape[0], HEAD_DIM), rows.dtype)
    blocks = [rows[:, c] for c in head_columns(0, rows.shape[1])]
    return jnp.concatenate(
        [
            jnp.concatenate([blocks[h] if g == h else zero for g in range(heads)], axis=1)
            for h in range(heads)
        ],
        axis=0,
    )


def head_columns(low, high, heads=1):
    wide = heads * HEAD_DIM
    return [slice(c, c + wide) for c in range(low, high, wide)]


def device_first(tok):
    place = lax.axis_index("seq") * lax.axis_size("head") + lax.axis_index("head")
    return place * tok


def fours(rows):
    table = jnp.concatenate(rows, axis=0)
    half = table.shape[1] // 4
    lane = lax.broadcasted_iota(jnp.int32, (1, table.shape[1]), 1)
    turned = [pltpu.roll(table, turn * half, 1) for turn in (3, 2, 1)]
    merged = []
    for at in range(0, len(rows), 2):
        now, after = slice(at, at + 1), slice(at + 1, at + 2)
        row = jnp.where(lane < 3 * half, turned[1][after], turned[2][after])
        row = jnp.where(lane < 2 * half, turned[0][now], row)
        merged.append(jnp.where(lane < half, table[now], row))
    return merged


def split_bf16(row):
    parts = []
    for _ in range(3):
        part = row.astype(jnp.bfloat16)
        parts.append(part)
        row = row - part.astype(jnp.float32)
    return jnp.concatenate([*parts, jnp.zeros_like(parts[0])], axis=1)


def joined(parts):
    parts = parts.astype(jnp.float32)
    count = parts.shape[1] // 4
    return parts[:, :count] + parts[:, count : 2 * count] + parts[:, 2 * count : 3 * count]


def pack_copies(prior, at, k_ref, v_ref, packed_ref, sems):
    half, tok = prior // 2, k_ref.shape[0]
    rows = pl.ds(tok - (at + 1) * half, half)
    return [
        pltpu.make_async_copy(
            ref.at[rows, :], packed_ref.at[pl.ds(n * half, half), :], sems.at[n]
        )
        for n, ref in enumerate((k_ref, v_ref))
    ]


def pack_kernel(prior, k_ref, v_ref, near_ref, far_ref, near_sems, far_sems):
    copies = pack_copies(prior, 0, k_ref, v_ref, near_ref, near_sems)
    copies += pack_copies(prior, 1, k_ref, v_ref, far_ref, far_sems)
    for copy in copies:
        copy.start()
    for copy in copies:
        copy.wait()


def ready_kernel(
    prior, len_hbm, q_hbm, k_hbm, v_hbm, do_hbm, q_ref, k_ref, v_ref, do_ref,
    own_bias_ref, near_bias_ref, lead_bias_ref, tail_bias_ref, len_ref, sems, len_sem,
):
    tok, half = k_ref.shape[0], prior // 2
    pairs = ((q_hbm, q_ref), (k_hbm, k_ref), (v_hbm, v_ref), (do_hbm, do_ref))
    copies = [pltpu.make_async_copy(hbm, ref, sems.at[n]) for n, (hbm, ref) in enumerate(pairs)]
    len_copy = pltpu.make_async_copy(len_hbm, len_ref, len_sem)
    len_copy.start()
    for copy in copies:
        copy.start()
    len_copy.wait()
    first = device_first(tok)
    lengths = len_ref[...].astype(jnp.float32)
    own_bias_ref[...] = bias_by_key(lengths, first + prior, tok - prior, first, tok, 2)
    near_bias_ref[...] = bias_by_key(lengths, first, prior, first - half, prior + half, 2)
    lead_bias_ref[...] = bias_by_key(lengths, first, prior, first - prior, 2 * prior, 2)
    tail_bias_ref[...] = bias_by_key(lengths, first + tok, half, first + tok - prior, prior, 4)
    for copy in copies:
        copy.wait()


def own_diagonal(both):
    rows = both.shape[0] // 2
    return jnp.concatenate([both[:rows, :HEAD_DIM], both[rows:, HEAD_DIM:]], axis=1)


def pair_columns(at, step):
    wide = 2 * HEAD_DIM
    return [pl.ds(pl.multiple_of(at * step + c, wide), wide) for c in range(0, step, wide)]


def own_kernel(
    prior, step, bias_ref, q_ref, k_ref, v_ref, do_ref, attn_ref, gq_ref, gk_ref, gv_ref
):
    tok, width = k_ref.shape
    late = slice(prior, tok)

    @pl.loop(0, width // step)
    def _(at):
        bias = bias_ref[...]
        columns = pair_columns(at, step)
        queries = [side_by_side(q_ref[late, c]) for c in columns]
        cotangents = [side_by_side(do_ref[late, c]) for c in columns]
        pairs = [
            score_pair(k_ref[:, c], q, v_ref[:, c], do, bias)
            for c, q, do in zip(columns, queries, cotangents)
        ]
        weights, _, deltas = softmax_columns(pairs)
        grads = score_grads_of(pairs, weights, deltas)
        for c, w, g, q, do in zip(columns, weights, grads, queries, cotangents):
            w = w.astype(jnp.bfloat16)
            attn_ref[:, c] = own_diagonal(dot(w, v_ref[:, c], 0, 0)).astype(jnp.bfloat16)
            gq_ref[:, c] = own_diagonal(dot(g, k_ref[:, c], 0, 0)).astype(jnp.bfloat16)
            gk_ref[:, c] = dot(g, q, 1, 0)
            gv_ref[:, c] = dot(w, do, 1, 0)


def near_kernel(
    prior, near_bias_ref, lead_bias_ref, q_ref, k_ref, v_ref, do_ref, near_ref, *back_refs
):
    width, half = q_ref.shape[1], prior // 2
    far = lead_bias_ref[half - 1 : half, 0:1] == 0.0
    key = lax.broadcasted_iota(jnp.int32, (prior + half, 1), 0)
    bias = jnp.where(far & (key < half), MASKED, near_bias_ref[...])
    spare = lax.broadcasted_iota(jnp.int32, (half, 1), 0) == half - 1
    early, first, second = slice(0, prior), slice(0, half), slice(half, prior)
    columns = head_columns(0, width, 2)
    queries = [side_by_side(q_ref[early, c]) for c in columns]
    cotangents = [side_by_side(do_ref[early, c]) for c in columns]
    pairs = []
    for c, q, do in zip(columns, queries, cotangents):
        k = jnp.concatenate([near_ref[first, c], k_ref[early, c]], axis=0)
        v = jnp.concatenate([near_ref[second, c], v_ref[early, c]], axis=0)
        pairs.append(score_pair(k, q, v, do, bias))
    weights, logs, deltas = softmax_columns(pairs)
    weights = [w[:half] for w in weights]
    grads = score_grads_of([(s[:half], dp[:half]) for s, dp in pairs], weights, deltas)
    k_terms = [dot(g, q, 1, 0) for g, q in zip(grads, queries)]
    v_terms = [dot(w.astype(jnp.bfloat16), do, 1, 0) for w, do in zip(weights, cotangents)]
    logs, deltas = fours(logs), fours(deltas)
    for at, c in enumerate(head_columns(0, width, 4)):
        back_ref = back_refs[c.start * len(back_refs) // width]
        low = c.start % back_ref.shape[1]
        here = slice(low, low + c.stop - c.start)
        for row, terms, ref, place in (
            (logs[at], k_terms, q_ref, first), (deltas[at], v_terms, do_ref, second)
        ):
            rows = jnp.where(spare, split_bf16(row), ref[first, c])
            terms = jnp.concatenate(terms[2 * at : 2 * at + 2], axis=1).astype(jnp.bfloat16)
            back_ref[place, here] = jnp.where(far, rows, terms)


def lead_kernel(
    prior, step, bias_ref, q_ref, k_ref, v_ref, do_ref, near_ref, far_ref, gk_part_ref, gv_part_ref,
    attn_late_ref, gq_late_ref, attn_hbm, gq_hbm, gk_hbm, gv_hbm,
    attn_ref, gq_ref, gk_ref, gv_ref, sems, late_sems,
):
    tok, width = q_ref.shape
    half = prior // 2
    early, first, second = slice(0, prior), slice(0, half), slice(half, prior)
    late = pl.ds(prior, tok - prior)
    late_copies = [
        pltpu.make_async_copy(attn_late_ref, attn_hbm.at[late, :], late_sems.at[0]),
        pltpu.make_async_copy(gq_late_ref, gq_hbm.at[late, :], late_sems.at[1]),
    ]
    for copy in late_copies:
        copy.start()

    def copies(at):
        cols = pl.ds(pl.multiple_of(at * step, step), step)
        pairs = ((attn_ref, attn_hbm), (gq_ref, gq_hbm), (gk_ref, gk_hbm), (gv_ref, gv_hbm))
        return [
            pltpu.make_async_copy(ref.at[:, cols], hbm.at[pl.ds(0, prior), cols], sems.at[at, n])
            for n, (ref, hbm) in enumerate(pairs)
        ]

    @pl.loop(0, width // step)
    def _(at):
        bias = bias_ref[...]
        columns = pair_columns(at, step)
        queries = [side_by_side(q_ref[early, c]) for c in columns]
        cotangents = [side_by_side(do_ref[early, c]) for c in columns]
        keys = [
            jnp.concatenate([far_ref[first, c], near_ref[first, c], k_ref[early, c]], axis=0)
            for c in columns
        ]
        values = [
            jnp.concatenate([far_ref[second, c], near_ref[second, c], v_ref[early, c]], axis=0)
            for c in columns
        ]
        pairs = [
            score_pair(k, q, v, do, bias)
            for k, q, v, do in zip(keys, queries, values, cotangents)
        ]
        weights, _, deltas = softmax_columns(pairs)
        grads = score_grads_of(pairs, weights, deltas)
        for n, c in enumerate(columns):
            w, g = weights[n].astype(jnp.bfloat16), grads[n]
            attn_ref[:, c] = own_diagonal(dot(w, values[n], 0, 0)).astype(jnp.bfloat16)
            gq_ref[:, c] = own_diagonal(dot(g, keys[n], 0, 0)).astype(jnp.bfloat16)
            gk = gk_part_ref[early, c] + dot(g[prior:], queries[n], 1, 0)
            gv = gv_part_ref[early, c] + dot(w[prior:], cotangents[n], 1, 0)
            gk_ref[:, c] = gk.astype(jnp.bfloat16)
            gv_ref[:, c] = gv.astype(jnp.bfloat16)
        for copy in copies(at):
            copy.start()

    for at in range(width // step):
        for copy in copies(at):
            copy.wait()
    for copy in late_copies:
        copy.wait()


def tail_kernel(prior, bias_ref, k_ref, v_ref, gk_part_ref, gv_part_ref, *refs):
    *after_refs, _, _, gk_hbm, gv_hbm, gk_ref, gv_ref, sems = refs
    tok, width = k_ref.shape
    half = prior // 2
    far = bias_ref[half - 1 : half, 0:1] == 0.0
    bias = jnp.where(far, bias_ref[...], MASKED)
    first, second, last = slice(0, half), slice(half, prior), slice(tok - prior, tok)
    columns = head_columns(0, width, 4)
    afters = [
        (after_ref, p) for after_ref in after_refs for p in head_columns(0, after_ref.shape[1], 4)
    ]
    queries = [side_by_side(after_ref[first, p]) for after_ref, p in afters]
    cotangents = [side_by_side(after_ref[second, p]) for after_ref, p in afters]
    pairs = [
        score_pair(k_ref[last, c], q, v_ref[last, c], do, bias)
        for c, q, do in zip(columns, queries, cotangents)
    ]
    own = [
        (joined(after_ref[half - 1 : half, p]), joined(after_ref[prior - 1 : prior, p]))
        for after_ref, p in afters
    ]
    weights, grads = merged_columns(pairs, own)
    copies = []
    for at, (ref, hbm, part_ref, lefts, rights, rows) in enumerate(
        (
            (gv_ref, gv_hbm, gv_part_ref, weights, cotangents, second),
            (gk_ref, gk_hbm, gk_part_ref, grads, queries, first),
        )
    ):
        for (after_ref, p), c, left, right in zip(afters, columns, lefts, rights):
            total = part_ref[last, c] + dot(left, right, 1, 0)
            terms = jnp.where(far, 0.0, after_ref[rows, p].astype(jnp.float32))
            ref[first, c] = total[first].astype(jnp.bfloat16)
            ref[second, c] = (total[second] + terms).astype(jnp.bfloat16)
        copies.append(
            pltpu.make_async_copy(ref, hbm.at[pl.ds(tok - prior, prior), :], sems.at[at])
        )
        copies[-1].start()
    for copy in copies:
        copy.wait()


def neighbour(value, by):
    peers = lax.axis_size("seq") * lax.axis_size("head")
    pairs = [(i, i + by) for i in range(peers) if 0 <= i + by < peers]
    return lax.ppermute(value, ("seq", "head"), pairs)


def cost(heads, queries, keys, products, moved):
    return pl.CostEstimate(
        flops=2 * heads * queries * keys * HEAD_DIM * products,
        bytes_accessed=moved,
        transcendentals=heads * queries * keys,
    )


def halo_shards(query_in, key_in, value_in, grad_out, module_lengths):
    tok, width = query_in.shape
    prior = tok * lax.axis_size("head") // 8
    step = math.gcd(width, 8 * HEAD_DIM)
    groups = width // step
    anywhere = pl.BlockSpec(memory_space=pl.ANY)
    inside = pl.BlockSpec(memory_space=pltpu.VMEM)
    full16 = jax.ShapeDtypeStruct((tok, width), jnp.bfloat16)

    def near16(rows, columns):
        return pltpu.VMEM((rows, columns), jnp.bfloat16)

    def near32(rows, columns):
        return pltpu.VMEM((rows, columns), jnp.float32)

    def in_hbm(*values):
        return [pltpu.with_memory_space_constraint(value, pltpu.HBM) for value in values]

    def in_vmem(*values):
        return [pltpu.with_memory_space_constraint(value, pltpu.VMEM) for value in values]

    def call(kernel, name, ins, outs, shapes, scratch, work, moved, aliases=None):
        return pl.pallas_call(
            kernel,
            in_specs=ins,
            out_specs=outs,
            out_shape=shapes,
            scratch_shapes=scratch,
            input_output_aliases=aliases or {},
            cost_estimate=cost(*work, moved),
            compiler_params=pltpu.CompilerParams(vmem_limit_bytes=16 * 2**20),
            name=name,
        )

    near, far = call(
        functools.partial(pack_kernel, prior), "late_keys",
        [anywhere] * 2, [inside] * 2, [near16(prior, width)] * 2,
        [pltpu.SemaphoreType.DMA((2,))] * 2, (0, 0, 0, 0), 8 * prior * width,
    )(*in_hbm(key_in, value_in))
    near, far = neighbour(near, 1), neighbour(far, 1)

    lengths = module_lengths.reshape(1, -1)
    q, k, v, do, own_bias, near_bias, lead_bias, tail_bias = call(
        functools.partial(ready_kernel, prior), "operands",
        [anywhere] * 5, [inside] * 8,
        [near16(tok, width)] * 4
        + [near32(tok, 2 * prior), near32(prior + prior // 2, 2 * prior)]
        + [near32(2 * prior, 2 * prior), near32(prior, 2 * prior)],
        [
            pltpu.VMEM(lengths.shape, jnp.int32), pltpu.SemaphoreType.DMA((4,)),
            pltpu.SemaphoreType.DMA(()),
        ],
        (0, 0, 0, 0), 16 * tok * width,
    )(*in_hbm(lengths, query_in, key_in, value_in, grad_out))

    attn, gq, gk_part, gv_part = call(
        functools.partial(own_kernel, prior, step), "own_block",
        [inside] * 5, [inside] * 4,
        [near16(tok - prior, width)] * 2 + [near32(tok, width)] * 2, (),
        (width // HEAD_DIM, tok - prior, tok, 6), 18 * tok * width,
    )(*in_vmem(own_bias, q, k, v, do))

    near_bias, attn = lax.optimization_barrier((near_bias, attn))
    backs = call(
        functools.partial(near_kernel, prior), "near_terms",
        [inside] * 7, [inside] * groups, [near16(prior, step)] * groups, (),
        (width // HEAD_DIM, prior, prior + prior // 2, 3), 8 * tok * width,
    )(*in_vmem(near_bias, lead_bias, q, k, v, do, near))
    backs = [neighbour(back, -1) for back in backs]

    attn, gq, gk, gv = call(
        functools.partial(lead_kernel, prior, step), "lead_rows",
        [inside] * 11, [anywhere] * 4, [full16] * 4,
        [near16(prior, width)] * 4
        + [pltpu.SemaphoreType.DMA((groups, 4)), pltpu.SemaphoreType.DMA((2,))],
        (width // HEAD_DIM, prior, 2 * prior, 6), 20 * tok * width,
    )(*in_vmem(lead_bias, q, k, v, do, near, far, gk_part, gv_part, attn, gq))

    gk, gv = call(
        functools.partial(tail_kernel, prior), "tail_keys",
        [inside] * (5 + groups) + [anywhere] * 2, [anywhere] * 2, [full16] * 2,
        [near16(prior, width)] * 2 + [pltpu.SemaphoreType.DMA((2,))],
        (width // HEAD_DIM, prior, prior // 2, 4), 10 * tok * width,
        {5 + groups: 0, 6 + groups: 1},
    )(*in_vmem(tail_bias, k, v, gk_part, gv_part, *backs), gk, gv)
    return (attn, gq, gk, gv)


def shards(query_in, key_in, value_in, grad_out, module_lengths):
    tok = query_in.shape[0]
    prior = tok * lax.axis_size("head") // 8
    plan = halo_shards if 2 * prior == tok else gathered_shards
    return plan(query_in, key_in, value_in, grad_out, module_lengths)


def solution(mesh):
    placed = (
        P(("seq", "head"), None),
        P(("seq", "head"), None),
        P(("seq", "head"), None),
        P(("seq", "head"), None),
        P(),
    )
    return jax.shard_map(
        shards,
        mesh=mesh,
        in_specs=placed,
        out_specs=(
            P(("seq", "head"), None),
            P(("seq", "head"), None),
            P(("seq", "head"), None),
            P(("seq", "head"), None),
        ),
        check_vma=False,
    )
```

```python
import functools
import math

import jax
import jax.numpy as jnp
from jax import lax
from jax.experimental import pallas as pl
from jax.experimental.pallas import tpu as pltpu
from jax.sharding import PartitionSpec as P

HEAD_DIM = 128
SCALE = HEAD_DIM ** (-0.5)
LOG2E = math.log2(math.e)
MASKED = -1e30


def shifted(value, axis, by):
    peers = lax.axis_size(axis)
    pairs = [(i, i + by) for i in range(peers) if 0 <= i + by < peers]
    return lax.ppermute(value, axis, pairs)


def module_ids(module_lengths, positions):
    module_ends = jnp.cumsum(module_lengths)
    counted = jnp.sum((positions[:, None] >= module_ends[None, :]).astype(jnp.int32), axis=1)
    return jnp.where(positions >= 0, counted, -1)


def allowed_pairs(module_lengths, query_pos, key_pos):
    same = (
        module_ids(module_lengths, query_pos)[:, None]
        == module_ids(module_lengths, key_pos)[None, :]
    )
    return same & (key_pos[None, :] <= query_pos[:, None])


def score_grads(grad_rows, value_block, weights, row_delta, score_scale):
    dprobs = jnp.einsum("qd,kd->qk", grad_rows, value_block, preferred_element_type=jnp.float32)
    return (weights * (dprobs - row_delta[:, None]) * score_scale).astype(jnp.bfloat16)


def key_terms(dscores, weight_bf, query_rows, grad_rows):
    key_grad = jnp.einsum("qk,qd->kd", dscores, query_rows, preferred_element_type=jnp.float32)
    value_grad = jnp.einsum("qk,qd->kd", weight_bf, grad_rows, preferred_element_type=jnp.float32)
    return (key_grad, value_grad)


def one_block(query_rows, key_block, value_block, grad_rows, allowed, score_scale):
    scores = (
        jnp.einsum("qd,kd->qk", query_rows, key_block, preferred_element_type=jnp.float32)
        * score_scale
    )
    row_top = jnp.max(jnp.where(allowed, scores, -jnp.inf), axis=1, keepdims=True)
    row_total = jnp.sum(jnp.where(allowed, jnp.exp(scores - row_top), 0.0), axis=1, keepdims=True)
    log_total = row_top + jnp.log(row_total)
    weights = jnp.where(allowed, jnp.exp(scores - log_total), 0.0)
    weight_bf = weights.astype(jnp.bfloat16)
    attn_rows = jnp.einsum(
        "qk,kd->qd", weight_bf, value_block, preferred_element_type=jnp.float32
    ).astype(jnp.bfloat16)
    row_delta = jnp.sum(grad_rows.astype(jnp.float32) * attn_rows.astype(jnp.float32), axis=1)
    dscores = score_grads(grad_rows, value_block, weights, row_delta, score_scale)
    grad_q = jnp.einsum("qk,kd->qd", dscores, key_block, preferred_element_type=jnp.float32).astype(
        jnp.bfloat16
    )
    key_grad, value_grad = key_terms(dscores, weight_bf, query_rows, grad_rows)
    return (attn_rows, grad_q, key_grad, value_grad, log_total[:, 0], row_delta)


def gathered_shards(query_in, key_in, value_in, grad_out, module_lengths):
    head_q, head_k, head_v, head_do = (
        lax.all_to_all(query_in, "head", split_axis=1, concat_axis=0, tiled=True),
        lax.all_to_all(key_in, "head", split_axis=1, concat_axis=0, tiled=True),
        lax.all_to_all(value_in, "head", split_axis=1, concat_axis=0, tiled=True),
        lax.all_to_all(grad_out, "head", split_axis=1, concat_axis=0, tiled=True),
    )
    row_count = head_q.shape[0]
    width = head_q.shape[1]
    local_heads = width // HEAD_DIM
    prior_rows = row_count // 8
    score_scale = HEAD_DIM ** (-0.5)
    tail_start = row_count - prior_rows
    prior_k, prior_v = shifted((head_k[tail_start:], head_v[tail_start:]), "seq", 1)
    row_start = lax.axis_index("seq") * row_count
    query_pos = row_start + jnp.arange(row_count, dtype=jnp.int32)
    before_pos = row_start - prior_rows + jnp.arange(prior_rows, dtype=jnp.int32)
    key_pos = jnp.concatenate([before_pos, query_pos])
    block_rows = math.gcd(row_count, 512)
    block_count = row_count // block_rows
    pos_blocks = query_pos.reshape(block_count, block_rows)

    def by_head(flat, rows):
        return jnp.moveaxis(flat.reshape(rows, local_heads, HEAD_DIM), 1, 0)

    def to_flat(stacked):
        return jnp.moveaxis(stacked, 0, 1).reshape(stacked.shape[1], width)

    query_h = by_head(head_q, row_count)
    grad_h = by_head(head_do, row_count)
    key_h = by_head(jnp.concatenate([prior_k, head_k], axis=0), row_count + prior_rows)
    value_h = by_head(jnp.concatenate([prior_v, head_v], axis=0), row_count + prior_rows)

    def run_head(packed):
        query_rows, key_block, value_block, grad_rows = packed
        query_blocks = query_rows.reshape(block_count, block_rows, HEAD_DIM)
        grad_blocks = grad_rows.reshape(block_count, block_rows, HEAD_DIM)

        def run_block(inner):
            query_part, grad_part, pos_part = inner
            allowed = allowed_pairs(module_lengths, pos_part, key_pos)
            return one_block(query_part, key_block, value_block, grad_part, allowed, score_scale)

        attn_b, grad_qb, key_b, value_b, lse_b, delta_b = lax.map(
            run_block, (query_blocks, grad_blocks, pos_blocks)
        )
        return (
            attn_b.reshape(row_count, HEAD_DIM),
            grad_qb.reshape(row_count, HEAD_DIM),
            jnp.sum(key_b, axis=0),
            jnp.sum(value_b, axis=0),
            lse_b.reshape(row_count),
            delta_b.reshape(row_count),
        )

    attn_h, grad_qh, key_grad, value_grad, log_total, row_delta = lax.map(
        run_head, (query_h, key_h, value_h, grad_h)
    )
    attn_flat = to_flat(attn_h)
    attn_back = lax.all_to_all(attn_flat, "head", split_axis=0, concat_axis=1, tiled=True)
    grad_q = to_flat(grad_qh)
    later_k, later_v = shifted((key_grad[:, :prior_rows], value_grad[:, :prior_rows]), "seq", -1)
    key_total = key_grad[:, prior_rows:].at[:, tail_start:].add(later_k)
    value_total = value_grad[:, prior_rows:].at[:, tail_start:].add(later_v)
    grad_k = to_flat(key_total.astype(jnp.bfloat16))
    grad_v = to_flat(value_total.astype(jnp.bfloat16))
    back_q, back_k, back_v = (
        lax.all_to_all(grad_q, "head", split_axis=0, concat_axis=1, tiled=True),
        lax.all_to_all(grad_k, "head", split_axis=0, concat_axis=1, tiled=True),
        lax.all_to_all(grad_v, "head", split_axis=0, concat_axis=1, tiled=True),
    )
    return (attn_back, back_q, back_k, back_v)


def dot(left, right, left_dim, right_dim):
    return lax.dot_general(
        left, right, (((left_dim,), (right_dim,)), ((), ())), preferred_element_type=jnp.float32
    )


def module_ends_col(lengths_row):
    count = lengths_row.shape[1]
    row = lax.broadcasted_iota(jnp.int32, (count, count), 0)
    col = lax.broadcasted_iota(jnp.int32, (count, count), 1)
    return jnp.sum(jnp.where(col <= row, lengths_row, 0.0), axis=1, keepdims=True)


def bias_by_key(lengths_row, first_query, queries, first_key, keys, heads):
    ends = module_ends_col(lengths_row)
    lane = lax.broadcasted_iota(jnp.int32, (1, heads * queries), 1)
    query = (first_query + lane % queries).astype(jnp.float32)
    start = jnp.max(jnp.where(ends <= query, ends, 0.0), axis=0, keepdims=True)
    key = (first_key + lax.broadcasted_iota(jnp.int32, (keys, heads * queries), 0)).astype(
        jnp.float32
    )
    return jnp.where((key >= start) & (key <= query), 0.0, MASKED)


def score_pair(k, q, v, do, bias):
    return dot(k, q, 1, 1) * (SCALE * LOG2E) + bias, dot(v, do, 1, 1)


def softmax_columns(pairs):
    tops = [jnp.max(s, axis=0, keepdims=True) for s, _ in pairs]
    raws = [jnp.exp2(s - top) for (s, _), top in zip(pairs, tops)]
    totals = [jnp.sum(raw, axis=0, keepdims=True) for raw in raws]
    weights = [raw * (1.0 / total) for raw, total in zip(raws, totals)]
    deltas = [jnp.sum(w * dp, axis=0, keepdims=True) for w, (_, dp) in zip(weights, pairs)]
    logs = [top + jnp.log2(total) for top, total in zip(tops, totals)]
    return weights, logs, deltas


def score_grads_of(pairs, weights, deltas):
    return [
        (w * (dp - delta) * SCALE).astype(jnp.bfloat16)
        for w, (_, dp), delta in zip(weights, pairs, deltas)
    ]


def merged_columns(pairs, own):
    tops = [
        jnp.maximum(jnp.max(s, axis=0, keepdims=True), log) for (s, _), (log, _) in zip(pairs, own)
    ]
    raws = [jnp.exp2(s - top) for (s, _), top in zip(pairs, tops)]
    own_raws = [jnp.exp2(log - top) for (log, _), top in zip(own, tops)]
    parts = [
        1.0 / (jnp.sum(raw, axis=0, keepdims=True) + own_raw)
        for raw, own_raw in zip(raws, own_raws)
    ]
    weights = [raw * part for raw, part in zip(raws, parts)]
    deltas = [
        jnp.sum(w * dp, axis=0, keepdims=True) + own_raw * part * own_delta
        for w, (_, dp), own_raw, part, (_, own_delta) in zip(weights, pairs, own_raws, parts, own)
    ]
    grads = [w * (dp - delta) * SCALE for w, (_, dp), delta in zip(weights, pairs, deltas)]
    return [w.astype(jnp.bfloat16) for w in weights], [g.astype(jnp.bfloat16) for g in grads]


def side_by_side(rows):
    heads = rows.shape[1] // HEAD_DIM
    zero = jnp.zeros((rows.shape[0], HEAD_DIM), rows.dtype)
    blocks = [rows[:, c] for c in head_columns(0, rows.shape[1])]
    return jnp.concatenate(
        [
            jnp.concatenate([blocks[h] if g == h else zero for g in range(heads)], axis=1)
            for h in range(heads)
        ],
        axis=0,
    )


def head_columns(low, high, heads=1):
    wide = heads * HEAD_DIM
    return [slice(c, c + wide) for c in range(low, high, wide)]


def device_first(tok):
    place = lax.axis_index("seq") * lax.axis_size("head") + lax.axis_index("head")
    return place * tok


def fours(rows):
    table = jnp.concatenate(rows, axis=0)
    half = table.shape[1] // 4
    lane = lax.broadcasted_iota(jnp.int32, (1, table.shape[1]), 1)
    turned = [pltpu.roll(table, turn * half, 1) for turn in (3, 2, 1)]
    merged = []
    for at in range(0, len(rows), 2):
        now, after = slice(at, at + 1), slice(at + 1, at + 2)
        row = jnp.where(lane < 3 * half, turned[1][after], turned[2][after])
        row = jnp.where(lane < 2 * half, turned[0][now], row)
        merged.append(jnp.where(lane < half, table[now], row))
    return merged


def split_bf16(row):
    parts = []
    for _ in range(3):
        part = row.astype(jnp.bfloat16)
        parts.append(part)
        row = row - part.astype(jnp.float32)
    return jnp.concatenate([*parts, jnp.zeros_like(parts[0])], axis=1)


def joined(parts):
    parts = parts.astype(jnp.float32)
    count = parts.shape[1] // 4
    return parts[:, :count] + parts[:, count : 2 * count] + parts[:, 2 * count : 3 * count]


def pack_copies(prior, at, k_ref, v_ref, packed_ref, sems):
    half, tok = prior // 2, k_ref.shape[0]
    rows = pl.ds(tok - (at + 1) * half, half)
    return [
        pltpu.make_async_copy(
            ref.at[rows, :], packed_ref.at[pl.ds(n * half, half), :], sems.at[n]
        )
        for n, ref in enumerate((k_ref, v_ref))
    ]


def pack_kernel(prior, k_ref, v_ref, near_ref, sems):
    copies = pack_copies(prior, 0, k_ref, v_ref, near_ref, sems)
    for copy in copies:
        copy.start()
    for copy in copies:
        copy.wait()


def ready_kernel(
    prior, len_hbm, q_hbm, k_hbm, v_hbm, do_hbm, far_ref, q_ref, k_ref, v_ref, do_ref,
    own_bias_ref, near_bias_ref, lead_bias_ref, tail_bias_ref, len_ref, sems, far_sems, len_sem,
):
    tok, half = k_ref.shape[0], prior // 2
    pairs = ((q_hbm, q_ref), (k_hbm, k_ref), (v_hbm, v_ref), (do_hbm, do_ref))
    copies = pack_copies(prior, 1, k_hbm, v_hbm, far_ref, far_sems)
    copies += [pltpu.make_async_copy(hbm, ref, sems.at[n]) for n, (hbm, ref) in enumerate(pairs)]
    len_copy = pltpu.make_async_copy(len_hbm, len_ref, len_sem)
    len_copy.start()
    for copy in copies:
        copy.start()
    len_copy.wait()
    first = device_first(tok)
    lengths = len_ref[...].astype(jnp.float32)
    own_bias_ref[...] = bias_by_key(lengths, first + prior, tok - prior, first, tok, 2)
    near_bias_ref[...] = bias_by_key(lengths, first, prior, first - half, prior + half, 2)
    lead_bias_ref[...] = bias_by_key(lengths, first, prior, first - prior, 2 * prior, 2)
    tail_bias_ref[...] = bias_by_key(lengths, first + tok, half, first + tok - prior, prior, 4)
    for copy in copies:
        copy.wait()


def own_diagonal(both):
    rows = both.shape[0] // 2
    return jnp.concatenate([both[:rows, :HEAD_DIM], both[rows:, HEAD_DIM:]], axis=1)


def pair_columns(at, step):
    wide = 2 * HEAD_DIM
    return [pl.ds(pl.multiple_of(at * step + c, wide), wide) for c in range(0, step, wide)]


def own_kernel(
    prior, step, bias_ref, q_ref, k_ref, v_ref, do_ref, attn_ref, gq_ref, gk_ref, gv_ref
):
    tok, width = k_ref.shape
    late = slice(prior, tok)

    @pl.loop(0, width // step)
    def _(at):
        bias = bias_ref[...]
        columns = pair_columns(at, step)
        queries = [side_by_side(q_ref[late, c]) for c in columns]
        cotangents = [side_by_side(do_ref[late, c]) for c in columns]
        pairs = [
            score_pair(k_ref[:, c], q, v_ref[:, c], do, bias)
            for c, q, do in zip(columns, queries, cotangents)
        ]
        weights, _, deltas = softmax_columns(pairs)
        grads = score_grads_of(pairs, weights, deltas)
        for c, w, g, q, do in zip(columns, weights, grads, queries, cotangents):
            w = w.astype(jnp.bfloat16)
            attn_ref[:, c] = own_diagonal(dot(w, v_ref[:, c], 0, 0)).astype(jnp.bfloat16)
            gq_ref[:, c] = own_diagonal(dot(g, k_ref[:, c], 0, 0)).astype(jnp.bfloat16)
            gk_ref[:, c] = dot(g, q, 1, 0)
            gv_ref[:, c] = dot(w, do, 1, 0)


def near_kernel(
    prior, near_bias_ref, lead_bias_ref, q_ref, k_ref, v_ref, do_ref, near_ref, *back_refs
):
    width, half = q_ref.shape[1], prior // 2
    far = lead_bias_ref[half - 1 : half, 0:1] == 0.0
    key = lax.broadcasted_iota(jnp.int32, (prior + half, 1), 0)
    bias = jnp.where(far & (key < half), MASKED, near_bias_ref[...])
    spare = lax.broadcasted_iota(jnp.int32, (half, 1), 0) == half - 1
    early, first, second = slice(0, prior), slice(0, half), slice(half, prior)
    columns = head_columns(0, width, 2)
    queries = [side_by_side(q_ref[early, c]) for c in columns]
    cotangents = [side_by_side(do_ref[early, c]) for c in columns]
    pairs = []
    for c, q, do in zip(columns, queries, cotangents):
        k = jnp.concatenate([near_ref[first, c], k_ref[early, c]], axis=0)
        v = jnp.concatenate([near_ref[second, c], v_ref[early, c]], axis=0)
        pairs.append(score_pair(k, q, v, do, bias))
    weights, logs, deltas = softmax_columns(pairs)
    weights = [w[:half] for w in weights]
    grads = score_grads_of([(s[:half], dp[:half]) for s, dp in pairs], weights, deltas)
    k_terms = [dot(g, q, 1, 0) for g, q in zip(grads, queries)]
    v_terms = [dot(w.astype(jnp.bfloat16), do, 1, 0) for w, do in zip(weights, cotangents)]
    logs, deltas = fours(logs), fours(deltas)
    for at, c in enumerate(head_columns(0, width, 4)):
        back_ref = back_refs[c.start * len(back_refs) // width]
        low = c.start % back_ref.shape[1]
        here = slice(low, low + c.stop - c.start)
        for row, terms, ref, place in (
            (logs[at], k_terms, q_ref, first), (deltas[at], v_terms, do_ref, second)
        ):
            rows = jnp.where(spare, split_bf16(row), ref[first, c])
            terms = jnp.concatenate(terms[2 * at : 2 * at + 2], axis=1).astype(jnp.bfloat16)
            back_ref[place, here] = jnp.where(far, rows, terms)


def lead_kernel(
    prior, step, bias_ref, q_ref, k_ref, v_ref, do_ref, near_ref, far_ref, gk_part_ref, gv_part_ref,
    attn_late_ref, gq_late_ref, attn_hbm, gq_hbm, gk_hbm, gv_hbm,
    attn_ref, gq_ref, gk_ref, gv_ref, sems, late_sems,
):
    tok, width = q_ref.shape
    half = prior // 2
    early, first, second = slice(0, prior), slice(0, half), slice(half, prior)
    late = pl.ds(prior, tok - prior)
    late_copies = [
        pltpu.make_async_copy(attn_late_ref, attn_hbm.at[late, :], late_sems.at[0]),
        pltpu.make_async_copy(gq_late_ref, gq_hbm.at[late, :], late_sems.at[1]),
    ]
    for copy in late_copies:
        copy.start()

    def copies(at):
        cols = pl.ds(pl.multiple_of(at * step, step), step)
        pairs = ((attn_ref, attn_hbm), (gq_ref, gq_hbm), (gk_ref, gk_hbm), (gv_ref, gv_hbm))
        return [
            pltpu.make_async_copy(ref.at[:, cols], hbm.at[pl.ds(0, prior), cols], sems.at[at, n])
            for n, (ref, hbm) in enumerate(pairs)
        ]

    @pl.loop(0, width // step)
    def _(at):
        bias = bias_ref[...]
        columns = pair_columns(at, step)
        queries = [side_by_side(q_ref[early, c]) for c in columns]
        cotangents = [side_by_side(do_ref[early, c]) for c in columns]
        keys = [
            jnp.concatenate([far_ref[first, c], near_ref[first, c], k_ref[early, c]], axis=0)
            for c in columns
        ]
        values = [
            jnp.concatenate([far_ref[second, c], near_ref[second, c], v_ref[early, c]], axis=0)
            for c in columns
        ]
        pairs = [
            score_pair(k, q, v, do, bias)
            for k, q, v, do in zip(keys, queries, values, cotangents)
        ]
        weights, _, deltas = softmax_columns(pairs)
        grads = score_grads_of(pairs, weights, deltas)
        for n, c in enumerate(columns):
            w, g = weights[n].astype(jnp.bfloat16), grads[n]
            attn_ref[:, c] = own_diagonal(dot(w, values[n], 0, 0)).astype(jnp.bfloat16)
            gq_ref[:, c] = own_diagonal(dot(g, keys[n], 0, 0)).astype(jnp.bfloat16)
            gk = gk_part_ref[early, c] + dot(g[prior:], queries[n], 1, 0)
            gv = gv_part_ref[early, c] + dot(w[prior:], cotangents[n], 1, 0)
            gk_ref[:, c] = gk.astype(jnp.bfloat16)
            gv_ref[:, c] = gv.astype(jnp.bfloat16)
        for copy in copies(at):
            copy.start()

    for at in range(width // step):
        for copy in copies(at):
            copy.wait()
    for copy in late_copies:
        copy.wait()


def tail_kernel(prior, bias_ref, k_ref, v_ref, gk_part_ref, gv_part_ref, *refs):
    *after_refs, _, _, gk_hbm, gv_hbm, gk_ref, gv_ref, sems = refs
    tok, width = k_ref.shape
    half = prior // 2
    far = bias_ref[half - 1 : half, 0:1] == 0.0
    bias = jnp.where(far, bias_ref[...], MASKED)
    first, second, last = slice(0, half), slice(half, prior), slice(tok - prior, tok)
    columns = head_columns(0, width, 4)
    afters = [
        (after_ref, p) for after_ref in after_refs for p in head_columns(0, after_ref.shape[1], 4)
    ]
    queries = [side_by_side(after_ref[first, p]) for after_ref, p in afters]
    cotangents = [side_by_side(after_ref[second, p]) for after_ref, p in afters]
    pairs = [
        score_pair(k_ref[last, c], q, v_ref[last, c], do, bias)
        for c, q, do in zip(columns, queries, cotangents)
    ]
    own = [
        (joined(after_ref[half - 1 : half, p]), joined(after_ref[prior - 1 : prior, p]))
        for after_ref, p in afters
    ]
    weights, grads = merged_columns(pairs, own)
    copies = []
    for at, (ref, hbm, part_ref, lefts, rights, rows) in enumerate(
        (
            (gv_ref, gv_hbm, gv_part_ref, weights, cotangents, second),
            (gk_ref, gk_hbm, gk_part_ref, grads, queries, first),
        )
    ):
        for (after_ref, p), c, left, right in zip(afters, columns, lefts, rights):
            total = part_ref[last, c] + dot(left, right, 1, 0)
            terms = jnp.where(far, 0.0, after_ref[rows, p].astype(jnp.float32))
            ref[first, c] = total[first].astype(jnp.bfloat16)
            ref[second, c] = (total[second] + terms).astype(jnp.bfloat16)
        copies.append(
            pltpu.make_async_copy(ref, hbm.at[pl.ds(tok - prior, prior), :], sems.at[at])
        )
        copies[-1].start()
    for copy in copies:
        copy.wait()


def neighbour(value, by):
    peers = lax.axis_size("seq") * lax.axis_size("head")
    pairs = [(i, i + by) for i in range(peers) if 0 <= i + by < peers]
    return lax.ppermute(value, ("seq", "head"), pairs)


def cost(heads, queries, keys, products, moved):
    return pl.CostEstimate(
        flops=2 * heads * queries * keys * HEAD_DIM * products,
        bytes_accessed=moved,
        transcendentals=heads * queries * keys,
    )


def halo_shards(query_in, key_in, value_in, grad_out, module_lengths):
    tok, width = query_in.shape
    prior = tok * lax.axis_size("head") // 8
    step = math.gcd(width, 8 * HEAD_DIM)
    groups = width // step
    anywhere = pl.BlockSpec(memory_space=pl.ANY)
    inside = pl.BlockSpec(memory_space=pltpu.VMEM)
    full16 = jax.ShapeDtypeStruct((tok, width), jnp.bfloat16)

    def near16(rows, columns):
        return pltpu.VMEM((rows, columns), jnp.bfloat16)

    def near32(rows, columns):
        return pltpu.VMEM((rows, columns), jnp.float32)

    def in_hbm(*values):
        return [pltpu.with_memory_space_constraint(value, pltpu.HBM) for value in values]

    def in_vmem(*values):
        return [pltpu.with_memory_space_constraint(value, pltpu.VMEM) for value in values]

    def call(kernel, name, ins, outs, shapes, scratch, work, moved, aliases=None):
        return pl.pallas_call(
            kernel,
            in_specs=ins,
            out_specs=outs,
            out_shape=shapes,
            scratch_shapes=scratch,
            input_output_aliases=aliases or {},
            cost_estimate=cost(*work, moved),
            compiler_params=pltpu.CompilerParams(vmem_limit_bytes=16 * 2**20),
            name=name,
        )

    near = call(
        functools.partial(pack_kernel, prior), "near_keys",
        [anywhere] * 2, inside, near16(prior, width),
        [pltpu.SemaphoreType.DMA((2,))], (0, 0, 0, 0), 4 * prior * width,
    )(*in_hbm(key_in, value_in))
    near = neighbour(near, 1)

    lengths = module_lengths.reshape(1, -1)
    far, q, k, v, do, own_bias, near_bias, lead_bias, tail_bias = call(
        functools.partial(ready_kernel, prior), "operands",
        [anywhere] * 5, [inside] * 9,
        [near16(prior, width)] + [near16(tok, width)] * 4
        + [near32(tok, 2 * prior), near32(prior + prior // 2, 2 * prior)]
        + [near32(2 * prior, 2 * prior), near32(prior, 2 * prior)],
        [
            pltpu.VMEM(lengths.shape, jnp.int32), pltpu.SemaphoreType.DMA((4,)),
            pltpu.SemaphoreType.DMA((2,)), pltpu.SemaphoreType.DMA(()),
        ],
        (0, 0, 0, 0), 18 * tok * width,
    )(*in_hbm(lengths, query_in, key_in, value_in, grad_out))

    attn, gq, gk_part, gv_part = call(
        functools.partial(own_kernel, prior, step), "own_block",
        [inside] * 5, [inside] * 4,
        [near16(tok - prior, width)] * 2 + [near32(tok, width)] * 2, (),
        (width // HEAD_DIM, tok - prior, tok, 6), 18 * tok * width,
    )(*in_vmem(own_bias, q, k, v, do))

    far, near_bias, attn = lax.optimization_barrier((far, near_bias, attn))
    far = neighbour(far, 1)

    backs = call(
        functools.partial(near_kernel, prior), "near_terms",
        [inside] * 7, [inside] * groups, [near16(prior, step)] * groups, (),
        (width // HEAD_DIM, prior, prior + prior // 2, 3), 8 * tok * width,
    )(*in_vmem(near_bias, lead_bias, q, k, v, do, near))
    backs = [neighbour(back, -1) for back in backs]

    attn, gq, gk, gv = call(
        functools.partial(lead_kernel, prior, step), "lead_rows",
        [inside] * 11, [anywhere] * 4, [full16] * 4,
        [near16(prior, width)] * 4
        + [pltpu.SemaphoreType.DMA((groups, 4)), pltpu.SemaphoreType.DMA((2,))],
        (width // HEAD_DIM, prior, 2 * prior, 6), 20 * tok * width,
    )(*in_vmem(lead_bias, q, k, v, do, near, far, gk_part, gv_part, attn, gq))

    gk, gv = call(
        functools.partial(tail_kernel, prior), "tail_keys",
        [inside] * (5 + groups) + [anywhere] * 2, [anywhere] * 2, [full16] * 2,
        [near16(prior, width)] * 2 + [pltpu.SemaphoreType.DMA((2,))],
        (width // HEAD_DIM, prior, prior // 2, 4), 10 * tok * width,
        {5 + groups: 0, 6 + groups: 1},
    )(*in_vmem(tail_bias, k, v, gk_part, gv_part, *backs), gk, gv)
    return (attn, gq, gk, gv)


def shards(query_in, key_in, value_in, grad_out, module_lengths):
    tok = query_in.shape[0]
    prior = tok * lax.axis_size("head") // 8
    plan = halo_shards if 2 * prior == tok else gathered_shards
    return plan(query_in, key_in, value_in, grad_out, module_lengths)


def solution(mesh):
    placed = (
        P(("seq", "head"), None),
        P(("seq", "head"), None),
        P(("seq", "head"), None),
        P(("seq", "head"), None),
        P(),
    )
    return jax.shard_map(
        shards,
        mesh=mesh,
        in_specs=placed,
        out_specs=(
            P(("seq", "head"), None),
            P(("seq", "head"), None),
            P(("seq", "head"), None),
            P(("seq", "head"), None),
        ),
        check_vma=False,
    )
```

```python
import functools
import math

import jax
import jax.numpy as jnp
from jax import lax
from jax.experimental import pallas as pl
from jax.experimental.pallas import tpu as pltpu
from jax.sharding import PartitionSpec as P

HEAD_DIM = 128
SCALE = HEAD_DIM ** (-0.5)
LOG2E = math.log2(math.e)
MASKED = -1e30


def shifted(value, axis, by):
    peers = lax.axis_size(axis)
    pairs = [(i, i + by) for i in range(peers) if 0 <= i + by < peers]
    return lax.ppermute(value, axis, pairs)


def module_ids(module_lengths, positions):
    module_ends = jnp.cumsum(module_lengths)
    counted = jnp.sum((positions[:, None] >= module_ends[None, :]).astype(jnp.int32), axis=1)
    return jnp.where(positions >= 0, counted, -1)


def allowed_pairs(module_lengths, query_pos, key_pos):
    same = (
        module_ids(module_lengths, query_pos)[:, None]
        == module_ids(module_lengths, key_pos)[None, :]
    )
    return same & (key_pos[None, :] <= query_pos[:, None])


def score_grads(grad_rows, value_block, weights, row_delta, score_scale):
    dprobs = jnp.einsum("qd,kd->qk", grad_rows, value_block, preferred_element_type=jnp.float32)
    return (weights * (dprobs - row_delta[:, None]) * score_scale).astype(jnp.bfloat16)


def key_terms(dscores, weight_bf, query_rows, grad_rows):
    key_grad = jnp.einsum("qk,qd->kd", dscores, query_rows, preferred_element_type=jnp.float32)
    value_grad = jnp.einsum("qk,qd->kd", weight_bf, grad_rows, preferred_element_type=jnp.float32)
    return (key_grad, value_grad)


def one_block(query_rows, key_block, value_block, grad_rows, allowed, score_scale):
    scores = (
        jnp.einsum("qd,kd->qk", query_rows, key_block, preferred_element_type=jnp.float32)
        * score_scale
    )
    row_top = jnp.max(jnp.where(allowed, scores, -jnp.inf), axis=1, keepdims=True)
    row_total = jnp.sum(jnp.where(allowed, jnp.exp(scores - row_top), 0.0), axis=1, keepdims=True)
    log_total = row_top + jnp.log(row_total)
    weights = jnp.where(allowed, jnp.exp(scores - log_total), 0.0)
    weight_bf = weights.astype(jnp.bfloat16)
    attn_rows = jnp.einsum(
        "qk,kd->qd", weight_bf, value_block, preferred_element_type=jnp.float32
    ).astype(jnp.bfloat16)
    row_delta = jnp.sum(grad_rows.astype(jnp.float32) * attn_rows.astype(jnp.float32), axis=1)
    dscores = score_grads(grad_rows, value_block, weights, row_delta, score_scale)
    grad_q = jnp.einsum("qk,kd->qd", dscores, key_block, preferred_element_type=jnp.float32).astype(
        jnp.bfloat16
    )
    key_grad, value_grad = key_terms(dscores, weight_bf, query_rows, grad_rows)
    return (attn_rows, grad_q, key_grad, value_grad, log_total[:, 0], row_delta)


def gathered_shards(query_in, key_in, value_in, grad_out, module_lengths):
    head_q, head_k, head_v, head_do = (
        lax.all_to_all(query_in, "head", split_axis=1, concat_axis=0, tiled=True),
        lax.all_to_all(key_in, "head", split_axis=1, concat_axis=0, tiled=True),
        lax.all_to_all(value_in, "head", split_axis=1, concat_axis=0, tiled=True),
        lax.all_to_all(grad_out, "head", split_axis=1, concat_axis=0, tiled=True),
    )
    row_count = head_q.shape[0]
    width = head_q.shape[1]
    local_heads = width // HEAD_DIM
    prior_rows = row_count // 8
    score_scale = HEAD_DIM ** (-0.5)
    tail_start = row_count - prior_rows
    prior_k, prior_v = shifted((head_k[tail_start:], head_v[tail_start:]), "seq", 1)
    row_start = lax.axis_index("seq") * row_count
    query_pos = row_start + jnp.arange(row_count, dtype=jnp.int32)
    before_pos = row_start - prior_rows + jnp.arange(prior_rows, dtype=jnp.int32)
    key_pos = jnp.concatenate([before_pos, query_pos])
    block_rows = math.gcd(row_count, 512)
    block_count = row_count // block_rows
    pos_blocks = query_pos.reshape(block_count, block_rows)

    def by_head(flat, rows):
        return jnp.moveaxis(flat.reshape(rows, local_heads, HEAD_DIM), 1, 0)

    def to_flat(stacked):
        return jnp.moveaxis(stacked, 0, 1).reshape(stacked.shape[1], width)

    query_h = by_head(head_q, row_count)
    grad_h = by_head(head_do, row_count)
    key_h = by_head(jnp.concatenate([prior_k, head_k], axis=0), row_count + prior_rows)
    value_h = by_head(jnp.concatenate([prior_v, head_v], axis=0), row_count + prior_rows)

    def run_head(packed):
        query_rows, key_block, value_block, grad_rows = packed
        query_blocks = query_rows.reshape(block_count, block_rows, HEAD_DIM)
        grad_blocks = grad_rows.reshape(block_count, block_rows, HEAD_DIM)

        def run_block(inner):
            query_part, grad_part, pos_part = inner
            allowed = allowed_pairs(module_lengths, pos_part, key_pos)
            return one_block(query_part, key_block, value_block, grad_part, allowed, score_scale)

        attn_b, grad_qb, key_b, value_b, lse_b, delta_b = lax.map(
            run_block, (query_blocks, grad_blocks, pos_blocks)
        )
        return (
            attn_b.reshape(row_count, HEAD_DIM),
            grad_qb.reshape(row_count, HEAD_DIM),
            jnp.sum(key_b, axis=0),
            jnp.sum(value_b, axis=0),
            lse_b.reshape(row_count),
            delta_b.reshape(row_count),
        )

    attn_h, grad_qh, key_grad, value_grad, log_total, row_delta = lax.map(
        run_head, (query_h, key_h, value_h, grad_h)
    )
    attn_flat = to_flat(attn_h)
    attn_back = lax.all_to_all(attn_flat, "head", split_axis=0, concat_axis=1, tiled=True)
    grad_q = to_flat(grad_qh)
    later_k, later_v = shifted((key_grad[:, :prior_rows], value_grad[:, :prior_rows]), "seq", -1)
    key_total = key_grad[:, prior_rows:].at[:, tail_start:].add(later_k)
    value_total = value_grad[:, prior_rows:].at[:, tail_start:].add(later_v)
    grad_k = to_flat(key_total.astype(jnp.bfloat16))
    grad_v = to_flat(value_total.astype(jnp.bfloat16))
    back_q, back_k, back_v = (
        lax.all_to_all(grad_q, "head", split_axis=0, concat_axis=1, tiled=True),
        lax.all_to_all(grad_k, "head", split_axis=0, concat_axis=1, tiled=True),
        lax.all_to_all(grad_v, "head", split_axis=0, concat_axis=1, tiled=True),
    )
    return (attn_back, back_q, back_k, back_v)


def dot(left, right, left_dim, right_dim):
    return lax.dot_general(
        left, right, (((left_dim,), (right_dim,)), ((), ())), preferred_element_type=jnp.float32
    )


def module_ends_col(lengths_row):
    count = lengths_row.shape[1]
    row = lax.broadcasted_iota(jnp.int32, (count, count), 0)
    col = lax.broadcasted_iota(jnp.int32, (count, count), 1)
    return jnp.sum(jnp.where(col <= row, lengths_row, 0.0), axis=1, keepdims=True)


def bias_by_key(lengths_row, first_query, queries, first_key, keys, heads):
    ends = module_ends_col(lengths_row)
    lane = lax.broadcasted_iota(jnp.int32, (1, heads * queries), 1)
    query = (first_query + lane % queries).astype(jnp.float32)
    start = jnp.max(jnp.where(ends <= query, ends, 0.0), axis=0, keepdims=True)
    key = (first_key + lax.broadcasted_iota(jnp.int32, (keys, heads * queries), 0)).astype(
        jnp.float32
    )
    return jnp.where((key >= start) & (key <= query), 0.0, MASKED)


def score_pair(k, q, v, do, bias):
    return dot(k, q, 1, 1) * (SCALE * LOG2E) + bias, dot(v, do, 1, 1)


def softmax_columns(pairs):
    tops = [jnp.max(s, axis=0, keepdims=True) for s, _ in pairs]
    raws = [jnp.exp2(s - top) for (s, _), top in zip(pairs, tops)]
    totals = [jnp.sum(raw, axis=0, keepdims=True) for raw in raws]
    weights = [raw * (1.0 / total) for raw, total in zip(raws, totals)]
    deltas = [jnp.sum(w * dp, axis=0, keepdims=True) for w, (_, dp) in zip(weights, pairs)]
    logs = [top + jnp.log2(total) for top, total in zip(tops, totals)]
    return weights, logs, deltas


def score_grads_of(pairs, weights, deltas):
    return [
        (w * (dp - delta) * SCALE).astype(jnp.bfloat16)
        for w, (_, dp), delta in zip(weights, pairs, deltas)
    ]


def merged_columns(pairs, own):
    tops = [
        jnp.maximum(jnp.max(s, axis=0, keepdims=True), log) for (s, _), (log, _) in zip(pairs, own)
    ]
    raws = [jnp.exp2(s - top) for (s, _), top in zip(pairs, tops)]
    own_raws = [jnp.exp2(log - top) for (log, _), top in zip(own, tops)]
    parts = [
        1.0 / (jnp.sum(raw, axis=0, keepdims=True) + own_raw)
        for raw, own_raw in zip(raws, own_raws)
    ]
    weights = [raw * part for raw, part in zip(raws, parts)]
    deltas = [
        jnp.sum(w * dp, axis=0, keepdims=True) + own_raw * part * own_delta
        for w, (_, dp), own_raw, part, (_, own_delta) in zip(weights, pairs, own_raws, parts, own)
    ]
    grads = [w * (dp - delta) * SCALE for w, (_, dp), delta in zip(weights, pairs, deltas)]
    return [w.astype(jnp.bfloat16) for w in weights], [g.astype(jnp.bfloat16) for g in grads]


def side_by_side(rows):
    heads = rows.shape[1] // HEAD_DIM
    zero = jnp.zeros((rows.shape[0], HEAD_DIM), rows.dtype)
    blocks = [rows[:, c] for c in head_columns(0, rows.shape[1])]
    return jnp.concatenate(
        [
            jnp.concatenate([blocks[h] if g == h else zero for g in range(heads)], axis=1)
            for h in range(heads)
        ],
        axis=0,
    )


def head_columns(low, high, heads=1):
    wide = heads * HEAD_DIM
    return [slice(c, c + wide) for c in range(low, high, wide)]


def device_first(tok):
    place = lax.axis_index("seq") * lax.axis_size("head") + lax.axis_index("head")
    return place * tok


def fours(rows):
    table = jnp.concatenate(rows, axis=0)
    half = table.shape[1] // 4
    lane = lax.broadcasted_iota(jnp.int32, (1, table.shape[1]), 1)
    turned = [pltpu.roll(table, turn * half, 1) for turn in (3, 2, 1)]
    merged = []
    for at in range(0, len(rows), 2):
        now, after = slice(at, at + 1), slice(at + 1, at + 2)
        row = jnp.where(lane < 3 * half, turned[1][after], turned[2][after])
        row = jnp.where(lane < 2 * half, turned[0][now], row)
        merged.append(jnp.where(lane < half, table[now], row))
    return merged


def split_bf16(row):
    parts = []
    for _ in range(3):
        part = row.astype(jnp.bfloat16)
        parts.append(part)
        row = row - part.astype(jnp.float32)
    return jnp.concatenate([*parts, jnp.zeros_like(parts[0])], axis=1)


def joined(parts):
    parts = parts.astype(jnp.float32)
    count = parts.shape[1] // 4
    return parts[:, :count] + parts[:, count : 2 * count] + parts[:, 2 * count : 3 * count]


def pack_copies(prior, at, k_ref, v_ref, packed_ref, sems):
    half, tok = prior // 2, k_ref.shape[0]
    rows = pl.ds(tok - (at + 1) * half, half)
    return [
        pltpu.make_async_copy(
            ref.at[rows, :], packed_ref.at[pl.ds(n * half, half), :], sems.at[n]
        )
        for n, ref in enumerate((k_ref, v_ref))
    ]


def pack_kernel(prior, k_ref, v_ref, near_ref, sems):
    copies = pack_copies(prior, 0, k_ref, v_ref, near_ref, sems)
    for copy in copies:
        copy.start()
    for copy in copies:
        copy.wait()


def ready_kernel(
    prior, len_hbm, q_hbm, k_hbm, v_hbm, do_hbm, far_ref, q_ref, k_ref, v_ref, do_ref,
    own_bias_ref, near_bias_ref, lead_bias_ref, tail_bias_ref, len_ref, sems, far_sems, len_sem,
):
    tok, half = k_ref.shape[0], prior // 2
    pairs = ((q_hbm, q_ref), (k_hbm, k_ref), (v_hbm, v_ref), (do_hbm, do_ref))
    copies = pack_copies(prior, 1, k_hbm, v_hbm, far_ref, far_sems)
    copies += [pltpu.make_async_copy(hbm, ref, sems.at[n]) for n, (hbm, ref) in enumerate(pairs)]
    len_copy = pltpu.make_async_copy(len_hbm, len_ref, len_sem)
    len_copy.start()
    for copy in copies:
        copy.start()
    len_copy.wait()
    first = device_first(tok)
    lengths = len_ref[...].astype(jnp.float32)
    own_bias_ref[...] = bias_by_key(lengths, first + prior, tok - prior, first, tok, 2)
    near_bias_ref[...] = bias_by_key(lengths, first, prior, first - half, prior + half, 2)
    lead_bias_ref[...] = bias_by_key(lengths, first, prior, first - prior, 2 * prior, 2)
    tail_bias_ref[...] = bias_by_key(lengths, first + tok, half, first + tok - prior, prior, 4)
    for copy in copies:
        copy.wait()


def own_diagonal(both):
    rows = both.shape[0] // 2
    return jnp.concatenate([both[:rows, :HEAD_DIM], both[rows:, HEAD_DIM:]], axis=1)


def pair_columns(at, step):
    wide = 2 * HEAD_DIM
    return [pl.ds(pl.multiple_of(at * step + c, wide), wide) for c in range(0, step, wide)]


def own_kernel(
    prior, step, bias_ref, q_ref, k_ref, v_ref, do_ref, attn_ref, gq_ref, gk_ref, gv_ref
):
    tok, width = k_ref.shape
    late = slice(prior, tok)

    @pl.loop(0, width // step)
    def _(at):
        bias = bias_ref[...]
        columns = pair_columns(at, step)
        queries = [side_by_side(q_ref[late, c]) for c in columns]
        cotangents = [side_by_side(do_ref[late, c]) for c in columns]
        pairs = [
            score_pair(k_ref[:, c], q, v_ref[:, c], do, bias)
            for c, q, do in zip(columns, queries, cotangents)
        ]
        weights, _, deltas = softmax_columns(pairs)
        grads = score_grads_of(pairs, weights, deltas)
        for c, w, g, q, do in zip(columns, weights, grads, queries, cotangents):
            w = w.astype(jnp.bfloat16)
            attn_ref[:, c] = own_diagonal(dot(w, v_ref[:, c], 0, 0)).astype(jnp.bfloat16)
            gq_ref[:, c] = own_diagonal(dot(g, k_ref[:, c], 0, 0)).astype(jnp.bfloat16)
            gk_ref[:, c] = dot(g, q, 1, 0)
            gv_ref[:, c] = dot(w, do, 1, 0)


def near_kernel(
    prior, near_bias_ref, lead_bias_ref, q_ref, k_ref, v_ref, do_ref, near_ref, *back_refs
):
    width, half = q_ref.shape[1], prior // 2
    far = lead_bias_ref[half - 1 : half, 0:1] == 0.0
    key = lax.broadcasted_iota(jnp.int32, (prior + half, 1), 0)
    bias = jnp.where(far & (key < half), MASKED, near_bias_ref[...])
    spare = lax.broadcasted_iota(jnp.int32, (half, 1), 0) == half - 1
    early, first, second = slice(0, prior), slice(0, half), slice(half, prior)
    columns = head_columns(0, width, 2)
    queries = [side_by_side(q_ref[early, c]) for c in columns]
    cotangents = [side_by_side(do_ref[early, c]) for c in columns]
    pairs = []
    for c, q, do in zip(columns, queries, cotangents):
        k = jnp.concatenate([near_ref[first, c], k_ref[early, c]], axis=0)
        v = jnp.concatenate([near_ref[second, c], v_ref[early, c]], axis=0)
        pairs.append(score_pair(k, q, v, do, bias))
    weights, logs, deltas = softmax_columns(pairs)
    weights = [w[:half] for w in weights]
    grads = score_grads_of([(s[:half], dp[:half]) for s, dp in pairs], weights, deltas)
    k_terms = [dot(g, q, 1, 0) for g, q in zip(grads, queries)]
    v_terms = [dot(w.astype(jnp.bfloat16), do, 1, 0) for w, do in zip(weights, cotangents)]
    logs, deltas = fours(logs), fours(deltas)
    for at, c in enumerate(head_columns(0, width, 4)):
        back_ref = back_refs[c.start * len(back_refs) // width]
        low = c.start % back_ref.shape[1]
        here = slice(low, low + c.stop - c.start)
        for row, terms, ref, place in (
            (logs[at], k_terms, q_ref, first), (deltas[at], v_terms, do_ref, second)
        ):
            rows = jnp.where(spare, split_bf16(row), ref[first, c])
            terms = jnp.concatenate(terms[2 * at : 2 * at + 2], axis=1).astype(jnp.bfloat16)
            back_ref[place, here] = jnp.where(far, rows, terms)


def lead_kernel(
    prior, step, bias_ref, q_ref, k_ref, v_ref, do_ref, near_ref, far_ref, gk_part_ref, gv_part_ref,
    attn_late_ref, gq_late_ref, attn_hbm, gq_hbm, gk_hbm, gv_hbm,
    attn_ref, gq_ref, gk_ref, gv_ref, sems, late_sems,
):
    tok, width = q_ref.shape
    half = prior // 2
    early, first, second = slice(0, prior), slice(0, half), slice(half, prior)
    late = pl.ds(prior, tok - prior)
    late_copies = [
        pltpu.make_async_copy(attn_late_ref, attn_hbm.at[late, :], late_sems.at[0]),
        pltpu.make_async_copy(gq_late_ref, gq_hbm.at[late, :], late_sems.at[1]),
    ]
    for copy in late_copies:
        copy.start()

    def copies(at):
        cols = pl.ds(pl.multiple_of(at * step, step), step)
        pairs = ((attn_ref, attn_hbm), (gq_ref, gq_hbm), (gk_ref, gk_hbm), (gv_ref, gv_hbm))
        return [
            pltpu.make_async_copy(ref.at[:, cols], hbm.at[pl.ds(0, prior), cols], sems.at[at, n])
            for n, (ref, hbm) in enumerate(pairs)
        ]

    @pl.loop(0, width // step)
    def _(at):
        bias = bias_ref[...]
        columns = pair_columns(at, step)
        queries = [side_by_side(q_ref[early, c]) for c in columns]
        cotangents = [side_by_side(do_ref[early, c]) for c in columns]
        keys = [
            jnp.concatenate([far_ref[first, c], near_ref[first, c], k_ref[early, c]], axis=0)
            for c in columns
        ]
        values = [
            jnp.concatenate([far_ref[second, c], near_ref[second, c], v_ref[early, c]], axis=0)
            for c in columns
        ]
        pairs = [
            score_pair(k, q, v, do, bias)
            for k, q, v, do in zip(keys, queries, values, cotangents)
        ]
        weights, _, deltas = softmax_columns(pairs)
        grads = score_grads_of(pairs, weights, deltas)
        for n, c in enumerate(columns):
            w, g = weights[n].astype(jnp.bfloat16), grads[n]
            attn_ref[:, c] = own_diagonal(dot(w, values[n], 0, 0)).astype(jnp.bfloat16)
            gq_ref[:, c] = own_diagonal(dot(g, keys[n], 0, 0)).astype(jnp.bfloat16)
            gk = gk_part_ref[early, c] + dot(g[prior:], queries[n], 1, 0)
            gv = gv_part_ref[early, c] + dot(w[prior:], cotangents[n], 1, 0)
            gk_ref[:, c] = gk.astype(jnp.bfloat16)
            gv_ref[:, c] = gv.astype(jnp.bfloat16)
        for copy in copies(at):
            copy.start()

    for at in range(width // step):
        for copy in copies(at):
            copy.wait()
    for copy in late_copies:
        copy.wait()


def tail_half(prior, low, bias_ref, k_ref, v_ref, gk_part_ref, gv_part_ref, after_ref):
    tok, half = k_ref.shape[0], prior // 2
    far = bias_ref[half - 1 : half, 0:1] == 0.0
    bias = jnp.where(far, bias_ref[...], MASKED)
    first, second, last = slice(0, half), slice(half, prior), slice(tok - prior, tok)
    places = head_columns(0, after_ref.shape[1], 4)
    columns = head_columns(low, low + after_ref.shape[1], 4)
    queries = [side_by_side(after_ref[first, p]) for p in places]
    cotangents = [side_by_side(after_ref[second, p]) for p in places]
    pairs = [
        score_pair(k_ref[last, c], q, v_ref[last, c], do, bias)
        for c, q, do in zip(columns, queries, cotangents)
    ]
    own = [
        (joined(after_ref[half - 16 : half, p][15:]), joined(after_ref[prior - 16 : prior, p][15:]))
        for p in places
    ]
    weights, grads = merged_columns(pairs, own)

    def fill(ref, part_ref, lefts, rights, rows):
        for p, c, left, right in zip(places, columns, lefts, rights):
            total = part_ref[last, c] + dot(left, right, 1, 0)
            terms = jnp.where(far, 0.0, after_ref[rows, p].astype(jnp.float32))
            ref[first, p] = total[first].astype(jnp.bfloat16)
            ref[second, p] = (total[second] + terms).astype(jnp.bfloat16)

    return (
        lambda ref: fill(ref, gv_part_ref, weights, cotangents, second),
        lambda ref: fill(ref, gk_part_ref, grads, queries, first),
    )


def tail_kernel(prior, bias_ref, k_ref, v_ref, gk_part_ref, gv_part_ref, after_ref, gk_ref, gv_ref):
    fill_gv, fill_gk = tail_half(
        prior, 0, bias_ref, k_ref, v_ref, gk_part_ref, gv_part_ref, after_ref
    )
    fill_gv(gv_ref)
    fill_gk(gk_ref)


def last_kernel(
    prior, bias_ref, k_ref, v_ref, gk_part_ref, gv_part_ref, after_ref, gk_first_ref, gv_first_ref,
    gk_in, gv_in, gk_hbm, gv_hbm, gk_ref, gv_ref, sems,
):
    rows = pl.ds(k_ref.shape[0] - prior, prior)
    low = gk_first_ref.shape[1]
    copies = []

    def send(ref, hbm, start):
        cols = pl.ds(start, ref.shape[1])
        copies.append(pltpu.make_async_copy(ref, hbm.at[rows, cols], sems.at[len(copies)]))
        copies[-1].start()

    send(gv_first_ref, gv_hbm, 0)
    send(gk_first_ref, gk_hbm, 0)
    fill_gv, fill_gk = tail_half(
        prior, low, bias_ref, k_ref, v_ref, gk_part_ref, gv_part_ref, after_ref
    )
    fill_gv(gv_ref)
    send(gv_ref, gv_hbm, low)
    fill_gk(gk_ref)
    send(gk_ref, gk_hbm, low)
    for copy in copies:
        copy.wait()


def neighbour(value, by):
    peers = lax.axis_size("seq") * lax.axis_size("head")
    pairs = [(i, i + by) for i in range(peers) if 0 <= i + by < peers]
    return lax.ppermute(value, ("seq", "head"), pairs)


def cost(heads, queries, keys, products, moved):
    return pl.CostEstimate(
        flops=2 * heads * queries * keys * HEAD_DIM * products,
        bytes_accessed=moved,
        transcendentals=heads * queries * keys,
    )


def halo_shards(query_in, key_in, value_in, grad_out, module_lengths):
    tok, width = query_in.shape
    prior = tok * lax.axis_size("head") // 8
    step = math.gcd(width, 8 * HEAD_DIM)
    groups = width // step
    anywhere = pl.BlockSpec(memory_space=pl.ANY)
    inside = pl.BlockSpec(memory_space=pltpu.VMEM)
    full16 = jax.ShapeDtypeStruct((tok, width), jnp.bfloat16)

    def near16(rows, columns):
        return pltpu.VMEM((rows, columns), jnp.bfloat16)

    def near32(rows, columns):
        return pltpu.VMEM((rows, columns), jnp.float32)

    def in_hbm(*values):
        return [pltpu.with_memory_space_constraint(value, pltpu.HBM) for value in values]

    def in_vmem(*values):
        return [pltpu.with_memory_space_constraint(value, pltpu.VMEM) for value in values]

    def call(kernel, name, ins, outs, shapes, scratch, work, moved, aliases=None):
        return pl.pallas_call(
            kernel,
            in_specs=ins,
            out_specs=outs,
            out_shape=shapes,
            scratch_shapes=scratch,
            input_output_aliases=aliases or {},
            cost_estimate=cost(*work, moved),
            compiler_params=pltpu.CompilerParams(vmem_limit_bytes=16 * 2**20),
            name=name,
        )

    near = call(
        functools.partial(pack_kernel, prior), "near_keys",
        [anywhere] * 2, inside, near16(prior, width),
        [pltpu.SemaphoreType.DMA((2,))], (0, 0, 0, 0), 4 * prior * width,
    )(*in_hbm(key_in, value_in))
    near = neighbour(near, 1)

    lengths = module_lengths.reshape(1, -1)
    far, q, k, v, do, own_bias, near_bias, lead_bias, tail_bias = call(
        functools.partial(ready_kernel, prior), "operands",
        [anywhere] * 5, [inside] * 9,
        [near16(prior, width)] + [near16(tok, width)] * 4
        + [near32(tok, 2 * prior), near32(prior + prior // 2, 2 * prior)]
        + [near32(2 * prior, 2 * prior), near32(prior, 2 * prior)],
        [
            pltpu.VMEM(lengths.shape, jnp.int32), pltpu.SemaphoreType.DMA((4,)),
            pltpu.SemaphoreType.DMA((2,)), pltpu.SemaphoreType.DMA(()),
        ],
        (0, 0, 0, 0), 18 * tok * width,
    )(*in_hbm(lengths, query_in, key_in, value_in, grad_out))
    far = neighbour(far, 1)

    attn, gq, gk_part, gv_part = call(
        functools.partial(own_kernel, prior, step), "own_block",
        [inside] * 5, [inside] * 4,
        [near16(tok - prior, width)] * 2 + [near32(tok, width)] * 2, (),
        (width // HEAD_DIM, tok - prior, tok, 6), 18 * tok * width,
    )(*in_vmem(own_bias, q, k, v, do))

    near_bias, attn = lax.optimization_barrier((near_bias, attn))
    backs = call(
        functools.partial(near_kernel, prior), "near_terms",
        [inside] * 7, [inside] * 2, [near16(prior, width // 2)] * 2, (),
        (width // HEAD_DIM, prior, prior + prior // 2, 3), 8 * tok * width,
    )(*in_vmem(near_bias, lead_bias, q, k, v, do, near))
    backs = [neighbour(back, -1) for back in backs]

    attn, gq, gk, gv = call(
        functools.partial(lead_kernel, prior, step), "lead_rows",
        [inside] * 11, [anywhere] * 4, [full16] * 4,
        [near16(prior, width)] * 4
        + [pltpu.SemaphoreType.DMA((groups, 4)), pltpu.SemaphoreType.DMA((2,))],
        (width // HEAD_DIM, prior, 2 * prior, 6), 20 * tok * width,
    )(*in_vmem(lead_bias, q, k, v, do, near, far, gk_part, gv_part, attn, gq))

    here = in_vmem(tail_bias, k, v, gk_part, gv_part)
    work = (width // HEAD_DIM // 2, prior, prior // 2, 4)
    halves = call(
        functools.partial(tail_kernel, prior), "tail_keys",
        [inside] * 6, [inside] * 2, [near16(prior, width // 2)] * 2, (), work, 4 * tok * width,
    )(*here, *in_vmem(backs[0]))
    gk, gv = call(
        functools.partial(last_kernel, prior), "last_keys",
        [inside] * 8 + [anywhere] * 2, [anywhere] * 2, [full16] * 2,
        [near16(prior, width // 2)] * 2 + [pltpu.SemaphoreType.DMA((4,))],
        work, 6 * tok * width, {8: 0, 9: 1},
    )(*here, *in_vmem(backs[1], *halves), gk, gv)
    return (attn, gq, gk, gv)


def shards(query_in, key_in, value_in, grad_out, module_lengths):
    tok = query_in.shape[0]
    prior = tok * lax.axis_size("head") // 8
    plan = halo_shards if 2 * prior == tok else gathered_shards
    return plan(query_in, key_in, value_in, grad_out, module_lengths)


def solution(mesh):
    placed = (
        P(("seq", "head"), None),
        P(("seq", "head"), None),
        P(("seq", "head"), None),
        P(("seq", "head"), None),
        P(),
    )
    return jax.shard_map(
        shards,
        mesh=mesh,
        in_specs=placed,
        out_specs=(
            P(("seq", "head"), None),
            P(("seq", "head"), None),
            P(("seq", "head"), None),
            P(("seq", "head"), None),
        ),
        check_vma=False,
    )
```

```python
import functools
import math

import jax
import jax.numpy as jnp
from jax import lax
from jax.experimental import pallas as pl
from jax.experimental.pallas import tpu as pltpu
from jax.sharding import PartitionSpec as P

HEAD_DIM = 128
SCALE = HEAD_DIM ** (-0.5)
LOG2E = math.log2(math.e)
MASKED = -1e30


def shifted(value, axis, by):
    peers = lax.axis_size(axis)
    pairs = [(i, i + by) for i in range(peers) if 0 <= i + by < peers]
    return lax.ppermute(value, axis, pairs)


def module_ids(module_lengths, positions):
    module_ends = jnp.cumsum(module_lengths)
    counted = jnp.sum((positions[:, None] >= module_ends[None, :]).astype(jnp.int32), axis=1)
    return jnp.where(positions >= 0, counted, -1)


def allowed_pairs(module_lengths, query_pos, key_pos):
    same = (
        module_ids(module_lengths, query_pos)[:, None]
        == module_ids(module_lengths, key_pos)[None, :]
    )
    return same & (key_pos[None, :] <= query_pos[:, None])


def score_grads(grad_rows, value_block, weights, row_delta, score_scale):
    dprobs = jnp.einsum("qd,kd->qk", grad_rows, value_block, preferred_element_type=jnp.float32)
    return (weights * (dprobs - row_delta[:, None]) * score_scale).astype(jnp.bfloat16)


def key_terms(dscores, weight_bf, query_rows, grad_rows):
    key_grad = jnp.einsum("qk,qd->kd", dscores, query_rows, preferred_element_type=jnp.float32)
    value_grad = jnp.einsum("qk,qd->kd", weight_bf, grad_rows, preferred_element_type=jnp.float32)
    return (key_grad, value_grad)


def one_block(query_rows, key_block, value_block, grad_rows, allowed, score_scale):
    scores = (
        jnp.einsum("qd,kd->qk", query_rows, key_block, preferred_element_type=jnp.float32)
        * score_scale
    )
    row_top = jnp.max(jnp.where(allowed, scores, -jnp.inf), axis=1, keepdims=True)
    row_total = jnp.sum(jnp.where(allowed, jnp.exp(scores - row_top), 0.0), axis=1, keepdims=True)
    log_total = row_top + jnp.log(row_total)
    weights = jnp.where(allowed, jnp.exp(scores - log_total), 0.0)
    weight_bf = weights.astype(jnp.bfloat16)
    attn_rows = jnp.einsum(
        "qk,kd->qd", weight_bf, value_block, preferred_element_type=jnp.float32
    ).astype(jnp.bfloat16)
    row_delta = jnp.sum(grad_rows.astype(jnp.float32) * attn_rows.astype(jnp.float32), axis=1)
    dscores = score_grads(grad_rows, value_block, weights, row_delta, score_scale)
    grad_q = jnp.einsum("qk,kd->qd", dscores, key_block, preferred_element_type=jnp.float32).astype(
        jnp.bfloat16
    )
    key_grad, value_grad = key_terms(dscores, weight_bf, query_rows, grad_rows)
    return (attn_rows, grad_q, key_grad, value_grad, log_total[:, 0], row_delta)


def gathered_shards(query_in, key_in, value_in, grad_out, module_lengths):
    head_q, head_k, head_v, head_do = (
        lax.all_to_all(query_in, "head", split_axis=1, concat_axis=0, tiled=True),
        lax.all_to_all(key_in, "head", split_axis=1, concat_axis=0, tiled=True),
        lax.all_to_all(value_in, "head", split_axis=1, concat_axis=0, tiled=True),
        lax.all_to_all(grad_out, "head", split_axis=1, concat_axis=0, tiled=True),
    )
    row_count = head_q.shape[0]
    width = head_q.shape[1]
    local_heads = width // HEAD_DIM
    prior_rows = row_count // 8
    score_scale = HEAD_DIM ** (-0.5)
    tail_start = row_count - prior_rows
    prior_k, prior_v = shifted((head_k[tail_start:], head_v[tail_start:]), "seq", 1)
    row_start = lax.axis_index("seq") * row_count
    query_pos = row_start + jnp.arange(row_count, dtype=jnp.int32)
    before_pos = row_start - prior_rows + jnp.arange(prior_rows, dtype=jnp.int32)
    key_pos = jnp.concatenate([before_pos, query_pos])
    block_rows = math.gcd(row_count, 512)
    block_count = row_count // block_rows
    pos_blocks = query_pos.reshape(block_count, block_rows)

    def by_head(flat, rows):
        return jnp.moveaxis(flat.reshape(rows, local_heads, HEAD_DIM), 1, 0)

    def to_flat(stacked):
        return jnp.moveaxis(stacked, 0, 1).reshape(stacked.shape[1], width)

    query_h = by_head(head_q, row_count)
    grad_h = by_head(head_do, row_count)
    key_h = by_head(jnp.concatenate([prior_k, head_k], axis=0), row_count + prior_rows)
    value_h = by_head(jnp.concatenate([prior_v, head_v], axis=0), row_count + prior_rows)

    def run_head(packed):
        query_rows, key_block, value_block, grad_rows = packed
        query_blocks = query_rows.reshape(block_count, block_rows, HEAD_DIM)
        grad_blocks = grad_rows.reshape(block_count, block_rows, HEAD_DIM)

        def run_block(inner):
            query_part, grad_part, pos_part = inner
            allowed = allowed_pairs(module_lengths, pos_part, key_pos)
            return one_block(query_part, key_block, value_block, grad_part, allowed, score_scale)

        attn_b, grad_qb, key_b, value_b, lse_b, delta_b = lax.map(
            run_block, (query_blocks, grad_blocks, pos_blocks)
        )
        return (
            attn_b.reshape(row_count, HEAD_DIM),
            grad_qb.reshape(row_count, HEAD_DIM),
            jnp.sum(key_b, axis=0),
            jnp.sum(value_b, axis=0),
            lse_b.reshape(row_count),
            delta_b.reshape(row_count),
        )

    attn_h, grad_qh, key_grad, value_grad, log_total, row_delta = lax.map(
        run_head, (query_h, key_h, value_h, grad_h)
    )
    attn_flat = to_flat(attn_h)
    attn_back = lax.all_to_all(attn_flat, "head", split_axis=0, concat_axis=1, tiled=True)
    grad_q = to_flat(grad_qh)
    later_k, later_v = shifted((key_grad[:, :prior_rows], value_grad[:, :prior_rows]), "seq", -1)
    key_total = key_grad[:, prior_rows:].at[:, tail_start:].add(later_k)
    value_total = value_grad[:, prior_rows:].at[:, tail_start:].add(later_v)
    grad_k = to_flat(key_total.astype(jnp.bfloat16))
    grad_v = to_flat(value_total.astype(jnp.bfloat16))
    back_q, back_k, back_v = (
        lax.all_to_all(grad_q, "head", split_axis=0, concat_axis=1, tiled=True),
        lax.all_to_all(grad_k, "head", split_axis=0, concat_axis=1, tiled=True),
        lax.all_to_all(grad_v, "head", split_axis=0, concat_axis=1, tiled=True),
    )
    return (attn_back, back_q, back_k, back_v)


def dot(left, right, left_dim, right_dim):
    return lax.dot_general(
        left, right, (((left_dim,), (right_dim,)), ((), ())), preferred_element_type=jnp.float32
    )


def module_ends_col(lengths_row):
    count = lengths_row.shape[1]
    row = lax.broadcasted_iota(jnp.int32, (count, count), 0)
    col = lax.broadcasted_iota(jnp.int32, (count, count), 1)
    return jnp.sum(jnp.where(col <= row, lengths_row, 0.0), axis=1, keepdims=True)


def bias_by_key(lengths_row, first_query, queries, first_key, keys, heads):
    ends = module_ends_col(lengths_row)
    lane = lax.broadcasted_iota(jnp.int32, (1, heads * queries), 1)
    query = (first_query + lane % queries).astype(jnp.float32)
    start = jnp.max(jnp.where(ends <= query, ends, 0.0), axis=0, keepdims=True)
    key = (first_key + lax.broadcasted_iota(jnp.int32, (keys, heads * queries), 0)).astype(
        jnp.float32
    )
    return jnp.where((key >= start) & (key <= query), 0.0, MASKED)


def score_pair(k, q, v, do, bias):
    return dot(k, q, 1, 1) * (SCALE * LOG2E) + bias, dot(v, do, 1, 1)


def softmax_columns(pairs):
    tops = [jnp.max(s, axis=0, keepdims=True) for s, _ in pairs]
    raws = [jnp.exp2(s - top) for (s, _), top in zip(pairs, tops)]
    totals = [jnp.sum(raw, axis=0, keepdims=True) for raw in raws]
    weights = [raw * (1.0 / total) for raw, total in zip(raws, totals)]
    deltas = [jnp.sum(w * dp, axis=0, keepdims=True) for w, (_, dp) in zip(weights, pairs)]
    logs = [top + jnp.log2(total) for top, total in zip(tops, totals)]
    return weights, logs, deltas


def score_grads_of(pairs, weights, deltas):
    return [
        (w * (dp - delta) * SCALE).astype(jnp.bfloat16)
        for w, (_, dp), delta in zip(weights, pairs, deltas)
    ]


def merged_columns(pairs, own):
    tops = [
        jnp.maximum(jnp.max(s, axis=0, keepdims=True), log) for (s, _), (log, _) in zip(pairs, own)
    ]
    raws = [jnp.exp2(s - top) for (s, _), top in zip(pairs, tops)]
    own_raws = [jnp.exp2(log - top) for (log, _), top in zip(own, tops)]
    parts = [
        1.0 / (jnp.sum(raw, axis=0, keepdims=True) + own_raw)
        for raw, own_raw in zip(raws, own_raws)
    ]
    weights = [raw * part for raw, part in zip(raws, parts)]
    deltas = [
        jnp.sum(w * dp, axis=0, keepdims=True) + own_raw * part * own_delta
        for w, (_, dp), own_raw, part, (_, own_delta) in zip(weights, pairs, own_raws, parts, own)
    ]
    grads = [w * (dp - delta) * SCALE for w, (_, dp), delta in zip(weights, pairs, deltas)]
    return [w.astype(jnp.bfloat16) for w in weights], [g.astype(jnp.bfloat16) for g in grads]


def side_by_side(rows):
    heads = rows.shape[1] // HEAD_DIM
    zero = jnp.zeros((rows.shape[0], HEAD_DIM), rows.dtype)
    blocks = [rows[:, c] for c in head_columns(0, rows.shape[1])]
    return jnp.concatenate(
        [
            jnp.concatenate([blocks[h] if g == h else zero for g in range(heads)], axis=1)
            for h in range(heads)
        ],
        axis=0,
    )


def head_columns(low, high, heads=1):
    wide = heads * HEAD_DIM
    return [slice(c, c + wide) for c in range(low, high, wide)]


def device_first(tok):
    place = lax.axis_index("seq") * lax.axis_size("head") + lax.axis_index("head")
    return place * tok


def fours(rows):
    table = jnp.concatenate(rows, axis=0)
    half = table.shape[1] // 4
    lane = lax.broadcasted_iota(jnp.int32, (1, table.shape[1]), 1)
    turned = [pltpu.roll(table, turn * half, 1) for turn in (3, 2, 1)]
    merged = []
    for at in range(0, len(rows), 2):
        now, after = slice(at, at + 1), slice(at + 1, at + 2)
        row = jnp.where(lane < 3 * half, turned[1][after], turned[2][after])
        row = jnp.where(lane < 2 * half, turned[0][now], row)
        merged.append(jnp.where(lane < half, table[now], row))
    return merged


def split_bf16(row):
    parts = []
    for _ in range(3):
        part = row.astype(jnp.bfloat16)
        parts.append(part)
        row = row - part.astype(jnp.float32)
    return jnp.concatenate([*parts, jnp.zeros_like(parts[0])], axis=1)


def joined(parts):
    parts = parts.astype(jnp.float32)
    count = parts.shape[1] // 4
    return parts[:, :count] + parts[:, count : 2 * count] + parts[:, 2 * count : 3 * count]


def pack_copies(prior, at, low, k_ref, v_ref, packed_ref, sems):
    half, tok = prior // 2, k_ref.shape[0]
    rows, cols = pl.ds(tok - (at + 1) * half, half), pl.ds(low, packed_ref.shape[1])
    return [
        pltpu.make_async_copy(
            ref.at[rows, cols], packed_ref.at[pl.ds(n * half, half), :], sems.at[n]
        )
        for n, ref in enumerate((k_ref, v_ref))
    ]


def pack_kernel(prior, k_ref, v_ref, near_ref, sems):
    copies = pack_copies(prior, 0, 0, k_ref, v_ref, near_ref, sems)
    for copy in copies:
        copy.start()
    for copy in copies:
        copy.wait()


def ready_kernel(
    prior, len_hbm, q_hbm, k_hbm, v_hbm, do_hbm, far_ref, far_late_ref, q_ref, k_ref, v_ref, do_ref,
    own_bias_ref, near_bias_ref, lead_bias_ref, tail_bias_ref, len_ref, sems, far_sems, far_late_sems,
    len_sem,
):
    tok, half = k_ref.shape[0], prior // 2
    pairs = ((q_hbm, q_ref), (k_hbm, k_ref), (v_hbm, v_ref), (do_hbm, do_ref))
    copies = pack_copies(prior, 1, 0, k_hbm, v_hbm, far_ref, far_sems)
    copies += pack_copies(prior, 1, far_ref.shape[1], k_hbm, v_hbm, far_late_ref, far_late_sems)
    copies += [pltpu.make_async_copy(hbm, ref, sems.at[n]) for n, (hbm, ref) in enumerate(pairs)]
    len_copy = pltpu.make_async_copy(len_hbm, len_ref, len_sem)
    len_copy.start()
    for copy in copies:
        copy.start()
    len_copy.wait()
    first = device_first(tok)
    lengths = len_ref[...].astype(jnp.float32)
    own_bias_ref[...] = bias_by_key(lengths, first + prior, tok - prior, first, tok, 2)
    near_bias_ref[...] = bias_by_key(lengths, first, prior, first - half, prior + half, 2)
    lead_bias_ref[...] = bias_by_key(lengths, first, prior, first - prior, 2 * prior, 2)
    tail_bias_ref[...] = bias_by_key(lengths, first + tok, half, first + tok - prior, prior, 4)
    for copy in copies:
        copy.wait()


def own_diagonal(both):
    rows = both.shape[0] // 2
    return jnp.concatenate([both[:rows, :HEAD_DIM], both[rows:, HEAD_DIM:]], axis=1)


def pair_columns(at, step):
    wide = 2 * HEAD_DIM
    return [pl.ds(pl.multiple_of(at * step + c, wide), wide) for c in range(0, step, wide)]


def own_kernel(
    prior, step, bias_ref, q_ref, k_ref, v_ref, do_ref, attn_ref, gq_ref, gk_ref, gv_ref
):
    tok, width = k_ref.shape
    late = slice(prior, tok)

    @pl.loop(0, width // step)
    def _(at):
        bias = bias_ref[...]
        columns = pair_columns(at, step)
        queries = [side_by_side(q_ref[late, c]) for c in columns]
        cotangents = [side_by_side(do_ref[late, c]) for c in columns]
        pairs = [
            score_pair(k_ref[:, c], q, v_ref[:, c], do, bias)
            for c, q, do in zip(columns, queries, cotangents)
        ]
        weights, _, deltas = softmax_columns(pairs)
        grads = score_grads_of(pairs, weights, deltas)
        for c, w, g, q, do in zip(columns, weights, grads, queries, cotangents):
            w = w.astype(jnp.bfloat16)
            attn_ref[:, c] = own_diagonal(dot(w, v_ref[:, c], 0, 0)).astype(jnp.bfloat16)
            gq_ref[:, c] = own_diagonal(dot(g, k_ref[:, c], 0, 0)).astype(jnp.bfloat16)
            gk_ref[:, c] = dot(g, q, 1, 0)
            gv_ref[:, c] = dot(w, do, 1, 0)


def near_kernel(
    prior, near_bias_ref, lead_bias_ref, q_ref, k_ref, v_ref, do_ref, near_ref, *back_refs
):
    width, half = q_ref.shape[1], prior // 2
    far = lead_bias_ref[half - 1 : half, 0:1] == 0.0
    key = lax.broadcasted_iota(jnp.int32, (prior + half, 1), 0)
    bias = jnp.where(far & (key < half), MASKED, near_bias_ref[...])
    spare = lax.broadcasted_iota(jnp.int32, (half, 1), 0) == half - 1
    early, first, second = slice(0, prior), slice(0, half), slice(half, prior)
    columns = head_columns(0, width, 2)
    queries = [side_by_side(q_ref[early, c]) for c in columns]
    cotangents = [side_by_side(do_ref[early, c]) for c in columns]
    pairs = []
    for c, q, do in zip(columns, queries, cotangents):
        k = jnp.concatenate([near_ref[first, c], k_ref[early, c]], axis=0)
        v = jnp.concatenate([near_ref[second, c], v_ref[early, c]], axis=0)
        pairs.append(score_pair(k, q, v, do, bias))
    weights, logs, deltas = softmax_columns(pairs)
    weights = [w[:half] for w in weights]
    grads = score_grads_of([(s[:half], dp[:half]) for s, dp in pairs], weights, deltas)
    k_terms = [dot(g, q, 1, 0) for g, q in zip(grads, queries)]
    v_terms = [dot(w.astype(jnp.bfloat16), do, 1, 0) for w, do in zip(weights, cotangents)]
    logs, deltas = fours(logs), fours(deltas)
    for at, c in enumerate(head_columns(0, width, 4)):
        back_ref = back_refs[c.start * len(back_refs) // width]
        low = c.start % back_ref.shape[1]
        here = slice(low, low + c.stop - c.start)
        for row, terms, ref, place in (
            (logs[at], k_terms, q_ref, first), (deltas[at], v_terms, do_ref, second)
        ):
            rows = jnp.where(spare, split_bf16(row), ref[first, c])
            terms = jnp.concatenate(terms[2 * at : 2 * at + 2], axis=1).astype(jnp.bfloat16)
            back_ref[place, here] = jnp.where(far, rows, terms)


def lead_kernel(
    prior, bias_ref, q_ref, k_ref, v_ref, do_ref, near_ref, far_ref, far_late_ref,
    gk_part_ref, gv_part_ref, attn_late_ref, gq_late_ref, attn_hbm, gq_hbm, gk_hbm, gv_hbm,
    attn_ref, gq_ref, gk_ref, gv_ref, sems, late_sems,
):
    tok, width = q_ref.shape
    half = prior // 2
    early, first, second = slice(0, prior), slice(0, half), slice(half, prior)
    late = pl.ds(prior, tok - prior)
    late_copies = [
        pltpu.make_async_copy(attn_late_ref, attn_hbm.at[late, :], late_sems.at[0]),
        pltpu.make_async_copy(gq_late_ref, gq_hbm.at[late, :], late_sems.at[1]),
    ]
    for copy in late_copies:
        copy.start()

    step = far_ref.shape[1]

    def copies(at):
        cols = pl.ds(at * step, step)
        pairs = ((attn_ref, attn_hbm), (gq_ref, gq_hbm), (gk_ref, gk_hbm), (gv_ref, gv_hbm))
        return [
            pltpu.make_async_copy(ref.at[:, cols], hbm.at[pl.ds(0, prior), cols], sems.at[at, n])
            for n, (ref, hbm) in enumerate(pairs)
        ]

    bias = bias_ref[...]
    for at, far_part_ref in enumerate((far_ref, far_late_ref)):
        columns = head_columns(at * step, (at + 1) * step, 2)
        places = head_columns(0, step, 2)
        queries = [side_by_side(q_ref[early, c]) for c in columns]
        cotangents = [side_by_side(do_ref[early, c]) for c in columns]
        keys = [
            jnp.concatenate([far_part_ref[first, p], near_ref[first, c], k_ref[early, c]], axis=0)
            for p, c in zip(places, columns)
        ]
        values = [
            jnp.concatenate([far_part_ref[second, p], near_ref[second, c], v_ref[early, c]], axis=0)
            for p, c in zip(places, columns)
        ]
        pairs = [
            score_pair(k, q, v, do, bias)
            for k, q, v, do in zip(keys, queries, values, cotangents)
        ]
        weights, _, deltas = softmax_columns(pairs)
        grads = score_grads_of(pairs, weights, deltas)
        for n, c in enumerate(columns):
            w, g = weights[n].astype(jnp.bfloat16), grads[n]
            attn_ref[:, c] = own_diagonal(dot(w, values[n], 0, 0)).astype(jnp.bfloat16)
            gq_ref[:, c] = own_diagonal(dot(g, keys[n], 0, 0)).astype(jnp.bfloat16)
            gk = gk_part_ref[early, c] + dot(g[prior:], queries[n], 1, 0)
            gv = gv_part_ref[early, c] + dot(w[prior:], cotangents[n], 1, 0)
            gk_ref[:, c] = gk.astype(jnp.bfloat16)
            gv_ref[:, c] = gv.astype(jnp.bfloat16)
        for copy in copies(at):
            copy.start()

    for at in range(2):
        for copy in copies(at):
            copy.wait()
    for copy in late_copies:
        copy.wait()


def tail_half(prior, low, bias_ref, k_ref, v_ref, gk_part_ref, gv_part_ref, after_ref):
    tok, half = k_ref.shape[0], prior // 2
    far = bias_ref[half - 1 : half, 0:1] == 0.0
    bias = jnp.where(far, bias_ref[...], MASKED)
    first, second, last = slice(0, half), slice(half, prior), slice(tok - prior, tok)
    places = head_columns(0, after_ref.shape[1], 4)
    columns = head_columns(low, low + after_ref.shape[1], 4)
    queries = [side_by_side(after_ref[first, p]) for p in places]
    cotangents = [side_by_side(after_ref[second, p]) for p in places]
    pairs = [
        score_pair(k_ref[last, c], q, v_ref[last, c], do, bias)
        for c, q, do in zip(columns, queries, cotangents)
    ]
    own = [
        (joined(after_ref[half - 16 : half, p][15:]), joined(after_ref[prior - 16 : prior, p][15:]))
        for p in places
    ]
    weights, grads = merged_columns(pairs, own)

    def fill(ref, part_ref, lefts, rights, rows):
        for p, c, left, right in zip(places, columns, lefts, rights):
            total = part_ref[last, c] + dot(left, right, 1, 0)
            terms = jnp.where(far, 0.0, after_ref[rows, p].astype(jnp.float32))
            ref[first, p] = total[first].astype(jnp.bfloat16)
            ref[second, p] = (total[second] + terms).astype(jnp.bfloat16)

    return (
        lambda ref: fill(ref, gv_part_ref, weights, cotangents, second),
        lambda ref: fill(ref, gk_part_ref, grads, queries, first),
    )


def tail_kernel(prior, bias_ref, k_ref, v_ref, gk_part_ref, gv_part_ref, after_ref, gk_ref, gv_ref):
    fill_gv, fill_gk = tail_half(
        prior, 0, bias_ref, k_ref, v_ref, gk_part_ref, gv_part_ref, after_ref
    )
    fill_gv(gv_ref)
    fill_gk(gk_ref)


def last_kernel(
    prior, bias_ref, k_ref, v_ref, gk_part_ref, gv_part_ref, after_ref, gk_first_ref, gv_first_ref,
    gk_in, gv_in, gk_hbm, gv_hbm, gk_ref, gv_ref, sems,
):
    rows = pl.ds(k_ref.shape[0] - prior, prior)
    low = gk_first_ref.shape[1]
    copies = []

    def send(ref, hbm, start):
        cols = pl.ds(start, ref.shape[1])
        copies.append(pltpu.make_async_copy(ref, hbm.at[rows, cols], sems.at[len(copies)]))
        copies[-1].start()

    send(gv_first_ref, gv_hbm, 0)
    send(gk_first_ref, gk_hbm, 0)
    fill_gv, fill_gk = tail_half(
        prior, low, bias_ref, k_ref, v_ref, gk_part_ref, gv_part_ref, after_ref
    )
    fill_gv(gv_ref)
    send(gv_ref, gv_hbm, low)
    fill_gk(gk_ref)
    send(gk_ref, gk_hbm, low)
    for copy in copies:
        copy.wait()


def neighbour(value, by):
    peers = lax.axis_size("seq") * lax.axis_size("head")
    pairs = [(i, i + by) for i in range(peers) if 0 <= i + by < peers]
    return lax.ppermute(value, ("seq", "head"), pairs)


def cost(heads, queries, keys, products, moved):
    return pl.CostEstimate(
        flops=2 * heads * queries * keys * HEAD_DIM * products,
        bytes_accessed=moved,
        transcendentals=heads * queries * keys,
    )


def halo_shards(query_in, key_in, value_in, grad_out, module_lengths):
    tok, width = query_in.shape
    prior = tok * lax.axis_size("head") // 8
    step = math.gcd(width, 8 * HEAD_DIM)
    anywhere = pl.BlockSpec(memory_space=pl.ANY)
    inside = pl.BlockSpec(memory_space=pltpu.VMEM)
    full16 = jax.ShapeDtypeStruct((tok, width), jnp.bfloat16)

    def near16(rows, columns):
        return pltpu.VMEM((rows, columns), jnp.bfloat16)

    def near32(rows, columns):
        return pltpu.VMEM((rows, columns), jnp.float32)

    def in_hbm(*values):
        return [pltpu.with_memory_space_constraint(value, pltpu.HBM) for value in values]

    def in_vmem(*values):
        return [pltpu.with_memory_space_constraint(value, pltpu.VMEM) for value in values]

    def call(kernel, name, ins, outs, shapes, scratch, work, moved, aliases=None):
        return pl.pallas_call(
            kernel,
            in_specs=ins,
            out_specs=outs,
            out_shape=shapes,
            scratch_shapes=scratch,
            input_output_aliases=aliases or {},
            cost_estimate=cost(*work, moved),
            compiler_params=pltpu.CompilerParams(vmem_limit_bytes=16 * 2**20),
            name=name,
        )

    near = call(
        functools.partial(pack_kernel, prior), "near_keys",
        [anywhere] * 2, inside, near16(prior, width),
        [pltpu.SemaphoreType.DMA((2,))], (0, 0, 0, 0), 4 * prior * width,
    )(*in_hbm(key_in, value_in))
    near = neighbour(near, 1)

    lengths = module_lengths.reshape(1, -1)
    far, far_late, q, k, v, do, own_bias, near_bias, lead_bias, tail_bias = call(
        functools.partial(ready_kernel, prior), "operands",
        [anywhere] * 5, [inside] * 10,
        [near16(prior, width // 2)] * 2 + [near16(tok, width)] * 4
        + [near32(tok, 2 * prior), near32(prior + prior // 2, 2 * prior)]
        + [near32(2 * prior, 2 * prior), near32(prior, 2 * prior)],
        [
            pltpu.VMEM(lengths.shape, jnp.int32), pltpu.SemaphoreType.DMA((4,)),
            pltpu.SemaphoreType.DMA((2,)), pltpu.SemaphoreType.DMA((2,)),
            pltpu.SemaphoreType.DMA(()),
        ],
        (0, 0, 0, 0), 18 * tok * width,
    )(*in_hbm(lengths, query_in, key_in, value_in, grad_out))
    far = neighbour(far, 1)

    attn, gq, gk_part, gv_part = call(
        functools.partial(own_kernel, prior, step), "own_block",
        [inside] * 5, [inside] * 4,
        [near16(tok - prior, width)] * 2 + [near32(tok, width)] * 2, (),
        (width // HEAD_DIM, tok - prior, tok, 6), 18 * tok * width,
    )(*in_vmem(own_bias, q, k, v, do))

    far_late, near_bias, attn = lax.optimization_barrier((far_late, near_bias, attn))
    far_late = neighbour(far_late, 1)

    backs = call(
        functools.partial(near_kernel, prior), "near_terms",
        [inside] * 7, [inside] * 2, [near16(prior, width // 2)] * 2, (),
        (width // HEAD_DIM, prior, prior + prior // 2, 3), 8 * tok * width,
    )(*in_vmem(near_bias, lead_bias, q, k, v, do, near))
    backs = [neighbour(back, -1) for back in backs]

    attn, gq, gk, gv = call(
        functools.partial(lead_kernel, prior), "lead_rows",
        [inside] * 12, [anywhere] * 4, [full16] * 4,
        [near16(prior, width)] * 4
        + [pltpu.SemaphoreType.DMA((2, 4)), pltpu.SemaphoreType.DMA((2,))],
        (width // HEAD_DIM, prior, 2 * prior, 6), 20 * tok * width,
    )(*in_vmem(lead_bias, q, k, v, do, near, far, far_late, gk_part, gv_part, attn, gq))

    here = in_vmem(tail_bias, k, v, gk_part, gv_part)
    work = (width // HEAD_DIM // 2, prior, prior // 2, 4)
    halves = call(
        functools.partial(tail_kernel, prior), "tail_keys",
        [inside] * 6, [inside] * 2, [near16(prior, width // 2)] * 2, (), work, 4 * tok * width,
    )(*here, *in_vmem(backs[0]))
    gk, gv = call(
        functools.partial(last_kernel, prior), "last_keys",
        [inside] * 8 + [anywhere] * 2, [anywhere] * 2, [full16] * 2,
        [near16(prior, width // 2)] * 2 + [pltpu.SemaphoreType.DMA((4,))],
        work, 6 * tok * width, {8: 0, 9: 1},
    )(*here, *in_vmem(backs[1], *halves), gk, gv)
    return (attn, gq, gk, gv)


def shards(query_in, key_in, value_in, grad_out, module_lengths):
    tok = query_in.shape[0]
    prior = tok * lax.axis_size("head") // 8
    plan = halo_shards if 2 * prior == tok else gathered_shards
    return plan(query_in, key_in, value_in, grad_out, module_lengths)


def solution(mesh):
    placed = (
        P(("seq", "head"), None),
        P(("seq", "head"), None),
        P(("seq", "head"), None),
        P(("seq", "head"), None),
        P(),
    )
    return jax.shard_map(
        shards,
        mesh=mesh,
        in_specs=placed,
        out_specs=(
            P(("seq", "head"), None),
            P(("seq", "head"), None),
            P(("seq", "head"), None),
            P(("seq", "head"), None),
        ),
        check_vma=False,
    )
```

```python
import functools
import math

import jax
import jax.numpy as jnp
from jax import lax
from jax.experimental import pallas as pl
from jax.experimental.pallas import tpu as pltpu
from jax.sharding import PartitionSpec as P

HEAD_DIM = 128
SCALE = HEAD_DIM ** (-0.5)
LOG2E = math.log2(math.e)
MASKED = -1e30


def shifted(value, axis, by):
    peers = lax.axis_size(axis)
    pairs = [(i, i + by) for i in range(peers) if 0 <= i + by < peers]
    return lax.ppermute(value, axis, pairs)


def module_ids(module_lengths, positions):
    module_ends = jnp.cumsum(module_lengths)
    counted = jnp.sum((positions[:, None] >= module_ends[None, :]).astype(jnp.int32), axis=1)
    return jnp.where(positions >= 0, counted, -1)


def allowed_pairs(module_lengths, query_pos, key_pos):
    same = (
        module_ids(module_lengths, query_pos)[:, None]
        == module_ids(module_lengths, key_pos)[None, :]
    )
    return same & (key_pos[None, :] <= query_pos[:, None])


def score_grads(grad_rows, value_block, weights, row_delta, score_scale):
    dprobs = jnp.einsum("qd,kd->qk", grad_rows, value_block, preferred_element_type=jnp.float32)
    return (weights * (dprobs - row_delta[:, None]) * score_scale).astype(jnp.bfloat16)


def key_terms(dscores, weight_bf, query_rows, grad_rows):
    key_grad = jnp.einsum("qk,qd->kd", dscores, query_rows, preferred_element_type=jnp.float32)
    value_grad = jnp.einsum("qk,qd->kd", weight_bf, grad_rows, preferred_element_type=jnp.float32)
    return (key_grad, value_grad)


def one_block(query_rows, key_block, value_block, grad_rows, allowed, score_scale):
    scores = (
        jnp.einsum("qd,kd->qk", query_rows, key_block, preferred_element_type=jnp.float32)
        * score_scale
    )
    row_top = jnp.max(jnp.where(allowed, scores, -jnp.inf), axis=1, keepdims=True)
    row_total = jnp.sum(jnp.where(allowed, jnp.exp(scores - row_top), 0.0), axis=1, keepdims=True)
    log_total = row_top + jnp.log(row_total)
    weights = jnp.where(allowed, jnp.exp(scores - log_total), 0.0)
    weight_bf = weights.astype(jnp.bfloat16)
    attn_rows = jnp.einsum(
        "qk,kd->qd", weight_bf, value_block, preferred_element_type=jnp.float32
    ).astype(jnp.bfloat16)
    row_delta = jnp.sum(grad_rows.astype(jnp.float32) * attn_rows.astype(jnp.float32), axis=1)
    dscores = score_grads(grad_rows, value_block, weights, row_delta, score_scale)
    grad_q = jnp.einsum("qk,kd->qd", dscores, key_block, preferred_element_type=jnp.float32).astype(
        jnp.bfloat16
    )
    key_grad, value_grad = key_terms(dscores, weight_bf, query_rows, grad_rows)
    return (attn_rows, grad_q, key_grad, value_grad, log_total[:, 0], row_delta)


def gathered_shards(query_in, key_in, value_in, grad_out, module_lengths):
    head_q, head_k, head_v, head_do = (
        lax.all_to_all(query_in, "head", split_axis=1, concat_axis=0, tiled=True),
        lax.all_to_all(key_in, "head", split_axis=1, concat_axis=0, tiled=True),
        lax.all_to_all(value_in, "head", split_axis=1, concat_axis=0, tiled=True),
        lax.all_to_all(grad_out, "head", split_axis=1, concat_axis=0, tiled=True),
    )
    row_count = head_q.shape[0]
    width = head_q.shape[1]
    local_heads = width // HEAD_DIM
    prior_rows = row_count // 8
    score_scale = HEAD_DIM ** (-0.5)
    tail_start = row_count - prior_rows
    prior_k, prior_v = shifted((head_k[tail_start:], head_v[tail_start:]), "seq", 1)
    row_start = lax.axis_index("seq") * row_count
    query_pos = row_start + jnp.arange(row_count, dtype=jnp.int32)
    before_pos = row_start - prior_rows + jnp.arange(prior_rows, dtype=jnp.int32)
    key_pos = jnp.concatenate([before_pos, query_pos])
    block_rows = math.gcd(row_count, 512)
    block_count = row_count // block_rows
    pos_blocks = query_pos.reshape(block_count, block_rows)

    def by_head(flat, rows):
        return jnp.moveaxis(flat.reshape(rows, local_heads, HEAD_DIM), 1, 0)

    def to_flat(stacked):
        return jnp.moveaxis(stacked, 0, 1).reshape(stacked.shape[1], width)

    query_h = by_head(head_q, row_count)
    grad_h = by_head(head_do, row_count)
    key_h = by_head(jnp.concatenate([prior_k, head_k], axis=0), row_count + prior_rows)
    value_h = by_head(jnp.concatenate([prior_v, head_v], axis=0), row_count + prior_rows)

    def run_head(packed):
        query_rows, key_block, value_block, grad_rows = packed
        query_blocks = query_rows.reshape(block_count, block_rows, HEAD_DIM)
        grad_blocks = grad_rows.reshape(block_count, block_rows, HEAD_DIM)

        def run_block(inner):
            query_part, grad_part, pos_part = inner
            allowed = allowed_pairs(module_lengths, pos_part, key_pos)
            return one_block(query_part, key_block, value_block, grad_part, allowed, score_scale)

        attn_b, grad_qb, key_b, value_b, lse_b, delta_b = lax.map(
            run_block, (query_blocks, grad_blocks, pos_blocks)
        )
        return (
            attn_b.reshape(row_count, HEAD_DIM),
            grad_qb.reshape(row_count, HEAD_DIM),
            jnp.sum(key_b, axis=0),
            jnp.sum(value_b, axis=0),
            lse_b.reshape(row_count),
            delta_b.reshape(row_count),
        )

    attn_h, grad_qh, key_grad, value_grad, log_total, row_delta = lax.map(
        run_head, (query_h, key_h, value_h, grad_h)
    )
    attn_flat = to_flat(attn_h)
    attn_back = lax.all_to_all(attn_flat, "head", split_axis=0, concat_axis=1, tiled=True)
    grad_q = to_flat(grad_qh)
    later_k, later_v = shifted((key_grad[:, :prior_rows], value_grad[:, :prior_rows]), "seq", -1)
    key_total = key_grad[:, prior_rows:].at[:, tail_start:].add(later_k)
    value_total = value_grad[:, prior_rows:].at[:, tail_start:].add(later_v)
    grad_k = to_flat(key_total.astype(jnp.bfloat16))
    grad_v = to_flat(value_total.astype(jnp.bfloat16))
    back_q, back_k, back_v = (
        lax.all_to_all(grad_q, "head", split_axis=0, concat_axis=1, tiled=True),
        lax.all_to_all(grad_k, "head", split_axis=0, concat_axis=1, tiled=True),
        lax.all_to_all(grad_v, "head", split_axis=0, concat_axis=1, tiled=True),
    )
    return (attn_back, back_q, back_k, back_v)


def dot(left, right, left_dim, right_dim):
    return lax.dot_general(
        left, right, (((left_dim,), (right_dim,)), ((), ())), preferred_element_type=jnp.float32
    )


def module_ends_col(lengths_row):
    count = lengths_row.shape[1]
    row = lax.broadcasted_iota(jnp.int32, (count, count), 0)
    col = lax.broadcasted_iota(jnp.int32, (count, count), 1)
    return jnp.sum(jnp.where(col <= row, lengths_row, 0.0), axis=1, keepdims=True)


def bias_by_key(lengths_row, first_query, queries, first_key, keys, heads):
    ends = module_ends_col(lengths_row)
    lane = lax.broadcasted_iota(jnp.int32, (1, heads * queries), 1)
    query = (first_query + lane % queries).astype(jnp.float32)
    start = jnp.max(jnp.where(ends <= query, ends, 0.0), axis=0, keepdims=True)
    key = (first_key + lax.broadcasted_iota(jnp.int32, (keys, heads * queries), 0)).astype(
        jnp.float32
    )
    return jnp.where((key >= start) & (key <= query), 0.0, MASKED)


def score_pair(k, q, v, do, bias):
    return dot(k, q, 1, 1) * (SCALE * LOG2E) + bias, dot(v, do, 1, 1)


def softmax_columns(pairs):
    tops = [jnp.max(s, axis=0, keepdims=True) for s, _ in pairs]
    raws = [jnp.exp2(s - top) for (s, _), top in zip(pairs, tops)]
    totals = [jnp.sum(raw, axis=0, keepdims=True) for raw in raws]
    weights = [raw * (1.0 / total) for raw, total in zip(raws, totals)]
    deltas = [jnp.sum(w * dp, axis=0, keepdims=True) for w, (_, dp) in zip(weights, pairs)]
    logs = [top + jnp.log2(total) for top, total in zip(tops, totals)]
    return weights, logs, deltas


def score_grads_of(pairs, weights, deltas):
    return [
        (w * (dp - delta) * SCALE).astype(jnp.bfloat16)
        for w, (_, dp), delta in zip(weights, pairs, deltas)
    ]


def merged_columns(pairs, own):
    tops = [
        jnp.maximum(jnp.max(s, axis=0, keepdims=True), log) for (s, _), (log, _) in zip(pairs, own)
    ]
    raws = [jnp.exp2(s - top) for (s, _), top in zip(pairs, tops)]
    own_raws = [jnp.exp2(log - top) for (log, _), top in zip(own, tops)]
    parts = [
        1.0 / (jnp.sum(raw, axis=0, keepdims=True) + own_raw)
        for raw, own_raw in zip(raws, own_raws)
    ]
    weights = [raw * part for raw, part in zip(raws, parts)]
    deltas = [
        jnp.sum(w * dp, axis=0, keepdims=True) + own_raw * part * own_delta
        for w, (_, dp), own_raw, part, (_, own_delta) in zip(weights, pairs, own_raws, parts, own)
    ]
    grads = [w * (dp - delta) * SCALE for w, (_, dp), delta in zip(weights, pairs, deltas)]
    return [w.astype(jnp.bfloat16) for w in weights], [g.astype(jnp.bfloat16) for g in grads]


def side_by_side(rows):
    heads = rows.shape[1] // HEAD_DIM
    zero = jnp.zeros((rows.shape[0], HEAD_DIM), rows.dtype)
    blocks = [rows[:, c] for c in head_columns(0, rows.shape[1])]
    return jnp.concatenate(
        [
            jnp.concatenate([blocks[h] if g == h else zero for g in range(heads)], axis=1)
            for h in range(heads)
        ],
        axis=0,
    )


def head_columns(low, high, heads=1):
    wide = heads * HEAD_DIM
    return [slice(c, c + wide) for c in range(low, high, wide)]


def device_first(tok):
    place = lax.axis_index("seq") * lax.axis_size("head") + lax.axis_index("head")
    return place * tok


def fours(rows):
    table = jnp.concatenate(rows, axis=0)
    half = table.shape[1] // 4
    lane = lax.broadcasted_iota(jnp.int32, (1, table.shape[1]), 1)
    turned = [pltpu.roll(table, turn * half, 1) for turn in (3, 2, 1)]
    merged = []
    for at in range(0, len(rows), 2):
        now, after = slice(at, at + 1), slice(at + 1, at + 2)
        row = jnp.where(lane < 3 * half, turned[1][after], turned[2][after])
        row = jnp.where(lane < 2 * half, turned[0][now], row)
        merged.append(jnp.where(lane < half, table[now], row))
    return merged


def split_bf16(row):
    parts = []
    for _ in range(3):
        part = row.astype(jnp.bfloat16)
        parts.append(part)
        row = row - part.astype(jnp.float32)
    return jnp.concatenate([*parts, jnp.zeros_like(parts[0])], axis=1)


def joined(parts):
    parts = parts.astype(jnp.float32)
    count = parts.shape[1] // 4
    return parts[:, :count] + parts[:, count : 2 * count] + parts[:, 2 * count : 3 * count]


def pack_copies(prior, at, k_ref, v_ref, packed_ref, sems):
    half, tok = prior // 2, k_ref.shape[0]
    rows = pl.ds(tok - (at + 1) * half, half)
    return [
        pltpu.make_async_copy(
            ref.at[rows, :], packed_ref.at[pl.ds(n * half, half), :], sems.at[n]
        )
        for n, ref in enumerate((k_ref, v_ref))
    ]


def pack_kernel(prior, k_ref, v_ref, near_ref, sems):
    copies = pack_copies(prior, 0, k_ref, v_ref, near_ref, sems)
    for copy in copies:
        copy.start()
    for copy in copies:
        copy.wait()


def ready_kernel(
    prior, len_hbm, q_hbm, k_hbm, v_hbm, do_hbm, far_ref, q_ref, k_ref, v_ref, do_ref,
    own_bias_ref, near_bias_ref, lead_bias_ref, tail_bias_ref, len_ref, sems, far_sems, len_sem,
):
    tok, half = k_ref.shape[0], prior // 2
    pairs = ((q_hbm, q_ref), (k_hbm, k_ref), (v_hbm, v_ref), (do_hbm, do_ref))
    copies = pack_copies(prior, 1, k_hbm, v_hbm, far_ref, far_sems)
    copies += [pltpu.make_async_copy(hbm, ref, sems.at[n]) for n, (hbm, ref) in enumerate(pairs)]
    len_copy = pltpu.make_async_copy(len_hbm, len_ref, len_sem)
    len_copy.start()
    for copy in copies:
        copy.start()
    len_copy.wait()
    first = device_first(tok)
    lengths = len_ref[...].astype(jnp.float32)
    own_bias_ref[...] = bias_by_key(lengths, first + prior, tok - prior, first, tok, 2)
    near_bias_ref[...] = bias_by_key(lengths, first, prior, first - half, prior + half, 2)
    lead_bias_ref[...] = bias_by_key(lengths, first, prior, first - prior, 2 * prior, 2)
    tail_bias_ref[...] = bias_by_key(lengths, first + tok, half, first + tok - prior, prior, 4)
    for copy in copies:
        copy.wait()


def own_diagonal(both):
    rows = both.shape[0] // 2
    return jnp.concatenate([both[:rows, :HEAD_DIM], both[rows:, HEAD_DIM:]], axis=1)


def pair_columns(at, step):
    wide = 2 * HEAD_DIM
    return [pl.ds(pl.multiple_of(at * step + c, wide), wide) for c in range(0, step, wide)]


def own_kernel(prior, step, odd, bias_ref, q_ref, k_ref, v_ref, do_ref, *refs):
    attn_ref, gq_ref, gk_ref, gv_ref = refs[-4:]
    tok, width = k_ref.shape
    late = slice(prior, tok)

    @pl.when(lax.axis_index("seq") % 2 == odd)
    def _():
        @pl.loop(0, width // step)
        def _(at):
            bias = bias_ref[...]
            columns = pair_columns(at, step)
            queries = [side_by_side(q_ref[late, c]) for c in columns]
            cotangents = [side_by_side(do_ref[late, c]) for c in columns]
            pairs = [
                score_pair(k_ref[:, c], q, v_ref[:, c], do, bias)
                for c, q, do in zip(columns, queries, cotangents)
            ]
            weights, _, deltas = softmax_columns(pairs)
            grads = score_grads_of(pairs, weights, deltas)
            for c, w, g, q, do in zip(columns, weights, grads, queries, cotangents):
                w = w.astype(jnp.bfloat16)
                attn_ref[:, c] = own_diagonal(dot(w, v_ref[:, c], 0, 0)).astype(jnp.bfloat16)
                gq_ref[:, c] = own_diagonal(dot(g, k_ref[:, c], 0, 0)).astype(jnp.bfloat16)
                gk_ref[:, c] = dot(g, q, 1, 0)
                gv_ref[:, c] = dot(w, do, 1, 0)


def near_kernel(
    prior, near_bias_ref, lead_bias_ref, q_ref, k_ref, v_ref, do_ref, near_ref, *back_refs
):
    width, half = q_ref.shape[1], prior // 2
    far = lead_bias_ref[half - 1 : half, 0:1] == 0.0
    key = lax.broadcasted_iota(jnp.int32, (prior + half, 1), 0)
    bias = jnp.where(far & (key < half), MASKED, near_bias_ref[...])
    spare = lax.broadcasted_iota(jnp.int32, (half, 1), 0) == half - 1
    early, first, second = slice(0, prior), slice(0, half), slice(half, prior)
    columns = head_columns(0, width, 2)
    queries = [side_by_side(q_ref[early, c]) for c in columns]
    cotangents = [side_by_side(do_ref[early, c]) for c in columns]
    pairs = []
    for c, q, do in zip(columns, queries, cotangents):
        k = jnp.concatenate([near_ref[first, c], k_ref[early, c]], axis=0)
        v = jnp.concatenate([near_ref[second, c], v_ref[early, c]], axis=0)
        pairs.append(score_pair(k, q, v, do, bias))
    weights, logs, deltas = softmax_columns(pairs)
    weights = [w[:half] for w in weights]
    grads = score_grads_of([(s[:half], dp[:half]) for s, dp in pairs], weights, deltas)
    k_terms = [dot(g, q, 1, 0) for g, q in zip(grads, queries)]
    v_terms = [dot(w.astype(jnp.bfloat16), do, 1, 0) for w, do in zip(weights, cotangents)]
    logs, deltas = fours(logs), fours(deltas)
    for at, c in enumerate(head_columns(0, width, 4)):
        back_ref = back_refs[c.start * len(back_refs) // width]
        low = c.start % back_ref.shape[1]
        here = slice(low, low + c.stop - c.start)
        for row, terms, ref, place in (
            (logs[at], k_terms, q_ref, first), (deltas[at], v_terms, do_ref, second)
        ):
            rows = jnp.where(spare, split_bf16(row), ref[first, c])
            terms = jnp.concatenate(terms[2 * at : 2 * at + 2], axis=1).astype(jnp.bfloat16)
            back_ref[place, here] = jnp.where(far, rows, terms)


def lead_kernel(
    prior, step, bias_ref, q_ref, k_ref, v_ref, do_ref, near_ref, far_ref, gk_part_ref, gv_part_ref,
    attn_late_ref, gq_late_ref, attn_hbm, gq_hbm, gk_hbm, gv_hbm,
    attn_ref, gq_ref, gk_ref, gv_ref, sems, late_sems,
):
    tok, width = q_ref.shape
    half = prior // 2
    early, first, second = slice(0, prior), slice(0, half), slice(half, prior)
    late = pl.ds(prior, tok - prior)
    late_copies = [
        pltpu.make_async_copy(attn_late_ref, attn_hbm.at[late, :], late_sems.at[0]),
        pltpu.make_async_copy(gq_late_ref, gq_hbm.at[late, :], late_sems.at[1]),
    ]
    for copy in late_copies:
        copy.start()

    def copies(at):
        cols = pl.ds(pl.multiple_of(at * step, step), step)
        pairs = ((attn_ref, attn_hbm), (gq_ref, gq_hbm), (gk_ref, gk_hbm), (gv_ref, gv_hbm))
        return [
            pltpu.make_async_copy(ref.at[:, cols], hbm.at[pl.ds(0, prior), cols], sems.at[at, n])
            for n, (ref, hbm) in enumerate(pairs)
        ]

    @pl.loop(0, width // step)
    def _(at):
        bias = bias_ref[...]
        columns = pair_columns(at, step)
        queries = [side_by_side(q_ref[early, c]) for c in columns]
        cotangents = [side_by_side(do_ref[early, c]) for c in columns]
        keys = [
            jnp.concatenate([far_ref[first, c], near_ref[first, c], k_ref[early, c]], axis=0)
            for c in columns
        ]
        values = [
            jnp.concatenate([far_ref[second, c], near_ref[second, c], v_ref[early, c]], axis=0)
            for c in columns
        ]
        pairs = [
            score_pair(k, q, v, do, bias)
            for k, q, v, do in zip(keys, queries, values, cotangents)
        ]
        weights, _, deltas = softmax_columns(pairs)
        grads = score_grads_of(pairs, weights, deltas)
        for n, c in enumerate(columns):
            w, g = weights[n].astype(jnp.bfloat16), grads[n]
            attn_ref[:, c] = own_diagonal(dot(w, values[n], 0, 0)).astype(jnp.bfloat16)
            gq_ref[:, c] = own_diagonal(dot(g, keys[n], 0, 0)).astype(jnp.bfloat16)
            gk = gk_part_ref[early, c] + dot(g[prior:], queries[n], 1, 0)
            gv = gv_part_ref[early, c] + dot(w[prior:], cotangents[n], 1, 0)
            gk_ref[:, c] = gk.astype(jnp.bfloat16)
            gv_ref[:, c] = gv.astype(jnp.bfloat16)
        for copy in copies(at):
            copy.start()

    for at in range(width // step):
        for copy in copies(at):
            copy.wait()
    for copy in late_copies:
        copy.wait()


def tail_half(prior, low, bias_ref, k_ref, v_ref, gk_part_ref, gv_part_ref, after_ref):
    tok, half = k_ref.shape[0], prior // 2
    far = bias_ref[half - 1 : half, 0:1] == 0.0
    bias = jnp.where(far, bias_ref[...], MASKED)
    first, second, last = slice(0, half), slice(half, prior), slice(tok - prior, tok)
    places = head_columns(0, after_ref.shape[1], 4)
    columns = head_columns(low, low + after_ref.shape[1], 4)
    queries = [side_by_side(after_ref[first, p]) for p in places]
    cotangents = [side_by_side(after_ref[second, p]) for p in places]
    pairs = [
        score_pair(k_ref[last, c], q, v_ref[last, c], do, bias)
        for c, q, do in zip(columns, queries, cotangents)
    ]
    own = [
        (joined(after_ref[half - 16 : half, p][15:]), joined(after_ref[prior - 16 : prior, p][15:]))
        for p in places
    ]
    weights, grads = merged_columns(pairs, own)

    def fill(ref, part_ref, lefts, rights, rows):
        for p, c, left, right in zip(places, columns, lefts, rights):
            total = part_ref[last, c] + dot(left, right, 1, 0)
            terms = jnp.where(far, 0.0, after_ref[rows, p].astype(jnp.float32))
            ref[first, p] = total[first].astype(jnp.bfloat16)
            ref[second, p] = (total[second] + terms).astype(jnp.bfloat16)

    return (
        lambda ref: fill(ref, gv_part_ref, weights, cotangents, second),
        lambda ref: fill(ref, gk_part_ref, grads, queries, first),
    )


def tail_kernel(prior, bias_ref, k_ref, v_ref, gk_part_ref, gv_part_ref, after_ref, gk_ref, gv_ref):
    fill_gv, fill_gk = tail_half(
        prior, 0, bias_ref, k_ref, v_ref, gk_part_ref, gv_part_ref, after_ref
    )
    fill_gv(gv_ref)
    fill_gk(gk_ref)


def last_kernel(
    prior, bias_ref, k_ref, v_ref, gk_part_ref, gv_part_ref, after_ref, gk_first_ref, gv_first_ref,
    gk_in, gv_in, gk_hbm, gv_hbm, gk_ref, gv_ref, sems,
):
    rows = pl.ds(k_ref.shape[0] - prior, prior)
    low = gk_first_ref.shape[1]
    copies = []

    def send(ref, hbm, start):
        cols = pl.ds(start, ref.shape[1])
        copies.append(pltpu.make_async_copy(ref, hbm.at[rows, cols], sems.at[len(copies)]))
        copies[-1].start()

    send(gv_first_ref, gv_hbm, 0)
    send(gk_first_ref, gk_hbm, 0)
    fill_gv, fill_gk = tail_half(
        prior, low, bias_ref, k_ref, v_ref, gk_part_ref, gv_part_ref, after_ref
    )
    fill_gv(gv_ref)
    send(gv_ref, gv_hbm, low)
    fill_gk(gk_ref)
    send(gk_ref, gk_hbm, low)
    for copy in copies:
        copy.wait()


def neighbour(value, by):
    peers = lax.axis_size("seq") * lax.axis_size("head")
    pairs = [(i, i + by) for i in range(peers) if 0 <= i + by < peers]
    return lax.ppermute(value, ("seq", "head"), pairs)


def cost(heads, queries, keys, products, moved):
    return pl.CostEstimate(
        flops=2 * heads * queries * keys * HEAD_DIM * products,
        bytes_accessed=moved,
        transcendentals=heads * queries * keys,
    )


def halo_shards(query_in, key_in, value_in, grad_out, module_lengths):
    tok, width = query_in.shape
    prior = tok * lax.axis_size("head") // 8
    step = math.gcd(width, 8 * HEAD_DIM)
    groups = width // step
    anywhere = pl.BlockSpec(memory_space=pl.ANY)
    inside = pl.BlockSpec(memory_space=pltpu.VMEM)
    full16 = jax.ShapeDtypeStruct((tok, width), jnp.bfloat16)

    def near16(rows, columns):
        return pltpu.VMEM((rows, columns), jnp.bfloat16)

    def near32(rows, columns):
        return pltpu.VMEM((rows, columns), jnp.float32)

    def in_hbm(*values):
        return [pltpu.with_memory_space_constraint(value, pltpu.HBM) for value in values]

    def in_vmem(*values):
        return [pltpu.with_memory_space_constraint(value, pltpu.VMEM) for value in values]

    def call(kernel, name, ins, outs, shapes, scratch, work, moved, aliases=None):
        return pl.pallas_call(
            kernel,
            in_specs=ins,
            out_specs=outs,
            out_shape=shapes,
            scratch_shapes=scratch,
            input_output_aliases=aliases or {},
            cost_estimate=cost(*work, moved),
            compiler_params=pltpu.CompilerParams(vmem_limit_bytes=16 * 2**20),
            name=name,
        )

    near = call(
        functools.partial(pack_kernel, prior), "near_keys",
        [anywhere] * 2, inside, near16(prior, width),
        [pltpu.SemaphoreType.DMA((2,))], (0, 0, 0, 0), 4 * prior * width,
    )(*in_hbm(key_in, value_in))
    near = neighbour(near, 1)

    lengths = module_lengths.reshape(1, -1)
    far, q, k, v, do, own_bias, near_bias, lead_bias, tail_bias = call(
        functools.partial(ready_kernel, prior), "operands",
        [anywhere] * 5, [inside] * 9,
        [near16(prior, width)] + [near16(tok, width)] * 4
        + [near32(tok, 2 * prior), near32(prior + prior // 2, 2 * prior)]
        + [near32(2 * prior, 2 * prior), near32(prior, 2 * prior)],
        [
            pltpu.VMEM(lengths.shape, jnp.int32), pltpu.SemaphoreType.DMA((4,)),
            pltpu.SemaphoreType.DMA((2,)), pltpu.SemaphoreType.DMA(()),
        ],
        (0, 0, 0, 0), 18 * tok * width,
    )(*in_hbm(lengths, query_in, key_in, value_in, grad_out))

    def own_block(odd, *partial):
        return call(
            functools.partial(own_kernel, prior, step, odd), "own_block",
            [inside] * (5 + len(partial)), [inside] * 4,
            [near16(tok - prior, width)] * 2 + [near32(tok, width)] * 2, (),
            (width // HEAD_DIM, tok - prior, tok, 6), 18 * tok * width,
            {5 + n: n for n in range(len(partial))},
        )(*in_vmem(own_bias, q, k, v, do, *partial))

    partial = own_block(1)
    far, partial = lax.optimization_barrier((far, partial))
    far = neighbour(far, 1)
    attn, gq, gk_part, gv_part = own_block(0, *partial)
    near_bias, attn = lax.optimization_barrier((near_bias, attn))
    backs = call(
        functools.partial(near_kernel, prior), "near_terms",
        [inside] * 7, [inside] * 2, [near16(prior, width // 2)] * 2, (),
        (width // HEAD_DIM, prior, prior + prior // 2, 3), 8 * tok * width,
    )(*in_vmem(near_bias, lead_bias, q, k, v, do, near))
    backs = [neighbour(back, -1) for back in backs]

    attn, gq, gk, gv = call(
        functools.partial(lead_kernel, prior, step), "lead_rows",
        [inside] * 11, [anywhere] * 4, [full16] * 4,
        [near16(prior, width)] * 4
        + [pltpu.SemaphoreType.DMA((groups, 4)), pltpu.SemaphoreType.DMA((2,))],
        (width // HEAD_DIM, prior, 2 * prior, 6), 20 * tok * width,
    )(*in_vmem(lead_bias, q, k, v, do, near, far, gk_part, gv_part, attn, gq))

    here = in_vmem(tail_bias, k, v, gk_part, gv_part)
    work = (width // HEAD_DIM // 2, prior, prior // 2, 4)
    halves = call(
        functools.partial(tail_kernel, prior), "tail_keys",
        [inside] * 6, [inside] * 2, [near16(prior, width // 2)] * 2, (), work, 4 * tok * width,
    )(*here, *in_vmem(backs[0]))
    gk, gv = call(
        functools.partial(last_kernel, prior), "last_keys",
        [inside] * 8 + [anywhere] * 2, [anywhere] * 2, [full16] * 2,
        [near16(prior, width // 2)] * 2 + [pltpu.SemaphoreType.DMA((4,))],
        work, 6 * tok * width, {8: 0, 9: 1},
    )(*here, *in_vmem(backs[1], *halves), gk, gv)
    return (attn, gq, gk, gv)


def shards(query_in, key_in, value_in, grad_out, module_lengths):
    tok = query_in.shape[0]
    prior = tok * lax.axis_size("head") // 8
    plan = halo_shards if 2 * prior == tok else gathered_shards
    return plan(query_in, key_in, value_in, grad_out, module_lengths)


def solution(mesh):
    placed = (
        P(("seq", "head"), None),
        P(("seq", "head"), None),
        P(("seq", "head"), None),
        P(("seq", "head"), None),
        P(),
    )
    return jax.shard_map(
        shards,
        mesh=mesh,
        in_specs=placed,
        out_specs=(
            P(("seq", "head"), None),
            P(("seq", "head"), None),
            P(("seq", "head"), None),
            P(("seq", "head"), None),
        ),
        check_vma=False,
    )
```

```python
import functools
import math

import jax
import jax.numpy as jnp
from jax import lax
from jax.experimental import pallas as pl
from jax.experimental.pallas import tpu as pltpu
from jax.sharding import PartitionSpec as P

HEAD_DIM = 128
SCALE = HEAD_DIM ** (-0.5)
LOG2E = math.log2(math.e)
MASKED = -1e30


def shifted(value, axis, by):
    peers = lax.axis_size(axis)
    pairs = [(i, i + by) for i in range(peers) if 0 <= i + by < peers]
    return lax.ppermute(value, axis, pairs)


def module_ids(module_lengths, positions):
    module_ends = jnp.cumsum(module_lengths)
    counted = jnp.sum((positions[:, None] >= module_ends[None, :]).astype(jnp.int32), axis=1)
    return jnp.where(positions >= 0, counted, -1)


def allowed_pairs(module_lengths, query_pos, key_pos):
    same = (
        module_ids(module_lengths, query_pos)[:, None]
        == module_ids(module_lengths, key_pos)[None, :]
    )
    return same & (key_pos[None, :] <= query_pos[:, None])


def score_grads(grad_rows, value_block, weights, row_delta, score_scale):
    dprobs = jnp.einsum("qd,kd->qk", grad_rows, value_block, preferred_element_type=jnp.float32)
    return (weights * (dprobs - row_delta[:, None]) * score_scale).astype(jnp.bfloat16)


def key_terms(dscores, weight_bf, query_rows, grad_rows):
    key_grad = jnp.einsum("qk,qd->kd", dscores, query_rows, preferred_element_type=jnp.float32)
    value_grad = jnp.einsum("qk,qd->kd", weight_bf, grad_rows, preferred_element_type=jnp.float32)
    return (key_grad, value_grad)


def one_block(query_rows, key_block, value_block, grad_rows, allowed, score_scale):
    scores = (
        jnp.einsum("qd,kd->qk", query_rows, key_block, preferred_element_type=jnp.float32)
        * score_scale
    )
    row_top = jnp.max(jnp.where(allowed, scores, -jnp.inf), axis=1, keepdims=True)
    row_total = jnp.sum(jnp.where(allowed, jnp.exp(scores - row_top), 0.0), axis=1, keepdims=True)
    log_total = row_top + jnp.log(row_total)
    weights = jnp.where(allowed, jnp.exp(scores - log_total), 0.0)
    weight_bf = weights.astype(jnp.bfloat16)
    attn_rows = jnp.einsum(
        "qk,kd->qd", weight_bf, value_block, preferred_element_type=jnp.float32
    ).astype(jnp.bfloat16)
    row_delta = jnp.sum(grad_rows.astype(jnp.float32) * attn_rows.astype(jnp.float32), axis=1)
    dscores = score_grads(grad_rows, value_block, weights, row_delta, score_scale)
    grad_q = jnp.einsum("qk,kd->qd", dscores, key_block, preferred_element_type=jnp.float32).astype(
        jnp.bfloat16
    )
    key_grad, value_grad = key_terms(dscores, weight_bf, query_rows, grad_rows)
    return (attn_rows, grad_q, key_grad, value_grad, log_total[:, 0], row_delta)


def gathered_shards(query_in, key_in, value_in, grad_out, module_lengths):
    head_q, head_k, head_v, head_do = (
        lax.all_to_all(query_in, "head", split_axis=1, concat_axis=0, tiled=True),
        lax.all_to_all(key_in, "head", split_axis=1, concat_axis=0, tiled=True),
        lax.all_to_all(value_in, "head", split_axis=1, concat_axis=0, tiled=True),
        lax.all_to_all(grad_out, "head", split_axis=1, concat_axis=0, tiled=True),
    )
    row_count = head_q.shape[0]
    width = head_q.shape[1]
    local_heads = width // HEAD_DIM
    prior_rows = row_count // 8
    score_scale = HEAD_DIM ** (-0.5)
    tail_start = row_count - prior_rows
    prior_k, prior_v = shifted((head_k[tail_start:], head_v[tail_start:]), "seq", 1)
    row_start = lax.axis_index("seq") * row_count
    query_pos = row_start + jnp.arange(row_count, dtype=jnp.int32)
    before_pos = row_start - prior_rows + jnp.arange(prior_rows, dtype=jnp.int32)
    key_pos = jnp.concatenate([before_pos, query_pos])
    block_rows = math.gcd(row_count, 512)
    block_count = row_count // block_rows
    pos_blocks = query_pos.reshape(block_count, block_rows)

    def by_head(flat, rows):
        return jnp.moveaxis(flat.reshape(rows, local_heads, HEAD_DIM), 1, 0)

    def to_flat(stacked):
        return jnp.moveaxis(stacked, 0, 1).reshape(stacked.shape[1], width)

    query_h = by_head(head_q, row_count)
    grad_h = by_head(head_do, row_count)
    key_h = by_head(jnp.concatenate([prior_k, head_k], axis=0), row_count + prior_rows)
    value_h = by_head(jnp.concatenate([prior_v, head_v], axis=0), row_count + prior_rows)

    def run_head(packed):
        query_rows, key_block, value_block, grad_rows = packed
        query_blocks = query_rows.reshape(block_count, block_rows, HEAD_DIM)
        grad_blocks = grad_rows.reshape(block_count, block_rows, HEAD_DIM)

        def run_block(inner):
            query_part, grad_part, pos_part = inner
            allowed = allowed_pairs(module_lengths, pos_part, key_pos)
            return one_block(query_part, key_block, value_block, grad_part, allowed, score_scale)

        attn_b, grad_qb, key_b, value_b, lse_b, delta_b = lax.map(
            run_block, (query_blocks, grad_blocks, pos_blocks)
        )
        return (
            attn_b.reshape(row_count, HEAD_DIM),
            grad_qb.reshape(row_count, HEAD_DIM),
            jnp.sum(key_b, axis=0),
            jnp.sum(value_b, axis=0),
            lse_b.reshape(row_count),
            delta_b.reshape(row_count),
        )

    attn_h, grad_qh, key_grad, value_grad, log_total, row_delta = lax.map(
        run_head, (query_h, key_h, value_h, grad_h)
    )
    attn_flat = to_flat(attn_h)
    attn_back = lax.all_to_all(attn_flat, "head", split_axis=0, concat_axis=1, tiled=True)
    grad_q = to_flat(grad_qh)
    later_k, later_v = shifted((key_grad[:, :prior_rows], value_grad[:, :prior_rows]), "seq", -1)
    key_total = key_grad[:, prior_rows:].at[:, tail_start:].add(later_k)
    value_total = value_grad[:, prior_rows:].at[:, tail_start:].add(later_v)
    grad_k = to_flat(key_total.astype(jnp.bfloat16))
    grad_v = to_flat(value_total.astype(jnp.bfloat16))
    back_q, back_k, back_v = (
        lax.all_to_all(grad_q, "head", split_axis=0, concat_axis=1, tiled=True),
        lax.all_to_all(grad_k, "head", split_axis=0, concat_axis=1, tiled=True),
        lax.all_to_all(grad_v, "head", split_axis=0, concat_axis=1, tiled=True),
    )
    return (attn_back, back_q, back_k, back_v)


def dot(left, right, left_dim, right_dim):
    return lax.dot_general(
        left, right, (((left_dim,), (right_dim,)), ((), ())), preferred_element_type=jnp.float32
    )


def module_ends_col(lengths_row):
    count = lengths_row.shape[1]
    row = lax.broadcasted_iota(jnp.int32, (count, count), 0)
    col = lax.broadcasted_iota(jnp.int32, (count, count), 1)
    return jnp.sum(jnp.where(col <= row, lengths_row, 0.0), axis=1, keepdims=True)


def bias_by_key(lengths_row, first_query, queries, first_key, keys, heads):
    ends = module_ends_col(lengths_row)
    lane = lax.broadcasted_iota(jnp.int32, (1, heads * queries), 1)
    query = (first_query + lane % queries).astype(jnp.float32)
    start = jnp.max(jnp.where(ends <= query, ends, 0.0), axis=0, keepdims=True)
    key = (first_key + lax.broadcasted_iota(jnp.int32, (keys, heads * queries), 0)).astype(
        jnp.float32
    )
    return jnp.where((key >= start) & (key <= query), 0.0, MASKED)


def score_pair(k, q, v, do, bias):
    return dot(k, q, 1, 1) * (SCALE * LOG2E) + bias, dot(v, do, 1, 1)


def softmax_columns(pairs):
    tops = [jnp.max(s, axis=0, keepdims=True) for s, _ in pairs]
    raws = [jnp.exp2(s - top) for (s, _), top in zip(pairs, tops)]
    totals = [jnp.sum(raw, axis=0, keepdims=True) for raw in raws]
    weights = [raw * (1.0 / total) for raw, total in zip(raws, totals)]
    deltas = [jnp.sum(w * dp, axis=0, keepdims=True) for w, (_, dp) in zip(weights, pairs)]
    logs = [top + jnp.log2(total) for top, total in zip(tops, totals)]
    return weights, logs, deltas


def score_grads_of(pairs, weights, deltas):
    return [
        (w * (dp - delta) * SCALE).astype(jnp.bfloat16)
        for w, (_, dp), delta in zip(weights, pairs, deltas)
    ]


def merged_columns(pairs, own):
    tops = [
        jnp.maximum(jnp.max(s, axis=0, keepdims=True), log) for (s, _), (log, _) in zip(pairs, own)
    ]
    raws = [jnp.exp2(s - top) for (s, _), top in zip(pairs, tops)]
    own_raws = [jnp.exp2(log - top) for (log, _), top in zip(own, tops)]
    parts = [
        1.0 / (jnp.sum(raw, axis=0, keepdims=True) + own_raw)
        for raw, own_raw in zip(raws, own_raws)
    ]
    weights = [raw * part for raw, part in zip(raws, parts)]
    deltas = [
        jnp.sum(w * dp, axis=0, keepdims=True) + own_raw * part * own_delta
        for w, (_, dp), own_raw, part, (_, own_delta) in zip(weights, pairs, own_raws, parts, own)
    ]
    grads = [w * (dp - delta) * SCALE for w, (_, dp), delta in zip(weights, pairs, deltas)]
    return [w.astype(jnp.bfloat16) for w in weights], [g.astype(jnp.bfloat16) for g in grads]


def side_by_side(rows):
    heads = rows.shape[1] // HEAD_DIM
    zero = jnp.zeros((rows.shape[0], HEAD_DIM), rows.dtype)
    blocks = [rows[:, c] for c in head_columns(0, rows.shape[1])]
    return jnp.concatenate(
        [
            jnp.concatenate([blocks[h] if g == h else zero for g in range(heads)], axis=1)
            for h in range(heads)
        ],
        axis=0,
    )


def head_columns(low, high, heads=1):
    wide = heads * HEAD_DIM
    return [slice(c, c + wide) for c in range(low, high, wide)]


def device_first(tok):
    place = lax.axis_index("seq") * lax.axis_size("head") + lax.axis_index("head")
    return place * tok


def fours(rows):
    table = jnp.concatenate(rows, axis=0)
    half = table.shape[1] // 4
    lane = lax.broadcasted_iota(jnp.int32, (1, table.shape[1]), 1)
    turned = [pltpu.roll(table, turn * half, 1) for turn in (3, 2, 1)]
    merged = []
    for at in range(0, len(rows), 2):
        now, after = slice(at, at + 1), slice(at + 1, at + 2)
        row = jnp.where(lane < 3 * half, turned[1][after], turned[2][after])
        row = jnp.where(lane < 2 * half, turned[0][now], row)
        merged.append(jnp.where(lane < half, table[now], row))
    return merged


def split_bf16(row):
    parts = []
    for _ in range(3):
        part = row.astype(jnp.bfloat16)
        parts.append(part)
        row = row - part.astype(jnp.float32)
    return jnp.concatenate([*parts, jnp.zeros_like(parts[0])], axis=1)


def joined(parts):
    parts = parts.astype(jnp.float32)
    count = parts.shape[1] // 4
    return parts[:, :count] + parts[:, count : 2 * count] + parts[:, 2 * count : 3 * count]


def pack_copies(prior, at, k_ref, v_ref, packed_ref, sems):
    half, tok = prior // 2, k_ref.shape[0]
    rows = pl.ds(tok - (at + 1) * half, half)
    return [
        pltpu.make_async_copy(
            ref.at[rows, :], packed_ref.at[pl.ds(n * half, half), :], sems.at[n]
        )
        for n, ref in enumerate((k_ref, v_ref))
    ]


def pack_kernel(prior, k_ref, v_ref, near_ref, sems):
    copies = pack_copies(prior, 0, k_ref, v_ref, near_ref, sems)
    for copy in copies:
        copy.start()
    for copy in copies:
        copy.wait()


def ready_kernel(
    prior, len_hbm, q_hbm, k_hbm, v_hbm, do_hbm, far_ref, q_ref, k_ref, v_ref, do_ref,
    own_bias_ref, near_bias_ref, lead_bias_ref, tail_bias_ref, len_ref, sems, far_sems, len_sem,
):
    tok, half = k_ref.shape[0], prior // 2
    pairs = ((q_hbm, q_ref), (k_hbm, k_ref), (v_hbm, v_ref), (do_hbm, do_ref))
    copies = pack_copies(prior, 1, k_hbm, v_hbm, far_ref, far_sems)
    copies += [pltpu.make_async_copy(hbm, ref, sems.at[n]) for n, (hbm, ref) in enumerate(pairs)]
    len_copy = pltpu.make_async_copy(len_hbm, len_ref, len_sem)
    len_copy.start()
    for copy in copies:
        copy.start()
    len_copy.wait()
    first = device_first(tok)
    lengths = len_ref[...].astype(jnp.float32)
    own_bias_ref[...] = bias_by_key(lengths, first + prior, tok - prior, first, tok, 2)
    near_bias_ref[...] = bias_by_key(lengths, first, prior, first - half, prior + half, 2)
    lead_bias_ref[...] = bias_by_key(lengths, first, prior, first - prior, 2 * prior, 2)
    tail_bias_ref[...] = bias_by_key(lengths, first + tok, half, first + tok - prior, prior, 4)
    for copy in copies:
        copy.wait()


def own_diagonal(both):
    rows = both.shape[0] // 2
    return jnp.concatenate([both[:rows, :HEAD_DIM], both[rows:, HEAD_DIM:]], axis=1)


def pair_columns(at, step):
    wide = 2 * HEAD_DIM
    return [pl.ds(pl.multiple_of(at * step + c, wide), wide) for c in range(0, step, wide)]


def own_kernel(prior, step, odd, bias_ref, q_ref, k_ref, v_ref, do_ref, *refs):
    attn_ref, gq_ref, gk_ref, gv_ref = refs[-4:]
    tok, width = k_ref.shape
    late = slice(prior, tok)

    @pl.when(lax.axis_index("seq") % 2 == odd)
    def _():
        @pl.loop(0, width // step)
        def _(at):
            bias = bias_ref[...]
            columns = pair_columns(at, step)
            queries = [side_by_side(q_ref[late, c]) for c in columns]
            cotangents = [side_by_side(do_ref[late, c]) for c in columns]
            pairs = [
                score_pair(k_ref[:, c], q, v_ref[:, c], do, bias)
                for c, q, do in zip(columns, queries, cotangents)
            ]
            weights, _, deltas = softmax_columns(pairs)
            grads = score_grads_of(pairs, weights, deltas)
            for c, w, g, q, do in zip(columns, weights, grads, queries, cotangents):
                w = w.astype(jnp.bfloat16)
                attn_ref[:, c] = own_diagonal(dot(w, v_ref[:, c], 0, 0)).astype(jnp.bfloat16)
                gq_ref[:, c] = own_diagonal(dot(g, k_ref[:, c], 0, 0)).astype(jnp.bfloat16)
                gk_ref[:, c] = dot(g, q, 1, 0)
                gv_ref[:, c] = dot(w, do, 1, 0)


def near_kernel(
    prior, near_bias_ref, lead_bias_ref, q_ref, k_ref, v_ref, do_ref, near_ref, *back_refs
):
    width, half = q_ref.shape[1], prior // 2
    far = lead_bias_ref[half - 1 : half, 0:1] == 0.0
    key = lax.broadcasted_iota(jnp.int32, (prior + half, 1), 0)
    bias = jnp.where(far & (key < half), MASKED, near_bias_ref[...])
    spare = lax.broadcasted_iota(jnp.int32, (half, 1), 0) == half - 1
    early, first, second = slice(0, prior), slice(0, half), slice(half, prior)
    columns = head_columns(0, width, 2)
    queries = [side_by_side(q_ref[early, c]) for c in columns]
    cotangents = [side_by_side(do_ref[early, c]) for c in columns]
    pairs = []
    for c, q, do in zip(columns, queries, cotangents):
        k = jnp.concatenate([near_ref[first, c], k_ref[early, c]], axis=0)
        v = jnp.concatenate([near_ref[second, c], v_ref[early, c]], axis=0)
        pairs.append(score_pair(k, q, v, do, bias))
    weights, logs, deltas = softmax_columns(pairs)
    weights = [w[:half] for w in weights]
    grads = score_grads_of([(s[:half], dp[:half]) for s, dp in pairs], weights, deltas)
    k_terms = [dot(g, q, 1, 0) for g, q in zip(grads, queries)]
    v_terms = [dot(w.astype(jnp.bfloat16), do, 1, 0) for w, do in zip(weights, cotangents)]
    logs, deltas = fours(logs), fours(deltas)
    for at, c in enumerate(head_columns(0, width, 4)):
        back_ref = back_refs[c.start * len(back_refs) // width]
        low = c.start % back_ref.shape[1]
        here = slice(low, low + c.stop - c.start)
        for row, terms, ref, place in (
            (logs[at], k_terms, q_ref, first), (deltas[at], v_terms, do_ref, second)
        ):
            rows = jnp.where(spare, split_bf16(row), ref[first, c])
            terms = jnp.concatenate(terms[2 * at : 2 * at + 2], axis=1).astype(jnp.bfloat16)
            back_ref[place, here] = jnp.where(far, rows, terms)


def lead_kernel(
    prior, step, bias_ref, q_ref, k_ref, v_ref, do_ref, near_ref, far_ref, gk_part_ref, gv_part_ref,
    attn_late_ref, gq_late_ref, attn_hbm, gq_hbm, gk_hbm, gv_hbm,
    attn_ref, gq_ref, gk_ref, gv_ref, sems, late_sems,
):
    tok, width = q_ref.shape
    half = prior // 2
    early, first, second = slice(0, prior), slice(0, half), slice(half, prior)
    late = pl.ds(prior, tok - prior)
    late_copies = [
        pltpu.make_async_copy(attn_late_ref, attn_hbm.at[late, :], late_sems.at[0]),
        pltpu.make_async_copy(gq_late_ref, gq_hbm.at[late, :], late_sems.at[1]),
    ]
    for copy in late_copies:
        copy.start()

    def copies(at):
        cols = pl.ds(pl.multiple_of(at * step, step), step)
        pairs = ((attn_ref, attn_hbm), (gq_ref, gq_hbm), (gk_ref, gk_hbm), (gv_ref, gv_hbm))
        return [
            pltpu.make_async_copy(ref.at[:, cols], hbm.at[pl.ds(0, prior), cols], sems.at[at, n])
            for n, (ref, hbm) in enumerate(pairs)
        ]

    @pl.loop(0, width // step)
    def _(at):
        bias = bias_ref[...]
        columns = pair_columns(at, step)
        queries = [side_by_side(q_ref[early, c]) for c in columns]
        cotangents = [side_by_side(do_ref[early, c]) for c in columns]
        keys = [
            jnp.concatenate([far_ref[first, c], near_ref[first, c], k_ref[early, c]], axis=0)
            for c in columns
        ]
        values = [
            jnp.concatenate([far_ref[second, c], near_ref[second, c], v_ref[early, c]], axis=0)
            for c in columns
        ]
        pairs = [
            score_pair(k, q, v, do, bias)
            for k, q, v, do in zip(keys, queries, values, cotangents)
        ]
        weights, _, deltas = softmax_columns(pairs)
        grads = score_grads_of(pairs, weights, deltas)
        for n, c in enumerate(columns):
            w, g = weights[n].astype(jnp.bfloat16), grads[n]
            attn_ref[:, c] = own_diagonal(dot(w, values[n], 0, 0)).astype(jnp.bfloat16)
            gq_ref[:, c] = own_diagonal(dot(g, keys[n], 0, 0)).astype(jnp.bfloat16)
            gk = gk_part_ref[early, c] + dot(g[prior:], queries[n], 1, 0)
            gv = gv_part_ref[early, c] + dot(w[prior:], cotangents[n], 1, 0)
            gk_ref[:, c] = gk.astype(jnp.bfloat16)
            gv_ref[:, c] = gv.astype(jnp.bfloat16)
        for copy in copies(at):
            copy.start()

    for at in range(width // step):
        for copy in copies(at):
            copy.wait()
    for copy in late_copies:
        copy.wait()


def tail_half(prior, low, bias_ref, k_ref, v_ref, gk_part_ref, gv_part_ref, after_ref):
    tok, half = k_ref.shape[0], prior // 2
    far = bias_ref[half - 1 : half, 0:1] == 0.0
    bias = jnp.where(far, bias_ref[...], MASKED)
    first, second, last = slice(0, half), slice(half, prior), slice(tok - prior, tok)
    places = head_columns(0, after_ref.shape[1], 4)
    columns = head_columns(low, low + after_ref.shape[1], 4)
    queries = [side_by_side(after_ref[first, p]) for p in places]
    cotangents = [side_by_side(after_ref[second, p]) for p in places]
    pairs = [
        score_pair(k_ref[last, c], q, v_ref[last, c], do, bias)
        for c, q, do in zip(columns, queries, cotangents)
    ]
    own = [
        (joined(after_ref[half - 16 : half, p][15:]), joined(after_ref[prior - 16 : prior, p][15:]))
        for p in places
    ]
    weights, grads = merged_columns(pairs, own)

    def fill(ref, part_ref, lefts, rights, rows):
        for p, c, left, right in zip(places, columns, lefts, rights):
            total = part_ref[last, c] + dot(left, right, 1, 0)
            terms = jnp.where(far, 0.0, after_ref[rows, p].astype(jnp.float32))
            ref[first, p] = total[first].astype(jnp.bfloat16)
            ref[second, p] = (total[second] + terms).astype(jnp.bfloat16)

    return (
        lambda ref: fill(ref, gv_part_ref, weights, cotangents, second),
        lambda ref: fill(ref, gk_part_ref, grads, queries, first),
    )


def tail_kernel(prior, bias_ref, k_ref, v_ref, gk_part_ref, gv_part_ref, after_ref, gk_ref, gv_ref):
    fill_gv, fill_gk = tail_half(
        prior, 0, bias_ref, k_ref, v_ref, gk_part_ref, gv_part_ref, after_ref
    )
    fill_gv(gv_ref)
    fill_gk(gk_ref)


def last_kernel(
    prior, bias_ref, k_ref, v_ref, gk_part_ref, gv_part_ref, after_ref, gk_first_ref, gv_first_ref,
    gk_in, gv_in, gk_hbm, gv_hbm, gk_ref, gv_ref, sems,
):
    rows = pl.ds(k_ref.shape[0] - prior, prior)
    low = gk_first_ref.shape[1]
    copies = []

    def send(ref, hbm, start):
        cols = pl.ds(start, ref.shape[1])
        copies.append(pltpu.make_async_copy(ref, hbm.at[rows, cols], sems.at[len(copies)]))
        copies[-1].start()

    send(gv_first_ref, gv_hbm, 0)
    send(gk_first_ref, gk_hbm, 0)
    fill_gv, fill_gk = tail_half(
        prior, low, bias_ref, k_ref, v_ref, gk_part_ref, gv_part_ref, after_ref
    )
    fill_gv(gv_ref)
    send(gv_ref, gv_hbm, low)
    fill_gk(gk_ref)
    send(gk_ref, gk_hbm, low)
    for copy in copies:
        copy.wait()


def neighbour(value, by):
    peers = lax.axis_size("seq") * lax.axis_size("head")
    pairs = [(i, i + by) for i in range(peers) if 0 <= i + by < peers]
    return lax.ppermute(value, ("seq", "head"), pairs)


def cost(heads, queries, keys, products, moved):
    return pl.CostEstimate(
        flops=2 * heads * queries * keys * HEAD_DIM * products,
        bytes_accessed=moved,
        transcendentals=heads * queries * keys,
    )


def halo_shards(query_in, key_in, value_in, grad_out, module_lengths):
    tok, width = query_in.shape
    prior = tok * lax.axis_size("head") // 8
    step = math.gcd(width, 8 * HEAD_DIM)
    groups = width // step
    anywhere = pl.BlockSpec(memory_space=pl.ANY)
    inside = pl.BlockSpec(memory_space=pltpu.VMEM)
    full16 = jax.ShapeDtypeStruct((tok, width), jnp.bfloat16)

    def near16(rows, columns):
        return pltpu.VMEM((rows, columns), jnp.bfloat16)

    def near32(rows, columns):
        return pltpu.VMEM((rows, columns), jnp.float32)

    def in_hbm(*values):
        return [pltpu.with_memory_space_constraint(value, pltpu.HBM) for value in values]

    def in_vmem(*values):
        return [pltpu.with_memory_space_constraint(value, pltpu.VMEM) for value in values]

    def call(kernel, name, ins, outs, shapes, scratch, work, moved, aliases=None):
        return pl.pallas_call(
            kernel,
            in_specs=ins,
            out_specs=outs,
            out_shape=shapes,
            scratch_shapes=scratch,
            input_output_aliases=aliases or {},
            cost_estimate=cost(*work, moved),
            compiler_params=pltpu.CompilerParams(vmem_limit_bytes=16 * 2**20),
            name=name,
        )

    near = call(
        functools.partial(pack_kernel, prior), "near_keys",
        [anywhere] * 2, inside, near16(prior, width),
        [pltpu.SemaphoreType.DMA((2,))], (0, 0, 0, 0), 4 * prior * width,
    )(*in_hbm(key_in, value_in))
    near = neighbour(near, 1)

    lengths = module_lengths.reshape(1, -1)
    far, q, k, v, do, own_bias, near_bias, lead_bias, tail_bias = call(
        functools.partial(ready_kernel, prior), "operands",
        [anywhere] * 5, [inside] * 9,
        [near16(prior, width)] + [near16(tok, width)] * 4
        + [near32(tok, 2 * prior), near32(prior + prior // 2, 2 * prior)]
        + [near32(2 * prior, 2 * prior), near32(prior, 2 * prior)],
        [
            pltpu.VMEM(lengths.shape, jnp.int32), pltpu.SemaphoreType.DMA((4,)),
            pltpu.SemaphoreType.DMA((2,)), pltpu.SemaphoreType.DMA(()),
        ],
        (0, 0, 0, 0), 18 * tok * width,
    )(*in_hbm(lengths, query_in, key_in, value_in, grad_out))

    def own_block(odd, *partial):
        return call(
            functools.partial(own_kernel, prior, step, odd), "own_block",
            [inside] * (5 + len(partial)), [inside] * 4,
            [near16(tok - prior, width)] * 2 + [near32(tok, width)] * 2, (),
            (width // HEAD_DIM, tok - prior, tok, 6), 18 * tok * width,
            {5 + n: n for n in range(len(partial))},
        )(*in_vmem(own_bias, q, k, v, do, *partial))

    partial = own_block(0)
    far, partial = lax.optimization_barrier((far, partial))
    far = neighbour(far, 1)
    attn, gq, gk_part, gv_part = own_block(1, *partial)
    near_bias, attn = lax.optimization_barrier((near_bias, attn))
    backs = call(
        functools.partial(near_kernel, prior), "near_terms",
        [inside] * 7, [inside] * 2, [near16(prior, width // 2)] * 2, (),
        (width // HEAD_DIM, prior, prior + prior // 2, 3), 8 * tok * width,
    )(*in_vmem(near_bias, lead_bias, q, k, v, do, near))
    backs = [neighbour(back, -1) for back in backs]

    attn, gq, gk, gv = call(
        functools.partial(lead_kernel, prior, step), "lead_rows",
        [inside] * 11, [anywhere] * 4, [full16] * 4,
        [near16(prior, width)] * 4
        + [pltpu.SemaphoreType.DMA((groups, 4)), pltpu.SemaphoreType.DMA((2,))],
        (width // HEAD_DIM, prior, 2 * prior, 6), 20 * tok * width,
    )(*in_vmem(lead_bias, q, k, v, do, near, far, gk_part, gv_part, attn, gq))

    here = in_vmem(tail_bias, k, v, gk_part, gv_part)
    work = (width // HEAD_DIM // 2, prior, prior // 2, 4)
    halves = call(
        functools.partial(tail_kernel, prior), "tail_keys",
        [inside] * 6, [inside] * 2, [near16(prior, width // 2)] * 2, (), work, 4 * tok * width,
    )(*here, *in_vmem(backs[0]))
    gk, gv = call(
        functools.partial(last_kernel, prior), "last_keys",
        [inside] * 8 + [anywhere] * 2, [anywhere] * 2, [full16] * 2,
        [near16(prior, width // 2)] * 2 + [pltpu.SemaphoreType.DMA((4,))],
        work, 6 * tok * width, {8: 0, 9: 1},
    )(*here, *in_vmem(backs[1], *halves), gk, gv)
    return (attn, gq, gk, gv)


def shards(query_in, key_in, value_in, grad_out, module_lengths):
    tok = query_in.shape[0]
    prior = tok * lax.axis_size("head") // 8
    plan = halo_shards if 2 * prior == tok else gathered_shards
    return plan(query_in, key_in, value_in, grad_out, module_lengths)


def solution(mesh):
    placed = (
        P(("seq", "head"), None),
        P(("seq", "head"), None),
        P(("seq", "head"), None),
        P(("seq", "head"), None),
        P(),
    )
    return jax.shard_map(
        shards,
        mesh=mesh,
        in_specs=placed,
        out_specs=(
            P(("seq", "head"), None),
            P(("seq", "head"), None),
            P(("seq", "head"), None),
            P(("seq", "head"), None),
        ),
        check_vma=False,
    )
```

```python
import functools
import math

import jax
import jax.numpy as jnp
from jax import lax
from jax.experimental import pallas as pl
from jax.experimental.pallas import tpu as pltpu
from jax.sharding import PartitionSpec as P

HEAD_DIM = 128
SCALE = HEAD_DIM ** (-0.5)
LOG2E = math.log2(math.e)
MASKED = -1e30


def shifted(value, axis, by):
    peers = lax.axis_size(axis)
    pairs = [(i, i + by) for i in range(peers) if 0 <= i + by < peers]
    return lax.ppermute(value, axis, pairs)


def module_ids(module_lengths, positions):
    module_ends = jnp.cumsum(module_lengths)
    counted = jnp.sum((positions[:, None] >= module_ends[None, :]).astype(jnp.int32), axis=1)
    return jnp.where(positions >= 0, counted, -1)


def allowed_pairs(module_lengths, query_pos, key_pos):
    same = (
        module_ids(module_lengths, query_pos)[:, None]
        == module_ids(module_lengths, key_pos)[None, :]
    )
    return same & (key_pos[None, :] <= query_pos[:, None])


def score_grads(grad_rows, value_block, weights, row_delta, score_scale):
    dprobs = jnp.einsum("qd,kd->qk", grad_rows, value_block, preferred_element_type=jnp.float32)
    return (weights * (dprobs - row_delta[:, None]) * score_scale).astype(jnp.bfloat16)


def key_terms(dscores, weight_bf, query_rows, grad_rows):
    key_grad = jnp.einsum("qk,qd->kd", dscores, query_rows, preferred_element_type=jnp.float32)
    value_grad = jnp.einsum("qk,qd->kd", weight_bf, grad_rows, preferred_element_type=jnp.float32)
    return (key_grad, value_grad)


def one_block(query_rows, key_block, value_block, grad_rows, allowed, score_scale):
    scores = (
        jnp.einsum("qd,kd->qk", query_rows, key_block, preferred_element_type=jnp.float32)
        * score_scale
    )
    row_top = jnp.max(jnp.where(allowed, scores, -jnp.inf), axis=1, keepdims=True)
    row_total = jnp.sum(jnp.where(allowed, jnp.exp(scores - row_top), 0.0), axis=1, keepdims=True)
    log_total = row_top + jnp.log(row_total)
    weights = jnp.where(allowed, jnp.exp(scores - log_total), 0.0)
    weight_bf = weights.astype(jnp.bfloat16)
    attn_rows = jnp.einsum(
        "qk,kd->qd", weight_bf, value_block, preferred_element_type=jnp.float32
    ).astype(jnp.bfloat16)
    row_delta = jnp.sum(grad_rows.astype(jnp.float32) * attn_rows.astype(jnp.float32), axis=1)
    dscores = score_grads(grad_rows, value_block, weights, row_delta, score_scale)
    grad_q = jnp.einsum("qk,kd->qd", dscores, key_block, preferred_element_type=jnp.float32).astype(
        jnp.bfloat16
    )
    key_grad, value_grad = key_terms(dscores, weight_bf, query_rows, grad_rows)
    return (attn_rows, grad_q, key_grad, value_grad, log_total[:, 0], row_delta)


def gathered_shards(query_in, key_in, value_in, grad_out, module_lengths):
    head_q, head_k, head_v, head_do = (
        lax.all_to_all(query_in, "head", split_axis=1, concat_axis=0, tiled=True),
        lax.all_to_all(key_in, "head", split_axis=1, concat_axis=0, tiled=True),
        lax.all_to_all(value_in, "head", split_axis=1, concat_axis=0, tiled=True),
        lax.all_to_all(grad_out, "head", split_axis=1, concat_axis=0, tiled=True),
    )
    row_count = head_q.shape[0]
    width = head_q.shape[1]
    local_heads = width // HEAD_DIM
    prior_rows = row_count // 8
    score_scale = HEAD_DIM ** (-0.5)
    tail_start = row_count - prior_rows
    prior_k, prior_v = shifted((head_k[tail_start:], head_v[tail_start:]), "seq", 1)
    row_start = lax.axis_index("seq") * row_count
    query_pos = row_start + jnp.arange(row_count, dtype=jnp.int32)
    before_pos = row_start - prior_rows + jnp.arange(prior_rows, dtype=jnp.int32)
    key_pos = jnp.concatenate([before_pos, query_pos])
    block_rows = math.gcd(row_count, 512)
    block_count = row_count // block_rows
    pos_blocks = query_pos.reshape(block_count, block_rows)

    def by_head(flat, rows):
        return jnp.moveaxis(flat.reshape(rows, local_heads, HEAD_DIM), 1, 0)

    def to_flat(stacked):
        return jnp.moveaxis(stacked, 0, 1).reshape(stacked.shape[1], width)

    query_h = by_head(head_q, row_count)
    grad_h = by_head(head_do, row_count)
    key_h = by_head(jnp.concatenate([prior_k, head_k], axis=0), row_count + prior_rows)
    value_h = by_head(jnp.concatenate([prior_v, head_v], axis=0), row_count + prior_rows)

    def run_head(packed):
        query_rows, key_block, value_block, grad_rows = packed
        query_blocks = query_rows.reshape(block_count, block_rows, HEAD_DIM)
        grad_blocks = grad_rows.reshape(block_count, block_rows, HEAD_DIM)

        def run_block(inner):
            query_part, grad_part, pos_part = inner
            allowed = allowed_pairs(module_lengths, pos_part, key_pos)
            return one_block(query_part, key_block, value_block, grad_part, allowed, score_scale)

        attn_b, grad_qb, key_b, value_b, lse_b, delta_b = lax.map(
            run_block, (query_blocks, grad_blocks, pos_blocks)
        )
        return (
            attn_b.reshape(row_count, HEAD_DIM),
            grad_qb.reshape(row_count, HEAD_DIM),
            jnp.sum(key_b, axis=0),
            jnp.sum(value_b, axis=0),
            lse_b.reshape(row_count),
            delta_b.reshape(row_count),
        )

    attn_h, grad_qh, key_grad, value_grad, log_total, row_delta = lax.map(
        run_head, (query_h, key_h, value_h, grad_h)
    )
    attn_flat = to_flat(attn_h)
    attn_back = lax.all_to_all(attn_flat, "head", split_axis=0, concat_axis=1, tiled=True)
    grad_q = to_flat(grad_qh)
    later_k, later_v = shifted((key_grad[:, :prior_rows], value_grad[:, :prior_rows]), "seq", -1)
    key_total = key_grad[:, prior_rows:].at[:, tail_start:].add(later_k)
    value_total = value_grad[:, prior_rows:].at[:, tail_start:].add(later_v)
    grad_k = to_flat(key_total.astype(jnp.bfloat16))
    grad_v = to_flat(value_total.astype(jnp.bfloat16))
    back_q, back_k, back_v = (
        lax.all_to_all(grad_q, "head", split_axis=0, concat_axis=1, tiled=True),
        lax.all_to_all(grad_k, "head", split_axis=0, concat_axis=1, tiled=True),
        lax.all_to_all(grad_v, "head", split_axis=0, concat_axis=1, tiled=True),
    )
    return (attn_back, back_q, back_k, back_v)


def dot(left, right, left_dim, right_dim):
    return lax.dot_general(
        left, right, (((left_dim,), (right_dim,)), ((), ())), preferred_element_type=jnp.float32
    )


def module_ends_col(lengths_row):
    count = lengths_row.shape[1]
    row = lax.broadcasted_iota(jnp.int32, (count, count), 0)
    col = lax.broadcasted_iota(jnp.int32, (count, count), 1)
    return jnp.sum(jnp.where(col <= row, lengths_row, 0.0), axis=1, keepdims=True)


def bias_by_key(lengths_row, first_query, queries, first_key, keys, heads):
    ends = module_ends_col(lengths_row)
    lane = lax.broadcasted_iota(jnp.int32, (1, heads * queries), 1)
    query = (first_query + lane % queries).astype(jnp.float32)
    start = jnp.max(jnp.where(ends <= query, ends, 0.0), axis=0, keepdims=True)
    key = (first_key + lax.broadcasted_iota(jnp.int32, (keys, heads * queries), 0)).astype(
        jnp.float32
    )
    return jnp.where((key >= start) & (key <= query), 0.0, MASKED)


def score_pair(k, q, v, do, bias):
    return dot(k, q, 1, 1) * (SCALE * LOG2E) + bias, dot(v, do, 1, 1)


def softmax_columns(pairs):
    tops = [jnp.max(s, axis=0, keepdims=True) for s, _ in pairs]
    raws = [jnp.exp2(s - top) for (s, _), top in zip(pairs, tops)]
    totals = [jnp.sum(raw, axis=0, keepdims=True) for raw in raws]
    weights = [raw * (1.0 / total) for raw, total in zip(raws, totals)]
    deltas = [jnp.sum(w * dp, axis=0, keepdims=True) for w, (_, dp) in zip(weights, pairs)]
    logs = [top + jnp.log2(total) for top, total in zip(tops, totals)]
    return weights, logs, deltas


def score_grads_of(pairs, weights, deltas):
    return [
        (w * (dp - delta) * SCALE).astype(jnp.bfloat16)
        for w, (_, dp), delta in zip(weights, pairs, deltas)
    ]


def merged_columns(pairs, own):
    tops = [
        jnp.maximum(jnp.max(s, axis=0, keepdims=True), log) for (s, _), (log, _) in zip(pairs, own)
    ]
    raws = [jnp.exp2(s - top) for (s, _), top in zip(pairs, tops)]
    own_raws = [jnp.exp2(log - top) for (log, _), top in zip(own, tops)]
    parts = [
        1.0 / (jnp.sum(raw, axis=0, keepdims=True) + own_raw)
        for raw, own_raw in zip(raws, own_raws)
    ]
    weights = [raw * part for raw, part in zip(raws, parts)]
    deltas = [
        jnp.sum(w * dp, axis=0, keepdims=True) + own_raw * part * own_delta
        for w, (_, dp), own_raw, part, (_, own_delta) in zip(weights, pairs, own_raws, parts, own)
    ]
    grads = [w * (dp - delta) * SCALE for w, (_, dp), delta in zip(weights, pairs, deltas)]
    return [w.astype(jnp.bfloat16) for w in weights], [g.astype(jnp.bfloat16) for g in grads]


def side_by_side(rows):
    heads = rows.shape[1] // HEAD_DIM
    zero = jnp.zeros((rows.shape[0], HEAD_DIM), rows.dtype)
    blocks = [rows[:, c] for c in head_columns(0, rows.shape[1])]
    return jnp.concatenate(
        [
            jnp.concatenate([blocks[h] if g == h else zero for g in range(heads)], axis=1)
            for h in range(heads)
        ],
        axis=0,
    )


def head_columns(low, high, heads=1):
    wide = heads * HEAD_DIM
    return [slice(c, c + wide) for c in range(low, high, wide)]


def device_first(tok):
    place = lax.axis_index("seq") * lax.axis_size("head") + lax.axis_index("head")
    return place * tok


def fours(rows):
    table = jnp.concatenate(rows, axis=0)
    half = table.shape[1] // 4
    lane = lax.broadcasted_iota(jnp.int32, (1, table.shape[1]), 1)
    turned = [pltpu.roll(table, turn * half, 1) for turn in (3, 2, 1)]
    merged = []
    for at in range(0, len(rows), 2):
        now, after = slice(at, at + 1), slice(at + 1, at + 2)
        row = jnp.where(lane < 3 * half, turned[1][after], turned[2][after])
        row = jnp.where(lane < 2 * half, turned[0][now], row)
        merged.append(jnp.where(lane < half, table[now], row))
    return merged


def split_bf16(row):
    parts = []
    for _ in range(3):
        part = row.astype(jnp.bfloat16)
        parts.append(part)
        row = row - part.astype(jnp.float32)
    return jnp.concatenate([*parts, jnp.zeros_like(parts[0])], axis=1)


def joined(parts):
    parts = parts.astype(jnp.float32)
    count = parts.shape[1] // 4
    return parts[:, :count] + parts[:, count : 2 * count] + parts[:, 2 * count : 3 * count]


def pack_copies(prior, at, pieces, k_ref, v_ref, packed_ref, sems):
    half, (tok, width) = prior // 2, k_ref.shape
    rows, wide = pl.ds(tok - (at + 1) * half, half), width // pieces
    return [
        pltpu.make_async_copy(
            ref.at[rows, pl.ds(piece * wide, wide)],
            packed_ref.at[pl.ds(n * half, half), pl.ds(piece * wide, wide)],
            sems.at[n, piece],
        )
        for piece in range(pieces)
        for n, ref in enumerate((k_ref, v_ref))
    ]


def pack_kernel(prior, k_ref, v_ref, near_ref, sems):
    copies = pack_copies(prior, 0, 2, k_ref, v_ref, near_ref, sems)
    for copy in copies:
        copy.start()
    for copy in copies:
        copy.wait()


def ready_kernel(
    prior, len_hbm, q_hbm, k_hbm, v_hbm, do_hbm, far_ref, q_ref, k_ref, v_ref, do_ref,
    own_bias_ref, near_bias_ref, lead_bias_ref, tail_bias_ref, len_ref, sems, far_sems, len_sem,
):
    tok, half = k_ref.shape[0], prior // 2
    pairs = ((q_hbm, q_ref), (k_hbm, k_ref), (v_hbm, v_ref), (do_hbm, do_ref))
    copies = pack_copies(prior, 1, 1, k_hbm, v_hbm, far_ref, far_sems)
    copies += [pltpu.make_async_copy(hbm, ref, sems.at[n]) for n, (hbm, ref) in enumerate(pairs)]
    len_copy = pltpu.make_async_copy(len_hbm, len_ref, len_sem)
    len_copy.start()
    for copy in copies:
        copy.start()
    len_copy.wait()
    first = device_first(tok)
    lengths = len_ref[...].astype(jnp.float32)
    own_bias_ref[...] = bias_by_key(lengths, first + prior, tok - prior, first, tok, 2)
    near_bias_ref[...] = bias_by_key(lengths, first, prior, first - half, prior + half, 2)
    lead_bias_ref[...] = bias_by_key(lengths, first, prior, first - prior, 2 * prior, 2)
    tail_bias_ref[...] = bias_by_key(lengths, first + tok, half, first + tok - prior, prior, 4)
    for copy in copies:
        copy.wait()


def own_diagonal(both):
    rows = both.shape[0] // 2
    return jnp.concatenate([both[:rows, :HEAD_DIM], both[rows:, HEAD_DIM:]], axis=1)


def pair_columns(at, step):
    wide = 2 * HEAD_DIM
    return [pl.ds(pl.multiple_of(at * step + c, wide), wide) for c in range(0, step, wide)]


def own_kernel(
    prior, step, bias_ref, q_ref, k_ref, v_ref, do_ref, attn_ref, gq_ref, gk_ref, gv_ref
):
    tok, width = k_ref.shape
    late = slice(prior, tok)

    @pl.loop(0, width // step)
    def _(at):
        bias = bias_ref[...]
        columns = pair_columns(at, step)
        queries = [side_by_side(q_ref[late, c]) for c in columns]
        cotangents = [side_by_side(do_ref[late, c]) for c in columns]
        pairs = [
            score_pair(k_ref[:, c], q, v_ref[:, c], do, bias)
            for c, q, do in zip(columns, queries, cotangents)
        ]
        weights, _, deltas = softmax_columns(pairs)
        grads = score_grads_of(pairs, weights, deltas)
        for c, w, g, q, do in zip(columns, weights, grads, queries, cotangents):
            w = w.astype(jnp.bfloat16)
            attn_ref[:, c] = own_diagonal(dot(w, v_ref[:, c], 0, 0)).astype(jnp.bfloat16)
            gq_ref[:, c] = own_diagonal(dot(g, k_ref[:, c], 0, 0)).astype(jnp.bfloat16)
            gk_ref[:, c] = dot(g, q, 1, 0)
            gv_ref[:, c] = dot(w, do, 1, 0)


def near_kernel(
    prior, near_bias_ref, lead_bias_ref, q_ref, k_ref, v_ref, do_ref, near_ref, *back_refs
):
    width, half = q_ref.shape[1], prior // 2
    far = lead_bias_ref[half - 1 : half, 0:1] == 0.0
    key = lax.broadcasted_iota(jnp.int32, (prior + half, 1), 0)
    bias = jnp.where(far & (key < half), MASKED, near_bias_ref[...])
    spare = lax.broadcasted_iota(jnp.int32, (half, 1), 0) == half - 1
    early, first, second = slice(0, prior), slice(0, half), slice(half, prior)
    columns = head_columns(0, width, 2)
    queries = [side_by_side(q_ref[early, c]) for c in columns]
    cotangents = [side_by_side(do_ref[early, c]) for c in columns]
    pairs = []
    for c, q, do in zip(columns, queries, cotangents):
        k = jnp.concatenate([near_ref[first, c], k_ref[early, c]], axis=0)
        v = jnp.concatenate([near_ref[second, c], v_ref[early, c]], axis=0)
        pairs.append(score_pair(k, q, v, do, bias))
    weights, logs, deltas = softmax_columns(pairs)
    weights = [w[:half] for w in weights]
    grads = score_grads_of([(s[:half], dp[:half]) for s, dp in pairs], weights, deltas)
    k_terms = [dot(g, q, 1, 0) for g, q in zip(grads, queries)]
    v_terms = [dot(w.astype(jnp.bfloat16), do, 1, 0) for w, do in zip(weights, cotangents)]
    logs, deltas = fours(logs), fours(deltas)
    for at, c in enumerate(head_columns(0, width, 4)):
        back_ref = back_refs[c.start * len(back_refs) // width]
        low = c.start % back_ref.shape[1]
        here = slice(low, low + c.stop - c.start)
        for row, terms, ref, place in (
            (logs[at], k_terms, q_ref, first), (deltas[at], v_terms, do_ref, second)
        ):
            rows = jnp.where(spare, split_bf16(row), ref[first, c])
            terms = jnp.concatenate(terms[2 * at : 2 * at + 2], axis=1).astype(jnp.bfloat16)
            back_ref[place, here] = jnp.where(far, rows, terms)


def lead_kernel(
    prior, step, bias_ref, q_ref, k_ref, v_ref, do_ref, near_ref, far_ref, gk_part_ref, gv_part_ref,
    attn_late_ref, gq_late_ref, attn_hbm, gq_hbm, gk_hbm, gv_hbm,
    attn_ref, gq_ref, gk_ref, gv_ref, sems, late_sems,
):
    tok, width = q_ref.shape
    half = prior // 2
    early, first, second = slice(0, prior), slice(0, half), slice(half, prior)
    late = pl.ds(prior, tok - prior)
    late_copies = [
        pltpu.make_async_copy(attn_late_ref, attn_hbm.at[late, :], late_sems.at[0]),
        pltpu.make_async_copy(gq_late_ref, gq_hbm.at[late, :], late_sems.at[1]),
    ]
    for copy in late_copies:
        copy.start()

    def copies(at):
        cols = pl.ds(pl.multiple_of(at * step, step), step)
        pairs = ((attn_ref, attn_hbm), (gq_ref, gq_hbm), (gk_ref, gk_hbm), (gv_ref, gv_hbm))
        return [
            pltpu.make_async_copy(ref.at[:, cols], hbm.at[pl.ds(0, prior), cols], sems.at[at, n])
            for n, (ref, hbm) in enumerate(pairs)
        ]

    @pl.loop(0, width // step)
    def _(at):
        bias = bias_ref[...]
        columns = pair_columns(at, step)
        queries = [side_by_side(q_ref[early, c]) for c in columns]
        cotangents = [side_by_side(do_ref[early, c]) for c in columns]
        keys = [
            jnp.concatenate([far_ref[first, c], near_ref[first, c], k_ref[early, c]], axis=0)
            for c in columns
        ]
        values = [
            jnp.concatenate([far_ref[second, c], near_ref[second, c], v_ref[early, c]], axis=0)
            for c in columns
        ]
        pairs = [
            score_pair(k, q, v, do, bias)
            for k, q, v, do in zip(keys, queries, values, cotangents)
        ]
        weights, _, deltas = softmax_columns(pairs)
        grads = score_grads_of(pairs, weights, deltas)
        for n, c in enumerate(columns):
            w, g = weights[n].astype(jnp.bfloat16), grads[n]
            attn_ref[:, c] = own_diagonal(dot(w, values[n], 0, 0)).astype(jnp.bfloat16)
            gq_ref[:, c] = own_diagonal(dot(g, keys[n], 0, 0)).astype(jnp.bfloat16)
            gk = gk_part_ref[early, c] + dot(g[prior:], queries[n], 1, 0)
            gv = gv_part_ref[early, c] + dot(w[prior:], cotangents[n], 1, 0)
            gk_ref[:, c] = gk.astype(jnp.bfloat16)
            gv_ref[:, c] = gv.astype(jnp.bfloat16)
        for copy in copies(at):
            copy.start()

    for at in range(width // step):
        for copy in copies(at):
            copy.wait()
    for copy in late_copies:
        copy.wait()


def tail_half(prior, low, bias_ref, k_ref, v_ref, gk_part_ref, gv_part_ref, after_ref):
    tok, half = k_ref.shape[0], prior // 2
    far = bias_ref[half - 1 : half, 0:1] == 0.0
    bias = jnp.where(far, bias_ref[...], MASKED)
    first, second, last = slice(0, half), slice(half, prior), slice(tok - prior, tok)
    places = head_columns(0, after_ref.shape[1], 4)
    columns = head_columns(low, low + after_ref.shape[1], 4)
    queries = [side_by_side(after_ref[first, p]) for p in places]
    cotangents = [side_by_side(after_ref[second, p]) for p in places]
    pairs = [
        score_pair(k_ref[last, c], q, v_ref[last, c], do, bias)
        for c, q, do in zip(columns, queries, cotangents)
    ]
    own = [
        (joined(after_ref[half - 16 : half, p][15:]), joined(after_ref[prior - 16 : prior, p][15:]))
        for p in places
    ]
    weights, grads = merged_columns(pairs, own)

    def fill(ref, part_ref, lefts, rights, rows, send):
        for p, c, left, right in zip(places, columns, lefts, rights):
            total = part_ref[last, c] + dot(left, right, 1, 0)
            terms = jnp.where(far, 0.0, after_ref[rows, p].astype(jnp.float32))
            ref[first, p] = total[first].astype(jnp.bfloat16)
            ref[second, p] = (total[second] + terms).astype(jnp.bfloat16)
            send(p, c)

    def unsent(p, c):
        del p, c

    return (
        lambda ref, send=unsent: fill(ref, gv_part_ref, weights, cotangents, second, send),
        lambda ref, send=unsent: fill(ref, gk_part_ref, grads, queries, first, send),
    )


def tail_kernel(prior, bias_ref, k_ref, v_ref, gk_part_ref, gv_part_ref, after_ref, gk_ref, gv_ref):
    fill_gv, fill_gk = tail_half(
        prior, 0, bias_ref, k_ref, v_ref, gk_part_ref, gv_part_ref, after_ref
    )
    fill_gv(gv_ref)
    fill_gk(gk_ref)


def last_kernel(
    prior, bias_ref, k_ref, v_ref, gk_part_ref, gv_part_ref, after_ref, gk_first_ref, gv_first_ref,
    gk_in, gv_in, gk_hbm, gv_hbm, gk_ref, gv_ref, sems,
):
    rows = pl.ds(k_ref.shape[0] - prior, prior)
    low = gk_first_ref.shape[1]
    copies = []

    def send(ref, hbm, cols):
        copies.append(pltpu.make_async_copy(ref, hbm.at[rows, cols], sems.at[len(copies)]))
        copies[-1].start()

    send(gv_first_ref, gv_hbm, pl.ds(0, low))
    send(gk_first_ref, gk_hbm, pl.ds(0, low))
    fill_gv, fill_gk = tail_half(
        prior, low, bias_ref, k_ref, v_ref, gk_part_ref, gv_part_ref, after_ref
    )
    fill_gv(gv_ref, lambda p, c: send(gv_ref.at[:, p], gv_hbm, c))
    fill_gk(gk_ref, lambda p, c: send(gk_ref.at[:, p], gk_hbm, c))
    for copy in copies:
        copy.wait()


def neighbour(value, by):
    peers = lax.axis_size("seq") * lax.axis_size("head")
    pairs = [(i, i + by) for i in range(peers) if 0 <= i + by < peers]
    return lax.ppermute(value, ("seq", "head"), pairs)


def cost(heads, queries, keys, products, moved):
    return pl.CostEstimate(
        flops=2 * heads * queries * keys * HEAD_DIM * products,
        bytes_accessed=moved,
        transcendentals=heads * queries * keys,
    )


def halo_shards(query_in, key_in, value_in, grad_out, module_lengths):
    tok, width = query_in.shape
    prior = tok * lax.axis_size("head") // 8
    step = math.gcd(width, 8 * HEAD_DIM)
    groups = width // step
    anywhere = pl.BlockSpec(memory_space=pl.ANY)
    inside = pl.BlockSpec(memory_space=pltpu.VMEM)
    full16 = jax.ShapeDtypeStruct((tok, width), jnp.bfloat16)

    def near16(rows, columns):
        return pltpu.VMEM((rows, columns), jnp.bfloat16)

    def near32(rows, columns):
        return pltpu.VMEM((rows, columns), jnp.float32)

    def in_hbm(*values):
        return [pltpu.with_memory_space_constraint(value, pltpu.HBM) for value in values]

    def in_vmem(*values):
        return [pltpu.with_memory_space_constraint(value, pltpu.VMEM) for value in values]

    def call(kernel, name, ins, outs, shapes, scratch, work, moved, aliases=None):
        return pl.pallas_call(
            kernel,
            in_specs=ins,
            out_specs=outs,
            out_shape=shapes,
            scratch_shapes=scratch,
            input_output_aliases=aliases or {},
            cost_estimate=cost(*work, moved),
            compiler_params=pltpu.CompilerParams(vmem_limit_bytes=16 * 2**20),
            name=name,
        )

    four = 4 * HEAD_DIM
    near = call(
        functools.partial(pack_kernel, prior), "near_keys",
        [anywhere] * 2, inside, near16(prior, width),
        [pltpu.SemaphoreType.DMA((2, 2))], (0, 0, 0, 0), 4 * prior * width,
    )(*in_hbm(key_in, value_in))
    near = neighbour(near, 1)

    lengths = module_lengths.reshape(1, -1)
    far, q, k, v, do, own_bias, near_bias, lead_bias, tail_bias = call(
        functools.partial(ready_kernel, prior), "operands",
        [anywhere] * 5, [inside] * 9,
        [near16(prior, width)] + [near16(tok, width)] * 4
        + [near32(tok, 2 * prior), near32(prior + prior // 2, 2 * prior)]
        + [near32(2 * prior, 2 * prior), near32(prior, 2 * prior)],
        [
            pltpu.VMEM(lengths.shape, jnp.int32), pltpu.SemaphoreType.DMA((4,)),
            pltpu.SemaphoreType.DMA((2, 1)), pltpu.SemaphoreType.DMA(()),
        ],
        (0, 0, 0, 0), 18 * tok * width,
    )(*in_hbm(lengths, query_in, key_in, value_in, grad_out))
    far = neighbour(far, 1)

    attn, gq, gk_part, gv_part = call(
        functools.partial(own_kernel, prior, step), "own_block",
        [inside] * 5, [inside] * 4,
        [near16(tok - prior, width)] * 2 + [near32(tok, width)] * 2, (),
        (width // HEAD_DIM, tok - prior, tok, 6), 18 * tok * width,
    )(*in_vmem(own_bias, q, k, v, do))

    near_bias, attn = lax.optimization_barrier((near_bias, attn))
    backs = call(
        functools.partial(near_kernel, prior), "near_terms",
        [inside] * 7, [inside] * 2, [near16(prior, width // 2)] * 2, (),
        (width // HEAD_DIM, prior, prior + prior // 2, 3), 8 * tok * width,
    )(*in_vmem(near_bias, lead_bias, q, k, v, do, near))
    backs = [neighbour(back, -1) for back in backs]

    attn, gq, gk, gv = call(
        functools.partial(lead_kernel, prior, step), "lead_rows",
        [inside] * 11, [anywhere] * 4, [full16] * 4,
        [near16(prior, width)] * 4
        + [pltpu.SemaphoreType.DMA((groups, 4)), pltpu.SemaphoreType.DMA((2,))],
        (width // HEAD_DIM, prior, 2 * prior, 6), 20 * tok * width,
    )(*in_vmem(lead_bias, q, k, v, do, near, far, gk_part, gv_part, attn, gq))

    here = in_vmem(tail_bias, k, v, gk_part, gv_part)
    work = (width // HEAD_DIM // 2, prior, prior // 2, 4)
    halves = call(
        functools.partial(tail_kernel, prior), "tail_keys",
        [inside] * 6, [inside] * 2, [near16(prior, width // 2)] * 2, (), work, 4 * tok * width,
    )(*here, *in_vmem(backs[0]))
    gk, gv = call(
        functools.partial(last_kernel, prior), "last_keys",
        [inside] * 8 + [anywhere] * 2, [anywhere] * 2, [full16] * 2,
        [near16(prior, width // 2)] * 2 + [pltpu.SemaphoreType.DMA((2 + width // four,))],
        work, 6 * tok * width, {8: 0, 9: 1},
    )(*here, *in_vmem(backs[1], *halves), gk, gv)
    return (attn, gq, gk, gv)


def shards(query_in, key_in, value_in, grad_out, module_lengths):
    tok = query_in.shape[0]
    prior = tok * lax.axis_size("head") // 8
    plan = halo_shards if 2 * prior == tok else gathered_shards
    return plan(query_in, key_in, value_in, grad_out, module_lengths)


def solution(mesh):
    placed = (
        P(("seq", "head"), None),
        P(("seq", "head"), None),
        P(("seq", "head"), None),
        P(("seq", "head"), None),
        P(),
    )
    return jax.shard_map(
        shards,
        mesh=mesh,
        in_specs=placed,
        out_specs=(
            P(("seq", "head"), None),
            P(("seq", "head"), None),
            P(("seq", "head"), None),
            P(("seq", "head"), None),
        ),
        check_vma=False,
    )
```

```python
import functools
import math

import jax
import jax.numpy as jnp
from jax import lax
from jax.experimental import pallas as pl
from jax.experimental.pallas import tpu as pltpu
from jax.sharding import PartitionSpec as P

HEAD_DIM = 128
SCALE = HEAD_DIM ** (-0.5)
LOG2E = math.log2(math.e)
MASKED = -1e30


def shifted(value, axis, by):
    peers = lax.axis_size(axis)
    pairs = [(i, i + by) for i in range(peers) if 0 <= i + by < peers]
    return lax.ppermute(value, axis, pairs)


def module_ids(module_lengths, positions):
    module_ends = jnp.cumsum(module_lengths)
    counted = jnp.sum((positions[:, None] >= module_ends[None, :]).astype(jnp.int32), axis=1)
    return jnp.where(positions >= 0, counted, -1)


def allowed_pairs(module_lengths, query_pos, key_pos):
    same = (
        module_ids(module_lengths, query_pos)[:, None]
        == module_ids(module_lengths, key_pos)[None, :]
    )
    return same & (key_pos[None, :] <= query_pos[:, None])


def score_grads(grad_rows, value_block, weights, row_delta, score_scale):
    dprobs = jnp.einsum("qd,kd->qk", grad_rows, value_block, preferred_element_type=jnp.float32)
    return (weights * (dprobs - row_delta[:, None]) * score_scale).astype(jnp.bfloat16)


def key_terms(dscores, weight_bf, query_rows, grad_rows):
    key_grad = jnp.einsum("qk,qd->kd", dscores, query_rows, preferred_element_type=jnp.float32)
    value_grad = jnp.einsum("qk,qd->kd", weight_bf, grad_rows, preferred_element_type=jnp.float32)
    return (key_grad, value_grad)


def one_block(query_rows, key_block, value_block, grad_rows, allowed, score_scale):
    scores = (
        jnp.einsum("qd,kd->qk", query_rows, key_block, preferred_element_type=jnp.float32)
        * score_scale
    )
    row_top = jnp.max(jnp.where(allowed, scores, -jnp.inf), axis=1, keepdims=True)
    row_total = jnp.sum(jnp.where(allowed, jnp.exp(scores - row_top), 0.0), axis=1, keepdims=True)
    log_total = row_top + jnp.log(row_total)
    weights = jnp.where(allowed, jnp.exp(scores - log_total), 0.0)
    weight_bf = weights.astype(jnp.bfloat16)
    attn_rows = jnp.einsum(
        "qk,kd->qd", weight_bf, value_block, preferred_element_type=jnp.float32
    ).astype(jnp.bfloat16)
    row_delta = jnp.sum(grad_rows.astype(jnp.float32) * attn_rows.astype(jnp.float32), axis=1)
    dscores = score_grads(grad_rows, value_block, weights, row_delta, score_scale)
    grad_q = jnp.einsum("qk,kd->qd", dscores, key_block, preferred_element_type=jnp.float32).astype(
        jnp.bfloat16
    )
    key_grad, value_grad = key_terms(dscores, weight_bf, query_rows, grad_rows)
    return (attn_rows, grad_q, key_grad, value_grad, log_total[:, 0], row_delta)


def gathered_shards(query_in, key_in, value_in, grad_out, module_lengths):
    head_q, head_k, head_v, head_do = (
        lax.all_to_all(query_in, "head", split_axis=1, concat_axis=0, tiled=True),
        lax.all_to_all(key_in, "head", split_axis=1, concat_axis=0, tiled=True),
        lax.all_to_all(value_in, "head", split_axis=1, concat_axis=0, tiled=True),
        lax.all_to_all(grad_out, "head", split_axis=1, concat_axis=0, tiled=True),
    )
    row_count = head_q.shape[0]
    width = head_q.shape[1]
    local_heads = width // HEAD_DIM
    prior_rows = row_count // 8
    score_scale = HEAD_DIM ** (-0.5)
    tail_start = row_count - prior_rows
    prior_k, prior_v = shifted((head_k[tail_start:], head_v[tail_start:]), "seq", 1)
    row_start = lax.axis_index("seq") * row_count
    query_pos = row_start + jnp.arange(row_count, dtype=jnp.int32)
    before_pos = row_start - prior_rows + jnp.arange(prior_rows, dtype=jnp.int32)
    key_pos = jnp.concatenate([before_pos, query_pos])
    block_rows = math.gcd(row_count, 512)
    block_count = row_count // block_rows
    pos_blocks = query_pos.reshape(block_count, block_rows)

    def by_head(flat, rows):
        return jnp.moveaxis(flat.reshape(rows, local_heads, HEAD_DIM), 1, 0)

    def to_flat(stacked):
        return jnp.moveaxis(stacked, 0, 1).reshape(stacked.shape[1], width)

    query_h = by_head(head_q, row_count)
    grad_h = by_head(head_do, row_count)
    key_h = by_head(jnp.concatenate([prior_k, head_k], axis=0), row_count + prior_rows)
    value_h = by_head(jnp.concatenate([prior_v, head_v], axis=0), row_count + prior_rows)

    def run_head(packed):
        query_rows, key_block, value_block, grad_rows = packed
        query_blocks = query_rows.reshape(block_count, block_rows, HEAD_DIM)
        grad_blocks = grad_rows.reshape(block_count, block_rows, HEAD_DIM)

        def run_block(inner):
            query_part, grad_part, pos_part = inner
            allowed = allowed_pairs(module_lengths, pos_part, key_pos)
            return one_block(query_part, key_block, value_block, grad_part, allowed, score_scale)

        attn_b, grad_qb, key_b, value_b, lse_b, delta_b = lax.map(
            run_block, (query_blocks, grad_blocks, pos_blocks)
        )
        return (
            attn_b.reshape(row_count, HEAD_DIM),
            grad_qb.reshape(row_count, HEAD_DIM),
            jnp.sum(key_b, axis=0),
            jnp.sum(value_b, axis=0),
            lse_b.reshape(row_count),
            delta_b.reshape(row_count),
        )

    attn_h, grad_qh, key_grad, value_grad, log_total, row_delta = lax.map(
        run_head, (query_h, key_h, value_h, grad_h)
    )
    attn_flat = to_flat(attn_h)
    attn_back = lax.all_to_all(attn_flat, "head", split_axis=0, concat_axis=1, tiled=True)
    grad_q = to_flat(grad_qh)
    later_k, later_v = shifted((key_grad[:, :prior_rows], value_grad[:, :prior_rows]), "seq", -1)
    key_total = key_grad[:, prior_rows:].at[:, tail_start:].add(later_k)
    value_total = value_grad[:, prior_rows:].at[:, tail_start:].add(later_v)
    grad_k = to_flat(key_total.astype(jnp.bfloat16))
    grad_v = to_flat(value_total.astype(jnp.bfloat16))
    back_q, back_k, back_v = (
        lax.all_to_all(grad_q, "head", split_axis=0, concat_axis=1, tiled=True),
        lax.all_to_all(grad_k, "head", split_axis=0, concat_axis=1, tiled=True),
        lax.all_to_all(grad_v, "head", split_axis=0, concat_axis=1, tiled=True),
    )
    return (attn_back, back_q, back_k, back_v)


def dot(left, right, left_dim, right_dim):
    return lax.dot_general(
        left, right, (((left_dim,), (right_dim,)), ((), ())), preferred_element_type=jnp.float32
    )


def module_ends_col(lengths_row):
    count = lengths_row.shape[1]
    row = lax.broadcasted_iota(jnp.int32, (count, count), 0)
    col = lax.broadcasted_iota(jnp.int32, (count, count), 1)
    return jnp.sum(jnp.where(col <= row, lengths_row, 0.0), axis=1, keepdims=True)


def bias_by_key(lengths_row, first_query, queries, first_key, keys, heads):
    ends = module_ends_col(lengths_row)
    lane = lax.broadcasted_iota(jnp.int32, (1, heads * queries), 1)
    query = (first_query + lane % queries).astype(jnp.float32)
    start = jnp.max(jnp.where(ends <= query, ends, 0.0), axis=0, keepdims=True)
    key = (first_key + lax.broadcasted_iota(jnp.int32, (keys, heads * queries), 0)).astype(
        jnp.float32
    )
    return jnp.where((key >= start) & (key <= query), 0.0, MASKED)


def score_pair(k, q, v, do, bias):
    return dot(k, q, 1, 1) * (SCALE * LOG2E) + bias, dot(v, do, 1, 1)


def softmax_columns(pairs):
    tops = [jnp.max(s, axis=0, keepdims=True) for s, _ in pairs]
    raws = [jnp.exp2(s - top) for (s, _), top in zip(pairs, tops)]
    totals = [jnp.sum(raw, axis=0, keepdims=True) for raw in raws]
    weights = [raw * (1.0 / total) for raw, total in zip(raws, totals)]
    deltas = [jnp.sum(w * dp, axis=0, keepdims=True) for w, (_, dp) in zip(weights, pairs)]
    logs = [top + jnp.log2(total) for top, total in zip(tops, totals)]
    return weights, logs, deltas


def score_grads_of(pairs, weights, deltas):
    return [
        (w * (dp - delta) * SCALE).astype(jnp.bfloat16)
        for w, (_, dp), delta in zip(weights, pairs, deltas)
    ]


def merged_columns(pairs, own):
    tops = [
        jnp.maximum(jnp.max(s, axis=0, keepdims=True), log) for (s, _), (log, _) in zip(pairs, own)
    ]
    raws = [jnp.exp2(s - top) for (s, _), top in zip(pairs, tops)]
    own_raws = [jnp.exp2(log - top) for (log, _), top in zip(own, tops)]
    parts = [
        1.0 / (jnp.sum(raw, axis=0, keepdims=True) + own_raw)
        for raw, own_raw in zip(raws, own_raws)
    ]
    weights = [raw * part for raw, part in zip(raws, parts)]
    deltas = [
        jnp.sum(w * dp, axis=0, keepdims=True) + own_raw * part * own_delta
        for w, (_, dp), own_raw, part, (_, own_delta) in zip(weights, pairs, own_raws, parts, own)
    ]
    grads = [w * (dp - delta) * SCALE for w, (_, dp), delta in zip(weights, pairs, deltas)]
    return [w.astype(jnp.bfloat16) for w in weights], [g.astype(jnp.bfloat16) for g in grads]


def side_by_side(rows):
    heads = rows.shape[1] // HEAD_DIM
    zero = jnp.zeros((rows.shape[0], HEAD_DIM), rows.dtype)
    blocks = [rows[:, c] for c in head_columns(0, rows.shape[1])]
    return jnp.concatenate(
        [
            jnp.concatenate([blocks[h] if g == h else zero for g in range(heads)], axis=1)
            for h in range(heads)
        ],
        axis=0,
    )


def head_columns(low, high, heads=1):
    wide = heads * HEAD_DIM
    return [slice(c, c + wide) for c in range(low, high, wide)]


def device_first(tok):
    place = lax.axis_index("seq") * lax.axis_size("head") + lax.axis_index("head")
    return place * tok


def fours(rows):
    table = jnp.concatenate(rows, axis=0)
    half = table.shape[1] // 4
    lane = lax.broadcasted_iota(jnp.int32, (1, table.shape[1]), 1)
    turned = [pltpu.roll(table, turn * half, 1) for turn in (3, 2, 1)]
    merged = []
    for at in range(0, len(rows), 2):
        now, after = slice(at, at + 1), slice(at + 1, at + 2)
        row = jnp.where(lane < 3 * half, turned[1][after], turned[2][after])
        row = jnp.where(lane < 2 * half, turned[0][now], row)
        merged.append(jnp.where(lane < half, table[now], row))
    return merged


def split_bf16(row):
    parts = []
    for _ in range(3):
        part = row.astype(jnp.bfloat16)
        parts.append(part)
        row = row - part.astype(jnp.float32)
    return jnp.concatenate([*parts, jnp.zeros_like(parts[0])], axis=1)


def joined(parts):
    parts = parts.astype(jnp.float32)
    count = parts.shape[1] // 4
    return parts[:, :count] + parts[:, count : 2 * count] + parts[:, 2 * count : 3 * count]


def pack_copies(prior, at, k_ref, v_ref, packed_ref, sems):
    half, tok = prior // 2, k_ref.shape[0]
    rows = pl.ds(tok - (at + 1) * half, half)
    return [
        pltpu.make_async_copy(
            ref.at[rows, :], packed_ref.at[pl.ds(n * half, half), :], sems.at[n]
        )
        for n, ref in enumerate((k_ref, v_ref))
    ]


def pack_kernel(prior, odd, k_ref, v_ref, near_ref, sems):
    @pl.when(lax.axis_index("head") % 2 == odd)
    def _():
        copies = pack_copies(prior, 0, k_ref, v_ref, near_ref, sems)
        for copy in copies:
            copy.start()
        for copy in copies:
            copy.wait()


def ready_kernel(
    prior, len_hbm, q_hbm, k_hbm, v_hbm, do_hbm, far_ref, q_ref, k_ref, v_ref, do_ref,
    own_bias_ref, near_bias_ref, lead_bias_ref, tail_bias_ref, len_ref, sems, far_sems, len_sem,
):
    tok, half = k_ref.shape[0], prior // 2
    pairs = ((q_hbm, q_ref), (k_hbm, k_ref), (v_hbm, v_ref), (do_hbm, do_ref))
    copies = pack_copies(prior, 1, k_hbm, v_hbm, far_ref, far_sems)
    copies += [pltpu.make_async_copy(hbm, ref, sems.at[n]) for n, (hbm, ref) in enumerate(pairs)]
    len_copy = pltpu.make_async_copy(len_hbm, len_ref, len_sem)
    len_copy.start()
    for copy in copies:
        copy.start()
    len_copy.wait()
    first = device_first(tok)
    lengths = len_ref[...].astype(jnp.float32)
    own_bias_ref[...] = bias_by_key(lengths, first + prior, tok - prior, first, tok, 2)
    near_bias_ref[...] = bias_by_key(lengths, first, prior, first - half, prior + half, 2)
    lead_bias_ref[...] = bias_by_key(lengths, first, prior, first - prior, 2 * prior, 2)
    tail_bias_ref[...] = bias_by_key(lengths, first + tok, half, first + tok - prior, prior, 4)
    for copy in copies:
        copy.wait()


def own_diagonal(both):
    rows = both.shape[0] // 2
    return jnp.concatenate([both[:rows, :HEAD_DIM], both[rows:, HEAD_DIM:]], axis=1)


def pair_columns(at, step):
    wide = 2 * HEAD_DIM
    return [pl.ds(pl.multiple_of(at * step + c, wide), wide) for c in range(0, step, wide)]


def own_kernel(
    prior, step, bias_ref, q_ref, k_ref, v_ref, do_ref, attn_ref, gq_ref, gk_ref, gv_ref
):
    tok, width = k_ref.shape
    late = slice(prior, tok)

    @pl.loop(0, width // step)
    def _(at):
        bias = bias_ref[...]
        columns = pair_columns(at, step)
        queries = [side_by_side(q_ref[late, c]) for c in columns]
        cotangents = [side_by_side(do_ref[late, c]) for c in columns]
        pairs = [
            score_pair(k_ref[:, c], q, v_ref[:, c], do, bias)
            for c, q, do in zip(columns, queries, cotangents)
        ]
        weights, _, deltas = softmax_columns(pairs)
        grads = score_grads_of(pairs, weights, deltas)
        for c, w, g, q, do in zip(columns, weights, grads, queries, cotangents):
            w = w.astype(jnp.bfloat16)
            attn_ref[:, c] = own_diagonal(dot(w, v_ref[:, c], 0, 0)).astype(jnp.bfloat16)
            gq_ref[:, c] = own_diagonal(dot(g, k_ref[:, c], 0, 0)).astype(jnp.bfloat16)
            gk_ref[:, c] = dot(g, q, 1, 0)
            gv_ref[:, c] = dot(w, do, 1, 0)


def came(odd_ref, even_ref, rows, cols):
    to_odd = lax.axis_index("head") % 2 == 1
    return jnp.where(to_odd, even_ref[rows, cols], odd_ref[rows, cols])


def near_kernel(
    prior, near_bias_ref, lead_bias_ref, q_ref, k_ref, v_ref, do_ref, near_odd_ref, near_even_ref,
    *back_refs,
):
    width, half = q_ref.shape[1], prior // 2
    far = lead_bias_ref[half - 1 : half, 0:1] == 0.0
    key = lax.broadcasted_iota(jnp.int32, (prior + half, 1), 0)
    bias = jnp.where(far & (key < half), MASKED, near_bias_ref[...])
    spare = lax.broadcasted_iota(jnp.int32, (half, 1), 0) == half - 1
    early, first, second = slice(0, prior), slice(0, half), slice(half, prior)
    columns = head_columns(0, width, 2)
    queries = [side_by_side(q_ref[early, c]) for c in columns]
    cotangents = [side_by_side(do_ref[early, c]) for c in columns]
    pairs = []
    for c, q, do in zip(columns, queries, cotangents):
        k = jnp.concatenate([came(near_odd_ref, near_even_ref, first, c), k_ref[early, c]], axis=0)
        v = jnp.concatenate([came(near_odd_ref, near_even_ref, second, c), v_ref[early, c]], axis=0)
        pairs.append(score_pair(k, q, v, do, bias))
    weights, logs, deltas = softmax_columns(pairs)
    weights = [w[:half] for w in weights]
    grads = score_grads_of([(s[:half], dp[:half]) for s, dp in pairs], weights, deltas)
    k_terms = [dot(g, q, 1, 0) for g, q in zip(grads, queries)]
    v_terms = [dot(w.astype(jnp.bfloat16), do, 1, 0) for w, do in zip(weights, cotangents)]
    logs, deltas = fours(logs), fours(deltas)
    for at, c in enumerate(head_columns(0, width, 4)):
        back_ref = back_refs[c.start * len(back_refs) // width]
        low = c.start % back_ref.shape[1]
        here = slice(low, low + c.stop - c.start)
        for row, terms, ref, place in (
            (logs[at], k_terms, q_ref, first), (deltas[at], v_terms, do_ref, second)
        ):
            rows = jnp.where(spare, split_bf16(row), ref[first, c])
            terms = jnp.concatenate(terms[2 * at : 2 * at + 2], axis=1).astype(jnp.bfloat16)
            back_ref[place, here] = jnp.where(far, rows, terms)


def lead_kernel(
    prior, step, bias_ref, q_ref, k_ref, v_ref, do_ref, near_odd_ref, near_even_ref, far_ref,
    gk_part_ref, gv_part_ref, attn_late_ref, gq_late_ref, attn_hbm, gq_hbm, gk_hbm, gv_hbm,
    attn_ref, gq_ref, gk_ref, gv_ref, sems, late_sems,
):
    tok, width = q_ref.shape
    half = prior // 2
    early, first, second = slice(0, prior), slice(0, half), slice(half, prior)
    late = pl.ds(prior, tok - prior)
    late_copies = [
        pltpu.make_async_copy(attn_late_ref, attn_hbm.at[late, :], late_sems.at[0]),
        pltpu.make_async_copy(gq_late_ref, gq_hbm.at[late, :], late_sems.at[1]),
    ]
    for copy in late_copies:
        copy.start()

    def copies(at):
        cols = pl.ds(pl.multiple_of(at * step, step), step)
        pairs = ((attn_ref, attn_hbm), (gq_ref, gq_hbm), (gk_ref, gk_hbm), (gv_ref, gv_hbm))
        return [
            pltpu.make_async_copy(ref.at[:, cols], hbm.at[pl.ds(0, prior), cols], sems.at[at, n])
            for n, (ref, hbm) in enumerate(pairs)
        ]

    @pl.loop(0, width // step)
    def _(at):
        bias = bias_ref[...]
        columns = pair_columns(at, step)
        queries = [side_by_side(q_ref[early, c]) for c in columns]
        cotangents = [side_by_side(do_ref[early, c]) for c in columns]
        keys = [
            jnp.concatenate(
                [far_ref[first, c], came(near_odd_ref, near_even_ref, first, c), k_ref[early, c]],
                axis=0,
            )
            for c in columns
        ]
        values = [
            jnp.concatenate(
                [far_ref[second, c], came(near_odd_ref, near_even_ref, second, c), v_ref[early, c]],
                axis=0,
            )
            for c in columns
        ]
        pairs = [
            score_pair(k, q, v, do, bias)
            for k, q, v, do in zip(keys, queries, values, cotangents)
        ]
        weights, _, deltas = softmax_columns(pairs)
        grads = score_grads_of(pairs, weights, deltas)
        for n, c in enumerate(columns):
            w, g = weights[n].astype(jnp.bfloat16), grads[n]
            attn_ref[:, c] = own_diagonal(dot(w, values[n], 0, 0)).astype(jnp.bfloat16)
            gq_ref[:, c] = own_diagonal(dot(g, keys[n], 0, 0)).astype(jnp.bfloat16)
            gk = gk_part_ref[early, c] + dot(g[prior:], queries[n], 1, 0)
            gv = gv_part_ref[early, c] + dot(w[prior:], cotangents[n], 1, 0)
            gk_ref[:, c] = gk.astype(jnp.bfloat16)
            gv_ref[:, c] = gv.astype(jnp.bfloat16)
        for copy in copies(at):
            copy.start()

    for at in range(width // step):
        for copy in copies(at):
            copy.wait()
    for copy in late_copies:
        copy.wait()


def tail_half(prior, low, bias_ref, k_ref, v_ref, gk_part_ref, gv_part_ref, after_ref):
    tok, half = k_ref.shape[0], prior // 2
    far = bias_ref[half - 1 : half, 0:1] == 0.0
    bias = jnp.where(far, bias_ref[...], MASKED)
    first, second, last = slice(0, half), slice(half, prior), slice(tok - prior, tok)
    places = head_columns(0, after_ref.shape[1], 4)
    columns = head_columns(low, low + after_ref.shape[1], 4)
    queries = [side_by_side(after_ref[first, p]) for p in places]
    cotangents = [side_by_side(after_ref[second, p]) for p in places]
    pairs = [
        score_pair(k_ref[last, c], q, v_ref[last, c], do, bias)
        for c, q, do in zip(columns, queries, cotangents)
    ]
    own = [
        (joined(after_ref[half - 16 : half, p][15:]), joined(after_ref[prior - 16 : prior, p][15:]))
        for p in places
    ]
    weights, grads = merged_columns(pairs, own)

    def fill(ref, part_ref, lefts, rights, rows):
        for p, c, left, right in zip(places, columns, lefts, rights):
            total = part_ref[last, c] + dot(left, right, 1, 0)
            terms = jnp.where(far, 0.0, after_ref[rows, p].astype(jnp.float32))
            ref[first, p] = total[first].astype(jnp.bfloat16)
            ref[second, p] = (total[second] + terms).astype(jnp.bfloat16)

    return (
        lambda ref: fill(ref, gv_part_ref, weights, cotangents, second),
        lambda ref: fill(ref, gk_part_ref, grads, queries, first),
    )


def tail_kernel(prior, bias_ref, k_ref, v_ref, gk_part_ref, gv_part_ref, after_ref, gk_ref, gv_ref):
    fill_gv, fill_gk = tail_half(
        prior, 0, bias_ref, k_ref, v_ref, gk_part_ref, gv_part_ref, after_ref
    )
    fill_gv(gv_ref)
    fill_gk(gk_ref)


def last_kernel(
    prior, bias_ref, k_ref, v_ref, gk_part_ref, gv_part_ref, after_ref, gk_first_ref, gv_first_ref,
    gk_in, gv_in, gk_hbm, gv_hbm, gk_ref, gv_ref, sems,
):
    rows = pl.ds(k_ref.shape[0] - prior, prior)
    low = gk_first_ref.shape[1]
    copies = []

    def send(ref, hbm, start):
        cols = pl.ds(start, ref.shape[1])
        copies.append(pltpu.make_async_copy(ref, hbm.at[rows, cols], sems.at[len(copies)]))
        copies[-1].start()

    send(gv_first_ref, gv_hbm, 0)
    send(gk_first_ref, gk_hbm, 0)
    fill_gv, fill_gk = tail_half(
        prior, low, bias_ref, k_ref, v_ref, gk_part_ref, gv_part_ref, after_ref
    )
    fill_gv(gv_ref)
    send(gv_ref, gv_hbm, low)
    fill_gk(gk_ref)
    send(gk_ref, gk_hbm, low)
    for copy in copies:
        copy.wait()


def neighbour(value, by, sources=(0, 1)):
    peers = lax.axis_size("seq") * lax.axis_size("head")
    pairs = [(i, i + by) for i in range(peers) if 0 <= i + by < peers and i % 2 in sources]
    return lax.ppermute(value, ("seq", "head"), pairs)


def cost(heads, queries, keys, products, moved):
    return pl.CostEstimate(
        flops=2 * heads * queries * keys * HEAD_DIM * products,
        bytes_accessed=moved,
        transcendentals=heads * queries * keys,
    )


def halo_shards(query_in, key_in, value_in, grad_out, module_lengths):
    tok, width = query_in.shape
    prior = tok * lax.axis_size("head") // 8
    step = math.gcd(width, 8 * HEAD_DIM)
    groups = width // step
    anywhere = pl.BlockSpec(memory_space=pl.ANY)
    inside = pl.BlockSpec(memory_space=pltpu.VMEM)
    full16 = jax.ShapeDtypeStruct((tok, width), jnp.bfloat16)

    def near16(rows, columns):
        return pltpu.VMEM((rows, columns), jnp.bfloat16)

    def near32(rows, columns):
        return pltpu.VMEM((rows, columns), jnp.float32)

    def in_hbm(*values):
        return [pltpu.with_memory_space_constraint(value, pltpu.HBM) for value in values]

    def in_vmem(*values):
        return [pltpu.with_memory_space_constraint(value, pltpu.VMEM) for value in values]

    def call(kernel, name, ins, outs, shapes, scratch, work, moved, aliases=None):
        return pl.pallas_call(
            kernel,
            in_specs=ins,
            out_specs=outs,
            out_shape=shapes,
            scratch_shapes=scratch,
            input_output_aliases=aliases or {},
            cost_estimate=cost(*work, moved),
            compiler_params=pltpu.CompilerParams(vmem_limit_bytes=16 * 2**20),
            name=name,
        )

    nears = [
        neighbour(
            call(
                functools.partial(pack_kernel, prior, odd), "near_keys",
                [anywhere] * 2, inside, near16(prior, width),
                [pltpu.SemaphoreType.DMA((2,))], (0, 0, 0, 0), 4 * prior * width,
            )(*in_hbm(key_in, value_in)),
            1, (odd,),
        )
        for odd in (1, 0)
    ]

    lengths = module_lengths.reshape(1, -1)
    far, q, k, v, do, own_bias, near_bias, lead_bias, tail_bias = call(
        functools.partial(ready_kernel, prior), "operands",
        [anywhere] * 5, [inside] * 9,
        [near16(prior, width)] + [near16(tok, width)] * 4
        + [near32(tok, 2 * prior), near32(prior + prior // 2, 2 * prior)]
        + [near32(2 * prior, 2 * prior), near32(prior, 2 * prior)],
        [
            pltpu.VMEM(lengths.shape, jnp.int32), pltpu.SemaphoreType.DMA((4,)),
            pltpu.SemaphoreType.DMA((2,)), pltpu.SemaphoreType.DMA(()),
        ],
        (0, 0, 0, 0), 18 * tok * width,
    )(*in_hbm(lengths, query_in, key_in, value_in, grad_out))
    far = neighbour(far, 1)

    attn, gq, gk_part, gv_part = call(
        functools.partial(own_kernel, prior, step), "own_block",
        [inside] * 5, [inside] * 4,
        [near16(tok - prior, width)] * 2 + [near32(tok, width)] * 2, (),
        (width // HEAD_DIM, tok - prior, tok, 6), 18 * tok * width,
    )(*in_vmem(own_bias, q, k, v, do))

    near_bias, attn = lax.optimization_barrier((near_bias, attn))
    backs = call(
        functools.partial(near_kernel, prior), "near_terms",
        [inside] * 8, [inside] * 2, [near16(prior, width // 2)] * 2, (),
        (width // HEAD_DIM, prior, prior + prior // 2, 3), 8 * tok * width,
    )(*in_vmem(near_bias, lead_bias, q, k, v, do, *nears))
    backs = [neighbour(back, -1) for back in backs]

    attn, gq, gk, gv = call(
        functools.partial(lead_kernel, prior, step), "lead_rows",
        [inside] * 12, [anywhere] * 4, [full16] * 4,
        [near16(prior, width)] * 4
        + [pltpu.SemaphoreType.DMA((groups, 4)), pltpu.SemaphoreType.DMA((2,))],
        (width // HEAD_DIM, prior, 2 * prior, 6), 20 * tok * width,
    )(*in_vmem(lead_bias, q, k, v, do, *nears, far, gk_part, gv_part, attn, gq))

    here = in_vmem(tail_bias, k, v, gk_part, gv_part)
    work = (width // HEAD_DIM // 2, prior, prior // 2, 4)
    halves = call(
        functools.partial(tail_kernel, prior), "tail_keys",
        [inside] * 6, [inside] * 2, [near16(prior, width // 2)] * 2, (), work, 4 * tok * width,
    )(*here, *in_vmem(backs[0]))
    gk, gv = call(
        functools.partial(last_kernel, prior), "last_keys",
        [inside] * 8 + [anywhere] * 2, [anywhere] * 2, [full16] * 2,
        [near16(prior, width // 2)] * 2 + [pltpu.SemaphoreType.DMA((4,))],
        work, 6 * tok * width, {8: 0, 9: 1},
    )(*here, *in_vmem(backs[1], *halves), gk, gv)
    return (attn, gq, gk, gv)


def shards(query_in, key_in, value_in, grad_out, module_lengths):
    tok = query_in.shape[0]
    prior = tok * lax.axis_size("head") // 8
    plan = halo_shards if 2 * prior == tok else gathered_shards
    return plan(query_in, key_in, value_in, grad_out, module_lengths)


def solution(mesh):
    placed = (
        P(("seq", "head"), None),
        P(("seq", "head"), None),
        P(("seq", "head"), None),
        P(("seq", "head"), None),
        P(),
    )
    return jax.shard_map(
        shards,
        mesh=mesh,
        in_specs=placed,
        out_specs=(
            P(("seq", "head"), None),
            P(("seq", "head"), None),
            P(("seq", "head"), None),
            P(("seq", "head"), None),
        ),
        check_vma=False,
    )
```

```python
import functools
import math

import jax
import jax.numpy as jnp
from jax import lax
from jax.experimental import pallas as pl
from jax.experimental.pallas import tpu as pltpu
from jax.sharding import PartitionSpec as P

HEAD_DIM = 128
SCALE = HEAD_DIM ** (-0.5)
LOG2E = math.log2(math.e)
MASKED = -1e30


def shifted(value, axis, by):
    peers = lax.axis_size(axis)
    pairs = [(i, i + by) for i in range(peers) if 0 <= i + by < peers]
    return lax.ppermute(value, axis, pairs)


def module_ids(module_lengths, positions):
    module_ends = jnp.cumsum(module_lengths)
    counted = jnp.sum((positions[:, None] >= module_ends[None, :]).astype(jnp.int32), axis=1)
    return jnp.where(positions >= 0, counted, -1)


def allowed_pairs(module_lengths, query_pos, key_pos):
    same = (
        module_ids(module_lengths, query_pos)[:, None]
        == module_ids(module_lengths, key_pos)[None, :]
    )
    return same & (key_pos[None, :] <= query_pos[:, None])


def score_grads(grad_rows, value_block, weights, row_delta, score_scale):
    dprobs = jnp.einsum("qd,kd->qk", grad_rows, value_block, preferred_element_type=jnp.float32)
    return (weights * (dprobs - row_delta[:, None]) * score_scale).astype(jnp.bfloat16)


def key_terms(dscores, weight_bf, query_rows, grad_rows):
    key_grad = jnp.einsum("qk,qd->kd", dscores, query_rows, preferred_element_type=jnp.float32)
    value_grad = jnp.einsum("qk,qd->kd", weight_bf, grad_rows, preferred_element_type=jnp.float32)
    return (key_grad, value_grad)


def one_block(query_rows, key_block, value_block, grad_rows, allowed, score_scale):
    scores = (
        jnp.einsum("qd,kd->qk", query_rows, key_block, preferred_element_type=jnp.float32)
        * score_scale
    )
    row_top = jnp.max(jnp.where(allowed, scores, -jnp.inf), axis=1, keepdims=True)
    row_total = jnp.sum(jnp.where(allowed, jnp.exp(scores - row_top), 0.0), axis=1, keepdims=True)
    log_total = row_top + jnp.log(row_total)
    weights = jnp.where(allowed, jnp.exp(scores - log_total), 0.0)
    weight_bf = weights.astype(jnp.bfloat16)
    attn_rows = jnp.einsum(
        "qk,kd->qd", weight_bf, value_block, preferred_element_type=jnp.float32
    ).astype(jnp.bfloat16)
    row_delta = jnp.sum(grad_rows.astype(jnp.float32) * attn_rows.astype(jnp.float32), axis=1)
    dscores = score_grads(grad_rows, value_block, weights, row_delta, score_scale)
    grad_q = jnp.einsum("qk,kd->qd", dscores, key_block, preferred_element_type=jnp.float32).astype(
        jnp.bfloat16
    )
    key_grad, value_grad = key_terms(dscores, weight_bf, query_rows, grad_rows)
    return (attn_rows, grad_q, key_grad, value_grad, log_total[:, 0], row_delta)


def gathered_shards(query_in, key_in, value_in, grad_out, module_lengths):
    head_q, head_k, head_v, head_do = (
        lax.all_to_all(query_in, "head", split_axis=1, concat_axis=0, tiled=True),
        lax.all_to_all(key_in, "head", split_axis=1, concat_axis=0, tiled=True),
        lax.all_to_all(value_in, "head", split_axis=1, concat_axis=0, tiled=True),
        lax.all_to_all(grad_out, "head", split_axis=1, concat_axis=0, tiled=True),
    )
    row_count = head_q.shape[0]
    width = head_q.shape[1]
    local_heads = width // HEAD_DIM
    prior_rows = row_count // 8
    score_scale = HEAD_DIM ** (-0.5)
    tail_start = row_count - prior_rows
    prior_k, prior_v = shifted((head_k[tail_start:], head_v[tail_start:]), "seq", 1)
    row_start = lax.axis_index("seq") * row_count
    query_pos = row_start + jnp.arange(row_count, dtype=jnp.int32)
    before_pos = row_start - prior_rows + jnp.arange(prior_rows, dtype=jnp.int32)
    key_pos = jnp.concatenate([before_pos, query_pos])
    block_rows = math.gcd(row_count, 512)
    block_count = row_count // block_rows
    pos_blocks = query_pos.reshape(block_count, block_rows)

    def by_head(flat, rows):
        return jnp.moveaxis(flat.reshape(rows, local_heads, HEAD_DIM), 1, 0)

    def to_flat(stacked):
        return jnp.moveaxis(stacked, 0, 1).reshape(stacked.shape[1], width)

    query_h = by_head(head_q, row_count)
    grad_h = by_head(head_do, row_count)
    key_h = by_head(jnp.concatenate([prior_k, head_k], axis=0), row_count + prior_rows)
    value_h = by_head(jnp.concatenate([prior_v, head_v], axis=0), row_count + prior_rows)

    def run_head(packed):
        query_rows, key_block, value_block, grad_rows = packed
        query_blocks = query_rows.reshape(block_count, block_rows, HEAD_DIM)
        grad_blocks = grad_rows.reshape(block_count, block_rows, HEAD_DIM)

        def run_block(inner):
            query_part, grad_part, pos_part = inner
            allowed = allowed_pairs(module_lengths, pos_part, key_pos)
            return one_block(query_part, key_block, value_block, grad_part, allowed, score_scale)

        attn_b, grad_qb, key_b, value_b, lse_b, delta_b = lax.map(
            run_block, (query_blocks, grad_blocks, pos_blocks)
        )
        return (
            attn_b.reshape(row_count, HEAD_DIM),
            grad_qb.reshape(row_count, HEAD_DIM),
            jnp.sum(key_b, axis=0),
            jnp.sum(value_b, axis=0),
            lse_b.reshape(row_count),
            delta_b.reshape(row_count),
        )

    attn_h, grad_qh, key_grad, value_grad, log_total, row_delta = lax.map(
        run_head, (query_h, key_h, value_h, grad_h)
    )
    attn_flat = to_flat(attn_h)
    attn_back = lax.all_to_all(attn_flat, "head", split_axis=0, concat_axis=1, tiled=True)
    grad_q = to_flat(grad_qh)
    later_k, later_v = shifted((key_grad[:, :prior_rows], value_grad[:, :prior_rows]), "seq", -1)
    key_total = key_grad[:, prior_rows:].at[:, tail_start:].add(later_k)
    value_total = value_grad[:, prior_rows:].at[:, tail_start:].add(later_v)
    grad_k = to_flat(key_total.astype(jnp.bfloat16))
    grad_v = to_flat(value_total.astype(jnp.bfloat16))
    back_q, back_k, back_v = (
        lax.all_to_all(grad_q, "head", split_axis=0, concat_axis=1, tiled=True),
        lax.all_to_all(grad_k, "head", split_axis=0, concat_axis=1, tiled=True),
        lax.all_to_all(grad_v, "head", split_axis=0, concat_axis=1, tiled=True),
    )
    return (attn_back, back_q, back_k, back_v)


def dot(left, right, left_dim, right_dim):
    return lax.dot_general(
        left, right, (((left_dim,), (right_dim,)), ((), ())), preferred_element_type=jnp.float32
    )


def module_ends_col(lengths_row):
    count = lengths_row.shape[1]
    row = lax.broadcasted_iota(jnp.int32, (count, count), 0)
    col = lax.broadcasted_iota(jnp.int32, (count, count), 1)
    return jnp.sum(jnp.where(col <= row, lengths_row, 0.0), axis=1, keepdims=True)


def bias_by_key(lengths_row, first_query, queries, first_key, keys, heads):
    ends = module_ends_col(lengths_row)
    lane = lax.broadcasted_iota(jnp.int32, (1, heads * queries), 1)
    query = (first_query + lane % queries).astype(jnp.float32)
    start = jnp.max(jnp.where(ends <= query, ends, 0.0), axis=0, keepdims=True)
    key = (first_key + lax.broadcasted_iota(jnp.int32, (keys, heads * queries), 0)).astype(
        jnp.float32
    )
    return jnp.where((key >= start) & (key <= query), 0.0, MASKED)


def score_pair(k, q, v, do, bias):
    return dot(k, q, 1, 1) * (SCALE * LOG2E) + bias, dot(v, do, 1, 1)


def softmax_columns(pairs):
    tops = [jnp.max(s, axis=0, keepdims=True) for s, _ in pairs]
    raws = [jnp.exp2(s - top) for (s, _), top in zip(pairs, tops)]
    totals = [jnp.sum(raw, axis=0, keepdims=True) for raw in raws]
    weights = [raw * (1.0 / total) for raw, total in zip(raws, totals)]
    deltas = [jnp.sum(w * dp, axis=0, keepdims=True) for w, (_, dp) in zip(weights, pairs)]
    logs = [top + jnp.log2(total) for top, total in zip(tops, totals)]
    return weights, logs, deltas


def score_grads_of(pairs, weights, deltas):
    return [
        (w * (dp - delta) * SCALE).astype(jnp.bfloat16)
        for w, (_, dp), delta in zip(weights, pairs, deltas)
    ]


def merged_columns(pairs, own):
    tops = [
        jnp.maximum(jnp.max(s, axis=0, keepdims=True), log) for (s, _), (log, _) in zip(pairs, own)
    ]
    raws = [jnp.exp2(s - top) for (s, _), top in zip(pairs, tops)]
    own_raws = [jnp.exp2(log - top) for (log, _), top in zip(own, tops)]
    parts = [
        1.0 / (jnp.sum(raw, axis=0, keepdims=True) + own_raw)
        for raw, own_raw in zip(raws, own_raws)
    ]
    weights = [raw * part for raw, part in zip(raws, parts)]
    deltas = [
        jnp.sum(w * dp, axis=0, keepdims=True) + own_raw * part * own_delta
        for w, (_, dp), own_raw, part, (_, own_delta) in zip(weights, pairs, own_raws, parts, own)
    ]
    grads = [w * (dp - delta) * SCALE for w, (_, dp), delta in zip(weights, pairs, deltas)]
    return [w.astype(jnp.bfloat16) for w in weights], [g.astype(jnp.bfloat16) for g in grads]


def side_by_side(rows):
    heads = rows.shape[1] // HEAD_DIM
    zero = jnp.zeros((rows.shape[0], HEAD_DIM), rows.dtype)
    blocks = [rows[:, c] for c in head_columns(0, rows.shape[1])]
    return jnp.concatenate(
        [
            jnp.concatenate([blocks[h] if g == h else zero for g in range(heads)], axis=1)
            for h in range(heads)
        ],
        axis=0,
    )


def head_columns(low, high, heads=1):
    wide = heads * HEAD_DIM
    return [slice(c, c + wide) for c in range(low, high, wide)]


def device_first(tok):
    place = lax.axis_index("seq") * lax.axis_size("head") + lax.axis_index("head")
    return place * tok


def fours(rows):
    table = jnp.concatenate(rows, axis=0)
    half = table.shape[1] // 4
    lane = lax.broadcasted_iota(jnp.int32, (1, table.shape[1]), 1)
    turned = [pltpu.roll(table, turn * half, 1) for turn in (3, 2, 1)]
    merged = []
    for at in range(0, len(rows), 2):
        now, after = slice(at, at + 1), slice(at + 1, at + 2)
        row = jnp.where(lane < 3 * half, turned[1][after], turned[2][after])
        row = jnp.where(lane < 2 * half, turned[0][now], row)
        merged.append(jnp.where(lane < half, table[now], row))
    return merged


def split_bf16(row):
    parts = []
    for _ in range(3):
        part = row.astype(jnp.bfloat16)
        parts.append(part)
        row = row - part.astype(jnp.float32)
    return jnp.concatenate([*parts, jnp.zeros_like(parts[0])], axis=1)


def joined(parts):
    parts = parts.astype(jnp.float32)
    count = parts.shape[1] // 4
    return parts[:, :count] + parts[:, count : 2 * count] + parts[:, 2 * count : 3 * count]


def pack_copies(prior, at, k_ref, v_ref, packed_ref, sems):
    half, tok = prior // 2, k_ref.shape[0]
    rows = pl.ds(tok - (at + 1) * half, half)
    return [
        pltpu.make_async_copy(
            ref.at[rows, :], packed_ref.at[pl.ds(n * half, half), :], sems.at[n]
        )
        for n, ref in enumerate((k_ref, v_ref))
    ]


def pack_kernel(prior, k_ref, v_ref, near_ref, far_ref, near_sems, far_sems):
    copies = pack_copies(prior, 0, k_ref, v_ref, near_ref, near_sems)
    copies += pack_copies(prior, 1, k_ref, v_ref, far_ref, far_sems)
    for copy in copies:
        copy.start()
    for copy in copies:
        copy.wait()


def ready_kernel(prior, first_place, len_hbm, q_hbm, k_hbm, v_hbm, do_hbm, *refs):
    (
        q_ref, k_ref, v_ref, do_ref, own_bias_ref, near_bias_ref, lead_bias_ref, tail_bias_ref,
        len_ref, sems, len_sem,
    ) = refs[-11:]
    tok, half = k_ref.shape[0], prior // 2
    pairs = ((q_hbm, q_ref), (k_hbm, k_ref), (v_hbm, v_ref), (do_hbm, do_ref))

    @pl.when((lax.axis_index("head") == 0) == first_place)
    def _():
        copies = [pltpu.make_async_copy(hbm, ref, sems.at[n]) for n, (hbm, ref) in enumerate(pairs)]
        len_copy = pltpu.make_async_copy(len_hbm, len_ref, len_sem)
        len_copy.start()
        for copy in copies:
            copy.start()
        len_copy.wait()
        first = device_first(tok)
        lengths = len_ref[...].astype(jnp.float32)
        own_bias_ref[...] = bias_by_key(lengths, first + prior, tok - prior, first, tok, 2)
        near_bias_ref[...] = bias_by_key(lengths, first, prior, first - half, prior + half, 2)
        lead_bias_ref[...] = bias_by_key(lengths, first, prior, first - prior, 2 * prior, 2)
        tail_bias_ref[...] = bias_by_key(
            lengths, first + tok, half, first + tok - prior, prior, 4
        )
        for copy in copies:
            copy.wait()


def own_diagonal(both):
    rows = both.shape[0] // 2
    return jnp.concatenate([both[:rows, :HEAD_DIM], both[rows:, HEAD_DIM:]], axis=1)


def pair_columns(at, step):
    wide = 2 * HEAD_DIM
    return [pl.ds(pl.multiple_of(at * step + c, wide), wide) for c in range(0, step, wide)]


def own_kernel(prior, step, last_place, bias_ref, q_ref, k_ref, v_ref, do_ref, *refs):
    attn_ref, gq_ref, gk_ref, gv_ref = refs[-4:]
    tok, width = k_ref.shape
    late = slice(prior, tok)

    @pl.when((lax.axis_index("head") == lax.axis_size("head") - 1) == last_place)
    def _():
        @pl.loop(0, width // step)
        def _(at):
            bias = bias_ref[...]
            columns = pair_columns(at, step)
            queries = [side_by_side(q_ref[late, c]) for c in columns]
            cotangents = [side_by_side(do_ref[late, c]) for c in columns]
            pairs = [
                score_pair(k_ref[:, c], q, v_ref[:, c], do, bias)
                for c, q, do in zip(columns, queries, cotangents)
            ]
            weights, _, deltas = softmax_columns(pairs)
            grads = score_grads_of(pairs, weights, deltas)
            for c, w, g, q, do in zip(columns, weights, grads, queries, cotangents):
                w = w.astype(jnp.bfloat16)
                attn_ref[:, c] = own_diagonal(dot(w, v_ref[:, c], 0, 0)).astype(jnp.bfloat16)
                gq_ref[:, c] = own_diagonal(dot(g, k_ref[:, c], 0, 0)).astype(jnp.bfloat16)
                gk_ref[:, c] = dot(g, q, 1, 0)
                gv_ref[:, c] = dot(w, do, 1, 0)


def near_kernel(
    prior, near_bias_ref, lead_bias_ref, q_ref, k_ref, v_ref, do_ref, near_ref, *back_refs
):
    width, half = q_ref.shape[1], prior // 2
    far = lead_bias_ref[half - 1 : half, 0:1] == 0.0
    key = lax.broadcasted_iota(jnp.int32, (prior + half, 1), 0)
    bias = jnp.where(far & (key < half), MASKED, near_bias_ref[...])
    spare = lax.broadcasted_iota(jnp.int32, (half, 1), 0) == half - 1
    early, first, second = slice(0, prior), slice(0, half), slice(half, prior)
    columns = head_columns(0, width, 2)
    queries = [side_by_side(q_ref[early, c]) for c in columns]
    cotangents = [side_by_side(do_ref[early, c]) for c in columns]
    pairs = []
    for c, q, do in zip(columns, queries, cotangents):
        k = jnp.concatenate([near_ref[first, c], k_ref[early, c]], axis=0)
        v = jnp.concatenate([near_ref[second, c], v_ref[early, c]], axis=0)
        pairs.append(score_pair(k, q, v, do, bias))
    weights, logs, deltas = softmax_columns(pairs)
    weights = [w[:half] for w in weights]
    grads = score_grads_of([(s[:half], dp[:half]) for s, dp in pairs], weights, deltas)
    k_terms = [dot(g, q, 1, 0) for g, q in zip(grads, queries)]
    v_terms = [dot(w.astype(jnp.bfloat16), do, 1, 0) for w, do in zip(weights, cotangents)]
    logs, deltas = fours(logs), fours(deltas)
    for at, c in enumerate(head_columns(0, width, 4)):
        back_ref = back_refs[c.start * len(back_refs) // width]
        low = c.start % back_ref.shape[1]
        here = slice(low, low + c.stop - c.start)
        for row, terms, ref, place in (
            (logs[at], k_terms, q_ref, first), (deltas[at], v_terms, do_ref, second)
        ):
            rows = jnp.where(spare, split_bf16(row), ref[first, c])
            terms = jnp.concatenate(terms[2 * at : 2 * at + 2], axis=1).astype(jnp.bfloat16)
            back_ref[place, here] = jnp.where(far, rows, terms)


def lead_kernel(
    prior, step, bias_ref, q_ref, k_ref, v_ref, do_ref, near_ref, far_ref, gk_part_ref, gv_part_ref,
    attn_late_ref, gq_late_ref, attn_hbm, gq_hbm, gk_hbm, gv_hbm,
    attn_ref, gq_ref, gk_ref, gv_ref, sems, late_sems,
):
    tok, width = q_ref.shape
    half = prior // 2
    early, first, second = slice(0, prior), slice(0, half), slice(half, prior)
    late = pl.ds(prior, tok - prior)
    late_copies = [
        pltpu.make_async_copy(attn_late_ref, attn_hbm.at[late, :], late_sems.at[0]),
        pltpu.make_async_copy(gq_late_ref, gq_hbm.at[late, :], late_sems.at[1]),
    ]
    for copy in late_copies:
        copy.start()

    def copies(at):
        cols = pl.ds(pl.multiple_of(at * step, step), step)
        pairs = ((attn_ref, attn_hbm), (gq_ref, gq_hbm), (gk_ref, gk_hbm), (gv_ref, gv_hbm))
        return [
            pltpu.make_async_copy(ref.at[:, cols], hbm.at[pl.ds(0, prior), cols], sems.at[at, n])
            for n, (ref, hbm) in enumerate(pairs)
        ]

    @pl.loop(0, width // step)
    def _(at):
        bias = bias_ref[...]
        columns = pair_columns(at, step)
        queries = [side_by_side(q_ref[early, c]) for c in columns]
        cotangents = [side_by_side(do_ref[early, c]) for c in columns]
        keys = [
            jnp.concatenate([far_ref[first, c], near_ref[first, c], k_ref[early, c]], axis=0)
            for c in columns
        ]
        values = [
            jnp.concatenate([far_ref[second, c], near_ref[second, c], v_ref[early, c]], axis=0)
            for c in columns
        ]
        pairs = [
            score_pair(k, q, v, do, bias)
            for k, q, v, do in zip(keys, queries, values, cotangents)
        ]
        weights, _, deltas = softmax_columns(pairs)
        grads = score_grads_of(pairs, weights, deltas)
        for n, c in enumerate(columns):
            w, g = weights[n].astype(jnp.bfloat16), grads[n]
            attn_ref[:, c] = own_diagonal(dot(w, values[n], 0, 0)).astype(jnp.bfloat16)
            gq_ref[:, c] = own_diagonal(dot(g, keys[n], 0, 0)).astype(jnp.bfloat16)
            gk = gk_part_ref[early, c] + dot(g[prior:], queries[n], 1, 0)
            gv = gv_part_ref[early, c] + dot(w[prior:], cotangents[n], 1, 0)
            gk_ref[:, c] = gk.astype(jnp.bfloat16)
            gv_ref[:, c] = gv.astype(jnp.bfloat16)
        for copy in copies(at):
            copy.start()

    for at in range(width // step):
        for copy in copies(at):
            copy.wait()
    for copy in late_copies:
        copy.wait()


def tail_half(prior, low, bias_ref, k_ref, v_ref, gk_part_ref, gv_part_ref, after_ref):
    tok, half = k_ref.shape[0], prior // 2
    far = bias_ref[half - 1 : half, 0:1] == 0.0
    bias = jnp.where(far, bias_ref[...], MASKED)
    first, second, last = slice(0, half), slice(half, prior), slice(tok - prior, tok)
    places = head_columns(0, after_ref.shape[1], 4)
    columns = head_columns(low, low + after_ref.shape[1], 4)
    queries = [side_by_side(after_ref[first, p]) for p in places]
    cotangents = [side_by_side(after_ref[second, p]) for p in places]
    pairs = [
        score_pair(k_ref[last, c], q, v_ref[last, c], do, bias)
        for c, q, do in zip(columns, queries, cotangents)
    ]
    own = [
        (joined(after_ref[half - 16 : half, p][15:]), joined(after_ref[prior - 16 : prior, p][15:]))
        for p in places
    ]
    weights, grads = merged_columns(pairs, own)

    def fill(ref, part_ref, lefts, rights, rows):
        for p, c, left, right in zip(places, columns, lefts, rights):
            total = part_ref[last, c] + dot(left, right, 1, 0)
            terms = jnp.where(far, 0.0, after_ref[rows, p].astype(jnp.float32))
            ref[first, p] = total[first].astype(jnp.bfloat16)
            ref[second, p] = (total[second] + terms).astype(jnp.bfloat16)

    return (
        lambda ref: fill(ref, gv_part_ref, weights, cotangents, second),
        lambda ref: fill(ref, gk_part_ref, grads, queries, first),
    )


def tail_kernel(prior, bias_ref, k_ref, v_ref, gk_part_ref, gv_part_ref, after_ref, gk_ref, gv_ref):
    fill_gv, fill_gk = tail_half(
        prior, 0, bias_ref, k_ref, v_ref, gk_part_ref, gv_part_ref, after_ref
    )
    fill_gv(gv_ref)
    fill_gk(gk_ref)


def last_kernel(
    prior, bias_ref, k_ref, v_ref, gk_part_ref, gv_part_ref, after_ref, gk_first_ref, gv_first_ref,
    gk_in, gv_in, gk_hbm, gv_hbm, gk_ref, gv_ref, sems,
):
    rows = pl.ds(k_ref.shape[0] - prior, prior)
    low = gk_first_ref.shape[1]
    copies = []

    def send(ref, hbm, start):
        cols = pl.ds(start, ref.shape[1])
        copies.append(pltpu.make_async_copy(ref, hbm.at[rows, cols], sems.at[len(copies)]))
        copies[-1].start()

    send(gv_first_ref, gv_hbm, 0)
    send(gk_first_ref, gk_hbm, 0)
    fill_gv, fill_gk = tail_half(
        prior, low, bias_ref, k_ref, v_ref, gk_part_ref, gv_part_ref, after_ref
    )
    fill_gv(gv_ref)
    send(gv_ref, gv_hbm, low)
    fill_gk(gk_ref)
    send(gk_ref, gk_hbm, low)
    for copy in copies:
        copy.wait()


def neighbour(value, by):
    peers = lax.axis_size("seq") * lax.axis_size("head")
    pairs = [(i, i + by) for i in range(peers) if 0 <= i + by < peers]
    return lax.ppermute(value, ("seq", "head"), pairs)


def cost(heads, queries, keys, products, moved):
    return pl.CostEstimate(
        flops=2 * heads * queries * keys * HEAD_DIM * products,
        bytes_accessed=moved,
        transcendentals=heads * queries * keys,
    )


def halo_shards(query_in, key_in, value_in, grad_out, module_lengths):
    tok, width = query_in.shape
    prior = tok * lax.axis_size("head") // 8
    step = math.gcd(width, 8 * HEAD_DIM)
    groups = width // step
    anywhere = pl.BlockSpec(memory_space=pl.ANY)
    inside = pl.BlockSpec(memory_space=pltpu.VMEM)
    full16 = jax.ShapeDtypeStruct((tok, width), jnp.bfloat16)

    def near16(rows, columns):
        return pltpu.VMEM((rows, columns), jnp.bfloat16)

    def near32(rows, columns):
        return pltpu.VMEM((rows, columns), jnp.float32)

    def in_hbm(*values):
        return [pltpu.with_memory_space_constraint(value, pltpu.HBM) for value in values]

    def in_vmem(*values):
        return [pltpu.with_memory_space_constraint(value, pltpu.VMEM) for value in values]

    def call(kernel, name, ins, outs, shapes, scratch, work, moved, aliases=None):
        return pl.pallas_call(
            kernel,
            in_specs=ins,
            out_specs=outs,
            out_shape=shapes,
            scratch_shapes=scratch,
            input_output_aliases=aliases or {},
            cost_estimate=cost(*work, moved),
            compiler_params=pltpu.CompilerParams(vmem_limit_bytes=16 * 2**20),
            name=name,
        )

    near, far = call(
        functools.partial(pack_kernel, prior), "late_keys",
        [anywhere] * 2, [inside] * 2, [near16(prior, width)] * 2,
        [pltpu.SemaphoreType.DMA((2,))] * 2, (0, 0, 0, 0), 8 * prior * width,
    )(*in_hbm(key_in, value_in))
    near = neighbour(near, 1)

    lengths = module_lengths.reshape(1, -1)

    def operands(first_place, *held):
        return call(
            functools.partial(ready_kernel, prior, first_place), "operands",
            [anywhere] * 5 + [inside] * len(held), [inside] * 8,
            [near16(tok, width)] * 4
            + [near32(tok, 2 * prior), near32(prior + prior // 2, 2 * prior)]
            + [near32(2 * prior, 2 * prior), near32(prior, 2 * prior)],
            [
                pltpu.VMEM(lengths.shape, jnp.int32), pltpu.SemaphoreType.DMA((4,)),
                pltpu.SemaphoreType.DMA(()),
            ],
            (0, 0, 0, 0), 16 * tok * width, {5 + n: n for n in range(len(held))},
        )(*in_hbm(lengths, query_in, key_in, value_in, grad_out), *in_vmem(*held))

    def own_block(last_place, *partial):
        return call(
            functools.partial(own_kernel, prior, step, last_place), "own_block",
            [inside] * (5 + len(partial)), [inside] * 4,
            [near16(tok - prior, width)] * 2 + [near32(tok, width)] * 2, (),
            (width // HEAD_DIM, tok - prior, tok, 6), 18 * tok * width,
            {5 + n: n for n in range(len(partial))},
        )(*in_vmem(own_bias, q, k, v, do, *partial))

    far, *held = lax.optimization_barrier((far, *operands(True)))
    far = neighbour(far, 1)
    q, k, v, do, own_bias, near_bias, lead_bias, tail_bias = operands(False, *held)
    near_bias, *partial = lax.optimization_barrier((near_bias, *own_block(False)))
    backs = call(
        functools.partial(near_kernel, prior), "near_terms",
        [inside] * 7, [inside] * 2, [near16(prior, width // 2)] * 2, (),
        (width // HEAD_DIM, prior, prior + prior // 2, 3), 8 * tok * width,
    )(*in_vmem(near_bias, lead_bias, q, k, v, do, near))
    own_bias, *backs = lax.optimization_barrier((own_bias, *backs))
    backs = [neighbour(back, -1) for back in backs]
    attn, gq, gk_part, gv_part = own_block(True, *partial)

    attn, gq, gk, gv = call(
        functools.partial(lead_kernel, prior, step), "lead_rows",
        [inside] * 11, [anywhere] * 4, [full16] * 4,
        [near16(prior, width)] * 4
        + [pltpu.SemaphoreType.DMA((groups, 4)), pltpu.SemaphoreType.DMA((2,))],
        (width // HEAD_DIM, prior, 2 * prior, 6), 20 * tok * width,
    )(*in_vmem(lead_bias, q, k, v, do, near, far, gk_part, gv_part, attn, gq))

    here = in_vmem(tail_bias, k, v, gk_part, gv_part)
    work = (width // HEAD_DIM // 2, prior, prior // 2, 4)
    halves = call(
        functools.partial(tail_kernel, prior), "tail_keys",
        [inside] * 6, [inside] * 2, [near16(prior, width // 2)] * 2, (), work, 4 * tok * width,
    )(*here, *in_vmem(backs[0]))
    gk, gv = call(
        functools.partial(last_kernel, prior), "last_keys",
        [inside] * 8 + [anywhere] * 2, [anywhere] * 2, [full16] * 2,
        [near16(prior, width // 2)] * 2 + [pltpu.SemaphoreType.DMA((4,))],
        work, 6 * tok * width, {8: 0, 9: 1},
    )(*here, *in_vmem(backs[1], *halves), gk, gv)
    return (attn, gq, gk, gv)


def shards(query_in, key_in, value_in, grad_out, module_lengths):
    tok = query_in.shape[0]
    prior = tok * lax.axis_size("head") // 8
    plan = halo_shards if 2 * prior == tok else gathered_shards
    return plan(query_in, key_in, value_in, grad_out, module_lengths)


def solution(mesh):
    placed = (
        P(("seq", "head"), None),
        P(("seq", "head"), None),
        P(("seq", "head"), None),
        P(("seq", "head"), None),
        P(),
    )
    return jax.shard_map(
        shards,
        mesh=mesh,
        in_specs=placed,
        out_specs=(
            P(("seq", "head"), None),
            P(("seq", "head"), None),
            P(("seq", "head"), None),
            P(("seq", "head"), None),
        ),
        check_vma=False,
    )
```

```python
import functools
import math

import jax
import jax.numpy as jnp
from jax import lax
from jax.experimental import pallas as pl
from jax.experimental.pallas import tpu as pltpu
from jax.sharding import PartitionSpec as P

HEAD_DIM = 128
SCALE = HEAD_DIM ** (-0.5)
LOG2E = math.log2(math.e)
MASKED = -1e30


def shifted(value, axis, by):
    peers = lax.axis_size(axis)
    pairs = [(i, i + by) for i in range(peers) if 0 <= i + by < peers]
    return lax.ppermute(value, axis, pairs)


def module_ids(module_lengths, positions):
    module_ends = jnp.cumsum(module_lengths)
    counted = jnp.sum((positions[:, None] >= module_ends[None, :]).astype(jnp.int32), axis=1)
    return jnp.where(positions >= 0, counted, -1)


def allowed_pairs(module_lengths, query_pos, key_pos):
    same = (
        module_ids(module_lengths, query_pos)[:, None]
        == module_ids(module_lengths, key_pos)[None, :]
    )
    return same & (key_pos[None, :] <= query_pos[:, None])


def score_grads(grad_rows, value_block, weights, row_delta, score_scale):
    dprobs = jnp.einsum("qd,kd->qk", grad_rows, value_block, preferred_element_type=jnp.float32)
    return (weights * (dprobs - row_delta[:, None]) * score_scale).astype(jnp.bfloat16)


def key_terms(dscores, weight_bf, query_rows, grad_rows):
    key_grad = jnp.einsum("qk,qd->kd", dscores, query_rows, preferred_element_type=jnp.float32)
    value_grad = jnp.einsum("qk,qd->kd", weight_bf, grad_rows, preferred_element_type=jnp.float32)
    return (key_grad, value_grad)


def one_block(query_rows, key_block, value_block, grad_rows, allowed, score_scale):
    scores = (
        jnp.einsum("qd,kd->qk", query_rows, key_block, preferred_element_type=jnp.float32)
        * score_scale
    )
    row_top = jnp.max(jnp.where(allowed, scores, -jnp.inf), axis=1, keepdims=True)
    row_total = jnp.sum(jnp.where(allowed, jnp.exp(scores - row_top), 0.0), axis=1, keepdims=True)
    log_total = row_top + jnp.log(row_total)
    weights = jnp.where(allowed, jnp.exp(scores - log_total), 0.0)
    weight_bf = weights.astype(jnp.bfloat16)
    attn_rows = jnp.einsum(
        "qk,kd->qd", weight_bf, value_block, preferred_element_type=jnp.float32
    ).astype(jnp.bfloat16)
    row_delta = jnp.sum(grad_rows.astype(jnp.float32) * attn_rows.astype(jnp.float32), axis=1)
    dscores = score_grads(grad_rows, value_block, weights, row_delta, score_scale)
    grad_q = jnp.einsum("qk,kd->qd", dscores, key_block, preferred_element_type=jnp.float32).astype(
        jnp.bfloat16
    )
    key_grad, value_grad = key_terms(dscores, weight_bf, query_rows, grad_rows)
    return (attn_rows, grad_q, key_grad, value_grad, log_total[:, 0], row_delta)


def gathered_shards(query_in, key_in, value_in, grad_out, module_lengths):
    head_q, head_k, head_v, head_do = (
        lax.all_to_all(query_in, "head", split_axis=1, concat_axis=0, tiled=True),
        lax.all_to_all(key_in, "head", split_axis=1, concat_axis=0, tiled=True),
        lax.all_to_all(value_in, "head", split_axis=1, concat_axis=0, tiled=True),
        lax.all_to_all(grad_out, "head", split_axis=1, concat_axis=0, tiled=True),
    )
    row_count = head_q.shape[0]
    width = head_q.shape[1]
    local_heads = width // HEAD_DIM
    prior_rows = row_count // 8
    score_scale = HEAD_DIM ** (-0.5)
    tail_start = row_count - prior_rows
    prior_k, prior_v = shifted((head_k[tail_start:], head_v[tail_start:]), "seq", 1)
    row_start = lax.axis_index("seq") * row_count
    query_pos = row_start + jnp.arange(row_count, dtype=jnp.int32)
    before_pos = row_start - prior_rows + jnp.arange(prior_rows, dtype=jnp.int32)
    key_pos = jnp.concatenate([before_pos, query_pos])
    block_rows = math.gcd(row_count, 512)
    block_count = row_count // block_rows
    pos_blocks = query_pos.reshape(block_count, block_rows)

    def by_head(flat, rows):
        return jnp.moveaxis(flat.reshape(rows, local_heads, HEAD_DIM), 1, 0)

    def to_flat(stacked):
        return jnp.moveaxis(stacked, 0, 1).reshape(stacked.shape[1], width)

    query_h = by_head(head_q, row_count)
    grad_h = by_head(head_do, row_count)
    key_h = by_head(jnp.concatenate([prior_k, head_k], axis=0), row_count + prior_rows)
    value_h = by_head(jnp.concatenate([prior_v, head_v], axis=0), row_count + prior_rows)

    def run_head(packed):
        query_rows, key_block, value_block, grad_rows = packed
        query_blocks = query_rows.reshape(block_count, block_rows, HEAD_DIM)
        grad_blocks = grad_rows.reshape(block_count, block_rows, HEAD_DIM)

        def run_block(inner):
            query_part, grad_part, pos_part = inner
            allowed = allowed_pairs(module_lengths, pos_part, key_pos)
            return one_block(query_part, key_block, value_block, grad_part, allowed, score_scale)

        attn_b, grad_qb, key_b, value_b, lse_b, delta_b = lax.map(
            run_block, (query_blocks, grad_blocks, pos_blocks)
        )
        return (
            attn_b.reshape(row_count, HEAD_DIM),
            grad_qb.reshape(row_count, HEAD_DIM),
            jnp.sum(key_b, axis=0),
            jnp.sum(value_b, axis=0),
            lse_b.reshape(row_count),
            delta_b.reshape(row_count),
        )

    attn_h, grad_qh, key_grad, value_grad, log_total, row_delta = lax.map(
        run_head, (query_h, key_h, value_h, grad_h)
    )
    attn_flat = to_flat(attn_h)
    attn_back = lax.all_to_all(attn_flat, "head", split_axis=0, concat_axis=1, tiled=True)
    grad_q = to_flat(grad_qh)
    later_k, later_v = shifted((key_grad[:, :prior_rows], value_grad[:, :prior_rows]), "seq", -1)
    key_total = key_grad[:, prior_rows:].at[:, tail_start:].add(later_k)
    value_total = value_grad[:, prior_rows:].at[:, tail_start:].add(later_v)
    grad_k = to_flat(key_total.astype(jnp.bfloat16))
    grad_v = to_flat(value_total.astype(jnp.bfloat16))
    back_q, back_k, back_v = (
        lax.all_to_all(grad_q, "head", split_axis=0, concat_axis=1, tiled=True),
        lax.all_to_all(grad_k, "head", split_axis=0, concat_axis=1, tiled=True),
        lax.all_to_all(grad_v, "head", split_axis=0, concat_axis=1, tiled=True),
    )
    return (attn_back, back_q, back_k, back_v)


def dot(left, right, left_dim, right_dim):
    return lax.dot_general(
        left, right, (((left_dim,), (right_dim,)), ((), ())), preferred_element_type=jnp.float32
    )


def module_ends_col(lengths_row):
    count = lengths_row.shape[1]
    row = lax.broadcasted_iota(jnp.int32, (count, count), 0)
    col = lax.broadcasted_iota(jnp.int32, (count, count), 1)
    return jnp.sum(jnp.where(col <= row, lengths_row, 0.0), axis=1, keepdims=True)


def bias_by_key(lengths_row, first_query, queries, first_key, keys, heads):
    ends = module_ends_col(lengths_row)
    lane = lax.broadcasted_iota(jnp.int32, (1, heads * queries), 1)
    query = (first_query + lane % queries).astype(jnp.float32)
    start = jnp.max(jnp.where(ends <= query, ends, 0.0), axis=0, keepdims=True)
    key = (first_key + lax.broadcasted_iota(jnp.int32, (keys, heads * queries), 0)).astype(
        jnp.float32
    )
    return jnp.where((key >= start) & (key <= query), 0.0, MASKED)


def score_pair(k, q, v, do, bias):
    return dot(k, q, 1, 1) * (SCALE * LOG2E) + bias, dot(v, do, 1, 1)


def softmax_columns(pairs):
    tops = [jnp.max(s, axis=0, keepdims=True) for s, _ in pairs]
    raws = [jnp.exp2(s - top) for (s, _), top in zip(pairs, tops)]
    totals = [jnp.sum(raw, axis=0, keepdims=True) for raw in raws]
    weights = [raw * (1.0 / total) for raw, total in zip(raws, totals)]
    deltas = [jnp.sum(w * dp, axis=0, keepdims=True) for w, (_, dp) in zip(weights, pairs)]
    logs = [top + jnp.log2(total) for top, total in zip(tops, totals)]
    return weights, logs, deltas


def score_grads_of(pairs, weights, deltas):
    return [
        (w * (dp - delta) * SCALE).astype(jnp.bfloat16)
        for w, (_, dp), delta in zip(weights, pairs, deltas)
    ]


def merged_columns(pairs, own):
    tops = [
        jnp.maximum(jnp.max(s, axis=0, keepdims=True), log) for (s, _), (log, _) in zip(pairs, own)
    ]
    raws = [jnp.exp2(s - top) for (s, _), top in zip(pairs, tops)]
    own_raws = [jnp.exp2(log - top) for (log, _), top in zip(own, tops)]
    parts = [
        1.0 / (jnp.sum(raw, axis=0, keepdims=True) + own_raw)
        for raw, own_raw in zip(raws, own_raws)
    ]
    weights = [raw * part for raw, part in zip(raws, parts)]
    deltas = [
        jnp.sum(w * dp, axis=0, keepdims=True) + own_raw * part * own_delta
        for w, (_, dp), own_raw, part, (_, own_delta) in zip(weights, pairs, own_raws, parts, own)
    ]
    grads = [w * (dp - delta) * SCALE for w, (_, dp), delta in zip(weights, pairs, deltas)]
    return [w.astype(jnp.bfloat16) for w in weights], [g.astype(jnp.bfloat16) for g in grads]


def side_by_side(rows):
    heads = rows.shape[1] // HEAD_DIM
    zero = jnp.zeros((rows.shape[0], HEAD_DIM), rows.dtype)
    blocks = [rows[:, c] for c in head_columns(0, rows.shape[1])]
    return jnp.concatenate(
        [
            jnp.concatenate([blocks[h] if g == h else zero for g in range(heads)], axis=1)
            for h in range(heads)
        ],
        axis=0,
    )


def head_columns(low, high, heads=1):
    wide = heads * HEAD_DIM
    return [slice(c, c + wide) for c in range(low, high, wide)]


def device_first(tok):
    place = lax.axis_index("seq") * lax.axis_size("head") + lax.axis_index("head")
    return place * tok


def fours(rows):
    table = jnp.concatenate(rows, axis=0)
    half = table.shape[1] // 4
    lane = lax.broadcasted_iota(jnp.int32, (1, table.shape[1]), 1)
    turned = [pltpu.roll(table, turn * half, 1) for turn in (3, 2, 1)]
    merged = []
    for at in range(0, len(rows), 2):
        now, after = slice(at, at + 1), slice(at + 1, at + 2)
        row = jnp.where(lane < 3 * half, turned[1][after], turned[2][after])
        row = jnp.where(lane < 2 * half, turned[0][now], row)
        merged.append(jnp.where(lane < half, table[now], row))
    return merged


def split_bf16(row):
    parts = []
    for _ in range(3):
        part = row.astype(jnp.bfloat16)
        parts.append(part)
        row = row - part.astype(jnp.float32)
    return jnp.concatenate([*parts, jnp.zeros_like(parts[0])], axis=1)


def joined(parts):
    parts = parts.astype(jnp.float32)
    count = parts.shape[1] // 4
    return parts[:, :count] + parts[:, count : 2 * count] + parts[:, 2 * count : 3 * count]


def pack_copies(prior, at, k_ref, v_ref, packed_ref, sems):
    half, tok = prior // 2, k_ref.shape[0]
    rows = pl.ds(tok - (at + 1) * half, half)
    return [
        pltpu.make_async_copy(
            ref.at[rows, :], packed_ref.at[pl.ds(n * half, half), :], sems.at[n]
        )
        for n, ref in enumerate((k_ref, v_ref))
    ]


def pack_kernel(prior, k_ref, v_ref, near_ref, far_ref, near_sems, far_sems):
    copies = pack_copies(prior, 0, k_ref, v_ref, near_ref, near_sems)
    copies += pack_copies(prior, 1, k_ref, v_ref, far_ref, far_sems)
    for copy in copies:
        copy.start()
    for copy in copies:
        copy.wait()


def ready_kernel(prior, at_end, len_hbm, q_hbm, k_hbm, v_hbm, do_hbm, *refs):
    (
        q_ref, k_ref, v_ref, do_ref, own_bias_ref, near_bias_ref, lead_bias_ref, tail_bias_ref,
        len_ref, sems, len_sem,
    ) = refs[-11:]
    tok, half = k_ref.shape[0], prior // 2
    pairs = ((q_hbm, q_ref), (k_hbm, k_ref), (v_hbm, v_ref), (do_hbm, do_ref))

    place, last = lax.axis_index("head"), lax.axis_size("head") - 1

    @pl.when(((place == 0) | (place == last)) == at_end)
    def _():
        copies = [pltpu.make_async_copy(hbm, ref, sems.at[n]) for n, (hbm, ref) in enumerate(pairs)]
        len_copy = pltpu.make_async_copy(len_hbm, len_ref, len_sem)
        len_copy.start()
        for copy in copies:
            copy.start()
        len_copy.wait()
        first = device_first(tok)
        lengths = len_ref[...].astype(jnp.float32)
        own_bias_ref[...] = bias_by_key(lengths, first + prior, tok - prior, first, tok, 2)
        near_bias_ref[...] = bias_by_key(lengths, first, prior, first - half, prior + half, 2)
        lead_bias_ref[...] = bias_by_key(lengths, first, prior, first - prior, 2 * prior, 2)
        tail_bias_ref[...] = bias_by_key(
            lengths, first + tok, half, first + tok - prior, prior, 4
        )
        for copy in copies:
            copy.wait()


def own_diagonal(both):
    rows = both.shape[0] // 2
    return jnp.concatenate([both[:rows, :HEAD_DIM], both[rows:, HEAD_DIM:]], axis=1)


def pair_columns(at, step):
    wide = 2 * HEAD_DIM
    return [pl.ds(pl.multiple_of(at * step + c, wide), wide) for c in range(0, step, wide)]


def own_kernel(prior, step, behind, bias_ref, q_ref, k_ref, v_ref, do_ref, *refs):
    attn_ref, gq_ref, gk_ref, gv_ref = refs[-4:]
    tok, width = k_ref.shape
    late = slice(prior, tok)

    @pl.when((lax.axis_index("head") == lax.axis_size("head") - 2) == behind)
    def _():
        @pl.loop(0, width // step)
        def _(at):
            bias = bias_ref[...]
            columns = pair_columns(at, step)
            queries = [side_by_side(q_ref[late, c]) for c in columns]
            cotangents = [side_by_side(do_ref[late, c]) for c in columns]
            pairs = [
                score_pair(k_ref[:, c], q, v_ref[:, c], do, bias)
                for c, q, do in zip(columns, queries, cotangents)
            ]
            weights, _, deltas = softmax_columns(pairs)
            grads = score_grads_of(pairs, weights, deltas)
            for c, w, g, q, do in zip(columns, weights, grads, queries, cotangents):
                w = w.astype(jnp.bfloat16)
                attn_ref[:, c] = own_diagonal(dot(w, v_ref[:, c], 0, 0)).astype(jnp.bfloat16)
                gq_ref[:, c] = own_diagonal(dot(g, k_ref[:, c], 0, 0)).astype(jnp.bfloat16)
                gk_ref[:, c] = dot(g, q, 1, 0)
                gv_ref[:, c] = dot(w, do, 1, 0)


def near_kernel(
    prior, near_bias_ref, lead_bias_ref, q_ref, k_ref, v_ref, do_ref, near_ref, *back_refs
):
    width, half = q_ref.shape[1], prior // 2
    far = lead_bias_ref[half - 1 : half, 0:1] == 0.0
    key = lax.broadcasted_iota(jnp.int32, (prior + half, 1), 0)
    bias = jnp.where(far & (key < half), MASKED, near_bias_ref[...])
    spare = lax.broadcasted_iota(jnp.int32, (half, 1), 0) == half - 1
    early, first, second = slice(0, prior), slice(0, half), slice(half, prior)
    columns = head_columns(0, width, 2)
    queries = [side_by_side(q_ref[early, c]) for c in columns]
    cotangents = [side_by_side(do_ref[early, c]) for c in columns]
    pairs = []
    for c, q, do in zip(columns, queries, cotangents):
        k = jnp.concatenate([near_ref[first, c], k_ref[early, c]], axis=0)
        v = jnp.concatenate([near_ref[second, c], v_ref[early, c]], axis=0)
        pairs.append(score_pair(k, q, v, do, bias))
    weights, logs, deltas = softmax_columns(pairs)
    weights = [w[:half] for w in weights]
    grads = score_grads_of([(s[:half], dp[:half]) for s, dp in pairs], weights, deltas)
    k_terms = [dot(g, q, 1, 0) for g, q in zip(grads, queries)]
    v_terms = [dot(w.astype(jnp.bfloat16), do, 1, 0) for w, do in zip(weights, cotangents)]
    logs, deltas = fours(logs), fours(deltas)
    for at, c in enumerate(head_columns(0, width, 4)):
        back_ref = back_refs[c.start * len(back_refs) // width]
        low = c.start % back_ref.shape[1]
        here = slice(low, low + c.stop - c.start)
        for row, terms, ref, place in (
            (logs[at], k_terms, q_ref, first), (deltas[at], v_terms, do_ref, second)
        ):
            rows = jnp.where(spare, split_bf16(row), ref[first, c])
            terms = jnp.concatenate(terms[2 * at : 2 * at + 2], axis=1).astype(jnp.bfloat16)
            back_ref[place, here] = jnp.where(far, rows, terms)


def lead_kernel(
    prior, step, bias_ref, q_ref, k_ref, v_ref, do_ref, near_ref, far_ref, gk_part_ref, gv_part_ref,
    attn_late_ref, gq_late_ref, attn_hbm, gq_hbm, gk_hbm, gv_hbm,
    attn_ref, gq_ref, gk_ref, gv_ref, sems, late_sems,
):
    tok, width = q_ref.shape
    half = prior // 2
    early, first, second = slice(0, prior), slice(0, half), slice(half, prior)
    late = pl.ds(prior, tok - prior)
    late_copies = [
        pltpu.make_async_copy(attn_late_ref, attn_hbm.at[late, :], late_sems.at[0]),
        pltpu.make_async_copy(gq_late_ref, gq_hbm.at[late, :], late_sems.at[1]),
    ]
    for copy in late_copies:
        copy.start()

    def copies(at):
        cols = pl.ds(pl.multiple_of(at * step, step), step)
        pairs = ((attn_ref, attn_hbm), (gq_ref, gq_hbm), (gk_ref, gk_hbm), (gv_ref, gv_hbm))
        return [
            pltpu.make_async_copy(ref.at[:, cols], hbm.at[pl.ds(0, prior), cols], sems.at[at, n])
            for n, (ref, hbm) in enumerate(pairs)
        ]

    @pl.loop(0, width // step)
    def _(at):
        bias = bias_ref[...]
        columns = pair_columns(at, step)
        queries = [side_by_side(q_ref[early, c]) for c in columns]
        cotangents = [side_by_side(do_ref[early, c]) for c in columns]
        keys = [
            jnp.concatenate([far_ref[first, c], near_ref[first, c], k_ref[early, c]], axis=0)
            for c in columns
        ]
        values = [
            jnp.concatenate([far_ref[second, c], near_ref[second, c], v_ref[early, c]], axis=0)
            for c in columns
        ]
        pairs = [
            score_pair(k, q, v, do, bias)
            for k, q, v, do in zip(keys, queries, values, cotangents)
        ]
        weights, _, deltas = softmax_columns(pairs)
        grads = score_grads_of(pairs, weights, deltas)
        for n, c in enumerate(columns):
            w, g = weights[n].astype(jnp.bfloat16), grads[n]
            attn_ref[:, c] = own_diagonal(dot(w, values[n], 0, 0)).astype(jnp.bfloat16)
            gq_ref[:, c] = own_diagonal(dot(g, keys[n], 0, 0)).astype(jnp.bfloat16)
            gk = gk_part_ref[early, c] + dot(g[prior:], queries[n], 1, 0)
            gv = gv_part_ref[early, c] + dot(w[prior:], cotangents[n], 1, 0)
            gk_ref[:, c] = gk.astype(jnp.bfloat16)
            gv_ref[:, c] = gv.astype(jnp.bfloat16)
        for copy in copies(at):
            copy.start()

    for at in range(width // step):
        for copy in copies(at):
            copy.wait()
    for copy in late_copies:
        copy.wait()


def tail_half(prior, low, bias_ref, k_ref, v_ref, gk_part_ref, gv_part_ref, after_ref):
    tok, half = k_ref.shape[0], prior // 2
    far = bias_ref[half - 1 : half, 0:1] == 0.0
    bias = jnp.where(far, bias_ref[...], MASKED)
    first, second, last = slice(0, half), slice(half, prior), slice(tok - prior, tok)
    places = head_columns(0, after_ref.shape[1], 4)
    columns = head_columns(low, low + after_ref.shape[1], 4)
    queries = [side_by_side(after_ref[first, p]) for p in places]
    cotangents = [side_by_side(after_ref[second, p]) for p in places]
    pairs = [
        score_pair(k_ref[last, c], q, v_ref[last, c], do, bias)
        for c, q, do in zip(columns, queries, cotangents)
    ]
    own = [
        (joined(after_ref[half - 16 : half, p][15:]), joined(after_ref[prior - 16 : prior, p][15:]))
        for p in places
    ]
    weights, grads = merged_columns(pairs, own)

    def fill(ref, part_ref, lefts, rights, rows):
        for p, c, left, right in zip(places, columns, lefts, rights):
            total = part_ref[last, c] + dot(left, right, 1, 0)
            terms = jnp.where(far, 0.0, after_ref[rows, p].astype(jnp.float32))
            ref[first, p] = total[first].astype(jnp.bfloat16)
            ref[second, p] = (total[second] + terms).astype(jnp.bfloat16)

    return (
        lambda ref: fill(ref, gv_part_ref, weights, cotangents, second),
        lambda ref: fill(ref, gk_part_ref, grads, queries, first),
    )


def tail_kernel(prior, bias_ref, k_ref, v_ref, gk_part_ref, gv_part_ref, after_ref, gk_ref, gv_ref):
    fill_gv, fill_gk = tail_half(
        prior, 0, bias_ref, k_ref, v_ref, gk_part_ref, gv_part_ref, after_ref
    )
    fill_gv(gv_ref)
    fill_gk(gk_ref)


def last_kernel(
    prior, bias_ref, k_ref, v_ref, gk_part_ref, gv_part_ref, after_ref, gk_first_ref, gv_first_ref,
    gk_in, gv_in, gk_hbm, gv_hbm, gk_ref, gv_ref, sems,
):
    rows = pl.ds(k_ref.shape[0] - prior, prior)
    low = gk_first_ref.shape[1]
    copies = []

    def send(ref, hbm, start):
        cols = pl.ds(start, ref.shape[1])
        copies.append(pltpu.make_async_copy(ref, hbm.at[rows, cols], sems.at[len(copies)]))
        copies[-1].start()

    send(gv_first_ref, gv_hbm, 0)
    send(gk_first_ref, gk_hbm, 0)
    fill_gv, fill_gk = tail_half(
        prior, low, bias_ref, k_ref, v_ref, gk_part_ref, gv_part_ref, after_ref
    )
    fill_gv(gv_ref)
    send(gv_ref, gv_hbm, low)
    fill_gk(gk_ref)
    send(gk_ref, gk_hbm, low)
    for copy in copies:
        copy.wait()


def neighbour(value, by):
    peers = lax.axis_size("seq") * lax.axis_size("head")
    pairs = [(i, i + by) for i in range(peers) if 0 <= i + by < peers]
    return lax.ppermute(value, ("seq", "head"), pairs)


def cost(heads, queries, keys, products, moved):
    return pl.CostEstimate(
        flops=2 * heads * queries * keys * HEAD_DIM * products,
        bytes_accessed=moved,
        transcendentals=heads * queries * keys,
    )


def halo_shards(query_in, key_in, value_in, grad_out, module_lengths):
    tok, width = query_in.shape
    prior = tok * lax.axis_size("head") // 8
    step = math.gcd(width, 8 * HEAD_DIM)
    groups = width // step
    anywhere = pl.BlockSpec(memory_space=pl.ANY)
    inside = pl.BlockSpec(memory_space=pltpu.VMEM)
    full16 = jax.ShapeDtypeStruct((tok, width), jnp.bfloat16)

    def near16(rows, columns):
        return pltpu.VMEM((rows, columns), jnp.bfloat16)

    def near32(rows, columns):
        return pltpu.VMEM((rows, columns), jnp.float32)

    def in_hbm(*values):
        return [pltpu.with_memory_space_constraint(value, pltpu.HBM) for value in values]

    def in_vmem(*values):
        return [pltpu.with_memory_space_constraint(value, pltpu.VMEM) for value in values]

    def call(kernel, name, ins, outs, shapes, scratch, work, moved, aliases=None):
        return pl.pallas_call(
            kernel,
            in_specs=ins,
            out_specs=outs,
            out_shape=shapes,
            scratch_shapes=scratch,
            input_output_aliases=aliases or {},
            cost_estimate=cost(*work, moved),
            compiler_params=pltpu.CompilerParams(vmem_limit_bytes=16 * 2**20),
            name=name,
        )

    near, far = call(
        functools.partial(pack_kernel, prior), "late_keys",
        [anywhere] * 2, [inside] * 2, [near16(prior, width)] * 2,
        [pltpu.SemaphoreType.DMA((2,))] * 2, (0, 0, 0, 0), 8 * prior * width,
    )(*in_hbm(key_in, value_in))
    near = neighbour(near, 1)

    lengths = module_lengths.reshape(1, -1)

    def operands(at_end, *held):
        return call(
            functools.partial(ready_kernel, prior, at_end), "operands",
            [anywhere] * 5 + [inside] * len(held), [inside] * 8,
            [near16(tok, width)] * 4
            + [near32(tok, 2 * prior), near32(prior + prior // 2, 2 * prior)]
            + [near32(2 * prior, 2 * prior), near32(prior, 2 * prior)],
            [
                pltpu.VMEM(lengths.shape, jnp.int32), pltpu.SemaphoreType.DMA((4,)),
                pltpu.SemaphoreType.DMA(()),
            ],
            (0, 0, 0, 0), 16 * tok * width, {5 + n: n for n in range(len(held))},
        )(*in_hbm(lengths, query_in, key_in, value_in, grad_out), *in_vmem(*held))

    def own_block(behind, *partial):
        return call(
            functools.partial(own_kernel, prior, step, behind), "own_block",
            [inside] * (5 + len(partial)), [inside] * 4,
            [near16(tok - prior, width)] * 2 + [near32(tok, width)] * 2, (),
            (width // HEAD_DIM, tok - prior, tok, 6), 18 * tok * width,
            {5 + n: n for n in range(len(partial))},
        )(*in_vmem(own_bias, q, k, v, do, *partial))

    far, *held = lax.optimization_barrier((far, *operands(True)))
    far = neighbour(far, 1)
    q, k, v, do, own_bias, near_bias, lead_bias, tail_bias = operands(False, *held)
    near_bias, *partial = lax.optimization_barrier((near_bias, *own_block(False)))
    backs = call(
        functools.partial(near_kernel, prior), "near_terms",
        [inside] * 7, [inside] * 2, [near16(prior, width // 2)] * 2, (),
        (width // HEAD_DIM, prior, prior + prior // 2, 3), 8 * tok * width,
    )(*in_vmem(near_bias, lead_bias, q, k, v, do, near))
    own_bias, *backs = lax.optimization_barrier((own_bias, *backs))
    backs = [neighbour(back, -1) for back in backs]
    attn, gq, gk_part, gv_part = own_block(True, *partial)

    attn, gq, gk, gv = call(
        functools.partial(lead_kernel, prior, step), "lead_rows",
        [inside] * 11, [anywhere] * 4, [full16] * 4,
        [near16(prior, width)] * 4
        + [pltpu.SemaphoreType.DMA((groups, 4)), pltpu.SemaphoreType.DMA((2,))],
        (width // HEAD_DIM, prior, 2 * prior, 6), 20 * tok * width,
    )(*in_vmem(lead_bias, q, k, v, do, near, far, gk_part, gv_part, attn, gq))

    here = in_vmem(tail_bias, k, v, gk_part, gv_part)
    work = (width // HEAD_DIM // 2, prior, prior // 2, 4)
    halves = call(
        functools.partial(tail_kernel, prior), "tail_keys",
        [inside] * 6, [inside] * 2, [near16(prior, width // 2)] * 2, (), work, 4 * tok * width,
    )(*here, *in_vmem(backs[0]))
    gk, gv = call(
        functools.partial(last_kernel, prior), "last_keys",
        [inside] * 8 + [anywhere] * 2, [anywhere] * 2, [full16] * 2,
        [near16(prior, width // 2)] * 2 + [pltpu.SemaphoreType.DMA((4,))],
        work, 6 * tok * width, {8: 0, 9: 1},
    )(*here, *in_vmem(backs[1], *halves), gk, gv)
    return (attn, gq, gk, gv)


def shards(query_in, key_in, value_in, grad_out, module_lengths):
    tok = query_in.shape[0]
    prior = tok * lax.axis_size("head") // 8
    plan = halo_shards if 2 * prior == tok else gathered_shards
    return plan(query_in, key_in, value_in, grad_out, module_lengths)


def solution(mesh):
    placed = (
        P(("seq", "head"), None),
        P(("seq", "head"), None),
        P(("seq", "head"), None),
        P(("seq", "head"), None),
        P(),
    )
    return jax.shard_map(
        shards,
        mesh=mesh,
        in_specs=placed,
        out_specs=(
            P(("seq", "head"), None),
            P(("seq", "head"), None),
            P(("seq", "head"), None),
            P(("seq", "head"), None),
        ),
        check_vma=False,
    )
```

```python
import functools
import math

import jax
import jax.numpy as jnp
from jax import lax
from jax.experimental import pallas as pl
from jax.experimental.pallas import tpu as pltpu
from jax.sharding import PartitionSpec as P

HEAD_DIM = 128
SCALE = HEAD_DIM ** (-0.5)
LOG2E = math.log2(math.e)
MASKED = -1e30


def shifted(value, axis, by):
    peers = lax.axis_size(axis)
    pairs = [(i, i + by) for i in range(peers) if 0 <= i + by < peers]
    return lax.ppermute(value, axis, pairs)


def module_ids(module_lengths, positions):
    module_ends = jnp.cumsum(module_lengths)
    counted = jnp.sum((positions[:, None] >= module_ends[None, :]).astype(jnp.int32), axis=1)
    return jnp.where(positions >= 0, counted, -1)


def allowed_pairs(module_lengths, query_pos, key_pos):
    same = (
        module_ids(module_lengths, query_pos)[:, None]
        == module_ids(module_lengths, key_pos)[None, :]
    )
    return same & (key_pos[None, :] <= query_pos[:, None])


def score_grads(grad_rows, value_block, weights, row_delta, score_scale):
    dprobs = jnp.einsum("qd,kd->qk", grad_rows, value_block, preferred_element_type=jnp.float32)
    return (weights * (dprobs - row_delta[:, None]) * score_scale).astype(jnp.bfloat16)


def key_terms(dscores, weight_bf, query_rows, grad_rows):
    key_grad = jnp.einsum("qk,qd->kd", dscores, query_rows, preferred_element_type=jnp.float32)
    value_grad = jnp.einsum("qk,qd->kd", weight_bf, grad_rows, preferred_element_type=jnp.float32)
    return (key_grad, value_grad)


def one_block(query_rows, key_block, value_block, grad_rows, allowed, score_scale):
    scores = (
        jnp.einsum("qd,kd->qk", query_rows, key_block, preferred_element_type=jnp.float32)
        * score_scale
    )
    row_top = jnp.max(jnp.where(allowed, scores, -jnp.inf), axis=1, keepdims=True)
    row_total = jnp.sum(jnp.where(allowed, jnp.exp(scores - row_top), 0.0), axis=1, keepdims=True)
    log_total = row_top + jnp.log(row_total)
    weights = jnp.where(allowed, jnp.exp(scores - log_total), 0.0)
    weight_bf = weights.astype(jnp.bfloat16)
    attn_rows = jnp.einsum(
        "qk,kd->qd", weight_bf, value_block, preferred_element_type=jnp.float32
    ).astype(jnp.bfloat16)
    row_delta = jnp.sum(grad_rows.astype(jnp.float32) * attn_rows.astype(jnp.float32), axis=1)
    dscores = score_grads(grad_rows, value_block, weights, row_delta, score_scale)
    grad_q = jnp.einsum("qk,kd->qd", dscores, key_block, preferred_element_type=jnp.float32).astype(
        jnp.bfloat16
    )
    key_grad, value_grad = key_terms(dscores, weight_bf, query_rows, grad_rows)
    return (attn_rows, grad_q, key_grad, value_grad, log_total[:, 0], row_delta)


def gathered_shards(query_in, key_in, value_in, grad_out, module_lengths):
    head_q, head_k, head_v, head_do = (
        lax.all_to_all(query_in, "head", split_axis=1, concat_axis=0, tiled=True),
        lax.all_to_all(key_in, "head", split_axis=1, concat_axis=0, tiled=True),
        lax.all_to_all(value_in, "head", split_axis=1, concat_axis=0, tiled=True),
        lax.all_to_all(grad_out, "head", split_axis=1, concat_axis=0, tiled=True),
    )
    row_count = head_q.shape[0]
    width = head_q.shape[1]
    local_heads = width // HEAD_DIM
    prior_rows = row_count // 8
    score_scale = HEAD_DIM ** (-0.5)
    tail_start = row_count - prior_rows
    prior_k, prior_v = shifted((head_k[tail_start:], head_v[tail_start:]), "seq", 1)
    row_start = lax.axis_index("seq") * row_count
    query_pos = row_start + jnp.arange(row_count, dtype=jnp.int32)
    before_pos = row_start - prior_rows + jnp.arange(prior_rows, dtype=jnp.int32)
    key_pos = jnp.concatenate([before_pos, query_pos])
    block_rows = math.gcd(row_count, 512)
    block_count = row_count // block_rows
    pos_blocks = query_pos.reshape(block_count, block_rows)

    def by_head(flat, rows):
        return jnp.moveaxis(flat.reshape(rows, local_heads, HEAD_DIM), 1, 0)

    def to_flat(stacked):
        return jnp.moveaxis(stacked, 0, 1).reshape(stacked.shape[1], width)

    query_h = by_head(head_q, row_count)
    grad_h = by_head(head_do, row_count)
    key_h = by_head(jnp.concatenate([prior_k, head_k], axis=0), row_count + prior_rows)
    value_h = by_head(jnp.concatenate([prior_v, head_v], axis=0), row_count + prior_rows)

    def run_head(packed):
        query_rows, key_block, value_block, grad_rows = packed
        query_blocks = query_rows.reshape(block_count, block_rows, HEAD_DIM)
        grad_blocks = grad_rows.reshape(block_count, block_rows, HEAD_DIM)

        def run_block(inner):
            query_part, grad_part, pos_part = inner
            allowed = allowed_pairs(module_lengths, pos_part, key_pos)
            return one_block(query_part, key_block, value_block, grad_part, allowed, score_scale)

        attn_b, grad_qb, key_b, value_b, lse_b, delta_b = lax.map(
            run_block, (query_blocks, grad_blocks, pos_blocks)
        )
        return (
            attn_b.reshape(row_count, HEAD_DIM),
            grad_qb.reshape(row_count, HEAD_DIM),
            jnp.sum(key_b, axis=0),
            jnp.sum(value_b, axis=0),
            lse_b.reshape(row_count),
            delta_b.reshape(row_count),
        )

    attn_h, grad_qh, key_grad, value_grad, log_total, row_delta = lax.map(
        run_head, (query_h, key_h, value_h, grad_h)
    )
    attn_flat = to_flat(attn_h)
    attn_back = lax.all_to_all(attn_flat, "head", split_axis=0, concat_axis=1, tiled=True)
    grad_q = to_flat(grad_qh)
    later_k, later_v = shifted((key_grad[:, :prior_rows], value_grad[:, :prior_rows]), "seq", -1)
    key_total = key_grad[:, prior_rows:].at[:, tail_start:].add(later_k)
    value_total = value_grad[:, prior_rows:].at[:, tail_start:].add(later_v)
    grad_k = to_flat(key_total.astype(jnp.bfloat16))
    grad_v = to_flat(value_total.astype(jnp.bfloat16))
    back_q, back_k, back_v = (
        lax.all_to_all(grad_q, "head", split_axis=0, concat_axis=1, tiled=True),
        lax.all_to_all(grad_k, "head", split_axis=0, concat_axis=1, tiled=True),
        lax.all_to_all(grad_v, "head", split_axis=0, concat_axis=1, tiled=True),
    )
    return (attn_back, back_q, back_k, back_v)


def dot(left, right, left_dim, right_dim):
    return lax.dot_general(
        left, right, (((left_dim,), (right_dim,)), ((), ())), preferred_element_type=jnp.float32
    )


def module_ends_col(lengths_row):
    count = lengths_row.shape[1]
    row = lax.broadcasted_iota(jnp.int32, (count, count), 0)
    col = lax.broadcasted_iota(jnp.int32, (count, count), 1)
    return jnp.sum(jnp.where(col <= row, lengths_row, 0.0), axis=1, keepdims=True)


def bias_by_key(lengths_row, first_query, queries, first_key, keys, heads):
    ends = module_ends_col(lengths_row)
    lane = lax.broadcasted_iota(jnp.int32, (1, heads * queries), 1)
    query = (first_query + lane % queries).astype(jnp.float32)
    start = jnp.max(jnp.where(ends <= query, ends, 0.0), axis=0, keepdims=True)
    key = (first_key + lax.broadcasted_iota(jnp.int32, (keys, heads * queries), 0)).astype(
        jnp.float32
    )
    return jnp.where((key >= start) & (key <= query), 0.0, MASKED)


def score_pair(k, q, v, do, bias):
    return dot(k, q, 1, 1) * (SCALE * LOG2E) + bias, dot(v, do, 1, 1)


def softmax_columns(pairs):
    tops = [jnp.max(s, axis=0, keepdims=True) for s, _ in pairs]
    raws = [jnp.exp2(s - top) for (s, _), top in zip(pairs, tops)]
    totals = [jnp.sum(raw, axis=0, keepdims=True) for raw in raws]
    weights = [raw * (1.0 / total) for raw, total in zip(raws, totals)]
    deltas = [jnp.sum(w * dp, axis=0, keepdims=True) for w, (_, dp) in zip(weights, pairs)]
    logs = [top + jnp.log2(total) for top, total in zip(tops, totals)]
    return weights, logs, deltas


def score_grads_of(pairs, weights, deltas):
    return [
        (w * (dp - delta) * SCALE).astype(jnp.bfloat16)
        for w, (_, dp), delta in zip(weights, pairs, deltas)
    ]


def merged_columns(pairs, own):
    tops = [
        jnp.maximum(jnp.max(s, axis=0, keepdims=True), log) for (s, _), (log, _) in zip(pairs, own)
    ]
    raws = [jnp.exp2(s - top) for (s, _), top in zip(pairs, tops)]
    own_raws = [jnp.exp2(log - top) for (log, _), top in zip(own, tops)]
    parts = [
        1.0 / (jnp.sum(raw, axis=0, keepdims=True) + own_raw)
        for raw, own_raw in zip(raws, own_raws)
    ]
    weights = [raw * part for raw, part in zip(raws, parts)]
    deltas = [
        jnp.sum(w * dp, axis=0, keepdims=True) + own_raw * part * own_delta
        for w, (_, dp), own_raw, part, (_, own_delta) in zip(weights, pairs, own_raws, parts, own)
    ]
    grads = [w * (dp - delta) * SCALE for w, (_, dp), delta in zip(weights, pairs, deltas)]
    return [w.astype(jnp.bfloat16) for w in weights], [g.astype(jnp.bfloat16) for g in grads]


def side_by_side(rows):
    heads = rows.shape[1] // HEAD_DIM
    zero = jnp.zeros((rows.shape[0], HEAD_DIM), rows.dtype)
    blocks = [rows[:, c] for c in head_columns(0, rows.shape[1])]
    return jnp.concatenate(
        [
            jnp.concatenate([blocks[h] if g == h else zero for g in range(heads)], axis=1)
            for h in range(heads)
        ],
        axis=0,
    )


def head_columns(low, high, heads=1):
    wide = heads * HEAD_DIM
    return [slice(c, c + wide) for c in range(low, high, wide)]


def device_first(tok):
    place = lax.axis_index("seq") * lax.axis_size("head") + lax.axis_index("head")
    return place * tok


def fours(rows):
    table = jnp.concatenate(rows, axis=0)
    half = table.shape[1] // 4
    lane = lax.broadcasted_iota(jnp.int32, (1, table.shape[1]), 1)
    turned = [pltpu.roll(table, turn * half, 1) for turn in (3, 2, 1)]
    merged = []
    for at in range(0, len(rows), 2):
        now, after = slice(at, at + 1), slice(at + 1, at + 2)
        row = jnp.where(lane < 3 * half, turned[1][after], turned[2][after])
        row = jnp.where(lane < 2 * half, turned[0][now], row)
        merged.append(jnp.where(lane < half, table[now], row))
    return merged


def split_bf16(row):
    parts = []
    for _ in range(3):
        part = row.astype(jnp.bfloat16)
        parts.append(part)
        row = row - part.astype(jnp.float32)
    return jnp.concatenate([*parts, jnp.zeros_like(parts[0])], axis=1)


def joined(parts):
    parts = parts.astype(jnp.float32)
    count = parts.shape[1] // 4
    return parts[:, :count] + parts[:, count : 2 * count] + parts[:, 2 * count : 3 * count]


def pack_copies(prior, at, k_ref, v_ref, packed_ref, sems):
    half, tok = prior // 2, k_ref.shape[0]
    rows = pl.ds(tok - (at + 1) * half, half)
    return [
        pltpu.make_async_copy(
            ref.at[rows, :], packed_ref.at[pl.ds(n * half, half), :], sems.at[n]
        )
        for n, ref in enumerate((k_ref, v_ref))
    ]


def fill_masks(prior, tok, len_ref, own_bias_ref, near_bias_ref, lead_bias_ref, tail_bias_ref):
    first, half = device_first(tok), prior // 2
    lengths = len_ref[...].astype(jnp.float32)
    own_bias_ref[...] = bias_by_key(lengths, first + prior, tok - prior, first, tok, 2)
    near_bias_ref[...] = bias_by_key(lengths, first, prior, first - half, prior + half, 2)
    lead_bias_ref[...] = bias_by_key(lengths, first, prior, first - prior, 2 * prior, 2)
    tail_bias_ref[...] = bias_by_key(lengths, first + tok, half, first + tok - prior, prior, 4)


def pack_kernel(prior, len_hbm, k_ref, v_ref, near_ref, *refs):
    *mask_refs, len_ref, sems, len_sem = refs
    copies = pack_copies(prior, 0, k_ref, v_ref, near_ref, sems)
    for copy in copies:
        copy.start()

    @pl.when(lax.axis_index("seq") % 2 == 1)
    def _():
        len_copy = pltpu.make_async_copy(len_hbm, len_ref, len_sem)
        len_copy.start()
        len_copy.wait()
        fill_masks(prior, k_ref.shape[0], len_ref, *mask_refs)

    for copy in copies:
        copy.wait()


def ready_kernel(
    prior, len_hbm, q_hbm, k_hbm, v_hbm, do_hbm, _own, _near, _lead, _tail,
    far_ref, q_ref, k_ref, v_ref, do_ref, *refs,
):
    *mask_refs, len_ref, sems, far_sems, len_sem = refs
    pairs = ((q_hbm, q_ref), (k_hbm, k_ref), (v_hbm, v_ref), (do_hbm, do_ref))
    copies = pack_copies(prior, 1, k_hbm, v_hbm, far_ref, far_sems)
    copies += [pltpu.make_async_copy(hbm, ref, sems.at[n]) for n, (hbm, ref) in enumerate(pairs)]
    for copy in copies:
        copy.start()

    @pl.when(lax.axis_index("seq") % 2 == 0)
    def _():
        len_copy = pltpu.make_async_copy(len_hbm, len_ref, len_sem)
        len_copy.start()
        len_copy.wait()
        fill_masks(prior, k_ref.shape[0], len_ref, *mask_refs)

    for copy in copies:
        copy.wait()


def own_diagonal(both):
    rows = both.shape[0] // 2
    return jnp.concatenate([both[:rows, :HEAD_DIM], both[rows:, HEAD_DIM:]], axis=1)


def pair_columns(at, step):
    wide = 2 * HEAD_DIM
    return [pl.ds(pl.multiple_of(at * step + c, wide), wide) for c in range(0, step, wide)]


def own_kernel(
    prior, step, bias_ref, q_ref, k_ref, v_ref, do_ref, attn_ref, gq_ref, gk_ref, gv_ref
):
    tok, width = k_ref.shape
    late = slice(prior, tok)

    @pl.loop(0, width // step)
    def _(at):
        bias = bias_ref[...]
        columns = pair_columns(at, step)
        queries = [side_by_side(q_ref[late, c]) for c in columns]
        cotangents = [side_by_side(do_ref[late, c]) for c in columns]
        pairs = [
            score_pair(k_ref[:, c], q, v_ref[:, c], do, bias)
            for c, q, do in zip(columns, queries, cotangents)
        ]
        weights, _, deltas = softmax_columns(pairs)
        grads = score_grads_of(pairs, weights, deltas)
        for c, w, g, q, do in zip(columns, weights, grads, queries, cotangents):
            w = w.astype(jnp.bfloat16)
            attn_ref[:, c] = own_diagonal(dot(w, v_ref[:, c], 0, 0)).astype(jnp.bfloat16)
            gq_ref[:, c] = own_diagonal(dot(g, k_ref[:, c], 0, 0)).astype(jnp.bfloat16)
            gk_ref[:, c] = dot(g, q, 1, 0)
            gv_ref[:, c] = dot(w, do, 1, 0)


def near_kernel(
    prior, near_bias_ref, lead_bias_ref, q_ref, k_ref, v_ref, do_ref, near_ref, *back_refs
):
    width, half = q_ref.shape[1], prior // 2
    far = lead_bias_ref[half - 1 : half, 0:1] == 0.0
    key = lax.broadcasted_iota(jnp.int32, (prior + half, 1), 0)
    bias = jnp.where(far & (key < half), MASKED, near_bias_ref[...])
    spare = lax.broadcasted_iota(jnp.int32, (half, 1), 0) == half - 1
    early, first, second = slice(0, prior), slice(0, half), slice(half, prior)
    columns = head_columns(0, width, 2)
    queries = [side_by_side(q_ref[early, c]) for c in columns]
    cotangents = [side_by_side(do_ref[early, c]) for c in columns]
    pairs = []
    for c, q, do in zip(columns, queries, cotangents):
        k = jnp.concatenate([near_ref[first, c], k_ref[early, c]], axis=0)
        v = jnp.concatenate([near_ref[second, c], v_ref[early, c]], axis=0)
        pairs.append(score_pair(k, q, v, do, bias))
    weights, logs, deltas = softmax_columns(pairs)
    weights = [w[:half] for w in weights]
    grads = score_grads_of([(s[:half], dp[:half]) for s, dp in pairs], weights, deltas)
    k_terms = [dot(g, q, 1, 0) for g, q in zip(grads, queries)]
    v_terms = [dot(w.astype(jnp.bfloat16), do, 1, 0) for w, do in zip(weights, cotangents)]
    logs, deltas = fours(logs), fours(deltas)
    for at, c in enumerate(head_columns(0, width, 4)):
        back_ref = back_refs[c.start * len(back_refs) // width]
        low = c.start % back_ref.shape[1]
        here = slice(low, low + c.stop - c.start)
        for row, terms, ref, place in (
            (logs[at], k_terms, q_ref, first), (deltas[at], v_terms, do_ref, second)
        ):
            rows = jnp.where(spare, split_bf16(row), ref[first, c])
            terms = jnp.concatenate(terms[2 * at : 2 * at + 2], axis=1).astype(jnp.bfloat16)
            back_ref[place, here] = jnp.where(far, rows, terms)


def lead_kernel(
    prior, step, bias_ref, q_ref, k_ref, v_ref, do_ref, near_ref, far_ref, gk_part_ref, gv_part_ref,
    attn_late_ref, gq_late_ref, attn_hbm, gq_hbm, gk_hbm, gv_hbm,
    attn_ref, gq_ref, gk_ref, gv_ref, sems, late_sems,
):
    tok, width = q_ref.shape
    half = prior // 2
    early, first, second = slice(0, prior), slice(0, half), slice(half, prior)
    late = pl.ds(prior, tok - prior)
    late_copies = [
        pltpu.make_async_copy(attn_late_ref, attn_hbm.at[late, :], late_sems.at[0]),
        pltpu.make_async_copy(gq_late_ref, gq_hbm.at[late, :], late_sems.at[1]),
    ]
    for copy in late_copies:
        copy.start()

    def copies(at):
        cols = pl.ds(pl.multiple_of(at * step, step), step)
        pairs = ((attn_ref, attn_hbm), (gq_ref, gq_hbm), (gk_ref, gk_hbm), (gv_ref, gv_hbm))
        return [
            pltpu.make_async_copy(ref.at[:, cols], hbm.at[pl.ds(0, prior), cols], sems.at[at, n])
            for n, (ref, hbm) in enumerate(pairs)
        ]

    @pl.loop(0, width // step)
    def _(at):
        bias = bias_ref[...]
        columns = pair_columns(at, step)
        queries = [side_by_side(q_ref[early, c]) for c in columns]
        cotangents = [side_by_side(do_ref[early, c]) for c in columns]
        keys = [
            jnp.concatenate([far_ref[first, c], near_ref[first, c], k_ref[early, c]], axis=0)
            for c in columns
        ]
        values = [
            jnp.concatenate([far_ref[second, c], near_ref[second, c], v_ref[early, c]], axis=0)
            for c in columns
        ]
        pairs = [
            score_pair(k, q, v, do, bias)
            for k, q, v, do in zip(keys, queries, values, cotangents)
        ]
        weights, _, deltas = softmax_columns(pairs)
        grads = score_grads_of(pairs, weights, deltas)
        for n, c in enumerate(columns):
            w, g = weights[n].astype(jnp.bfloat16), grads[n]
            attn_ref[:, c] = own_diagonal(dot(w, values[n], 0, 0)).astype(jnp.bfloat16)
            gq_ref[:, c] = own_diagonal(dot(g, keys[n], 0, 0)).astype(jnp.bfloat16)
            gk = gk_part_ref[early, c] + dot(g[prior:], queries[n], 1, 0)
            gv = gv_part_ref[early, c] + dot(w[prior:], cotangents[n], 1, 0)
            gk_ref[:, c] = gk.astype(jnp.bfloat16)
            gv_ref[:, c] = gv.astype(jnp.bfloat16)
        for copy in copies(at):
            copy.start()

    for at in range(width // step):
        for copy in copies(at):
            copy.wait()
    for copy in late_copies:
        copy.wait()


def tail_half(prior, low, bias_ref, k_ref, v_ref, gk_part_ref, gv_part_ref, after_ref):
    tok, half = k_ref.shape[0], prior // 2
    far = bias_ref[half - 1 : half, 0:1] == 0.0
    bias = jnp.where(far, bias_ref[...], MASKED)
    first, second, last = slice(0, half), slice(half, prior), slice(tok - prior, tok)
    places = head_columns(0, after_ref.shape[1], 4)
    columns = head_columns(low, low + after_ref.shape[1], 4)
    queries = [side_by_side(after_ref[first, p]) for p in places]
    cotangents = [side_by_side(after_ref[second, p]) for p in places]
    pairs = [
        score_pair(k_ref[last, c], q, v_ref[last, c], do, bias)
        for c, q, do in zip(columns, queries, cotangents)
    ]
    own = [
        (joined(after_ref[half - 16 : half, p][15:]), joined(after_ref[prior - 16 : prior, p][15:]))
        for p in places
    ]
    weights, grads = merged_columns(pairs, own)

    def fill(ref, part_ref, lefts, rights, rows):
        for p, c, left, right in zip(places, columns, lefts, rights):
            total = part_ref[last, c] + dot(left, right, 1, 0)
            terms = jnp.where(far, 0.0, after_ref[rows, p].astype(jnp.float32))
            ref[first, p] = total[first].astype(jnp.bfloat16)
            ref[second, p] = (total[second] + terms).astype(jnp.bfloat16)

    return (
        lambda ref: fill(ref, gv_part_ref, weights, cotangents, second),
        lambda ref: fill(ref, gk_part_ref, grads, queries, first),
    )


def tail_kernel(prior, bias_ref, k_ref, v_ref, gk_part_ref, gv_part_ref, after_ref, gk_ref, gv_ref):
    fill_gv, fill_gk = tail_half(
        prior, 0, bias_ref, k_ref, v_ref, gk_part_ref, gv_part_ref, after_ref
    )
    fill_gv(gv_ref)
    fill_gk(gk_ref)


def last_kernel(
    prior, bias_ref, k_ref, v_ref, gk_part_ref, gv_part_ref, after_ref, gk_first_ref, gv_first_ref,
    gk_in, gv_in, gk_hbm, gv_hbm, gk_ref, gv_ref, sems,
):
    rows = pl.ds(k_ref.shape[0] - prior, prior)
    low = gk_first_ref.shape[1]
    copies = []

    def send(ref, hbm, start):
        cols = pl.ds(start, ref.shape[1])
        copies.append(pltpu.make_async_copy(ref, hbm.at[rows, cols], sems.at[len(copies)]))
        copies[-1].start()

    send(gv_first_ref, gv_hbm, 0)
    send(gk_first_ref, gk_hbm, 0)
    fill_gv, fill_gk = tail_half(
        prior, low, bias_ref, k_ref, v_ref, gk_part_ref, gv_part_ref, after_ref
    )
    fill_gv(gv_ref)
    send(gv_ref, gv_hbm, low)
    fill_gk(gk_ref)
    send(gk_ref, gk_hbm, low)
    for copy in copies:
        copy.wait()


def neighbour(value, by):
    peers = lax.axis_size("seq") * lax.axis_size("head")
    pairs = [(i, i + by) for i in range(peers) if 0 <= i + by < peers]
    return lax.ppermute(value, ("seq", "head"), pairs)


def cost(heads, queries, keys, products, moved):
    return pl.CostEstimate(
        flops=2 * heads * queries * keys * HEAD_DIM * products,
        bytes_accessed=moved,
        transcendentals=heads * queries * keys,
    )


def halo_shards(query_in, key_in, value_in, grad_out, module_lengths):
    tok, width = query_in.shape
    prior = tok * lax.axis_size("head") // 8
    step = math.gcd(width, 8 * HEAD_DIM)
    groups = width // step
    anywhere = pl.BlockSpec(memory_space=pl.ANY)
    inside = pl.BlockSpec(memory_space=pltpu.VMEM)
    full16 = jax.ShapeDtypeStruct((tok, width), jnp.bfloat16)

    def near16(rows, columns):
        return pltpu.VMEM((rows, columns), jnp.bfloat16)

    def near32(rows, columns):
        return pltpu.VMEM((rows, columns), jnp.float32)

    def in_hbm(*values):
        return [pltpu.with_memory_space_constraint(value, pltpu.HBM) for value in values]

    def in_vmem(*values):
        return [pltpu.with_memory_space_constraint(value, pltpu.VMEM) for value in values]

    def call(kernel, name, ins, outs, shapes, scratch, work, moved, aliases=None):
        return pl.pallas_call(
            kernel,
            in_specs=ins,
            out_specs=outs,
            out_shape=shapes,
            scratch_shapes=scratch,
            input_output_aliases=aliases or {},
            cost_estimate=cost(*work, moved),
            compiler_params=pltpu.CompilerParams(vmem_limit_bytes=16 * 2**20),
            name=name,
        )

    lengths = module_lengths.reshape(1, -1)
    len_row = pltpu.VMEM(lengths.shape, jnp.int32)
    mask_shapes = [
        near32(tok, 2 * prior), near32(prior + prior // 2, 2 * prior),
        near32(2 * prior, 2 * prior), near32(prior, 2 * prior),
    ]
    near, *masks = call(
        functools.partial(pack_kernel, prior), "near_keys",
        [anywhere] * 3, [inside] * 5, [near16(prior, width), *mask_shapes],
        [len_row, pltpu.SemaphoreType.DMA((2,)), pltpu.SemaphoreType.DMA(())],
        (0, 0, 0, 0), 4 * prior * width,
    )(*in_hbm(lengths, key_in, value_in))
    near = neighbour(near, 1)

    far, q, k, v, do, own_bias, near_bias, lead_bias, tail_bias = call(
        functools.partial(ready_kernel, prior), "operands",
        [anywhere] * 5 + [inside] * 4, [inside] * 9,
        [near16(prior, width)] + [near16(tok, width)] * 4 + mask_shapes,
        [
            len_row, pltpu.SemaphoreType.DMA((4,)), pltpu.SemaphoreType.DMA((2,)),
            pltpu.SemaphoreType.DMA(()),
        ],
        (0, 0, 0, 0), 18 * tok * width, {5: 5, 6: 6, 7: 7, 8: 8},
    )(*in_hbm(lengths, query_in, key_in, value_in, grad_out), *in_vmem(*masks))
    far = neighbour(far, 1)

    attn, gq, gk_part, gv_part = call(
        functools.partial(own_kernel, prior, step), "own_block",
        [inside] * 5, [inside] * 4,
        [near16(tok - prior, width)] * 2 + [near32(tok, width)] * 2, (),
        (width // HEAD_DIM, tok - prior, tok, 6), 18 * tok * width,
    )(*in_vmem(own_bias, q, k, v, do))

    near_bias, attn = lax.optimization_barrier((near_bias, attn))
    backs = call(
        functools.partial(near_kernel, prior), "near_terms",
        [inside] * 7, [inside] * 2, [near16(prior, width // 2)] * 2, (),
        (width // HEAD_DIM, prior, prior + prior // 2, 3), 8 * tok * width,
    )(*in_vmem(near_bias, lead_bias, q, k, v, do, near))
    backs = [neighbour(back, -1) for back in backs]

    attn, gq, gk, gv = call(
        functools.partial(lead_kernel, prior, step), "lead_rows",
        [inside] * 11, [anywhere] * 4, [full16] * 4,
        [near16(prior, width)] * 4
        + [pltpu.SemaphoreType.DMA((groups, 4)), pltpu.SemaphoreType.DMA((2,))],
        (width // HEAD_DIM, prior, 2 * prior, 6), 20 * tok * width,
    )(*in_vmem(lead_bias, q, k, v, do, near, far, gk_part, gv_part, attn, gq))

    here = in_vmem(tail_bias, k, v, gk_part, gv_part)
    work = (width // HEAD_DIM // 2, prior, prior // 2, 4)
    halves = call(
        functools.partial(tail_kernel, prior), "tail_keys",
        [inside] * 6, [inside] * 2, [near16(prior, width // 2)] * 2, (), work, 4 * tok * width,
    )(*here, *in_vmem(backs[0]))
    gk, gv = call(
        functools.partial(last_kernel, prior), "last_keys",
        [inside] * 8 + [anywhere] * 2, [anywhere] * 2, [full16] * 2,
        [near16(prior, width // 2)] * 2 + [pltpu.SemaphoreType.DMA((4,))],
        work, 6 * tok * width, {8: 0, 9: 1},
    )(*here, *in_vmem(backs[1], *halves), gk, gv)
    return (attn, gq, gk, gv)


def shards(query_in, key_in, value_in, grad_out, module_lengths):
    tok = query_in.shape[0]
    prior = tok * lax.axis_size("head") // 8
    plan = halo_shards if 2 * prior == tok else gathered_shards
    return plan(query_in, key_in, value_in, grad_out, module_lengths)


def solution(mesh):
    placed = (
        P(("seq", "head"), None),
        P(("seq", "head"), None),
        P(("seq", "head"), None),
        P(("seq", "head"), None),
        P(),
    )
    return jax.shard_map(
        shards,
        mesh=mesh,
        in_specs=placed,
        out_specs=(
            P(("seq", "head"), None),
            P(("seq", "head"), None),
            P(("seq", "head"), None),
            P(("seq", "head"), None),
        ),
        check_vma=False,
    )
```

```python
import functools
import math

import jax
import jax.numpy as jnp
from jax import lax
from jax.experimental import pallas as pl
from jax.experimental.pallas import tpu as pltpu
from jax.sharding import PartitionSpec as P

HEAD_DIM = 128
SCALE = HEAD_DIM ** (-0.5)
LOG2E = math.log2(math.e)
MASKED = -1e30


def shifted(value, axis, by):
    peers = lax.axis_size(axis)
    pairs = [(i, i + by) for i in range(peers) if 0 <= i + by < peers]
    return lax.ppermute(value, axis, pairs)


def module_ids(module_lengths, positions):
    module_ends = jnp.cumsum(module_lengths)
    counted = jnp.sum((positions[:, None] >= module_ends[None, :]).astype(jnp.int32), axis=1)
    return jnp.where(positions >= 0, counted, -1)


def allowed_pairs(module_lengths, query_pos, key_pos):
    same = (
        module_ids(module_lengths, query_pos)[:, None]
        == module_ids(module_lengths, key_pos)[None, :]
    )
    return same & (key_pos[None, :] <= query_pos[:, None])


def score_grads(grad_rows, value_block, weights, row_delta, score_scale):
    dprobs = jnp.einsum("qd,kd->qk", grad_rows, value_block, preferred_element_type=jnp.float32)
    return (weights * (dprobs - row_delta[:, None]) * score_scale).astype(jnp.bfloat16)


def key_terms(dscores, weight_bf, query_rows, grad_rows):
    key_grad = jnp.einsum("qk,qd->kd", dscores, query_rows, preferred_element_type=jnp.float32)
    value_grad = jnp.einsum("qk,qd->kd", weight_bf, grad_rows, preferred_element_type=jnp.float32)
    return (key_grad, value_grad)


def one_block(query_rows, key_block, value_block, grad_rows, allowed, score_scale):
    scores = (
        jnp.einsum("qd,kd->qk", query_rows, key_block, preferred_element_type=jnp.float32)
        * score_scale
    )
    row_top = jnp.max(jnp.where(allowed, scores, -jnp.inf), axis=1, keepdims=True)
    row_total = jnp.sum(jnp.where(allowed, jnp.exp(scores - row_top), 0.0), axis=1, keepdims=True)
    log_total = row_top + jnp.log(row_total)
    weights = jnp.where(allowed, jnp.exp(scores - log_total), 0.0)
    weight_bf = weights.astype(jnp.bfloat16)
    attn_rows = jnp.einsum(
        "qk,kd->qd", weight_bf, value_block, preferred_element_type=jnp.float32
    ).astype(jnp.bfloat16)
    row_delta = jnp.sum(grad_rows.astype(jnp.float32) * attn_rows.astype(jnp.float32), axis=1)
    dscores = score_grads(grad_rows, value_block, weights, row_delta, score_scale)
    grad_q = jnp.einsum("qk,kd->qd", dscores, key_block, preferred_element_type=jnp.float32).astype(
        jnp.bfloat16
    )
    key_grad, value_grad = key_terms(dscores, weight_bf, query_rows, grad_rows)
    return (attn_rows, grad_q, key_grad, value_grad, log_total[:, 0], row_delta)


def gathered_shards(query_in, key_in, value_in, grad_out, module_lengths):
    head_q, head_k, head_v, head_do = (
        lax.all_to_all(query_in, "head", split_axis=1, concat_axis=0, tiled=True),
        lax.all_to_all(key_in, "head", split_axis=1, concat_axis=0, tiled=True),
        lax.all_to_all(value_in, "head", split_axis=1, concat_axis=0, tiled=True),
        lax.all_to_all(grad_out, "head", split_axis=1, concat_axis=0, tiled=True),
    )
    row_count = head_q.shape[0]
    width = head_q.shape[1]
    local_heads = width // HEAD_DIM
    prior_rows = row_count // 8
    score_scale = HEAD_DIM ** (-0.5)
    tail_start = row_count - prior_rows
    prior_k, prior_v = shifted((head_k[tail_start:], head_v[tail_start:]), "seq", 1)
    row_start = lax.axis_index("seq") * row_count
    query_pos = row_start + jnp.arange(row_count, dtype=jnp.int32)
    before_pos = row_start - prior_rows + jnp.arange(prior_rows, dtype=jnp.int32)
    key_pos = jnp.concatenate([before_pos, query_pos])
    block_rows = math.gcd(row_count, 512)
    block_count = row_count // block_rows
    pos_blocks = query_pos.reshape(block_count, block_rows)

    def by_head(flat, rows):
        return jnp.moveaxis(flat.reshape(rows, local_heads, HEAD_DIM), 1, 0)

    def to_flat(stacked):
        return jnp.moveaxis(stacked, 0, 1).reshape(stacked.shape[1], width)

    query_h = by_head(head_q, row_count)
    grad_h = by_head(head_do, row_count)
    key_h = by_head(jnp.concatenate([prior_k, head_k], axis=0), row_count + prior_rows)
    value_h = by_head(jnp.concatenate([prior_v, head_v], axis=0), row_count + prior_rows)

    def run_head(packed):
        query_rows, key_block, value_block, grad_rows = packed
        query_blocks = query_rows.reshape(block_count, block_rows, HEAD_DIM)
        grad_blocks = grad_rows.reshape(block_count, block_rows, HEAD_DIM)

        def run_block(inner):
            query_part, grad_part, pos_part = inner
            allowed = allowed_pairs(module_lengths, pos_part, key_pos)
            return one_block(query_part, key_block, value_block, grad_part, allowed, score_scale)

        attn_b, grad_qb, key_b, value_b, lse_b, delta_b = lax.map(
            run_block, (query_blocks, grad_blocks, pos_blocks)
        )
        return (
            attn_b.reshape(row_count, HEAD_DIM),
            grad_qb.reshape(row_count, HEAD_DIM),
            jnp.sum(key_b, axis=0),
            jnp.sum(value_b, axis=0),
            lse_b.reshape(row_count),
            delta_b.reshape(row_count),
        )

    attn_h, grad_qh, key_grad, value_grad, log_total, row_delta = lax.map(
        run_head, (query_h, key_h, value_h, grad_h)
    )
    attn_flat = to_flat(attn_h)
    attn_back = lax.all_to_all(attn_flat, "head", split_axis=0, concat_axis=1, tiled=True)
    grad_q = to_flat(grad_qh)
    later_k, later_v = shifted((key_grad[:, :prior_rows], value_grad[:, :prior_rows]), "seq", -1)
    key_total = key_grad[:, prior_rows:].at[:, tail_start:].add(later_k)
    value_total = value_grad[:, prior_rows:].at[:, tail_start:].add(later_v)
    grad_k = to_flat(key_total.astype(jnp.bfloat16))
    grad_v = to_flat(value_total.astype(jnp.bfloat16))
    back_q, back_k, back_v = (
        lax.all_to_all(grad_q, "head", split_axis=0, concat_axis=1, tiled=True),
        lax.all_to_all(grad_k, "head", split_axis=0, concat_axis=1, tiled=True),
        lax.all_to_all(grad_v, "head", split_axis=0, concat_axis=1, tiled=True),
    )
    return (attn_back, back_q, back_k, back_v)


def dot(left, right, left_dim, right_dim):
    return lax.dot_general(
        left, right, (((left_dim,), (right_dim,)), ((), ())), preferred_element_type=jnp.float32
    )


def module_ends_col(lengths_row):
    count = lengths_row.shape[1]
    row = lax.broadcasted_iota(jnp.int32, (count, count), 0)
    col = lax.broadcasted_iota(jnp.int32, (count, count), 1)
    return jnp.sum(jnp.where(col <= row, lengths_row, 0.0), axis=1, keepdims=True)


def bias_by_key(lengths_row, first_query, queries, first_key, keys, heads):
    ends = module_ends_col(lengths_row)
    lane = lax.broadcasted_iota(jnp.int32, (1, heads * queries), 1)
    query = (first_query + lane % queries).astype(jnp.float32)
    start = jnp.max(jnp.where(ends <= query, ends, 0.0), axis=0, keepdims=True)
    key = (first_key + lax.broadcasted_iota(jnp.int32, (keys, heads * queries), 0)).astype(
        jnp.float32
    )
    return jnp.where((key >= start) & (key <= query), 0.0, MASKED)


def score_pair(k, q, v, do, bias):
    return dot(k, q, 1, 1) * (SCALE * LOG2E) + bias, dot(v, do, 1, 1)


def softmax_columns(pairs):
    tops = [jnp.max(s, axis=0, keepdims=True) for s, _ in pairs]
    raws = [jnp.exp2(s - top) for (s, _), top in zip(pairs, tops)]
    totals = [jnp.sum(raw, axis=0, keepdims=True) for raw in raws]
    weights = [raw * (1.0 / total) for raw, total in zip(raws, totals)]
    deltas = [jnp.sum(w * dp, axis=0, keepdims=True) for w, (_, dp) in zip(weights, pairs)]
    logs = [top + jnp.log2(total) for top, total in zip(tops, totals)]
    return weights, logs, deltas


def score_grads_of(pairs, weights, deltas):
    return [
        (w * (dp - delta) * SCALE).astype(jnp.bfloat16)
        for w, (_, dp), delta in zip(weights, pairs, deltas)
    ]


def merged_columns(pairs, own):
    tops = [
        jnp.maximum(jnp.max(s, axis=0, keepdims=True), log) for (s, _), (log, _) in zip(pairs, own)
    ]
    raws = [jnp.exp2(s - top) for (s, _), top in zip(pairs, tops)]
    own_raws = [jnp.exp2(log - top) for (log, _), top in zip(own, tops)]
    parts = [
        1.0 / (jnp.sum(raw, axis=0, keepdims=True) + own_raw)
        for raw, own_raw in zip(raws, own_raws)
    ]
    weights = [raw * part for raw, part in zip(raws, parts)]
    deltas = [
        jnp.sum(w * dp, axis=0, keepdims=True) + own_raw * part * own_delta
        for w, (_, dp), own_raw, part, (_, own_delta) in zip(weights, pairs, own_raws, parts, own)
    ]
    grads = [w * (dp - delta) * SCALE for w, (_, dp), delta in zip(weights, pairs, deltas)]
    return [w.astype(jnp.bfloat16) for w in weights], [g.astype(jnp.bfloat16) for g in grads]


def side_by_side(rows):
    heads = rows.shape[1] // HEAD_DIM
    zero = jnp.zeros((rows.shape[0], HEAD_DIM), rows.dtype)
    blocks = [rows[:, c] for c in head_columns(0, rows.shape[1])]
    return jnp.concatenate(
        [
            jnp.concatenate([blocks[h] if g == h else zero for g in range(heads)], axis=1)
            for h in range(heads)
        ],
        axis=0,
    )


def head_columns(low, high, heads=1):
    wide = heads * HEAD_DIM
    return [slice(c, c + wide) for c in range(low, high, wide)]


def device_first(tok):
    place = lax.axis_index("seq") * lax.axis_size("head") + lax.axis_index("head")
    return place * tok


def fours(rows):
    table = jnp.concatenate(rows, axis=0)
    half = table.shape[1] // 4
    lane = lax.broadcasted_iota(jnp.int32, (1, table.shape[1]), 1)
    turned = [pltpu.roll(table, turn * half, 1) for turn in (3, 2, 1)]
    merged = []
    for at in range(0, len(rows), 2):
        now, after = slice(at, at + 1), slice(at + 1, at + 2)
        row = jnp.where(lane < 3 * half, turned[1][after], turned[2][after])
        row = jnp.where(lane < 2 * half, turned[0][now], row)
        merged.append(jnp.where(lane < half, table[now], row))
    return merged


def split_bf16(row):
    parts = []
    for _ in range(3):
        part = row.astype(jnp.bfloat16)
        parts.append(part)
        row = row - part.astype(jnp.float32)
    return jnp.concatenate([*parts, jnp.zeros_like(parts[0])], axis=1)


def joined(parts):
    parts = parts.astype(jnp.float32)
    count = parts.shape[1] // 4
    return parts[:, :count] + parts[:, count : 2 * count] + parts[:, 2 * count : 3 * count]


def pack_copies(prior, at, k_ref, v_ref, packed_ref, sems):
    half, tok = prior // 2, k_ref.shape[0]
    rows = pl.ds(tok - (at + 1) * half, half)
    return [
        pltpu.make_async_copy(
            ref.at[rows, :], packed_ref.at[pl.ds(n * half, half), :], sems.at[n]
        )
        for n, ref in enumerate((k_ref, v_ref))
    ]


def fill_masks(prior, tok, len_ref, own_bias_ref, near_bias_ref, lead_bias_ref, tail_bias_ref):
    first, half = device_first(tok), prior // 2
    lengths = len_ref[...].astype(jnp.float32)
    own_bias_ref[...] = bias_by_key(lengths, first + prior, tok - prior, first, tok, 2)
    near_bias_ref[...] = bias_by_key(lengths, first, prior, first - half, prior + half, 2)
    lead_bias_ref[...] = bias_by_key(lengths, first, prior, first - prior, 2 * prior, 2)
    tail_bias_ref[...] = bias_by_key(lengths, first + tok, half, first + tok - prior, prior, 4)


def pack_kernel(prior, len_hbm, k_ref, v_ref, near_ref, *refs):
    *mask_refs, len_ref, sems, len_sem = refs
    copies = pack_copies(prior, 0, k_ref, v_ref, near_ref, sems)
    for copy in copies:
        copy.start()

    for copy in copies:
        copy.wait()

    @pl.when(lax.axis_index("seq") % 2 == 1)
    def _():
        len_copy = pltpu.make_async_copy(len_hbm, len_ref, len_sem)
        len_copy.start()
        len_copy.wait()
        fill_masks(prior, k_ref.shape[0], len_ref, *mask_refs)


def ready_kernel(
    prior, len_hbm, q_hbm, k_hbm, v_hbm, do_hbm, _own, _near, _lead, _tail,
    far_ref, q_ref, k_ref, v_ref, do_ref, *refs,
):
    *mask_refs, len_ref, sems, far_sems, len_sem = refs
    pairs = ((q_hbm, q_ref), (k_hbm, k_ref), (v_hbm, v_ref), (do_hbm, do_ref))
    copies = pack_copies(prior, 1, k_hbm, v_hbm, far_ref, far_sems)
    copies += [pltpu.make_async_copy(hbm, ref, sems.at[n]) for n, (hbm, ref) in enumerate(pairs)]
    for copy in copies:
        copy.start()

    @pl.when(lax.axis_index("seq") % 2 == 0)
    def _():
        len_copy = pltpu.make_async_copy(len_hbm, len_ref, len_sem)
        len_copy.start()
        len_copy.wait()
        fill_masks(prior, k_ref.shape[0], len_ref, *mask_refs)

    for copy in copies:
        copy.wait()


def own_diagonal(both):
    rows = both.shape[0] // 2
    return jnp.concatenate([both[:rows, :HEAD_DIM], both[rows:, HEAD_DIM:]], axis=1)


def pair_columns(at, step):
    wide = 2 * HEAD_DIM
    return [pl.ds(pl.multiple_of(at * step + c, wide), wide) for c in range(0, step, wide)]


def own_kernel(
    prior, step, bias_ref, q_ref, k_ref, v_ref, do_ref, attn_ref, gq_ref, gk_ref, gv_ref
):
    tok, width = k_ref.shape
    late = slice(prior, tok)

    @pl.loop(0, width // step)
    def _(at):
        bias = bias_ref[...]
        columns = pair_columns(at, step)
        queries = [side_by_side(q_ref[late, c]) for c in columns]
        cotangents = [side_by_side(do_ref[late, c]) for c in columns]
        pairs = [
            score_pair(k_ref[:, c], q, v_ref[:, c], do, bias)
            for c, q, do in zip(columns, queries, cotangents)
        ]
        weights, _, deltas = softmax_columns(pairs)
        grads = score_grads_of(pairs, weights, deltas)
        for c, w, g, q, do in zip(columns, weights, grads, queries, cotangents):
            w = w.astype(jnp.bfloat16)
            attn_ref[:, c] = own_diagonal(dot(w, v_ref[:, c], 0, 0)).astype(jnp.bfloat16)
            gq_ref[:, c] = own_diagonal(dot(g, k_ref[:, c], 0, 0)).astype(jnp.bfloat16)
            gk_ref[:, c] = dot(g, q, 1, 0)
            gv_ref[:, c] = dot(w, do, 1, 0)


def near_kernel(
    prior, near_bias_ref, lead_bias_ref, q_ref, k_ref, v_ref, do_ref, near_ref, *back_refs
):
    width, half = q_ref.shape[1], prior // 2
    far = lead_bias_ref[half - 1 : half, 0:1] == 0.0
    key = lax.broadcasted_iota(jnp.int32, (prior + half, 1), 0)
    bias = jnp.where(far & (key < half), MASKED, near_bias_ref[...])
    spare = lax.broadcasted_iota(jnp.int32, (half, 1), 0) == half - 1
    early, first, second = slice(0, prior), slice(0, half), slice(half, prior)
    columns = head_columns(0, width, 2)
    queries = [side_by_side(q_ref[early, c]) for c in columns]
    cotangents = [side_by_side(do_ref[early, c]) for c in columns]
    pairs = []
    for c, q, do in zip(columns, queries, cotangents):
        k = jnp.concatenate([near_ref[first, c], k_ref[early, c]], axis=0)
        v = jnp.concatenate([near_ref[second, c], v_ref[early, c]], axis=0)
        pairs.append(score_pair(k, q, v, do, bias))
    weights, logs, deltas = softmax_columns(pairs)
    weights = [w[:half] for w in weights]
    grads = score_grads_of([(s[:half], dp[:half]) for s, dp in pairs], weights, deltas)
    k_terms = [dot(g, q, 1, 0) for g, q in zip(grads, queries)]
    v_terms = [dot(w.astype(jnp.bfloat16), do, 1, 0) for w, do in zip(weights, cotangents)]
    logs, deltas = fours(logs), fours(deltas)
    for at, c in enumerate(head_columns(0, width, 4)):
        back_ref = back_refs[c.start * len(back_refs) // width]
        low = c.start % back_ref.shape[1]
        here = slice(low, low + c.stop - c.start)
        for row, terms, ref, place in (
            (logs[at], k_terms, q_ref, first), (deltas[at], v_terms, do_ref, second)
        ):
            rows = jnp.where(spare, split_bf16(row), ref[first, c])
            terms = jnp.concatenate(terms[2 * at : 2 * at + 2], axis=1).astype(jnp.bfloat16)
            back_ref[place, here] = jnp.where(far, rows, terms)


def lead_kernel(
    prior, step, bias_ref, q_ref, k_ref, v_ref, do_ref, near_ref, far_ref, gk_part_ref, gv_part_ref,
    attn_late_ref, gq_late_ref, attn_hbm, gq_hbm, gk_hbm, gv_hbm,
    attn_ref, gq_ref, gk_ref, gv_ref, sems, late_sems,
):
    tok, width = q_ref.shape
    half = prior // 2
    early, first, second = slice(0, prior), slice(0, half), slice(half, prior)
    late = pl.ds(prior, tok - prior)
    late_copies = [
        pltpu.make_async_copy(attn_late_ref, attn_hbm.at[late, :], late_sems.at[0]),
        pltpu.make_async_copy(gq_late_ref, gq_hbm.at[late, :], late_sems.at[1]),
    ]
    for copy in late_copies:
        copy.start()

    def copies(at):
        cols = pl.ds(pl.multiple_of(at * step, step), step)
        pairs = ((attn_ref, attn_hbm), (gq_ref, gq_hbm), (gk_ref, gk_hbm), (gv_ref, gv_hbm))
        return [
            pltpu.make_async_copy(ref.at[:, cols], hbm.at[pl.ds(0, prior), cols], sems.at[at, n])
            for n, (ref, hbm) in enumerate(pairs)
        ]

    @pl.loop(0, width // step)
    def _(at):
        bias = bias_ref[...]
        columns = pair_columns(at, step)
        queries = [side_by_side(q_ref[early, c]) for c in columns]
        cotangents = [side_by_side(do_ref[early, c]) for c in columns]
        keys = [
            jnp.concatenate([far_ref[first, c], near_ref[first, c], k_ref[early, c]], axis=0)
            for c in columns
        ]
        values = [
            jnp.concatenate([far_ref[second, c], near_ref[second, c], v_ref[early, c]], axis=0)
            for c in columns
        ]
        pairs = [
            score_pair(k, q, v, do, bias)
            for k, q, v, do in zip(keys, queries, values, cotangents)
        ]
        weights, _, deltas = softmax_columns(pairs)
        grads = score_grads_of(pairs, weights, deltas)
        for n, c in enumerate(columns):
            w, g = weights[n].astype(jnp.bfloat16), grads[n]
            attn_ref[:, c] = own_diagonal(dot(w, values[n], 0, 0)).astype(jnp.bfloat16)
            gq_ref[:, c] = own_diagonal(dot(g, keys[n], 0, 0)).astype(jnp.bfloat16)
            gk = gk_part_ref[early, c] + dot(g[prior:], queries[n], 1, 0)
            gv = gv_part_ref[early, c] + dot(w[prior:], cotangents[n], 1, 0)
            gk_ref[:, c] = gk.astype(jnp.bfloat16)
            gv_ref[:, c] = gv.astype(jnp.bfloat16)
        for copy in copies(at):
            copy.start()

    for at in range(width // step):
        for copy in copies(at):
            copy.wait()
    for copy in late_copies:
        copy.wait()


def tail_half(prior, low, bias_ref, k_ref, v_ref, gk_part_ref, gv_part_ref, after_ref):
    tok, half = k_ref.shape[0], prior // 2
    far = bias_ref[half - 1 : half, 0:1] == 0.0
    bias = jnp.where(far, bias_ref[...], MASKED)
    first, second, last = slice(0, half), slice(half, prior), slice(tok - prior, tok)
    places = head_columns(0, after_ref.shape[1], 4)
    columns = head_columns(low, low + after_ref.shape[1], 4)
    queries = [side_by_side(after_ref[first, p]) for p in places]
    cotangents = [side_by_side(after_ref[second, p]) for p in places]
    pairs = [
        score_pair(k_ref[last, c], q, v_ref[last, c], do, bias)
        for c, q, do in zip(columns, queries, cotangents)
    ]
    own = [
        (joined(after_ref[half - 16 : half, p][15:]), joined(after_ref[prior - 16 : prior, p][15:]))
        for p in places
    ]
    weights, grads = merged_columns(pairs, own)

    def fill(ref, part_ref, lefts, rights, rows):
        for p, c, left, right in zip(places, columns, lefts, rights):
            total = part_ref[last, c] + dot(left, right, 1, 0)
            terms = jnp.where(far, 0.0, after_ref[rows, p].astype(jnp.float32))
            ref[first, p] = total[first].astype(jnp.bfloat16)
            ref[second, p] = (total[second] + terms).astype(jnp.bfloat16)

    return (
        lambda ref: fill(ref, gv_part_ref, weights, cotangents, second),
        lambda ref: fill(ref, gk_part_ref, grads, queries, first),
    )


def tail_kernel(prior, bias_ref, k_ref, v_ref, gk_part_ref, gv_part_ref, after_ref, gk_ref, gv_ref):
    fill_gv, fill_gk = tail_half(
        prior, 0, bias_ref, k_ref, v_ref, gk_part_ref, gv_part_ref, after_ref
    )
    fill_gv(gv_ref)
    fill_gk(gk_ref)


def last_kernel(
    prior, bias_ref, k_ref, v_ref, gk_part_ref, gv_part_ref, after_ref, gk_first_ref, gv_first_ref,
    gk_in, gv_in, gk_hbm, gv_hbm, gk_ref, gv_ref, sems,
):
    rows = pl.ds(k_ref.shape[0] - prior, prior)
    low = gk_first_ref.shape[1]
    copies = []

    def send(ref, hbm, start):
        cols = pl.ds(start, ref.shape[1])
        copies.append(pltpu.make_async_copy(ref, hbm.at[rows, cols], sems.at[len(copies)]))
        copies[-1].start()

    send(gv_first_ref, gv_hbm, 0)
    send(gk_first_ref, gk_hbm, 0)
    fill_gv, fill_gk = tail_half(
        prior, low, bias_ref, k_ref, v_ref, gk_part_ref, gv_part_ref, after_ref
    )
    fill_gv(gv_ref)
    send(gv_ref, gv_hbm, low)
    fill_gk(gk_ref)
    send(gk_ref, gk_hbm, low)
    for copy in copies:
        copy.wait()


def neighbour(value, by):
    peers = lax.axis_size("seq") * lax.axis_size("head")
    pairs = [(i, i + by) for i in range(peers) if 0 <= i + by < peers]
    return lax.ppermute(value, ("seq", "head"), pairs)


def cost(heads, queries, keys, products, moved):
    return pl.CostEstimate(
        flops=2 * heads * queries * keys * HEAD_DIM * products,
        bytes_accessed=moved,
        transcendentals=heads * queries * keys,
    )


def halo_shards(query_in, key_in, value_in, grad_out, module_lengths):
    tok, width = query_in.shape
    prior = tok * lax.axis_size("head") // 8
    step = math.gcd(width, 8 * HEAD_DIM)
    groups = width // step
    anywhere = pl.BlockSpec(memory_space=pl.ANY)
    inside = pl.BlockSpec(memory_space=pltpu.VMEM)
    full16 = jax.ShapeDtypeStruct((tok, width), jnp.bfloat16)

    def near16(rows, columns):
        return pltpu.VMEM((rows, columns), jnp.bfloat16)

    def near32(rows, columns):
        return pltpu.VMEM((rows, columns), jnp.float32)

    def in_hbm(*values):
        return [pltpu.with_memory_space_constraint(value, pltpu.HBM) for value in values]

    def in_vmem(*values):
        return [pltpu.with_memory_space_constraint(value, pltpu.VMEM) for value in values]

    def call(kernel, name, ins, outs, shapes, scratch, work, moved, aliases=None):
        return pl.pallas_call(
            kernel,
            in_specs=ins,
            out_specs=outs,
            out_shape=shapes,
            scratch_shapes=scratch,
            input_output_aliases=aliases or {},
            cost_estimate=cost(*work, moved),
            compiler_params=pltpu.CompilerParams(vmem_limit_bytes=16 * 2**20),
            name=name,
        )

    lengths = module_lengths.reshape(1, -1)
    len_row = pltpu.VMEM(lengths.shape, jnp.int32)
    mask_shapes = [
        near32(tok, 2 * prior), near32(prior + prior // 2, 2 * prior),
        near32(2 * prior, 2 * prior), near32(prior, 2 * prior),
    ]
    near, *masks = call(
        functools.partial(pack_kernel, prior), "near_keys",
        [anywhere] * 3, [inside] * 5, [near16(prior, width), *mask_shapes],
        [len_row, pltpu.SemaphoreType.DMA((2,)), pltpu.SemaphoreType.DMA(())],
        (0, 0, 0, 0), 4 * prior * width,
    )(*in_hbm(lengths, key_in, value_in))
    near = neighbour(near, 1)

    far, q, k, v, do, own_bias, near_bias, lead_bias, tail_bias = call(
        functools.partial(ready_kernel, prior), "operands",
        [anywhere] * 5 + [inside] * 4, [inside] * 9,
        [near16(prior, width)] + [near16(tok, width)] * 4 + mask_shapes,
        [
            len_row, pltpu.SemaphoreType.DMA((4,)), pltpu.SemaphoreType.DMA((2,)),
            pltpu.SemaphoreType.DMA(()),
        ],
        (0, 0, 0, 0), 18 * tok * width, {5: 5, 6: 6, 7: 7, 8: 8},
    )(*in_hbm(lengths, query_in, key_in, value_in, grad_out), *in_vmem(*masks))
    far = neighbour(far, 1)

    attn, gq, gk_part, gv_part = call(
        functools.partial(own_kernel, prior, step), "own_block",
        [inside] * 5, [inside] * 4,
        [near16(tok - prior, width)] * 2 + [near32(tok, width)] * 2, (),
        (width // HEAD_DIM, tok - prior, tok, 6), 18 * tok * width,
    )(*in_vmem(own_bias, q, k, v, do))

    near_bias, attn = lax.optimization_barrier((near_bias, attn))
    backs = call(
        functools.partial(near_kernel, prior), "near_terms",
        [inside] * 7, [inside] * 2, [near16(prior, width // 2)] * 2, (),
        (width // HEAD_DIM, prior, prior + prior // 2, 3), 8 * tok * width,
    )(*in_vmem(near_bias, lead_bias, q, k, v, do, near))
    backs = [neighbour(back, -1) for back in backs]

    attn, gq, gk, gv = call(
        functools.partial(lead_kernel, prior, step), "lead_rows",
        [inside] * 11, [anywhere] * 4, [full16] * 4,
        [near16(prior, width)] * 4
        + [pltpu.SemaphoreType.DMA((groups, 4)), pltpu.SemaphoreType.DMA((2,))],
        (width // HEAD_DIM, prior, 2 * prior, 6), 20 * tok * width,
    )(*in_vmem(lead_bias, q, k, v, do, near, far, gk_part, gv_part, attn, gq))

    here = in_vmem(tail_bias, k, v, gk_part, gv_part)
    work = (width // HEAD_DIM // 2, prior, prior // 2, 4)
    halves = call(
        functools.partial(tail_kernel, prior), "tail_keys",
        [inside] * 6, [inside] * 2, [near16(prior, width // 2)] * 2, (), work, 4 * tok * width,
    )(*here, *in_vmem(backs[0]))
    gk, gv = call(
        functools.partial(last_kernel, prior), "last_keys",
        [inside] * 8 + [anywhere] * 2, [anywhere] * 2, [full16] * 2,
        [near16(prior, width // 2)] * 2 + [pltpu.SemaphoreType.DMA((4,))],
        work, 6 * tok * width, {8: 0, 9: 1},
    )(*here, *in_vmem(backs[1], *halves), gk, gv)
    return (attn, gq, gk, gv)


def shards(query_in, key_in, value_in, grad_out, module_lengths):
    tok = query_in.shape[0]
    prior = tok * lax.axis_size("head") // 8
    plan = halo_shards if 2 * prior == tok else gathered_shards
    return plan(query_in, key_in, value_in, grad_out, module_lengths)


def solution(mesh):
    placed = (
        P(("seq", "head"), None),
        P(("seq", "head"), None),
        P(("seq", "head"), None),
        P(("seq", "head"), None),
        P(),
    )
    return jax.shard_map(
        shards,
        mesh=mesh,
        in_specs=placed,
        out_specs=(
            P(("seq", "head"), None),
            P(("seq", "head"), None),
            P(("seq", "head"), None),
            P(("seq", "head"), None),
        ),
        check_vma=False,
    )
```

```python
import functools
import math

import jax
import jax.numpy as jnp
from jax import lax
from jax.experimental import pallas as pl
from jax.experimental.pallas import tpu as pltpu
from jax.sharding import PartitionSpec as P

HEAD_DIM = 128
SCALE = HEAD_DIM ** (-0.5)
LOG2E = math.log2(math.e)
MASKED = -1e30


def shifted(value, axis, by):
    peers = lax.axis_size(axis)
    pairs = [(i, i + by) for i in range(peers) if 0 <= i + by < peers]
    return lax.ppermute(value, axis, pairs)


def module_ids(module_lengths, positions):
    module_ends = jnp.cumsum(module_lengths)
    counted = jnp.sum((positions[:, None] >= module_ends[None, :]).astype(jnp.int32), axis=1)
    return jnp.where(positions >= 0, counted, -1)


def allowed_pairs(module_lengths, query_pos, key_pos):
    same = (
        module_ids(module_lengths, query_pos)[:, None]
        == module_ids(module_lengths, key_pos)[None, :]
    )
    return same & (key_pos[None, :] <= query_pos[:, None])


def score_grads(grad_rows, value_block, weights, row_delta, score_scale):
    dprobs = jnp.einsum("qd,kd->qk", grad_rows, value_block, preferred_element_type=jnp.float32)
    return (weights * (dprobs - row_delta[:, None]) * score_scale).astype(jnp.bfloat16)


def key_terms(dscores, weight_bf, query_rows, grad_rows):
    key_grad = jnp.einsum("qk,qd->kd", dscores, query_rows, preferred_element_type=jnp.float32)
    value_grad = jnp.einsum("qk,qd->kd", weight_bf, grad_rows, preferred_element_type=jnp.float32)
    return (key_grad, value_grad)


def one_block(query_rows, key_block, value_block, grad_rows, allowed, score_scale):
    scores = (
        jnp.einsum("qd,kd->qk", query_rows, key_block, preferred_element_type=jnp.float32)
        * score_scale
    )
    row_top = jnp.max(jnp.where(allowed, scores, -jnp.inf), axis=1, keepdims=True)
    row_total = jnp.sum(jnp.where(allowed, jnp.exp(scores - row_top), 0.0), axis=1, keepdims=True)
    log_total = row_top + jnp.log(row_total)
    weights = jnp.where(allowed, jnp.exp(scores - log_total), 0.0)
    weight_bf = weights.astype(jnp.bfloat16)
    attn_rows = jnp.einsum(
        "qk,kd->qd", weight_bf, value_block, preferred_element_type=jnp.float32
    ).astype(jnp.bfloat16)
    row_delta = jnp.sum(grad_rows.astype(jnp.float32) * attn_rows.astype(jnp.float32), axis=1)
    dscores = score_grads(grad_rows, value_block, weights, row_delta, score_scale)
    grad_q = jnp.einsum("qk,kd->qd", dscores, key_block, preferred_element_type=jnp.float32).astype(
        jnp.bfloat16
    )
    key_grad, value_grad = key_terms(dscores, weight_bf, query_rows, grad_rows)
    return (attn_rows, grad_q, key_grad, value_grad, log_total[:, 0], row_delta)


def gathered_shards(query_in, key_in, value_in, grad_out, module_lengths):
    head_q, head_k, head_v, head_do = (
        lax.all_to_all(query_in, "head", split_axis=1, concat_axis=0, tiled=True),
        lax.all_to_all(key_in, "head", split_axis=1, concat_axis=0, tiled=True),
        lax.all_to_all(value_in, "head", split_axis=1, concat_axis=0, tiled=True),
        lax.all_to_all(grad_out, "head", split_axis=1, concat_axis=0, tiled=True),
    )
    row_count = head_q.shape[0]
    width = head_q.shape[1]
    local_heads = width // HEAD_DIM
    prior_rows = row_count // 8
    score_scale = HEAD_DIM ** (-0.5)
    tail_start = row_count - prior_rows
    prior_k, prior_v = shifted((head_k[tail_start:], head_v[tail_start:]), "seq", 1)
    row_start = lax.axis_index("seq") * row_count
    query_pos = row_start + jnp.arange(row_count, dtype=jnp.int32)
    before_pos = row_start - prior_rows + jnp.arange(prior_rows, dtype=jnp.int32)
    key_pos = jnp.concatenate([before_pos, query_pos])
    block_rows = math.gcd(row_count, 512)
    block_count = row_count // block_rows
    pos_blocks = query_pos.reshape(block_count, block_rows)

    def by_head(flat, rows):
        return jnp.moveaxis(flat.reshape(rows, local_heads, HEAD_DIM), 1, 0)

    def to_flat(stacked):
        return jnp.moveaxis(stacked, 0, 1).reshape(stacked.shape[1], width)

    query_h = by_head(head_q, row_count)
    grad_h = by_head(head_do, row_count)
    key_h = by_head(jnp.concatenate([prior_k, head_k], axis=0), row_count + prior_rows)
    value_h = by_head(jnp.concatenate([prior_v, head_v], axis=0), row_count + prior_rows)

    def run_head(packed):
        query_rows, key_block, value_block, grad_rows = packed
        query_blocks = query_rows.reshape(block_count, block_rows, HEAD_DIM)
        grad_blocks = grad_rows.reshape(block_count, block_rows, HEAD_DIM)

        def run_block(inner):
            query_part, grad_part, pos_part = inner
            allowed = allowed_pairs(module_lengths, pos_part, key_pos)
            return one_block(query_part, key_block, value_block, grad_part, allowed, score_scale)

        attn_b, grad_qb, key_b, value_b, lse_b, delta_b = lax.map(
            run_block, (query_blocks, grad_blocks, pos_blocks)
        )
        return (
            attn_b.reshape(row_count, HEAD_DIM),
            grad_qb.reshape(row_count, HEAD_DIM),
            jnp.sum(key_b, axis=0),
            jnp.sum(value_b, axis=0),
            lse_b.reshape(row_count),
            delta_b.reshape(row_count),
        )

    attn_h, grad_qh, key_grad, value_grad, log_total, row_delta = lax.map(
        run_head, (query_h, key_h, value_h, grad_h)
    )
    attn_flat = to_flat(attn_h)
    attn_back = lax.all_to_all(attn_flat, "head", split_axis=0, concat_axis=1, tiled=True)
    grad_q = to_flat(grad_qh)
    later_k, later_v = shifted((key_grad[:, :prior_rows], value_grad[:, :prior_rows]), "seq", -1)
    key_total = key_grad[:, prior_rows:].at[:, tail_start:].add(later_k)
    value_total = value_grad[:, prior_rows:].at[:, tail_start:].add(later_v)
    grad_k = to_flat(key_total.astype(jnp.bfloat16))
    grad_v = to_flat(value_total.astype(jnp.bfloat16))
    back_q, back_k, back_v = (
        lax.all_to_all(grad_q, "head", split_axis=0, concat_axis=1, tiled=True),
        lax.all_to_all(grad_k, "head", split_axis=0, concat_axis=1, tiled=True),
        lax.all_to_all(grad_v, "head", split_axis=0, concat_axis=1, tiled=True),
    )
    return (attn_back, back_q, back_k, back_v)


def dot(left, right, left_dim, right_dim):
    return lax.dot_general(
        left, right, (((left_dim,), (right_dim,)), ((), ())), preferred_element_type=jnp.float32
    )


def module_ends_col(lengths_row):
    count = lengths_row.shape[1]
    row = lax.broadcasted_iota(jnp.int32, (count, count), 0)
    col = lax.broadcasted_iota(jnp.int32, (count, count), 1)
    return jnp.sum(jnp.where(col <= row, lengths_row, 0.0), axis=1, keepdims=True)


def bias_by_key(lengths_row, first_query, queries, first_key, keys, heads):
    ends = module_ends_col(lengths_row)
    lane = lax.broadcasted_iota(jnp.int32, (1, heads * queries), 1)
    query = (first_query + lane % queries).astype(jnp.float32)
    start = jnp.max(jnp.where(ends <= query, ends, 0.0), axis=0, keepdims=True)
    key = (first_key + lax.broadcasted_iota(jnp.int32, (keys, heads * queries), 0)).astype(
        jnp.float32
    )
    return jnp.where((key >= start) & (key <= query), 0.0, MASKED)


def score_pair(k, q, v, do, bias):
    return dot(k, q, 1, 1) * (SCALE * LOG2E) + bias, dot(v, do, 1, 1)


def softmax_columns(pairs):
    tops = [jnp.max(s, axis=0, keepdims=True) for s, _ in pairs]
    raws = [jnp.exp2(s - top) for (s, _), top in zip(pairs, tops)]
    totals = [jnp.sum(raw, axis=0, keepdims=True) for raw in raws]
    weights = [raw * (1.0 / total) for raw, total in zip(raws, totals)]
    deltas = [jnp.sum(w * dp, axis=0, keepdims=True) for w, (_, dp) in zip(weights, pairs)]
    logs = [top + jnp.log2(total) for top, total in zip(tops, totals)]
    return weights, logs, deltas


def score_grads_of(pairs, weights, deltas):
    return [
        (w * (dp - delta) * SCALE).astype(jnp.bfloat16)
        for w, (_, dp), delta in zip(weights, pairs, deltas)
    ]


def merged_columns(pairs, own):
    tops = [
        jnp.maximum(jnp.max(s, axis=0, keepdims=True), log) for (s, _), (log, _) in zip(pairs, own)
    ]
    raws = [jnp.exp2(s - top) for (s, _), top in zip(pairs, tops)]
    own_raws = [jnp.exp2(log - top) for (log, _), top in zip(own, tops)]
    parts = [
        1.0 / (jnp.sum(raw, axis=0, keepdims=True) + own_raw)
        for raw, own_raw in zip(raws, own_raws)
    ]
    weights = [raw * part for raw, part in zip(raws, parts)]
    deltas = [
        jnp.sum(w * dp, axis=0, keepdims=True) + own_raw * part * own_delta
        for w, (_, dp), own_raw, part, (_, own_delta) in zip(weights, pairs, own_raws, parts, own)
    ]
    grads = [w * (dp - delta) * SCALE for w, (_, dp), delta in zip(weights, pairs, deltas)]
    return [w.astype(jnp.bfloat16) for w in weights], [g.astype(jnp.bfloat16) for g in grads]


def side_by_side(rows):
    heads = rows.shape[1] // HEAD_DIM
    zero = jnp.zeros((rows.shape[0], HEAD_DIM), rows.dtype)
    blocks = [rows[:, c] for c in head_columns(0, rows.shape[1])]
    return jnp.concatenate(
        [
            jnp.concatenate([blocks[h] if g == h else zero for g in range(heads)], axis=1)
            for h in range(heads)
        ],
        axis=0,
    )


def head_columns(low, high, heads=1):
    wide = heads * HEAD_DIM
    return [slice(c, c + wide) for c in range(low, high, wide)]


def device_first(tok):
    place = lax.axis_index("seq") * lax.axis_size("head") + lax.axis_index("head")
    return place * tok


def fours(rows):
    table = jnp.concatenate(rows, axis=0)
    half = table.shape[1] // 4
    lane = lax.broadcasted_iota(jnp.int32, (1, table.shape[1]), 1)
    turned = [pltpu.roll(table, turn * half, 1) for turn in (3, 2, 1)]
    merged = []
    for at in range(0, len(rows), 2):
        now, after = slice(at, at + 1), slice(at + 1, at + 2)
        row = jnp.where(lane < 3 * half, turned[1][after], turned[2][after])
        row = jnp.where(lane < 2 * half, turned[0][now], row)
        merged.append(jnp.where(lane < half, table[now], row))
    return merged


def split_bf16(row):
    parts = []
    for _ in range(3):
        part = row.astype(jnp.bfloat16)
        parts.append(part)
        row = row - part.astype(jnp.float32)
    return jnp.concatenate([*parts, jnp.zeros_like(parts[0])], axis=1)


def joined(parts):
    parts = parts.astype(jnp.float32)
    count = parts.shape[1] // 4
    return parts[:, :count] + parts[:, count : 2 * count] + parts[:, 2 * count : 3 * count]


def pack_copies(prior, at, k_ref, v_ref, packed_ref, sems):
    half, tok = prior // 2, k_ref.shape[0]
    rows = pl.ds(tok - (at + 1) * half, half)
    return [
        pltpu.make_async_copy(
            ref.at[rows, :], packed_ref.at[pl.ds(n * half, half), :], sems.at[n]
        )
        for n, ref in enumerate((k_ref, v_ref))
    ]


def fill_masks(prior, tok, len_ref, own_bias_ref, near_bias_ref, lead_bias_ref, tail_bias_ref):
    first, half = device_first(tok), prior // 2
    lengths = len_ref[...].astype(jnp.float32)
    own_bias_ref[...] = bias_by_key(lengths, first + prior, tok - prior, first, tok, 2)
    near_bias_ref[...] = bias_by_key(lengths, first, prior, first - half, prior + half, 2)
    lead_bias_ref[...] = bias_by_key(lengths, first, prior, first - prior, 2 * prior, 2)
    tail_bias_ref[...] = bias_by_key(lengths, first + tok, half, first + tok - prior, prior, 4)


def pack_kernel(prior, len_hbm, k_ref, v_ref, near_ref, *refs):
    *mask_refs, len_ref, sems, len_sem = refs
    len_copy = pltpu.make_async_copy(len_hbm, len_ref, len_sem)
    len_copy.start()
    copies = pack_copies(prior, 0, k_ref, v_ref, near_ref, sems)
    for copy in copies:
        copy.start()
    len_copy.wait()
    fill_masks(prior, k_ref.shape[0], len_ref, *mask_refs)
    for copy in copies:
        copy.wait()


def ready_kernel(
    prior, q_hbm, k_hbm, v_hbm, do_hbm, far_ref, q_ref, k_ref, v_ref, do_ref, sems, far_sems
):
    pairs = ((q_hbm, q_ref), (k_hbm, k_ref), (v_hbm, v_ref), (do_hbm, do_ref))
    copies = pack_copies(prior, 1, k_hbm, v_hbm, far_ref, far_sems)
    copies += [pltpu.make_async_copy(hbm, ref, sems.at[n]) for n, (hbm, ref) in enumerate(pairs)]
    for copy in copies:
        copy.start()
    for copy in copies:
        copy.wait()


def own_diagonal(both):
    rows = both.shape[0] // 2
    return jnp.concatenate([both[:rows, :HEAD_DIM], both[rows:, HEAD_DIM:]], axis=1)


def pair_columns(at, step):
    wide = 2 * HEAD_DIM
    return [pl.ds(pl.multiple_of(at * step + c, wide), wide) for c in range(0, step, wide)]


def own_kernel(
    prior, step, bias_ref, q_ref, k_ref, v_ref, do_ref, attn_ref, gq_ref, gk_ref, gv_ref
):
    tok, width = k_ref.shape
    late = slice(prior, tok)

    @pl.loop(0, width // step)
    def _(at):
        bias = bias_ref[...]
        columns = pair_columns(at, step)
        queries = [side_by_side(q_ref[late, c]) for c in columns]
        cotangents = [side_by_side(do_ref[late, c]) for c in columns]
        pairs = [
            score_pair(k_ref[:, c], q, v_ref[:, c], do, bias)
            for c, q, do in zip(columns, queries, cotangents)
        ]
        weights, _, deltas = softmax_columns(pairs)
        grads = score_grads_of(pairs, weights, deltas)
        for c, w, g, q, do in zip(columns, weights, grads, queries, cotangents):
            w = w.astype(jnp.bfloat16)
            attn_ref[:, c] = own_diagonal(dot(w, v_ref[:, c], 0, 0)).astype(jnp.bfloat16)
            gq_ref[:, c] = own_diagonal(dot(g, k_ref[:, c], 0, 0)).astype(jnp.bfloat16)
            gk_ref[:, c] = dot(g, q, 1, 0)
            gv_ref[:, c] = dot(w, do, 1, 0)


def near_kernel(
    prior, near_bias_ref, lead_bias_ref, q_ref, k_ref, v_ref, do_ref, near_ref, *back_refs
):
    width, half = q_ref.shape[1], prior // 2
    far = lead_bias_ref[half - 1 : half, 0:1] == 0.0
    key = lax.broadcasted_iota(jnp.int32, (prior + half, 1), 0)
    bias = jnp.where(far & (key < half), MASKED, near_bias_ref[...])
    spare = lax.broadcasted_iota(jnp.int32, (half, 1), 0) == half - 1
    early, first, second = slice(0, prior), slice(0, half), slice(half, prior)
    columns = head_columns(0, width, 2)
    queries = [side_by_side(q_ref[early, c]) for c in columns]
    cotangents = [side_by_side(do_ref[early, c]) for c in columns]
    pairs = []
    for c, q, do in zip(columns, queries, cotangents):
        k = jnp.concatenate([near_ref[first, c], k_ref[early, c]], axis=0)
        v = jnp.concatenate([near_ref[second, c], v_ref[early, c]], axis=0)
        pairs.append(score_pair(k, q, v, do, bias))
    weights, logs, deltas = softmax_columns(pairs)
    weights = [w[:half] for w in weights]
    grads = score_grads_of([(s[:half], dp[:half]) for s, dp in pairs], weights, deltas)
    k_terms = [dot(g, q, 1, 0) for g, q in zip(grads, queries)]
    v_terms = [dot(w.astype(jnp.bfloat16), do, 1, 0) for w, do in zip(weights, cotangents)]
    logs, deltas = fours(logs), fours(deltas)
    for at, c in enumerate(head_columns(0, width, 4)):
        back_ref = back_refs[c.start * len(back_refs) // width]
        low = c.start % back_ref.shape[1]
        here = slice(low, low + c.stop - c.start)
        for row, terms, ref, place in (
            (logs[at], k_terms, q_ref, first), (deltas[at], v_terms, do_ref, second)
        ):
            rows = jnp.where(spare, split_bf16(row), ref[first, c])
            terms = jnp.concatenate(terms[2 * at : 2 * at + 2], axis=1).astype(jnp.bfloat16)
            back_ref[place, here] = jnp.where(far, rows, terms)


def lead_kernel(
    prior, step, bias_ref, q_ref, k_ref, v_ref, do_ref, near_ref, far_ref, gk_part_ref, gv_part_ref,
    attn_late_ref, gq_late_ref, attn_hbm, gq_hbm, gk_hbm, gv_hbm,
    attn_ref, gq_ref, gk_ref, gv_ref, sems, late_sems,
):
    tok, width = q_ref.shape
    half = prior // 2
    early, first, second = slice(0, prior), slice(0, half), slice(half, prior)
    late = pl.ds(prior, tok - prior)
    late_copies = [
        pltpu.make_async_copy(attn_late_ref, attn_hbm.at[late, :], late_sems.at[0]),
        pltpu.make_async_copy(gq_late_ref, gq_hbm.at[late, :], late_sems.at[1]),
    ]
    for copy in late_copies:
        copy.start()

    def copies(at):
        cols = pl.ds(pl.multiple_of(at * step, step), step)
        pairs = ((attn_ref, attn_hbm), (gq_ref, gq_hbm), (gk_ref, gk_hbm), (gv_ref, gv_hbm))
        return [
            pltpu.make_async_copy(ref.at[:, cols], hbm.at[pl.ds(0, prior), cols], sems.at[at, n])
            for n, (ref, hbm) in enumerate(pairs)
        ]

    @pl.loop(0, width // step)
    def _(at):
        bias = bias_ref[...]
        columns = pair_columns(at, step)
        queries = [side_by_side(q_ref[early, c]) for c in columns]
        cotangents = [side_by_side(do_ref[early, c]) for c in columns]
        keys = [
            jnp.concatenate([far_ref[first, c], near_ref[first, c], k_ref[early, c]], axis=0)
            for c in columns
        ]
        values = [
            jnp.concatenate([far_ref[second, c], near_ref[second, c], v_ref[early, c]], axis=0)
            for c in columns
        ]
        pairs = [
            score_pair(k, q, v, do, bias)
            for k, q, v, do in zip(keys, queries, values, cotangents)
        ]
        weights, _, deltas = softmax_columns(pairs)
        grads = score_grads_of(pairs, weights, deltas)
        for n, c in enumerate(columns):
            w, g = weights[n].astype(jnp.bfloat16), grads[n]
            attn_ref[:, c] = own_diagonal(dot(w, values[n], 0, 0)).astype(jnp.bfloat16)
            gq_ref[:, c] = own_diagonal(dot(g, keys[n], 0, 0)).astype(jnp.bfloat16)
            gk = gk_part_ref[early, c] + dot(g[prior:], queries[n], 1, 0)
            gv = gv_part_ref[early, c] + dot(w[prior:], cotangents[n], 1, 0)
            gk_ref[:, c] = gk.astype(jnp.bfloat16)
            gv_ref[:, c] = gv.astype(jnp.bfloat16)
        for copy in copies(at):
            copy.start()

    for at in range(width // step):
        for copy in copies(at):
            copy.wait()
    for copy in late_copies:
        copy.wait()


def tail_half(prior, low, bias_ref, k_ref, v_ref, gk_part_ref, gv_part_ref, after_ref):
    tok, half = k_ref.shape[0], prior // 2
    far = bias_ref[half - 1 : half, 0:1] == 0.0
    bias = jnp.where(far, bias_ref[...], MASKED)
    first, second, last = slice(0, half), slice(half, prior), slice(tok - prior, tok)
    places = head_columns(0, after_ref.shape[1], 4)
    columns = head_columns(low, low + after_ref.shape[1], 4)
    queries = [side_by_side(after_ref[first, p]) for p in places]
    cotangents = [side_by_side(after_ref[second, p]) for p in places]
    pairs = [
        score_pair(k_ref[last, c], q, v_ref[last, c], do, bias)
        for c, q, do in zip(columns, queries, cotangents)
    ]
    own = [
        (joined(after_ref[half - 16 : half, p][15:]), joined(after_ref[prior - 16 : prior, p][15:]))
        for p in places
    ]
    weights, grads = merged_columns(pairs, own)

    def fill(ref, part_ref, lefts, rights, rows):
        for p, c, left, right in zip(places, columns, lefts, rights):
            total = part_ref[last, c] + dot(left, right, 1, 0)
            terms = jnp.where(far, 0.0, after_ref[rows, p].astype(jnp.float32))
            ref[first, p] = total[first].astype(jnp.bfloat16)
            ref[second, p] = (total[second] + terms).astype(jnp.bfloat16)

    return (
        lambda ref: fill(ref, gv_part_ref, weights, cotangents, second),
        lambda ref: fill(ref, gk_part_ref, grads, queries, first),
    )


def tail_kernel(prior, bias_ref, k_ref, v_ref, gk_part_ref, gv_part_ref, after_ref, gk_ref, gv_ref):
    fill_gv, fill_gk = tail_half(
        prior, 0, bias_ref, k_ref, v_ref, gk_part_ref, gv_part_ref, after_ref
    )
    fill_gv(gv_ref)
    fill_gk(gk_ref)


def last_kernel(
    prior, bias_ref, k_ref, v_ref, gk_part_ref, gv_part_ref, after_ref, gk_first_ref, gv_first_ref,
    gk_in, gv_in, gk_hbm, gv_hbm, gk_ref, gv_ref, sems,
):
    rows = pl.ds(k_ref.shape[0] - prior, prior)
    low = gk_first_ref.shape[1]
    copies = []

    def send(ref, hbm, start):
        cols = pl.ds(start, ref.shape[1])
        copies.append(pltpu.make_async_copy(ref, hbm.at[rows, cols], sems.at[len(copies)]))
        copies[-1].start()

    send(gv_first_ref, gv_hbm, 0)
    send(gk_first_ref, gk_hbm, 0)
    fill_gv, fill_gk = tail_half(
        prior, low, bias_ref, k_ref, v_ref, gk_part_ref, gv_part_ref, after_ref
    )
    fill_gv(gv_ref)
    send(gv_ref, gv_hbm, low)
    fill_gk(gk_ref)
    send(gk_ref, gk_hbm, low)
    for copy in copies:
        copy.wait()


def neighbour(value, by):
    peers = lax.axis_size("seq") * lax.axis_size("head")
    pairs = [(i, i + by) for i in range(peers) if 0 <= i + by < peers]
    return lax.ppermute(value, ("seq", "head"), pairs)


def cost(heads, queries, keys, products, moved):
    return pl.CostEstimate(
        flops=2 * heads * queries * keys * HEAD_DIM * products,
        bytes_accessed=moved,
        transcendentals=heads * queries * keys,
    )


def halo_shards(query_in, key_in, value_in, grad_out, module_lengths):
    tok, width = query_in.shape
    prior = tok * lax.axis_size("head") // 8
    step = math.gcd(width, 8 * HEAD_DIM)
    groups = width // step
    anywhere = pl.BlockSpec(memory_space=pl.ANY)
    inside = pl.BlockSpec(memory_space=pltpu.VMEM)
    full16 = jax.ShapeDtypeStruct((tok, width), jnp.bfloat16)

    def near16(rows, columns):
        return pltpu.VMEM((rows, columns), jnp.bfloat16)

    def near32(rows, columns):
        return pltpu.VMEM((rows, columns), jnp.float32)

    def in_hbm(*values):
        return [pltpu.with_memory_space_constraint(value, pltpu.HBM) for value in values]

    def in_vmem(*values):
        return [pltpu.with_memory_space_constraint(value, pltpu.VMEM) for value in values]

    def call(kernel, name, ins, outs, shapes, scratch, work, moved, aliases=None):
        return pl.pallas_call(
            kernel,
            in_specs=ins,
            out_specs=outs,
            out_shape=shapes,
            scratch_shapes=scratch,
            input_output_aliases=aliases or {},
            cost_estimate=cost(*work, moved),
            compiler_params=pltpu.CompilerParams(vmem_limit_bytes=16 * 2**20),
            name=name,
        )

    lengths = module_lengths.reshape(1, -1)
    len_row = pltpu.VMEM(lengths.shape, jnp.int32)
    mask_shapes = [
        near32(tok, 2 * prior), near32(prior + prior // 2, 2 * prior),
        near32(2 * prior, 2 * prior), near32(prior, 2 * prior),
    ]
    near, own_bias, near_bias, lead_bias, tail_bias = call(
        functools.partial(pack_kernel, prior), "near_keys",
        [anywhere] * 3, [inside] * 5, [near16(prior, width), *mask_shapes],
        [len_row, pltpu.SemaphoreType.DMA((2,)), pltpu.SemaphoreType.DMA(())],
        (0, 0, 0, 0), 4 * prior * width,
    )(*in_hbm(lengths, key_in, value_in))
    near = neighbour(near, 1)

    far, q, k, v, do = call(
        functools.partial(ready_kernel, prior), "operands",
        [anywhere] * 4, [inside] * 5, [near16(prior, width)] + [near16(tok, width)] * 4,
        [pltpu.SemaphoreType.DMA((4,)), pltpu.SemaphoreType.DMA((2,))],
        (0, 0, 0, 0), 18 * tok * width,
    )(*in_hbm(query_in, key_in, value_in, grad_out))
    far = neighbour(far, 1)

    attn, gq, gk_part, gv_part = call(
        functools.partial(own_kernel, prior, step), "own_block",
        [inside] * 5, [inside] * 4,
        [near16(tok - prior, width)] * 2 + [near32(tok, width)] * 2, (),
        (width // HEAD_DIM, tok - prior, tok, 6), 18 * tok * width,
    )(*in_vmem(own_bias, q, k, v, do))

    near_bias, attn = lax.optimization_barrier((near_bias, attn))
    backs = call(
        functools.partial(near_kernel, prior), "near_terms",
        [inside] * 7, [inside] * 2, [near16(prior, width // 2)] * 2, (),
        (width // HEAD_DIM, prior, prior + prior // 2, 3), 8 * tok * width,
    )(*in_vmem(near_bias, lead_bias, q, k, v, do, near))
    backs = [neighbour(back, -1) for back in backs]

    attn, gq, gk, gv = call(
        functools.partial(lead_kernel, prior, step), "lead_rows",
        [inside] * 11, [anywhere] * 4, [full16] * 4,
        [near16(prior, width)] * 4
        + [pltpu.SemaphoreType.DMA((groups, 4)), pltpu.SemaphoreType.DMA((2,))],
        (width // HEAD_DIM, prior, 2 * prior, 6), 20 * tok * width,
    )(*in_vmem(lead_bias, q, k, v, do, near, far, gk_part, gv_part, attn, gq))

    here = in_vmem(tail_bias, k, v, gk_part, gv_part)
    work = (width // HEAD_DIM // 2, prior, prior // 2, 4)
    halves = call(
        functools.partial(tail_kernel, prior), "tail_keys",
        [inside] * 6, [inside] * 2, [near16(prior, width // 2)] * 2, (), work, 4 * tok * width,
    )(*here, *in_vmem(backs[0]))
    gk, gv = call(
        functools.partial(last_kernel, prior), "last_keys",
        [inside] * 8 + [anywhere] * 2, [anywhere] * 2, [full16] * 2,
        [near16(prior, width // 2)] * 2 + [pltpu.SemaphoreType.DMA((4,))],
        work, 6 * tok * width, {8: 0, 9: 1},
    )(*here, *in_vmem(backs[1], *halves), gk, gv)
    return (attn, gq, gk, gv)


def shards(query_in, key_in, value_in, grad_out, module_lengths):
    tok = query_in.shape[0]
    prior = tok * lax.axis_size("head") // 8
    plan = halo_shards if 2 * prior == tok else gathered_shards
    return plan(query_in, key_in, value_in, grad_out, module_lengths)


def solution(mesh):
    placed = (
        P(("seq", "head"), None),
        P(("seq", "head"), None),
        P(("seq", "head"), None),
        P(("seq", "head"), None),
        P(),
    )
    return jax.shard_map(
        shards,
        mesh=mesh,
        in_specs=placed,
        out_specs=(
            P(("seq", "head"), None),
            P(("seq", "head"), None),
            P(("seq", "head"), None),
            P(("seq", "head"), None),
        ),
        check_vma=False,
    )
```

```python
import functools
import math

import jax
import jax.numpy as jnp
from jax import lax
from jax.experimental import pallas as pl
from jax.experimental.pallas import tpu as pltpu
from jax.sharding import PartitionSpec as P

HEAD_DIM = 128
SCALE = HEAD_DIM ** (-0.5)
LOG2E = math.log2(math.e)
MASKED = -1e30


def shifted(value, axis, by):
    peers = lax.axis_size(axis)
    pairs = [(i, i + by) for i in range(peers) if 0 <= i + by < peers]
    return lax.ppermute(value, axis, pairs)


def module_ids(module_lengths, positions):
    module_ends = jnp.cumsum(module_lengths)
    counted = jnp.sum((positions[:, None] >= module_ends[None, :]).astype(jnp.int32), axis=1)
    return jnp.where(positions >= 0, counted, -1)


def allowed_pairs(module_lengths, query_pos, key_pos):
    same = (
        module_ids(module_lengths, query_pos)[:, None]
        == module_ids(module_lengths, key_pos)[None, :]
    )
    return same & (key_pos[None, :] <= query_pos[:, None])


def score_grads(grad_rows, value_block, weights, row_delta, score_scale):
    dprobs = jnp.einsum("qd,kd->qk", grad_rows, value_block, preferred_element_type=jnp.float32)
    return (weights * (dprobs - row_delta[:, None]) * score_scale).astype(jnp.bfloat16)


def key_terms(dscores, weight_bf, query_rows, grad_rows):
    key_grad = jnp.einsum("qk,qd->kd", dscores, query_rows, preferred_element_type=jnp.float32)
    value_grad = jnp.einsum("qk,qd->kd", weight_bf, grad_rows, preferred_element_type=jnp.float32)
    return (key_grad, value_grad)


def one_block(query_rows, key_block, value_block, grad_rows, allowed, score_scale):
    scores = (
        jnp.einsum("qd,kd->qk", query_rows, key_block, preferred_element_type=jnp.float32)
        * score_scale
    )
    row_top = jnp.max(jnp.where(allowed, scores, -jnp.inf), axis=1, keepdims=True)
    row_total = jnp.sum(jnp.where(allowed, jnp.exp(scores - row_top), 0.0), axis=1, keepdims=True)
    log_total = row_top + jnp.log(row_total)
    weights = jnp.where(allowed, jnp.exp(scores - log_total), 0.0)
    weight_bf = weights.astype(jnp.bfloat16)
    attn_rows = jnp.einsum(
        "qk,kd->qd", weight_bf, value_block, preferred_element_type=jnp.float32
    ).astype(jnp.bfloat16)
    row_delta = jnp.sum(grad_rows.astype(jnp.float32) * attn_rows.astype(jnp.float32), axis=1)
    dscores = score_grads(grad_rows, value_block, weights, row_delta, score_scale)
    grad_q = jnp.einsum("qk,kd->qd", dscores, key_block, preferred_element_type=jnp.float32).astype(
        jnp.bfloat16
    )
    key_grad, value_grad = key_terms(dscores, weight_bf, query_rows, grad_rows)
    return (attn_rows, grad_q, key_grad, value_grad, log_total[:, 0], row_delta)


def gathered_shards(query_in, key_in, value_in, grad_out, module_lengths):
    head_q, head_k, head_v, head_do = (
        lax.all_to_all(query_in, "head", split_axis=1, concat_axis=0, tiled=True),
        lax.all_to_all(key_in, "head", split_axis=1, concat_axis=0, tiled=True),
        lax.all_to_all(value_in, "head", split_axis=1, concat_axis=0, tiled=True),
        lax.all_to_all(grad_out, "head", split_axis=1, concat_axis=0, tiled=True),
    )
    row_count = head_q.shape[0]
    width = head_q.shape[1]
    local_heads = width // HEAD_DIM
    prior_rows = row_count // 8
    score_scale = HEAD_DIM ** (-0.5)
    tail_start = row_count - prior_rows
    prior_k, prior_v = shifted((head_k[tail_start:], head_v[tail_start:]), "seq", 1)
    row_start = lax.axis_index("seq") * row_count
    query_pos = row_start + jnp.arange(row_count, dtype=jnp.int32)
    before_pos = row_start - prior_rows + jnp.arange(prior_rows, dtype=jnp.int32)
    key_pos = jnp.concatenate([before_pos, query_pos])
    block_rows = math.gcd(row_count, 512)
    block_count = row_count // block_rows
    pos_blocks = query_pos.reshape(block_count, block_rows)

    def by_head(flat, rows):
        return jnp.moveaxis(flat.reshape(rows, local_heads, HEAD_DIM), 1, 0)

    def to_flat(stacked):
        return jnp.moveaxis(stacked, 0, 1).reshape(stacked.shape[1], width)

    query_h = by_head(head_q, row_count)
    grad_h = by_head(head_do, row_count)
    key_h = by_head(jnp.concatenate([prior_k, head_k], axis=0), row_count + prior_rows)
    value_h = by_head(jnp.concatenate([prior_v, head_v], axis=0), row_count + prior_rows)

    def run_head(packed):
        query_rows, key_block, value_block, grad_rows = packed
        query_blocks = query_rows.reshape(block_count, block_rows, HEAD_DIM)
        grad_blocks = grad_rows.reshape(block_count, block_rows, HEAD_DIM)

        def run_block(inner):
            query_part, grad_part, pos_part = inner
            allowed = allowed_pairs(module_lengths, pos_part, key_pos)
            return one_block(query_part, key_block, value_block, grad_part, allowed, score_scale)

        attn_b, grad_qb, key_b, value_b, lse_b, delta_b = lax.map(
            run_block, (query_blocks, grad_blocks, pos_blocks)
        )
        return (
            attn_b.reshape(row_count, HEAD_DIM),
            grad_qb.reshape(row_count, HEAD_DIM),
            jnp.sum(key_b, axis=0),
            jnp.sum(value_b, axis=0),
            lse_b.reshape(row_count),
            delta_b.reshape(row_count),
        )

    attn_h, grad_qh, key_grad, value_grad, log_total, row_delta = lax.map(
        run_head, (query_h, key_h, value_h, grad_h)
    )
    attn_flat = to_flat(attn_h)
    attn_back = lax.all_to_all(attn_flat, "head", split_axis=0, concat_axis=1, tiled=True)
    grad_q = to_flat(grad_qh)
    later_k, later_v = shifted((key_grad[:, :prior_rows], value_grad[:, :prior_rows]), "seq", -1)
    key_total = key_grad[:, prior_rows:].at[:, tail_start:].add(later_k)
    value_total = value_grad[:, prior_rows:].at[:, tail_start:].add(later_v)
    grad_k = to_flat(key_total.astype(jnp.bfloat16))
    grad_v = to_flat(value_total.astype(jnp.bfloat16))
    back_q, back_k, back_v = (
        lax.all_to_all(grad_q, "head", split_axis=0, concat_axis=1, tiled=True),
        lax.all_to_all(grad_k, "head", split_axis=0, concat_axis=1, tiled=True),
        lax.all_to_all(grad_v, "head", split_axis=0, concat_axis=1, tiled=True),
    )
    return (attn_back, back_q, back_k, back_v)


def dot(left, right, left_dim, right_dim):
    return lax.dot_general(
        left, right, (((left_dim,), (right_dim,)), ((), ())), preferred_element_type=jnp.float32
    )


def module_ends_col(lengths_row):
    count = lengths_row.shape[1]
    row = lax.broadcasted_iota(jnp.int32, (count, count), 0)
    col = lax.broadcasted_iota(jnp.int32, (count, count), 1)
    return jnp.sum(jnp.where(col <= row, lengths_row, 0.0), axis=1, keepdims=True)


def bias_by_key(lengths_row, first_query, queries, first_key, keys, heads):
    ends = module_ends_col(lengths_row)
    lane = lax.broadcasted_iota(jnp.int32, (1, heads * queries), 1)
    query = (first_query + lane % queries).astype(jnp.float32)
    start = jnp.max(jnp.where(ends <= query, ends, 0.0), axis=0, keepdims=True)
    key = (first_key + lax.broadcasted_iota(jnp.int32, (keys, heads * queries), 0)).astype(
        jnp.float32
    )
    return jnp.where((key >= start) & (key <= query), 0.0, MASKED)


def score_pair(k, q, v, do, bias):
    return dot(k, q, 1, 1) * (SCALE * LOG2E) + bias, dot(v, do, 1, 1)


def softmax_columns(pairs):
    tops = [jnp.max(s, axis=0, keepdims=True) for s, _ in pairs]
    raws = [jnp.exp2(s - top) for (s, _), top in zip(pairs, tops)]
    totals = [jnp.sum(raw, axis=0, keepdims=True) for raw in raws]
    weights = [raw * (1.0 / total) for raw, total in zip(raws, totals)]
    deltas = [jnp.sum(w * dp, axis=0, keepdims=True) for w, (_, dp) in zip(weights, pairs)]
    logs = [top + jnp.log2(total) for top, total in zip(tops, totals)]
    return weights, logs, deltas


def score_grads_of(pairs, weights, deltas):
    return [
        (w * (dp - delta) * SCALE).astype(jnp.bfloat16)
        for w, (_, dp), delta in zip(weights, pairs, deltas)
    ]


def merged_columns(pairs, own):
    tops = [
        jnp.maximum(jnp.max(s, axis=0, keepdims=True), log) for (s, _), (log, _) in zip(pairs, own)
    ]
    raws = [jnp.exp2(s - top) for (s, _), top in zip(pairs, tops)]
    own_raws = [jnp.exp2(log - top) for (log, _), top in zip(own, tops)]
    parts = [
        1.0 / (jnp.sum(raw, axis=0, keepdims=True) + own_raw)
        for raw, own_raw in zip(raws, own_raws)
    ]
    weights = [raw * part for raw, part in zip(raws, parts)]
    deltas = [
        jnp.sum(w * dp, axis=0, keepdims=True) + own_raw * part * own_delta
        for w, (_, dp), own_raw, part, (_, own_delta) in zip(weights, pairs, own_raws, parts, own)
    ]
    grads = [w * (dp - delta) * SCALE for w, (_, dp), delta in zip(weights, pairs, deltas)]
    return [w.astype(jnp.bfloat16) for w in weights], [g.astype(jnp.bfloat16) for g in grads]


def side_by_side(rows):
    heads = rows.shape[1] // HEAD_DIM
    zero = jnp.zeros((rows.shape[0], HEAD_DIM), rows.dtype)
    blocks = [rows[:, c] for c in head_columns(0, rows.shape[1])]
    return jnp.concatenate(
        [
            jnp.concatenate([blocks[h] if g == h else zero for g in range(heads)], axis=1)
            for h in range(heads)
        ],
        axis=0,
    )


def head_columns(low, high, heads=1):
    wide = heads * HEAD_DIM
    return [slice(c, c + wide) for c in range(low, high, wide)]


def device_first(tok):
    place = lax.axis_index("seq") * lax.axis_size("head") + lax.axis_index("head")
    return place * tok


def fours(rows):
    table = jnp.concatenate(rows, axis=0)
    half = table.shape[1] // 4
    lane = lax.broadcasted_iota(jnp.int32, (1, table.shape[1]), 1)
    turned = [pltpu.roll(table, turn * half, 1) for turn in (3, 2, 1)]
    merged = []
    for at in range(0, len(rows), 2):
        now, after = slice(at, at + 1), slice(at + 1, at + 2)
        row = jnp.where(lane < 3 * half, turned[1][after], turned[2][after])
        row = jnp.where(lane < 2 * half, turned[0][now], row)
        merged.append(jnp.where(lane < half, table[now], row))
    return merged


def split_bf16(row):
    parts = []
    for _ in range(3):
        part = row.astype(jnp.bfloat16)
        parts.append(part)
        row = row - part.astype(jnp.float32)
    return jnp.concatenate([*parts, jnp.zeros_like(parts[0])], axis=1)


def joined(parts):
    parts = parts.astype(jnp.float32)
    count = parts.shape[1] // 4
    return parts[:, :count] + parts[:, count : 2 * count] + parts[:, 2 * count : 3 * count]


def pack_copies(prior, at, k_ref, v_ref, packed_ref, sems):
    half, tok = prior // 2, k_ref.shape[0]
    rows = pl.ds(tok - (at + 1) * half, half)
    return [
        pltpu.make_async_copy(
            ref.at[rows, :], packed_ref.at[pl.ds(n * half, half), :], sems.at[n]
        )
        for n, ref in enumerate((k_ref, v_ref))
    ]


def fill_masks(prior, tok, len_ref, own_bias_ref, near_bias_ref, lead_bias_ref, tail_bias_ref):
    first, half = device_first(tok), prior // 2
    lengths = len_ref[...].astype(jnp.float32)
    own_bias_ref[...] = bias_by_key(lengths, first + prior, tok - prior, first, tok, 2)
    near_bias_ref[...] = bias_by_key(lengths, first, prior, first - half, prior + half, 2)
    lead_bias_ref[...] = bias_by_key(lengths, first, prior, first - prior, 2 * prior, 2)
    tail_bias_ref[...] = bias_by_key(lengths, first + tok, half, first + tok - prior, prior, 4)


def pack_kernel(prior, len_hbm, k_ref, v_ref, near_ref, *refs):
    *mask_refs, len_ref, sems, len_sem = refs
    len_copy = pltpu.make_async_copy(len_hbm, len_ref, len_sem)
    len_copy.start()
    copies = pack_copies(prior, 0, k_ref, v_ref, near_ref, sems)
    for copy in copies:
        copy.start()
    len_copy.wait()
    fill_masks(prior, k_ref.shape[0], len_ref, *mask_refs)
    for copy in copies:
        copy.wait()


def ready_kernel(
    prior, q_hbm, k_hbm, v_hbm, do_hbm, far_ref, q_ref, k_ref, v_ref, do_ref, sems, far_sems
):
    pairs = ((q_hbm, q_ref), (k_hbm, k_ref), (v_hbm, v_ref), (do_hbm, do_ref))
    copies = pack_copies(prior, 1, k_hbm, v_hbm, far_ref, far_sems)
    copies += [pltpu.make_async_copy(hbm, ref, sems.at[n]) for n, (hbm, ref) in enumerate(pairs)]
    for copy in copies:
        copy.start()
    for copy in copies:
        copy.wait()


def own_diagonal(both):
    rows = both.shape[0] // 2
    return jnp.concatenate([both[:rows, :HEAD_DIM], both[rows:, HEAD_DIM:]], axis=1)


def pair_columns(at, step):
    wide = 2 * HEAD_DIM
    return [pl.ds(pl.multiple_of(at * step + c, wide), wide) for c in range(0, step, wide)]


def own_kernel(
    prior, step, bias_ref, q_ref, k_ref, v_ref, do_ref, attn_ref, gq_ref, gk_ref, gv_ref
):
    tok, width = k_ref.shape
    late = slice(prior, tok)

    @pl.loop(0, width // step)
    def _(at):
        bias = bias_ref[...]
        columns = pair_columns(at, step)
        queries = [side_by_side(q_ref[late, c]) for c in columns]
        cotangents = [side_by_side(do_ref[late, c]) for c in columns]
        pairs = [
            score_pair(k_ref[:, c], q, v_ref[:, c], do, bias)
            for c, q, do in zip(columns, queries, cotangents)
        ]
        weights, _, deltas = softmax_columns(pairs)
        grads = score_grads_of(pairs, weights, deltas)
        for c, w, g, q, do in zip(columns, weights, grads, queries, cotangents):
            w = w.astype(jnp.bfloat16)
            attn_ref[:, c] = own_diagonal(dot(w, v_ref[:, c], 0, 0)).astype(jnp.bfloat16)
            gq_ref[:, c] = own_diagonal(dot(g, k_ref[:, c], 0, 0)).astype(jnp.bfloat16)
            gk_ref[:, c] = dot(g, q, 1, 0)
            gv_ref[:, c] = dot(w, do, 1, 0)


def near_kernel(
    prior, near_bias_ref, lead_bias_ref, q_ref, k_ref, v_ref, do_ref, near_ref, *back_refs
):
    width, half = q_ref.shape[1], prior // 2
    far = lead_bias_ref[half - 1 : half, 0:1] == 0.0
    key = lax.broadcasted_iota(jnp.int32, (prior + half, 1), 0)
    bias = jnp.where(far & (key < half), MASKED, near_bias_ref[...])
    spare = lax.broadcasted_iota(jnp.int32, (half, 1), 0) == half - 1
    early, first, second = slice(0, prior), slice(0, half), slice(half, prior)
    columns = head_columns(0, width, 2)
    queries = [side_by_side(q_ref[early, c]) for c in columns]
    cotangents = [side_by_side(do_ref[early, c]) for c in columns]
    pairs = []
    for c, q, do in zip(columns, queries, cotangents):
        k = jnp.concatenate([near_ref[first, c], k_ref[early, c]], axis=0)
        v = jnp.concatenate([near_ref[second, c], v_ref[early, c]], axis=0)
        pairs.append(score_pair(k, q, v, do, bias))
    weights, logs, deltas = softmax_columns(pairs)
    weights = [w[:half] for w in weights]
    grads = score_grads_of([(s[:half], dp[:half]) for s, dp in pairs], weights, deltas)
    k_terms = [dot(g, q, 1, 0) for g, q in zip(grads, queries)]
    v_terms = [dot(w.astype(jnp.bfloat16), do, 1, 0) for w, do in zip(weights, cotangents)]
    logs, deltas = fours(logs), fours(deltas)
    for at, c in enumerate(head_columns(0, width, 4)):
        back_ref = back_refs[c.start * len(back_refs) // width]
        low = c.start % back_ref.shape[1]
        here = slice(low, low + c.stop - c.start)
        for row, terms, ref, place in (
            (logs[at], k_terms, q_ref, first), (deltas[at], v_terms, do_ref, second)
        ):
            rows = jnp.where(spare, split_bf16(row), ref[first, c])
            terms = jnp.concatenate(terms[2 * at : 2 * at + 2], axis=1).astype(jnp.bfloat16)
            back_ref[place, here] = jnp.where(far, rows, terms)


def lead_kernel(
    prior, step, bias_ref, q_ref, k_ref, v_ref, do_ref, near_ref, far_ref, gk_part_ref, gv_part_ref,
    attn_late_ref, gq_late_ref, attn_hbm, gq_hbm, gk_hbm, gv_hbm,
    attn_ref, gq_ref, gk_ref, gv_ref, sems, late_sems,
):
    tok, width = q_ref.shape
    half = prior // 2
    early, first, second = slice(0, prior), slice(0, half), slice(half, prior)
    late = pl.ds(prior, tok - prior)
    late_copies = [
        pltpu.make_async_copy(attn_late_ref, attn_hbm.at[late, :], late_sems.at[0]),
        pltpu.make_async_copy(gq_late_ref, gq_hbm.at[late, :], late_sems.at[1]),
    ]
    for copy in late_copies:
        copy.start()

    def copies(at):
        cols = pl.ds(pl.multiple_of(at * step, step), step)
        pairs = ((attn_ref, attn_hbm), (gq_ref, gq_hbm), (gk_ref, gk_hbm), (gv_ref, gv_hbm))
        return [
            pltpu.make_async_copy(ref.at[:, cols], hbm.at[pl.ds(0, prior), cols], sems.at[at, n])
            for n, (ref, hbm) in enumerate(pairs)
        ]

    @pl.loop(0, width // step)
    def _(at):
        bias = bias_ref[...]
        columns = pair_columns(at, step)
        queries = [side_by_side(q_ref[early, c]) for c in columns]
        cotangents = [side_by_side(do_ref[early, c]) for c in columns]
        keys = [
            jnp.concatenate([far_ref[first, c], near_ref[first, c], k_ref[early, c]], axis=0)
            for c in columns
        ]
        values = [
            jnp.concatenate([far_ref[second, c], near_ref[second, c], v_ref[early, c]], axis=0)
            for c in columns
        ]
        pairs = [
            score_pair(k, q, v, do, bias)
            for k, q, v, do in zip(keys, queries, values, cotangents)
        ]
        weights, _, deltas = softmax_columns(pairs)
        grads = score_grads_of(pairs, weights, deltas)
        for n, c in enumerate(columns):
            w, g = weights[n].astype(jnp.bfloat16), grads[n]
            attn_ref[:, c] = own_diagonal(dot(w, values[n], 0, 0)).astype(jnp.bfloat16)
            gq_ref[:, c] = own_diagonal(dot(g, keys[n], 0, 0)).astype(jnp.bfloat16)
            gk = gk_part_ref[early, c] + dot(g[prior:], queries[n], 1, 0)
            gv = gv_part_ref[early, c] + dot(w[prior:], cotangents[n], 1, 0)
            gk_ref[:, c] = gk.astype(jnp.bfloat16)
            gv_ref[:, c] = gv.astype(jnp.bfloat16)
        for copy in copies(at):
            copy.start()

    for at in range(width // step):
        for copy in copies(at):
            copy.wait()
    for copy in late_copies:
        copy.wait()


def tail_half(prior, low, bias_ref, k_ref, v_ref, gk_part_ref, gv_part_ref, after_ref):
    tok, half = k_ref.shape[0], prior // 2
    far = bias_ref[half - 1 : half, 0:1] == 0.0
    bias = jnp.where(far, bias_ref[...], MASKED)
    first, second, last = slice(0, half), slice(half, prior), slice(tok - prior, tok)
    places = head_columns(0, after_ref.shape[1], 4)
    columns = head_columns(low, low + after_ref.shape[1], 4)
    queries = [side_by_side(after_ref[first, p]) for p in places]
    cotangents = [side_by_side(after_ref[second, p]) for p in places]
    pairs = [
        score_pair(k_ref[last, c], q, v_ref[last, c], do, bias)
        for c, q, do in zip(columns, queries, cotangents)
    ]
    own = [
        (joined(after_ref[half - 16 : half, p][15:]), joined(after_ref[prior - 16 : prior, p][15:]))
        for p in places
    ]
    weights, grads = merged_columns(pairs, own)

    def fill(ref, part_ref, lefts, rights, rows):
        for p, c, left, right in zip(places, columns, lefts, rights):
            total = part_ref[last, c] + dot(left, right, 1, 0)
            terms = jnp.where(far, 0.0, after_ref[rows, p].astype(jnp.float32))
            ref[first, p] = total[first].astype(jnp.bfloat16)
            ref[second, p] = (total[second] + terms).astype(jnp.bfloat16)

    return (
        lambda ref: fill(ref, gv_part_ref, weights, cotangents, second),
        lambda ref: fill(ref, gk_part_ref, grads, queries, first),
    )


def tail_kernel(prior, bias_ref, k_ref, v_ref, gk_part_ref, gv_part_ref, after_ref, gk_ref, gv_ref):
    fill_gv, fill_gk = tail_half(
        prior, 0, bias_ref, k_ref, v_ref, gk_part_ref, gv_part_ref, after_ref
    )
    fill_gv(gv_ref)
    fill_gk(gk_ref)


def last_kernel(
    prior, bias_ref, k_ref, v_ref, gk_part_ref, gv_part_ref, after_ref, gk_first_ref, gv_first_ref,
    gk_in, gv_in, gk_hbm, gv_hbm, gk_ref, gv_ref, sems,
):
    rows = pl.ds(k_ref.shape[0] - prior, prior)
    low = gk_first_ref.shape[1]
    copies = []

    def send(ref, hbm, start):
        cols = pl.ds(start, ref.shape[1])
        copies.append(pltpu.make_async_copy(ref, hbm.at[rows, cols], sems.at[len(copies)]))
        copies[-1].start()

    send(gv_first_ref, gv_hbm, 0)
    send(gk_first_ref, gk_hbm, 0)
    fill_gv, fill_gk = tail_half(
        prior, low, bias_ref, k_ref, v_ref, gk_part_ref, gv_part_ref, after_ref
    )
    fill_gv(gv_ref)
    send(gv_ref, gv_hbm, low)
    fill_gk(gk_ref)
    send(gk_ref, gk_hbm, low)
    for copy in copies:
        copy.wait()


def neighbour(value, by):
    peers = lax.axis_size("seq") * lax.axis_size("head")
    pairs = [(i, i + by) for i in range(peers) if 0 <= i + by < peers]
    return lax.ppermute(value, ("seq", "head"), pairs)


def cost(heads, queries, keys, products, moved):
    return pl.CostEstimate(
        flops=2 * heads * queries * keys * HEAD_DIM * products,
        bytes_accessed=moved,
        transcendentals=heads * queries * keys,
    )


def halo_shards(query_in, key_in, value_in, grad_out, module_lengths):
    tok, width = query_in.shape
    prior = tok * lax.axis_size("head") // 8
    step = math.gcd(width, 8 * HEAD_DIM)
    groups = width // step
    anywhere = pl.BlockSpec(memory_space=pl.ANY)
    inside = pl.BlockSpec(memory_space=pltpu.VMEM)
    full16 = jax.ShapeDtypeStruct((tok, width), jnp.bfloat16)

    def near16(rows, columns):
        return pltpu.VMEM((rows, columns), jnp.bfloat16)

    def near32(rows, columns):
        return pltpu.VMEM((rows, columns), jnp.float32)

    def in_hbm(*values):
        return [pltpu.with_memory_space_constraint(value, pltpu.HBM) for value in values]

    def in_vmem(*values):
        return [pltpu.with_memory_space_constraint(value, pltpu.VMEM) for value in values]

    def call(kernel, name, ins, outs, shapes, scratch, work, moved, aliases=None):
        return pl.pallas_call(
            kernel,
            in_specs=ins,
            out_specs=outs,
            out_shape=shapes,
            scratch_shapes=scratch,
            input_output_aliases=aliases or {},
            cost_estimate=cost(*work, moved),
            compiler_params=pltpu.CompilerParams(vmem_limit_bytes=16 * 2**20),
            name=name,
        )

    lengths = module_lengths.reshape(1, -1)
    len_row = pltpu.VMEM(lengths.shape, jnp.int32)
    mask_shapes = [
        near32(tok, 2 * prior), near32(prior + prior // 2, 2 * prior),
        near32(2 * prior, 2 * prior), near32(prior, 2 * prior),
    ]
    near, own_bias, near_bias, lead_bias, tail_bias = call(
        functools.partial(pack_kernel, prior), "near_keys",
        [anywhere] * 3, [inside] * 5, [near16(prior, width), *mask_shapes],
        [len_row, pltpu.SemaphoreType.DMA((2,)), pltpu.SemaphoreType.DMA(())],
        (0, 0, 0, 0), 4 * prior * width,
    )(*in_hbm(lengths, key_in, value_in))
    near = neighbour(near, 1)

    far, q, k, v, do = call(
        functools.partial(ready_kernel, prior), "operands",
        [anywhere] * 4, [inside] * 5, [near16(prior, width)] + [near16(tok, width)] * 4,
        [pltpu.SemaphoreType.DMA((4,)), pltpu.SemaphoreType.DMA((2,))],
        (0, 0, 0, 0), 18 * tok * width,
    )(*in_hbm(query_in, key_in, value_in, grad_out))
    far = neighbour(far, 1)

    attn, gq, gk_part, gv_part = call(
        functools.partial(own_kernel, prior, width), "own_block",
        [inside] * 5, [inside] * 4,
        [near16(tok - prior, width)] * 2 + [near32(tok, width)] * 2, (),
        (width // HEAD_DIM, tok - prior, tok, 6), 18 * tok * width,
    )(*in_vmem(own_bias, q, k, v, do))

    near_bias, attn = lax.optimization_barrier((near_bias, attn))
    backs = call(
        functools.partial(near_kernel, prior), "near_terms",
        [inside] * 7, [inside] * 2, [near16(prior, width // 2)] * 2, (),
        (width // HEAD_DIM, prior, prior + prior // 2, 3), 8 * tok * width,
    )(*in_vmem(near_bias, lead_bias, q, k, v, do, near))
    backs = [neighbour(back, -1) for back in backs]

    attn, gq, gk, gv = call(
        functools.partial(lead_kernel, prior, step), "lead_rows",
        [inside] * 11, [anywhere] * 4, [full16] * 4,
        [near16(prior, width)] * 4
        + [pltpu.SemaphoreType.DMA((groups, 4)), pltpu.SemaphoreType.DMA((2,))],
        (width // HEAD_DIM, prior, 2 * prior, 6), 20 * tok * width,
    )(*in_vmem(lead_bias, q, k, v, do, near, far, gk_part, gv_part, attn, gq))

    here = in_vmem(tail_bias, k, v, gk_part, gv_part)
    work = (width // HEAD_DIM // 2, prior, prior // 2, 4)
    halves = call(
        functools.partial(tail_kernel, prior), "tail_keys",
        [inside] * 6, [inside] * 2, [near16(prior, width // 2)] * 2, (), work, 4 * tok * width,
    )(*here, *in_vmem(backs[0]))
    gk, gv = call(
        functools.partial(last_kernel, prior), "last_keys",
        [inside] * 8 + [anywhere] * 2, [anywhere] * 2, [full16] * 2,
        [near16(prior, width // 2)] * 2 + [pltpu.SemaphoreType.DMA((4,))],
        work, 6 * tok * width, {8: 0, 9: 1},
    )(*here, *in_vmem(backs[1], *halves), gk, gv)
    return (attn, gq, gk, gv)


def shards(query_in, key_in, value_in, grad_out, module_lengths):
    tok = query_in.shape[0]
    prior = tok * lax.axis_size("head") // 8
    plan = halo_shards if 2 * prior == tok else gathered_shards
    return plan(query_in, key_in, value_in, grad_out, module_lengths)


def solution(mesh):
    placed = (
        P(("seq", "head"), None),
        P(("seq", "head"), None),
        P(("seq", "head"), None),
        P(("seq", "head"), None),
        P(),
    )
    return jax.shard_map(
        shards,
        mesh=mesh,
        in_specs=placed,
        out_specs=(
            P(("seq", "head"), None),
            P(("seq", "head"), None),
            P(("seq", "head"), None),
            P(("seq", "head"), None),
        ),
        check_vma=False,
    )
```

```python
import functools
import math

import jax
import jax.numpy as jnp
from jax import lax
from jax.experimental import pallas as pl
from jax.experimental.pallas import tpu as pltpu
from jax.sharding import PartitionSpec as P

HEAD_DIM = 128
SCALE = HEAD_DIM ** (-0.5)
LOG2E = math.log2(math.e)
MASKED = -1e30


def shifted(value, axis, by):
    peers = lax.axis_size(axis)
    pairs = [(i, i + by) for i in range(peers) if 0 <= i + by < peers]
    return lax.ppermute(value, axis, pairs)


def module_ids(module_lengths, positions):
    module_ends = jnp.cumsum(module_lengths)
    counted = jnp.sum((positions[:, None] >= module_ends[None, :]).astype(jnp.int32), axis=1)
    return jnp.where(positions >= 0, counted, -1)


def allowed_pairs(module_lengths, query_pos, key_pos):
    same = (
        module_ids(module_lengths, query_pos)[:, None]
        == module_ids(module_lengths, key_pos)[None, :]
    )
    return same & (key_pos[None, :] <= query_pos[:, None])


def score_grads(grad_rows, value_block, weights, row_delta, score_scale):
    dprobs = jnp.einsum("qd,kd->qk", grad_rows, value_block, preferred_element_type=jnp.float32)
    return (weights * (dprobs - row_delta[:, None]) * score_scale).astype(jnp.bfloat16)


def key_terms(dscores, weight_bf, query_rows, grad_rows):
    key_grad = jnp.einsum("qk,qd->kd", dscores, query_rows, preferred_element_type=jnp.float32)
    value_grad = jnp.einsum("qk,qd->kd", weight_bf, grad_rows, preferred_element_type=jnp.float32)
    return (key_grad, value_grad)


def one_block(query_rows, key_block, value_block, grad_rows, allowed, score_scale):
    scores = (
        jnp.einsum("qd,kd->qk", query_rows, key_block, preferred_element_type=jnp.float32)
        * score_scale
    )
    row_top = jnp.max(jnp.where(allowed, scores, -jnp.inf), axis=1, keepdims=True)
    row_total = jnp.sum(jnp.where(allowed, jnp.exp(scores - row_top), 0.0), axis=1, keepdims=True)
    log_total = row_top + jnp.log(row_total)
    weights = jnp.where(allowed, jnp.exp(scores - log_total), 0.0)
    weight_bf = weights.astype(jnp.bfloat16)
    attn_rows = jnp.einsum(
        "qk,kd->qd", weight_bf, value_block, preferred_element_type=jnp.float32
    ).astype(jnp.bfloat16)
    row_delta = jnp.sum(grad_rows.astype(jnp.float32) * attn_rows.astype(jnp.float32), axis=1)
    dscores = score_grads(grad_rows, value_block, weights, row_delta, score_scale)
    grad_q = jnp.einsum("qk,kd->qd", dscores, key_block, preferred_element_type=jnp.float32).astype(
        jnp.bfloat16
    )
    key_grad, value_grad = key_terms(dscores, weight_bf, query_rows, grad_rows)
    return (attn_rows, grad_q, key_grad, value_grad, log_total[:, 0], row_delta)


def gathered_shards(query_in, key_in, value_in, grad_out, module_lengths):
    head_q, head_k, head_v, head_do = (
        lax.all_to_all(query_in, "head", split_axis=1, concat_axis=0, tiled=True),
        lax.all_to_all(key_in, "head", split_axis=1, concat_axis=0, tiled=True),
        lax.all_to_all(value_in, "head", split_axis=1, concat_axis=0, tiled=True),
        lax.all_to_all(grad_out, "head", split_axis=1, concat_axis=0, tiled=True),
    )
    row_count = head_q.shape[0]
    width = head_q.shape[1]
    local_heads = width // HEAD_DIM
    prior_rows = row_count // 8
    score_scale = HEAD_DIM ** (-0.5)
    tail_start = row_count - prior_rows
    prior_k, prior_v = shifted((head_k[tail_start:], head_v[tail_start:]), "seq", 1)
    row_start = lax.axis_index("seq") * row_count
    query_pos = row_start + jnp.arange(row_count, dtype=jnp.int32)
    before_pos = row_start - prior_rows + jnp.arange(prior_rows, dtype=jnp.int32)
    key_pos = jnp.concatenate([before_pos, query_pos])
    block_rows = math.gcd(row_count, 512)
    block_count = row_count // block_rows
    pos_blocks = query_pos.reshape(block_count, block_rows)

    def by_head(flat, rows):
        return jnp.moveaxis(flat.reshape(rows, local_heads, HEAD_DIM), 1, 0)

    def to_flat(stacked):
        return jnp.moveaxis(stacked, 0, 1).reshape(stacked.shape[1], width)

    query_h = by_head(head_q, row_count)
    grad_h = by_head(head_do, row_count)
    key_h = by_head(jnp.concatenate([prior_k, head_k], axis=0), row_count + prior_rows)
    value_h = by_head(jnp.concatenate([prior_v, head_v], axis=0), row_count + prior_rows)

    def run_head(packed):
        query_rows, key_block, value_block, grad_rows = packed
        query_blocks = query_rows.reshape(block_count, block_rows, HEAD_DIM)
        grad_blocks = grad_rows.reshape(block_count, block_rows, HEAD_DIM)

        def run_block(inner):
            query_part, grad_part, pos_part = inner
            allowed = allowed_pairs(module_lengths, pos_part, key_pos)
            return one_block(query_part, key_block, value_block, grad_part, allowed, score_scale)

        attn_b, grad_qb, key_b, value_b, lse_b, delta_b = lax.map(
            run_block, (query_blocks, grad_blocks, pos_blocks)
        )
        return (
            attn_b.reshape(row_count, HEAD_DIM),
            grad_qb.reshape(row_count, HEAD_DIM),
            jnp.sum(key_b, axis=0),
            jnp.sum(value_b, axis=0),
            lse_b.reshape(row_count),
            delta_b.reshape(row_count),
        )

    attn_h, grad_qh, key_grad, value_grad, log_total, row_delta = lax.map(
        run_head, (query_h, key_h, value_h, grad_h)
    )
    attn_flat = to_flat(attn_h)
    attn_back = lax.all_to_all(attn_flat, "head", split_axis=0, concat_axis=1, tiled=True)
    grad_q = to_flat(grad_qh)
    later_k, later_v = shifted((key_grad[:, :prior_rows], value_grad[:, :prior_rows]), "seq", -1)
    key_total = key_grad[:, prior_rows:].at[:, tail_start:].add(later_k)
    value_total = value_grad[:, prior_rows:].at[:, tail_start:].add(later_v)
    grad_k = to_flat(key_total.astype(jnp.bfloat16))
    grad_v = to_flat(value_total.astype(jnp.bfloat16))
    back_q, back_k, back_v = (
        lax.all_to_all(grad_q, "head", split_axis=0, concat_axis=1, tiled=True),
        lax.all_to_all(grad_k, "head", split_axis=0, concat_axis=1, tiled=True),
        lax.all_to_all(grad_v, "head", split_axis=0, concat_axis=1, tiled=True),
    )
    return (attn_back, back_q, back_k, back_v)


def dot(left, right, left_dim, right_dim):
    return lax.dot_general(
        left, right, (((left_dim,), (right_dim,)), ((), ())), preferred_element_type=jnp.float32
    )


def module_ends_col(lengths_row):
    count = lengths_row.shape[1]
    row = lax.broadcasted_iota(jnp.int32, (count, count), 0)
    col = lax.broadcasted_iota(jnp.int32, (count, count), 1)
    return jnp.sum(jnp.where(col <= row, lengths_row, 0.0), axis=1, keepdims=True)


def bias_by_key(lengths_row, first_query, queries, first_key, keys, heads):
    ends = module_ends_col(lengths_row)
    lane = lax.broadcasted_iota(jnp.int32, (1, heads * queries), 1)
    query = (first_query + lane % queries).astype(jnp.float32)
    start = jnp.max(jnp.where(ends <= query, ends, 0.0), axis=0, keepdims=True)
    key = (first_key + lax.broadcasted_iota(jnp.int32, (keys, heads * queries), 0)).astype(
        jnp.float32
    )
    return jnp.where((key >= start) & (key <= query), 0.0, MASKED)


def score_pair(k, q, v, do, bias):
    return dot(k, q, 1, 1) * (SCALE * LOG2E) + bias, dot(v, do, 1, 1)


def softmax_columns(pairs):
    tops = [jnp.max(s, axis=0, keepdims=True) for s, _ in pairs]
    raws = [jnp.exp2(s - top) for (s, _), top in zip(pairs, tops)]
    totals = [jnp.sum(raw, axis=0, keepdims=True) for raw in raws]
    weights = [raw * (1.0 / total) for raw, total in zip(raws, totals)]
    deltas = [jnp.sum(w * dp, axis=0, keepdims=True) for w, (_, dp) in zip(weights, pairs)]
    logs = [top + jnp.log2(total) for top, total in zip(tops, totals)]
    return weights, logs, deltas


def score_grads_of(pairs, weights, deltas):
    return [
        (w * (dp - delta) * SCALE).astype(jnp.bfloat16)
        for w, (_, dp), delta in zip(weights, pairs, deltas)
    ]


def merged_columns(pairs, own):
    tops = [
        jnp.maximum(jnp.max(s, axis=0, keepdims=True), log) for (s, _), (log, _) in zip(pairs, own)
    ]
    raws = [jnp.exp2(s - top) for (s, _), top in zip(pairs, tops)]
    own_raws = [jnp.exp2(log - top) for (log, _), top in zip(own, tops)]
    parts = [
        1.0 / (jnp.sum(raw, axis=0, keepdims=True) + own_raw)
        for raw, own_raw in zip(raws, own_raws)
    ]
    weights = [raw * part for raw, part in zip(raws, parts)]
    deltas = [
        jnp.sum(w * dp, axis=0, keepdims=True) + own_raw * part * own_delta
        for w, (_, dp), own_raw, part, (_, own_delta) in zip(weights, pairs, own_raws, parts, own)
    ]
    grads = [w * (dp - delta) * SCALE for w, (_, dp), delta in zip(weights, pairs, deltas)]
    return [w.astype(jnp.bfloat16) for w in weights], [g.astype(jnp.bfloat16) for g in grads]


def side_by_side(rows):
    heads = rows.shape[1] // HEAD_DIM
    zero = jnp.zeros((rows.shape[0], HEAD_DIM), rows.dtype)
    blocks = [rows[:, c] for c in head_columns(0, rows.shape[1])]
    return jnp.concatenate(
        [
            jnp.concatenate([blocks[h] if g == h else zero for g in range(heads)], axis=1)
            for h in range(heads)
        ],
        axis=0,
    )


def head_columns(low, high, heads=1):
    wide = heads * HEAD_DIM
    return [slice(c, c + wide) for c in range(low, high, wide)]


def device_first(tok):
    place = lax.axis_index("seq") * lax.axis_size("head") + lax.axis_index("head")
    return place * tok


def fours(rows):
    table = jnp.concatenate(rows, axis=0)
    half = table.shape[1] // 4
    lane = lax.broadcasted_iota(jnp.int32, (1, table.shape[1]), 1)
    turned = [pltpu.roll(table, turn * half, 1) for turn in (3, 2, 1)]
    merged = []
    for at in range(0, len(rows), 2):
        now, after = slice(at, at + 1), slice(at + 1, at + 2)
        row = jnp.where(lane < 3 * half, turned[1][after], turned[2][after])
        row = jnp.where(lane < 2 * half, turned[0][now], row)
        merged.append(jnp.where(lane < half, table[now], row))
    return merged


def split_bf16(row):
    parts = []
    for _ in range(3):
        part = row.astype(jnp.bfloat16)
        parts.append(part)
        row = row - part.astype(jnp.float32)
    return jnp.concatenate([*parts, jnp.zeros_like(parts[0])], axis=1)


def joined(parts):
    parts = parts.astype(jnp.float32)
    count = parts.shape[1] // 4
    return parts[:, :count] + parts[:, count : 2 * count] + parts[:, 2 * count : 3 * count]


def pack_copies(prior, at, k_ref, v_ref, packed_ref, sems):
    half, tok = prior // 2, k_ref.shape[0]
    rows = pl.ds(tok - (at + 1) * half, half)
    return [
        pltpu.make_async_copy(
            ref.at[rows, :], packed_ref.at[pl.ds(n * half, half), :], sems.at[n]
        )
        for n, ref in enumerate((k_ref, v_ref))
    ]


def fill_masks(prior, tok, len_ref, own_bias_ref, near_bias_ref, lead_bias_ref, tail_bias_ref):
    first, half = device_first(tok), prior // 2
    lengths = len_ref[...].astype(jnp.float32)
    own_bias_ref[...] = bias_by_key(lengths, first + prior, tok - prior, first, tok, 2)
    near_bias_ref[...] = bias_by_key(lengths, first, prior, first - half, prior + half, 2)
    lead_bias_ref[...] = bias_by_key(lengths, first, prior, first - prior, 2 * prior, 2)
    tail_bias_ref[...] = bias_by_key(lengths, first + tok, half, first + tok - prior, prior, 4)


def pack_kernel(prior, len_hbm, k_ref, v_ref, near_ref, *refs):
    *mask_refs, len_ref, sems, len_sem = refs
    len_copy = pltpu.make_async_copy(len_hbm, len_ref, len_sem)
    len_copy.start()
    copies = pack_copies(prior, 0, k_ref, v_ref, near_ref, sems)
    for copy in copies:
        copy.start()
    len_copy.wait()
    fill_masks(prior, k_ref.shape[0], len_ref, *mask_refs)
    for copy in copies:
        copy.wait()


def ready_kernel(
    prior, q_hbm, k_hbm, v_hbm, do_hbm, far_ref, q_ref, k_ref, v_ref, do_ref, sems, far_sems
):
    pairs = ((q_hbm, q_ref), (k_hbm, k_ref), (v_hbm, v_ref), (do_hbm, do_ref))
    copies = pack_copies(prior, 1, k_hbm, v_hbm, far_ref, far_sems)
    copies += [pltpu.make_async_copy(hbm, ref, sems.at[n]) for n, (hbm, ref) in enumerate(pairs)]
    for copy in copies:
        copy.start()
    for copy in copies:
        copy.wait()


def own_diagonal(both):
    rows = both.shape[0] // 2
    return jnp.concatenate([both[:rows, :HEAD_DIM], both[rows:, HEAD_DIM:]], axis=1)


def pair_columns(at, step):
    wide = 2 * HEAD_DIM
    return [pl.ds(pl.multiple_of(at * step + c, wide), wide) for c in range(0, step, wide)]


def own_kernel(
    prior, step, bias_ref, q_ref, k_ref, v_ref, do_ref, attn_ref, gq_ref, gk_ref, gv_ref
):
    tok, width = k_ref.shape
    late = slice(prior, tok)

    @pl.loop(0, width // step)
    def _(at):
        bias = bias_ref[...]
        columns = pair_columns(at, step)
        queries = [side_by_side(q_ref[late, c]) for c in columns]
        cotangents = [side_by_side(do_ref[late, c]) for c in columns]
        pairs = [
            score_pair(k_ref[:, c], q, v_ref[:, c], do, bias)
            for c, q, do in zip(columns, queries, cotangents)
        ]
        weights, _, deltas = softmax_columns(pairs)
        grads = score_grads_of(pairs, weights, deltas)
        for c, w, g, q, do in zip(columns, weights, grads, queries, cotangents):
            w = w.astype(jnp.bfloat16)
            attn_ref[:, c] = own_diagonal(dot(w, v_ref[:, c], 0, 0)).astype(jnp.bfloat16)
            gq_ref[:, c] = own_diagonal(dot(g, k_ref[:, c], 0, 0)).astype(jnp.bfloat16)
            gk_ref[:, c] = dot(g, q, 1, 0)
            gv_ref[:, c] = dot(w, do, 1, 0)


def near_kernel(
    prior, near_bias_ref, lead_bias_ref, q_ref, k_ref, v_ref, do_ref, near_ref, *back_refs
):
    width, half = q_ref.shape[1], prior // 2
    far = lead_bias_ref[half - 1 : half, 0:1] == 0.0
    key = lax.broadcasted_iota(jnp.int32, (prior + half, 1), 0)
    bias = jnp.where(far & (key < half), MASKED, near_bias_ref[...])
    spare = lax.broadcasted_iota(jnp.int32, (half, 1), 0) == half - 1
    early, first, second = slice(0, prior), slice(0, half), slice(half, prior)
    columns = head_columns(0, width, 2)
    queries = [side_by_side(q_ref[early, c]) for c in columns]
    cotangents = [side_by_side(do_ref[early, c]) for c in columns]
    pairs = []
    for c, q, do in zip(columns, queries, cotangents):
        k = jnp.concatenate([near_ref[first, c], k_ref[early, c]], axis=0)
        v = jnp.concatenate([near_ref[second, c], v_ref[early, c]], axis=0)
        pairs.append(score_pair(k, q, v, do, bias))
    weights, logs, deltas = softmax_columns(pairs)
    weights = [w[:half] for w in weights]
    grads = score_grads_of([(s[:half], dp[:half]) for s, dp in pairs], weights, deltas)
    k_terms = [dot(g, q, 1, 0) for g, q in zip(grads, queries)]
    v_terms = [dot(w.astype(jnp.bfloat16), do, 1, 0) for w, do in zip(weights, cotangents)]
    logs, deltas = fours(logs), fours(deltas)
    for at, c in enumerate(head_columns(0, width, 4)):
        back_ref = back_refs[c.start * len(back_refs) // width]
        low = c.start % back_ref.shape[1]
        here = slice(low, low + c.stop - c.start)
        for row, terms, ref, place in (
            (logs[at], k_terms, q_ref, first), (deltas[at], v_terms, do_ref, second)
        ):
            rows = jnp.where(spare, split_bf16(row), ref[first, c])
            terms = jnp.concatenate(terms[2 * at : 2 * at + 2], axis=1).astype(jnp.bfloat16)
            back_ref[place, here] = jnp.where(far, rows, terms)


def lead_kernel(
    prior, step, bias_ref, q_ref, k_ref, v_ref, do_ref, near_ref, far_ref, gk_part_ref, gv_part_ref,
    attn_late_ref, gq_late_ref, attn_hbm, gq_hbm, gk_hbm, gv_hbm,
    attn_ref, gq_ref, gk_ref, gv_ref, sems, late_sems,
):
    tok, width = q_ref.shape
    half = prior // 2
    early, first, second = slice(0, prior), slice(0, half), slice(half, prior)
    late = pl.ds(prior, tok - prior)
    late_copies = [
        pltpu.make_async_copy(attn_late_ref, attn_hbm.at[late, :], late_sems.at[0]),
        pltpu.make_async_copy(gq_late_ref, gq_hbm.at[late, :], late_sems.at[1]),
    ]
    for copy in late_copies:
        copy.start()

    def copies(at):
        cols = pl.ds(pl.multiple_of(at * step, step), step)
        pairs = ((attn_ref, attn_hbm), (gq_ref, gq_hbm), (gk_ref, gk_hbm), (gv_ref, gv_hbm))
        return [
            pltpu.make_async_copy(ref.at[:, cols], hbm.at[pl.ds(0, prior), cols], sems.at[at, n])
            for n, (ref, hbm) in enumerate(pairs)
        ]

    @pl.loop(0, width // step)
    def _(at):
        bias = bias_ref[...]
        columns = pair_columns(at, step)
        queries = [side_by_side(q_ref[early, c]) for c in columns]
        cotangents = [side_by_side(do_ref[early, c]) for c in columns]
        keys = [
            jnp.concatenate([far_ref[first, c], near_ref[first, c], k_ref[early, c]], axis=0)
            for c in columns
        ]
        values = [
            jnp.concatenate([far_ref[second, c], near_ref[second, c], v_ref[early, c]], axis=0)
            for c in columns
        ]
        pairs = [
            score_pair(k, q, v, do, bias)
            for k, q, v, do in zip(keys, queries, values, cotangents)
        ]
        weights, _, deltas = softmax_columns(pairs)
        grads = score_grads_of(pairs, weights, deltas)
        for n, c in enumerate(columns):
            w, g = weights[n].astype(jnp.bfloat16), grads[n]
            attn_ref[:, c] = own_diagonal(dot(w, values[n], 0, 0)).astype(jnp.bfloat16)
            gq_ref[:, c] = own_diagonal(dot(g, keys[n], 0, 0)).astype(jnp.bfloat16)
            gk = gk_part_ref[early, c] + dot(g[prior:], queries[n], 1, 0)
            gv = gv_part_ref[early, c] + dot(w[prior:], cotangents[n], 1, 0)
            gk_ref[:, c] = gk.astype(jnp.bfloat16)
            gv_ref[:, c] = gv.astype(jnp.bfloat16)
        for copy in copies(at):
            copy.start()

    for at in range(width // step):
        for copy in copies(at):
            copy.wait()
    for copy in late_copies:
        copy.wait()


def tail_half(prior, low, bias_ref, k_ref, v_ref, gk_part_ref, gv_part_ref, after_ref):
    tok, half = k_ref.shape[0], prior // 2
    far = bias_ref[half - 1 : half, 0:1] == 0.0
    bias = jnp.where(far, bias_ref[...], MASKED)
    first, second, last = slice(0, half), slice(half, prior), slice(tok - prior, tok)
    places = head_columns(0, after_ref.shape[1], 4)
    columns = head_columns(low, low + after_ref.shape[1], 4)
    queries = [side_by_side(after_ref[first, p]) for p in places]
    cotangents = [side_by_side(after_ref[second, p]) for p in places]
    pairs = [
        score_pair(k_ref[last, c], q, v_ref[last, c], do, bias)
        for c, q, do in zip(columns, queries, cotangents)
    ]
    own = [
        (joined(after_ref[half - 16 : half, p][15:]), joined(after_ref[prior - 16 : prior, p][15:]))
        for p in places
    ]
    weights, grads = merged_columns(pairs, own)

    def fill(ref, part_ref, lefts, rights, rows):
        for p, c, left, right in zip(places, columns, lefts, rights):
            total = part_ref[last, c] + dot(left, right, 1, 0)
            terms = jnp.where(far, 0.0, after_ref[rows, p].astype(jnp.float32))
            ref[first, p] = total[first].astype(jnp.bfloat16)
            ref[second, p] = (total[second] + terms).astype(jnp.bfloat16)

    return (
        lambda ref: fill(ref, gv_part_ref, weights, cotangents, second),
        lambda ref: fill(ref, gk_part_ref, grads, queries, first),
    )


def tail_kernel(prior, bias_ref, k_ref, v_ref, gk_part_ref, gv_part_ref, after_ref, gk_ref, gv_ref):
    fill_gv, fill_gk = tail_half(
        prior, 0, bias_ref, k_ref, v_ref, gk_part_ref, gv_part_ref, after_ref
    )
    fill_gv(gv_ref)
    fill_gk(gk_ref)


def last_kernel(
    prior, bias_ref, k_ref, v_ref, gk_part_ref, gv_part_ref, after_ref, gk_first_ref, gv_first_ref,
    gk_in, gv_in, gk_hbm, gv_hbm, gk_ref, gv_ref, sems,
):
    rows = pl.ds(k_ref.shape[0] - prior, prior)
    low = gk_first_ref.shape[1]
    copies = []

    def send(ref, hbm, start):
        cols = pl.ds(start, ref.shape[1])
        copies.append(pltpu.make_async_copy(ref, hbm.at[rows, cols], sems.at[len(copies)]))
        copies[-1].start()

    send(gv_first_ref, gv_hbm, 0)
    send(gk_first_ref, gk_hbm, 0)
    fill_gv, fill_gk = tail_half(
        prior, low, bias_ref, k_ref, v_ref, gk_part_ref, gv_part_ref, after_ref
    )
    fill_gv(gv_ref)
    send(gv_ref, gv_hbm, low)
    fill_gk(gk_ref)
    send(gk_ref, gk_hbm, low)
    for copy in copies:
        copy.wait()


def neighbour(value, by):
    peers = lax.axis_size("seq") * lax.axis_size("head")
    pairs = [(i, i + by) for i in range(peers) if 0 <= i + by < peers]
    return lax.ppermute(value, ("seq", "head"), pairs)


def cost(heads, queries, keys, products, moved):
    return pl.CostEstimate(
        flops=2 * heads * queries * keys * HEAD_DIM * products,
        bytes_accessed=moved,
        transcendentals=heads * queries * keys,
    )


def halo_shards(query_in, key_in, value_in, grad_out, module_lengths):
    tok, width = query_in.shape
    prior = tok * lax.axis_size("head") // 8
    step = math.gcd(width, 8 * HEAD_DIM)
    groups = width // step
    anywhere = pl.BlockSpec(memory_space=pl.ANY)
    inside = pl.BlockSpec(memory_space=pltpu.VMEM)
    full16 = jax.ShapeDtypeStruct((tok, width), jnp.bfloat16)

    def near16(rows, columns):
        return pltpu.VMEM((rows, columns), jnp.bfloat16)

    def near32(rows, columns):
        return pltpu.VMEM((rows, columns), jnp.float32)

    def in_hbm(*values):
        return [pltpu.with_memory_space_constraint(value, pltpu.HBM) for value in values]

    def in_vmem(*values):
        return [pltpu.with_memory_space_constraint(value, pltpu.VMEM) for value in values]

    def call(kernel, name, ins, outs, shapes, scratch, work, moved, aliases=None):
        return pl.pallas_call(
            kernel,
            in_specs=ins,
            out_specs=outs,
            out_shape=shapes,
            scratch_shapes=scratch,
            input_output_aliases=aliases or {},
            cost_estimate=cost(*work, moved),
            compiler_params=pltpu.CompilerParams(vmem_limit_bytes=16 * 2**20),
            name=name,
        )

    lengths = module_lengths.reshape(1, -1)
    len_row = pltpu.VMEM(lengths.shape, jnp.int32)
    mask_shapes = [
        near32(tok, 2 * prior), near32(prior + prior // 2, 2 * prior),
        near32(2 * prior, 2 * prior), near32(prior, 2 * prior),
    ]
    near, own_bias, near_bias, lead_bias, tail_bias = call(
        functools.partial(pack_kernel, prior), "near_keys",
        [anywhere] * 3, [inside] * 5, [near16(prior, width), *mask_shapes],
        [len_row, pltpu.SemaphoreType.DMA((2,)), pltpu.SemaphoreType.DMA(())],
        (0, 0, 0, 0), 4 * prior * width,
    )(*in_hbm(lengths, key_in, value_in))
    near = neighbour(near, 1)

    far, q, k, v, do = call(
        functools.partial(ready_kernel, prior), "operands",
        [anywhere] * 4, [inside] * 5, [near16(prior, width)] + [near16(tok, width)] * 4,
        [pltpu.SemaphoreType.DMA((4,)), pltpu.SemaphoreType.DMA((2,))],
        (0, 0, 0, 0), 18 * tok * width,
    )(*in_hbm(query_in, key_in, value_in, grad_out))
    far = neighbour(far, 1)

    attn, gq, gk_part, gv_part = call(
        functools.partial(own_kernel, prior, width), "own_block",
        [inside] * 5, [inside] * 4,
        [near16(tok - prior, width)] * 2 + [near32(tok, width)] * 2, (),
        (width // HEAD_DIM, tok - prior, tok, 6), 18 * tok * width,
    )(*in_vmem(own_bias, q, k, v, do))

    near_bias, attn = lax.optimization_barrier((near_bias, attn))
    backs = call(
        functools.partial(near_kernel, prior), "near_terms",
        [inside] * 7, [inside] * 2, [near16(prior, width // 2)] * 2, (),
        (width // HEAD_DIM, prior, prior + prior // 2, 3), 8 * tok * width,
    )(*in_vmem(near_bias, lead_bias, q, k, v, do, near))
    backs = [neighbour(back, -1) for back in backs]

    attn, gq, gk, gv = call(
        functools.partial(lead_kernel, prior, width), "lead_rows",
        [inside] * 11, [anywhere] * 4, [full16] * 4,
        [near16(prior, width)] * 4
        + [pltpu.SemaphoreType.DMA((groups, 4)), pltpu.SemaphoreType.DMA((2,))],
        (width // HEAD_DIM, prior, 2 * prior, 6), 20 * tok * width,
    )(*in_vmem(lead_bias, q, k, v, do, near, far, gk_part, gv_part, attn, gq))

    here = in_vmem(tail_bias, k, v, gk_part, gv_part)
    work = (width // HEAD_DIM // 2, prior, prior // 2, 4)
    halves = call(
        functools.partial(tail_kernel, prior), "tail_keys",
        [inside] * 6, [inside] * 2, [near16(prior, width // 2)] * 2, (), work, 4 * tok * width,
    )(*here, *in_vmem(backs[0]))
    gk, gv = call(
        functools.partial(last_kernel, prior), "last_keys",
        [inside] * 8 + [anywhere] * 2, [anywhere] * 2, [full16] * 2,
        [near16(prior, width // 2)] * 2 + [pltpu.SemaphoreType.DMA((4,))],
        work, 6 * tok * width, {8: 0, 9: 1},
    )(*here, *in_vmem(backs[1], *halves), gk, gv)
    return (attn, gq, gk, gv)


def shards(query_in, key_in, value_in, grad_out, module_lengths):
    tok = query_in.shape[0]
    prior = tok * lax.axis_size("head") // 8
    plan = halo_shards if 2 * prior == tok else gathered_shards
    return plan(query_in, key_in, value_in, grad_out, module_lengths)


def solution(mesh):
    placed = (
        P(("seq", "head"), None),
        P(("seq", "head"), None),
        P(("seq", "head"), None),
        P(("seq", "head"), None),
        P(),
    )
    return jax.shard_map(
        shards,
        mesh=mesh,
        in_specs=placed,
        out_specs=(
            P(("seq", "head"), None),
            P(("seq", "head"), None),
            P(("seq", "head"), None),
            P(("seq", "head"), None),
        ),
        check_vma=False,
    )
```

```python
import functools
import math

import jax
import jax.numpy as jnp
from jax import lax
from jax.experimental import pallas as pl
from jax.experimental.pallas import tpu as pltpu
from jax.sharding import PartitionSpec as P

HEAD_DIM = 128
SCALE = HEAD_DIM ** (-0.5)
LOG2E = math.log2(math.e)
MASKED = -1e30


def shifted(value, axis, by):
    peers = lax.axis_size(axis)
    pairs = [(i, i + by) for i in range(peers) if 0 <= i + by < peers]
    return lax.ppermute(value, axis, pairs)


def module_ids(module_lengths, positions):
    module_ends = jnp.cumsum(module_lengths)
    counted = jnp.sum((positions[:, None] >= module_ends[None, :]).astype(jnp.int32), axis=1)
    return jnp.where(positions >= 0, counted, -1)


def allowed_pairs(module_lengths, query_pos, key_pos):
    same = (
        module_ids(module_lengths, query_pos)[:, None]
        == module_ids(module_lengths, key_pos)[None, :]
    )
    return same & (key_pos[None, :] <= query_pos[:, None])


def score_grads(grad_rows, value_block, weights, row_delta, score_scale):
    dprobs = jnp.einsum("qd,kd->qk", grad_rows, value_block, preferred_element_type=jnp.float32)
    return (weights * (dprobs - row_delta[:, None]) * score_scale).astype(jnp.bfloat16)


def key_terms(dscores, weight_bf, query_rows, grad_rows):
    key_grad = jnp.einsum("qk,qd->kd", dscores, query_rows, preferred_element_type=jnp.float32)
    value_grad = jnp.einsum("qk,qd->kd", weight_bf, grad_rows, preferred_element_type=jnp.float32)
    return (key_grad, value_grad)


def one_block(query_rows, key_block, value_block, grad_rows, allowed, score_scale):
    scores = (
        jnp.einsum("qd,kd->qk", query_rows, key_block, preferred_element_type=jnp.float32)
        * score_scale
    )
    row_top = jnp.max(jnp.where(allowed, scores, -jnp.inf), axis=1, keepdims=True)
    row_total = jnp.sum(jnp.where(allowed, jnp.exp(scores - row_top), 0.0), axis=1, keepdims=True)
    log_total = row_top + jnp.log(row_total)
    weights = jnp.where(allowed, jnp.exp(scores - log_total), 0.0)
    weight_bf = weights.astype(jnp.bfloat16)
    attn_rows = jnp.einsum(
        "qk,kd->qd", weight_bf, value_block, preferred_element_type=jnp.float32
    ).astype(jnp.bfloat16)
    row_delta = jnp.sum(grad_rows.astype(jnp.float32) * attn_rows.astype(jnp.float32), axis=1)
    dscores = score_grads(grad_rows, value_block, weights, row_delta, score_scale)
    grad_q = jnp.einsum("qk,kd->qd", dscores, key_block, preferred_element_type=jnp.float32).astype(
        jnp.bfloat16
    )
    key_grad, value_grad = key_terms(dscores, weight_bf, query_rows, grad_rows)
    return (attn_rows, grad_q, key_grad, value_grad, log_total[:, 0], row_delta)


def gathered_shards(query_in, key_in, value_in, grad_out, module_lengths):
    head_q, head_k, head_v, head_do = (
        lax.all_to_all(query_in, "head", split_axis=1, concat_axis=0, tiled=True),
        lax.all_to_all(key_in, "head", split_axis=1, concat_axis=0, tiled=True),
        lax.all_to_all(value_in, "head", split_axis=1, concat_axis=0, tiled=True),
        lax.all_to_all(grad_out, "head", split_axis=1, concat_axis=0, tiled=True),
    )
    row_count = head_q.shape[0]
    width = head_q.shape[1]
    local_heads = width // HEAD_DIM
    prior_rows = row_count // 8
    score_scale = HEAD_DIM ** (-0.5)
    tail_start = row_count - prior_rows
    prior_k, prior_v = shifted((head_k[tail_start:], head_v[tail_start:]), "seq", 1)
    row_start = lax.axis_index("seq") * row_count
    query_pos = row_start + jnp.arange(row_count, dtype=jnp.int32)
    before_pos = row_start - prior_rows + jnp.arange(prior_rows, dtype=jnp.int32)
    key_pos = jnp.concatenate([before_pos, query_pos])
    block_rows = math.gcd(row_count, 512)
    block_count = row_count // block_rows
    pos_blocks = query_pos.reshape(block_count, block_rows)

    def by_head(flat, rows):
        return jnp.moveaxis(flat.reshape(rows, local_heads, HEAD_DIM), 1, 0)

    def to_flat(stacked):
        return jnp.moveaxis(stacked, 0, 1).reshape(stacked.shape[1], width)

    query_h = by_head(head_q, row_count)
    grad_h = by_head(head_do, row_count)
    key_h = by_head(jnp.concatenate([prior_k, head_k], axis=0), row_count + prior_rows)
    value_h = by_head(jnp.concatenate([prior_v, head_v], axis=0), row_count + prior_rows)

    def run_head(packed):
        query_rows, key_block, value_block, grad_rows = packed
        query_blocks = query_rows.reshape(block_count, block_rows, HEAD_DIM)
        grad_blocks = grad_rows.reshape(block_count, block_rows, HEAD_DIM)

        def run_block(inner):
            query_part, grad_part, pos_part = inner
            allowed = allowed_pairs(module_lengths, pos_part, key_pos)
            return one_block(query_part, key_block, value_block, grad_part, allowed, score_scale)

        attn_b, grad_qb, key_b, value_b, lse_b, delta_b = lax.map(
            run_block, (query_blocks, grad_blocks, pos_blocks)
        )
        return (
            attn_b.reshape(row_count, HEAD_DIM),
            grad_qb.reshape(row_count, HEAD_DIM),
            jnp.sum(key_b, axis=0),
            jnp.sum(value_b, axis=0),
            lse_b.reshape(row_count),
            delta_b.reshape(row_count),
        )

    attn_h, grad_qh, key_grad, value_grad, log_total, row_delta = lax.map(
        run_head, (query_h, key_h, value_h, grad_h)
    )
    attn_flat = to_flat(attn_h)
    attn_back = lax.all_to_all(attn_flat, "head", split_axis=0, concat_axis=1, tiled=True)
    grad_q = to_flat(grad_qh)
    later_k, later_v = shifted((key_grad[:, :prior_rows], value_grad[:, :prior_rows]), "seq", -1)
    key_total = key_grad[:, prior_rows:].at[:, tail_start:].add(later_k)
    value_total = value_grad[:, prior_rows:].at[:, tail_start:].add(later_v)
    grad_k = to_flat(key_total.astype(jnp.bfloat16))
    grad_v = to_flat(value_total.astype(jnp.bfloat16))
    back_q, back_k, back_v = (
        lax.all_to_all(grad_q, "head", split_axis=0, concat_axis=1, tiled=True),
        lax.all_to_all(grad_k, "head", split_axis=0, concat_axis=1, tiled=True),
        lax.all_to_all(grad_v, "head", split_axis=0, concat_axis=1, tiled=True),
    )
    return (attn_back, back_q, back_k, back_v)


def dot(left, right, left_dim, right_dim):
    return lax.dot_general(
        left, right, (((left_dim,), (right_dim,)), ((), ())), preferred_element_type=jnp.float32
    )


def module_ends_col(lengths_row):
    count = lengths_row.shape[1]
    row = lax.broadcasted_iota(jnp.int32, (count, count), 0)
    col = lax.broadcasted_iota(jnp.int32, (count, count), 1)
    return jnp.sum(jnp.where(col <= row, lengths_row, 0.0), axis=1, keepdims=True)


def bias_by_key(lengths_row, first_query, queries, first_key, keys, heads):
    ends = module_ends_col(lengths_row)
    lane = lax.broadcasted_iota(jnp.int32, (1, heads * queries), 1)
    query = (first_query + lane % queries).astype(jnp.float32)
    start = jnp.max(jnp.where(ends <= query, ends, 0.0), axis=0, keepdims=True)
    key = (first_key + lax.broadcasted_iota(jnp.int32, (keys, heads * queries), 0)).astype(
        jnp.float32
    )
    return jnp.where((key >= start) & (key <= query), 0.0, MASKED)


def score_pair(k, q, v, do, bias):
    return dot(k, q, 1, 1) * (SCALE * LOG2E) + bias, dot(v, do, 1, 1)


def softmax_columns(pairs):
    tops = [jnp.max(s, axis=0, keepdims=True) for s, _ in pairs]
    raws = [jnp.exp2(s - top) for (s, _), top in zip(pairs, tops)]
    totals = [jnp.sum(raw, axis=0, keepdims=True) for raw in raws]
    weights = [raw * (1.0 / total) for raw, total in zip(raws, totals)]
    deltas = [jnp.sum(w * dp, axis=0, keepdims=True) for w, (_, dp) in zip(weights, pairs)]
    logs = [top + jnp.log2(total) for top, total in zip(tops, totals)]
    return weights, logs, deltas


def score_grads_of(pairs, weights, deltas):
    return [
        (w * (dp - delta) * SCALE).astype(jnp.bfloat16)
        for w, (_, dp), delta in zip(weights, pairs, deltas)
    ]


def merged_columns(pairs, own):
    tops = [
        jnp.maximum(jnp.max(s, axis=0, keepdims=True), log) for (s, _), (log, _) in zip(pairs, own)
    ]
    raws = [jnp.exp2(s - top) for (s, _), top in zip(pairs, tops)]
    own_raws = [jnp.exp2(log - top) for (log, _), top in zip(own, tops)]
    parts = [
        1.0 / (jnp.sum(raw, axis=0, keepdims=True) + own_raw)
        for raw, own_raw in zip(raws, own_raws)
    ]
    weights = [raw * part for raw, part in zip(raws, parts)]
    deltas = [
        jnp.sum(w * dp, axis=0, keepdims=True) + own_raw * part * own_delta
        for w, (_, dp), own_raw, part, (_, own_delta) in zip(weights, pairs, own_raws, parts, own)
    ]
    grads = [w * (dp - delta) * SCALE for w, (_, dp), delta in zip(weights, pairs, deltas)]
    return [w.astype(jnp.bfloat16) for w in weights], [g.astype(jnp.bfloat16) for g in grads]


def side_by_side(rows):
    heads = rows.shape[1] // HEAD_DIM
    zero = jnp.zeros((rows.shape[0], HEAD_DIM), rows.dtype)
    blocks = [rows[:, c] for c in head_columns(0, rows.shape[1])]
    return jnp.concatenate(
        [
            jnp.concatenate([blocks[h] if g == h else zero for g in range(heads)], axis=1)
            for h in range(heads)
        ],
        axis=0,
    )


def head_columns(low, high, heads=1):
    wide = heads * HEAD_DIM
    return [slice(c, c + wide) for c in range(low, high, wide)]


def device_first(tok):
    place = lax.axis_index("seq") * lax.axis_size("head") + lax.axis_index("head")
    return place * tok


def fours(rows):
    table = jnp.concatenate(rows, axis=0)
    half = table.shape[1] // 4
    lane = lax.broadcasted_iota(jnp.int32, (1, table.shape[1]), 1)
    turned = [pltpu.roll(table, turn * half, 1) for turn in (3, 2, 1)]
    merged = []
    for at in range(0, len(rows), 2):
        now, after = slice(at, at + 1), slice(at + 1, at + 2)
        row = jnp.where(lane < 3 * half, turned[1][after], turned[2][after])
        row = jnp.where(lane < 2 * half, turned[0][now], row)
        merged.append(jnp.where(lane < half, table[now], row))
    return merged


def split_bf16(row):
    parts = []
    for _ in range(3):
        part = row.astype(jnp.bfloat16)
        parts.append(part)
        row = row - part.astype(jnp.float32)
    return jnp.concatenate([*parts, jnp.zeros_like(parts[0])], axis=1)


def joined(parts):
    parts = parts.astype(jnp.float32)
    count = parts.shape[1] // 4
    return parts[:, :count] + parts[:, count : 2 * count] + parts[:, 2 * count : 3 * count]


def pack_copies(prior, at, k_ref, v_ref, packed_ref, sems):
    half, tok = prior // 2, k_ref.shape[0]
    rows = pl.ds(tok - (at + 1) * half, half)
    return [
        pltpu.make_async_copy(
            ref.at[rows, :], packed_ref.at[pl.ds(n * half, half), :], sems.at[n]
        )
        for n, ref in enumerate((k_ref, v_ref))
    ]


def fill_masks(prior, tok, len_ref, own_bias_ref, near_bias_ref, lead_bias_ref, tail_bias_ref):
    first, half = device_first(tok), prior // 2
    lengths = len_ref[...].astype(jnp.float32)
    own_bias_ref[...] = bias_by_key(lengths, first + prior, tok - prior, first, tok, 2)
    near_bias_ref[...] = bias_by_key(lengths, first, prior, first - half, prior + half, 2)
    lead_bias_ref[...] = bias_by_key(lengths, first, prior, first - prior, 2 * prior, 2)
    tail_bias_ref[...] = bias_by_key(lengths, first + tok, half, first + tok - prior, prior, 4)


def pack_kernel(prior, len_hbm, k_ref, v_ref, near_ref, *refs):
    *mask_refs, len_ref, sems, len_sem = refs
    len_copy = pltpu.make_async_copy(len_hbm, len_ref, len_sem)
    len_copy.start()
    copies = pack_copies(prior, 0, k_ref, v_ref, near_ref, sems)
    for copy in copies:
        copy.start()
    len_copy.wait()
    fill_masks(prior, k_ref.shape[0], len_ref, *mask_refs)
    for copy in copies:
        copy.wait()


def ready_kernel(
    prior, q_hbm, k_hbm, v_hbm, do_hbm, far_ref, q_ref, k_ref, v_ref, do_ref, sems, far_sems
):
    pairs = ((q_hbm, q_ref), (k_hbm, k_ref), (v_hbm, v_ref), (do_hbm, do_ref))
    copies = pack_copies(prior, 1, k_hbm, v_hbm, far_ref, far_sems)
    copies += [pltpu.make_async_copy(hbm, ref, sems.at[n]) for n, (hbm, ref) in enumerate(pairs)]
    for copy in copies:
        copy.start()
    for copy in copies:
        copy.wait()


def own_diagonal(both):
    rows = both.shape[0] // 2
    return jnp.concatenate([both[:rows, :HEAD_DIM], both[rows:, HEAD_DIM:]], axis=1)


def pair_columns(at, step):
    wide = 2 * HEAD_DIM
    return [pl.ds(pl.multiple_of(at * step + c, wide), wide) for c in range(0, step, wide)]


def own_kernel(
    prior, step, bias_ref, q_ref, k_ref, v_ref, do_ref, attn_ref, gq_ref, gk_ref, gv_ref
):
    tok, width = k_ref.shape
    late = slice(prior, tok)

    @pl.loop(0, width // step)
    def _(at):
        bias = bias_ref[...]
        columns = pair_columns(at, step)
        queries = [side_by_side(q_ref[late, c]) for c in columns]
        cotangents = [side_by_side(do_ref[late, c]) for c in columns]
        pairs = [
            score_pair(k_ref[:, c], q, v_ref[:, c], do, bias)
            for c, q, do in zip(columns, queries, cotangents)
        ]
        weights, _, deltas = softmax_columns(pairs)
        grads = score_grads_of(pairs, weights, deltas)
        for c, w, g, q, do in zip(columns, weights, grads, queries, cotangents):
            w = w.astype(jnp.bfloat16)
            attn_ref[:, c] = own_diagonal(dot(w, v_ref[:, c], 0, 0)).astype(jnp.bfloat16)
            gq_ref[:, c] = own_diagonal(dot(g, k_ref[:, c], 0, 0)).astype(jnp.bfloat16)
            gk_ref[:, c] = dot(g, q, 1, 0)
            gv_ref[:, c] = dot(w, do, 1, 0)


def near_kernel(
    prior, near_bias_ref, lead_bias_ref, q_ref, k_ref, v_ref, do_ref, near_ref, *back_refs
):
    width, half = q_ref.shape[1], prior // 2
    far = lead_bias_ref[half - 1 : half, 0:1] == 0.0
    key = lax.broadcasted_iota(jnp.int32, (prior + half, 1), 0)
    bias = jnp.where(far & (key < half), MASKED, near_bias_ref[...])
    spare = lax.broadcasted_iota(jnp.int32, (half, 1), 0) == half - 1
    early, first, second = slice(0, prior), slice(0, half), slice(half, prior)
    columns = head_columns(0, width, 2)
    queries = [side_by_side(q_ref[early, c]) for c in columns]
    cotangents = [side_by_side(do_ref[early, c]) for c in columns]
    pairs = []
    for c, q, do in zip(columns, queries, cotangents):
        k = jnp.concatenate([near_ref[first, c], k_ref[early, c]], axis=0)
        v = jnp.concatenate([near_ref[second, c], v_ref[early, c]], axis=0)
        pairs.append(score_pair(k, q, v, do, bias))
    weights, logs, deltas = softmax_columns(pairs)
    weights = [w[:half] for w in weights]
    grads = score_grads_of([(s[:half], dp[:half]) for s, dp in pairs], weights, deltas)
    k_terms = [dot(g, q, 1, 0) for g, q in zip(grads, queries)]
    v_terms = [dot(w.astype(jnp.bfloat16), do, 1, 0) for w, do in zip(weights, cotangents)]
    logs, deltas = fours(logs), fours(deltas)
    for at, c in enumerate(head_columns(0, width, 4)):
        back_ref = back_refs[c.start * len(back_refs) // width]
        low = c.start % back_ref.shape[1]
        here = slice(low, low + c.stop - c.start)
        for row, terms, ref, place in (
            (logs[at], k_terms, q_ref, first), (deltas[at], v_terms, do_ref, second)
        ):
            rows = jnp.where(spare, split_bf16(row), ref[first, c])
            terms = jnp.concatenate(terms[2 * at : 2 * at + 2], axis=1).astype(jnp.bfloat16)
            back_ref[place, here] = jnp.where(far, rows, terms)


def lead_kernel(
    prior, step, bias_ref, q_ref, k_ref, v_ref, do_ref, near_ref, far_ref, gk_part_ref, gv_part_ref,
    attn_late_ref, gq_late_ref, attn_hbm, gq_hbm, gk_hbm, gv_hbm,
    attn_ref, gq_ref, gk_ref, gv_ref, sems, late_sems,
):
    tok, width = q_ref.shape
    half = prior // 2
    early, first, second = slice(0, prior), slice(0, half), slice(half, prior)
    late = pl.ds(prior, tok - prior)
    late_copies = [
        pltpu.make_async_copy(attn_late_ref, attn_hbm.at[late, :], late_sems.at[0]),
        pltpu.make_async_copy(gq_late_ref, gq_hbm.at[late, :], late_sems.at[1]),
    ]
    for copy in late_copies:
        copy.start()

    def copies(at):
        cols = pl.ds(pl.multiple_of(at * step, step), step)
        pairs = ((attn_ref, attn_hbm), (gq_ref, gq_hbm), (gk_ref, gk_hbm), (gv_ref, gv_hbm))
        return [
            pltpu.make_async_copy(ref.at[:, cols], hbm.at[pl.ds(0, prior), cols], sems.at[at, n])
            for n, (ref, hbm) in enumerate(pairs)
        ]

    @pl.loop(0, width // step)
    def _(at):
        bias = bias_ref[...]
        columns = pair_columns(at, step)
        queries = [side_by_side(q_ref[early, c]) for c in columns]
        cotangents = [side_by_side(do_ref[early, c]) for c in columns]
        keys = [
            jnp.concatenate([far_ref[first, c], near_ref[first, c], k_ref[early, c]], axis=0)
            for c in columns
        ]
        values = [
            jnp.concatenate([far_ref[second, c], near_ref[second, c], v_ref[early, c]], axis=0)
            for c in columns
        ]
        pairs = [
            score_pair(k, q, v, do, bias)
            for k, q, v, do in zip(keys, queries, values, cotangents)
        ]
        weights, _, deltas = softmax_columns(pairs)
        grads = score_grads_of(pairs, weights, deltas)
        for n, c in enumerate(columns):
            w, g = weights[n].astype(jnp.bfloat16), grads[n]
            attn_ref[:, c] = own_diagonal(dot(w, values[n], 0, 0)).astype(jnp.bfloat16)
            gq_ref[:, c] = own_diagonal(dot(g, keys[n], 0, 0)).astype(jnp.bfloat16)
            gk = gk_part_ref[early, c] + dot(g[prior:], queries[n], 1, 0)
            gv = gv_part_ref[early, c] + dot(w[prior:], cotangents[n], 1, 0)
            gk_ref[:, c] = gk.astype(jnp.bfloat16)
            gv_ref[:, c] = gv.astype(jnp.bfloat16)
        for copy in copies(at):
            copy.start()

    for at in range(width // step):
        for copy in copies(at):
            copy.wait()
    for copy in late_copies:
        copy.wait()


def tail_half(prior, low, bias_ref, k_ref, v_ref, gk_part_ref, gv_part_ref, after_ref):
    tok, half = k_ref.shape[0], prior // 2
    far = bias_ref[half - 1 : half, 0:1] == 0.0
    bias = jnp.where(far, bias_ref[...], MASKED)
    first, second, last = slice(0, half), slice(half, prior), slice(tok - prior, tok)
    places = head_columns(0, after_ref.shape[1], 4)
    columns = head_columns(low, low + after_ref.shape[1], 4)
    queries = [side_by_side(after_ref[first, p]) for p in places]
    cotangents = [side_by_side(after_ref[second, p]) for p in places]
    pairs = [
        score_pair(k_ref[last, c], q, v_ref[last, c], do, bias)
        for c, q, do in zip(columns, queries, cotangents)
    ]
    own = [
        (joined(after_ref[half - 16 : half, p][15:]), joined(after_ref[prior - 16 : prior, p][15:]))
        for p in places
    ]
    weights, grads = merged_columns(pairs, own)

    def fill(ref, part_ref, lefts, rights, rows):
        for p, c, left, right in zip(places, columns, lefts, rights):
            total = part_ref[last, c] + dot(left, right, 1, 0)
            terms = jnp.where(far, 0.0, after_ref[rows, p].astype(jnp.float32))
            ref[first, p] = total[first].astype(jnp.bfloat16)
            ref[second, p] = (total[second] + terms).astype(jnp.bfloat16)

    return (
        lambda ref: fill(ref, gv_part_ref, weights, cotangents, second),
        lambda ref: fill(ref, gk_part_ref, grads, queries, first),
    )


def tail_kernel(prior, bias_ref, k_ref, v_ref, gk_part_ref, gv_part_ref, after_ref, gk_ref, gv_ref):
    fill_gv, fill_gk = tail_half(
        prior, 0, bias_ref, k_ref, v_ref, gk_part_ref, gv_part_ref, after_ref
    )
    fill_gv(gv_ref)
    fill_gk(gk_ref)


def last_kernel(
    prior, bias_ref, k_ref, v_ref, gk_part_ref, gv_part_ref, after_ref, gk_first_ref, gv_first_ref,
    gk_in, gv_in, gk_hbm, gv_hbm, gk_ref, gv_ref, sems,
):
    rows = pl.ds(k_ref.shape[0] - prior, prior)
    low = gk_first_ref.shape[1]
    copies = []

    def send(ref, hbm, start):
        cols = pl.ds(start, ref.shape[1])
        copies.append(pltpu.make_async_copy(ref, hbm.at[rows, cols], sems.at[len(copies)]))
        copies[-1].start()

    fill_gv, fill_gk = tail_half(
        prior, low, bias_ref, k_ref, v_ref, gk_part_ref, gv_part_ref, after_ref
    )
    fill_gv(gv_ref)
    send(gv_ref, gv_hbm, low)
    send(gv_first_ref, gv_hbm, 0)
    fill_gk(gk_ref)
    send(gk_ref, gk_hbm, low)
    send(gk_first_ref, gk_hbm, 0)
    for copy in copies:
        copy.wait()


def neighbour(value, by):
    peers = lax.axis_size("seq") * lax.axis_size("head")
    pairs = [(i, i + by) for i in range(peers) if 0 <= i + by < peers]
    return lax.ppermute(value, ("seq", "head"), pairs)


def cost(heads, queries, keys, products, moved):
    return pl.CostEstimate(
        flops=2 * heads * queries * keys * HEAD_DIM * products,
        bytes_accessed=moved,
        transcendentals=heads * queries * keys,
    )


def halo_shards(query_in, key_in, value_in, grad_out, module_lengths):
    tok, width = query_in.shape
    prior = tok * lax.axis_size("head") // 8
    step = math.gcd(width, 8 * HEAD_DIM)
    groups = width // step
    anywhere = pl.BlockSpec(memory_space=pl.ANY)
    inside = pl.BlockSpec(memory_space=pltpu.VMEM)
    full16 = jax.ShapeDtypeStruct((tok, width), jnp.bfloat16)

    def near16(rows, columns):
        return pltpu.VMEM((rows, columns), jnp.bfloat16)

    def near32(rows, columns):
        return pltpu.VMEM((rows, columns), jnp.float32)

    def in_hbm(*values):
        return [pltpu.with_memory_space_constraint(value, pltpu.HBM) for value in values]

    def in_vmem(*values):
        return [pltpu.with_memory_space_constraint(value, pltpu.VMEM) for value in values]

    def call(kernel, name, ins, outs, shapes, scratch, work, moved, aliases=None):
        return pl.pallas_call(
            kernel,
            in_specs=ins,
            out_specs=outs,
            out_shape=shapes,
            scratch_shapes=scratch,
            input_output_aliases=aliases or {},
            cost_estimate=cost(*work, moved),
            compiler_params=pltpu.CompilerParams(vmem_limit_bytes=16 * 2**20),
            name=name,
        )

    lengths = module_lengths.reshape(1, -1)
    len_row = pltpu.VMEM(lengths.shape, jnp.int32)
    mask_shapes = [
        near32(tok, 2 * prior), near32(prior + prior // 2, 2 * prior),
        near32(2 * prior, 2 * prior), near32(prior, 2 * prior),
    ]
    near, own_bias, near_bias, lead_bias, tail_bias = call(
        functools.partial(pack_kernel, prior), "near_keys",
        [anywhere] * 3, [inside] * 5, [near16(prior, width), *mask_shapes],
        [len_row, pltpu.SemaphoreType.DMA((2,)), pltpu.SemaphoreType.DMA(())],
        (0, 0, 0, 0), 4 * prior * width,
    )(*in_hbm(lengths, key_in, value_in))
    near = neighbour(near, 1)

    far, q, k, v, do = call(
        functools.partial(ready_kernel, prior), "operands",
        [anywhere] * 4, [inside] * 5, [near16(prior, width)] + [near16(tok, width)] * 4,
        [pltpu.SemaphoreType.DMA((4,)), pltpu.SemaphoreType.DMA((2,))],
        (0, 0, 0, 0), 18 * tok * width,
    )(*in_hbm(query_in, key_in, value_in, grad_out))
    far = neighbour(far, 1)

    attn, gq, gk_part, gv_part = call(
        functools.partial(own_kernel, prior, width), "own_block",
        [inside] * 5, [inside] * 4,
        [near16(tok - prior, width)] * 2 + [near32(tok, width)] * 2, (),
        (width // HEAD_DIM, tok - prior, tok, 6), 18 * tok * width,
    )(*in_vmem(own_bias, q, k, v, do))

    near_bias, attn = lax.optimization_barrier((near_bias, attn))
    backs = call(
        functools.partial(near_kernel, prior), "near_terms",
        [inside] * 7, [inside] * 2, [near16(prior, width // 2)] * 2, (),
        (width // HEAD_DIM, prior, prior + prior // 2, 3), 8 * tok * width,
    )(*in_vmem(near_bias, lead_bias, q, k, v, do, near))
    backs = [neighbour(back, -1) for back in backs]

    attn, gq, gk, gv = call(
        functools.partial(lead_kernel, prior, width), "lead_rows",
        [inside] * 11, [anywhere] * 4, [full16] * 4,
        [near16(prior, width)] * 4
        + [pltpu.SemaphoreType.DMA((groups, 4)), pltpu.SemaphoreType.DMA((2,))],
        (width // HEAD_DIM, prior, 2 * prior, 6), 20 * tok * width,
    )(*in_vmem(lead_bias, q, k, v, do, near, far, gk_part, gv_part, attn, gq))

    here = in_vmem(tail_bias, k, v, gk_part, gv_part)
    work = (width // HEAD_DIM // 2, prior, prior // 2, 4)
    halves = call(
        functools.partial(tail_kernel, prior), "tail_keys",
        [inside] * 6, [inside] * 2, [near16(prior, width // 2)] * 2, (), work, 4 * tok * width,
    )(*here, *in_vmem(backs[0]))
    gk, gv = call(
        functools.partial(last_kernel, prior), "last_keys",
        [inside] * 8 + [anywhere] * 2, [anywhere] * 2, [full16] * 2,
        [near16(prior, width // 2)] * 2 + [pltpu.SemaphoreType.DMA((4,))],
        work, 6 * tok * width, {8: 0, 9: 1},
    )(*here, *in_vmem(backs[1], *halves), gk, gv)
    return (attn, gq, gk, gv)


def shards(query_in, key_in, value_in, grad_out, module_lengths):
    tok = query_in.shape[0]
    prior = tok * lax.axis_size("head") // 8
    plan = halo_shards if 2 * prior == tok else gathered_shards
    return plan(query_in, key_in, value_in, grad_out, module_lengths)


def solution(mesh):
    placed = (
        P(("seq", "head"), None),
        P(("seq", "head"), None),
        P(("seq", "head"), None),
        P(("seq", "head"), None),
        P(),
    )
    return jax.shard_map(
        shards,
        mesh=mesh,
        in_specs=placed,
        out_specs=(
            P(("seq", "head"), None),
            P(("seq", "head"), None),
            P(("seq", "head"), None),
            P(("seq", "head"), None),
        ),
        check_vma=False,
    )
```
